32 devices in a mesh: dp: 16 (over z, x, core), tensor: 2 (over y).
Axes of the slice: x: 2, y: 2, z: 4, core: 2. Of those that a mesh axis runs over, the one named last changes fastest.
Arguments:
- block_input: bfloat16 [8192, 1536], P(('dp', 'tensor')), may hold values from -6 to 6
- norm_gains: float32 [1536, 2], replicated, may hold values from 0.1 to 1.9
- router_weight: bfloat16 [1536, 8], replicated, may hold values from -0.078125 to 0.078125
- query_matrix: bfloat16 [1536, 1536], P('dp', 'tensor'), may hold values from -0.15625 to 0.15625
- key_matrix: bfloat16 [1536, 256], P('dp', 'tensor'), may hold values from -0.15625 to 0.15625
- value_matrix: bfloat16 [1536, 256], P('dp', 'tensor'), may hold values from -0.15625 to 0.15625
- output_weight: bfloat16 [1536, 1536], P('dp', 'tensor'), may hold values from -0.875 to 0.875
- gate_weight: bfloat16 [1536, 8, 768], P('dp', None, 'tensor'), may hold values from -0.15625 to 0.15625
- up_weight: bfloat16 [1536, 8, 768], P('dp', None, 'tensor'), may hold values from -0.15625 to 0.15625
- down_weight: bfloat16 [1536, 8, 768], P('dp', None, 'tensor'), may hold values from -0.4375 to 0.4375
- segment_ids: int32 [8192], P('dp'), may hold values from 0 to 15, never falling along the last dimension, each value on 1 to 2048 neighbouring positions
- routes: int32 [8192, 4], P('dp'), may hold values from 0 to 7, all different within a row
- priority: int32 [32768], P('dp'), may hold values from 0 to 2047, as said below
- cotangent: bfloat16 [8192, 1536], P(('dp', 'tensor')), may hold values from -6 to 6
Outputs:
- block_output: float32 [8192, 1536], P(('dp', 'tensor'))
- input_grad: float32 [8192, 1536], P(('dp', 'tensor'))
- gains_grad: float32 [1536, 2], P(('dp', 'tensor'))
- router_grad: float32 [1536, 8], P(('dp', 'tensor'))
- query_grad: float32 [1536, 1536], P('dp', 'tensor')
- key_grad: float32 [1536, 256], P('dp', 'tensor')
- value_grad: float32 [1536, 256], P('dp', 'tensor')
- output_weight_grad: float32 [1536, 1536], P('dp', 'tensor')
- gate_grad: float32 [1536, 8, 768], P('dp', None, 'tensor')
- up_grad: float32 [1536, 8, 768], P('dp', None, 'tensor')
- down_grad: float32 [1536, 8, 768], P('dp', None, 'tensor')
The draws below stay inside these ranges and needn't reach their ends.
Inputs may be any that keep to these rules, and one draw needn't show every extreme that they name: `segment_ids`: segment numbers never fall along the tokens; a segment covers 1 to 2048 consecutive tokens. `routes`: each token names 4 different experts. `priority`: each aligned block of 2048 entries (one group's pairs) holds every number of 0 to 2047 once.
All inputs are finite; a program needn't handle non-finite values.
Results may differ from the reference program's by a relative error of at most 0.02.
Values may be sent and summed in bfloat16 or wider, within the bound.
No kernel may reach another device: no remote copies, remote signals or barrier semaphores. Data moves between devices by JAX's collectives and lax.ppermute only.
A program may use at most 256 MiB of HBM per device.

```python
import math
import jax
import jax.numpy as jnp
import numpy as np
from jax import lax

MODEL_DIMENSION = 1536
QUERY_HEADS = 12
KEY_VALUE_HEADS = 2
HEAD_SIZE = 128
FF = 768
TOPK = 4
EXPERTS = 8
ATTEND_SPAN = 1024
QB = 512
TOK_DEV = 256
GROUP = 512
TOKEN_TOTAL = 8192
SEQ = 8192
CAP = 256
N_DP = 16
N_TENSOR = 2


def draw_priority(key, part):
    key = jax.random.fold_in(key, 7)
    span = TOK_DEV * N_TENSOR * TOPK
    group_keys = jax.random.split(key, N_DP)
    orders = jax.vmap(lambda group_key: jax.random.permutation(group_key, span))(group_keys)
    return orders.reshape(-1).astype(jnp.int32)


def shard_levels(key, extent, shards, least, high):
    def one(axis_at, shards_of):
        draws = jax.random.uniform(jax.random.fold_in(jax.random.fold_in(key, 6), axis_at), (shards_of,), jnp.float32, least / len(shards), high / len(shards))
        return jnp.repeat(jnp.exp(draws), extent[axis_at] // shards_of).reshape((-1,) + (1,) * (len(extent) - axis_at - 1))

    level = one(*shards[0])
    for cut in shards[1:]:
        level = level * one(*cut)
    return level


def different_ones(rng, rows, amount, top, lift):
    order = jax.random.permutation(jax.random.fold_in(rng, 1), amount)
    favour = order
    for power in range(3):
        favour = favour * favour // amount
    favour = favour * lift // amount
    chance = jax.random.randint(jax.random.fold_in(rng, 2), (rows, amount), 0, 4096) + favour
    sure = jax.random.permutation(jax.random.fold_in(rng, 3), rows)[jnp.arange(amount) % rows]
    chance = jnp.where(jnp.arange(rows)[:, None] == sure[None, :], 1 << 14, chance)
    score = chance * amount + jnp.arange(amount)
    return lax.top_k(score.astype(jnp.int32), top)[1].astype(jnp.int32)


def length_profile(number_of, total, reach, lean):
    weights = [(1 << 20) // math.isqrt(standing ** lean) + 1 for standing in range(2, number_of + 1)]
    surplus, given = total - reach - (number_of - 1), [1] * (number_of - 1)
    while surplus > 0:
        candidates = [i for i in range(number_of - 1) if given[i] < reach]
        whole, budget = sum([weights[i] for i in candidates]), surplus
        for i in candidates:
            more = min(reach - given[i], max(1, budget * weights[i] // whole), surplus)
            given[i] = given[i] + more
            surplus = surplus - more
    return np.array([reach] + given)


def ragged_sizes(key, amount, total, reach, skew):
    if amount == 2:
        one = jax.random.randint(key, (), max(1, total - reach), min(reach, total - 1) + 1)
        return jnp.stack([one, total - one])
    sizes = jnp.asarray(length_profile(amount, total, reach, skew), jnp.int32)
    twos = (amount - 1) // 2
    source_of, sink = sizes[1:1 + 2 * twos:2], sizes[2:2 + 2 * twos:2]
    room = jnp.minimum(source_of - 1, reach - sink)
    passed = jax.random.randint(jax.random.fold_in(key, 1), (twos,), 0, 1 << 20) % (room + 1)
    sizes = sizes.at[1:1 + 2 * twos:2].set(source_of - passed).at[2:2 + 2 * twos:2].set(sink + passed)
    return sizes[jax.random.permutation(jax.random.fold_in(key, 2), amount)]


def centred(own_key, extent, width, most, pieces=(), held_as=jnp.bfloat16):
    values = jax.random.normal(own_key, extent, jnp.float32) * width
    if len(pieces) > 0:
        values = shard_levels(own_key, extent, pieces, -0.22, 0.18) * values
    return jnp.clip(values, min=-most, max=most).astype(held_as)


def setup_inputs(seed: int = 0) -> dict:
    splits = jax.random.split(jax.random.key(seed), 15)
    block_input = centred(splits[0], (TOKEN_TOTAL, MODEL_DIMENSION), 1.0, 6.0, ((0, 32),))
    norm_gains = jnp.clip(1.0 + 0.18 * jax.random.normal(splits[1], (MODEL_DIMENSION, 2), jnp.float32), 0.1, 1.9)
    router_weight = centred(splits[2], (MODEL_DIMENSION, EXPERTS), (4 * MODEL_DIMENSION) ** -0.5, 0.078125)
    query_matrix = centred(splits[3], (MODEL_DIMENSION, QUERY_HEADS * HEAD_SIZE), MODEL_DIMENSION ** -0.5, 0.15625, ((0, 16), (1, 2)))
    key_matrix = centred(splits[4], (MODEL_DIMENSION, KEY_VALUE_HEADS * HEAD_SIZE), MODEL_DIMENSION ** -0.5, 0.15625, ((0, 16), (1, 2)))
    value_matrix = centred(splits[5], (MODEL_DIMENSION, KEY_VALUE_HEADS * HEAD_SIZE), MODEL_DIMENSION ** -0.5, 0.15625, ((0, 16), (1, 2)))
    output_weight = centred(splits[6], (MODEL_DIMENSION, QUERY_HEADS * HEAD_SIZE), (QUERY_HEADS * HEAD_SIZE // 32) ** -0.5, 0.875, ((0, 16), (1, 2)))
    gate_weight = centred(splits[7], (MODEL_DIMENSION, EXPERTS, FF), MODEL_DIMENSION ** -0.5, 0.15625, ((0, 16), (2, 2)))
    up_weight = centred(splits[8], (MODEL_DIMENSION, EXPERTS, FF), MODEL_DIMENSION ** -0.5, 0.15625, ((0, 16), (2, 2)))
    down_weight = centred(splits[9], (MODEL_DIMENSION, EXPERTS, FF), (FF // 4) ** -0.5, 0.4375, ((0, 16), (2, 2)))
    segment_ids = jnp.searchsorted(jnp.cumsum(ragged_sizes(splits[10], TOKEN_TOTAL * 2 // ATTEND_SPAN, TOKEN_TOTAL, 2 * ATTEND_SPAN, 2)), jnp.arange(TOKEN_TOTAL), side="right").astype(jnp.int32)
    routes = different_ones(splits[11], TOKEN_TOTAL, EXPERTS, TOPK, 4096)
    priority = draw_priority(jax.random.fold_in(splits[14], 71), 0)
    cotangent = centred(splits[13], (TOKEN_TOTAL, MODEL_DIMENSION), 1.0, 6.0, ((0, 32),))
    return dict(block_input=block_input, norm_gains=norm_gains, router_weight=router_weight, query_matrix=query_matrix, key_matrix=key_matrix, value_matrix=value_matrix, output_weight=output_weight, gate_weight=gate_weight, up_weight=up_weight, down_weight=down_weight, segment_ids=segment_ids, routes=routes, priority=priority, cotangent=cotangent)


FULL_PRECISION = lax.Precision.HIGHEST
EPSILON = 1e-06
ROPE_BASE = 10000.0

@jax.custom_vjp
def low(v):
    return lax.optimization_barrier(v.astype(jnp.bfloat16)).astype(jnp.float32)

@jax.custom_vjp
def low_back(v):
    return v

def low_keep(v):
    return (low(v), None)

def low_pass(kept, grad):
    return (grad,)

def back_keep(v):
    return (v, None)

def back_low(kept, grad):
    return (low(grad),)
low.defvjp(low_keep, low_pass)
low_back.defvjp(back_keep, back_low)

def rotary_tables(position):
    halfway = HEAD_SIZE // 2
    inverse = jnp.exp(jnp.arange(halfway, dtype=jnp.float32) * (-2.0 * math.log(ROPE_BASE) / HEAD_SIZE))
    angles = position.astype(jnp.float32)[:, None] * inverse[None, :]
    return (jnp.cos(angles), jnp.sin(angles))

def rotate(value_rows, cosine, sine):
    halfway = value_rows.shape[-1] // 2
    first_half = value_rows[..., :halfway]
    second_half = value_rows[..., halfway:]
    return jnp.concatenate([first_half * cosine - second_half * sine, second_half * cosine + first_half * sine], axis=-1)

def rms_norm(value_rows, gain):
    factor = lax.rsqrt(lax.optimization_barrier(jnp.mean(value_rows * value_rows, axis=-1, keepdims=True)) + EPSILON)
    return value_rows * factor * gain

def place_pairs(routes, priority):
    groups = TOKEN_TOTAL // GROUP
    pair_expert = routes.reshape(groups, GROUP * TOPK)
    ranked = priority.reshape(groups, GROUP * TOPK)
    in_order = jnp.take_along_axis(pair_expert, ranked, axis=1)
    one_hot = (in_order[:, :, None] == jnp.arange(EXPERTS, dtype=jnp.int32)[None, None, :]).astype(jnp.int32)
    earlier = jnp.cumsum(one_hot, axis=1) - one_hot
    slot_in_order = lax.optimization_barrier(jnp.sum(earlier * one_hot, axis=2))
    group_rows = jnp.arange(groups, dtype=jnp.int32)[:, None]
    slot_number = jnp.zeros_like(ranked).at[group_rows, ranked].set(slot_in_order)
    kept_pair = slot_number < CAP
    slot_index = jnp.where(kept_pair, pair_expert * CAP + slot_number, EXPERTS * CAP).astype(jnp.int32)
    pair_token = jnp.broadcast_to(jnp.arange(GROUP * TOPK, dtype=jnp.int32) // TOPK, slot_index.shape)
    slot_token = jnp.full((groups, EXPERTS * CAP + 1), GROUP, jnp.int32).at[group_rows, slot_index].set(pair_token)
    return (slot_index.reshape(groups, GROUP, TOPK), kept_pair.reshape(TOKEN_TOTAL, TOPK), slot_token[:, :EXPERTS * CAP])

def attend(queries, key_rows, value_rows, segment_ids):
    score_scale = 1.0 / math.sqrt(HEAD_SIZE)
    span = ATTEND_SPAN + QB
    key_padded_rows = jnp.concatenate([jnp.zeros((ATTEND_SPAN, KEY_VALUE_HEADS, HEAD_SIZE), jnp.float32), key_rows], axis=0)
    value_padded_rows = jnp.concatenate([jnp.zeros((ATTEND_SPAN, KEY_VALUE_HEADS, HEAD_SIZE), jnp.float32), value_rows], axis=0)
    segment_pad = jnp.concatenate([jnp.full((ATTEND_SPAN,), -1, jnp.int32), segment_ids])

    def one_block(start):
        query_block = lax.dynamic_slice_in_dim(queries, start, QB, 0)
        key_block = lax.dynamic_slice_in_dim(key_padded_rows, start, span, 0)
        value_block = lax.dynamic_slice_in_dim(value_padded_rows, start, span, 0)
        query_pos = start + jnp.arange(QB, dtype=jnp.int32)
        key_pos = start - ATTEND_SPAN + jnp.arange(span, dtype=jnp.int32)
        query_seg = lax.dynamic_slice_in_dim(segment_ids, start, QB, 0)
        key_seg = lax.dynamic_slice_in_dim(segment_pad, start, span, 0)
        distance = query_pos[:, None] - key_pos[None, :]
        allowed = (key_pos[None, :] >= 0) & (distance >= 0) & (distance < ATTEND_SPAN)
        allowed = allowed & (query_pos[:, None] // SEQ == key_pos[None, :] // SEQ)
        allowed = allowed & (query_seg[:, None] == key_seg[None, :])
        scores = low_back(jnp.einsum('qgjd,kgd->gjqk', query_block, key_block, precision=FULL_PRECISION) * score_scale)
        scores = jnp.where(allowed[None, None], scores, -1e+30)
        row_top = lax.optimization_barrier(jnp.max(scores, axis=-1, keepdims=True))
        weights = jnp.exp(scores - row_top)
        probability = low(weights / lax.optimization_barrier(jnp.sum(weights, axis=-1, keepdims=True)))
        return jnp.einsum('gjqk,kgd->qgjd', probability, value_block, precision=FULL_PRECISION)
    starts = jnp.arange(TOKEN_TOTAL // QB, dtype=jnp.int32) * QB
    blocks = lax.map(jax.checkpoint(one_block), starts)
    return blocks.reshape(TOKEN_TOTAL, QUERY_HEADS * HEAD_SIZE)

def forward(block_input, norm_gains, router_weight, query_matrix, key_matrix, value_matrix, output_weight, gate_weight, up_weight, down_weight, segment_ids, routes, slot_index, kept_pair, slot_token):
    positions = jnp.arange(TOKEN_TOTAL, dtype=jnp.int32) % SEQ
    cosine, sine = rotary_tables(positions)
    normalized_input = low(rms_norm(block_input, norm_gains[:, 0]))
    query_before_rope = low_back(jnp.dot(normalized_input, query_matrix, precision=FULL_PRECISION)).reshape(TOKEN_TOTAL, KEY_VALUE_HEADS, QUERY_HEADS // KEY_VALUE_HEADS, HEAD_SIZE)
    key_before_rope = low_back(jnp.dot(normalized_input, key_matrix, precision=FULL_PRECISION)).reshape(TOKEN_TOTAL, KEY_VALUE_HEADS, HEAD_SIZE)
    value_rows = low(low_back(jnp.dot(normalized_input, value_matrix, precision=FULL_PRECISION))).reshape(TOKEN_TOTAL, KEY_VALUE_HEADS, HEAD_SIZE)
    queries = low(rotate(query_before_rope, cosine[:, None, None, :], sine[:, None, None, :]))
    key_rows = low(rotate(key_before_rope, cosine[:, None, :], sine[:, None, :]))
    heads = low(low_back(attend(queries, key_rows, value_rows, segment_ids)))
    attn_out = low_back(jnp.dot(heads, output_weight.T, precision=FULL_PRECISION))
    hidden_state = block_input + attn_out
    normed_mid = low(rms_norm(hidden_state, norm_gains[:, 1]))
    logits = jnp.dot(normed_mid, router_weight, precision=FULL_PRECISION)
    picked_logits = jnp.take_along_axis(logits, routes, axis=1)
    gates = jax.nn.softmax(picked_logits, axis=-1)
    coefficient = jnp.where(kept_pair, gates, 0.0)
    groups = TOKEN_TOTAL // GROUP

    def expert_group(inputs):
        group_rows, group_coeff, group_index, group_token = inputs
        padded = jnp.concatenate([group_rows, jnp.zeros((1, MODEL_DIMENSION), group_rows.dtype)], axis=0)
        expert_in = padded[group_token].reshape(EXPERTS, CAP, MODEL_DIMENSION)
        gate_pre = low_back(jnp.einsum('ecd,def->ecf', expert_in, gate_weight, precision=FULL_PRECISION))
        up_pre = low_back(jnp.einsum('ecd,def->ecf', expert_in, up_weight, precision=FULL_PRECISION))
        expert_hidden = low(jax.nn.silu(gate_pre) * up_pre)
        expert_out = low_back(jnp.einsum('ecf,def->ecd', expert_hidden, down_weight, precision=FULL_PRECISION))
        expert_out = jnp.concatenate([expert_out.reshape(EXPERTS * CAP, MODEL_DIMENSION), jnp.zeros((1, MODEL_DIMENSION), expert_out.dtype)], axis=0)
        gathered = expert_out[group_index]
        return lax.optimization_barrier(jnp.sum(group_coeff[..., None] * gathered, axis=1))
    moe_groups = lax.map(jax.checkpoint(expert_group), (normed_mid.reshape(groups, GROUP, MODEL_DIMENSION), coefficient.reshape(groups, GROUP, TOPK), slot_index, slot_token))
    moe_out = low_back(moe_groups.reshape(TOKEN_TOTAL, MODEL_DIMENSION))
    return hidden_state + moe_out

def widen(array):
    return array.astype(jnp.float32)

def reference(block_input, norm_gains, router_weight, query_matrix, key_matrix, value_matrix, output_weight, gate_weight, up_weight, down_weight, segment_ids, routes, priority, cotangent):
    slot_index, kept_pair, slot_token = place_pairs(routes, priority)

    def layer(input_wide, gains_wide, router_wide, query_wide, key_wide, value_wide, output_wide, gate_wide, up_wide, down_wide):
        return forward(input_wide, gains_wide, router_wide, query_wide, key_wide, value_wide, output_wide, gate_wide, up_wide, down_wide, segment_ids, routes, slot_index, kept_pair, slot_token)
    block_output, pull_back = jax.vjp(layer, widen(block_input), widen(norm_gains), widen(router_weight), widen(query_matrix), widen(key_matrix), widen(value_matrix), widen(output_weight), widen(gate_weight), widen(up_weight), widen(down_weight))
    gradients = pull_back(widen(cotangent))
    input_grad, gains_grad, router_grad, query_grad, key_grad, value_grad, output_weight_grad, gate_grad, up_grad, down_grad = gradients
    return (block_output, input_grad, gains_grad, router_grad, query_grad, key_grad, value_grad, output_weight_grad, gate_grad, up_grad, down_grad)
```

```python
import math

import jax
import jax.numpy as jnp
from jax import lax
from jax.sharding import Mesh
from jax.sharding import PartitionSpec as P

HEAD_SIZE = 128
TOPK = 4
EXPERTS = 8
ATTEND_SPAN = 1024
SEQ_MOST = 16384
EPSILON = 1e-06
ROPE_BASE = 10000.0
FULL_PRECISION = lax.Precision.HIGHEST
BF16 = jnp.bfloat16
F32 = jnp.float32

DP = ("outer", "x", "core")
PLANE = ("x", "core", "tensor")
ALL = ("outer", "x", "core", "tensor")


def shift_all(x, by):
    length = lax.axis_size(ALL)
    pairs = [(i, i + by) for i in range(length) if 0 <= i + by < length]
    return lax.ppermute(x, ALL, pairs)


def rotary_tables(position):
    halfway = HEAD_SIZE // 2
    inverse = jnp.exp(
        jnp.arange(halfway, dtype=F32) * (-2.0 * math.log(ROPE_BASE) / HEAD_SIZE)
    )
    angles = position.astype(F32)[:, None] * inverse[None, :]
    return (jnp.cos(angles), jnp.sin(angles))


def rotate(value_rows, cosine, sine):
    halfway = value_rows.shape[-1] // 2
    first_half = value_rows[..., :halfway]
    second_half = value_rows[..., halfway:]
    return jnp.concatenate(
        [first_half * cosine - second_half * sine, second_half * cosine + first_half * sine],
        axis=-1,
    )


def norm_factor(value_rows):
    return lax.rsqrt(jnp.mean(value_rows * value_rows, axis=-1, keepdims=True) + EPSILON)


def norm_back(value_rows, factor, gain, upstream):
    weighted = upstream * gain
    gain_part = jnp.sum(upstream * value_rows * factor, axis=0)
    input_part = factor * weighted - value_rows * (factor * factor * factor) * jnp.mean(
        weighted * value_rows, axis=-1, keepdims=True
    )
    return (input_part, gain_part)


def dot(a, b, dims):
    return lax.dot_general(a, b, (dims, ((), ())), preferred_element_type=F32)


def on_device(
    block_input,
    norm_gains,
    router_weight,
    query_matrix,
    key_matrix,
    value_matrix,
    output_weight,
    gate_weight,
    up_weight,
    down_weight,
    segment_ids,
    routes,
    priority,
    cotangent,
):
    tensor_index = lax.axis_index("tensor")
    own_rows, width = block_input.shape
    group_rows = segment_ids.shape[0]
    halves = lax.axis_size("tensor")
    outer = lax.axis_size("outer")
    groups = lax.axis_size("x") * lax.axis_size("core")
    plane = groups * halves
    shard_rows = query_matrix.shape[0]
    dp_size = outer * groups
    seq_len = min(SEQ_MOST, group_rows * dp_size)
    own_start = lax.axis_index(ALL) * own_rows
    capacity = group_rows * TOPK // EXPERTS
    score_scale = 1.0 / math.sqrt(HEAD_SIZE)
    reach = ATTEND_SPAN // own_rows
    group_heads = query_matrix.shape[1] // HEAD_SIZE
    half_ff = gate_weight.shape[2]
    ff = half_ff * halves

    qkv_shard = jnp.concatenate([query_matrix, key_matrix, value_matrix], axis=1)
    qkv_shard = lax.all_gather(qkv_shard, "tensor", axis=1, tiled=True)
    qkv_full = lax.all_gather(qkv_shard, DP, axis=0, tiled=True)
    output_shard = lax.all_gather(output_weight, "tensor", axis=1, tiled=True)
    output_full = lax.all_gather(output_shard, DP, axis=0, tiled=True)

    expert_shard = jnp.stack([gate_weight, up_weight, down_weight])
    expert_shard = jnp.transpose(expert_shard, (2, 0, 1, 3))
    expert_shard = lax.all_to_all(expert_shard, PLANE, 0, 0, tiled=True)
    expert_shard = expert_shard.reshape(groups, halves, 3, shard_rows, half_ff)
    expert_shard = jnp.transpose(expert_shard, (2, 0, 3, 1, 4)).reshape(
        3, groups * shard_rows, ff
    )
    gate_full = lax.all_gather(expert_shard[0], "outer", axis=0, tiled=True)
    up_full = lax.all_gather(expert_shard[1], "outer", axis=0, tiled=True)
    down_full = lax.all_gather(expert_shard[2], "outer", axis=0, tiled=True)

    pair_count = group_rows * TOPK
    rank = (
        jnp.zeros((pair_count,), jnp.int32)
        .at[priority]
        .set(jnp.arange(pair_count, dtype=jnp.int32))
        .reshape(group_rows, TOPK)
    )
    expert_ids = jnp.arange(EXPERTS, dtype=jnp.int32)
    named = routes[:, :, None] == expert_ids[None, None, :]
    ranked = jnp.sum(jnp.where(named, rank[:, :, None] + 1, 0), axis=1)
    ranked = jnp.where(ranked > 0, ranked, pair_count + 1)
    ranked_all = lax.all_gather(ranked, ("x", "core"), axis=0, tiled=False)
    routed_all = ranked_all <= pair_count
    expert = lax.axis_index(PLANE)
    own_column = expert_ids == expert
    rank_own = jnp.sum(jnp.where(own_column, ranked_all, 0), axis=-1)
    slot_own = jnp.sum(
        (rank_own[:, None, :] < rank_own[:, :, None]).astype(jnp.int32), axis=-1
    )
    slot_own = jnp.where(rank_own <= pair_count, slot_own, capacity)
    place = (
        slot_own[:, None, :] == jnp.arange(capacity, dtype=jnp.int32)[None, :, None]
    ).astype(BF16)

    cotangent_all = lax.all_gather(cotangent, PLANE, axis=0, tiled=True).reshape(
        groups, group_rows, width
    )

    input_wide = block_input.astype(F32)
    first_gain = norm_gains[:, 0]
    second_gain = norm_gains[:, 1]
    first_factor = norm_factor(input_wide)
    normed_in = (input_wide * first_factor * first_gain).astype(BF16)
    positions = own_start + jnp.arange(own_rows, dtype=jnp.int32)
    cosine, sine = rotary_tables(positions % seq_len)
    cosine_heads, sine_heads = cosine[:, None, None, :], sine[:, None, None, :]
    qkv = dot(normed_in, qkv_full, ((1,), (0,))).reshape(
        own_rows, halves, group_heads + 2, HEAD_SIZE
    )
    queries = rotate(qkv[:, :, :group_heads], cosine_heads, sine_heads).astype(BF16)
    keys_own = rotate(qkv[:, :, group_heads : group_heads + 1], cosine_heads, sine_heads)
    key_value_own = jnp.concatenate([keys_own, qkv[:, :, group_heads + 1 :]], axis=2).astype(BF16)
    pieces = [shift_all(key_value_own, k) for k in range(reach, 0, -1)] + [key_value_own]
    key_value = jnp.concatenate(pieces, axis=0)
    key_ext, value_ext = key_value[:, :, 0], key_value[:, :, 1]
    earlier_groups = (ATTEND_SPAN + group_rows - 1) // group_rows
    group_pairs = [
        [(i, i + k) for i in range(dp_size - k)] for k in range(earlier_groups, 0, -1)
    ]
    segment_near = jnp.concatenate(
        [lax.ppermute(segment_ids, DP, pairs) for pairs in group_pairs] + [segment_ids]
    )
    span = ATTEND_SPAN + own_rows
    segment_ext = lax.dynamic_slice_in_dim(segment_near, tensor_index * own_rows, span)
    segment_own = segment_ext[ATTEND_SPAN:]
    key_pos = own_start - ATTEND_SPAN + jnp.arange(span, dtype=jnp.int32)
    distance = positions[:, None] - key_pos[None, :]
    allowed = (key_pos[None, :] >= 0) & (distance >= 0) & (distance < ATTEND_SPAN)
    allowed = allowed & (positions[:, None] // seq_len == key_pos[None, :] // seq_len)
    allowed = allowed & (segment_own[:, None] == segment_ext[None, :])

    def attention_scores():
        raw = jnp.einsum("qgjd,kgd->gjqk", queries, key_ext, preferred_element_type=F32)
        return jnp.where(allowed[None, None], raw * score_scale, -1e30)

    scores = attention_scores()
    row_top = jnp.max(scores, axis=-1, keepdims=True)
    weights = jnp.exp(scores - row_top)
    row_total = jnp.sum(weights, axis=-1, keepdims=True)
    probability = (weights / row_total).astype(BF16)
    heads_low = (
        jnp.einsum("gjqk,kgd->qgjd", probability, value_ext, preferred_element_type=F32)
        .astype(BF16)
        .reshape(own_rows, -1)
    )
    log_total = row_top + jnp.log(row_total)
    hidden_state = input_wide + dot(heads_low, output_full, ((1,), (1,)))
    second_factor = norm_factor(hidden_state)
    normed_mid_own = (hidden_state * second_factor * second_gain).astype(BF16)

    normed_mid = lax.all_gather(normed_mid_own, PLANE, axis=0, tiled=True)
    logits = dot(normed_mid, router_weight, ((1,), (0,))).reshape(groups, group_rows, EXPERTS)
    logits = jnp.where(routed_all, logits, -1e30)
    gate_weights = jnp.where(
        routed_all, jnp.exp(logits - jnp.max(logits, axis=-1, keepdims=True)), 0.0
    )
    gates = gate_weights / jnp.sum(gate_weights, axis=-1, keepdims=True)
    gate_own = jnp.sum(jnp.where(own_column, gates, 0.0), axis=-1)
    normed_groups = normed_mid.reshape(groups, group_rows, width)
    expert_in = (
        jnp.einsum("gct,gtd->gcd", place, normed_groups, preferred_element_type=F32)
        .astype(BF16)
        .reshape(groups * capacity, width)
    )
    cotangent_slots = jnp.einsum(
        "gct,gtd->gcd", place, cotangent_all, preferred_element_type=F32
    ).reshape(groups * capacity, width)
    coefficient = jnp.sum(place.astype(F32) * gate_own[:, None, :], axis=-1).reshape(-1, 1)
    gate_pre = dot(expert_in, gate_full, ((1,), (0,)))
    up_pre = dot(expert_in, up_full, ((1,), (0,)))
    sigmoid_gate = jax.nn.sigmoid(gate_pre)
    silu_gate = gate_pre * sigmoid_gate
    expert_hidden = (silu_gate * up_pre).astype(BF16)
    expert_out = dot(expert_hidden, down_full, ((1,), (1,)))
    grad_expert_out = (coefficient * cotangent_slots).astype(BF16)
    grad_hidden = dot(grad_expert_out, down_full, ((1,), (0,)))
    grad_up = (grad_hidden * silu_gate).astype(BF16)
    grad_gate = (
        grad_hidden * up_pre * sigmoid_gate * (1.0 + gate_pre * (1.0 - sigmoid_gate))
    ).astype(BF16)
    grad_expert_in = dot(grad_gate, gate_full, ((1,), (1,))) + dot(grad_up, up_full, ((1,), (1,)))

    def to_tokens(rows):
        return jnp.einsum(
            "gct,gcd->gtd",
            place,
            rows.astype(BF16).reshape(groups, capacity, width),
            preferred_element_type=F32,
        )

    grad_gate_slots = jnp.sum(cotangent_slots * expert_out, axis=-1).reshape(groups, capacity)
    grad_gate_tokens = jnp.sum(place.astype(F32) * grad_gate_slots[:, :, None], axis=1)
    grad_logits = (grad_gate_tokens * gate_own)[:, :, None] * (
        own_column.astype(F32)[None, None, :] - gates
    )
    grad_logits = grad_logits.reshape(groups * group_rows, EXPERTS)
    grad_mid_part = to_tokens(grad_expert_in).reshape(-1, width) + jnp.dot(
        grad_logits, router_weight.astype(F32).T, precision=FULL_PRECISION
    )
    router_part = jnp.dot(normed_mid.astype(F32).T, grad_logits, precision=FULL_PRECISION)
    grad_mid = lax.psum_scatter(
        grad_mid_part.astype(BF16), PLANE, scatter_dimension=0, tiled=True
    ).astype(F32)
    moe_part = to_tokens(coefficient * expert_out).reshape(-1, width)
    moe_own = lax.psum_scatter(
        moe_part.astype(BF16), PLANE, scatter_dimension=0, tiled=True
    ).astype(F32)
    block_output = hidden_state + moe_own

    down_part = dot(grad_expert_out, expert_hidden, ((0,), (0,))).astype(BF16)
    gate_part = dot(expert_in, grad_gate, ((0,), (0,))).astype(BF16)
    up_part = dot(expert_in, grad_up, ((0,), (0,))).astype(BF16)
    expert_sums = [
        lax.psum_scatter(part, "outer", scatter_dimension=0, tiled=True)
        for part in (gate_part, up_part, down_part)
    ]
    expert_sum = jnp.stack(expert_sums).reshape(3, groups, shard_rows, halves, half_ff)
    expert_sum = jnp.transpose(expert_sum, (1, 3, 0, 2, 4)).reshape(
        plane, 3, shard_rows, half_ff
    )
    expert_sum = lax.all_to_all(expert_sum, PLANE, 0, 0, tiled=True)
    expert_grads = jnp.transpose(expert_sum, (1, 2, 0, 3)).astype(F32)
    gate_grad, up_grad, down_grad = expert_grads[0], expert_grads[1], expert_grads[2]

    norm_input_part, second_gain_part = norm_back(
        hidden_state, second_factor, second_gain, grad_mid
    )
    grad_state = cotangent.astype(F32) + norm_input_part
    grad_attn = grad_state.astype(BF16)
    grad_heads = dot(grad_attn, output_full, ((1,), (0,))).astype(BF16)
    output_part = dot(grad_attn, heads_low, ((0,), (0,)))
    small_part = jnp.concatenate([router_part, second_gain_part[:, None]], axis=1)
    small_part = jnp.pad(small_part, ((0, 0), (0, HEAD_SIZE - small_part.shape[1])))
    output_sum = lax.psum_scatter(
        jnp.concatenate([output_part, small_part], axis=1).astype(BF16),
        DP,
        scatter_dimension=0,
        tiled=True,
    )
    grad_heads = grad_heads.reshape(queries.shape)
    scores = attention_scores()
    probability = jnp.exp(scores - log_total)
    grad_prob = jnp.einsum("qgjd,kgd->gjqk", grad_heads, value_ext, preferred_element_type=F32)
    row_dot = jnp.sum(probability * grad_prob, axis=-1, keepdims=True)
    grad_scores = (probability * (grad_prob - row_dot)).astype(BF16)
    grad_queries = (
        jnp.einsum("gjqk,kgd->qgjd", grad_scores, key_ext, preferred_element_type=F32)
        * score_scale
    )
    grad_keys = (
        jnp.einsum("gjqk,qgjd->kgd", grad_scores, queries, preferred_element_type=F32)
        * score_scale
    )
    grad_values = jnp.einsum(
        "gjqk,qgjd->kgd", probability.astype(BF16), grad_heads, preferred_element_type=F32
    )
    grad_key_value = jnp.stack([grad_keys, grad_values], axis=2)
    grad_own = grad_key_value[ATTEND_SPAN:]
    for k in range(1, reach + 1):
        first_row = ATTEND_SPAN - k * own_rows
        piece = grad_key_value[first_row : first_row + own_rows].astype(BF16)
        grad_own = grad_own + shift_all(piece, -k).astype(F32)
    grad_qkv = jnp.concatenate(
        [
            rotate(
                jnp.concatenate([grad_queries, grad_own[:, :, :1]], axis=2),
                cosine_heads,
                -sine_heads,
            ),
            grad_own[:, :, 1:],
        ],
        axis=2,
    )
    grad_qkv = grad_qkv.astype(BF16).reshape(own_rows, -1)
    qkv_part = dot(normed_in, grad_qkv, ((0,), (0,)))
    grad_in = dot(grad_qkv, qkv_full, ((1,), (1,)))
    first_input_part, first_gain_part = norm_back(input_wide, first_factor, first_gain, grad_in)
    input_grad = grad_state + first_input_part
    first_part = jnp.pad(first_gain_part[:, None], ((0, 0), (0, HEAD_SIZE - 1)))
    qkv_sum = lax.psum_scatter(
        jnp.concatenate([qkv_part, first_part], axis=1).astype(BF16),
        DP,
        scatter_dimension=0,
        tiled=True,
    )

    def pair_sum(sums, pair_columns):
        half = pair_columns // 2
        columns, small = sums[:, :pair_columns], sums[:, pair_columns:]
        half_rows = shard_rows // 2
        kept = lax.dynamic_slice_in_dim(columns, tensor_index * half, half, 1)
        sent = lax.dynamic_slice_in_dim(columns, (1 - tensor_index) * half, half, 1)
        small_kept = lax.dynamic_slice_in_dim(small, tensor_index * half_rows, half_rows, 0)
        small_sent = lax.dynamic_slice_in_dim(small, (1 - tensor_index) * half_rows, half_rows, 0)
        got, small_got = lax.ppermute((sent, small_sent), "tensor", [(0, 1), (1, 0)])
        return (
            kept.astype(F32) + got.astype(F32),
            small_kept.astype(F32) + small_got.astype(F32),
        )

    output_weight_grad, small_sum = pair_sum(output_sum, output_part.shape[1])
    router_grad = small_sum[:, :EXPERTS]
    qkv_grad, first_sum = pair_sum(qkv_sum, qkv_part.shape[1])
    gains_grad = jnp.concatenate([first_sum[:, :1], small_sum[:, EXPERTS : EXPERTS + 1]], axis=1)
    query_columns = group_heads * HEAD_SIZE
    query_grad = qkv_grad[:, :query_columns]
    key_grad = qkv_grad[:, query_columns : query_columns + HEAD_SIZE]
    value_grad = qkv_grad[:, query_columns + HEAD_SIZE :]
    return (
        block_output,
        input_grad,
        gains_grad,
        router_grad,
        query_grad,
        key_grad,
        value_grad,
        output_weight_grad,
        gate_grad,
        up_grad,
        down_grad,
    )


def solution(mesh):
    dp_size, tensor_size = mesh.shape["dp"], mesh.shape["tensor"]
    split = Mesh(mesh.devices.reshape(dp_size // 4, 2, 2, tensor_size), ALL)
    return jax.shard_map(
        on_device,
        mesh=split,
        in_specs=(
            P(ALL, None),
            P(),
            P(),
            P(DP, "tensor"),
            P(DP, "tensor"),
            P(DP, "tensor"),
            P(DP, "tensor"),
            P(DP, None, "tensor"),
            P(DP, None, "tensor"),
            P(DP, None, "tensor"),
            P(DP),
            P(DP, None),
            P(DP),
            P(ALL, None),
        ),
        out_specs=(
            P(ALL, None),
            P(ALL, None),
            P(ALL, None),
            P(ALL, None),
            P(DP, "tensor"),
            P(DP, "tensor"),
            P(DP, "tensor"),
            P(DP, "tensor"),
            P(DP, None, "tensor"),
            P(DP, None, "tensor"),
            P(DP, None, "tensor"),
        ),
        check_vma=False,
    )
```

```python
import math

import jax
import jax.numpy as jnp
from jax import lax
from jax.sharding import Mesh
from jax.sharding import PartitionSpec as P

HEAD_SIZE = 128
TOPK = 4
EXPERTS = 8
ATTEND_SPAN = 1024
SEQ_MOST = 16384
EPSILON = 1e-06
ROPE_BASE = 10000.0
FULL_PRECISION = lax.Precision.HIGHEST
BF16 = jnp.bfloat16
F32 = jnp.float32

DP = ("outer", "x", "core")
PLANE = ("x", "core", "tensor")
ALL = ("outer", "x", "core", "tensor")


def shift_all(x, by):
    length = lax.axis_size(ALL)
    pairs = [(i, i + by) for i in range(length) if 0 <= i + by < length]
    return lax.ppermute(x, ALL, pairs)


def swap(x, axis):
    length = lax.axis_size(axis)
    return lax.ppermute(x, axis, [(i, length - 1 - i) for i in range(length)])


def plane_gather(own):
    near = jnp.stack([own, swap(own, "tensor"), swap(own, "x"), swap(own, ("x", "tensor"))])
    far = swap(near, "core")
    shape = (2, 2) + own.shape
    return near.reshape(shape), far.reshape(shape)


def plane_scatter(near, far):
    total = (near.astype(F32) + swap(far, "core").astype(F32)).astype(BF16)
    parts = [
        total[0, 0],
        swap(total[0, 1], "tensor"),
        swap(total[1, 0], "x"),
        swap(total[1, 1], ("x", "tensor")),
    ]
    return sum(part.astype(F32) for part in parts)


def by_distance(x, axis_name, axis):
    return jnp.where(lax.axis_index(axis_name) == 1, jnp.flip(x, axis), x)


def next_outer(x):
    length = lax.axis_size("outer")
    return lax.ppermute(x, "outer", [(i, (i + 1) % length) for i in range(length)])


def outer_gather(shard):
    length, here = lax.axis_size("outer"), lax.axis_index("outer")
    count, rows, columns = shard.shape
    full = [jnp.zeros((length * rows, columns), shard.dtype) for _ in range(count)]
    for step in range(length):
        start = ((here - step) % length) * rows
        full = [
            lax.dynamic_update_slice_in_dim(full[i], shard[i], start, 0) for i in range(count)
        ]
        if step < length - 1:
            shard = next_outer(shard)
    return full


def outer_scatter(parts):
    length, here = lax.axis_size("outer"), lax.axis_index("outer")
    rows = parts[0].shape[0] // length

    def block(step):
        start = ((here - 1 - step) % length) * rows
        return jnp.stack([lax.dynamic_slice_in_dim(part, start, rows, 0) for part in parts])

    total = block(0)
    for step in range(1, length):
        got = next_outer(total)
        total = (got.astype(F32) + block(step).astype(F32)).astype(BF16)
    return total


def rotary_tables(position):
    halfway = HEAD_SIZE // 2
    inverse = jnp.exp(
        jnp.arange(halfway, dtype=F32) * (-2.0 * math.log(ROPE_BASE) / HEAD_SIZE)
    )
    angles = position.astype(F32)[:, None] * inverse[None, :]
    return (jnp.cos(angles), jnp.sin(angles))


def rotate(value_rows, cosine, sine):
    halfway = value_rows.shape[-1] // 2
    first_half = value_rows[..., :halfway]
    second_half = value_rows[..., halfway:]
    return jnp.concatenate(
        [first_half * cosine - second_half * sine, second_half * cosine + first_half * sine],
        axis=-1,
    )


def norm_factor(value_rows):
    return lax.rsqrt(jnp.mean(value_rows * value_rows, axis=-1, keepdims=True) + EPSILON)


def norm_back(value_rows, factor, gain, upstream):
    weighted = upstream * gain
    gain_part = jnp.sum(upstream * value_rows * factor, axis=0)
    input_part = factor * weighted - value_rows * (factor * factor * factor) * jnp.mean(
        weighted * value_rows, axis=-1, keepdims=True
    )
    return (input_part, gain_part)


def dot(a, b, dims):
    return lax.dot_general(a, b, (dims, ((), ())), preferred_element_type=F32)


def on_device(
    block_input,
    norm_gains,
    router_weight,
    query_matrix,
    key_matrix,
    value_matrix,
    output_weight,
    gate_weight,
    up_weight,
    down_weight,
    segment_ids,
    routes,
    priority,
    cotangent,
):
    tensor_index = lax.axis_index("tensor")
    own_rows, width = block_input.shape
    group_rows = segment_ids.shape[0]
    halves = lax.axis_size("tensor")
    outer = lax.axis_size("outer")
    groups = lax.axis_size("x") * lax.axis_size("core")
    plane = groups * halves
    shard_rows = query_matrix.shape[0]
    dp_size = outer * groups
    seq_len = min(SEQ_MOST, group_rows * dp_size)
    own_start = lax.axis_index(ALL) * own_rows
    capacity = group_rows * TOPK // EXPERTS
    score_scale = 1.0 / math.sqrt(HEAD_SIZE)
    reach = ATTEND_SPAN // own_rows
    group_heads = query_matrix.shape[1] // HEAD_SIZE
    half_ff = gate_weight.shape[2]
    ff = half_ff * halves

    qkv_shard = jnp.concatenate([query_matrix, key_matrix, value_matrix], axis=1)
    def both_halves(shard):
        other = swap(shard, "tensor")
        first = tensor_index == 0
        return jnp.concatenate(
            [jnp.where(first, shard, other), jnp.where(first, other, shard)], axis=1
        )

    qkv_shard = both_halves(qkv_shard)
    qkv_full = lax.all_gather(qkv_shard, DP, axis=0, tiled=True)
    qkv_shard, output_weight, gate_weight, up_weight, down_weight = lax.optimization_barrier(
        (qkv_shard, output_weight, gate_weight, up_weight, down_weight)
    )
    output_full = lax.all_gather(both_halves(output_weight), DP, axis=0, tiled=True)

    expert_shard = jnp.stack([gate_weight, up_weight, down_weight])
    expert_shard = jnp.transpose(expert_shard, (2, 0, 1, 3))
    expert_shard = lax.all_to_all(expert_shard, PLANE, 0, 0, tiled=True)
    expert_shard = expert_shard.reshape(groups, halves, 3, shard_rows, half_ff)
    expert_shard = jnp.transpose(expert_shard, (2, 0, 3, 1, 4)).reshape(
        3, groups * shard_rows, ff
    )
    gate_full, up_full, down_full = outer_gather(expert_shard)

    pair_count = group_rows * TOPK
    rank = (
        jnp.zeros((pair_count,), jnp.int32)
        .at[priority]
        .set(jnp.arange(pair_count, dtype=jnp.int32))
        .reshape(group_rows, TOPK)
    )
    expert_ids = jnp.arange(EXPERTS, dtype=jnp.int32)
    named = routes[:, :, None] == expert_ids[None, None, :]
    ranked = jnp.sum(jnp.where(named, rank[:, :, None] + 1, 0), axis=1)
    ranked = jnp.where(ranked > 0, ranked, pair_count + 1)
    ranked_all = lax.all_gather(ranked, ("x", "core"), axis=0, tiled=False)
    ranked_all = ranked_all.reshape(2, 2, halves, own_rows, EXPERTS)
    ranked_all = by_distance(by_distance(ranked_all, "x", 0), "core", 1)
    ranked_all = by_distance(ranked_all, "tensor", 2)
    ranked_all = jnp.swapaxes(ranked_all, 0, 1).reshape(groups, group_rows, EXPERTS)
    routed_all = ranked_all <= pair_count
    expert = lax.axis_index(PLANE)
    own_column = expert_ids == expert
    rank_own = jnp.sum(jnp.where(own_column, ranked_all, 0), axis=-1)
    slot_own = jnp.sum(
        (rank_own[:, None, :] < rank_own[:, :, None]).astype(jnp.int32), axis=-1
    )
    slot_own = jnp.where(rank_own <= pair_count, slot_own, capacity)
    place = (
        slot_own[:, None, :] == jnp.arange(capacity, dtype=jnp.int32)[None, :, None]
    ).astype(BF16)

    cotangent_near, cotangent_far = plane_gather(cotangent)

    input_wide = block_input.astype(F32)
    first_gain = norm_gains[:, 0]
    second_gain = norm_gains[:, 1]
    first_factor = norm_factor(input_wide)
    normed_in = (input_wide * first_factor * first_gain).astype(BF16)
    positions = own_start + jnp.arange(own_rows, dtype=jnp.int32)
    cosine, sine = rotary_tables(positions % seq_len)
    cosine_heads, sine_heads = cosine[:, None, None, :], sine[:, None, None, :]
    qkv = dot(normed_in, qkv_full, ((1,), (0,))).reshape(
        own_rows, halves, group_heads + 2, HEAD_SIZE
    )
    queries = rotate(qkv[:, :, :group_heads], cosine_heads, sine_heads).astype(BF16)
    keys_own = rotate(qkv[:, :, group_heads : group_heads + 1], cosine_heads, sine_heads)
    key_value_own = jnp.concatenate([keys_own, qkv[:, :, group_heads + 1 :]], axis=2).astype(BF16)
    pieces = [shift_all(key_value_own, k) for k in range(reach, 0, -1)] + [key_value_own]
    key_value = jnp.concatenate(pieces, axis=0)
    key_ext, value_ext = key_value[:, :, 0], key_value[:, :, 1]
    earlier_groups = (ATTEND_SPAN + group_rows - 1) // group_rows
    group_pairs = [
        [(i, i + k) for i in range(dp_size - k)] for k in range(earlier_groups, 0, -1)
    ]
    segment_near = jnp.concatenate(
        [lax.ppermute(segment_ids, DP, pairs) for pairs in group_pairs] + [segment_ids]
    )
    span = ATTEND_SPAN + own_rows
    segment_ext = lax.dynamic_slice_in_dim(segment_near, tensor_index * own_rows, span)
    segment_own = segment_ext[ATTEND_SPAN:]
    key_pos = own_start - ATTEND_SPAN + jnp.arange(span, dtype=jnp.int32)
    distance = positions[:, None] - key_pos[None, :]
    allowed = (key_pos[None, :] >= 0) & (distance >= 0) & (distance < ATTEND_SPAN)
    allowed = allowed & (positions[:, None] // seq_len == key_pos[None, :] // seq_len)
    allowed = allowed & (segment_own[:, None] == segment_ext[None, :])

    def attention_scores():
        raw = jnp.einsum("qgjd,kgd->gjqk", queries, key_ext, preferred_element_type=F32)
        return jnp.where(allowed[None, None], raw * score_scale, -1e30)

    scores = attention_scores()
    row_top = jnp.max(scores, axis=-1, keepdims=True)
    weights = jnp.exp(scores - row_top)
    row_total = jnp.sum(weights, axis=-1, keepdims=True)
    probability = (weights / row_total).astype(BF16)
    heads_low = (
        jnp.einsum("gjqk,kgd->qgjd", probability, value_ext, preferred_element_type=F32)
        .astype(BF16)
        .reshape(own_rows, -1)
    )
    log_total = row_top + jnp.log(row_total)
    hidden_state = input_wide + dot(heads_low, output_full, ((1,), (1,)))
    second_factor = norm_factor(hidden_state)
    normed_mid_own = (hidden_state * second_factor * second_gain).astype(BF16)

    normed_near, normed_far = plane_gather(normed_mid_own)
    normed_mid = jnp.concatenate([normed_near, normed_far]).reshape(-1, width)
    logits = dot(normed_mid, router_weight, ((1,), (0,))).reshape(groups, group_rows, EXPERTS)
    logits = jnp.where(routed_all, logits, -1e30)
    gate_weights = jnp.where(
        routed_all, jnp.exp(logits - jnp.max(logits, axis=-1, keepdims=True)), 0.0
    )
    gates = gate_weights / jnp.sum(gate_weights, axis=-1, keepdims=True)
    gate_own = jnp.sum(jnp.where(own_column, gates, 0.0), axis=-1)

    def to_slots(near, far):
        halves_of = [
            jnp.einsum(
                "gct,gtd->gcd",
                place[first : first + 2],
                rows.reshape(2, group_rows, width),
                preferred_element_type=F32,
            ).astype(BF16)
            for first, rows in ((0, near), (2, far))
        ]
        return jnp.concatenate(halves_of).reshape(groups * capacity, width)

    expert_in = to_slots(normed_near, normed_far)
    cotangent_slots = to_slots(cotangent_near, cotangent_far).astype(F32)
    coefficient = jnp.sum(place.astype(F32) * gate_own[:, None, :], axis=-1).reshape(-1, 1)
    gate_pre = dot(expert_in, gate_full, ((1,), (0,)))
    up_pre = dot(expert_in, up_full, ((1,), (0,)))
    sigmoid_gate = jax.nn.sigmoid(gate_pre)
    silu_gate = gate_pre * sigmoid_gate
    expert_hidden = (silu_gate * up_pre).astype(BF16)
    expert_out = dot(expert_hidden, down_full, ((1,), (1,)))
    grad_expert_out = (coefficient * cotangent_slots).astype(BF16)
    grad_hidden = dot(grad_expert_out, down_full, ((1,), (0,)))
    grad_up = (grad_hidden * silu_gate).astype(BF16)
    grad_gate = (
        grad_hidden * up_pre * sigmoid_gate * (1.0 + gate_pre * (1.0 - sigmoid_gate))
    ).astype(BF16)
    grad_expert_in = dot(grad_gate, gate_full, ((1,), (1,))) + dot(grad_up, up_full, ((1,), (1,)))

    def to_tokens(rows, more):
        rows = rows.astype(BF16).reshape(groups, capacity, width)
        sides = []
        for first in (2, 0):
            tokens = jnp.einsum(
                "gct,gcd->gtd",
                place[first : first + 2],
                rows[first : first + 2],
                preferred_element_type=F32,
            )
            if more is not None:
                tokens = tokens + more[first : first + 2]
            sides.append(tokens.astype(BF16).reshape(2, halves, own_rows, width))
        far, near = sides
        return plane_scatter(near, far)

    grad_gate_slots = jnp.sum(cotangent_slots * expert_out, axis=-1).reshape(groups, capacity)
    grad_gate_tokens = jnp.sum(place.astype(F32) * grad_gate_slots[:, :, None], axis=1)
    grad_logits = (grad_gate_tokens * gate_own)[:, :, None] * (
        own_column.astype(F32)[None, None, :] - gates
    )
    grad_logits = grad_logits.reshape(groups * group_rows, EXPERTS)
    router_share = jnp.dot(
        grad_logits, router_weight.astype(F32).T, precision=FULL_PRECISION
    ).reshape(groups, group_rows, width)
    router_part = jnp.dot(normed_mid.astype(F32).T, grad_logits, precision=FULL_PRECISION)
    grad_mid = to_tokens(grad_expert_in, router_share)
    moe_own = to_tokens(coefficient * expert_out, None)
    block_output = hidden_state + moe_own

    down_part = dot(grad_expert_out, expert_hidden, ((0,), (0,))).astype(BF16)
    gate_part = dot(expert_in, grad_gate, ((0,), (0,))).astype(BF16)
    up_part = dot(expert_in, grad_up, ((0,), (0,))).astype(BF16)
    expert_sum = outer_scatter((gate_part, up_part, down_part))
    expert_sum = expert_sum.reshape(3, groups, shard_rows, halves, half_ff)
    expert_sum = jnp.transpose(expert_sum, (1, 3, 0, 2, 4)).reshape(
        plane, 3, shard_rows, half_ff
    )
    expert_sum = lax.all_to_all(expert_sum, PLANE, 0, 0, tiled=True)
    expert_grads = jnp.transpose(expert_sum, (1, 2, 0, 3)).astype(F32)
    gate_grad, up_grad, down_grad = expert_grads[0], expert_grads[1], expert_grads[2]

    norm_input_part, second_gain_part = norm_back(
        hidden_state, second_factor, second_gain, grad_mid
    )
    grad_state = cotangent.astype(F32) + norm_input_part
    grad_attn = grad_state.astype(BF16)
    grad_heads = dot(grad_attn, output_full, ((1,), (0,))).astype(BF16)
    output_part = dot(grad_attn, heads_low, ((0,), (0,)))
    small_part = jnp.concatenate([router_part, second_gain_part[:, None]], axis=1)
    small_part = jnp.pad(small_part, ((0, 0), (0, HEAD_SIZE - small_part.shape[1])))
    output_sum = lax.psum_scatter(
        jnp.concatenate([output_part, small_part], axis=1).astype(BF16),
        DP,
        scatter_dimension=0,
        tiled=True,
    )
    grad_heads = grad_heads.reshape(queries.shape)
    scores = attention_scores()
    probability = jnp.exp(scores - log_total)
    grad_prob = jnp.einsum("qgjd,kgd->gjqk", grad_heads, value_ext, preferred_element_type=F32)
    row_dot = jnp.sum(probability * grad_prob, axis=-1, keepdims=True)
    grad_scores = (probability * (grad_prob - row_dot)).astype(BF16)
    grad_queries = (
        jnp.einsum("gjqk,kgd->qgjd", grad_scores, key_ext, preferred_element_type=F32)
        * score_scale
    )
    grad_keys = (
        jnp.einsum("gjqk,qgjd->kgd", grad_scores, queries, preferred_element_type=F32)
        * score_scale
    )
    grad_values = jnp.einsum(
        "gjqk,qgjd->kgd", probability.astype(BF16), grad_heads, preferred_element_type=F32
    )
    grad_key_value = jnp.stack([grad_keys, grad_values], axis=2)
    grad_own = grad_key_value[ATTEND_SPAN:]
    for k in range(1, reach + 1):
        first_row = ATTEND_SPAN - k * own_rows
        piece = grad_key_value[first_row : first_row + own_rows].astype(BF16)
        grad_own = grad_own + shift_all(piece, -k).astype(F32)
    grad_qkv = jnp.concatenate(
        [
            rotate(
                jnp.concatenate([grad_queries, grad_own[:, :, :1]], axis=2),
                cosine_heads,
                -sine_heads,
            ),
            grad_own[:, :, 1:],
        ],
        axis=2,
    )
    grad_qkv = grad_qkv.astype(BF16).reshape(own_rows, -1)
    qkv_part = dot(normed_in, grad_qkv, ((0,), (0,)))
    grad_in = dot(grad_qkv, qkv_full, ((1,), (1,)))
    first_input_part, first_gain_part = norm_back(input_wide, first_factor, first_gain, grad_in)
    input_grad = grad_state + first_input_part
    first_part = jnp.pad(first_gain_part[:, None], ((0, 0), (0, HEAD_SIZE - 1)))
    qkv_sum = lax.psum_scatter(
        jnp.concatenate([qkv_part, first_part], axis=1).astype(BF16),
        DP,
        scatter_dimension=0,
        tiled=True,
    )

    def pair_sum(sums, pair_columns):
        half = pair_columns // 2
        columns, small = sums[:, :pair_columns], sums[:, pair_columns:]
        half_rows = shard_rows // 2
        kept = lax.dynamic_slice_in_dim(columns, tensor_index * half, half, 1)
        sent = lax.dynamic_slice_in_dim(columns, (1 - tensor_index) * half, half, 1)
        small_kept = lax.dynamic_slice_in_dim(small, tensor_index * half_rows, half_rows, 0)
        small_sent = lax.dynamic_slice_in_dim(small, (1 - tensor_index) * half_rows, half_rows, 0)
        got, small_got = lax.ppermute((sent, small_sent), "tensor", [(0, 1), (1, 0)])
        return (
            kept.astype(F32) + got.astype(F32),
            small_kept.astype(F32) + small_got.astype(F32),
        )

    output_weight_grad, small_sum = pair_sum(output_sum, output_part.shape[1])
    router_grad = small_sum[:, :EXPERTS]
    qkv_grad, first_sum = pair_sum(qkv_sum, qkv_part.shape[1])
    gains_grad = jnp.concatenate([first_sum[:, :1], small_sum[:, EXPERTS : EXPERTS + 1]], axis=1)
    query_columns = group_heads * HEAD_SIZE
    query_grad = qkv_grad[:, :query_columns]
    key_grad = qkv_grad[:, query_columns : query_columns + HEAD_SIZE]
    value_grad = qkv_grad[:, query_columns + HEAD_SIZE :]
    return (
        block_output,
        input_grad,
        gains_grad,
        router_grad,
        query_grad,
        key_grad,
        value_grad,
        output_weight_grad,
        gate_grad,
        up_grad,
        down_grad,
    )


def solution(mesh):
    dp_size, tensor_size = mesh.shape["dp"], mesh.shape["tensor"]
    split = Mesh(mesh.devices.reshape(dp_size // 4, 2, 2, tensor_size), ALL)
    return jax.shard_map(
        on_device,
        mesh=split,
        in_specs=(
            P(ALL, None),
            P(),
            P(),
            P(DP, "tensor"),
            P(DP, "tensor"),
            P(DP, "tensor"),
            P(DP, "tensor"),
            P(DP, None, "tensor"),
            P(DP, None, "tensor"),
            P(DP, None, "tensor"),
            P(DP),
            P(DP, None),
            P(DP),
            P(ALL, None),
        ),
        out_specs=(
            P(ALL, None),
            P(ALL, None),
            P(ALL, None),
            P(ALL, None),
            P(DP, "tensor"),
            P(DP, "tensor"),
            P(DP, "tensor"),
            P(DP, "tensor"),
            P(DP, None, "tensor"),
            P(DP, None, "tensor"),
            P(DP, None, "tensor"),
        ),
        check_vma=False,
    )
```

```python
import math

import jax
import jax.numpy as jnp
from jax import lax
from jax.sharding import Mesh
from jax.sharding import PartitionSpec as P

HEAD_SIZE = 128
TOPK = 4
EXPERTS = 8
ATTEND_SPAN = 1024
SEQ_MOST = 16384
EPSILON = 1e-06
ROPE_BASE = 10000.0
FULL_PRECISION = lax.Precision.HIGHEST
BF16 = jnp.bfloat16
F32 = jnp.float32

DP = ("outer", "x", "core")
PLANE = ("x", "core", "tensor")
ALL = ("outer", "x", "core", "tensor")


def shift_all(x, by):
    length = lax.axis_size(ALL)
    pairs = [(i, i + by) for i in range(length) if 0 <= i + by < length]
    return lax.ppermute(x, ALL, pairs)


def swap(x, axis):
    length = lax.axis_size(axis)
    return lax.ppermute(x, axis, [(i, length - 1 - i) for i in range(length)])


def plane_gather(own):
    near = jnp.stack([own, swap(own, "tensor"), swap(own, "x"), swap(own, ("x", "tensor"))])
    far = swap(near, "core")
    shape = (2, 2) + own.shape
    return near.reshape(shape), far.reshape(shape)


def plane_scatter(near, far):
    total = (near.astype(F32) + swap(far, "core").astype(F32)).astype(BF16)
    parts = [
        total[0, 0],
        swap(total[0, 1], "tensor"),
        swap(total[1, 0], "x"),
        swap(total[1, 1], ("x", "tensor")),
    ]
    return sum(part.astype(F32) for part in parts)


def outer_shift(x, by):
    length = lax.axis_size("outer")
    return lax.ppermute(x, "outer", [(i, (i + by) % length) for i in range(length)])


def outer_gather(shard):
    length, here = lax.axis_size("outer"), lax.axis_index("outer")
    if length > 4:
        return lax.all_gather(shard, "outer")
    full = jnp.zeros((length,) + shard.shape, shard.dtype)
    for by in range(length):
        piece = outer_shift(shard, by) if by else shard
        full = lax.dynamic_update_slice_in_dim(full, piece[None], (here - by) % length, 0)
    return full


def outer_scatter(parts):
    length, here = lax.axis_size("outer"), lax.axis_index("outer")
    if length > 4:
        return lax.psum_scatter(parts, "outer", scatter_dimension=0, tiled=False).astype(F32)
    total = None
    for by in range(length):
        piece = lax.dynamic_index_in_dim(parts, (here + by) % length, 0, keepdims=False)
        piece = (outer_shift(piece, by) if by else piece).astype(F32)
        total = piece if total is None else total + piece
    return total


def all_scatter(part):
    outer, groups = lax.axis_size("outer"), lax.axis_size("x") * lax.axis_size("core")
    x, core, tensor = (lax.axis_index(name) for name in PLANE)
    rows, columns = part.shape[0] // (outer * groups), part.shape[1] // 2
    part = part.astype(BF16).reshape(outer, 2, 2, rows, 2, columns)

    kept = lax.dynamic_index_in_dim(part, core, 2, keepdims=False)
    sent = lax.dynamic_index_in_dim(part, 1 - core, 2, keepdims=False)
    total = (kept.astype(F32) + swap(sent, "core").astype(F32)).astype(BF16)

    def block(x_at, tensor_at):
        picked = lax.dynamic_index_in_dim(total, x_at, 1, keepdims=False)
        return lax.dynamic_index_in_dim(picked, tensor_at, 2, keepdims=False)

    parts = [
        block(x, tensor),
        swap(block(x, 1 - tensor), "tensor"),
        swap(block(1 - x, tensor), "x"),
        swap(block(1 - x, 1 - tensor), ("x", "tensor")),
    ]
    return outer_scatter(sum(p.astype(F32) for p in parts).astype(BF16))


def rotary_tables(position):
    halfway = HEAD_SIZE // 2
    inverse = jnp.exp(
        jnp.arange(halfway, dtype=F32) * (-2.0 * math.log(ROPE_BASE) / HEAD_SIZE)
    )
    angles = position.astype(F32)[:, None] * inverse[None, :]
    return (jnp.cos(angles), jnp.sin(angles))


def rotate(value_rows, cosine, sine):
    halfway = value_rows.shape[-1] // 2
    first_half = value_rows[..., :halfway]
    second_half = value_rows[..., halfway:]
    return jnp.concatenate(
        [first_half * cosine - second_half * sine, second_half * cosine + first_half * sine],
        axis=-1,
    )


def norm_factor(value_rows):
    return lax.rsqrt(jnp.mean(value_rows * value_rows, axis=-1, keepdims=True) + EPSILON)


def norm_back(value_rows, factor, gain, upstream):
    weighted = upstream * gain
    return factor * weighted - value_rows * (factor * factor * factor) * jnp.mean(
        weighted * value_rows, axis=-1, keepdims=True
    )


def dot(a, b, dims):
    return lax.dot_general(a, b, (dims, ((), ())), preferred_element_type=F32)


def on_device(
    block_input,
    norm_gains,
    router_weight,
    query_matrix,
    key_matrix,
    value_matrix,
    output_weight,
    gate_weight,
    up_weight,
    down_weight,
    segment_ids,
    routes,
    priority,
    cotangent,
):
    tensor_index = lax.axis_index("tensor")
    own_rows, width = block_input.shape
    group_rows = segment_ids.shape[0]
    halves = lax.axis_size("tensor")
    outer = lax.axis_size("outer")
    groups = lax.axis_size("x") * lax.axis_size("core")
    plane = groups * halves
    shard_rows = query_matrix.shape[0]
    dp_size = outer * groups
    seq_len = min(SEQ_MOST, group_rows * dp_size)
    own_start = lax.axis_index(ALL) * own_rows
    capacity = group_rows * TOPK // EXPERTS
    score_scale = 1.0 / math.sqrt(HEAD_SIZE)
    reach = ATTEND_SPAN // own_rows
    group_heads = query_matrix.shape[1] // HEAD_SIZE
    half_ff = gate_weight.shape[2]
    ff = half_ff * halves

    query_columns = query_matrix.shape[1]
    first = tensor_index == 0
    qkv_own = jnp.concatenate([query_matrix, key_matrix, value_matrix], axis=1)
    qkv_other = swap(qkv_own, "tensor")
    qkv_first = jnp.where(first, qkv_own, qkv_other)
    qkv_second = jnp.where(first, qkv_other, qkv_own)
    qkv_shard = jnp.concatenate(
        [
            qkv_first[:, :query_columns],
            qkv_second[:, :query_columns],
            qkv_first[:, query_columns:],
            qkv_second[:, query_columns:],
        ],
        axis=1,
    )
    qkv_shard, output_own, gate_own, up_own, down_own = lax.optimization_barrier(
        (qkv_shard, output_weight, gate_weight, up_weight, down_weight)
    )
    qkv_full = lax.all_gather(qkv_shard, DP, axis=0, tiled=True)

    near, far = plane_gather(outer_gather(output_own))
    pieces = jnp.stack([near, far])
    x_index, core_index = lax.axis_index("x"), lax.axis_index("core")

    def piece_at(x_at, core_at, tensor_at):
        piece = lax.dynamic_index_in_dim(pieces, core_index ^ core_at, 0, keepdims=False)
        piece = lax.dynamic_index_in_dim(piece, x_index ^ x_at, 0, keepdims=False)
        return lax.dynamic_index_in_dim(piece, tensor_index ^ tensor_at, 0, keepdims=False)

    output_full = jnp.concatenate(
        [
            jnp.stack([piece_at(x_at, core_at, at) for x_at in range(2) for core_at in range(2)], 1)
            for at in range(2)
        ],
        axis=-1,
    ).reshape(width, -1)

    expert_shard = jnp.transpose(jnp.stack([gate_own, up_own, down_own]), (2, 0, 1, 3))
    expert_shard = lax.all_to_all(expert_shard, PLANE, 0, 0, tiled=True)
    expert_shard = expert_shard.reshape(groups, halves, 3, shard_rows, half_ff)
    expert_shard = jnp.transpose(expert_shard, (2, 0, 3, 1, 4)).reshape(
        3, groups * shard_rows, ff
    )
    gate_up = lax.all_gather(expert_shard[:2], "outer", axis=1, tiled=True)
    gate_full, up_full = gate_up[0], gate_up[1]
    down_full = outer_gather(expert_shard[2]).reshape(width, ff)

    pair_count = group_rows * TOPK
    rank = (
        jnp.zeros((pair_count,), jnp.int32)
        .at[priority]
        .set(jnp.arange(pair_count, dtype=jnp.int32))
        .reshape(group_rows, TOPK)
    )
    expert_ids = jnp.arange(EXPERTS, dtype=jnp.int32)
    named = routes[:, :, None] == expert_ids[None, None, :]
    ranked = jnp.sum(jnp.where(named, rank[:, :, None] + 1, 0), axis=1)
    ranked = jnp.where(ranked > 0, ranked, pair_count + 1)
    ranked_own = lax.dynamic_slice_in_dim(ranked, tensor_index * own_rows, own_rows, 0)
    digits = jnp.concatenate([ranked_own // 64, ranked_own % 64], axis=1).astype(BF16)
    digits = jnp.pad(digits, ((0, 0), (0, HEAD_SIZE - digits.shape[1])))
    cotangent_near, cotangent_far = plane_gather(jnp.concatenate([cotangent, digits], axis=1))
    digits = jnp.stack([cotangent_near[..., width:], cotangent_far[..., width:]])
    digits = digits.astype(jnp.int32).reshape(groups, group_rows, HEAD_SIZE)
    ranked_all = digits[..., :EXPERTS] * 64 + digits[..., EXPERTS : 2 * EXPERTS]
    cotangent_near, cotangent_far = cotangent_near[..., :width], cotangent_far[..., :width]
    routed_all = ranked_all <= pair_count
    expert = lax.axis_index(PLANE)
    own_column = expert_ids == expert
    rank_own = jnp.sum(jnp.where(own_column, ranked_all, 0), axis=-1)
    slot_own = jnp.sum(
        (rank_own[:, None, :] < rank_own[:, :, None]).astype(jnp.int32), axis=-1
    )
    slot_own = jnp.where(rank_own <= pair_count, slot_own, capacity)
    place = (
        slot_own[:, None, :] == jnp.arange(capacity, dtype=jnp.int32)[None, :, None]
    ).astype(BF16)


    input_wide = block_input.astype(F32)
    first_gain = norm_gains[:, 0]
    second_gain = norm_gains[:, 1]
    first_factor = norm_factor(input_wide)
    normed_in = (input_wide * first_factor * first_gain).astype(BF16)
    positions = own_start + jnp.arange(own_rows, dtype=jnp.int32)
    cosine, sine = rotary_tables(positions % seq_len)
    cosine_heads, sine_heads = cosine[:, None, None, :], sine[:, None, None, :]
    all_queries = halves * query_columns
    key_value_pre = dot(normed_in, qkv_full[:, all_queries:], ((1,), (0,))).reshape(
        own_rows, halves, 2, HEAD_SIZE
    )
    keys_own = rotate(key_value_pre[:, :, :1], cosine_heads, sine_heads)
    key_value_own = jnp.concatenate([keys_own, key_value_pre[:, :, 1:]], axis=2).astype(BF16)
    queries = rotate(
        dot(normed_in, qkv_full[:, :all_queries], ((1,), (0,))).reshape(
            own_rows, halves, group_heads, HEAD_SIZE
        ),
        cosine_heads,
        sine_heads,
    ).astype(BF16)
    pieces = [shift_all(key_value_own, k) for k in range(reach, 0, -1)] + [key_value_own]
    key_value = jnp.concatenate(pieces, axis=0)
    key_ext, value_ext = key_value[:, :, 0], key_value[:, :, 1]
    earlier_groups = (ATTEND_SPAN + group_rows - 1) // group_rows
    group_pairs = [
        [(i, i + k) for i in range(dp_size - k)] for k in range(earlier_groups, 0, -1)
    ]
    segment_near = jnp.concatenate(
        [lax.ppermute(segment_ids, DP, pairs) for pairs in group_pairs] + [segment_ids]
    )
    span = ATTEND_SPAN + own_rows
    segment_ext = lax.dynamic_slice_in_dim(segment_near, tensor_index * own_rows, span)
    segment_own = segment_ext[ATTEND_SPAN:]
    key_pos = own_start - ATTEND_SPAN + jnp.arange(span, dtype=jnp.int32)
    distance = positions[:, None] - key_pos[None, :]
    allowed = (key_pos[None, :] >= 0) & (distance >= 0) & (distance < ATTEND_SPAN)
    allowed = allowed & (positions[:, None] // seq_len == key_pos[None, :] // seq_len)
    allowed = allowed & (segment_own[:, None] == segment_ext[None, :])

    def attention_scores():
        raw = jnp.einsum("qgjd,kgd->gjqk", queries, key_ext, preferred_element_type=F32)
        return jnp.where(allowed[None, None], raw * score_scale, -1e30)

    scores = attention_scores()
    row_top = jnp.max(scores, axis=-1, keepdims=True)
    weights = jnp.exp(scores - row_top)
    row_total = jnp.sum(weights, axis=-1, keepdims=True)
    probability = (weights / row_total).astype(BF16)
    heads_low = (
        jnp.einsum("gjqk,kgd->qgjd", probability, value_ext, preferred_element_type=F32)
        .astype(BF16)
        .reshape(own_rows, -1)
    )
    log_total = row_top + jnp.log(row_total)
    hidden_state = input_wide + dot(heads_low, output_full, ((1,), (1,)))
    second_factor = norm_factor(hidden_state)
    normed_mid_own = (hidden_state * second_factor * second_gain).astype(BF16)

    normed_near, normed_far = plane_gather(normed_mid_own)
    normed_mid = jnp.concatenate([normed_near, normed_far]).reshape(-1, width)
    logits = dot(normed_mid, router_weight, ((1,), (0,))).reshape(groups, group_rows, EXPERTS)
    logits = jnp.where(routed_all, logits, -1e30)
    gate_weights = jnp.where(
        routed_all, jnp.exp(logits - jnp.max(logits, axis=-1, keepdims=True)), 0.0
    )
    gates = gate_weights / jnp.sum(gate_weights, axis=-1, keepdims=True)
    gate_own = jnp.sum(jnp.where(own_column, gates, 0.0), axis=-1)

    def to_slots(near, far):
        halves_of = [
            jnp.einsum(
                "gct,gtd->gcd",
                place[first : first + 2],
                rows.reshape(2, group_rows, width),
                preferred_element_type=F32,
            ).astype(BF16)
            for first, rows in ((0, near), (2, far))
        ]
        return jnp.concatenate(halves_of).reshape(groups * capacity, width)

    expert_in = to_slots(normed_near, normed_far)
    cotangent_slots = to_slots(cotangent_near, cotangent_far).astype(F32)
    coefficient = jnp.sum(place.astype(F32) * gate_own[:, None, :], axis=-1).reshape(-1, 1)
    gate_pre = dot(expert_in, gate_full, ((1,), (0,)))
    up_pre = dot(expert_in, up_full, ((1,), (0,)))
    sigmoid_gate = jax.nn.sigmoid(gate_pre)
    silu_gate = gate_pre * sigmoid_gate
    expert_hidden = (silu_gate * up_pre).astype(BF16)
    expert_out = dot(expert_hidden, down_full, ((1,), (1,)))
    grad_expert_out = (coefficient * cotangent_slots).astype(BF16)
    grad_hidden = dot(grad_expert_out, down_full, ((1,), (0,)))
    grad_up = (grad_hidden * silu_gate).astype(BF16)
    grad_gate = (
        grad_hidden * up_pre * sigmoid_gate * (1.0 + gate_pre * (1.0 - sigmoid_gate))
    ).astype(BF16)
    grad_expert_in = dot(grad_gate, gate_full, ((1,), (1,))) + dot(grad_up, up_full, ((1,), (1,)))

    def to_tokens(rows, more, after=None):
        rows = rows.astype(BF16).reshape(groups, capacity, width)
        sides = []
        for first in (2, 0):
            tokens = jnp.einsum(
                "gct,gcd->gtd",
                place[first : first + 2],
                rows[first : first + 2],
                preferred_element_type=F32,
            )
            if more is not None:
                tokens = tokens + more[first : first + 2]
            sides.append(tokens.astype(BF16).reshape(2, halves, own_rows, width))
        far, near = sides
        if after is not None:
            far, near, after = lax.optimization_barrier((far, near, after))
        return plane_scatter(near, far)

    grad_gate_slots = jnp.sum(cotangent_slots * expert_out, axis=-1).reshape(groups, capacity)
    grad_gate_tokens = jnp.sum(place.astype(F32) * grad_gate_slots[:, :, None], axis=1)
    grad_logits = (grad_gate_tokens * gate_own)[:, :, None] * (
        own_column.astype(F32)[None, None, :] - gates
    )
    grad_logits = grad_logits.reshape(groups * group_rows, EXPERTS)
    router_share = jnp.dot(
        grad_logits, router_weight.astype(F32).T, precision=FULL_PRECISION
    ).reshape(groups, group_rows, width)
    router_part = jnp.dot(normed_mid.astype(F32).T, grad_logits, precision=FULL_PRECISION)
    grad_mid = to_tokens(grad_expert_in, router_share)
    moe_own = to_tokens(coefficient * expert_out, None, grad_mid)
    block_output = hidden_state + moe_own

    expert_parts = jnp.concatenate(
        [
            dot(expert_in, grad_gate, ((0,), (0,))).astype(BF16),
            dot(expert_in, grad_up, ((0,), (0,))).astype(BF16),
            dot(grad_expert_out, expert_hidden, ((0,), (0,))).astype(BF16),
            jnp.pad(router_part.astype(BF16), ((0, 0), (0, HEAD_SIZE - EXPERTS))),
        ],
        axis=1,
    )
    expert_sum = lax.psum_scatter(expert_parts, "outer", scatter_dimension=0, tiled=True)
    router_rows = expert_sum[:, 3 * ff : 3 * ff + EXPERTS].reshape(plane, 1, -1)
    router_rows = jnp.pad(
        router_rows, ((0, 0), (0, 15), (0, half_ff - router_rows.shape[2]))
    )
    expert_sum = expert_sum[:, : 3 * ff].reshape(groups, shard_rows, 3, halves, half_ff)
    expert_sum = jnp.transpose(expert_sum, (0, 3, 2, 1, 4)).reshape(
        plane, 3 * shard_rows, half_ff
    )
    expert_sum = lax.all_to_all(
        jnp.concatenate([expert_sum, router_rows], axis=1), PLANE, 0, 0, tiled=True
    )
    router_grad = jnp.sum(
        expert_sum[:, 3 * shard_rows, : shard_rows // 2 * EXPERTS].astype(F32), axis=0
    ).reshape(shard_rows // 2, EXPERTS)
    expert_sum = expert_sum[:, : 3 * shard_rows].reshape(plane, 3, shard_rows, half_ff)
    expert_grads = jnp.transpose(expert_sum, (1, 2, 0, 3)).astype(F32)
    gate_grad, up_grad, down_grad = expert_grads[0], expert_grads[1], expert_grads[2]

    norm_input_part = norm_back(hidden_state, second_factor, second_gain, grad_mid)
    grad_state = cotangent.astype(F32) + norm_input_part
    grad_attn = grad_state.astype(BF16)
    grad_heads = dot(grad_attn, output_full, ((1,), (0,))).astype(BF16)
    output_weight_grad = all_scatter(dot(grad_attn, heads_low, ((0,), (0,))))
    grad_heads = grad_heads.reshape(queries.shape)
    scores = attention_scores()
    probability = jnp.exp(scores - log_total)
    grad_prob = jnp.einsum("qgjd,kgd->gjqk", grad_heads, value_ext, preferred_element_type=F32)
    row_dot = jnp.sum(probability * grad_prob, axis=-1, keepdims=True)
    grad_scores = (probability * (grad_prob - row_dot)).astype(BF16)
    grad_queries = (
        jnp.einsum("gjqk,kgd->qgjd", grad_scores, key_ext, preferred_element_type=F32)
        * score_scale
    )
    grad_keys = (
        jnp.einsum("gjqk,qgjd->kgd", grad_scores, queries, preferred_element_type=F32)
        * score_scale
    )
    grad_values = jnp.einsum(
        "gjqk,qgjd->kgd", probability.astype(BF16), grad_heads, preferred_element_type=F32
    )
    grad_key_value = jnp.stack([grad_keys, grad_values], axis=2)
    grad_own = grad_key_value[ATTEND_SPAN:]
    for k in range(1, reach + 1):
        first_row = ATTEND_SPAN - k * own_rows
        piece = grad_key_value[first_row : first_row + own_rows].astype(BF16)
        grad_own = grad_own + shift_all(piece, -k).astype(F32)
    grad_query_pre = (
        rotate(grad_queries, cosine_heads, -sine_heads).astype(BF16).reshape(own_rows, -1)
    )
    grad_keys_pre = rotate(grad_own[:, :, :1], cosine_heads, -sine_heads)
    grad_key_value_pre = (
        jnp.concatenate([grad_keys_pre, grad_own[:, :, 1:]], axis=2)
        .astype(BF16)
        .reshape(own_rows, -1)
    )
    query_part = dot(normed_in, grad_query_pre, ((0,), (0,))).reshape(width, halves, -1)
    key_value_part = dot(normed_in, grad_key_value_pre, ((0,), (0,))).reshape(width, halves, -1)
    qkv_part = jnp.concatenate([query_part, key_value_part], axis=2).reshape(width, -1)
    qkv_grad = all_scatter(qkv_part)
    query_grad = qkv_grad[:, :query_columns]
    key_grad = qkv_grad[:, query_columns : query_columns + HEAD_SIZE]
    value_grad = qkv_grad[:, query_columns + HEAD_SIZE :]
    grad_in = dot(grad_query_pre, qkv_full[:, :all_queries], ((1,), (1,))) + dot(
        grad_key_value_pre, qkv_full[:, all_queries:], ((1,), (1,))
    )
    input_grad = grad_state + norm_back(input_wide, first_factor, first_gain, grad_in)

    half_rows = shard_rows // 2
    own_gains = lax.dynamic_slice_in_dim(
        norm_gains, lax.axis_index(DP) * shard_rows, shard_rows, 0
    )
    first_sum = jnp.sum(qkv_grad * qkv_own.astype(F32), axis=-1)
    second_sum = jnp.sum(
        gate_grad * gate_weight.astype(F32) + up_grad * up_weight.astype(F32), axis=(1, 2)
    )
    gain_sums = jnp.stack([first_sum, second_sum], axis=1) / own_gains
    kept = lax.dynamic_slice_in_dim(gain_sums, tensor_index * half_rows, half_rows, 0)
    sent = lax.dynamic_slice_in_dim(gain_sums, (1 - tensor_index) * half_rows, half_rows, 0)
    own_router = lax.dynamic_slice_in_dim(
        router_weight, lax.axis_index(ALL) * half_rows, half_rows, 0
    )
    router_sum = jnp.sum(router_grad * own_router.astype(F32), axis=-1)
    half_gains = lax.dynamic_slice_in_dim(own_gains, tensor_index * half_rows, half_rows, 0)
    router_sum = router_sum / half_gains[:, 1]
    gains_grad = (
        kept
        + swap(sent, "tensor")
        + jnp.stack([jnp.zeros_like(router_sum), router_sum], axis=1)
    )
    return (
        block_output,
        input_grad,
        gains_grad,
        router_grad,
        query_grad,
        key_grad,
        value_grad,
        output_weight_grad,
        gate_grad,
        up_grad,
        down_grad,
    )


def solution(mesh):
    dp_size, tensor_size = mesh.shape["dp"], mesh.shape["tensor"]
    split = Mesh(mesh.devices.reshape(dp_size // 4, 2, 2, tensor_size), ALL)
    return jax.shard_map(
        on_device,
        mesh=split,
        in_specs=(
            P(ALL, None),
            P(),
            P(),
            P(DP, "tensor"),
            P(DP, "tensor"),
            P(DP, "tensor"),
            P(DP, "tensor"),
            P(DP, None, "tensor"),
            P(DP, None, "tensor"),
            P(DP, None, "tensor"),
            P(DP),
            P(DP, None),
            P(DP),
            P(ALL, None),
        ),
        out_specs=(
            P(ALL, None),
            P(ALL, None),
            P(ALL, None),
            P(ALL, None),
            P(DP, "tensor"),
            P(DP, "tensor"),
            P(DP, "tensor"),
            P(DP, "tensor"),
            P(DP, None, "tensor"),
            P(DP, None, "tensor"),
            P(DP, None, "tensor"),
        ),
        check_vma=False,
    )
```

```python
import math

import jax
import jax.numpy as jnp
from jax import lax
from jax.sharding import Mesh
from jax.sharding import PartitionSpec as P

HEAD_SIZE = 128
TOPK = 4
EXPERTS = 8
ATTEND_SPAN = 1024
SEQ_MOST = 16384
EPSILON = 1e-06
ROPE_BASE = 10000.0
FULL_PRECISION = lax.Precision.HIGHEST
BF16 = jnp.bfloat16
F32 = jnp.float32

DP = ("outer", "x", "core")
PLANE = ("x", "core", "tensor")
ALL = ("outer", "x", "core", "tensor")


def shift_all(x, by):
    length = lax.axis_size(ALL)
    pairs = [(i, i + by) for i in range(length) if 0 <= i + by < length]
    return lax.ppermute(x, ALL, pairs)


def swap(x, axis):
    length = lax.axis_size(axis)
    return lax.ppermute(x, axis, [(i, length - 1 - i) for i in range(length)])


def plane_gather(own):
    near = jnp.stack([own, swap(own, "tensor"), swap(own, "x"), swap(own, ("x", "tensor"))])
    far = swap(near, "core")
    shape = (2, 2) + own.shape
    return near.reshape(shape), far.reshape(shape)


def fold_core(kept, sent):
    return (kept.astype(F32) + swap(sent, "core").astype(F32)).astype(BF16)


def fold_plane(blocks):
    return [
        blocks[0],
        swap(blocks[1], "tensor"),
        swap(blocks[2], "x"),
        swap(blocks[3], ("x", "tensor")),
    ]


def wide_sum(parts):
    return sum(part.astype(F32) for part in parts)


def outer_shift(x, by):
    length = lax.axis_size("outer")
    return lax.ppermute(x, "outer", [(i, (i + by) % length) for i in range(length)])


def outer_gather(shard):
    length, here = lax.axis_size("outer"), lax.axis_index("outer")
    if length > 4:
        return lax.all_gather(shard, "outer")
    full = jnp.zeros((length,) + shard.shape, shard.dtype)
    for by in range(length):
        piece = outer_shift(shard, by) if by else shard
        full = lax.dynamic_update_slice_in_dim(full, piece[None], (here - by) % length, 0)
    return full


def outer_scatter(parts):
    length, here = lax.axis_size("outer"), lax.axis_index("outer")
    if length > 4:
        return lax.psum_scatter(parts, "outer", scatter_dimension=0, tiled=False).astype(F32)
    total = None
    for by in range(length):
        piece = lax.dynamic_index_in_dim(parts, (here + by) % length, 0, keepdims=False)
        piece = (outer_shift(piece, by) if by else piece).astype(F32)
        total = piece if total is None else total + piece
    return total


def core_columns(rows, core_at, shard_rows):
    count = rows.shape[0]
    split = rows.reshape(count, -1, 2, shard_rows)
    return lax.dynamic_index_in_dim(split, core_at, 2, keepdims=False).reshape(count, -1)


def fold_columns(left, right, shard_rows):
    core = lax.axis_index("core")
    sent = dot(core_columns(left, 1 - core, shard_rows), right, ((0,), (0,))).astype(BF16)
    kept = dot(core_columns(left, core, shard_rows), right, ((0,), (0,))).astype(BF16)
    return fold_core(kept, sent).reshape(-1, 2, shard_rows, right.shape[1])


def distance_blocks(total):
    x, tensor = lax.axis_index("x"), lax.axis_index("tensor")
    columns = total.shape[3] // 2
    blocks = []
    for x_by in range(2):
        for tensor_by in range(2):
            block = lax.dynamic_index_in_dim(total, x ^ x_by, 1, keepdims=False)
            start = (tensor ^ tensor_by) * columns
            blocks.append(lax.dynamic_slice_in_dim(block, start, columns, 2))
    return blocks


def rotary_tables(position):
    halfway = HEAD_SIZE // 2
    inverse = jnp.exp(
        jnp.arange(halfway, dtype=F32) * (-2.0 * math.log(ROPE_BASE) / HEAD_SIZE)
    )
    angles = position.astype(F32)[:, None] * inverse[None, :]
    return (jnp.cos(angles), jnp.sin(angles))


def rotate(value_rows, cosine, sine):
    halfway = value_rows.shape[-1] // 2
    first_half = value_rows[..., :halfway]
    second_half = value_rows[..., halfway:]
    return jnp.concatenate(
        [first_half * cosine - second_half * sine, second_half * cosine + first_half * sine],
        axis=-1,
    )


def norm_factor(value_rows):
    return lax.rsqrt(jnp.mean(value_rows * value_rows, axis=-1, keepdims=True) + EPSILON)


def norm_back(value_rows, factor, gain, upstream):
    weighted = upstream * gain
    return factor * weighted - value_rows * (factor * factor * factor) * jnp.mean(
        weighted * value_rows, axis=-1, keepdims=True
    )


def dot(a, b, dims):
    return lax.dot_general(a, b, (dims, ((), ())), preferred_element_type=F32)


def on_device(
    block_input,
    norm_gains,
    router_weight,
    query_matrix,
    key_matrix,
    value_matrix,
    output_weight,
    gate_weight,
    up_weight,
    down_weight,
    segment_ids,
    routes,
    priority,
    cotangent,
):
    tensor_index = lax.axis_index("tensor")
    own_rows, width = block_input.shape
    group_rows = segment_ids.shape[0]
    halves = lax.axis_size("tensor")
    outer = lax.axis_size("outer")
    groups = lax.axis_size("x") * lax.axis_size("core")
    plane = groups * halves
    shard_rows = query_matrix.shape[0]
    dp_size = outer * groups
    seq_len = min(SEQ_MOST, group_rows * dp_size)
    own_start = lax.axis_index(ALL) * own_rows
    capacity = group_rows * TOPK // EXPERTS
    score_scale = 1.0 / math.sqrt(HEAD_SIZE)
    reach = ATTEND_SPAN // own_rows
    group_heads = query_matrix.shape[1] // HEAD_SIZE
    half_ff = gate_weight.shape[2]
    ff = half_ff * halves

    query_columns = query_matrix.shape[1]
    first = tensor_index == 0
    qkv_own = jnp.concatenate([query_matrix, key_matrix, value_matrix], axis=1)
    qkv_other = swap(qkv_own, "tensor")
    qkv_first = jnp.where(first, qkv_own, qkv_other)
    qkv_second = jnp.where(first, qkv_other, qkv_own)
    qkv_shard = jnp.concatenate(
        [
            qkv_first[:, :query_columns],
            qkv_second[:, :query_columns],
            qkv_first[:, query_columns:],
            qkv_second[:, query_columns:],
        ],
        axis=1,
    )
    earlier_groups = (ATTEND_SPAN + group_rows - 1) // group_rows
    group_pairs = [
        [(i, i + k) for i in range(dp_size - k)] for k in range(earlier_groups, 0, -1)
    ]
    segment_near = jnp.concatenate(
        [lax.ppermute(segment_ids, DP, pairs) for pairs in group_pairs] + [segment_ids]
    )
    qkv_shard, segment_near, gate_own, up_own, down_own = lax.optimization_barrier(
        (qkv_shard, segment_near, gate_weight, up_weight, down_weight)
    )
    qkv_full = lax.all_gather(qkv_shard, DP, axis=0, tiled=True)

    expert_shard = jnp.transpose(jnp.stack([gate_own, up_own, down_own]), (2, 0, 1, 3))
    expert_shard = lax.all_to_all(expert_shard, PLANE, 0, 0, tiled=True)
    expert_shard, output_own = lax.optimization_barrier((expert_shard, output_weight))
    expert_shard = expert_shard.reshape(groups, halves, 3, shard_rows, half_ff)
    expert_shard = jnp.transpose(expert_shard, (2, 0, 3, 1, 4)).reshape(
        3, groups * shard_rows, ff
    )
    gate_up = lax.all_gather(expert_shard[:2], "outer", axis=1, tiled=True)
    gate_full, up_full = gate_up[0], gate_up[1]
    down_full = outer_gather(expert_shard[2]).reshape(width, ff)

    near, far = plane_gather(outer_gather(output_own))
    pieces = jnp.stack([near, far])
    x_index, core_index = lax.axis_index("x"), lax.axis_index("core")

    def piece_at(x_at, core_at, tensor_at):
        piece = lax.dynamic_index_in_dim(pieces, core_index ^ core_at, 0, keepdims=False)
        piece = lax.dynamic_index_in_dim(piece, x_index ^ x_at, 0, keepdims=False)
        return lax.dynamic_index_in_dim(piece, tensor_index ^ tensor_at, 0, keepdims=False)

    output_full = jnp.concatenate(
        [
            jnp.stack([piece_at(x_at, core_at, at) for x_at in range(2) for core_at in range(2)], 1)
            for at in range(2)
        ],
        axis=-1,
    ).reshape(width, -1)

    pair_count = group_rows * TOPK
    rank = (
        jnp.zeros((pair_count,), jnp.int32)
        .at[priority]
        .set(jnp.arange(pair_count, dtype=jnp.int32))
        .reshape(group_rows, TOPK)
    )
    expert_ids = jnp.arange(EXPERTS, dtype=jnp.int32)
    named = routes[:, :, None] == expert_ids[None, None, :]
    ranked = jnp.sum(jnp.where(named, rank[:, :, None] + 1, 0), axis=1)
    ranked = jnp.where(ranked > 0, ranked, pair_count + 1)
    ranked_own = lax.dynamic_slice_in_dim(ranked, tensor_index * own_rows, own_rows, 0)
    digits = jnp.concatenate([ranked_own // 64, ranked_own % 64], axis=1).astype(BF16)
    digits = jnp.pad(digits, ((0, 0), (0, HEAD_SIZE - digits.shape[1])))
    cotangent_sent = jnp.concatenate([cotangent, digits], axis=1)
    input_wide = block_input.astype(F32)
    first_gain = norm_gains[:, 0]
    second_gain = norm_gains[:, 1]
    first_factor = norm_factor(input_wide)
    normed_in = (input_wide * first_factor * first_gain).astype(BF16)
    positions = own_start + jnp.arange(own_rows, dtype=jnp.int32)
    cosine, sine = rotary_tables(positions % seq_len)
    cosine_heads, sine_heads = cosine[:, None, None, :], sine[:, None, None, :]
    all_queries = halves * query_columns
    key_value_pre = dot(normed_in, qkv_full[:, all_queries:], ((1,), (0,))).reshape(
        own_rows, halves, 2, HEAD_SIZE
    )
    keys_own = rotate(key_value_pre[:, :, :1], cosine_heads, sine_heads)
    key_value_own = jnp.concatenate([keys_own, key_value_pre[:, :, 1:]], axis=2).astype(BF16)
    queries = rotate(
        dot(normed_in, qkv_full[:, :all_queries], ((1,), (0,))).reshape(
            own_rows, halves, group_heads, HEAD_SIZE
        ),
        cosine_heads,
        sine_heads,
    ).astype(BF16)
    queries, cotangent_sent = lax.optimization_barrier((queries, cotangent_sent))
    cotangent_near, cotangent_far = plane_gather(cotangent_sent)
    pieces = [shift_all(key_value_own, k) for k in range(reach, 0, -1)] + [key_value_own]
    key_value = jnp.concatenate(pieces, axis=0)
    key_ext, value_ext = key_value[:, :, 0], key_value[:, :, 1]
    span = ATTEND_SPAN + own_rows
    segment_ext = lax.dynamic_slice_in_dim(segment_near, tensor_index * own_rows, span)
    segment_own = segment_ext[ATTEND_SPAN:]
    key_pos = own_start - ATTEND_SPAN + jnp.arange(span, dtype=jnp.int32)
    distance = positions[:, None] - key_pos[None, :]
    allowed = (key_pos[None, :] >= 0) & (distance >= 0) & (distance < ATTEND_SPAN)
    allowed = allowed & (positions[:, None] // seq_len == key_pos[None, :] // seq_len)
    allowed = allowed & (segment_own[:, None] == segment_ext[None, :])

    def attention_scores():
        raw = jnp.einsum("qgjd,kgd->gjqk", queries, key_ext, preferred_element_type=F32)
        return jnp.where(allowed[None, None], raw * score_scale, -1e30)

    scores = attention_scores()
    row_top = jnp.max(scores, axis=-1, keepdims=True)
    weights = jnp.exp(scores - row_top)
    row_total = jnp.sum(weights, axis=-1, keepdims=True)
    probability = (weights / row_total).astype(BF16)
    heads_low = (
        jnp.einsum("gjqk,kgd->qgjd", probability, value_ext, preferred_element_type=F32)
        .astype(BF16)
        .reshape(own_rows, -1)
    )
    log_total = row_top + jnp.log(row_total)
    hidden_state = input_wide + dot(heads_low, output_full, ((1,), (1,)))
    second_factor = norm_factor(hidden_state)
    normed_mid_own = (hidden_state * second_factor * second_gain).astype(BF16)

    digits = jnp.stack([cotangent_near[..., width:], cotangent_far[..., width:]])
    digits = digits.astype(jnp.int32).reshape(groups, group_rows, HEAD_SIZE)
    ranked_all = digits[..., :EXPERTS] * 64 + digits[..., EXPERTS : 2 * EXPERTS]
    cotangent_near, cotangent_far = cotangent_near[..., :width], cotangent_far[..., :width]
    routed_all = ranked_all <= pair_count
    expert = lax.axis_index(PLANE)
    own_column = expert_ids == expert
    rank_own = jnp.sum(jnp.where(own_column, ranked_all, 0), axis=-1)
    slot_own = jnp.sum(
        (rank_own[:, None, :] < rank_own[:, :, None]).astype(jnp.int32), axis=-1
    )
    slot_own = jnp.where(rank_own <= pair_count, slot_own, capacity)
    place = (
        slot_own[:, None, :] == jnp.arange(capacity, dtype=jnp.int32)[None, :, None]
    ).astype(BF16)

    normed_near, normed_far = plane_gather(normed_mid_own)
    normed_mid = jnp.concatenate([normed_near, normed_far]).reshape(-1, width)
    logits = dot(normed_mid, router_weight, ((1,), (0,))).reshape(groups, group_rows, EXPERTS)
    logits = jnp.where(routed_all, logits, -1e30)
    gate_weights = jnp.where(
        routed_all, jnp.exp(logits - jnp.max(logits, axis=-1, keepdims=True)), 0.0
    )
    gates = gate_weights / jnp.sum(gate_weights, axis=-1, keepdims=True)
    gate_own = jnp.sum(jnp.where(own_column, gates, 0.0), axis=-1)

    def to_slots(near, far):
        halves_of = [
            jnp.einsum(
                "gct,gtd->gcd",
                place[first : first + 2],
                rows.reshape(2, group_rows, width),
                preferred_element_type=F32,
            ).astype(BF16)
            for first, rows in ((0, near), (2, far))
        ]
        return jnp.concatenate(halves_of).reshape(groups * capacity, width)

    expert_in = to_slots(normed_near, normed_far)
    cotangent_slots = to_slots(cotangent_near, cotangent_far).astype(F32)
    coefficient = jnp.sum(place.astype(F32) * gate_own[:, None, :], axis=-1).reshape(-1, 1)
    gate_pre = dot(expert_in, gate_full, ((1,), (0,)))
    up_pre = dot(expert_in, up_full, ((1,), (0,)))
    sigmoid_gate = jax.nn.sigmoid(gate_pre)
    silu_gate = gate_pre * sigmoid_gate
    expert_hidden = (silu_gate * up_pre).astype(BF16)
    expert_out = dot(expert_hidden, down_full, ((1,), (1,)))
    grad_expert_out = (coefficient * cotangent_slots).astype(BF16)
    grad_hidden = dot(grad_expert_out, down_full, ((1,), (0,)))
    grad_up = (grad_hidden * silu_gate).astype(BF16)
    grad_gate = (
        grad_hidden * up_pre * sigmoid_gate * (1.0 + gate_pre * (1.0 - sigmoid_gate))
    ).astype(BF16)
    grad_expert_in = dot(grad_gate, gate_full, ((1,), (1,))) + dot(grad_up, up_full, ((1,), (1,)))

    def to_tokens(rows, more):
        rows = rows.astype(BF16).reshape(groups, capacity, width)
        sides = []
        for first in (2, 0):
            tokens = jnp.einsum(
                "gct,gcd->gtd",
                place[first : first + 2],
                rows[first : first + 2],
                preferred_element_type=F32,
            )
            if more is not None:
                tokens = tokens + jnp.einsum(
                    "gte,de->gtd",
                    more[first : first + 2].astype(BF16),
                    router_weight,
                    preferred_element_type=F32,
                )
            sides.append(tokens.astype(BF16).reshape(2 * halves, own_rows, width))
        return sides

    grad_gate_slots = jnp.sum(cotangent_slots * expert_out, axis=-1).reshape(groups, capacity)
    grad_gate_tokens = jnp.sum(place.astype(F32) * grad_gate_slots[:, :, None], axis=1)
    grad_logits = (grad_gate_tokens * gate_own)[:, :, None] * (
        own_column.astype(F32)[None, None, :] - gates
    )
    grad_logits = grad_logits.reshape(groups * group_rows, EXPERTS)
    router_part = jnp.dot(normed_mid.astype(F32).T, grad_logits, precision=FULL_PRECISION)
    grad_far, grad_near = to_tokens(
        grad_expert_in, grad_logits.reshape(groups, group_rows, EXPERTS)
    )
    grad_mid_parts = fold_plane(fold_core(grad_near, grad_far))
    gate_part = dot(expert_in, grad_gate, ((0,), (0,))).astype(BF16)
    up_part = dot(expert_in, grad_up, ((0,), (0,))).astype(BF16)
    down_part = dot(grad_expert_out, expert_hidden, ((0,), (0,))).astype(BF16)
    moe_far, moe_near = to_tokens(coefficient * expert_out, None)
    (grad_mid_parts, gate_part, up_part, down_part, moe_far, moe_near) = lax.optimization_barrier(
        (grad_mid_parts, gate_part, up_part, down_part, moe_far, moe_near)
    )
    grad_mid = wide_sum(grad_mid_parts)
    router_part = jnp.pad(router_part.astype(BF16), ((0, 0), (0, HEAD_SIZE - EXPERTS)))
    expert_sums = [
        lax.psum_scatter(part, "outer", scatter_dimension=0, tiled=True)
        for part in (gate_part, up_part, down_part, router_part)
    ]

    norm_input_part = norm_back(hidden_state, second_factor, second_gain, grad_mid)
    grad_state = cotangent.astype(F32) + norm_input_part
    grad_attn = grad_state.astype(BF16)
    grad_heads = dot(grad_attn, output_full, ((1,), (0,))).astype(BF16)
    grad_attn, moe_far, moe_near = lax.optimization_barrier((grad_attn, moe_far, moe_near))
    output_total = fold_columns(grad_attn, heads_low, shard_rows)
    moe_total = fold_core(moe_near, moe_far)
    grad_heads = grad_heads.reshape(queries.shape)
    scores = attention_scores()
    probability = jnp.exp(scores - log_total)
    grad_prob = jnp.einsum("qgjd,kgd->gjqk", grad_heads, value_ext, preferred_element_type=F32)
    row_dot = jnp.sum(probability * grad_prob, axis=-1, keepdims=True)
    grad_scores = (probability * (grad_prob - row_dot)).astype(BF16)
    late_scores, output_total, moe_total = lax.optimization_barrier(
        (grad_scores, output_total, moe_total)
    )
    output_parts = fold_plane(distance_blocks(output_total))
    moe_parts = fold_plane(moe_total)
    grad_queries = (
        jnp.einsum("gjqk,kgd->qgjd", late_scores, key_ext, preferred_element_type=F32)
        * score_scale
    )
    grad_keys = (
        jnp.einsum("gjqk,qgjd->kgd", grad_scores, queries, preferred_element_type=F32)
        * score_scale
    )
    grad_values = jnp.einsum(
        "gjqk,qgjd->kgd", probability.astype(BF16), grad_heads, preferred_element_type=F32
    )
    grad_key_value = jnp.stack([grad_keys, grad_values], axis=2)
    grad_own = grad_key_value[ATTEND_SPAN:]
    for k in range(1, reach + 1):
        first_row = ATTEND_SPAN - k * own_rows
        piece = grad_key_value[first_row : first_row + own_rows].astype(BF16)
        grad_own = grad_own + shift_all(piece, -k).astype(F32)
    grad_query_pre = (
        rotate(grad_queries, cosine_heads, -sine_heads).astype(BF16).reshape(own_rows, -1)
    )
    grad_keys_pre = rotate(grad_own[:, :, :1], cosine_heads, -sine_heads)
    grad_key_value_pre = (
        jnp.concatenate([grad_keys_pre, grad_own[:, :, 1:]], axis=2)
        .astype(BF16)
        .reshape(own_rows, -1)
    )
    grad_qkv_pre = jnp.concatenate(
        [
            grad_query_pre.reshape(own_rows, halves, -1),
            grad_key_value_pre.reshape(own_rows, halves, -1),
        ],
        axis=2,
    ).reshape(own_rows, -1)
    grad_qkv_pre, output_parts, moe_parts, expert_sums = lax.optimization_barrier(
        (grad_qkv_pre, output_parts, moe_parts, expert_sums)
    )
    qkv_total = fold_columns(normed_in, grad_qkv_pre, shard_rows)
    output_weight_grad = outer_scatter(wide_sum(output_parts).astype(BF16))
    block_output = hidden_state + wide_sum(moe_parts)
    qkv_parts = fold_plane(distance_blocks(qkv_total))
    grad_in = dot(grad_query_pre, qkv_full[:, :all_queries], ((1,), (1,))) + dot(
        grad_key_value_pre, qkv_full[:, all_queries:], ((1,), (1,))
    )
    input_grad = grad_state + norm_back(input_wide, first_factor, first_gain, grad_in)
    router_rows = expert_sums[3][:, :EXPERTS].reshape(plane, 1, -1)
    router_rows = jnp.pad(
        router_rows, ((0, 0), (0, 15), (0, half_ff - router_rows.shape[2]))
    )
    expert_sum = jnp.stack(expert_sums[:3]).reshape(3, groups, shard_rows, halves, half_ff)
    expert_sum = jnp.transpose(expert_sum, (1, 3, 0, 2, 4)).reshape(
        plane, 3 * shard_rows, half_ff
    )
    expert_sum = lax.all_to_all(
        jnp.concatenate([expert_sum, router_rows], axis=1), PLANE, 0, 0, tiled=True
    )
    router_grad = jnp.sum(
        expert_sum[:, 3 * shard_rows, : shard_rows // 2 * EXPERTS].astype(F32), axis=0
    ).reshape(shard_rows // 2, EXPERTS)
    expert_sum = expert_sum[:, : 3 * shard_rows].reshape(plane, 3, shard_rows, half_ff)
    expert_grads = jnp.transpose(expert_sum, (1, 2, 0, 3)).astype(F32)
    gate_grad, up_grad, down_grad = expert_grads[0], expert_grads[1], expert_grads[2]

    qkv_grad = outer_scatter(wide_sum(qkv_parts).astype(BF16))
    query_grad = qkv_grad[:, :query_columns]
    key_grad = qkv_grad[:, query_columns : query_columns + HEAD_SIZE]
    value_grad = qkv_grad[:, query_columns + HEAD_SIZE :]

    half_rows = shard_rows // 2
    own_gains = lax.dynamic_slice_in_dim(
        norm_gains, lax.axis_index(DP) * shard_rows, shard_rows, 0
    )
    first_sum = jnp.sum(qkv_grad * qkv_own.astype(F32), axis=-1)
    second_sum = jnp.sum(
        gate_grad * gate_weight.astype(F32) + up_grad * up_weight.astype(F32), axis=(1, 2)
    )
    gain_sums = jnp.stack([first_sum, second_sum], axis=1) / own_gains
    kept = lax.dynamic_slice_in_dim(gain_sums, tensor_index * half_rows, half_rows, 0)
    sent = lax.dynamic_slice_in_dim(gain_sums, (1 - tensor_index) * half_rows, half_rows, 0)
    own_router = lax.dynamic_slice_in_dim(
        router_weight, lax.axis_index(ALL) * half_rows, half_rows, 0
    )
    router_sum = jnp.sum(router_grad * own_router.astype(F32), axis=-1)
    half_gains = lax.dynamic_slice_in_dim(own_gains, tensor_index * half_rows, half_rows, 0)
    router_sum = router_sum / half_gains[:, 1]
    gains_grad = (
        kept
        + swap(sent, "tensor")
        + jnp.stack([jnp.zeros_like(router_sum), router_sum], axis=1)
    )
    return (
        block_output,
        input_grad,
        gains_grad,
        router_grad,
        query_grad,
        key_grad,
        value_grad,
        output_weight_grad,
        gate_grad,
        up_grad,
        down_grad,
    )


def solution(mesh):
    dp_size, tensor_size = mesh.shape["dp"], mesh.shape["tensor"]
    split = Mesh(mesh.devices.reshape(dp_size // 4, 2, 2, tensor_size), ALL)
    return jax.shard_map(
        on_device,
        mesh=split,
        in_specs=(
            P(ALL, None),
            P(),
            P(),
            P(DP, "tensor"),
            P(DP, "tensor"),
            P(DP, "tensor"),
            P(DP, "tensor"),
            P(DP, None, "tensor"),
            P(DP, None, "tensor"),
            P(DP, None, "tensor"),
            P(DP),
            P(DP, None),
            P(DP),
            P(ALL, None),
        ),
        out_specs=(
            P(ALL, None),
            P(ALL, None),
            P(ALL, None),
            P(ALL, None),
            P(DP, "tensor"),
            P(DP, "tensor"),
            P(DP, "tensor"),
            P(DP, "tensor"),
            P(DP, None, "tensor"),
            P(DP, None, "tensor"),
            P(DP, None, "tensor"),
        ),
        check_vma=False,
    )
```

```python
import functools
import math

import jax
import jax.numpy as jnp
from jax import lax
from jax.experimental import pallas as pl
from jax.experimental.pallas import tpu as pltpu
from jax.sharding import Mesh
from jax.sharding import PartitionSpec as P

HEAD_SIZE = 128
TOPK = 4
EXPERTS = 8
ATTEND_SPAN = 1024
SEQ_MOST = 16384
EPSILON = 1e-06
ROPE_BASE = 10000.0
BF16 = jnp.bfloat16
F32 = jnp.float32

DP = ("outer", "x", "core")
PLANE = ("x", "core", "tensor")
ALL = ("outer", "x", "core", "tensor")


def shift_all(x, by):
    length = lax.axis_size(ALL)
    pairs = [(i, i + by) for i in range(length) if 0 <= i + by < length]
    return lax.ppermute(x, ALL, pairs)


def swap(x, axis):
    length = lax.axis_size(axis)
    return lax.ppermute(x, axis, [(i, length - 1 - i) for i in range(length)])


def plane_gather(own):
    near = jnp.stack([own, swap(own, "tensor"), swap(own, "x"), swap(own, ("x", "tensor"))])
    far = swap(near, "core")
    shape = (2, 2) + own.shape
    return near.reshape(shape), far.reshape(shape)


def fold_core(kept, sent):
    return (kept.astype(F32) + swap(sent, "core").astype(F32)).astype(BF16)


def fold_plane(blocks):
    return [
        blocks[0],
        swap(blocks[1], "tensor"),
        swap(blocks[2], "x"),
        swap(blocks[3], ("x", "tensor")),
    ]


def wide_sum(parts):
    return sum(part.astype(F32) for part in parts)


def outer_shift(x, by):
    length = lax.axis_size("outer")
    return lax.ppermute(x, "outer", [(i, (i + by) % length) for i in range(length)])


def outer_gather(shard):
    length, here = lax.axis_size("outer"), lax.axis_index("outer")
    if length > 4:
        return lax.all_gather(shard, "outer")
    full = jnp.zeros((length,) + shard.shape, shard.dtype)
    for by in range(length):
        piece = outer_shift(shard, by) if by else shard
        full = lax.dynamic_update_slice_in_dim(full, piece[None], (here - by) % length, 0)
    return full


def outer_scatter(parts):
    length, here = lax.axis_size("outer"), lax.axis_index("outer")
    if length > 4:
        return lax.psum_scatter(parts, "outer", scatter_dimension=0, tiled=False).astype(F32)
    total = None
    for by in range(length):
        piece = lax.dynamic_index_in_dim(parts, (here + by) % length, 0, keepdims=False)
        piece = (outer_shift(piece, by) if by else piece).astype(F32)
        total = piece if total is None else total + piece
    return total


def core_columns(rows, core_at, shard_rows):
    count = rows.shape[0]
    split = rows.reshape(count, -1, 2, shard_rows)
    return lax.dynamic_index_in_dim(split, core_at, 2, keepdims=False).reshape(count, -1)


def fold_columns(left, right, shard_rows):
    core = lax.axis_index("core")
    sent = dot(core_columns(left, 1 - core, shard_rows), right, ((0,), (0,))).astype(BF16)
    kept = dot(core_columns(left, core, shard_rows), right, ((0,), (0,))).astype(BF16)
    return fold_core(kept, sent).reshape(-1, 2, shard_rows, right.shape[1])


def distance_blocks(total):
    x, tensor = lax.axis_index("x"), lax.axis_index("tensor")
    columns = total.shape[3] // 2
    blocks = []
    for x_by in range(2):
        for tensor_by in range(2):
            block = lax.dynamic_index_in_dim(total, x ^ x_by, 1, keepdims=False)
            start = (tensor ^ tensor_by) * columns
            blocks.append(lax.dynamic_slice_in_dim(block, start, columns, 2))
    return blocks


def rotary_tables(position):
    halfway = HEAD_SIZE // 2
    inverse = jnp.exp(
        jnp.arange(halfway, dtype=F32) * (-2.0 * math.log(ROPE_BASE) / HEAD_SIZE)
    )
    angles = position.astype(F32)[:, None] * inverse[None, :]
    cosine, sine = jnp.cos(angles), jnp.sin(angles)
    return (
        jnp.concatenate([cosine, cosine], axis=1),
        jnp.concatenate([-sine, sine], axis=1),
    )


def norm_factor(value_rows):
    return lax.rsqrt(jnp.mean(value_rows * value_rows, axis=-1, keepdims=True) + EPSILON)


def norm_back(value_rows, factor, gain, upstream):
    weighted = upstream * gain
    return factor * weighted - value_rows * (factor * factor * factor) * jnp.mean(
        weighted * value_rows, axis=-1, keepdims=True
    )


def dot(a, b, dims):
    return lax.dot_general(a, b, (dims, ((), ())), preferred_element_type=F32)


VMEM_LIMIT = 60 * 1024 * 1024
LIGHT = pl.CostEstimate(flops=1000, bytes_accessed=1000, transcendentals=0)
FROM_LAST = (((1,), (1,)), ((), ()))
PLAIN = (((1,), (0,)), ((), ()))


def mxu(a, b, dims=PLAIN):
    return lax.dot_general(a, b, dims, preferred_element_type=F32)


def turn(rows, cosine, sine):
    return rows * cosine + pltpu.roll(rows, HEAD_SIZE // 2, 1) * sine


def project_kernel(rows_ref, weight_ref, cosine_ref, sine_ref, out_ref, *, turned):
    product = mxu(rows_ref[...], weight_ref[...])
    for at, turns in enumerate(turned):
        part = product[:, at * HEAD_SIZE : (at + 1) * HEAD_SIZE]
        if turns:
            part = turn(part, cosine_ref[...], sine_ref[...])
        out_ref[:, at * HEAD_SIZE : (at + 1) * HEAD_SIZE] = part.astype(BF16)


def project(rows, weight, cosine, sine, first, count, turned):
    high, width = rows.shape
    columns = len(turned) * HEAD_SIZE
    return pl.pallas_call(
        functools.partial(project_kernel, turned=turned),
        grid=(count,),
        in_specs=[
            pl.BlockSpec((high, width), lambda j: (0, 0)),
            pl.BlockSpec((width, columns), lambda j: (0, first + j)),
            pl.BlockSpec((high, HEAD_SIZE), lambda j: (0, 0)),
            pl.BlockSpec((high, HEAD_SIZE), lambda j: (0, 0)),
        ],
        out_specs=pl.BlockSpec((high, columns), lambda j: (0, j)),
        out_shape=jax.ShapeDtypeStruct((high, count * columns), BF16),
        compiler_params=pltpu.CompilerParams(vmem_limit_bytes=VMEM_LIMIT),
        cost_estimate=LIGHT,
        name="project",
    )(rows, weight, cosine, sine)


def mask_bias(place_ref, segment_key_ref, segment_query_ref, bias_ref, seq_len):
    span, rows = bias_ref.shape
    start = place_ref[0]
    key_at = lax.broadcasted_iota(jnp.int32, (span, rows), 0)
    query_at = lax.broadcasted_iota(jnp.int32, (span, rows), 1) + ATTEND_SPAN
    distance = query_at - key_at
    position = start + query_at - ATTEND_SPAN
    sequence_at = query_at - lax.rem(position, seq_len)
    allowed = (distance >= 0) & (distance < ATTEND_SPAN) & (key_at >= sequence_at)
    allowed = allowed & (segment_key_ref[...] == segment_query_ref[...])
    bias_ref[...] = jnp.where(allowed, 0.0, -1e30)


def attention_kernel(
    place_ref,
    segment_key_ref,
    segment_query_ref,
    q_ref,
    kv_ref,
    heads_ref,
    lse_ref,
    bias_ref,
    *,
    seq_len,
    scale,
):
    @pl.when(pl.program_id(0) == 0)
    def _():
        mask_bias(place_ref, segment_key_ref, segment_query_ref, bias_ref, seq_len)

    rows = q_ref.shape[0]
    span = kv_ref.shape[0]
    count = q_ref.shape[1] // HEAD_SIZE
    value_t = kv_ref[:, HEAD_SIZE:].T
    chunks = span // rows
    for head in range(count):
        columns = slice(head * HEAD_SIZE, (head + 1) * HEAD_SIZE)
        query = q_ref[:, columns]
        scores = []
        for c in range(chunks):
            part = slice(c * rows, (c + 1) * rows)
            raw = mxu(kv_ref[part, :HEAD_SIZE], query, FROM_LAST)
            scores.append(raw * scale + bias_ref[part, :])
        top = functools.reduce(jnp.maximum, scores)
        top = jnp.max(top, axis=0, keepdims=True)
        total = jnp.zeros_like(top)
        out_t = jnp.zeros((HEAD_SIZE, rows), F32)
        for c in range(chunks):
            weight = jnp.exp(scores[c] - top)
            total = total + jnp.sum(weight, axis=0, keepdims=True)
            out_t = out_t + mxu(value_t[:, c * rows : (c + 1) * rows], weight.astype(BF16))
        heads_ref[:, columns] = (out_t / total).T.astype(BF16)
        lse_ref[0, head : head + 1, :] = top + jnp.log(total)


def attention(place, segment_key, segment_query, queries, key_value, seq_len):
    rows, all_columns = queries.shape
    span = key_value.shape[0]
    pairs = key_value.shape[1] // (2 * HEAD_SIZE)
    columns = all_columns // pairs
    return pl.pallas_call(
        functools.partial(attention_kernel, seq_len=seq_len, scale=1.0 / math.sqrt(HEAD_SIZE)),
        grid=(pairs,),
        in_specs=[
            pl.BlockSpec(memory_space=pltpu.SMEM),
            pl.BlockSpec((span, 1), lambda j: (0, 0)),
            pl.BlockSpec((1, rows), lambda j: (0, 0)),
            pl.BlockSpec((rows, columns), lambda j: (0, j)),
            pl.BlockSpec((span, 2 * HEAD_SIZE), lambda j: (0, j)),
        ],
        out_specs=[
            pl.BlockSpec((rows, columns), lambda j: (0, j)),
            pl.BlockSpec((1, columns // HEAD_SIZE, rows), lambda j: (j, 0, 0)),
        ],
        out_shape=[
            jax.ShapeDtypeStruct((rows, all_columns), BF16),
            jax.ShapeDtypeStruct((pairs, columns // HEAD_SIZE, rows), F32),
        ],
        scratch_shapes=[pltpu.VMEM((span, rows), F32)],
        compiler_params=pltpu.CompilerParams(vmem_limit_bytes=VMEM_LIMIT),
        cost_estimate=LIGHT,
        name="attention",
    )(place, segment_key, segment_query, queries, key_value)


def attention_back_kernel(
    place_ref,
    segment_key_ref,
    segment_query_ref,
    q_ref,
    kv_ref,
    lse_ref,
    dout_ref,
    cosine_ref,
    sine_ref,
    dq_ref,
    dkv_far_ref,
    dkv_own_ref,
    bias_ref,
    dkv_ref,
    *,
    seq_len,
    scale,
):
    @pl.when(pl.program_id(0) == 0)
    def _():
        mask_bias(place_ref, segment_key_ref, segment_query_ref, bias_ref, seq_len)

    rows = q_ref.shape[0]
    span = kv_ref.shape[0]
    count = q_ref.shape[1] // HEAD_SIZE
    key_t = kv_ref[:, :HEAD_SIZE].T
    chunks = span // rows
    dkv_ref[...] = jnp.zeros_like(dkv_ref)
    for head in range(count):
        columns = slice(head * HEAD_SIZE, (head + 1) * HEAD_SIZE)
        query = q_ref[:, columns]
        dout = dout_ref[:, columns]
        lse = lse_ref[0, head : head + 1, :]
        probs, dprobs = [], []
        row_dot = jnp.zeros_like(lse)
        for c in range(chunks):
            part = slice(c * rows, (c + 1) * rows)
            raw = mxu(kv_ref[part, :HEAD_SIZE], query, FROM_LAST)
            prob = jnp.exp(raw * scale + bias_ref[part, :] - lse)
            dprob = mxu(kv_ref[part, HEAD_SIZE:], dout, FROM_LAST)
            row_dot = row_dot + jnp.sum(prob * dprob, axis=0, keepdims=True)
            probs.append(prob)
            dprobs.append(dprob)
        dq_t = jnp.zeros((HEAD_SIZE, rows), F32)
        for c in range(chunks):
            part = slice(c * rows, (c + 1) * rows)
            dscore = (probs[c] * (dprobs[c] - row_dot)).astype(BF16)
            dkv_ref[part, :HEAD_SIZE] += mxu(dscore, query)
            dkv_ref[part, HEAD_SIZE:] += mxu(probs[c].astype(BF16), dout)
            dq_t = dq_t + mxu(key_t[:, part], dscore)
        dq_ref[:, columns] = turn(dq_t.T * scale, cosine_ref[...], -sine_ref[...]).astype(BF16)
    dkv_ref[:, :HEAD_SIZE] = dkv_ref[:, :HEAD_SIZE] * scale
    dkv_far_ref[...] = dkv_ref[: span - rows, :].astype(BF16)
    dkv_own_ref[...] = dkv_ref[span - rows :, :]


def attention_back(
    place, segment_key, segment_query, queries, key_value, lse, dout, cosine, sine, seq_len
):
    rows, all_columns = queries.shape
    span = key_value.shape[0]
    pairs = key_value.shape[1] // (2 * HEAD_SIZE)
    columns = all_columns // pairs
    return pl.pallas_call(
        functools.partial(
            attention_back_kernel, seq_len=seq_len, scale=1.0 / math.sqrt(HEAD_SIZE)
        ),
        grid=(pairs,),
        in_specs=[
            pl.BlockSpec(memory_space=pltpu.SMEM),
            pl.BlockSpec((span, 1), lambda j: (0, 0)),
            pl.BlockSpec((1, rows), lambda j: (0, 0)),
            pl.BlockSpec((rows, columns), lambda j: (0, j)),
            pl.BlockSpec((span, 2 * HEAD_SIZE), lambda j: (0, j)),
            pl.BlockSpec((1, columns // HEAD_SIZE, rows), lambda j: (j, 0, 0)),
            pl.BlockSpec((rows, columns), lambda j: (0, j)),
            pl.BlockSpec((rows, HEAD_SIZE), lambda j: (0, 0)),
            pl.BlockSpec((rows, HEAD_SIZE), lambda j: (0, 0)),
        ],
        out_specs=[
            pl.BlockSpec((rows, columns), lambda j: (0, j)),
            pl.BlockSpec((span - rows, 2 * HEAD_SIZE), lambda j: (0, j)),
            pl.BlockSpec((rows, 2 * HEAD_SIZE), lambda j: (0, j)),
        ],
        out_shape=[
            jax.ShapeDtypeStruct((rows, all_columns), BF16),
            jax.ShapeDtypeStruct((span - rows, key_value.shape[1]), BF16),
            jax.ShapeDtypeStruct((rows, key_value.shape[1]), F32),
        ],
        scratch_shapes=[
            pltpu.VMEM((span, rows), F32),
            pltpu.VMEM((span, 2 * HEAD_SIZE), F32),
        ],
        compiler_params=pltpu.CompilerParams(vmem_limit_bytes=VMEM_LIMIT),
        cost_estimate=LIGHT,
        name="attention_back",
    )(place, segment_key, segment_query, queries, key_value, lse, dout, cosine, sine)


def expert_kernel(
    slot_row_ref,
    slot_column_ref,
    routed_ref,
    own_ref,
    router_ref,
    tokens_ref,
    cotangent_ref,
    gate_ref,
    up_ref,
    down_ref,
    grad_ref,
    moe_ref,
    rows_in_ref,
    grad_out_ref,
    hidden_ref,
    grad_gate_ref,
    grad_up_ref,
    router_grad_ref,
    *,
    capacity,
):
    group_rows = tokens_ref.shape[1]
    tokens = tokens_ref[0]
    cotangent = cotangent_ref[0]
    routed = routed_ref[0] > 0.0
    logits = jnp.where(routed, mxu(router_ref[...], tokens, FROM_LAST), -1e30)
    weights = jnp.exp(logits - jnp.max(logits, axis=0, keepdims=True))
    weights = jnp.where(routed, weights, 0.0)
    gates = weights / jnp.sum(weights, axis=0, keepdims=True)
    own = own_ref[...]
    gate_own = jnp.sum(gates * own, axis=0, keepdims=True)
    place = slot_row_ref[0] == lax.broadcasted_iota(jnp.int32, (capacity, group_rows), 0)
    place_wide = jnp.where(place, 1.0, 0.0)
    place_low = place_wide.astype(BF16)
    back = slot_column_ref[0] == lax.broadcasted_iota(jnp.int32, (group_rows, capacity), 1)
    back_low = jnp.where(back, 1.0, 0.0).astype(BF16)
    coefficient = jnp.sum(place_wide * gate_own, axis=1, keepdims=True)

    rows_in = mxu(place_low, tokens).astype(BF16)
    rows_in_ref[...] = rows_in
    gate_pre = mxu(rows_in, gate_ref[...])
    up_pre = mxu(rows_in, up_ref[...])
    sigmoid = 1.0 / (1.0 + jnp.exp(-gate_pre))
    silu = gate_pre * sigmoid
    hidden = (silu * up_pre).astype(BF16)
    hidden_ref[...] = hidden
    slot_cotangent = mxu(place_low, cotangent)
    grad_out = (coefficient * slot_cotangent).astype(BF16)
    grad_out_ref[...] = grad_out
    grad_hidden = mxu(grad_out, down_ref[...])
    grad_up = (grad_hidden * silu).astype(BF16)
    grad_gate = (grad_hidden * up_pre * sigmoid * (1.0 + gate_pre * (1.0 - sigmoid))).astype(BF16)
    grad_up_ref[...] = grad_up
    grad_gate_ref[...] = grad_gate
    expert_out = mxu(hidden, down_ref[...], FROM_LAST)
    grad_slot = jnp.sum(slot_cotangent * expert_out, axis=1, keepdims=True)
    moe_ref[0] = mxu(back_low, (coefficient * expert_out).astype(BF16)).astype(BF16)

    grad_token = jnp.sum(place_wide * grad_slot, axis=0, keepdims=True)
    share = (grad_token * gate_own) * (own - gates)
    share_high = share.astype(BF16)
    share_low = (share - share_high.astype(F32)).astype(BF16)
    router_grad = mxu(share_high, tokens) + mxu(share_low, tokens)

    @pl.when(pl.program_id(0) == 0)
    def _():
        router_grad_ref[...] = router_grad

    @pl.when(pl.program_id(0) > 0)
    def _():
        router_grad_ref[...] += router_grad

    grad_in = mxu(grad_gate, gate_ref[...], FROM_LAST) + mxu(grad_up, up_ref[...], FROM_LAST)
    grad_ref[0] = (
        mxu(back_low, grad_in.astype(BF16)) + mxu(share.T.astype(BF16), router_ref[...])
    ).astype(BF16)


def expert_groups(slot, routed, own, router_t, tokens, cotangent, gate, up, down, capacity):
    count, group_rows, width = tokens.shape
    ff = gate.shape[1]
    experts = router_t.shape[0]
    whole = lambda g: (0, 0)
    by_group = lambda g: (g, 0, 0)
    slots = lambda columns: pl.BlockSpec((capacity, columns), lambda g: (g, 0))
    slots_shape = lambda columns: jax.ShapeDtypeStruct((count * capacity, columns), BF16)
    return pl.pallas_call(
        functools.partial(expert_kernel, capacity=capacity),
        grid=(count,),
        in_specs=[
            pl.BlockSpec((1, 1, group_rows), by_group),
            pl.BlockSpec((1, group_rows, 1), by_group),
            pl.BlockSpec((1, experts, group_rows), by_group),
            pl.BlockSpec((experts, 1), whole),
            pl.BlockSpec((experts, width), whole),
            pl.BlockSpec((1, group_rows, width), by_group),
            pl.BlockSpec((1, group_rows, width), by_group),
            pl.BlockSpec((width, ff), whole),
            pl.BlockSpec((width, ff), whole),
            pl.BlockSpec((width, ff), whole),
        ],
        out_specs=[
            pl.BlockSpec((1, group_rows, width), by_group),
            pl.BlockSpec((1, group_rows, width), by_group),
            slots(width),
            slots(width),
            slots(ff),
            slots(ff),
            slots(ff),
            pl.BlockSpec((experts, width), whole),
        ],
        out_shape=[
            jax.ShapeDtypeStruct(tokens.shape, BF16),
            jax.ShapeDtypeStruct(tokens.shape, BF16),
            slots_shape(width),
            slots_shape(width),
            slots_shape(ff),
            slots_shape(ff),
            slots_shape(ff),
            jax.ShapeDtypeStruct((experts, width), F32),
        ],
        compiler_params=pltpu.CompilerParams(vmem_limit_bytes=VMEM_LIMIT),
        cost_estimate=LIGHT,
        name="expert",
    )(
        slot[:, None, :],
        slot[:, :, None],
        routed,
        own,
        router_t,
        tokens,
        cotangent,
        gate,
        up,
        down,
    )


def on_device(
    block_input,
    norm_gains,
    router_weight,
    query_matrix,
    key_matrix,
    value_matrix,
    output_weight,
    gate_weight,
    up_weight,
    down_weight,
    segment_ids,
    routes,
    priority,
    cotangent,
):
    tensor_index = lax.axis_index("tensor")
    own_rows, width = block_input.shape
    group_rows = segment_ids.shape[0]
    halves = lax.axis_size("tensor")
    outer = lax.axis_size("outer")
    groups = lax.axis_size("x") * lax.axis_size("core")
    plane = groups * halves
    shard_rows = query_matrix.shape[0]
    dp_size = outer * groups
    seq_len = min(SEQ_MOST, group_rows * dp_size)
    own_start = lax.axis_index(ALL) * own_rows
    capacity = group_rows * TOPK // EXPERTS
    reach = ATTEND_SPAN // own_rows
    half_ff = gate_weight.shape[2]
    ff = half_ff * halves

    query_columns = query_matrix.shape[1]
    first = tensor_index == 0
    qkv_own = jnp.concatenate([query_matrix, key_matrix, value_matrix], axis=1)
    qkv_other = swap(qkv_own, "tensor")
    qkv_first = jnp.where(first, qkv_own, qkv_other)
    qkv_second = jnp.where(first, qkv_other, qkv_own)
    qkv_shard = jnp.concatenate(
        [
            qkv_first[:, :query_columns],
            qkv_second[:, :query_columns],
            qkv_first[:, query_columns:],
            qkv_second[:, query_columns:],
        ],
        axis=1,
    )
    earlier_groups = (ATTEND_SPAN + group_rows - 1) // group_rows
    group_pairs = [
        [(i, i + k) for i in range(dp_size - k)] for k in range(earlier_groups, 0, -1)
    ]
    segment_near = jnp.concatenate(
        [lax.ppermute(segment_ids, DP, pairs) for pairs in group_pairs] + [segment_ids]
    )
    qkv_shard, segment_near, gate_own, up_own, down_own = lax.optimization_barrier(
        (qkv_shard, segment_near, gate_weight, up_weight, down_weight)
    )
    qkv_full = lax.all_gather(qkv_shard, DP, axis=0, tiled=True)

    expert_shard = jnp.transpose(jnp.stack([gate_own, up_own, down_own]), (2, 0, 1, 3))
    expert_shard = lax.all_to_all(expert_shard, PLANE, 0, 0, tiled=True)
    expert_shard, output_own = lax.optimization_barrier((expert_shard, output_weight))
    expert_shard = expert_shard.reshape(groups, halves, 3, shard_rows, half_ff)
    expert_shard = jnp.transpose(expert_shard, (2, 0, 3, 1, 4)).reshape(
        3, groups * shard_rows, ff
    )
    gate_up = lax.all_gather(expert_shard[:2], "outer", axis=1, tiled=True)
    gate_full, up_full = gate_up[0], gate_up[1]
    down_full = outer_gather(expert_shard[2]).reshape(width, ff)

    near, far = plane_gather(outer_gather(output_own))
    pieces = jnp.stack([near, far])
    x_index, core_index = lax.axis_index("x"), lax.axis_index("core")

    def piece_at(x_at, core_at, tensor_at):
        piece = lax.dynamic_index_in_dim(pieces, core_index ^ core_at, 0, keepdims=False)
        piece = lax.dynamic_index_in_dim(piece, x_index ^ x_at, 0, keepdims=False)
        return lax.dynamic_index_in_dim(piece, tensor_index ^ tensor_at, 0, keepdims=False)

    output_full = jnp.concatenate(
        [
            jnp.stack([piece_at(x_at, core_at, at) for x_at in range(2) for core_at in range(2)], 1)
            for at in range(2)
        ],
        axis=-1,
    ).reshape(width, -1)

    pair_count = group_rows * TOPK
    rank = (
        jnp.zeros((pair_count,), jnp.int32)
        .at[priority]
        .set(jnp.arange(pair_count, dtype=jnp.int32))
        .reshape(group_rows, TOPK)
    )
    expert_ids = jnp.arange(EXPERTS, dtype=jnp.int32)
    named = routes[:, :, None] == expert_ids[None, None, :]
    ranked = jnp.sum(jnp.where(named, rank[:, :, None] + 1, 0), axis=1)
    ranked = jnp.where(ranked > 0, ranked, pair_count + 1)
    ranked_own = lax.dynamic_slice_in_dim(ranked, tensor_index * own_rows, own_rows, 0)
    digits = jnp.concatenate([ranked_own // 64, ranked_own % 64], axis=1).astype(BF16)
    digits = jnp.pad(digits, ((0, 0), (0, HEAD_SIZE - digits.shape[1])))
    cotangent_sent = jnp.concatenate([cotangent, digits], axis=1)
    input_wide = block_input.astype(F32)
    first_gain = norm_gains[:, 0]
    second_gain = norm_gains[:, 1]
    first_factor = norm_factor(input_wide)
    normed_in = (input_wide * first_factor * first_gain).astype(BF16)
    positions = own_start + jnp.arange(own_rows, dtype=jnp.int32)
    cosine, sine = rotary_tables(positions % seq_len)
    all_queries = halves * query_columns
    query_blocks = all_queries // (2 * HEAD_SIZE)
    key_value_own = project(
        normed_in, qkv_full, cosine, sine, query_blocks, halves, (True, False)
    )
    queries = project(normed_in, qkv_full, cosine, sine, 0, query_blocks, (True, True))
    queries, cotangent_sent = lax.optimization_barrier((queries, cotangent_sent))
    cotangent_near, cotangent_far = plane_gather(cotangent_sent)
    pieces = [shift_all(key_value_own, k) for k in range(reach, 0, -1)] + [key_value_own]
    key_value = jnp.concatenate(pieces, axis=0)
    span = ATTEND_SPAN + own_rows
    segment_ext = lax.dynamic_slice_in_dim(segment_near, tensor_index * own_rows, span)
    view = (
        jnp.reshape(own_start, (1,)),
        segment_ext[:, None],
        segment_ext[None, ATTEND_SPAN:],
        queries,
        key_value,
    )
    heads_low, log_total = attention(*view, seq_len)
    hidden_state = input_wide + dot(heads_low, output_full, ((1,), (1,)))
    second_factor = norm_factor(hidden_state)
    normed_mid_own = (hidden_state * second_factor * second_gain).astype(BF16)

    normed_near, normed_far = plane_gather(normed_mid_own)
    expert = lax.axis_index(PLANE)
    own_expert = (expert_ids == expert).astype(F32)[:, None]
    router_t = router_weight.T

    def experts_on(tokens, cotangents):
        digits = cotangents[..., width:].reshape(2, group_rows, HEAD_SIZE).astype(jnp.int32)
        ranked_all = digits[..., :EXPERTS] * 64 + digits[..., EXPERTS : 2 * EXPERTS]
        routed = jnp.swapaxes((ranked_all <= pair_count).astype(F32), 1, 2)
        rank_own = jnp.sum(jnp.where(expert_ids == expert, ranked_all, 0), axis=-1)
        earlier = (rank_own[:, None, :] < rank_own[:, :, None]).astype(jnp.int32)
        slot = jnp.where(rank_own <= pair_count, jnp.sum(earlier, axis=-1), capacity)
        return expert_groups(
            slot,
            routed,
            own_expert,
            router_t,
            tokens.reshape(2, group_rows, width),
            cotangents.reshape(2, group_rows, -1),
            gate_full,
            up_full,
            down_full,
            capacity,
        )

    on_near = experts_on(normed_near, cotangent_near)
    on_far = experts_on(normed_far, cotangent_far)
    blocks = (2 * halves, own_rows, width)
    (grad_near, moe_near), (grad_far, moe_far) = (
        [array.reshape(blocks) for array in side[:2]] for side in (on_near, on_far)
    )
    grad_mid_parts = fold_plane(fold_core(grad_near, grad_far))

    def over_slots(left, right):
        near = dot(on_near[left], on_near[right], ((0,), (0,)))
        return (near + dot(on_far[left], on_far[right], ((0,), (0,)))).astype(BF16)

    rows_at, grad_out_at, hidden_at, grad_gate_at, grad_up_at = range(2, 7)
    gate_part = over_slots(rows_at, grad_gate_at)
    up_part = over_slots(rows_at, grad_up_at)
    down_part = over_slots(grad_out_at, hidden_at)
    router_part = (on_near[7] + on_far[7]).T
    (grad_mid_parts, gate_part, up_part, down_part, moe_far, moe_near) = lax.optimization_barrier(
        (grad_mid_parts, gate_part, up_part, down_part, moe_far, moe_near)
    )
    grad_mid = wide_sum(grad_mid_parts)
    router_part = jnp.pad(router_part.astype(BF16), ((0, 0), (0, HEAD_SIZE - EXPERTS)))
    expert_sums = [
        lax.psum_scatter(part, "outer", scatter_dimension=0, tiled=True)
        for part in (gate_part, up_part, down_part, router_part)
    ]

    norm_input_part = norm_back(hidden_state, second_factor, second_gain, grad_mid)
    grad_state = cotangent.astype(F32) + norm_input_part
    grad_attn = grad_state.astype(BF16)
    grad_heads = dot(grad_attn, output_full, ((1,), (0,))).astype(BF16)
    grad_attn, moe_far, moe_near = lax.optimization_barrier((grad_attn, moe_far, moe_near))
    output_total = fold_columns(grad_attn, heads_low, shard_rows)
    moe_total = fold_core(moe_near, moe_far)
    grad_query_pre, grad_far_kv, grad_own = attention_back(
        *view, log_total, grad_heads, cosine, sine, seq_len
    )
    grad_far_kv, output_total, moe_total = lax.optimization_barrier(
        (grad_far_kv, output_total, moe_total)
    )
    output_parts = fold_plane(distance_blocks(output_total))
    moe_parts = fold_plane(moe_total)
    for k in range(1, reach + 1):
        first_row = ATTEND_SPAN - k * own_rows
        piece = grad_far_kv[first_row : first_row + own_rows]
        grad_own = grad_own + shift_all(piece, -k).astype(F32)
    grad_key_value = []
    for half in range(halves):
        start = half * 2 * HEAD_SIZE
        key_part = grad_own[:, start : start + HEAD_SIZE]
        turned = jnp.concatenate(
            [key_part[:, HEAD_SIZE // 2 :], key_part[:, : HEAD_SIZE // 2]], axis=1
        )
        grad_key_value.append(key_part * cosine - turned * sine)
        grad_key_value.append(grad_own[:, start + HEAD_SIZE : start + 2 * HEAD_SIZE])
    grad_key_value_pre = jnp.concatenate(grad_key_value, axis=1).astype(BF16)
    grad_qkv_pre = jnp.concatenate(
        [
            grad_query_pre.reshape(own_rows, halves, -1),
            grad_key_value_pre.reshape(own_rows, halves, -1),
        ],
        axis=2,
    ).reshape(own_rows, -1)
    grad_qkv_pre, output_parts, moe_parts, expert_sums = lax.optimization_barrier(
        (grad_qkv_pre, output_parts, moe_parts, expert_sums)
    )
    qkv_total = fold_columns(normed_in, grad_qkv_pre, shard_rows)
    output_weight_grad = outer_scatter(wide_sum(output_parts).astype(BF16))
    block_output = hidden_state + wide_sum(moe_parts)
    qkv_parts = fold_plane(distance_blocks(qkv_total))
    grad_in = dot(grad_query_pre, qkv_full[:, :all_queries], ((1,), (1,))) + dot(
        grad_key_value_pre, qkv_full[:, all_queries:], ((1,), (1,))
    )
    input_grad = grad_state + norm_back(input_wide, first_factor, first_gain, grad_in)
    router_rows = expert_sums[3][:, :EXPERTS].reshape(plane, 1, -1)
    router_rows = jnp.pad(
        router_rows, ((0, 0), (0, 15), (0, half_ff - router_rows.shape[2]))
    )
    expert_sum = jnp.stack(expert_sums[:3]).reshape(3, groups, shard_rows, halves, half_ff)
    expert_sum = jnp.transpose(expert_sum, (1, 3, 0, 2, 4)).reshape(
        plane, 3 * shard_rows, half_ff
    )
    expert_sum = lax.all_to_all(
        jnp.concatenate([expert_sum, router_rows], axis=1), PLANE, 0, 0, tiled=True
    )
    router_grad = jnp.sum(
        expert_sum[:, 3 * shard_rows, : shard_rows // 2 * EXPERTS].astype(F32), axis=0
    ).reshape(shard_rows // 2, EXPERTS)
    expert_sum = expert_sum[:, : 3 * shard_rows].reshape(plane, 3, shard_rows, half_ff)
    expert_grads = jnp.transpose(expert_sum, (1, 2, 0, 3)).astype(F32)
    gate_grad, up_grad, down_grad = expert_grads[0], expert_grads[1], expert_grads[2]

    qkv_grad = outer_scatter(wide_sum(qkv_parts).astype(BF16))
    query_grad = qkv_grad[:, :query_columns]
    key_grad = qkv_grad[:, query_columns : query_columns + HEAD_SIZE]
    value_grad = qkv_grad[:, query_columns + HEAD_SIZE :]

    half_rows = shard_rows // 2
    own_gains = lax.dynamic_slice_in_dim(
        norm_gains, lax.axis_index(DP) * shard_rows, shard_rows, 0
    )
    first_sum = jnp.sum(qkv_grad * qkv_own.astype(F32), axis=-1)
    second_sum = jnp.sum(
        gate_grad * gate_weight.astype(F32) + up_grad * up_weight.astype(F32), axis=(1, 2)
    )
    gain_sums = jnp.stack([first_sum, second_sum], axis=1) / own_gains
    kept = lax.dynamic_slice_in_dim(gain_sums, tensor_index * half_rows, half_rows, 0)
    sent = lax.dynamic_slice_in_dim(gain_sums, (1 - tensor_index) * half_rows, half_rows, 0)
    own_router = lax.dynamic_slice_in_dim(
        router_weight, lax.axis_index(ALL) * half_rows, half_rows, 0
    )
    router_sum = jnp.sum(router_grad * own_router.astype(F32), axis=-1)
    half_gains = lax.dynamic_slice_in_dim(own_gains, tensor_index * half_rows, half_rows, 0)
    router_sum = router_sum / half_gains[:, 1]
    gains_grad = (
        kept
        + swap(sent, "tensor")
        + jnp.stack([jnp.zeros_like(router_sum), router_sum], axis=1)
    )
    return (
        block_output,
        input_grad,
        gains_grad,
        router_grad,
        query_grad,
        key_grad,
        value_grad,
        output_weight_grad,
        gate_grad,
        up_grad,
        down_grad,
    )


def solution(mesh):
    dp_size, tensor_size = mesh.shape["dp"], mesh.shape["tensor"]
    split = Mesh(mesh.devices.reshape(dp_size // 4, 2, 2, tensor_size), ALL)
    return jax.shard_map(
        on_device,
        mesh=split,
        in_specs=(
            P(ALL, None),
            P(),
            P(),
            P(DP, "tensor"),
            P(DP, "tensor"),
            P(DP, "tensor"),
            P(DP, "tensor"),
            P(DP, None, "tensor"),
            P(DP, None, "tensor"),
            P(DP, None, "tensor"),
            P(DP),
            P(DP, None),
            P(DP),
            P(ALL, None),
        ),
        out_specs=(
            P(ALL, None),
            P(ALL, None),
            P(ALL, None),
            P(ALL, None),
            P(DP, "tensor"),
            P(DP, "tensor"),
            P(DP, "tensor"),
            P(DP, "tensor"),
            P(DP, None, "tensor"),
            P(DP, None, "tensor"),
            P(DP, None, "tensor"),
        ),
        check_vma=False,
    )
```

```python
import functools
import math

import jax
import jax.numpy as jnp
from jax import lax
from jax.experimental import pallas as pl
from jax.experimental.pallas import tpu as pltpu
from jax.sharding import Mesh
from jax.sharding import PartitionSpec as P

HEAD_SIZE = 128
TOPK = 4
EXPERTS = 8
ATTEND_SPAN = 1024
SEQ_MOST = 16384
EPSILON = 1e-06
ROPE_BASE = 10000.0
BF16 = jnp.bfloat16
F32 = jnp.float32

DP = ("outer", "x", "core")
PLANE = ("x", "core", "tensor")
ALL = ("outer", "x", "core", "tensor")


def shift_all(x, by):
    length = lax.axis_size(ALL)
    pairs = [(i, i + by) for i in range(length) if 0 <= i + by < length]
    return lax.ppermute(x, ALL, pairs)


def swap(x, axis):
    length = lax.axis_size(axis)
    return lax.ppermute(x, axis, [(i, length - 1 - i) for i in range(length)])


def plane_near(own):
    near = jnp.stack([own, swap(own, "tensor"), swap(own, "x"), swap(own, ("x", "tensor"))])
    return near.reshape((2, 2) + own.shape)


def plane_gather(own):
    near = plane_near(own)
    return near, swap(near, "core")


def fold_core(kept, sent):
    return (kept.astype(F32) + swap(sent, "core").astype(F32)).astype(BF16)


def fold_plane(blocks):
    return [
        blocks[0],
        swap(blocks[1], "tensor"),
        swap(blocks[2], "x"),
        swap(blocks[3], ("x", "tensor")),
    ]


def wide_sum(parts):
    return sum(part.astype(F32) for part in parts)


def outer_shift(x, by):
    length = lax.axis_size("outer")
    return lax.ppermute(x, "outer", [(i, (i + by) % length) for i in range(length)])


def outer_gather(shard):
    length, here = lax.axis_size("outer"), lax.axis_index("outer")
    if length > 4:
        return lax.all_gather(shard, "outer")
    full = jnp.zeros((length,) + shard.shape, shard.dtype)
    for by in range(length):
        piece = outer_shift(shard, by) if by else shard
        full = lax.dynamic_update_slice_in_dim(full, piece[None], (here - by) % length, 0)
    return full


def outer_scatter(parts):
    length, here = lax.axis_size("outer"), lax.axis_index("outer")
    if length > 4:
        return lax.psum_scatter(parts, "outer", scatter_dimension=0, tiled=False).astype(F32)
    total = None
    for by in range(length):
        piece = lax.dynamic_index_in_dim(parts, (here + by) % length, 0, keepdims=False)
        piece = (outer_shift(piece, by) if by else piece).astype(F32)
        total = piece if total is None else total + piece
    return total


def core_columns(rows, core_at, shard_rows):
    count = rows.shape[0]
    split = rows.reshape(count, -1, 2, shard_rows)
    return lax.dynamic_index_in_dim(split, core_at, 2, keepdims=False).reshape(count, -1)


def fold_columns(left, right, shard_rows):
    core = lax.axis_index("core")
    sent = dot(core_columns(left, 1 - core, shard_rows), right, ((0,), (0,))).astype(BF16)
    kept = dot(core_columns(left, core, shard_rows), right, ((0,), (0,))).astype(BF16)
    return fold_core(kept, sent).reshape(-1, 2, shard_rows, right.shape[1])


def distance_blocks(total):
    x, tensor = lax.axis_index("x"), lax.axis_index("tensor")
    columns = total.shape[3] // 2
    blocks = []
    for x_by in range(2):
        for tensor_by in range(2):
            block = lax.dynamic_index_in_dim(total, x ^ x_by, 1, keepdims=False)
            start = (tensor ^ tensor_by) * columns
            blocks.append(lax.dynamic_slice_in_dim(block, start, columns, 2))
    return blocks


def rotary_tables(position):
    halfway = HEAD_SIZE // 2
    inverse = jnp.exp(
        jnp.arange(halfway, dtype=F32) * (-2.0 * math.log(ROPE_BASE) / HEAD_SIZE)
    )
    angles = position.astype(F32)[:, None] * inverse[None, :]
    cosine, sine = jnp.cos(angles), jnp.sin(angles)
    return (
        jnp.concatenate([cosine, cosine], axis=1),
        jnp.concatenate([-sine, sine], axis=1),
    )


def norm_factor(value_rows):
    return lax.rsqrt(jnp.mean(value_rows * value_rows, axis=-1, keepdims=True) + EPSILON)


def norm_back(value_rows, factor, gain, upstream):
    weighted = upstream * gain
    return factor * weighted - value_rows * (factor * factor * factor) * jnp.mean(
        weighted * value_rows, axis=-1, keepdims=True
    )


def dot(a, b, dims):
    return lax.dot_general(a, b, (dims, ((), ())), preferred_element_type=F32)


VMEM_LIMIT = 60 * 1024 * 1024
LIGHT = pl.CostEstimate(flops=1000, bytes_accessed=1000, transcendentals=0)
FROM_LAST = (((1,), (1,)), ((), ()))
PLAIN = (((1,), (0,)), ((), ()))


def mxu(a, b, dims=PLAIN):
    return lax.dot_general(a, b, dims, preferred_element_type=F32)


def turn(rows, cosine, sine):
    return rows * cosine + pltpu.roll(rows, HEAD_SIZE // 2, 1) * sine


def project_kernel(rows_ref, weight_ref, cosine_ref, sine_ref, out_ref, *, turned):
    product = mxu(rows_ref[...], weight_ref[...])
    for at, turns in enumerate(turned):
        part = product[:, at * HEAD_SIZE : (at + 1) * HEAD_SIZE]
        if turns:
            part = turn(part, cosine_ref[...], sine_ref[...])
        out_ref[:, at * HEAD_SIZE : (at + 1) * HEAD_SIZE] = part.astype(BF16)


def project(rows, weight, cosine, sine, first, count, turned):
    high, width = rows.shape
    columns = len(turned) * HEAD_SIZE
    return pl.pallas_call(
        functools.partial(project_kernel, turned=turned),
        grid=(count,),
        in_specs=[
            pl.BlockSpec((high, width), lambda j: (0, 0)),
            pl.BlockSpec((width, columns), lambda j: (0, first + j)),
            pl.BlockSpec((high, HEAD_SIZE), lambda j: (0, 0)),
            pl.BlockSpec((high, HEAD_SIZE), lambda j: (0, 0)),
        ],
        out_specs=pl.BlockSpec((high, columns), lambda j: (0, j)),
        out_shape=jax.ShapeDtypeStruct((high, count * columns), BF16),
        compiler_params=pltpu.CompilerParams(vmem_limit_bytes=VMEM_LIMIT),
        cost_estimate=LIGHT,
        name="project",
    )(rows, weight, cosine, sine)


def mask_bias(place_ref, segment_key_ref, segment_query_ref, bias_ref, seq_len):
    span, rows = bias_ref.shape
    start = place_ref[0]
    key_at = lax.broadcasted_iota(jnp.int32, (span, rows), 0)
    query_at = lax.broadcasted_iota(jnp.int32, (span, rows), 1) + ATTEND_SPAN
    distance = query_at - key_at
    position = start + query_at - ATTEND_SPAN
    sequence_at = query_at - lax.rem(position, seq_len)
    allowed = (distance >= 0) & (distance < ATTEND_SPAN) & (key_at >= sequence_at)
    allowed = allowed & (segment_key_ref[...] == segment_query_ref[...])
    bias_ref[...] = jnp.where(allowed, 0.0, -1e30)


def attention_kernel(
    place_ref,
    segment_key_ref,
    segment_query_ref,
    q_ref,
    kv_ref,
    heads_ref,
    lse_ref,
    bias_ref,
    *,
    seq_len,
    scale,
):
    @pl.when(pl.program_id(0) == 0)
    def _():
        mask_bias(place_ref, segment_key_ref, segment_query_ref, bias_ref, seq_len)

    rows = q_ref.shape[0]
    span = kv_ref.shape[0]
    count = q_ref.shape[1] // HEAD_SIZE
    value_t = kv_ref[:, HEAD_SIZE:].T
    chunks = span // rows
    for head in range(count):
        columns = slice(head * HEAD_SIZE, (head + 1) * HEAD_SIZE)
        query = q_ref[:, columns]
        scores = []
        for c in range(chunks):
            part = slice(c * rows, (c + 1) * rows)
            raw = mxu(kv_ref[part, :HEAD_SIZE], query, FROM_LAST)
            scores.append(raw * scale + bias_ref[part, :])
        top = functools.reduce(jnp.maximum, scores)
        top = jnp.max(top, axis=0, keepdims=True)
        total = jnp.zeros_like(top)
        out_t = jnp.zeros((HEAD_SIZE, rows), F32)
        for c in range(chunks):
            weight = jnp.exp(scores[c] - top)
            total = total + jnp.sum(weight, axis=0, keepdims=True)
            out_t = out_t + mxu(value_t[:, c * rows : (c + 1) * rows], weight.astype(BF16))
        heads_ref[:, columns] = (out_t / total).T.astype(BF16)
        lse_ref[0, head : head + 1, :] = top + jnp.log(total)


def attention(place, segment_key, segment_query, queries, key_value, seq_len):
    rows, all_columns = queries.shape
    span = key_value.shape[0]
    pairs = key_value.shape[1] // (2 * HEAD_SIZE)
    columns = all_columns // pairs
    return pl.pallas_call(
        functools.partial(attention_kernel, seq_len=seq_len, scale=1.0 / math.sqrt(HEAD_SIZE)),
        grid=(pairs,),
        in_specs=[
            pl.BlockSpec(memory_space=pltpu.SMEM),
            pl.BlockSpec((span, 1), lambda j: (0, 0)),
            pl.BlockSpec((1, rows), lambda j: (0, 0)),
            pl.BlockSpec((rows, columns), lambda j: (0, j)),
            pl.BlockSpec((span, 2 * HEAD_SIZE), lambda j: (0, j)),
        ],
        out_specs=[
            pl.BlockSpec((rows, columns), lambda j: (0, j)),
            pl.BlockSpec((1, columns // HEAD_SIZE, rows), lambda j: (j, 0, 0)),
        ],
        out_shape=[
            jax.ShapeDtypeStruct((rows, all_columns), BF16),
            jax.ShapeDtypeStruct((pairs, columns // HEAD_SIZE, rows), F32),
        ],
        scratch_shapes=[pltpu.VMEM((span, rows), F32)],
        compiler_params=pltpu.CompilerParams(vmem_limit_bytes=VMEM_LIMIT),
        cost_estimate=LIGHT,
        name="attention",
    )(place, segment_key, segment_query, queries, key_value)


def attention_back_kernel(
    place_ref,
    segment_key_ref,
    segment_query_ref,
    q_ref,
    kv_ref,
    lse_ref,
    dout_ref,
    cosine_ref,
    sine_ref,
    dq_ref,
    dkv_far_ref,
    dkv_own_ref,
    bias_ref,
    dkv_ref,
    *,
    seq_len,
    scale,
):
    @pl.when(pl.program_id(0) == 0)
    def _():
        mask_bias(place_ref, segment_key_ref, segment_query_ref, bias_ref, seq_len)

    rows = q_ref.shape[0]
    span = kv_ref.shape[0]
    count = q_ref.shape[1] // HEAD_SIZE
    key_t = kv_ref[:, :HEAD_SIZE].T
    chunks = span // rows
    dkv_ref[...] = jnp.zeros_like(dkv_ref)
    for head in range(count):
        columns = slice(head * HEAD_SIZE, (head + 1) * HEAD_SIZE)
        query = q_ref[:, columns]
        dout = dout_ref[:, columns]
        lse = lse_ref[0, head : head + 1, :]
        probs, dprobs = [], []
        row_dot = jnp.zeros_like(lse)
        for c in range(chunks):
            part = slice(c * rows, (c + 1) * rows)
            raw = mxu(kv_ref[part, :HEAD_SIZE], query, FROM_LAST)
            prob = jnp.exp(raw * scale + bias_ref[part, :] - lse)
            dprob = mxu(kv_ref[part, HEAD_SIZE:], dout, FROM_LAST)
            row_dot = row_dot + jnp.sum(prob * dprob, axis=0, keepdims=True)
            probs.append(prob)
            dprobs.append(dprob)
        dq_t = jnp.zeros((HEAD_SIZE, rows), F32)
        for c in range(chunks):
            part = slice(c * rows, (c + 1) * rows)
            dscore = (probs[c] * (dprobs[c] - row_dot)).astype(BF16)
            dkv_ref[part, :HEAD_SIZE] += mxu(dscore, query)
            dkv_ref[part, HEAD_SIZE:] += mxu(probs[c].astype(BF16), dout)
            dq_t = dq_t + mxu(key_t[:, part], dscore)
        dq_ref[:, columns] = turn(dq_t.T * scale, cosine_ref[...], -sine_ref[...]).astype(BF16)
    dkv_ref[:, :HEAD_SIZE] = dkv_ref[:, :HEAD_SIZE] * scale
    dkv_far_ref[...] = dkv_ref[: span - rows, :].astype(BF16)
    dkv_own_ref[...] = dkv_ref[span - rows :, :]


def attention_back(
    place, segment_key, segment_query, queries, key_value, lse, dout, cosine, sine, seq_len
):
    rows, all_columns = queries.shape
    span = key_value.shape[0]
    pairs = key_value.shape[1] // (2 * HEAD_SIZE)
    columns = all_columns // pairs
    return pl.pallas_call(
        functools.partial(
            attention_back_kernel, seq_len=seq_len, scale=1.0 / math.sqrt(HEAD_SIZE)
        ),
        grid=(pairs,),
        in_specs=[
            pl.BlockSpec(memory_space=pltpu.SMEM),
            pl.BlockSpec((span, 1), lambda j: (0, 0)),
            pl.BlockSpec((1, rows), lambda j: (0, 0)),
            pl.BlockSpec((rows, columns), lambda j: (0, j)),
            pl.BlockSpec((span, 2 * HEAD_SIZE), lambda j: (0, j)),
            pl.BlockSpec((1, columns // HEAD_SIZE, rows), lambda j: (j, 0, 0)),
            pl.BlockSpec((rows, columns), lambda j: (0, j)),
            pl.BlockSpec((rows, HEAD_SIZE), lambda j: (0, 0)),
            pl.BlockSpec((rows, HEAD_SIZE), lambda j: (0, 0)),
        ],
        out_specs=[
            pl.BlockSpec((rows, columns), lambda j: (0, j)),
            pl.BlockSpec((span - rows, 2 * HEAD_SIZE), lambda j: (0, j)),
            pl.BlockSpec((rows, 2 * HEAD_SIZE), lambda j: (0, j)),
        ],
        out_shape=[
            jax.ShapeDtypeStruct((rows, all_columns), BF16),
            jax.ShapeDtypeStruct((span - rows, key_value.shape[1]), BF16),
            jax.ShapeDtypeStruct((rows, key_value.shape[1]), F32),
        ],
        scratch_shapes=[
            pltpu.VMEM((span, rows), F32),
            pltpu.VMEM((span, 2 * HEAD_SIZE), F32),
        ],
        compiler_params=pltpu.CompilerParams(vmem_limit_bytes=VMEM_LIMIT),
        cost_estimate=LIGHT,
        name="attention_back",
    )(place, segment_key, segment_query, queries, key_value, lse, dout, cosine, sine)


def expert_kernel(
    slot_row_ref,
    slot_column_ref,
    routed_ref,
    own_ref,
    router_ref,
    tokens_ref,
    cotangent_ref,
    gate_ref,
    up_ref,
    down_ref,
    grad_ref,
    moe_ref,
    rows_in_ref,
    grad_out_ref,
    hidden_ref,
    grad_gate_ref,
    grad_up_ref,
    router_grad_ref,
    *,
    capacity,
):
    group_rows = tokens_ref.shape[1]
    tokens = tokens_ref[0]
    gate_weight, up_weight, down_weight = (
        ref[:, 0].reshape(-1, ref.shape[3]) for ref in (gate_ref, up_ref, down_ref)
    )
    cotangent = cotangent_ref[0]
    routed = routed_ref[0] > 0.0
    logits = jnp.where(routed, mxu(router_ref[...], tokens, FROM_LAST), -1e30)
    weights = jnp.exp(logits - jnp.max(logits, axis=0, keepdims=True))
    weights = jnp.where(routed, weights, 0.0)
    gates = weights / jnp.sum(weights, axis=0, keepdims=True)
    own = own_ref[...]
    gate_own = jnp.sum(gates * own, axis=0, keepdims=True)
    place = slot_row_ref[0] == lax.broadcasted_iota(jnp.int32, (capacity, group_rows), 0)
    place_wide = jnp.where(place, 1.0, 0.0)
    place_low = place_wide.astype(BF16)
    back = slot_column_ref[0] == lax.broadcasted_iota(jnp.int32, (group_rows, capacity), 1)
    back_low = jnp.where(back, 1.0, 0.0).astype(BF16)
    coefficient = jnp.sum(place_wide * gate_own, axis=1, keepdims=True)

    rows_in = mxu(place_low, tokens).astype(BF16)
    rows_in_ref[...] = rows_in
    gate_pre = mxu(rows_in, gate_weight)
    up_pre = mxu(rows_in, up_weight)
    sigmoid = 1.0 / (1.0 + jnp.exp(-gate_pre))
    silu = gate_pre * sigmoid
    hidden = (silu * up_pre).astype(BF16)
    hidden_ref[...] = hidden
    slot_cotangent = mxu(place_low, cotangent)
    grad_out = (coefficient * slot_cotangent).astype(BF16)
    grad_out_ref[...] = grad_out
    grad_hidden = mxu(grad_out, down_weight)
    grad_up = (grad_hidden * silu).astype(BF16)
    grad_gate = (grad_hidden * up_pre * sigmoid * (1.0 + gate_pre * (1.0 - sigmoid))).astype(BF16)
    grad_up_ref[...] = grad_up
    grad_gate_ref[...] = grad_gate
    expert_out = mxu(hidden, down_weight, FROM_LAST)
    grad_slot = jnp.sum(slot_cotangent * expert_out, axis=1, keepdims=True)
    moe_ref[0] = mxu(back_low, (coefficient * expert_out).astype(BF16)).astype(BF16)

    grad_token = jnp.sum(place_wide * grad_slot, axis=0, keepdims=True)
    share = (grad_token * gate_own) * (own - gates)
    share_high = share.astype(BF16)
    share_low = (share - share_high.astype(F32)).astype(BF16)
    router_grad = mxu(share_high, tokens) + mxu(share_low, tokens)

    @pl.when(pl.program_id(0) == 0)
    def _():
        router_grad_ref[...] = router_grad

    @pl.when(pl.program_id(0) > 0)
    def _():
        router_grad_ref[...] += router_grad

    grad_in = mxu(grad_gate, gate_weight, FROM_LAST) + mxu(grad_up, up_weight, FROM_LAST)
    grad_ref[0] = (
        mxu(back_low, grad_in.astype(BF16)) + mxu(share.T.astype(BF16), router_ref[...])
    ).astype(BF16)


def expert_groups(slot, routed, own, router_t, tokens, cotangent, weights, capacity):
    count, group_rows, width = tokens.shape
    ff = weights.shape[3]
    experts = router_t.shape[0]
    weight = lambda at: pl.BlockSpec(
        (weights.shape[0], 1, weights.shape[2], ff), lambda g: (0, at, 0, 0)
    )
    whole = lambda g: (0, 0)
    by_group = lambda g: (g, 0, 0)
    slots = lambda columns: pl.BlockSpec((capacity, columns), lambda g: (g, 0))
    slots_shape = lambda columns: jax.ShapeDtypeStruct((count * capacity, columns), BF16)
    return pl.pallas_call(
        functools.partial(expert_kernel, capacity=capacity),
        grid=(count,),
        in_specs=[
            pl.BlockSpec((1, 1, group_rows), by_group),
            pl.BlockSpec((1, group_rows, 1), by_group),
            pl.BlockSpec((1, experts, group_rows), by_group),
            pl.BlockSpec((experts, 1), whole),
            pl.BlockSpec((experts, width), whole),
            pl.BlockSpec((1, group_rows, width), by_group),
            pl.BlockSpec((1, group_rows, width), by_group),
            weight(0),
            weight(1),
            weight(2),
        ],
        out_specs=[
            pl.BlockSpec((1, group_rows, width), by_group),
            pl.BlockSpec((1, group_rows, width), by_group),
            slots(width),
            slots(width),
            slots(ff),
            slots(ff),
            slots(ff),
            pl.BlockSpec((experts, width), whole),
        ],
        out_shape=[
            jax.ShapeDtypeStruct(tokens.shape, BF16),
            jax.ShapeDtypeStruct(tokens.shape, BF16),
            slots_shape(width),
            slots_shape(width),
            slots_shape(ff),
            slots_shape(ff),
            slots_shape(ff),
            jax.ShapeDtypeStruct((experts, width), F32),
        ],
        compiler_params=pltpu.CompilerParams(vmem_limit_bytes=VMEM_LIMIT),
        cost_estimate=LIGHT,
        name="expert",
    )(
        slot[:, None, :],
        slot[:, :, None],
        routed,
        own,
        router_t,
        tokens,
        cotangent,
        weights,
        weights,
        weights,
    )


def weight_grad_kernel(*refs, halves):
    rows, grad_out, hidden, grad_gate, grad_up, router = (
        refs[at : at + 2] for at in range(0, 12, 2)
    )
    out_ref = refs[12]
    columns = hidden[0].shape[1] // halves
    over = (((0,), (0,)), ((), ()))
    left_rows = [ref[...] for ref in rows]
    left_out = [ref[...] for ref in grad_out]
    router_columns = (router[0][...] + router[1][...]).T
    router_columns = jnp.concatenate(
        [
            router_columns,
            jnp.zeros((router_columns.shape[0], HEAD_SIZE - router_columns.shape[1]), F32),
        ],
        axis=1,
    ).astype(BF16)
    for half in range(halves):
        start = half * (3 * columns + HEAD_SIZE)
        part = slice(half * columns, (half + 1) * columns)
        for at, (left, right) in enumerate(
            ((left_rows, grad_gate), (left_rows, grad_up), (left_out, hidden))
        ):
            total = mxu(left[0], right[0][:, part], over) + mxu(left[1], right[1][:, part], over)
            out_ref[:, start + at * columns : start + (at + 1) * columns] = total.astype(BF16)
        out_ref[:, start + 3 * columns : start + 3 * columns + HEAD_SIZE] = router_columns


def weight_grads(near, far, halves, block=256):
    rows_at, grad_out_at, hidden_at, grad_gate_at, grad_up_at, router_at = range(6)
    slots, width = near[rows_at].shape
    ff = near[hidden_at].shape[1]
    experts = near[router_at].shape[0]
    specs, operands = [], []
    for at in (rows_at, grad_out_at, hidden_at, grad_gate_at, grad_up_at, router_at):
        if at in (rows_at, grad_out_at):
            spec = pl.BlockSpec((slots, block), lambda i: (0, i))
        elif at == router_at:
            spec = pl.BlockSpec((experts, block), lambda i: (0, i))
        else:
            spec = pl.BlockSpec((slots, ff), lambda i: (0, 0))
        specs += [spec, spec]
        operands += [near[at], far[at]]
    columns = 3 * ff + halves * HEAD_SIZE
    return pl.pallas_call(
        functools.partial(weight_grad_kernel, halves=halves),
        grid=(width // block,),
        in_specs=specs,
        out_specs=pl.BlockSpec((block, columns), lambda i: (i, 0)),
        out_shape=jax.ShapeDtypeStruct((width, columns), BF16),
        compiler_params=pltpu.CompilerParams(vmem_limit_bytes=VMEM_LIMIT),
        cost_estimate=LIGHT,
        name="weight_grads",
    )(*operands)


def on_device(
    block_input,
    norm_gains,
    router_weight,
    query_matrix,
    key_matrix,
    value_matrix,
    output_weight,
    gate_weight,
    up_weight,
    down_weight,
    segment_ids,
    routes,
    priority,
    cotangent,
):
    tensor_index = lax.axis_index("tensor")
    own_rows, width = block_input.shape
    group_rows = segment_ids.shape[0]
    halves = lax.axis_size("tensor")
    outer = lax.axis_size("outer")
    groups = lax.axis_size("x") * lax.axis_size("core")
    plane = groups * halves
    shard_rows = query_matrix.shape[0]
    dp_size = outer * groups
    seq_len = min(SEQ_MOST, group_rows * dp_size)
    own_start = lax.axis_index(ALL) * own_rows
    capacity = group_rows * TOPK // EXPERTS
    reach = ATTEND_SPAN // own_rows
    half_ff = gate_weight.shape[2]
    ff = half_ff * halves

    query_columns = query_matrix.shape[1]
    first = tensor_index == 0
    qkv_own = jnp.concatenate([query_matrix, key_matrix, value_matrix], axis=1)
    qkv_other = swap(qkv_own, "tensor")
    qkv_first = jnp.where(first, qkv_own, qkv_other)
    qkv_second = jnp.where(first, qkv_other, qkv_own)
    qkv_shard = jnp.concatenate(
        [
            qkv_first[:, :query_columns],
            qkv_second[:, :query_columns],
            qkv_first[:, query_columns:],
            qkv_second[:, query_columns:],
        ],
        axis=1,
    )
    earlier_groups = (ATTEND_SPAN + group_rows - 1) // group_rows
    group_pairs = [
        [(i, i + k) for i in range(dp_size - k)] for k in range(earlier_groups, 0, -1)
    ]
    segment_near = jnp.concatenate(
        [lax.ppermute(segment_ids, DP, pairs) for pairs in group_pairs] + [segment_ids]
    )
    qkv_shard, segment_near, gate_own, up_own, down_own = lax.optimization_barrier(
        (qkv_shard, segment_near, gate_weight, up_weight, down_weight)
    )
    qkv_full = lax.all_gather(qkv_shard, DP, axis=0, tiled=True)

    expert_shard = jnp.transpose(jnp.stack([gate_own, up_own, down_own]), (2, 0, 1, 3))
    expert_shard = lax.all_to_all(expert_shard, PLANE, 0, 0, tiled=True)
    expert_shard = expert_shard.reshape(groups, halves, 3, shard_rows, half_ff)
    expert_shard = jnp.transpose(expert_shard, (2, 0, 3, 1, 4)).reshape(-1, ff)
    expert_shard, output_own = lax.optimization_barrier((expert_shard, output_weight))
    expert_full = lax.all_gather(expert_shard, "outer").reshape(
        outer, 3, groups * shard_rows, ff
    )

    output_near = plane_near(outer_gather(output_own))

    pair_count = group_rows * TOPK
    rank = (
        jnp.zeros((pair_count,), jnp.int32)
        .at[priority]
        .set(jnp.arange(pair_count, dtype=jnp.int32))
        .reshape(group_rows, TOPK)
    )
    expert_ids = jnp.arange(EXPERTS, dtype=jnp.int32)
    named = routes[:, :, None] == expert_ids[None, None, :]
    ranked = jnp.sum(jnp.where(named, rank[:, :, None] + 1, 0), axis=1)
    ranked = jnp.where(ranked > 0, ranked, pair_count + 1)
    ranked_own = lax.dynamic_slice_in_dim(ranked, tensor_index * own_rows, own_rows, 0)
    digits = jnp.concatenate([ranked_own // 64, ranked_own % 64], axis=1).astype(BF16)
    digits = jnp.pad(digits, ((0, 0), (0, HEAD_SIZE - digits.shape[1])))
    cotangent_sent = jnp.concatenate([cotangent, digits], axis=1)
    input_wide = block_input.astype(F32)
    first_gain = norm_gains[:, 0]
    second_gain = norm_gains[:, 1]
    first_factor = norm_factor(input_wide)
    normed_in = (input_wide * first_factor * first_gain).astype(BF16)
    positions = own_start + jnp.arange(own_rows, dtype=jnp.int32)
    cosine, sine = rotary_tables(positions % seq_len)
    all_queries = halves * query_columns
    query_blocks = all_queries // (2 * HEAD_SIZE)
    key_value_own = project(
        normed_in, qkv_full, cosine, sine, query_blocks, halves, (True, False)
    )
    queries = project(normed_in, qkv_full, cosine, sine, 0, query_blocks, (True, True))
    queries, cotangent_sent = lax.optimization_barrier((queries, cotangent_sent))
    cotangent_near, cotangent_far = plane_gather(cotangent_sent)
    pieces = [shift_all(key_value_own, k) for k in range(reach, 0, -1)]
    output_near, key_value_own = lax.optimization_barrier((output_near, key_value_own))
    output_far = swap(output_near, "core")
    pieces.append(key_value_own)
    key_value = jnp.concatenate(pieces, axis=0)
    span = ATTEND_SPAN + own_rows
    segment_ext = lax.dynamic_slice_in_dim(segment_near, tensor_index * own_rows, span)
    view = (
        jnp.reshape(own_start, (1,)),
        segment_ext[:, None],
        segment_ext[None, ATTEND_SPAN:],
        queries,
        key_value,
    )
    heads_low, log_total = attention(*view, seq_len)
    at_first = lax.axis_index("core") == 0
    by_core = [
        jnp.where(at_first, output_near, output_far),
        jnp.where(at_first, output_far, output_near),
    ]

    def output_piece(x_at, core_at, tensor_at):
        piece = lax.dynamic_index_in_dim(
            by_core[core_at], lax.axis_index("x") ^ x_at, 0, keepdims=False
        )
        return lax.dynamic_index_in_dim(piece, tensor_index ^ tensor_at, 0, keepdims=False)

    places = [(x_at, core_at) for x_at in range(2) for core_at in range(2)]
    output_full = jnp.concatenate(
        [jnp.stack([output_piece(*place, at) for place in places], 1) for at in range(2)],
        axis=-1,
    ).reshape(width, -1)
    hidden_state = input_wide + dot(heads_low, output_full, ((1,), (1,)))
    second_factor = norm_factor(hidden_state)
    normed_mid_own = (hidden_state * second_factor * second_gain).astype(BF16)

    normed_near, normed_far = plane_gather(normed_mid_own)
    expert = lax.axis_index(PLANE)
    own_expert = (expert_ids == expert).astype(F32)[:, None]
    router_t = router_weight.T

    def experts_on(tokens, cotangents):
        digits = cotangents[..., width:].reshape(2, group_rows, HEAD_SIZE).astype(jnp.int32)
        ranked_all = digits[..., :EXPERTS] * 64 + digits[..., EXPERTS : 2 * EXPERTS]
        routed = jnp.swapaxes((ranked_all <= pair_count).astype(F32), 1, 2)
        rank_own = jnp.sum(jnp.where(expert_ids == expert, ranked_all, 0), axis=-1)
        earlier = (rank_own[:, None, :] < rank_own[:, :, None]).astype(jnp.int32)
        slot = jnp.where(rank_own <= pair_count, jnp.sum(earlier, axis=-1), capacity)
        return expert_groups(
            slot,
            routed,
            own_expert,
            router_t,
            tokens.reshape(2, group_rows, width),
            cotangents.reshape(2, group_rows, -1),
            expert_full,
            capacity,
        )

    on_near = experts_on(normed_near, cotangent_near)
    on_far = experts_on(normed_far, cotangent_far)
    blocks = (2 * halves, own_rows, width)
    (grad_near, moe_near), (grad_far, moe_far) = (
        [array.reshape(blocks) for array in side[:2]] for side in (on_near, on_far)
    )
    grad_total = fold_core(grad_near, grad_far)
    grad_total, on_near, on_far, moe_near, moe_far = lax.optimization_barrier(
        (grad_total, on_near[2:], on_far[2:], moe_near, moe_far)
    )
    grad_mid_parts = fold_plane(grad_total)
    expert_part = weight_grads(on_near, on_far, halves)
    expert_sum = lax.psum_scatter(expert_part, "outer", scatter_dimension=0, tiled=True)
    moe_total = fold_core(moe_near, moe_far)
    grad_mid_parts, moe_total = lax.optimization_barrier((grad_mid_parts, moe_total))
    moe_parts = fold_plane(moe_total)
    grad_mid = wide_sum(grad_mid_parts)

    norm_input_part = norm_back(hidden_state, second_factor, second_gain, grad_mid)
    grad_state = cotangent.astype(F32) + norm_input_part
    grad_attn = grad_state.astype(BF16)
    grad_heads = dot(grad_attn, output_full, ((1,), (0,))).astype(BF16)
    output_total = fold_columns(grad_attn, heads_low, shard_rows)
    grad_query_pre, grad_far_kv, grad_own = attention_back(
        *view, log_total, grad_heads, cosine, sine, seq_len
    )
    grad_far_kv, output_total = lax.optimization_barrier((grad_far_kv, output_total))
    output_parts = fold_plane(distance_blocks(output_total))
    for k in range(1, reach + 1):
        first_row = ATTEND_SPAN - k * own_rows
        piece = grad_far_kv[first_row : first_row + own_rows]
        grad_own = grad_own + shift_all(piece, -k).astype(F32)
    grad_key_value = []
    for half in range(halves):
        start = half * 2 * HEAD_SIZE
        key_part = grad_own[:, start : start + HEAD_SIZE]
        turned = jnp.concatenate(
            [key_part[:, HEAD_SIZE // 2 :], key_part[:, : HEAD_SIZE // 2]], axis=1
        )
        grad_key_value.append(key_part * cosine - turned * sine)
        grad_key_value.append(grad_own[:, start + HEAD_SIZE : start + 2 * HEAD_SIZE])
    grad_key_value_pre = jnp.concatenate(grad_key_value, axis=1).astype(BF16)
    grad_qkv_pre = jnp.concatenate(
        [
            grad_query_pre.reshape(own_rows, halves, -1),
            grad_key_value_pre.reshape(own_rows, halves, -1),
        ],
        axis=2,
    ).reshape(own_rows, -1)
    qkv_total = fold_columns(normed_in, grad_qkv_pre, shard_rows)
    qkv_parts = fold_plane(distance_blocks(qkv_total))
    grad_in = dot(grad_query_pre, qkv_full[:, :all_queries], ((1,), (1,))) + dot(
        grad_key_value_pre, qkv_full[:, all_queries:], ((1,), (1,))
    )
    input_grad = grad_state + norm_back(input_wide, first_factor, first_gain, grad_in)
    qkv_parts, output_parts, moe_parts, expert_sum = lax.optimization_barrier(
        (qkv_parts, output_parts, moe_parts, expert_sum)
    )
    output_weight_grad = outer_scatter(wide_sum(output_parts).astype(BF16))
    block_output = hidden_state + wide_sum(moe_parts)
    expert_sum = expert_sum.reshape(groups, shard_rows, halves, -1)
    expert_sum = jnp.swapaxes(expert_sum, 1, 2).reshape(plane, shard_rows, -1)
    expert_sum = lax.all_to_all(expert_sum, PLANE, 0, 0, tiled=True)
    gate_grad, up_grad, down_grad = (
        jnp.swapaxes(expert_sum[:, :, at * half_ff : (at + 1) * half_ff], 0, 1).astype(F32)
        for at in range(3)
    )
    router_grad = jnp.sum(expert_sum[:, :, 3 * half_ff : 3 * half_ff + EXPERTS].astype(F32), axis=0)
    router_grad = lax.dynamic_slice_in_dim(
        router_grad, tensor_index * (shard_rows // 2), shard_rows // 2, 0
    )
    qkv_grad = outer_scatter(wide_sum(qkv_parts).astype(BF16))
    query_grad = qkv_grad[:, :query_columns]
    key_grad = qkv_grad[:, query_columns : query_columns + HEAD_SIZE]
    value_grad = qkv_grad[:, query_columns + HEAD_SIZE :]

    half_rows = shard_rows // 2
    own_gains = lax.dynamic_slice_in_dim(
        norm_gains, lax.axis_index(DP) * shard_rows, shard_rows, 0
    )
    first_sum = jnp.sum(qkv_grad * qkv_own.astype(F32), axis=-1)
    second_sum = jnp.sum(
        gate_grad * gate_weight.astype(F32) + up_grad * up_weight.astype(F32), axis=(1, 2)
    )
    gain_sums = jnp.stack([first_sum, second_sum], axis=1) / own_gains
    kept = lax.dynamic_slice_in_dim(gain_sums, tensor_index * half_rows, half_rows, 0)
    sent = lax.dynamic_slice_in_dim(gain_sums, (1 - tensor_index) * half_rows, half_rows, 0)
    own_router = lax.dynamic_slice_in_dim(
        router_weight, lax.axis_index(ALL) * half_rows, half_rows, 0
    )
    router_sum = jnp.sum(router_grad * own_router.astype(F32), axis=-1)
    half_gains = lax.dynamic_slice_in_dim(own_gains, tensor_index * half_rows, half_rows, 0)
    router_sum = router_sum / half_gains[:, 1]
    gains_grad = (
        kept
        + swap(sent, "tensor")
        + jnp.stack([jnp.zeros_like(router_sum), router_sum], axis=1)
    )
    return (
        block_output,
        input_grad,
        gains_grad,
        router_grad,
        query_grad,
        key_grad,
        value_grad,
        output_weight_grad,
        gate_grad,
        up_grad,
        down_grad,
    )


def solution(mesh):
    dp_size, tensor_size = mesh.shape["dp"], mesh.shape["tensor"]
    split = Mesh(mesh.devices.reshape(dp_size // 4, 2, 2, tensor_size), ALL)
    return jax.shard_map(
        on_device,
        mesh=split,
        in_specs=(
            P(ALL, None),
            P(),
            P(),
            P(DP, "tensor"),
            P(DP, "tensor"),
            P(DP, "tensor"),
            P(DP, "tensor"),
            P(DP, None, "tensor"),
            P(DP, None, "tensor"),
            P(DP, None, "tensor"),
            P(DP),
            P(DP, None),
            P(DP),
            P(ALL, None),
        ),
        out_specs=(
            P(ALL, None),
            P(ALL, None),
            P(ALL, None),
            P(ALL, None),
            P(DP, "tensor"),
            P(DP, "tensor"),
            P(DP, "tensor"),
            P(DP, "tensor"),
            P(DP, None, "tensor"),
            P(DP, None, "tensor"),
            P(DP, None, "tensor"),
        ),
        check_vma=False,
    )
```

```python
import functools
import math

import jax
import jax.numpy as jnp
from jax import lax
from jax.experimental import pallas as pl
from jax.experimental.pallas import tpu as pltpu
from jax.sharding import Mesh
from jax.sharding import PartitionSpec as P

HEAD_SIZE = 128
TOPK = 4
EXPERTS = 8
ATTEND_SPAN = 1024
SEQ_MOST = 16384
EPSILON = 1e-06
ROPE_BASE = 10000.0
BF16 = jnp.bfloat16
F32 = jnp.float32

DP = ("outer", "x", "core")
PLANE = ("x", "core", "tensor")
ALL = ("outer", "x", "core", "tensor")


def shift_all(x, by):
    length = lax.axis_size(ALL)
    pairs = [(i, i + by) for i in range(length) if 0 <= i + by < length]
    return lax.ppermute(x, ALL, pairs)


def swap(x, axis):
    length = lax.axis_size(axis)
    return lax.ppermute(x, axis, [(i, length - 1 - i) for i in range(length)])


def plane_near(own):
    near = jnp.stack([own, swap(own, "tensor"), swap(own, "x"), swap(own, ("x", "tensor"))])
    return near.reshape((2, 2) + own.shape)


def plane_gather(own):
    near = plane_near(own)
    return near, swap(near, "core")


def fold_core(kept, sent):
    return (kept.astype(F32) + swap(sent, "core").astype(F32)).astype(BF16)


def fold_blocks(kept, got):
    return [
        (kept[at].astype(F32) + got[at].astype(F32)).astype(BF16) for at in range(kept.shape[0])
    ]


def in_order(own, other, axis_name, axis):
    first = lax.axis_index(axis_name) == 0
    return jnp.stack([jnp.where(first, own, other), jnp.where(first, other, own)], axis)


def fold_plane(blocks):
    return [
        blocks[0],
        swap(blocks[1], "tensor"),
        swap(blocks[2], "x"),
        swap(blocks[3], ("x", "tensor")),
    ]


def wide_sum(parts):
    return sum(part.astype(F32) for part in parts)


def outer_shift(x, by):
    length = lax.axis_size("outer")
    return lax.ppermute(x, "outer", [(i, (i + by) % length) for i in range(length)])


def outer_gather(shard):
    length, here = lax.axis_size("outer"), lax.axis_index("outer")
    if length > 4:
        return lax.all_gather(shard, "outer")
    full = jnp.zeros((length,) + shard.shape, shard.dtype)
    for by in range(length):
        piece = outer_shift(shard, by) if by else shard
        full = lax.dynamic_update_slice_in_dim(full, piece[None], (here - by) % length, 0)
    return full


def outer_scatter(parts):
    length, here = lax.axis_size("outer"), lax.axis_index("outer")
    if length > 4:
        return lax.psum_scatter(parts, "outer", scatter_dimension=0, tiled=False).astype(F32)
    total = None
    for by in range(length):
        piece = lax.dynamic_index_in_dim(parts, (here + by) % length, 0, keepdims=False)
        piece = (outer_shift(piece, by) if by else piece).astype(F32)
        total = piece if total is None else total + piece
    return total


def core_columns(rows, core_at, shard_rows):
    count = rows.shape[0]
    split = rows.reshape(count, -1, 2, shard_rows)
    return lax.dynamic_index_in_dim(split, core_at, 2, keepdims=False).reshape(count, -1)


def fold_columns(left, right, shard_rows):
    core = lax.axis_index("core")
    sent = dot(core_columns(left, 1 - core, shard_rows), right, ((0,), (0,))).astype(BF16)
    kept = dot(core_columns(left, core, shard_rows), right, ((0,), (0,))).astype(BF16)
    return fold_core(kept, sent).reshape(-1, 2, shard_rows, right.shape[1])


def distance_blocks(total):
    x, tensor = lax.axis_index("x"), lax.axis_index("tensor")
    columns = total.shape[3] // 2
    blocks = []
    for x_by in range(2):
        for tensor_by in range(2):
            block = lax.dynamic_index_in_dim(total, x ^ x_by, 1, keepdims=False)
            start = (tensor ^ tensor_by) * columns
            blocks.append(lax.dynamic_slice_in_dim(block, start, columns, 2))
    return blocks


def rotary_tables(position):
    halfway = HEAD_SIZE // 2
    inverse = jnp.exp(
        jnp.arange(halfway, dtype=F32) * (-2.0 * math.log(ROPE_BASE) / HEAD_SIZE)
    )
    angles = position.astype(F32)[:, None] * inverse[None, :]
    cosine, sine = jnp.cos(angles), jnp.sin(angles)
    return (
        jnp.concatenate([cosine, cosine], axis=1),
        jnp.concatenate([-sine, sine], axis=1),
    )


def norm_factor(value_rows):
    return lax.rsqrt(jnp.mean(value_rows * value_rows, axis=-1, keepdims=True) + EPSILON)


def norm_back(value_rows, factor, gain, upstream):
    weighted = upstream * gain
    return factor * weighted - value_rows * (factor * factor * factor) * jnp.mean(
        weighted * value_rows, axis=-1, keepdims=True
    )


def dot(a, b, dims):
    return lax.dot_general(a, b, (dims, ((), ())), preferred_element_type=F32)


VMEM_LIMIT = 60 * 1024 * 1024
LIGHT = pl.CostEstimate(flops=1000, bytes_accessed=1000, transcendentals=0)
FROM_LAST = (((1,), (1,)), ((), ()))
PLAIN = (((1,), (0,)), ((), ()))


def mxu(a, b, dims=PLAIN):
    return lax.dot_general(a, b, dims, preferred_element_type=F32)


def turn(rows, cosine, sine):
    return rows * cosine + pltpu.roll(rows, HEAD_SIZE // 2, 1) * sine


def project_kernel(rows_ref, weight_ref, cosine_ref, sine_ref, out_ref, *, turned):
    product = mxu(rows_ref[...], weight_ref[...])
    for at, turns in enumerate(turned):
        part = product[:, at * HEAD_SIZE : (at + 1) * HEAD_SIZE]
        if turns:
            part = turn(part, cosine_ref[...], sine_ref[...])
        out_ref[:, at * HEAD_SIZE : (at + 1) * HEAD_SIZE] = part.astype(BF16)


def project(rows, weight, cosine, sine, first, count, turned):
    high, width = rows.shape
    columns = len(turned) * HEAD_SIZE
    return pl.pallas_call(
        functools.partial(project_kernel, turned=turned),
        grid=(count,),
        in_specs=[
            pl.BlockSpec((high, width), lambda j: (0, 0)),
            pl.BlockSpec((width, columns), lambda j: (0, first + j)),
            pl.BlockSpec((high, HEAD_SIZE), lambda j: (0, 0)),
            pl.BlockSpec((high, HEAD_SIZE), lambda j: (0, 0)),
        ],
        out_specs=pl.BlockSpec((high, columns), lambda j: (0, j)),
        out_shape=jax.ShapeDtypeStruct((high, count * columns), BF16),
        compiler_params=pltpu.CompilerParams(vmem_limit_bytes=VMEM_LIMIT),
        cost_estimate=LIGHT,
        name="project",
    )(rows, weight, cosine, sine)


def mask_bias(place_ref, segment_key_ref, segment_query_ref, bias_ref, seq_len):
    span, rows = bias_ref.shape
    start = place_ref[0]
    key_at = lax.broadcasted_iota(jnp.int32, (span, rows), 0)
    query_at = lax.broadcasted_iota(jnp.int32, (span, rows), 1) + ATTEND_SPAN
    distance = query_at - key_at
    position = start + query_at - ATTEND_SPAN
    sequence_at = query_at - lax.rem(position, seq_len)
    allowed = (distance >= 0) & (distance < ATTEND_SPAN) & (key_at >= sequence_at)
    allowed = allowed & (segment_key_ref[...] == segment_query_ref[...])
    bias_ref[...] = jnp.where(allowed, 0.0, -1e30)


def attention_kernel(
    place_ref,
    segment_key_ref,
    segment_query_ref,
    q_ref,
    kv_ref,
    heads_ref,
    lse_ref,
    bias_ref,
    *,
    seq_len,
    scale,
):
    @pl.when(pl.program_id(0) == 0)
    def _():
        mask_bias(place_ref, segment_key_ref, segment_query_ref, bias_ref, seq_len)

    rows = q_ref.shape[0]
    span = kv_ref.shape[0]
    count = q_ref.shape[1] // HEAD_SIZE
    value_t = kv_ref[:, HEAD_SIZE:].T
    chunks = span // rows
    for head in range(count):
        columns = slice(head * HEAD_SIZE, (head + 1) * HEAD_SIZE)
        query = q_ref[:, columns]
        scores = []
        for c in range(chunks):
            part = slice(c * rows, (c + 1) * rows)
            raw = mxu(kv_ref[part, :HEAD_SIZE], query, FROM_LAST)
            scores.append(raw * scale + bias_ref[part, :])
        top = functools.reduce(jnp.maximum, scores)
        top = jnp.max(top, axis=0, keepdims=True)
        total = jnp.zeros_like(top)
        out_t = jnp.zeros((HEAD_SIZE, rows), F32)
        for c in range(chunks):
            weight = jnp.exp(scores[c] - top)
            total = total + jnp.sum(weight, axis=0, keepdims=True)
            out_t = out_t + mxu(value_t[:, c * rows : (c + 1) * rows], weight.astype(BF16))
        heads_ref[:, columns] = (out_t / total).T.astype(BF16)
        lse_ref[0, head : head + 1, :] = top + jnp.log(total)


def attention(place, segment_key, segment_query, queries, key_value, seq_len):
    rows, all_columns = queries.shape
    span = key_value.shape[0]
    pairs = key_value.shape[1] // (2 * HEAD_SIZE)
    columns = all_columns // pairs
    return pl.pallas_call(
        functools.partial(attention_kernel, seq_len=seq_len, scale=1.0 / math.sqrt(HEAD_SIZE)),
        grid=(pairs,),
        in_specs=[
            pl.BlockSpec(memory_space=pltpu.SMEM),
            pl.BlockSpec((span, 1), lambda j: (0, 0)),
            pl.BlockSpec((1, rows), lambda j: (0, 0)),
            pl.BlockSpec((rows, columns), lambda j: (0, j)),
            pl.BlockSpec((span, 2 * HEAD_SIZE), lambda j: (0, j)),
        ],
        out_specs=[
            pl.BlockSpec((rows, columns), lambda j: (0, j)),
            pl.BlockSpec((1, columns // HEAD_SIZE, rows), lambda j: (j, 0, 0)),
        ],
        out_shape=[
            jax.ShapeDtypeStruct((rows, all_columns), BF16),
            jax.ShapeDtypeStruct((pairs, columns // HEAD_SIZE, rows), F32),
        ],
        scratch_shapes=[pltpu.VMEM((span, rows), F32)],
        compiler_params=pltpu.CompilerParams(vmem_limit_bytes=VMEM_LIMIT),
        cost_estimate=LIGHT,
        name="attention",
    )(place, segment_key, segment_query, queries, key_value)


def attention_back_kernel(
    place_ref,
    segment_key_ref,
    segment_query_ref,
    q_ref,
    kv_ref,
    lse_ref,
    dout_ref,
    cosine_ref,
    sine_ref,
    dq_ref,
    dkv_far_ref,
    dkv_own_ref,
    bias_ref,
    dkv_ref,
    *,
    seq_len,
    scale,
):
    @pl.when(pl.program_id(0) == 0)
    def _():
        mask_bias(place_ref, segment_key_ref, segment_query_ref, bias_ref, seq_len)

    rows = q_ref.shape[0]
    span = kv_ref.shape[0]
    count = q_ref.shape[1] // HEAD_SIZE
    key_t = kv_ref[:, :HEAD_SIZE].T
    chunks = span // rows
    dkv_ref[...] = jnp.zeros_like(dkv_ref)
    for head in range(count):
        columns = slice(head * HEAD_SIZE, (head + 1) * HEAD_SIZE)
        query = q_ref[:, columns]
        dout = dout_ref[:, columns]
        lse = lse_ref[0, head : head + 1, :]
        probs, dprobs = [], []
        row_dot = jnp.zeros_like(lse)
        for c in range(chunks):
            part = slice(c * rows, (c + 1) * rows)
            raw = mxu(kv_ref[part, :HEAD_SIZE], query, FROM_LAST)
            prob = jnp.exp(raw * scale + bias_ref[part, :] - lse)
            dprob = mxu(kv_ref[part, HEAD_SIZE:], dout, FROM_LAST)
            row_dot = row_dot + jnp.sum(prob * dprob, axis=0, keepdims=True)
            probs.append(prob)
            dprobs.append(dprob)
        dq_t = jnp.zeros((HEAD_SIZE, rows), F32)
        for c in range(chunks):
            part = slice(c * rows, (c + 1) * rows)
            dscore = (probs[c] * (dprobs[c] - row_dot)).astype(BF16)
            dkv_ref[part, :HEAD_SIZE] += mxu(dscore, query)
            dkv_ref[part, HEAD_SIZE:] += mxu(probs[c].astype(BF16), dout)
            dq_t = dq_t + mxu(key_t[:, part], dscore)
        dq_ref[:, columns] = turn(dq_t.T * scale, cosine_ref[...], -sine_ref[...]).astype(BF16)
    dkv_ref[:, :HEAD_SIZE] = dkv_ref[:, :HEAD_SIZE] * scale
    dkv_far_ref[...] = dkv_ref[: span - rows, :].astype(BF16)
    dkv_own_ref[...] = dkv_ref[span - rows :, :]


def attention_back(
    place, segment_key, segment_query, queries, key_value, lse, dout, cosine, sine, seq_len
):
    rows, all_columns = queries.shape
    span = key_value.shape[0]
    pairs = key_value.shape[1] // (2 * HEAD_SIZE)
    columns = all_columns // pairs
    return pl.pallas_call(
        functools.partial(
            attention_back_kernel, seq_len=seq_len, scale=1.0 / math.sqrt(HEAD_SIZE)
        ),
        grid=(pairs,),
        in_specs=[
            pl.BlockSpec(memory_space=pltpu.SMEM),
            pl.BlockSpec((span, 1), lambda j: (0, 0)),
            pl.BlockSpec((1, rows), lambda j: (0, 0)),
            pl.BlockSpec((rows, columns), lambda j: (0, j)),
            pl.BlockSpec((span, 2 * HEAD_SIZE), lambda j: (0, j)),
            pl.BlockSpec((1, columns // HEAD_SIZE, rows), lambda j: (j, 0, 0)),
            pl.BlockSpec((rows, columns), lambda j: (0, j)),
            pl.BlockSpec((rows, HEAD_SIZE), lambda j: (0, 0)),
            pl.BlockSpec((rows, HEAD_SIZE), lambda j: (0, 0)),
        ],
        out_specs=[
            pl.BlockSpec((rows, columns), lambda j: (0, j)),
            pl.BlockSpec((span - rows, 2 * HEAD_SIZE), lambda j: (0, j)),
            pl.BlockSpec((rows, 2 * HEAD_SIZE), lambda j: (0, j)),
        ],
        out_shape=[
            jax.ShapeDtypeStruct((rows, all_columns), BF16),
            jax.ShapeDtypeStruct((span - rows, key_value.shape[1]), BF16),
            jax.ShapeDtypeStruct((rows, key_value.shape[1]), F32),
        ],
        scratch_shapes=[
            pltpu.VMEM((span, rows), F32),
            pltpu.VMEM((span, 2 * HEAD_SIZE), F32),
        ],
        compiler_params=pltpu.CompilerParams(vmem_limit_bytes=VMEM_LIMIT),
        cost_estimate=LIGHT,
        name="attention_back",
    )(place, segment_key, segment_query, queries, key_value, lse, dout, cosine, sine)


def expert_kernel(
    slot_row_ref,
    slot_column_ref,
    routed_ref,
    own_ref,
    router_ref,
    tokens_ref,
    cotangent_ref,
    gate_ref,
    up_ref,
    down_ref,
    grad_ref,
    moe_ref,
    rows_in_ref,
    grad_out_ref,
    hidden_ref,
    grad_gate_ref,
    grad_up_ref,
    router_grad_ref,
    *,
    capacity,
):
    group_rows = tokens_ref.shape[1]
    tokens = tokens_ref[0]
    gate_weight, up_weight, down_weight = (
        ref[:, 0].reshape(-1, ref.shape[3]) for ref in (gate_ref, up_ref, down_ref)
    )
    cotangent = cotangent_ref[0]
    routed = routed_ref[0] > 0.0
    logits = jnp.where(routed, mxu(router_ref[...], tokens, FROM_LAST), -1e30)
    weights = jnp.exp(logits - jnp.max(logits, axis=0, keepdims=True))
    weights = jnp.where(routed, weights, 0.0)
    gates = weights / jnp.sum(weights, axis=0, keepdims=True)
    own = own_ref[...]
    gate_own = jnp.sum(gates * own, axis=0, keepdims=True)
    place = slot_row_ref[0] == lax.broadcasted_iota(jnp.int32, (capacity, group_rows), 0)
    place_wide = jnp.where(place, 1.0, 0.0)
    place_low = place_wide.astype(BF16)
    back = slot_column_ref[0] == lax.broadcasted_iota(jnp.int32, (group_rows, capacity), 1)
    back_low = jnp.where(back, 1.0, 0.0).astype(BF16)
    coefficient = jnp.sum(place_wide * gate_own, axis=1, keepdims=True)

    rows_in = mxu(place_low, tokens).astype(BF16)
    rows_in_ref[...] = rows_in
    gate_pre = mxu(rows_in, gate_weight)
    up_pre = mxu(rows_in, up_weight)
    sigmoid = 1.0 / (1.0 + jnp.exp(-gate_pre))
    silu = gate_pre * sigmoid
    hidden = (silu * up_pre).astype(BF16)
    hidden_ref[...] = hidden
    slot_cotangent = mxu(place_low, cotangent)
    grad_out = (coefficient * slot_cotangent).astype(BF16)
    grad_out_ref[...] = grad_out
    grad_hidden = mxu(grad_out, down_weight)
    grad_up = (grad_hidden * silu).astype(BF16)
    grad_gate = (grad_hidden * up_pre * sigmoid * (1.0 + gate_pre * (1.0 - sigmoid))).astype(BF16)
    grad_up_ref[...] = grad_up
    grad_gate_ref[...] = grad_gate
    expert_out = mxu(hidden, down_weight, FROM_LAST)
    grad_slot = jnp.sum(slot_cotangent * expert_out, axis=1, keepdims=True)
    moe_ref[0] = mxu(back_low, (coefficient * expert_out).astype(BF16)).astype(BF16)

    grad_token = jnp.sum(place_wide * grad_slot, axis=0, keepdims=True)
    share = (grad_token * gate_own) * (own - gates)
    share_high = share.astype(BF16)
    share_low = (share - share_high.astype(F32)).astype(BF16)
    router_grad = mxu(share_high, tokens) + mxu(share_low, tokens)

    @pl.when(pl.program_id(0) == 0)
    def _():
        router_grad_ref[...] = router_grad

    @pl.when(pl.program_id(0) > 0)
    def _():
        router_grad_ref[...] += router_grad

    grad_in = mxu(grad_gate, gate_weight, FROM_LAST) + mxu(grad_up, up_weight, FROM_LAST)
    grad_ref[0] = (
        mxu(back_low, grad_in.astype(BF16)) + mxu(share.T.astype(BF16), router_ref[...])
    ).astype(BF16)


def expert_groups(slot, routed, own, router_t, tokens, cotangent, weights, capacity):
    count, group_rows, width = tokens.shape
    ff = weights.shape[3]
    experts = router_t.shape[0]
    weight = lambda at: pl.BlockSpec(
        (weights.shape[0], 1, weights.shape[2], ff), lambda g: (0, at, 0, 0)
    )
    whole = lambda g: (0, 0)
    by_group = lambda g: (g, 0, 0)
    slots = lambda columns: pl.BlockSpec((capacity, columns), lambda g: (g, 0))
    slots_shape = lambda columns: jax.ShapeDtypeStruct((count * capacity, columns), BF16)
    return pl.pallas_call(
        functools.partial(expert_kernel, capacity=capacity),
        grid=(count,),
        in_specs=[
            pl.BlockSpec((1, 1, group_rows), by_group),
            pl.BlockSpec((1, group_rows, 1), by_group),
            pl.BlockSpec((1, experts, group_rows), by_group),
            pl.BlockSpec((experts, 1), whole),
            pl.BlockSpec((experts, width), whole),
            pl.BlockSpec((1, group_rows, width), by_group),
            pl.BlockSpec((1, group_rows, width), by_group),
            weight(0),
            weight(1),
            weight(2),
        ],
        out_specs=[
            pl.BlockSpec((1, group_rows, width), by_group),
            pl.BlockSpec((1, group_rows, width), by_group),
            slots(width),
            slots(width),
            slots(ff),
            slots(ff),
            slots(ff),
            pl.BlockSpec((experts, width), whole),
        ],
        out_shape=[
            jax.ShapeDtypeStruct(tokens.shape, BF16),
            jax.ShapeDtypeStruct(tokens.shape, BF16),
            slots_shape(width),
            slots_shape(width),
            slots_shape(ff),
            slots_shape(ff),
            slots_shape(ff),
            jax.ShapeDtypeStruct((experts, width), F32),
        ],
        compiler_params=pltpu.CompilerParams(vmem_limit_bytes=VMEM_LIMIT),
        cost_estimate=LIGHT,
        name="expert",
    )(
        slot[:, None, :],
        slot[:, :, None],
        routed,
        own,
        router_t,
        tokens,
        cotangent,
        weights,
        weights,
        weights,
    )


def weight_grad_kernel(*refs, halves):
    rows, grad_out, hidden, grad_gate, grad_up, router = (
        refs[at : at + 2] for at in range(0, 12, 2)
    )
    moe_kept_ref, moe_got_ref, out_ref, moe_ref = refs[12:]
    moe_ref[...] = (moe_kept_ref[...].astype(F32) + moe_got_ref[...].astype(F32)).astype(BF16)
    columns = hidden[0].shape[1] // halves
    over = (((0,), (0,)), ((), ()))
    left_rows = [ref[...] for ref in rows]
    left_out = [ref[...] for ref in grad_out]
    router_columns = (router[0][...] + router[1][...]).T
    router_columns = jnp.concatenate(
        [
            router_columns,
            jnp.zeros((router_columns.shape[0], HEAD_SIZE - router_columns.shape[1]), F32),
        ],
        axis=1,
    ).astype(BF16)
    for half in range(halves):
        start = half * (3 * columns + HEAD_SIZE)
        part = slice(half * columns, (half + 1) * columns)
        for at, (left, right) in enumerate(
            ((left_rows, grad_gate), (left_rows, grad_up), (left_out, hidden))
        ):
            total = mxu(left[0], right[0][:, part], over) + mxu(left[1], right[1][:, part], over)
            out_ref[:, start + at * columns : start + (at + 1) * columns] = total.astype(BF16)
        out_ref[:, start + 3 * columns : start + 3 * columns + HEAD_SIZE] = router_columns


def weight_grads(near, far, moe_kept, moe_got, halves, block=256):
    rows_at, grad_out_at, hidden_at, grad_gate_at, grad_up_at, router_at = range(6)
    slots, width = near[rows_at].shape
    ff = near[hidden_at].shape[1]
    experts = near[router_at].shape[0]
    specs, operands = [], []
    for at in (rows_at, grad_out_at, hidden_at, grad_gate_at, grad_up_at, router_at):
        if at in (rows_at, grad_out_at):
            spec = pl.BlockSpec((slots, block), lambda i: (0, i))
        elif at == router_at:
            spec = pl.BlockSpec((experts, block), lambda i: (0, i))
        else:
            spec = pl.BlockSpec((slots, ff), lambda i: (0, 0))
        specs += [spec, spec]
        operands += [near[at], far[at]]
    columns = 3 * ff + halves * HEAD_SIZE
    moe_spec = pl.BlockSpec((moe_kept.shape[0], block), lambda i: (0, i))
    return pl.pallas_call(
        functools.partial(weight_grad_kernel, halves=halves),
        grid=(width // block,),
        in_specs=specs + [moe_spec, moe_spec],
        out_specs=[pl.BlockSpec((block, columns), lambda i: (i, 0)), moe_spec],
        out_shape=[
            jax.ShapeDtypeStruct((width, columns), BF16),
            jax.ShapeDtypeStruct(moe_kept.shape, BF16),
        ],
        compiler_params=pltpu.CompilerParams(vmem_limit_bytes=VMEM_LIMIT),
        cost_estimate=pl.CostEstimate(
            flops=15_000_000_000, bytes_accessed=50_000_000, transcendentals=0
        ),
        name="weight_grads",
    )(*operands, moe_kept, moe_got)


def on_device(
    block_input,
    norm_gains,
    router_weight,
    query_matrix,
    key_matrix,
    value_matrix,
    output_weight,
    gate_weight,
    up_weight,
    down_weight,
    segment_ids,
    routes,
    priority,
    cotangent,
):
    tensor_index = lax.axis_index("tensor")
    own_rows, width = block_input.shape
    group_rows = segment_ids.shape[0]
    halves = lax.axis_size("tensor")
    outer = lax.axis_size("outer")
    groups = lax.axis_size("x") * lax.axis_size("core")
    plane = groups * halves
    shard_rows = query_matrix.shape[0]
    dp_size = outer * groups
    seq_len = min(SEQ_MOST, group_rows * dp_size)
    own_start = lax.axis_index(ALL) * own_rows
    capacity = group_rows * TOPK // EXPERTS
    reach = ATTEND_SPAN // own_rows
    half_ff = gate_weight.shape[2]
    ff = half_ff * halves

    query_columns = query_matrix.shape[1]
    first = tensor_index == 0
    qkv_own = jnp.concatenate([query_matrix, key_matrix, value_matrix], axis=1)
    qkv_other = swap(qkv_own, "tensor")
    qkv_first = jnp.where(first, qkv_own, qkv_other)
    qkv_second = jnp.where(first, qkv_other, qkv_own)
    query_shard = jnp.concatenate(
        [qkv_first[:, :query_columns], qkv_second[:, :query_columns]], axis=1
    )
    early_shard = jnp.concatenate(
        [qkv_first[:, query_columns:], qkv_second[:, query_columns:], output_weight], axis=1
    )
    earlier_groups = (ATTEND_SPAN + group_rows - 1) // group_rows
    group_pairs = [
        [(i, i + k) for i in range(dp_size - k)] for k in range(earlier_groups, 0, -1)
    ]
    segment_near = jnp.concatenate(
        [lax.ppermute(segment_ids, DP, pairs) for pairs in group_pairs] + [segment_ids]
    )
    query_shard, early_shard, segment_near, gate_own, up_own, down_own = lax.optimization_barrier(
        (query_shard, early_shard, segment_near, gate_weight, up_weight, down_weight)
    )
    query_full = lax.all_gather(query_shard, DP, axis=0, tiled=True)

    early_shard = outer_gather(early_shard)
    pair_columns = 2 * halves * HEAD_SIZE
    key_value_full = early_shard[:, :, :pair_columns]
    key_value_full = in_order(key_value_full, swap(key_value_full, "x"), "x", 1)
    key_value_full = in_order(key_value_full, swap(key_value_full, "core"), "core", 2)
    key_value_full = key_value_full.reshape(width, pair_columns)
    output_near = plane_near(early_shard[:, :, pair_columns:])

    expert_shard = jnp.transpose(jnp.stack([gate_own, up_own, down_own]), (2, 0, 1, 3))
    expert_shard = lax.all_to_all(expert_shard, PLANE, 0, 0, tiled=True)

    pair_count = group_rows * TOPK
    rank = (
        jnp.zeros((pair_count,), jnp.int32)
        .at[priority]
        .set(jnp.arange(pair_count, dtype=jnp.int32))
        .reshape(group_rows, TOPK)
    )
    expert_ids = jnp.arange(EXPERTS, dtype=jnp.int32)
    named = routes[:, :, None] == expert_ids[None, None, :]
    ranked = jnp.sum(jnp.where(named, rank[:, :, None] + 1, 0), axis=1)
    ranked = jnp.where(ranked > 0, ranked, pair_count + 1)
    ranked_own = lax.dynamic_slice_in_dim(ranked, tensor_index * own_rows, own_rows, 0)
    digits = jnp.concatenate([ranked_own // 64, ranked_own % 64], axis=1).astype(BF16)
    digits = jnp.pad(digits, ((0, 0), (0, HEAD_SIZE - digits.shape[1])))
    cotangent_sent = jnp.concatenate([cotangent, digits], axis=1)
    input_wide = block_input.astype(F32)
    first_gain = norm_gains[:, 0]
    second_gain = norm_gains[:, 1]
    first_factor = norm_factor(input_wide)
    normed_in = (input_wide * first_factor * first_gain).astype(BF16)
    positions = own_start + jnp.arange(own_rows, dtype=jnp.int32)
    cosine, sine = rotary_tables(positions % seq_len)
    query_blocks = halves * query_columns // (2 * HEAD_SIZE)
    key_value_sent = project(
        normed_in, key_value_full, cosine, sine, 0, halves, (True, False)
    )
    key_value_own, expert_shard, cotangent_sent = lax.optimization_barrier(
        (key_value_sent, expert_shard, cotangent_sent)
    )
    expert_shard = expert_shard.reshape(groups, halves, 3, shard_rows, half_ff)
    expert_shard = jnp.transpose(expert_shard, (2, 0, 3, 1, 4)).reshape(-1, ff)
    expert_full = lax.all_gather(expert_shard, "outer").reshape(
        outer, 3, groups * shard_rows, ff
    )
    pieces = [shift_all(key_value_sent, k) for k in range(reach, 0, -1)] + [key_value_own]
    queries = project(normed_in, query_full, cosine, sine, 0, query_blocks, (True, True))
    queries, cotangent_sent = lax.optimization_barrier((queries, cotangent_sent))
    cotangent_near, cotangent_far = plane_gather(cotangent_sent)
    key_value = jnp.concatenate(pieces, axis=0)
    span = ATTEND_SPAN + own_rows
    segment_ext = lax.dynamic_slice_in_dim(segment_near, tensor_index * own_rows, span)
    view = (
        jnp.reshape(own_start, (1,)),
        segment_ext[:, None],
        segment_ext[None, ATTEND_SPAN:],
        queries,
        key_value,
    )
    output_far = swap(output_near, "core")
    heads_low, log_total = attention(*view, seq_len)
    at_first = lax.axis_index("core") == 0
    by_core = [
        jnp.where(at_first, output_near, output_far),
        jnp.where(at_first, output_far, output_near),
    ]

    def output_piece(x_at, core_at, tensor_at):
        piece = lax.dynamic_index_in_dim(
            by_core[core_at], lax.axis_index("x") ^ x_at, 0, keepdims=False
        )
        return lax.dynamic_index_in_dim(piece, tensor_index ^ tensor_at, 0, keepdims=False)

    places = [(x_at, core_at) for x_at in range(2) for core_at in range(2)]
    output_full = jnp.concatenate(
        [jnp.stack([output_piece(*place, at) for place in places], 1) for at in range(2)],
        axis=-1,
    ).reshape(width, -1)
    hidden_state = input_wide + dot(heads_low, output_full, ((1,), (1,)))
    second_factor = norm_factor(hidden_state)
    normed_mid_own = (hidden_state * second_factor * second_gain).astype(BF16)

    normed_near, normed_far = plane_gather(normed_mid_own)
    expert = lax.axis_index(PLANE)
    own_expert = (expert_ids == expert).astype(F32)[:, None]
    router_t = router_weight.T

    def experts_on(tokens, cotangents):
        digits = cotangents[..., width:].reshape(2, group_rows, HEAD_SIZE).astype(jnp.int32)
        ranked_all = digits[..., :EXPERTS] * 64 + digits[..., EXPERTS : 2 * EXPERTS]
        routed = jnp.swapaxes((ranked_all <= pair_count).astype(F32), 1, 2)
        rank_own = jnp.sum(jnp.where(expert_ids == expert, ranked_all, 0), axis=-1)
        earlier = (rank_own[:, None, :] < rank_own[:, :, None]).astype(jnp.int32)
        slot = jnp.where(rank_own <= pair_count, jnp.sum(earlier, axis=-1), capacity)
        return expert_groups(
            slot,
            routed,
            own_expert,
            router_t,
            tokens.reshape(2, group_rows, width),
            cotangents.reshape(2, group_rows, -1),
            expert_full,
            capacity,
        )

    on_near = experts_on(normed_near, cotangent_near)
    on_far = experts_on(normed_far, cotangent_far)
    blocks = (2 * halves, own_rows, width)
    (grad_near, moe_near), (grad_far, moe_far) = (
        [array.reshape(blocks) for array in side[:2]] for side in (on_near, on_far)
    )
    grad_got, moe_far = lax.optimization_barrier((swap(grad_far, "core"), moe_far))
    grad_blocks = fold_blocks(grad_near, grad_got)
    grad_blocks, on_near, on_far = lax.optimization_barrier(
        (grad_blocks, on_near[2:], on_far[2:])
    )
    grad_mid_parts = fold_plane(grad_blocks)
    expert_part, moe_total = weight_grads(
        on_near,
        on_far,
        moe_near.reshape(-1, width),
        swap(moe_far, "core").reshape(-1, width),
        halves,
    )
    expert_sum = lax.psum_scatter(expert_part, "outer", scatter_dimension=0, tiled=True)
    grad_mid_parts, moe_total = lax.optimization_barrier((grad_mid_parts, moe_total))
    moe_parts = fold_plane(list(moe_total.reshape(blocks)))
    grad_mid = wide_sum(grad_mid_parts)

    norm_input_part = norm_back(hidden_state, second_factor, second_gain, grad_mid)
    grad_state = cotangent.astype(F32) + norm_input_part
    grad_attn = grad_state.astype(BF16)
    grad_heads = dot(grad_attn, output_full, ((1,), (0,))).astype(BF16)
    output_total = fold_columns(grad_attn, heads_low, shard_rows)
    grad_query_pre, grad_far_kv, grad_own = attention_back(
        *view, log_total, grad_heads, cosine, sine, seq_len
    )
    grad_query_pre, grad_far_kv, output_total, moe_parts = lax.optimization_barrier(
        (grad_query_pre, grad_far_kv, output_total, moe_parts)
    )
    output_parts = fold_plane(distance_blocks(output_total))
    query_total = fold_columns(normed_in, grad_query_pre, shard_rows)
    query_parts = fold_plane(distance_blocks(query_total))
    for k in range(1, reach + 1):
        first_row = ATTEND_SPAN - k * own_rows
        piece = grad_far_kv[first_row : first_row + own_rows]
        grad_own = grad_own + shift_all(piece, -k).astype(F32)
    grad_own, output_parts = lax.optimization_barrier((grad_own, output_parts))
    grad_key_value = []
    for half in range(halves):
        start = half * 2 * HEAD_SIZE
        key_part = grad_own[:, start : start + HEAD_SIZE]
        turned = jnp.concatenate(
            [key_part[:, HEAD_SIZE // 2 :], key_part[:, : HEAD_SIZE // 2]], axis=1
        )
        grad_key_value.append(key_part * cosine - turned * sine)
        grad_key_value.append(grad_own[:, start + HEAD_SIZE : start + 2 * HEAD_SIZE])
    grad_key_value_pre = jnp.concatenate(grad_key_value, axis=1).astype(BF16)
    key_value_total = fold_columns(normed_in, grad_key_value_pre, shard_rows)
    key_value_parts = fold_plane(distance_blocks(key_value_total))
    grad_in = dot(grad_query_pre, query_full, ((1,), (1,))) + dot(
        grad_key_value_pre, key_value_full, ((1,), (1,))
    )
    input_grad = grad_state + norm_back(input_wide, first_factor, first_gain, grad_in)
    query_parts, key_value_parts, expert_sum = lax.optimization_barrier(
        (query_parts, key_value_parts, expert_sum)
    )
    output_weight_grad = outer_scatter(wide_sum(output_parts).astype(BF16))
    block_output = hidden_state + wide_sum(moe_parts)
    expert_sum = expert_sum.reshape(groups, shard_rows, halves, -1)
    expert_sum = jnp.swapaxes(expert_sum, 1, 2).reshape(plane, shard_rows, -1)
    expert_sum = lax.all_to_all(expert_sum, PLANE, 0, 0, tiled=True)
    gate_grad, up_grad, down_grad = (
        jnp.swapaxes(expert_sum[:, :, at * half_ff : (at + 1) * half_ff], 0, 1).astype(F32)
        for at in range(3)
    )
    router_grad = jnp.sum(expert_sum[:, :, 3 * half_ff : 3 * half_ff + EXPERTS].astype(F32), axis=0)
    router_grad = lax.dynamic_slice_in_dim(
        router_grad, tensor_index * (shard_rows // 2), shard_rows // 2, 0
    )
    qkv_grad = outer_scatter(
        jnp.concatenate([wide_sum(query_parts), wide_sum(key_value_parts)], axis=2).astype(BF16)
    )
    query_grad = qkv_grad[:, :query_columns]
    key_grad = qkv_grad[:, query_columns : query_columns + HEAD_SIZE]
    value_grad = qkv_grad[:, query_columns + HEAD_SIZE :]

    half_rows = shard_rows // 2
    own_gains = lax.dynamic_slice_in_dim(
        norm_gains, lax.axis_index(DP) * shard_rows, shard_rows, 0
    )
    first_sum = jnp.sum(qkv_grad * qkv_own.astype(F32), axis=-1)
    second_sum = jnp.sum(
        gate_grad * gate_weight.astype(F32) + up_grad * up_weight.astype(F32), axis=(1, 2)
    )
    gain_sums = jnp.stack([first_sum, second_sum], axis=1) / own_gains
    kept = lax.dynamic_slice_in_dim(gain_sums, tensor_index * half_rows, half_rows, 0)
    sent = lax.dynamic_slice_in_dim(gain_sums, (1 - tensor_index) * half_rows, half_rows, 0)
    own_router = lax.dynamic_slice_in_dim(
        router_weight, lax.axis_index(ALL) * half_rows, half_rows, 0
    )
    router_sum = jnp.sum(router_grad * own_router.astype(F32), axis=-1)
    half_gains = lax.dynamic_slice_in_dim(own_gains, tensor_index * half_rows, half_rows, 0)
    router_sum = router_sum / half_gains[:, 1]
    gains_grad = (
        kept
        + swap(sent, "tensor")
        + jnp.stack([jnp.zeros_like(router_sum), router_sum], axis=1)
    )
    return (
        block_output,
        input_grad,
        gains_grad,
        router_grad,
        query_grad,
        key_grad,
        value_grad,
        output_weight_grad,
        gate_grad,
        up_grad,
        down_grad,
    )


def solution(mesh):
    dp_size, tensor_size = mesh.shape["dp"], mesh.shape["tensor"]
    split = Mesh(mesh.devices.reshape(dp_size // 4, 2, 2, tensor_size), ALL)
    return jax.shard_map(
        on_device,
        mesh=split,
        in_specs=(
            P(ALL, None),
            P(),
            P(),
            P(DP, "tensor"),
            P(DP, "tensor"),
            P(DP, "tensor"),
            P(DP, "tensor"),
            P(DP, None, "tensor"),
            P(DP, None, "tensor"),
            P(DP, None, "tensor"),
            P(DP),
            P(DP, None),
            P(DP),
            P(ALL, None),
        ),
        out_specs=(
            P(ALL, None),
            P(ALL, None),
            P(ALL, None),
            P(ALL, None),
            P(DP, "tensor"),
            P(DP, "tensor"),
            P(DP, "tensor"),
            P(DP, "tensor"),
            P(DP, None, "tensor"),
            P(DP, None, "tensor"),
            P(DP, None, "tensor"),
        ),
        check_vma=False,
    )
```

```python
import functools
import math

import jax
import jax.numpy as jnp
from jax import lax
from jax.experimental import pallas as pl
from jax.experimental.pallas import tpu as pltpu
from jax.sharding import Mesh
from jax.sharding import PartitionSpec as P

HEAD_SIZE = 128
TOPK = 4
EXPERTS = 8
ATTEND_SPAN = 1024
SEQ_MOST = 16384
EPSILON = 1e-06
ROPE_BASE = 10000.0
BF16 = jnp.bfloat16
F32 = jnp.float32

DP = ("outer", "x", "core")
PLANE = ("x", "core", "tensor")
ALL = ("outer", "x", "core", "tensor")


def shift_groups(x, by):
    length = lax.axis_size(DP)
    return lax.ppermute(x, DP, [(i, i + by) for i in range(length) if 0 <= i + by < length])


def swap(x, axis):
    length = lax.axis_size(axis)
    return lax.ppermute(x, axis, [(i, length - 1 - i) for i in range(length)])


def plane_parts(own):
    return [own, swap(own, "tensor"), swap(own, "x"), swap(own, ("x", "tensor"))]


def plane_stack(parts):
    return jnp.stack(parts).reshape((2, 2) + parts[0].shape)


def plane_gather(own):
    near = plane_stack(plane_parts(own))
    return near, swap(near, "core")


def whole_weight(near, far):
    x, tensor = lax.axis_index("x"), lax.axis_index("tensor")
    first = lax.axis_index("core") == 0
    by_core = [jnp.where(first, near, far), jnp.where(first, far, near)]

    def piece(x_at, core_at, tensor_at):
        picked = lax.dynamic_index_in_dim(by_core[core_at], x ^ x_at, 0, keepdims=False)
        return lax.dynamic_index_in_dim(picked, tensor ^ tensor_at, 0, keepdims=False)

    places = [(x_at, core_at) for x_at in range(2) for core_at in range(2)]
    halves = [jnp.stack([piece(*place, at) for place in places], 1) for at in range(2)]
    return jnp.concatenate(halves, axis=-1).reshape(-1, 2 * near.shape[-1])


def fold_core(kept, sent):
    return (kept.astype(F32) + swap(sent, "core").astype(F32)).astype(BF16)


def fold_blocks(kept, got):
    return [
        (kept[at].astype(F32) + got[at].astype(F32)).astype(BF16) for at in range(kept.shape[0])
    ]


def in_order(own, other, axis_name, axis):
    first = lax.axis_index(axis_name) == 0
    return jnp.stack([jnp.where(first, own, other), jnp.where(first, other, own)], axis)


def fold_plane(blocks):
    return [
        blocks[0],
        swap(blocks[1], "tensor"),
        swap(blocks[2], "x"),
        swap(blocks[3], ("x", "tensor")),
    ]


def wide_sum(parts):
    return sum(part.astype(F32) for part in parts)


def next_outer(x):
    length = lax.axis_size("outer")
    return lax.ppermute(x, "outer", [(i, (i + 1) % length) for i in range(length)])


def round_planes(held):
    length, here = lax.axis_size("outer"), lax.axis_index("outer")
    if length > 4:
        return lax.all_gather(held[0], "outer")
    while len(held) < length:
        held = held + [next_outer(held[-1])]
    full = jnp.zeros((length,) + held[0].shape, held[0].dtype)
    for step in range(length):
        full = lax.dynamic_update_slice_in_dim(
            full, held[step][None], (here - step) % length, 0
        )
    return full


def outer_shift(x, by):
    length = lax.axis_size("outer")
    return lax.ppermute(x, "outer", [(i, (i + by) % length) for i in range(length)])


def outer_gather(shard):
    length, here = lax.axis_size("outer"), lax.axis_index("outer")
    if length > 4:
        return lax.all_gather(shard, "outer")
    full = jnp.zeros((length,) + shard.shape, shard.dtype)
    for by in range(length):
        piece = outer_shift(shard, by) if by else shard
        full = lax.dynamic_update_slice_in_dim(full, piece[None], (here - by) % length, 0)
    return full


def outer_scatter(parts):
    length, here = lax.axis_size("outer"), lax.axis_index("outer")
    if length > 4:
        return lax.psum_scatter(parts, "outer", scatter_dimension=0, tiled=False).astype(F32)
    total = None
    for by in range(length):
        piece = lax.dynamic_index_in_dim(parts, (here + by) % length, 0, keepdims=False)
        piece = (outer_shift(piece, by) if by else piece).astype(F32)
        total = piece if total is None else total + piece
    return total


def core_columns(rows, core_at, shard_rows):
    count = rows.shape[0]
    split = rows.reshape(count, -1, 2, shard_rows)
    return lax.dynamic_index_in_dim(split, core_at, 2, keepdims=False).reshape(count, -1)


def fold_columns(left, right, shard_rows):
    core = lax.axis_index("core")
    sent = dot(core_columns(left, 1 - core, shard_rows), right, ((0,), (0,))).astype(BF16)
    kept = dot(core_columns(left, core, shard_rows), right, ((0,), (0,))).astype(BF16)
    return fold_core(kept, sent).reshape(-1, 2, shard_rows, right.shape[1])


def distance_blocks(total):
    x, tensor = lax.axis_index("x"), lax.axis_index("tensor")
    columns = total.shape[3] // 2
    blocks = []
    for x_by in range(2):
        for tensor_by in range(2):
            block = lax.dynamic_index_in_dim(total, x ^ x_by, 1, keepdims=False)
            start = (tensor ^ tensor_by) * columns
            blocks.append(lax.dynamic_slice_in_dim(block, start, columns, 2))
    return blocks


def rotary_tables(position):
    halfway = HEAD_SIZE // 2
    inverse = jnp.exp(
        jnp.arange(halfway, dtype=F32) * (-2.0 * math.log(ROPE_BASE) / HEAD_SIZE)
    )
    angles = position.astype(F32)[:, None] * inverse[None, :]
    cosine, sine = jnp.cos(angles), jnp.sin(angles)
    return (
        jnp.concatenate([cosine, cosine], axis=1),
        jnp.concatenate([-sine, sine], axis=1),
    )


def norm_factor(value_rows):
    return lax.rsqrt(jnp.mean(value_rows * value_rows, axis=-1, keepdims=True) + EPSILON)


def norm_back(value_rows, factor, gain, upstream):
    weighted = upstream * gain
    return factor * weighted - value_rows * (factor * factor * factor) * jnp.mean(
        weighted * value_rows, axis=-1, keepdims=True
    )


def dot(a, b, dims):
    return lax.dot_general(a, b, (dims, ((), ())), preferred_element_type=F32)


VMEM_LIMIT = 60 * 1024 * 1024
LIGHT = pl.CostEstimate(flops=1000, bytes_accessed=1000, transcendentals=0)
FROM_LAST = (((1,), (1,)), ((), ()))
PLAIN = (((1,), (0,)), ((), ()))


def mxu(a, b, dims=PLAIN):
    return lax.dot_general(a, b, dims, preferred_element_type=F32)


def turn(rows, cosine, sine):
    return rows * cosine + pltpu.roll(rows, HEAD_SIZE // 2, 1) * sine


def project_kernel(rows_ref, weight_ref, cosine_ref, sine_ref, out_ref, *, turned):
    product = mxu(rows_ref[...], weight_ref[...])
    for at, turns in enumerate(turned):
        part = product[:, at * HEAD_SIZE : (at + 1) * HEAD_SIZE]
        if turns:
            part = turn(part, cosine_ref[...], sine_ref[...])
        out_ref[:, at * HEAD_SIZE : (at + 1) * HEAD_SIZE] = part.astype(BF16)


def project(rows, weight, cosine, sine, first, count, turned):
    high, width = rows.shape
    columns = len(turned) * HEAD_SIZE
    return pl.pallas_call(
        functools.partial(project_kernel, turned=turned),
        grid=(count,),
        in_specs=[
            pl.BlockSpec((high, width), lambda j: (0, 0)),
            pl.BlockSpec((width, columns), lambda j: (0, first + j)),
            pl.BlockSpec((high, HEAD_SIZE), lambda j: (0, 0)),
            pl.BlockSpec((high, HEAD_SIZE), lambda j: (0, 0)),
        ],
        out_specs=pl.BlockSpec((high, columns), lambda j: (0, j)),
        out_shape=jax.ShapeDtypeStruct((high, count * columns), BF16),
        compiler_params=pltpu.CompilerParams(vmem_limit_bytes=VMEM_LIMIT),
        cost_estimate=LIGHT,
        name="project",
    )(rows, weight, cosine, sine)


def mask_bias(place_ref, segment_key_ref, segment_query_ref, bias_ref, seq_len):
    span, rows = bias_ref.shape
    start = place_ref[0]
    key_at = lax.broadcasted_iota(jnp.int32, (span, rows), 0)
    query_at = lax.broadcasted_iota(jnp.int32, (span, rows), 1) + ATTEND_SPAN
    distance = query_at - key_at
    position = start + query_at - ATTEND_SPAN
    sequence_at = query_at - lax.rem(position, seq_len)
    allowed = (distance >= 0) & (distance < ATTEND_SPAN) & (key_at >= sequence_at)
    allowed = allowed & (segment_key_ref[...] == segment_query_ref[...])
    bias_ref[...] = jnp.where(allowed, 0.0, -1e30)


def attention_kernel(
    place_ref,
    segment_key_ref,
    segment_query_ref,
    q_ref,
    kv_ref,
    heads_ref,
    lse_ref,
    bias_ref,
    *,
    seq_len,
    scale,
):
    @pl.when(pl.program_id(0) == 0)
    def _():
        mask_bias(place_ref, segment_key_ref, segment_query_ref, bias_ref, seq_len)

    rows = q_ref.shape[0]
    span = kv_ref.shape[0]
    count = q_ref.shape[1] // HEAD_SIZE
    value_t = kv_ref[:, HEAD_SIZE:].T
    chunks = span // rows
    for head in range(count):
        columns = slice(head * HEAD_SIZE, (head + 1) * HEAD_SIZE)
        query = q_ref[:, columns]
        scores = []
        for c in range(chunks):
            part = slice(c * rows, (c + 1) * rows)
            raw = mxu(kv_ref[part, :HEAD_SIZE], query, FROM_LAST)
            scores.append(raw * scale + bias_ref[part, :])
        top = functools.reduce(jnp.maximum, scores)
        top = jnp.max(top, axis=0, keepdims=True)
        total = jnp.zeros_like(top)
        out_t = jnp.zeros((HEAD_SIZE, rows), F32)
        for c in range(chunks):
            weight = jnp.exp(scores[c] - top)
            total = total + jnp.sum(weight, axis=0, keepdims=True)
            out_t = out_t + mxu(value_t[:, c * rows : (c + 1) * rows], weight.astype(BF16))
        heads_ref[:, columns] = (out_t / total).T.astype(BF16)
        lse_ref[0, head : head + 1, :] = top + jnp.log(total)


def attention(place, segment_key, segment_query, queries, key_value, seq_len):
    rows, all_columns = queries.shape
    span = key_value.shape[0]
    pairs = key_value.shape[1] // (2 * HEAD_SIZE)
    columns = all_columns // pairs
    return pl.pallas_call(
        functools.partial(attention_kernel, seq_len=seq_len, scale=1.0 / math.sqrt(HEAD_SIZE)),
        grid=(pairs,),
        in_specs=[
            pl.BlockSpec(memory_space=pltpu.SMEM),
            pl.BlockSpec((span, 1), lambda j: (0, 0)),
            pl.BlockSpec((1, rows), lambda j: (0, 0)),
            pl.BlockSpec((rows, columns), lambda j: (0, j)),
            pl.BlockSpec((span, 2 * HEAD_SIZE), lambda j: (0, j)),
        ],
        out_specs=[
            pl.BlockSpec((rows, columns), lambda j: (0, j)),
            pl.BlockSpec((1, columns // HEAD_SIZE, rows), lambda j: (j, 0, 0)),
        ],
        out_shape=[
            jax.ShapeDtypeStruct((rows, all_columns), BF16),
            jax.ShapeDtypeStruct((pairs, columns // HEAD_SIZE, rows), F32),
        ],
        scratch_shapes=[pltpu.VMEM((span, rows), F32)],
        compiler_params=pltpu.CompilerParams(vmem_limit_bytes=VMEM_LIMIT),
        cost_estimate=LIGHT,
        name="attention",
    )(place, segment_key, segment_query, queries, key_value)


def attention_back_kernel(
    place_ref,
    segment_key_ref,
    segment_query_ref,
    q_ref,
    kv_ref,
    lse_ref,
    dout_ref,
    cosine_ref,
    sine_ref,
    dq_ref,
    dkv_far_ref,
    dkv_own_ref,
    bias_ref,
    dkv_ref,
    *,
    seq_len,
    scale,
):
    @pl.when(pl.program_id(0) == 0)
    def _():
        mask_bias(place_ref, segment_key_ref, segment_query_ref, bias_ref, seq_len)

    rows = q_ref.shape[0]
    span = kv_ref.shape[0]
    count = q_ref.shape[1] // HEAD_SIZE
    key_t = kv_ref[:, :HEAD_SIZE].T
    chunks = span // rows
    dkv_ref[...] = jnp.zeros_like(dkv_ref)
    for head in range(count):
        columns = slice(head * HEAD_SIZE, (head + 1) * HEAD_SIZE)
        query = q_ref[:, columns]
        dout = dout_ref[:, columns]
        lse = lse_ref[0, head : head + 1, :]
        probs, dprobs = [], []
        row_dot = jnp.zeros_like(lse)
        for c in range(chunks):
            part = slice(c * rows, (c + 1) * rows)
            raw = mxu(kv_ref[part, :HEAD_SIZE], query, FROM_LAST)
            prob = jnp.exp(raw * scale + bias_ref[part, :] - lse)
            dprob = mxu(kv_ref[part, HEAD_SIZE:], dout, FROM_LAST)
            row_dot = row_dot + jnp.sum(prob * dprob, axis=0, keepdims=True)
            probs.append(prob)
            dprobs.append(dprob)
        dq_t = jnp.zeros((HEAD_SIZE, rows), F32)
        for c in range(chunks):
            part = slice(c * rows, (c + 1) * rows)
            dscore = (probs[c] * (dprobs[c] - row_dot)).astype(BF16)
            dkv_ref[part, :HEAD_SIZE] += mxu(dscore, query)
            dkv_ref[part, HEAD_SIZE:] += mxu(probs[c].astype(BF16), dout)
            dq_t = dq_t + mxu(key_t[:, part], dscore)
        dq_ref[:, columns] = turn(dq_t.T * scale, cosine_ref[...], -sine_ref[...]).astype(BF16)
    dkv_ref[:, :HEAD_SIZE] = dkv_ref[:, :HEAD_SIZE] * scale
    dkv_far_ref[...] = dkv_ref[: span - rows, :].astype(BF16)
    dkv_own_ref[...] = dkv_ref[span - rows :, :]


def attention_back(
    place, segment_key, segment_query, queries, key_value, lse, dout, cosine, sine, seq_len
):
    rows, all_columns = queries.shape
    span = key_value.shape[0]
    pairs = key_value.shape[1] // (2 * HEAD_SIZE)
    columns = all_columns // pairs
    return pl.pallas_call(
        functools.partial(
            attention_back_kernel, seq_len=seq_len, scale=1.0 / math.sqrt(HEAD_SIZE)
        ),
        grid=(pairs,),
        in_specs=[
            pl.BlockSpec(memory_space=pltpu.SMEM),
            pl.BlockSpec((span, 1), lambda j: (0, 0)),
            pl.BlockSpec((1, rows), lambda j: (0, 0)),
            pl.BlockSpec((rows, columns), lambda j: (0, j)),
            pl.BlockSpec((span, 2 * HEAD_SIZE), lambda j: (0, j)),
            pl.BlockSpec((1, columns // HEAD_SIZE, rows), lambda j: (j, 0, 0)),
            pl.BlockSpec((rows, columns), lambda j: (0, j)),
            pl.BlockSpec((rows, HEAD_SIZE), lambda j: (0, 0)),
            pl.BlockSpec((rows, HEAD_SIZE), lambda j: (0, 0)),
        ],
        out_specs=[
            pl.BlockSpec((rows, columns), lambda j: (0, j)),
            pl.BlockSpec((span - rows, 2 * HEAD_SIZE), lambda j: (0, j)),
            pl.BlockSpec((rows, 2 * HEAD_SIZE), lambda j: (0, j)),
        ],
        out_shape=[
            jax.ShapeDtypeStruct((rows, all_columns), BF16),
            jax.ShapeDtypeStruct((span - rows, key_value.shape[1]), BF16),
            jax.ShapeDtypeStruct((rows, key_value.shape[1]), F32),
        ],
        scratch_shapes=[
            pltpu.VMEM((span, rows), F32),
            pltpu.VMEM((span, 2 * HEAD_SIZE), F32),
        ],
        compiler_params=pltpu.CompilerParams(vmem_limit_bytes=VMEM_LIMIT),
        cost_estimate=LIGHT,
        name="attention_back",
    )(place, segment_key, segment_query, queries, key_value, lse, dout, cosine, sine)


def expert_kernel(
    slot_row_ref,
    slot_column_ref,
    routed_ref,
    own_ref,
    router_ref,
    tokens_ref,
    cotangent_ref,
    gate_ref,
    up_ref,
    down_ref,
    grad_ref,
    moe_ref,
    rows_in_ref,
    grad_out_ref,
    hidden_ref,
    grad_gate_ref,
    grad_up_ref,
    router_grad_ref,
    *,
    capacity,
):
    group_rows = tokens_ref.shape[1]
    tokens = tokens_ref[0]
    gate_weight, up_weight, down_weight = (
        jnp.concatenate(
            [ref[:, 0, half].reshape(-1, ref.shape[4]) for half in range(ref.shape[2])], axis=1
        )
        for ref in (gate_ref, up_ref, down_ref)
    )
    cotangent = cotangent_ref[0]
    routed = routed_ref[0] > 0.0
    logits = jnp.where(routed, mxu(router_ref[...], tokens, FROM_LAST), -1e30)
    weights = jnp.exp(logits - jnp.max(logits, axis=0, keepdims=True))
    weights = jnp.where(routed, weights, 0.0)
    gates = weights / jnp.sum(weights, axis=0, keepdims=True)
    own = own_ref[...]
    gate_own = jnp.sum(gates * own, axis=0, keepdims=True)
    place = slot_row_ref[0] == lax.broadcasted_iota(jnp.int32, (capacity, group_rows), 0)
    place_wide = jnp.where(place, 1.0, 0.0)
    place_low = place_wide.astype(BF16)
    back = slot_column_ref[0] == lax.broadcasted_iota(jnp.int32, (group_rows, capacity), 1)
    back_low = jnp.where(back, 1.0, 0.0).astype(BF16)
    coefficient = jnp.sum(place_wide * gate_own, axis=1, keepdims=True)

    rows_in = mxu(place_low, tokens).astype(BF16)
    rows_in_ref[...] = rows_in
    gate_pre = mxu(rows_in, gate_weight)
    up_pre = mxu(rows_in, up_weight)
    sigmoid = 1.0 / (1.0 + jnp.exp(-gate_pre))
    silu = gate_pre * sigmoid
    hidden = (silu * up_pre).astype(BF16)
    hidden_ref[...] = hidden
    slot_cotangent = mxu(place_low, cotangent)
    grad_out = (coefficient * slot_cotangent).astype(BF16)
    grad_out_ref[...] = grad_out
    grad_hidden = mxu(grad_out, down_weight)
    grad_up = (grad_hidden * silu).astype(BF16)
    grad_gate = (grad_hidden * up_pre * sigmoid * (1.0 + gate_pre * (1.0 - sigmoid))).astype(BF16)
    grad_up_ref[...] = grad_up
    grad_gate_ref[...] = grad_gate
    expert_out = mxu(hidden, down_weight, FROM_LAST)
    grad_slot = jnp.sum(slot_cotangent * expert_out, axis=1, keepdims=True)
    moe_ref[0] = mxu(back_low, (coefficient * expert_out).astype(BF16)).astype(BF16)

    grad_token = jnp.sum(place_wide * grad_slot, axis=0, keepdims=True)
    share = (grad_token * gate_own) * (own - gates)
    share_high = share.astype(BF16)
    share_low = (share - share_high.astype(F32)).astype(BF16)
    router_grad = mxu(share_high, tokens) + mxu(share_low, tokens)

    @pl.when(pl.program_id(0) == 0)
    def _():
        router_grad_ref[...] = router_grad

    @pl.when(pl.program_id(0) > 0)
    def _():
        router_grad_ref[...] += router_grad

    grad_in = mxu(grad_gate, gate_weight, FROM_LAST) + mxu(grad_up, up_weight, FROM_LAST)
    grad_ref[0] = (
        mxu(back_low, grad_in.astype(BF16)) + mxu(share.T.astype(BF16), router_ref[...])
    ).astype(BF16)


def expert_groups(slot, routed, own, router_t, tokens, cotangent, weights, capacity):
    count, group_rows, width = tokens.shape
    ff = weights.shape[2] * weights.shape[4]
    experts = router_t.shape[0]
    weight = lambda at: pl.BlockSpec(
        (weights.shape[0], 1) + weights.shape[2:], lambda g: (0, at, 0, 0, 0)
    )
    whole = lambda g: (0, 0)
    by_group = lambda g: (g, 0, 0)
    slots = lambda columns: pl.BlockSpec((capacity, columns), lambda g: (g, 0))
    slots_shape = lambda columns: jax.ShapeDtypeStruct((count * capacity, columns), BF16)
    return pl.pallas_call(
        functools.partial(expert_kernel, capacity=capacity),
        grid=(count,),
        in_specs=[
            pl.BlockSpec((1, 1, group_rows), by_group),
            pl.BlockSpec((1, group_rows, 1), by_group),
            pl.BlockSpec((1, experts, group_rows), by_group),
            pl.BlockSpec((experts, 1), whole),
            pl.BlockSpec((experts, width), whole),
            pl.BlockSpec((1, group_rows, width), by_group),
            pl.BlockSpec((1, group_rows, width), by_group),
            weight(0),
            weight(1),
            weight(2),
        ],
        out_specs=[
            pl.BlockSpec((1, group_rows, width), by_group),
            pl.BlockSpec((1, group_rows, width), by_group),
            slots(width),
            slots(width),
            slots(ff),
            slots(ff),
            slots(ff),
            pl.BlockSpec((experts, width), whole),
        ],
        out_shape=[
            jax.ShapeDtypeStruct(tokens.shape, BF16),
            jax.ShapeDtypeStruct(tokens.shape, BF16),
            slots_shape(width),
            slots_shape(width),
            slots_shape(ff),
            slots_shape(ff),
            slots_shape(ff),
            jax.ShapeDtypeStruct((experts, width), F32),
        ],
        compiler_params=pltpu.CompilerParams(vmem_limit_bytes=VMEM_LIMIT),
        cost_estimate=LIGHT,
        name="expert",
    )(
        slot[:, None, :],
        slot[:, :, None],
        routed,
        own,
        router_t,
        tokens,
        cotangent,
        weights,
        weights,
        weights,
    )


def weight_grad_kernel(*refs, halves):
    rows, grad_out, hidden, grad_gate, grad_up, router = (
        refs[at : at + 2] for at in range(0, 12, 2)
    )
    moe_kept_ref, moe_got_ref, out_ref, moe_ref = refs[12:]
    moe_ref[...] = (moe_kept_ref[...].astype(F32) + moe_got_ref[...].astype(F32)).astype(BF16)
    columns = hidden[0].shape[1] // halves
    over = (((0,), (0,)), ((), ()))
    left_rows = [ref[...] for ref in rows]
    left_out = [ref[...] for ref in grad_out]
    router_columns = (router[0][...] + router[1][...]).T
    router_columns = jnp.concatenate(
        [
            router_columns,
            jnp.zeros((router_columns.shape[0], HEAD_SIZE - router_columns.shape[1]), F32),
        ],
        axis=1,
    ).astype(BF16)
    for half in range(halves):
        start = half * (3 * columns + HEAD_SIZE)
        part = slice(half * columns, (half + 1) * columns)
        for at, (left, right) in enumerate(
            ((left_rows, grad_gate), (left_rows, grad_up), (left_out, hidden))
        ):
            total = mxu(left[0], right[0][:, part], over) + mxu(left[1], right[1][:, part], over)
            out_ref[:, start + at * columns : start + (at + 1) * columns] = total.astype(BF16)
        out_ref[:, start + 3 * columns : start + 3 * columns + HEAD_SIZE] = router_columns


def weight_grads(near, far, moe_kept, moe_got, halves, block=256):
    rows_at, grad_out_at, hidden_at, grad_gate_at, grad_up_at, router_at = range(6)
    slots, width = near[rows_at].shape
    ff = near[hidden_at].shape[1]
    experts = near[router_at].shape[0]
    specs, operands = [], []
    for at in (rows_at, grad_out_at, hidden_at, grad_gate_at, grad_up_at, router_at):
        if at in (rows_at, grad_out_at):
            spec = pl.BlockSpec((slots, block), lambda i: (0, i))
        elif at == router_at:
            spec = pl.BlockSpec((experts, block), lambda i: (0, i))
        else:
            spec = pl.BlockSpec((slots, ff), lambda i: (0, 0))
        specs += [spec, spec]
        operands += [near[at], far[at]]
    columns = 3 * ff + halves * HEAD_SIZE
    moe_spec = pl.BlockSpec((moe_kept.shape[0], block), lambda i: (0, i))
    return pl.pallas_call(
        functools.partial(weight_grad_kernel, halves=halves),
        grid=(width // block,),
        in_specs=specs + [moe_spec, moe_spec],
        out_specs=[pl.BlockSpec((block, columns), lambda i: (i, 0)), moe_spec],
        out_shape=[
            jax.ShapeDtypeStruct((width, columns), BF16),
            jax.ShapeDtypeStruct(moe_kept.shape, BF16),
        ],
        compiler_params=pltpu.CompilerParams(vmem_limit_bytes=VMEM_LIMIT),
        cost_estimate=pl.CostEstimate(
            flops=15_000_000_000, bytes_accessed=50_000_000, transcendentals=0
        ),
        name="weight_grads",
    )(*operands, moe_kept, moe_got)


def on_device(
    block_input,
    norm_gains,
    router_weight,
    query_matrix,
    key_matrix,
    value_matrix,
    output_weight,
    gate_weight,
    up_weight,
    down_weight,
    segment_ids,
    routes,
    priority,
    cotangent,
):
    tensor_index = lax.axis_index("tensor")
    own_rows, width = block_input.shape
    group_rows = segment_ids.shape[0]
    halves = lax.axis_size("tensor")
    outer = lax.axis_size("outer")
    groups = lax.axis_size("x") * lax.axis_size("core")
    plane = groups * halves
    shard_rows = query_matrix.shape[0]
    dp_size = outer * groups
    seq_len = min(SEQ_MOST, group_rows * dp_size)
    own_start = lax.axis_index(ALL) * own_rows
    capacity = group_rows * TOPK // EXPERTS
    reach = ATTEND_SPAN // own_rows
    half_ff = gate_weight.shape[2]
    ff = half_ff * halves

    query_columns = query_matrix.shape[1]
    pair_columns = 2 * halves * HEAD_SIZE
    first = tensor_index == 0
    qkv_own = jnp.concatenate([query_matrix, key_matrix, value_matrix], axis=1)
    qkv_other = swap(qkv_own, "tensor")
    qkv_first = jnp.where(first, qkv_own, qkv_other)
    qkv_second = jnp.where(first, qkv_other, qkv_own)
    query_shard = jnp.concatenate(
        [qkv_first[:, :query_columns], qkv_second[:, :query_columns]], axis=1
    )
    early = jnp.concatenate(
        [qkv_first[:, query_columns:], qkv_second[:, query_columns:], output_weight], axis=1
    )
    segment_near = jnp.concatenate(
        [shift_groups(segment_ids, 2), shift_groups(segment_ids, 1), segment_ids]
    )
    query_shard, early, segment_near, gate_own, up_own, down_own = lax.optimization_barrier(
        (query_shard, early, segment_near, gate_weight, up_weight, down_weight)
    )
    query_full = lax.all_gather(query_shard, DP, axis=0, tiled=True)
    early = outer_gather(early)

    expert_shard = jnp.transpose(jnp.stack([gate_own, up_own, down_own]), (2, 0, 1, 3))
    expert_shard = lax.all_to_all(expert_shard, PLANE, 0, 0, tiled=True)
    early, expert_shard = lax.optimization_barrier((early, expert_shard))
    expert_shard = expert_shard.reshape(groups, halves, 3, shard_rows, half_ff)
    expert_shard = jnp.transpose(expert_shard, (2, 1, 0, 3, 4)).reshape(
        3, halves, groups * shard_rows, half_ff
    )
    expert_once = next_outer(expert_shard)

    key_value_full = early[:, :, :pair_columns]
    key_value_full = in_order(key_value_full, swap(key_value_full, "x"), "x", 1)
    key_value_full = in_order(key_value_full, swap(key_value_full, "core"), "core", 2)
    key_value_full = key_value_full.reshape(width, pair_columns)
    output_parts = plane_parts(early[:, :, pair_columns:])

    input_wide = block_input.astype(F32)
    first_gain = norm_gains[:, 0]
    second_gain = norm_gains[:, 1]
    first_factor = norm_factor(input_wide)
    normed_in = (input_wide * first_factor * first_gain).astype(BF16)
    positions = own_start + jnp.arange(own_rows, dtype=jnp.int32)
    cosine, sine = rotary_tables(positions % seq_len)
    query_blocks = halves * query_columns // (2 * HEAD_SIZE)
    key_value_sent = project(
        normed_in, key_value_full, cosine, sine, 0, halves, (True, False)
    )
    one_back, two_back = shift_groups(key_value_sent, 1), shift_groups(key_value_sent, 2)
    output_parts, one_back, two_back, priority_here = lax.optimization_barrier(
        (output_parts, one_back, two_back, priority)
    )
    pair_count = group_rows * TOPK
    rank = (
        jnp.zeros((pair_count,), jnp.int32)
        .at[priority_here]
        .set(jnp.arange(pair_count, dtype=jnp.int32))
        .reshape(group_rows, TOPK)
    )
    expert_ids = jnp.arange(EXPERTS, dtype=jnp.int32)
    named = routes[:, :, None] == expert_ids[None, None, :]
    ranked = jnp.sum(jnp.where(named, rank[:, :, None] + 1, 0), axis=1)
    ranked = jnp.where(ranked > 0, ranked, pair_count + 1)
    ranked_own = lax.dynamic_slice_in_dim(ranked, tensor_index * own_rows, own_rows, 0)
    digits = jnp.concatenate([ranked_own // 64, ranked_own % 64], axis=1).astype(BF16)
    digits = jnp.pad(digits, ((0, 0), (0, HEAD_SIZE - digits.shape[1])))
    cotangent_sent = jnp.concatenate([cotangent, digits], axis=1)
    pair_sent = jnp.where(
        first,
        jnp.stack([one_back, key_value_sent]),
        jnp.stack([two_back, one_back]),
    )
    pair_got = swap(pair_sent, "tensor")
    pieces = [two_back, pair_got[0], one_back, pair_got[1], key_value_sent]
    output_near = plane_stack(output_parts)
    output_far = swap(output_near, "core")
    queries = project(normed_in, query_full, cosine, sine, 0, query_blocks, (True, True))
    queries, expert_once, cotangent_sent = lax.optimization_barrier(
        (queries, expert_once, cotangent_sent)
    )
    expert_twice = next_outer(expert_once)
    cotangent_near, cotangent_far = plane_gather(cotangent_sent)
    key_value = jnp.concatenate(pieces, axis=0)
    span = ATTEND_SPAN + own_rows
    segment_ext = lax.dynamic_slice_in_dim(segment_near, tensor_index * own_rows, span)
    view = (
        jnp.reshape(own_start, (1,)),
        segment_ext[:, None],
        segment_ext[None, ATTEND_SPAN:],
        queries,
        key_value,
    )
    heads_low, log_total = attention(*view, seq_len)
    output_full = whole_weight(output_near, output_far)
    hidden_state = input_wide + dot(heads_low, output_full, ((1,), (1,)))
    second_factor = norm_factor(hidden_state)
    normed_mid_own = (hidden_state * second_factor * second_gain).astype(BF16)

    normed_parts, expert_twice = lax.optimization_barrier(
        (plane_parts(normed_mid_own), expert_twice)
    )
    normed_near = plane_stack(normed_parts)
    normed_far = swap(normed_near, "core")
    expert_full = round_planes([expert_shard, expert_once, expert_twice])
    expert = lax.axis_index(PLANE)
    own_expert = (expert_ids == expert).astype(F32)[:, None]
    router_t = router_weight.T

    def experts_on(tokens, cotangents):
        digits = cotangents[..., width:].reshape(2, group_rows, HEAD_SIZE).astype(jnp.int32)
        ranked_all = digits[..., :EXPERTS] * 64 + digits[..., EXPERTS : 2 * EXPERTS]
        routed = jnp.swapaxes((ranked_all <= pair_count).astype(F32), 1, 2)
        rank_own = jnp.sum(jnp.where(expert_ids == expert, ranked_all, 0), axis=-1)
        earlier = (rank_own[:, None, :] < rank_own[:, :, None]).astype(jnp.int32)
        slot = jnp.where(rank_own <= pair_count, jnp.sum(earlier, axis=-1), capacity)
        return expert_groups(
            slot,
            routed,
            own_expert,
            router_t,
            tokens.reshape(2, group_rows, width),
            cotangents.reshape(2, group_rows, -1),
            expert_full,
            capacity,
        )

    on_near = experts_on(normed_near, cotangent_near)
    on_far = experts_on(normed_far, cotangent_far)
    blocks = (2 * halves, own_rows, width)
    (grad_near, moe_near), (grad_far, moe_far) = (
        [array.reshape(blocks) for array in side[:2]] for side in (on_near, on_far)
    )
    grad_blocks = fold_blocks(grad_near, swap(grad_far, "core"))
    grad_blocks, moe_far, on_near, on_far = lax.optimization_barrier(
        (grad_blocks, moe_far, on_near[2:], on_far[2:])
    )
    grad_mid_parts = fold_plane(grad_blocks)
    expert_part, moe_total = weight_grads(
        on_near,
        on_far,
        moe_near.reshape(-1, width),
        swap(moe_far, "core").reshape(-1, width),
        halves,
    )
    expert_sum = lax.psum_scatter(expert_part, "outer", scatter_dimension=0, tiled=True)
    grad_mid_parts, moe_total = lax.optimization_barrier((grad_mid_parts, moe_total))
    moe_parts = fold_plane(list(moe_total.reshape(blocks)))
    grad_mid = wide_sum(grad_mid_parts)

    norm_input_part = norm_back(hidden_state, second_factor, second_gain, grad_mid)
    grad_state = cotangent.astype(F32) + norm_input_part
    grad_attn = grad_state.astype(BF16)
    grad_heads = dot(grad_attn, output_full, ((1,), (0,))).astype(BF16)
    output_total = fold_columns(grad_attn, heads_low, shard_rows)
    grad_query_pre, grad_far_kv, grad_own = attention_back(
        *view, log_total, grad_heads, cosine, sine, seq_len
    )
    grad_query_pre, output_total = lax.optimization_barrier((grad_query_pre, output_total))
    output_parts = fold_plane(distance_blocks(output_total))
    query_total = fold_columns(normed_in, grad_query_pre, shard_rows)
    query_parts = fold_plane(distance_blocks(query_total))
    two_back, pair_old, one_back, pair_new = grad_far_kv.reshape(reach, own_rows, -1)
    pair_old, pair_new = swap(jnp.stack([pair_old, pair_new]), "tensor").astype(F32)
    one_back = one_back.astype(F32) + jnp.where(first, pair_old, pair_new)
    two_back = two_back.astype(F32) + jnp.where(first, 0.0, pair_old)
    grad_own = grad_own + jnp.where(first, pair_new, 0.0)
    grad_own = grad_own + shift_groups(one_back.astype(BF16), -1).astype(F32)
    grad_own = grad_own + shift_groups(two_back.astype(BF16), -2).astype(F32)
    grad_own, output_parts, moe_parts = lax.optimization_barrier(
        (grad_own, output_parts, moe_parts)
    )
    grad_key_value = []
    for half in range(halves):
        start = half * 2 * HEAD_SIZE
        key_part = grad_own[:, start : start + HEAD_SIZE]
        turned = jnp.concatenate(
            [key_part[:, HEAD_SIZE // 2 :], key_part[:, : HEAD_SIZE // 2]], axis=1
        )
        grad_key_value.append(key_part * cosine - turned * sine)
        grad_key_value.append(grad_own[:, start + HEAD_SIZE : start + 2 * HEAD_SIZE])
    grad_key_value_pre = jnp.concatenate(grad_key_value, axis=1).astype(BF16)
    key_value_total = fold_columns(normed_in, grad_key_value_pre, shard_rows)
    key_value_parts = fold_plane(distance_blocks(key_value_total))
    grad_in = dot(grad_query_pre, query_full, ((1,), (1,))) + dot(
        grad_key_value_pre, key_value_full, ((1,), (1,))
    )
    input_grad = grad_state + norm_back(input_wide, first_factor, first_gain, grad_in)
    query_parts, key_value_parts, expert_sum = lax.optimization_barrier(
        (query_parts, key_value_parts, expert_sum)
    )
    output_weight_grad = outer_scatter(wide_sum(output_parts).astype(BF16))
    block_output = hidden_state + wide_sum(moe_parts)
    expert_sum = expert_sum.reshape(groups, shard_rows, halves, -1)
    expert_sum = jnp.swapaxes(expert_sum, 1, 2).reshape(plane, shard_rows, -1)
    expert_sum = lax.all_to_all(expert_sum, PLANE, 0, 0, tiled=True)
    gate_grad, up_grad, down_grad = (
        jnp.swapaxes(expert_sum[:, :, at * half_ff : (at + 1) * half_ff], 0, 1).astype(F32)
        for at in range(3)
    )
    router_grad = jnp.sum(expert_sum[:, :, 3 * half_ff : 3 * half_ff + EXPERTS].astype(F32), axis=0)
    router_grad = lax.dynamic_slice_in_dim(
        router_grad, tensor_index * (shard_rows // 2), shard_rows // 2, 0
    )
    qkv_grad = outer_scatter(
        jnp.concatenate([wide_sum(query_parts), wide_sum(key_value_parts)], axis=2).astype(BF16)
    )
    query_grad = qkv_grad[:, :query_columns]
    key_grad = qkv_grad[:, query_columns : query_columns + HEAD_SIZE]
    value_grad = qkv_grad[:, query_columns + HEAD_SIZE :]

    half_rows = shard_rows // 2
    own_gains = lax.dynamic_slice_in_dim(
        norm_gains, lax.axis_index(DP) * shard_rows, shard_rows, 0
    )
    first_sum = jnp.sum(qkv_grad * qkv_own.astype(F32), axis=-1)
    second_sum = jnp.sum(
        gate_grad * gate_weight.astype(F32) + up_grad * up_weight.astype(F32), axis=(1, 2)
    )
    gain_sums = jnp.stack([first_sum, second_sum], axis=1) / own_gains
    kept = lax.dynamic_slice_in_dim(gain_sums, tensor_index * half_rows, half_rows, 0)
    sent = lax.dynamic_slice_in_dim(gain_sums, (1 - tensor_index) * half_rows, half_rows, 0)
    own_router = lax.dynamic_slice_in_dim(
        router_weight, lax.axis_index(ALL) * half_rows, half_rows, 0
    )
    router_sum = jnp.sum(router_grad * own_router.astype(F32), axis=-1)
    half_gains = lax.dynamic_slice_in_dim(own_gains, tensor_index * half_rows, half_rows, 0)
    router_sum = router_sum / half_gains[:, 1]
    gains_grad = (
        kept
        + swap(sent, "tensor")
        + jnp.stack([jnp.zeros_like(router_sum), router_sum], axis=1)
    )
    return (
        block_output,
        input_grad,
        gains_grad,
        router_grad,
        query_grad,
        key_grad,
        value_grad,
        output_weight_grad,
        gate_grad,
        up_grad,
        down_grad,
    )


def solution(mesh):
    dp_size, tensor_size = mesh.shape["dp"], mesh.shape["tensor"]
    split = Mesh(mesh.devices.reshape(dp_size // 4, 2, 2, tensor_size), ALL)
    return jax.shard_map(
        on_device,
        mesh=split,
        in_specs=(
            P(ALL, None),
            P(),
            P(),
            P(DP, "tensor"),
            P(DP, "tensor"),
            P(DP, "tensor"),
            P(DP, "tensor"),
            P(DP, None, "tensor"),
            P(DP, None, "tensor"),
            P(DP, None, "tensor"),
            P(DP),
            P(DP, None),
            P(DP),
            P(ALL, None),
        ),
        out_specs=(
            P(ALL, None),
            P(ALL, None),
            P(ALL, None),
            P(ALL, None),
            P(DP, "tensor"),
            P(DP, "tensor"),
            P(DP, "tensor"),
            P(DP, "tensor"),
            P(DP, None, "tensor"),
            P(DP, None, "tensor"),
            P(DP, None, "tensor"),
        ),
        check_vma=False,
    )
```

```python
import functools
import math

import jax
import jax.numpy as jnp
from jax import lax
from jax.experimental import pallas as pl
from jax.experimental.pallas import tpu as pltpu
from jax.sharding import Mesh
from jax.sharding import PartitionSpec as P

HEAD_SIZE = 128
TOPK = 4
EXPERTS = 8
ATTEND_SPAN = 1024
SEQ_MOST = 16384
EPSILON = 1e-06
ROPE_BASE = 10000.0
BF16 = jnp.bfloat16
F32 = jnp.float32

DP = ("outer", "x", "core")
PLANE = ("x", "core", "tensor")
ALL = ("outer", "x", "core", "tensor")


def shift_groups(x, by):
    length = lax.axis_size(DP)
    return lax.ppermute(x, DP, [(i, i + by) for i in range(length) if 0 <= i + by < length])


def swap(x, axis):
    length = lax.axis_size(axis)
    return lax.ppermute(x, axis, [(i, length - 1 - i) for i in range(length)])


def plane_parts(own):
    return [own, swap(own, "tensor"), swap(own, "x"), swap(own, ("x", "tensor"))]


def plane_stack(parts):
    return jnp.stack(parts).reshape((2, 2) + parts[0].shape)


def plane_gather(own):
    near = plane_stack(plane_parts(own))
    return near, swap(near, "core")


def whole_weight(near, far):
    x, tensor = lax.axis_index("x"), lax.axis_index("tensor")
    first = lax.axis_index("core") == 0
    by_core = [jnp.where(first, near, far), jnp.where(first, far, near)]

    def piece(x_at, core_at, tensor_at):
        picked = lax.dynamic_index_in_dim(by_core[core_at], x ^ x_at, 0, keepdims=False)
        return lax.dynamic_index_in_dim(picked, tensor ^ tensor_at, 0, keepdims=False)

    places = [(x_at, core_at) for x_at in range(2) for core_at in range(2)]
    halves = [jnp.stack([piece(*place, at) for place in places], 1) for at in range(2)]
    return jnp.concatenate(halves, axis=-1).reshape(-1, 2 * near.shape[-1])


def fold_core(kept, sent):
    return (kept.astype(F32) + swap(sent, "core").astype(F32)).astype(BF16)


def fold_blocks(kept, got):
    return [
        (kept[at].astype(F32) + got[at].astype(F32)).astype(BF16) for at in range(kept.shape[0])
    ]


def in_order(own, other, axis_name, axis):
    first = lax.axis_index(axis_name) == 0
    return jnp.stack([jnp.where(first, own, other), jnp.where(first, other, own)], axis)


def fold_plane(blocks):
    return [
        blocks[0],
        swap(blocks[1], "tensor"),
        swap(blocks[2], "x"),
        swap(blocks[3], ("x", "tensor")),
    ]


def wide_sum(parts):
    return sum(part.astype(F32) for part in parts)


def outer_shift(x, by):
    length = lax.axis_size("outer")
    return lax.ppermute(x, "outer", [(i, (i + by) % length) for i in range(length)])


def outer_gather(shard):
    length, here = lax.axis_size("outer"), lax.axis_index("outer")
    if length > 4:
        return lax.all_gather(shard, "outer")
    full = jnp.zeros((length,) + shard.shape, shard.dtype)
    for by in range(length):
        piece = outer_shift(shard, by) if by else shard
        full = lax.dynamic_update_slice_in_dim(full, piece[None], (here - by) % length, 0)
    return full


def outer_scatter(parts):
    length, here = lax.axis_size("outer"), lax.axis_index("outer")
    if length > 4:
        return lax.psum_scatter(parts, "outer", scatter_dimension=0, tiled=False).astype(F32)
    total = None
    for by in range(length):
        piece = lax.dynamic_index_in_dim(parts, (here + by) % length, 0, keepdims=False)
        piece = (outer_shift(piece, by) if by else piece).astype(F32)
        total = piece if total is None else total + piece
    return total


def core_columns(rows, core_at, shard_rows):
    count = rows.shape[0]
    split = rows.reshape(count, -1, 2, shard_rows)
    return lax.dynamic_index_in_dim(split, core_at, 2, keepdims=False).reshape(count, -1)


def fold_columns(left, right, shard_rows):
    core = lax.axis_index("core")
    sent = dot(core_columns(left, 1 - core, shard_rows), right, ((0,), (0,))).astype(BF16)
    kept = dot(core_columns(left, core, shard_rows), right, ((0,), (0,))).astype(BF16)
    return fold_core(kept, sent).reshape(-1, 2, shard_rows, right.shape[1])


def distance_blocks(total):
    x, tensor = lax.axis_index("x"), lax.axis_index("tensor")
    columns = total.shape[3] // 2
    blocks = []
    for x_by in range(2):
        for tensor_by in range(2):
            block = lax.dynamic_index_in_dim(total, x ^ x_by, 1, keepdims=False)
            start = (tensor ^ tensor_by) * columns
            blocks.append(lax.dynamic_slice_in_dim(block, start, columns, 2))
    return blocks


def rotary_tables(position):
    halfway = HEAD_SIZE // 2
    inverse = jnp.exp(
        jnp.arange(halfway, dtype=F32) * (-2.0 * math.log(ROPE_BASE) / HEAD_SIZE)
    )
    angles = position.astype(F32)[:, None] * inverse[None, :]
    cosine, sine = jnp.cos(angles), jnp.sin(angles)
    return (
        jnp.concatenate([cosine, cosine], axis=1),
        jnp.concatenate([-sine, sine], axis=1),
    )


def norm_factor(value_rows):
    return lax.rsqrt(jnp.mean(value_rows * value_rows, axis=-1, keepdims=True) + EPSILON)


def norm_back(value_rows, factor, gain, upstream):
    weighted = upstream * gain
    return factor * weighted - value_rows * (factor * factor * factor) * jnp.mean(
        weighted * value_rows, axis=-1, keepdims=True
    )


def dot(a, b, dims):
    return lax.dot_general(a, b, (dims, ((), ())), preferred_element_type=F32)


VMEM_LIMIT = 60 * 1024 * 1024
LIGHT = pl.CostEstimate(flops=1000, bytes_accessed=1000, transcendentals=0)
FROM_LAST = (((1,), (1,)), ((), ()))
PLAIN = (((1,), (0,)), ((), ()))


def mxu(a, b, dims=PLAIN):
    return lax.dot_general(a, b, dims, preferred_element_type=F32)


def turn(rows, cosine, sine):
    return rows * cosine + pltpu.roll(rows, HEAD_SIZE // 2, 1) * sine


def project_kernel(rows_ref, weight_ref, cosine_ref, sine_ref, out_ref, *, turned):
    product = mxu(rows_ref[...], weight_ref[...])
    for at, turns in enumerate(turned):
        part = product[:, at * HEAD_SIZE : (at + 1) * HEAD_SIZE]
        if turns:
            part = turn(part, cosine_ref[...], sine_ref[...])
        out_ref[:, at * HEAD_SIZE : (at + 1) * HEAD_SIZE] = part.astype(BF16)


def project(rows, weight, cosine, sine, first, count, turned):
    high, width = rows.shape
    columns = len(turned) * HEAD_SIZE
    return pl.pallas_call(
        functools.partial(project_kernel, turned=turned),
        grid=(count,),
        in_specs=[
            pl.BlockSpec((high, width), lambda j: (0, 0)),
            pl.BlockSpec((width, columns), lambda j: (0, first + j)),
            pl.BlockSpec((high, HEAD_SIZE), lambda j: (0, 0)),
            pl.BlockSpec((high, HEAD_SIZE), lambda j: (0, 0)),
        ],
        out_specs=pl.BlockSpec((high, columns), lambda j: (0, j)),
        out_shape=jax.ShapeDtypeStruct((high, count * columns), BF16),
        compiler_params=pltpu.CompilerParams(vmem_limit_bytes=VMEM_LIMIT),
        cost_estimate=LIGHT,
        name="project",
    )(rows, weight, cosine, sine)


def mask_bias(place_ref, segment_key_ref, segment_query_ref, bias_ref, seq_len):
    span, rows = bias_ref.shape
    start = place_ref[0]
    key_at = lax.broadcasted_iota(jnp.int32, (span, rows), 0)
    query_at = lax.broadcasted_iota(jnp.int32, (span, rows), 1) + ATTEND_SPAN
    distance = query_at - key_at
    position = start + query_at - ATTEND_SPAN
    sequence_at = query_at - lax.rem(position, seq_len)
    allowed = (distance >= 0) & (distance < ATTEND_SPAN) & (key_at >= sequence_at)
    allowed = allowed & (segment_key_ref[...] == segment_query_ref[...])
    bias_ref[...] = jnp.where(allowed, 0.0, -1e30)


def attention_kernel(
    place_ref,
    segment_key_ref,
    segment_query_ref,
    q_ref,
    kv_ref,
    heads_ref,
    lse_ref,
    bias_ref,
    *,
    seq_len,
    scale,
):
    @pl.when(pl.program_id(0) == 0)
    def _():
        mask_bias(place_ref, segment_key_ref, segment_query_ref, bias_ref, seq_len)

    rows = q_ref.shape[0]
    span = kv_ref.shape[0]
    count = q_ref.shape[1] // HEAD_SIZE
    value_t = kv_ref[:, HEAD_SIZE:].T
    chunks = span // rows
    for head in range(count):
        columns = slice(head * HEAD_SIZE, (head + 1) * HEAD_SIZE)
        query = q_ref[:, columns]
        scores = []
        for c in range(chunks):
            part = slice(c * rows, (c + 1) * rows)
            raw = mxu(kv_ref[part, :HEAD_SIZE], query, FROM_LAST)
            scores.append(raw * scale + bias_ref[part, :])
        top = functools.reduce(jnp.maximum, scores)
        top = jnp.max(top, axis=0, keepdims=True)
        total = jnp.zeros_like(top)
        out_t = jnp.zeros((HEAD_SIZE, rows), F32)
        for c in range(chunks):
            weight = jnp.exp(scores[c] - top)
            total = total + jnp.sum(weight, axis=0, keepdims=True)
            out_t = out_t + mxu(value_t[:, c * rows : (c + 1) * rows], weight.astype(BF16))
        heads_ref[:, columns] = (out_t / total).T.astype(BF16)
        lse_ref[0, head : head + 1, :] = top + jnp.log(total)


def attention(place, segment_key, segment_query, queries, key_value, seq_len):
    rows, all_columns = queries.shape
    span = key_value.shape[0]
    pairs = key_value.shape[1] // (2 * HEAD_SIZE)
    columns = all_columns // pairs
    return pl.pallas_call(
        functools.partial(attention_kernel, seq_len=seq_len, scale=1.0 / math.sqrt(HEAD_SIZE)),
        grid=(pairs,),
        in_specs=[
            pl.BlockSpec(memory_space=pltpu.SMEM),
            pl.BlockSpec((span, 1), lambda j: (0, 0)),
            pl.BlockSpec((1, rows), lambda j: (0, 0)),
            pl.BlockSpec((rows, columns), lambda j: (0, j)),
            pl.BlockSpec((span, 2 * HEAD_SIZE), lambda j: (0, j)),
        ],
        out_specs=[
            pl.BlockSpec((rows, columns), lambda j: (0, j)),
            pl.BlockSpec((1, columns // HEAD_SIZE, rows), lambda j: (j, 0, 0)),
        ],
        out_shape=[
            jax.ShapeDtypeStruct((rows, all_columns), BF16),
            jax.ShapeDtypeStruct((pairs, columns // HEAD_SIZE, rows), F32),
        ],
        scratch_shapes=[pltpu.VMEM((span, rows), F32)],
        compiler_params=pltpu.CompilerParams(vmem_limit_bytes=VMEM_LIMIT),
        cost_estimate=LIGHT,
        name="attention",
    )(place, segment_key, segment_query, queries, key_value)


def attention_back_kernel(
    place_ref,
    segment_key_ref,
    segment_query_ref,
    q_ref,
    kv_ref,
    lse_ref,
    dout_ref,
    cosine_ref,
    sine_ref,
    dq_ref,
    dkv_far_ref,
    dkv_own_ref,
    bias_ref,
    dkv_ref,
    *,
    seq_len,
    scale,
):
    @pl.when(pl.program_id(0) == 0)
    def _():
        mask_bias(place_ref, segment_key_ref, segment_query_ref, bias_ref, seq_len)

    rows = q_ref.shape[0]
    span = kv_ref.shape[0]
    count = q_ref.shape[1] // HEAD_SIZE
    key_t = kv_ref[:, :HEAD_SIZE].T
    chunks = span // rows
    dkv_ref[...] = jnp.zeros_like(dkv_ref)
    for head in range(count):
        columns = slice(head * HEAD_SIZE, (head + 1) * HEAD_SIZE)
        query = q_ref[:, columns]
        dout = dout_ref[:, columns]
        lse = lse_ref[0, head : head + 1, :]
        probs, dprobs = [], []
        row_dot = jnp.zeros_like(lse)
        for c in range(chunks):
            part = slice(c * rows, (c + 1) * rows)
            raw = mxu(kv_ref[part, :HEAD_SIZE], query, FROM_LAST)
            prob = jnp.exp(raw * scale + bias_ref[part, :] - lse)
            dprob = mxu(kv_ref[part, HEAD_SIZE:], dout, FROM_LAST)
            row_dot = row_dot + jnp.sum(prob * dprob, axis=0, keepdims=True)
            probs.append(prob)
            dprobs.append(dprob)
        dq_t = jnp.zeros((HEAD_SIZE, rows), F32)
        for c in range(chunks):
            part = slice(c * rows, (c + 1) * rows)
            dscore = (probs[c] * (dprobs[c] - row_dot)).astype(BF16)
            dkv_ref[part, :HEAD_SIZE] += mxu(dscore, query)
            dkv_ref[part, HEAD_SIZE:] += mxu(probs[c].astype(BF16), dout)
            dq_t = dq_t + mxu(key_t[:, part], dscore)
        dq_ref[:, columns] = turn(dq_t.T * scale, cosine_ref[...], -sine_ref[...]).astype(BF16)
    dkv_ref[:, :HEAD_SIZE] = dkv_ref[:, :HEAD_SIZE] * scale
    dkv_far_ref[...] = dkv_ref[: span - rows, :].astype(BF16)
    dkv_own_ref[...] = dkv_ref[span - rows :, :]


def attention_back(
    place, segment_key, segment_query, queries, key_value, lse, dout, cosine, sine, seq_len
):
    rows, all_columns = queries.shape
    span = key_value.shape[0]
    pairs = key_value.shape[1] // (2 * HEAD_SIZE)
    columns = all_columns // pairs
    return pl.pallas_call(
        functools.partial(
            attention_back_kernel, seq_len=seq_len, scale=1.0 / math.sqrt(HEAD_SIZE)
        ),
        grid=(pairs,),
        in_specs=[
            pl.BlockSpec(memory_space=pltpu.SMEM),
            pl.BlockSpec((span, 1), lambda j: (0, 0)),
            pl.BlockSpec((1, rows), lambda j: (0, 0)),
            pl.BlockSpec((rows, columns), lambda j: (0, j)),
            pl.BlockSpec((span, 2 * HEAD_SIZE), lambda j: (0, j)),
            pl.BlockSpec((1, columns // HEAD_SIZE, rows), lambda j: (j, 0, 0)),
            pl.BlockSpec((rows, columns), lambda j: (0, j)),
            pl.BlockSpec((rows, HEAD_SIZE), lambda j: (0, 0)),
            pl.BlockSpec((rows, HEAD_SIZE), lambda j: (0, 0)),
        ],
        out_specs=[
            pl.BlockSpec((rows, columns), lambda j: (0, j)),
            pl.BlockSpec((span - rows, 2 * HEAD_SIZE), lambda j: (0, j)),
            pl.BlockSpec((rows, 2 * HEAD_SIZE), lambda j: (0, j)),
        ],
        out_shape=[
            jax.ShapeDtypeStruct((rows, all_columns), BF16),
            jax.ShapeDtypeStruct((span - rows, key_value.shape[1]), BF16),
            jax.ShapeDtypeStruct((rows, key_value.shape[1]), F32),
        ],
        scratch_shapes=[
            pltpu.VMEM((span, rows), F32),
            pltpu.VMEM((span, 2 * HEAD_SIZE), F32),
        ],
        compiler_params=pltpu.CompilerParams(vmem_limit_bytes=VMEM_LIMIT),
        cost_estimate=LIGHT,
        name="attention_back",
    )(place, segment_key, segment_query, queries, key_value, lse, dout, cosine, sine)


def expert_kernel(
    slot_row_ref,
    slot_column_ref,
    routed_ref,
    own_ref,
    router_ref,
    tokens_ref,
    cotangent_ref,
    gate_ref,
    up_ref,
    down_ref,
    grad_ref,
    moe_ref,
    rows_in_ref,
    grad_out_ref,
    hidden_ref,
    grad_gate_ref,
    grad_up_ref,
    router_grad_ref,
    *,
    capacity,
):
    group_rows = tokens_ref.shape[1]
    tokens = tokens_ref[0]
    gate_weight, up_weight, down_weight = (
        jnp.concatenate(
            [ref[:, 0, half].reshape(-1, ref.shape[4]) for half in range(ref.shape[2])], axis=1
        )
        for ref in (gate_ref, up_ref, down_ref)
    )
    cotangent = cotangent_ref[0]
    routed = routed_ref[0] > 0.0
    logits = jnp.where(routed, mxu(router_ref[...], tokens, FROM_LAST), -1e30)
    weights = jnp.exp(logits - jnp.max(logits, axis=0, keepdims=True))
    weights = jnp.where(routed, weights, 0.0)
    gates = weights / jnp.sum(weights, axis=0, keepdims=True)
    own = own_ref[...]
    gate_own = jnp.sum(gates * own, axis=0, keepdims=True)
    place = slot_row_ref[0] == lax.broadcasted_iota(jnp.int32, (capacity, group_rows), 0)
    place_wide = jnp.where(place, 1.0, 0.0)
    place_low = place_wide.astype(BF16)
    back = slot_column_ref[0] == lax.broadcasted_iota(jnp.int32, (group_rows, capacity), 1)
    back_low = jnp.where(back, 1.0, 0.0).astype(BF16)
    coefficient = jnp.sum(place_wide * gate_own, axis=1, keepdims=True)

    rows_in = mxu(place_low, tokens).astype(BF16)
    rows_in_ref[...] = rows_in
    gate_pre = mxu(rows_in, gate_weight)
    up_pre = mxu(rows_in, up_weight)
    sigmoid = 1.0 / (1.0 + jnp.exp(-gate_pre))
    silu = gate_pre * sigmoid
    hidden = (silu * up_pre).astype(BF16)
    hidden_ref[...] = hidden
    slot_cotangent = mxu(place_low, cotangent)
    grad_out = (coefficient * slot_cotangent).astype(BF16)
    grad_out_ref[...] = grad_out
    grad_hidden = mxu(grad_out, down_weight)
    grad_up = (grad_hidden * silu).astype(BF16)
    grad_gate = (grad_hidden * up_pre * sigmoid * (1.0 + gate_pre * (1.0 - sigmoid))).astype(BF16)
    grad_up_ref[...] = grad_up
    grad_gate_ref[...] = grad_gate
    expert_out = mxu(hidden, down_weight, FROM_LAST)
    grad_slot = jnp.sum(slot_cotangent * expert_out, axis=1, keepdims=True)
    moe_ref[0] = mxu(back_low, (coefficient * expert_out).astype(BF16)).astype(BF16)

    grad_token = jnp.sum(place_wide * grad_slot, axis=0, keepdims=True)
    share = (grad_token * gate_own) * (own - gates)
    share_high = share.astype(BF16)
    share_low = (share - share_high.astype(F32)).astype(BF16)
    router_grad = mxu(share_high, tokens) + mxu(share_low, tokens)

    @pl.when(pl.program_id(0) == 0)
    def _():
        router_grad_ref[...] = router_grad

    @pl.when(pl.program_id(0) > 0)
    def _():
        router_grad_ref[...] += router_grad

    grad_in = mxu(grad_gate, gate_weight, FROM_LAST) + mxu(grad_up, up_weight, FROM_LAST)
    grad_ref[0] = (
        mxu(back_low, grad_in.astype(BF16)) + mxu(share.T.astype(BF16), router_ref[...])
    ).astype(BF16)


def expert_groups(slot, routed, own, router_t, tokens, cotangent, weights, capacity):
    count, group_rows, width = tokens.shape
    ff = weights.shape[2] * weights.shape[4]
    experts = router_t.shape[0]
    weight = lambda at: pl.BlockSpec(
        (weights.shape[0], 1) + weights.shape[2:], lambda g: (0, at, 0, 0, 0)
    )
    whole = lambda g: (0, 0)
    by_group = lambda g: (g, 0, 0)
    slots = lambda columns: pl.BlockSpec((capacity, columns), lambda g: (g, 0))
    slots_shape = lambda columns: jax.ShapeDtypeStruct((count * capacity, columns), BF16)
    return pl.pallas_call(
        functools.partial(expert_kernel, capacity=capacity),
        grid=(count,),
        in_specs=[
            pl.BlockSpec((1, 1, group_rows), by_group),
            pl.BlockSpec((1, group_rows, 1), by_group),
            pl.BlockSpec((1, experts, group_rows), by_group),
            pl.BlockSpec((experts, 1), whole),
            pl.BlockSpec((experts, width), whole),
            pl.BlockSpec((1, group_rows, width), by_group),
            pl.BlockSpec((1, group_rows, width), by_group),
            weight(0),
            weight(1),
            weight(2),
        ],
        out_specs=[
            pl.BlockSpec((1, group_rows, width), by_group),
            pl.BlockSpec((1, group_rows, width), by_group),
            slots(width),
            slots(width),
            slots(ff),
            slots(ff),
            slots(ff),
            pl.BlockSpec((experts, width), whole),
        ],
        out_shape=[
            jax.ShapeDtypeStruct(tokens.shape, BF16),
            jax.ShapeDtypeStruct(tokens.shape, BF16),
            slots_shape(width),
            slots_shape(width),
            slots_shape(ff),
            slots_shape(ff),
            slots_shape(ff),
            jax.ShapeDtypeStruct((experts, width), F32),
        ],
        compiler_params=pltpu.CompilerParams(vmem_limit_bytes=VMEM_LIMIT),
        cost_estimate=LIGHT,
        name="expert",
    )(
        slot[:, None, :],
        slot[:, :, None],
        routed,
        own,
        router_t,
        tokens,
        cotangent,
        weights,
        weights,
        weights,
    )


def weight_grad_kernel(*refs, halves):
    rows, grad_out, hidden, grad_gate, grad_up, router = (
        refs[at : at + 2] for at in range(0, 12, 2)
    )
    moe_kept_ref, moe_got_ref, out_ref, moe_ref = refs[12:]
    moe_ref[...] = (moe_kept_ref[...].astype(F32) + moe_got_ref[...].astype(F32)).astype(BF16)
    columns = hidden[0].shape[1] // halves
    over = (((0,), (0,)), ((), ()))
    left_rows = [ref[...] for ref in rows]
    left_out = [ref[...] for ref in grad_out]
    router_columns = (router[0][...] + router[1][...]).T
    router_columns = jnp.concatenate(
        [
            router_columns,
            jnp.zeros((router_columns.shape[0], HEAD_SIZE - router_columns.shape[1]), F32),
        ],
        axis=1,
    ).astype(BF16)
    for half in range(halves):
        start = half * (3 * columns + HEAD_SIZE)
        part = slice(half * columns, (half + 1) * columns)
        for at, (left, right) in enumerate(
            ((left_rows, grad_gate), (left_rows, grad_up), (left_out, hidden))
        ):
            total = mxu(left[0], right[0][:, part], over) + mxu(left[1], right[1][:, part], over)
            out_ref[:, start + at * columns : start + (at + 1) * columns] = total.astype(BF16)
        out_ref[:, start + 3 * columns : start + 3 * columns + HEAD_SIZE] = router_columns


def weight_grads(near, far, moe_kept, moe_got, halves, block=256):
    rows_at, grad_out_at, hidden_at, grad_gate_at, grad_up_at, router_at = range(6)
    slots, width = near[rows_at].shape
    ff = near[hidden_at].shape[1]
    experts = near[router_at].shape[0]
    specs, operands = [], []
    for at in (rows_at, grad_out_at, hidden_at, grad_gate_at, grad_up_at, router_at):
        if at in (rows_at, grad_out_at):
            spec = pl.BlockSpec((slots, block), lambda i: (0, i))
        elif at == router_at:
            spec = pl.BlockSpec((experts, block), lambda i: (0, i))
        else:
            spec = pl.BlockSpec((slots, ff), lambda i: (0, 0))
        specs += [spec, spec]
        operands += [near[at], far[at]]
    columns = 3 * ff + halves * HEAD_SIZE
    moe_spec = pl.BlockSpec((moe_kept.shape[0], block), lambda i: (0, i))
    return pl.pallas_call(
        functools.partial(weight_grad_kernel, halves=halves),
        grid=(width // block,),
        in_specs=specs + [moe_spec, moe_spec],
        out_specs=[pl.BlockSpec((block, columns), lambda i: (i, 0)), moe_spec],
        out_shape=[
            jax.ShapeDtypeStruct((width, columns), BF16),
            jax.ShapeDtypeStruct(moe_kept.shape, BF16),
        ],
        compiler_params=pltpu.CompilerParams(vmem_limit_bytes=VMEM_LIMIT),
        cost_estimate=pl.CostEstimate(
            flops=15_000_000_000, bytes_accessed=50_000_000, transcendentals=0
        ),
        name="weight_grads",
    )(*operands, moe_kept, moe_got)


def on_device(
    block_input,
    norm_gains,
    router_weight,
    query_matrix,
    key_matrix,
    value_matrix,
    output_weight,
    gate_weight,
    up_weight,
    down_weight,
    segment_ids,
    routes,
    priority,
    cotangent,
):
    tensor_index = lax.axis_index("tensor")
    own_rows, width = block_input.shape
    group_rows = segment_ids.shape[0]
    halves = lax.axis_size("tensor")
    outer = lax.axis_size("outer")
    groups = lax.axis_size("x") * lax.axis_size("core")
    plane = groups * halves
    shard_rows = query_matrix.shape[0]
    dp_size = outer * groups
    seq_len = min(SEQ_MOST, group_rows * dp_size)
    own_start = lax.axis_index(ALL) * own_rows
    capacity = group_rows * TOPK // EXPERTS
    reach = ATTEND_SPAN // own_rows
    half_ff = gate_weight.shape[2]
    ff = half_ff * halves

    query_columns = query_matrix.shape[1]
    pair_columns = 2 * halves * HEAD_SIZE
    first = tensor_index == 0
    key_value_weight = jnp.concatenate([key_matrix, value_matrix], axis=1)
    other_weight = swap(key_value_weight, "tensor")
    early = jnp.concatenate(
        [
            jnp.where(first, key_value_weight, other_weight),
            jnp.where(first, other_weight, key_value_weight),
            query_matrix,
            output_weight,
        ],
        axis=1,
    )
    segment_near = jnp.concatenate(
        [shift_groups(segment_ids, 2), shift_groups(segment_ids, 1), segment_ids]
    )
    early, segment_near, gate_own, up_own, down_own = lax.optimization_barrier(
        (early, segment_near, gate_weight, up_weight, down_weight)
    )
    early = outer_gather(early)

    expert_shard = jnp.transpose(jnp.stack([gate_own, up_own, down_own]), (2, 0, 1, 3))
    expert_shard = lax.all_to_all(expert_shard, PLANE, 0, 0, tiled=True)
    early, expert_shard = lax.optimization_barrier((early, expert_shard))
    expert_shard = expert_shard.reshape(groups, halves, 3, shard_rows, half_ff)
    expert_shard = jnp.transpose(expert_shard, (2, 1, 0, 3, 4)).reshape(-1, half_ff)
    expert_full = lax.all_gather(expert_shard, "outer").reshape(
        outer, 3, halves, groups * shard_rows, half_ff
    )

    key_value_full = early[:, :, :pair_columns]
    key_value_full = in_order(key_value_full, swap(key_value_full, "x"), "x", 1)
    key_value_full = in_order(key_value_full, swap(key_value_full, "core"), "core", 2)
    key_value_full = key_value_full.reshape(width, pair_columns)
    query_parts = plane_parts(early[:, :, pair_columns : pair_columns + query_columns])

    input_wide = block_input.astype(F32)
    first_gain = norm_gains[:, 0]
    second_gain = norm_gains[:, 1]
    first_factor = norm_factor(input_wide)
    normed_in = (input_wide * first_factor * first_gain).astype(BF16)
    positions = own_start + jnp.arange(own_rows, dtype=jnp.int32)
    cosine, sine = rotary_tables(positions % seq_len)
    query_blocks = halves * query_columns // (2 * HEAD_SIZE)
    key_value_sent = project(
        normed_in, key_value_full, cosine, sine, 0, halves, (True, False)
    )
    one_back, two_back = shift_groups(key_value_sent, 1), shift_groups(key_value_sent, 2)
    query_parts, output_own, one_back, two_back, priority_here = lax.optimization_barrier(
        (query_parts, early[:, :, pair_columns + query_columns :], one_back, two_back, priority)
    )
    pair_count = group_rows * TOPK
    rank = (
        jnp.zeros((pair_count,), jnp.int32)
        .at[priority_here]
        .set(jnp.arange(pair_count, dtype=jnp.int32))
        .reshape(group_rows, TOPK)
    )
    expert_ids = jnp.arange(EXPERTS, dtype=jnp.int32)
    named = routes[:, :, None] == expert_ids[None, None, :]
    ranked = jnp.sum(jnp.where(named, rank[:, :, None] + 1, 0), axis=1)
    ranked = jnp.where(ranked > 0, ranked, pair_count + 1)
    ranked_own = lax.dynamic_slice_in_dim(ranked, tensor_index * own_rows, own_rows, 0)
    digits = jnp.concatenate([ranked_own // 64, ranked_own % 64], axis=1).astype(BF16)
    digits = jnp.pad(digits, ((0, 0), (0, HEAD_SIZE - digits.shape[1])))
    cotangent_sent = jnp.concatenate([cotangent, digits], axis=1)
    pair_sent = jnp.where(
        first,
        jnp.stack([one_back, key_value_sent]),
        jnp.stack([two_back, one_back]),
    )
    pair_got = swap(pair_sent, "tensor")
    pieces = [two_back, pair_got[0], one_back, pair_got[1], key_value_sent]
    query_near = plane_stack(query_parts)
    query_full = whole_weight(query_near, swap(query_near, "core"))
    output_parts = plane_parts(output_own)
    queries = project(normed_in, query_full, cosine, sine, 0, query_blocks, (True, True))
    queries, output_parts = lax.optimization_barrier((queries, output_parts))
    output_near = plane_stack(output_parts)
    output_far = swap(output_near, "core")
    cotangent_sent, output_near = lax.optimization_barrier((cotangent_sent, output_near))
    cotangent_near, cotangent_far = plane_gather(cotangent_sent)
    key_value = jnp.concatenate(pieces, axis=0)
    span = ATTEND_SPAN + own_rows
    segment_ext = lax.dynamic_slice_in_dim(segment_near, tensor_index * own_rows, span)
    view = (
        jnp.reshape(own_start, (1,)),
        segment_ext[:, None],
        segment_ext[None, ATTEND_SPAN:],
        queries,
        key_value,
    )
    heads_low, log_total = attention(*view, seq_len)
    output_full = whole_weight(output_near, output_far)
    hidden_state = input_wide + dot(heads_low, output_full, ((1,), (1,)))
    second_factor = norm_factor(hidden_state)
    normed_mid_own = (hidden_state * second_factor * second_gain).astype(BF16)

    normed_near, normed_far = plane_gather(normed_mid_own)
    expert = lax.axis_index(PLANE)
    own_expert = (expert_ids == expert).astype(F32)[:, None]
    router_t = router_weight.T

    def experts_on(tokens, cotangents):
        digits = cotangents[..., width:].reshape(2, group_rows, HEAD_SIZE).astype(jnp.int32)
        ranked_all = digits[..., :EXPERTS] * 64 + digits[..., EXPERTS : 2 * EXPERTS]
        routed = jnp.swapaxes((ranked_all <= pair_count).astype(F32), 1, 2)
        rank_own = jnp.sum(jnp.where(expert_ids == expert, ranked_all, 0), axis=-1)
        earlier = (rank_own[:, None, :] < rank_own[:, :, None]).astype(jnp.int32)
        slot = jnp.where(rank_own <= pair_count, jnp.sum(earlier, axis=-1), capacity)
        return expert_groups(
            slot,
            routed,
            own_expert,
            router_t,
            tokens.reshape(2, group_rows, width),
            cotangents.reshape(2, group_rows, -1),
            expert_full,
            capacity,
        )

    on_near = experts_on(normed_near, cotangent_near)
    on_far = experts_on(normed_far, cotangent_far)
    blocks = (2 * halves, own_rows, width)
    (grad_near, moe_near), (grad_far, moe_far) = (
        [array.reshape(blocks) for array in side[:2]] for side in (on_near, on_far)
    )
    grad_blocks = fold_blocks(grad_near, swap(grad_far, "core"))
    grad_blocks, moe_far, on_near, on_far = lax.optimization_barrier(
        (grad_blocks, moe_far, on_near[2:], on_far[2:])
    )
    grad_mid_parts = fold_plane(grad_blocks)
    moe_got = swap(moe_far, "core")
    moe_got, grad_mid_parts[1] = lax.optimization_barrier((moe_got, grad_mid_parts[1]))
    expert_part, moe_total = weight_grads(
        on_near, on_far, moe_near.reshape(-1, width), moe_got.reshape(-1, width), halves
    )
    expert_sum = lax.psum_scatter(expert_part, "outer", scatter_dimension=0, tiled=True)
    grad_mid_parts, moe_total = lax.optimization_barrier((grad_mid_parts, moe_total))
    moe_parts = fold_plane(list(moe_total.reshape(blocks)))
    grad_mid = wide_sum(grad_mid_parts)

    norm_input_part = norm_back(hidden_state, second_factor, second_gain, grad_mid)
    grad_state = cotangent.astype(F32) + norm_input_part
    grad_attn = grad_state.astype(BF16)
    grad_heads = dot(grad_attn, output_full, ((1,), (0,))).astype(BF16)
    output_total = fold_columns(grad_attn, heads_low, shard_rows)
    grad_query_pre, grad_far_kv, grad_own = attention_back(
        *view, log_total, grad_heads, cosine, sine, seq_len
    )
    grad_query_pre, grad_far_kv, output_total, moe_parts = lax.optimization_barrier(
        (grad_query_pre, grad_far_kv, output_total, moe_parts)
    )
    output_parts = fold_plane(distance_blocks(output_total))
    two_back, pair_old, one_back, pair_new = grad_far_kv.reshape(reach, own_rows, -1)
    pair_old, pair_new = swap(jnp.stack([pair_old, pair_new]), "tensor").astype(F32)
    one_back = one_back.astype(F32) + jnp.where(first, pair_old, pair_new)
    two_back = two_back.astype(F32) + jnp.where(first, 0.0, pair_old)
    grad_own = grad_own + jnp.where(first, pair_new, 0.0)
    grad_own = grad_own + shift_groups(one_back.astype(BF16), -1).astype(F32)
    grad_own = grad_own + shift_groups(two_back.astype(BF16), -2).astype(F32)
    grad_key_value = []
    for half in range(halves):
        start = half * 2 * HEAD_SIZE
        key_part = grad_own[:, start : start + HEAD_SIZE]
        turned = jnp.concatenate(
            [key_part[:, HEAD_SIZE // 2 :], key_part[:, : HEAD_SIZE // 2]], axis=1
        )
        grad_key_value.append(key_part * cosine - turned * sine)
        grad_key_value.append(grad_own[:, start + HEAD_SIZE : start + 2 * HEAD_SIZE])
    grad_key_value_pre = jnp.concatenate(grad_key_value, axis=1).astype(BF16)
    grad_qkv_pre = jnp.concatenate(
        [
            grad_query_pre.reshape(own_rows, halves, -1),
            grad_key_value_pre.reshape(own_rows, halves, -1),
        ],
        axis=2,
    ).reshape(own_rows, -1)
    qkv_total = fold_columns(normed_in, grad_qkv_pre, shard_rows)
    qkv_total, output_parts = lax.optimization_barrier((qkv_total, output_parts))
    qkv_parts = fold_plane(distance_blocks(qkv_total))
    grad_in = dot(grad_query_pre, query_full, ((1,), (1,))) + dot(
        grad_key_value_pre, key_value_full, ((1,), (1,))
    )
    input_grad = grad_state + norm_back(input_wide, first_factor, first_gain, grad_in)
    qkv_parts, expert_sum = lax.optimization_barrier((qkv_parts, expert_sum))
    attention_grad = outer_scatter(
        jnp.concatenate([wide_sum(qkv_parts), wide_sum(output_parts)], axis=2).astype(BF16)
    )
    qkv_columns = query_columns + 2 * HEAD_SIZE
    qkv_grad, output_weight_grad = (
        attention_grad[:, :qkv_columns],
        attention_grad[:, qkv_columns:],
    )
    block_output = hidden_state + wide_sum(moe_parts)
    expert_sum = expert_sum.reshape(groups, shard_rows, halves, -1)
    expert_sum = jnp.swapaxes(expert_sum, 1, 2).reshape(plane, shard_rows, -1)
    expert_sum = lax.all_to_all(expert_sum, PLANE, 0, 0, tiled=True)
    gate_grad, up_grad, down_grad = (
        jnp.swapaxes(expert_sum[:, :, at * half_ff : (at + 1) * half_ff], 0, 1).astype(F32)
        for at in range(3)
    )
    router_grad = jnp.sum(expert_sum[:, :, 3 * half_ff : 3 * half_ff + EXPERTS].astype(F32), axis=0)
    router_grad = lax.dynamic_slice_in_dim(
        router_grad, tensor_index * (shard_rows // 2), shard_rows // 2, 0
    )
    query_grad = qkv_grad[:, :query_columns]
    key_grad = qkv_grad[:, query_columns : query_columns + HEAD_SIZE]
    value_grad = qkv_grad[:, query_columns + HEAD_SIZE :]

    half_rows = shard_rows // 2
    own_gains = lax.dynamic_slice_in_dim(
        norm_gains, lax.axis_index(DP) * shard_rows, shard_rows, 0
    )
    qkv_own = jnp.concatenate([query_matrix, key_value_weight], axis=1)
    first_sum = jnp.sum(qkv_grad * qkv_own.astype(F32), axis=-1)
    second_sum = jnp.sum(
        gate_grad * gate_weight.astype(F32) + up_grad * up_weight.astype(F32), axis=(1, 2)
    )
    gain_sums = jnp.stack([first_sum, second_sum], axis=1) / own_gains
    kept = lax.dynamic_slice_in_dim(gain_sums, tensor_index * half_rows, half_rows, 0)
    sent = lax.dynamic_slice_in_dim(gain_sums, (1 - tensor_index) * half_rows, half_rows, 0)
    own_router = lax.dynamic_slice_in_dim(
        router_weight, lax.axis_index(ALL) * half_rows, half_rows, 0
    )
    router_sum = jnp.sum(router_grad * own_router.astype(F32), axis=-1)
    half_gains = lax.dynamic_slice_in_dim(own_gains, tensor_index * half_rows, half_rows, 0)
    router_sum = router_sum / half_gains[:, 1]
    gains_grad = (
        kept
        + swap(sent, "tensor")
        + jnp.stack([jnp.zeros_like(router_sum), router_sum], axis=1)
    )
    return (
        block_output,
        input_grad,
        gains_grad,
        router_grad,
        query_grad,
        key_grad,
        value_grad,
        output_weight_grad,
        gate_grad,
        up_grad,
        down_grad,
    )


def solution(mesh):
    dp_size, tensor_size = mesh.shape["dp"], mesh.shape["tensor"]
    split = Mesh(mesh.devices.reshape(dp_size // 4, 2, 2, tensor_size), ALL)
    return jax.shard_map(
        on_device,
        mesh=split,
        in_specs=(
            P(ALL, None),
            P(),
            P(),
            P(DP, "tensor"),
            P(DP, "tensor"),
            P(DP, "tensor"),
            P(DP, "tensor"),
            P(DP, None, "tensor"),
            P(DP, None, "tensor"),
            P(DP, None, "tensor"),
            P(DP),
            P(DP, None),
            P(DP),
            P(ALL, None),
        ),
        out_specs=(
            P(ALL, None),
            P(ALL, None),
            P(ALL, None),
            P(ALL, None),
            P(DP, "tensor"),
            P(DP, "tensor"),
            P(DP, "tensor"),
            P(DP, "tensor"),
            P(DP, None, "tensor"),
            P(DP, None, "tensor"),
            P(DP, None, "tensor"),
        ),
        check_vma=False,
    )
```

```python
import functools
import math

import jax
import jax.numpy as jnp
from jax import lax
from jax.experimental import pallas as pl
from jax.experimental.pallas import tpu as pltpu
from jax.sharding import Mesh
from jax.sharding import PartitionSpec as P

HEAD_SIZE = 128
TOPK = 4
EXPERTS = 8
ATTEND_SPAN = 1024
SEQ_MOST = 16384
EPSILON = 1e-06
ROPE_BASE = 10000.0
BF16 = jnp.bfloat16
F32 = jnp.float32

DP = ("outer", "x", "core")
PLANE = ("x", "core", "tensor")
ALL = ("outer", "x", "core", "tensor")


def shift_groups(x, by):
    length = lax.axis_size(DP)
    return lax.ppermute(x, DP, [(i, i + by) for i in range(length) if 0 <= i + by < length])


def swap(x, axis):
    length = lax.axis_size(axis)
    return lax.ppermute(x, axis, [(i, length - 1 - i) for i in range(length)])


def plane_parts(own):
    return [own, swap(own, "tensor"), swap(own, "x"), swap(own, ("x", "tensor"))]


def plane_stack(parts):
    return jnp.stack(parts).reshape((2, 2) + parts[0].shape)


def whole_weight(near, far):
    x, tensor = lax.axis_index("x"), lax.axis_index("tensor")
    first = lax.axis_index("core") == 0
    by_core = [jnp.where(first, near, far), jnp.where(first, far, near)]

    def piece(x_at, core_at, tensor_at):
        picked = lax.dynamic_index_in_dim(by_core[core_at], x ^ x_at, 0, keepdims=False)
        return lax.dynamic_index_in_dim(picked, tensor ^ tensor_at, 0, keepdims=False)

    places = [(x_at, core_at) for x_at in range(2) for core_at in range(2)]
    halves = [jnp.stack([piece(*place, at) for place in places], 1) for at in range(2)]
    return jnp.concatenate(halves, axis=-1).reshape(-1, 2 * near.shape[-1])


def fold_core(kept, sent):
    return (kept.astype(F32) + swap(sent, "core").astype(F32)).astype(BF16)


def fold_blocks(kept, got):
    return [
        (kept[at].astype(F32) + got[at].astype(F32)).astype(BF16) for at in range(kept.shape[0])
    ]


def in_order(own, other, axis_name, axis):
    first = lax.axis_index(axis_name) == 0
    return jnp.stack([jnp.where(first, own, other), jnp.where(first, other, own)], axis)


def fold_plane(blocks):
    return [
        blocks[0],
        swap(blocks[1], "tensor"),
        swap(blocks[2], "x"),
        swap(blocks[3], ("x", "tensor")),
    ]


def wide_sum(parts):
    return sum(part.astype(F32) for part in parts)


def outer_shift(x, by):
    length = lax.axis_size("outer")
    return lax.ppermute(x, "outer", [(i, (i + by) % length) for i in range(length)])


def outer_gather(shard):
    length, here = lax.axis_size("outer"), lax.axis_index("outer")
    if length > 4:
        return lax.all_gather(shard, "outer")
    full = jnp.zeros((length,) + shard.shape, shard.dtype)
    for by in range(length):
        piece = outer_shift(shard, by) if by else shard
        full = lax.dynamic_update_slice_in_dim(full, piece[None], (here - by) % length, 0)
    return full


def outer_scatter(parts):
    length, here = lax.axis_size("outer"), lax.axis_index("outer")
    if length > 4:
        return lax.psum_scatter(parts, "outer", scatter_dimension=0, tiled=False).astype(F32)
    total = None
    for by in range(length):
        piece = lax.dynamic_index_in_dim(parts, (here + by) % length, 0, keepdims=False)
        piece = (outer_shift(piece, by) if by else piece).astype(F32)
        total = piece if total is None else total + piece
    return total


def core_columns(rows, core_at, shard_rows):
    count = rows.shape[0]
    split = rows.reshape(count, -1, 2, shard_rows)
    return lax.dynamic_index_in_dim(split, core_at, 2, keepdims=False).reshape(count, -1)


def fold_columns(left, right, shard_rows):
    core = lax.axis_index("core")
    sent = dot(core_columns(left, 1 - core, shard_rows), right, ((0,), (0,))).astype(BF16)
    kept = dot(core_columns(left, core, shard_rows), right, ((0,), (0,))).astype(BF16)
    return fold_core(kept, sent).reshape(-1, 2, shard_rows, right.shape[1])


def distance_blocks(total):
    x, tensor = lax.axis_index("x"), lax.axis_index("tensor")
    columns = total.shape[3] // 2
    blocks = []
    for x_by in range(2):
        for tensor_by in range(2):
            block = lax.dynamic_index_in_dim(total, x ^ x_by, 1, keepdims=False)
            start = (tensor ^ tensor_by) * columns
            blocks.append(lax.dynamic_slice_in_dim(block, start, columns, 2))
    return blocks


def rotary_tables(position):
    halfway = HEAD_SIZE // 2
    inverse = jnp.exp(
        jnp.arange(halfway, dtype=F32) * (-2.0 * math.log(ROPE_BASE) / HEAD_SIZE)
    )
    angles = position.astype(F32)[:, None] * inverse[None, :]
    cosine, sine = jnp.cos(angles), jnp.sin(angles)
    return (
        jnp.concatenate([cosine, cosine], axis=1),
        jnp.concatenate([-sine, sine], axis=1),
    )


def norm_factor(value_rows):
    return lax.rsqrt(jnp.mean(value_rows * value_rows, axis=-1, keepdims=True) + EPSILON)


def norm_back(value_rows, factor, gain, upstream):
    weighted = upstream * gain
    return factor * weighted - value_rows * (factor * factor * factor) * jnp.mean(
        weighted * value_rows, axis=-1, keepdims=True
    )


def dot(a, b, dims):
    return lax.dot_general(a, b, (dims, ((), ())), preferred_element_type=F32)


VMEM_LIMIT = 60 * 1024 * 1024
LIGHT = pl.CostEstimate(flops=1000, bytes_accessed=1000, transcendentals=0)
FROM_LAST = (((1,), (1,)), ((), ()))
PLAIN = (((1,), (0,)), ((), ()))


def mxu(a, b, dims=PLAIN):
    return lax.dot_general(a, b, dims, preferred_element_type=F32)


def turn(rows, cosine, sine):
    return rows * cosine + pltpu.roll(rows, HEAD_SIZE // 2, 1) * sine


def project_kernel(rows_ref, weight_ref, cosine_ref, sine_ref, out_ref, *, turned):
    product = mxu(rows_ref[...], weight_ref[...])
    for at, turns in enumerate(turned):
        part = product[:, at * HEAD_SIZE : (at + 1) * HEAD_SIZE]
        if turns:
            part = turn(part, cosine_ref[...], sine_ref[...])
        out_ref[:, at * HEAD_SIZE : (at + 1) * HEAD_SIZE] = part.astype(BF16)


def project(rows, weight, cosine, sine, first, count, turned):
    high, width = rows.shape
    columns = len(turned) * HEAD_SIZE
    return pl.pallas_call(
        functools.partial(project_kernel, turned=turned),
        grid=(count,),
        in_specs=[
            pl.BlockSpec((high, width), lambda j: (0, 0)),
            pl.BlockSpec((width, columns), lambda j: (0, first + j)),
            pl.BlockSpec((high, HEAD_SIZE), lambda j: (0, 0)),
            pl.BlockSpec((high, HEAD_SIZE), lambda j: (0, 0)),
        ],
        out_specs=pl.BlockSpec((high, columns), lambda j: (0, j)),
        out_shape=jax.ShapeDtypeStruct((high, count * columns), BF16),
        compiler_params=pltpu.CompilerParams(vmem_limit_bytes=VMEM_LIMIT),
        cost_estimate=LIGHT,
        name="project",
    )(rows, weight, cosine, sine)


def mask_bias(place_ref, segment_key_ref, segment_query_ref, bias_ref, seq_len):
    span, rows = bias_ref.shape
    start = place_ref[0]
    key_at = lax.broadcasted_iota(jnp.int32, (span, rows), 0)
    query_at = lax.broadcasted_iota(jnp.int32, (span, rows), 1) + ATTEND_SPAN
    distance = query_at - key_at
    position = start + query_at - ATTEND_SPAN
    sequence_at = query_at - lax.rem(position, seq_len)
    allowed = (distance >= 0) & (distance < ATTEND_SPAN) & (key_at >= sequence_at)
    allowed = allowed & (segment_key_ref[...] == segment_query_ref[...])
    bias_ref[...] = jnp.where(allowed, 0.0, -1e30)


def attention_kernel(
    place_ref,
    segment_key_ref,
    segment_query_ref,
    q_ref,
    kv_ref,
    heads_ref,
    lse_ref,
    bias_ref,
    *,
    seq_len,
    scale,
):
    @pl.when(pl.program_id(0) == 0)
    def _():
        mask_bias(place_ref, segment_key_ref, segment_query_ref, bias_ref, seq_len)

    rows = q_ref.shape[0]
    span = kv_ref.shape[0]
    count = q_ref.shape[1] // HEAD_SIZE
    value_t = kv_ref[:, HEAD_SIZE:].T
    chunks = span // rows
    for head in range(count):
        columns = slice(head * HEAD_SIZE, (head + 1) * HEAD_SIZE)
        query = q_ref[:, columns]
        scores = []
        for c in range(chunks):
            part = slice(c * rows, (c + 1) * rows)
            raw = mxu(kv_ref[part, :HEAD_SIZE], query, FROM_LAST)
            scores.append(raw * scale + bias_ref[part, :])
        top = functools.reduce(jnp.maximum, scores)
        top = jnp.max(top, axis=0, keepdims=True)
        total = jnp.zeros_like(top)
        out_t = jnp.zeros((HEAD_SIZE, rows), F32)
        for c in range(chunks):
            weight = jnp.exp(scores[c] - top)
            total = total + jnp.sum(weight, axis=0, keepdims=True)
            out_t = out_t + mxu(value_t[:, c * rows : (c + 1) * rows], weight.astype(BF16))
        heads_ref[:, columns] = (out_t / total).T.astype(BF16)
        lse_ref[0, head : head + 1, :] = top + jnp.log(total)


def attention(place, segment_key, segment_query, queries, key_value, seq_len):
    rows, all_columns = queries.shape
    span = key_value.shape[0]
    pairs = key_value.shape[1] // (2 * HEAD_SIZE)
    columns = all_columns // pairs
    return pl.pallas_call(
        functools.partial(attention_kernel, seq_len=seq_len, scale=1.0 / math.sqrt(HEAD_SIZE)),
        grid=(pairs,),
        in_specs=[
            pl.BlockSpec(memory_space=pltpu.SMEM),
            pl.BlockSpec((span, 1), lambda j: (0, 0)),
            pl.BlockSpec((1, rows), lambda j: (0, 0)),
            pl.BlockSpec((rows, columns), lambda j: (0, j)),
            pl.BlockSpec((span, 2 * HEAD_SIZE), lambda j: (0, j)),
        ],
        out_specs=[
            pl.BlockSpec((rows, columns), lambda j: (0, j)),
            pl.BlockSpec((1, columns // HEAD_SIZE, rows), lambda j: (j, 0, 0)),
        ],
        out_shape=[
            jax.ShapeDtypeStruct((rows, all_columns), BF16),
            jax.ShapeDtypeStruct((pairs, columns // HEAD_SIZE, rows), F32),
        ],
        scratch_shapes=[pltpu.VMEM((span, rows), F32)],
        compiler_params=pltpu.CompilerParams(vmem_limit_bytes=VMEM_LIMIT),
        cost_estimate=LIGHT,
        name="attention",
    )(place, segment_key, segment_query, queries, key_value)


def attention_back_kernel(
    place_ref,
    segment_key_ref,
    segment_query_ref,
    q_ref,
    kv_ref,
    lse_ref,
    dout_ref,
    cosine_ref,
    sine_ref,
    dq_ref,
    dkv_far_ref,
    dkv_own_ref,
    bias_ref,
    dkv_ref,
    *,
    seq_len,
    scale,
):
    @pl.when(pl.program_id(0) == 0)
    def _():
        mask_bias(place_ref, segment_key_ref, segment_query_ref, bias_ref, seq_len)

    rows = q_ref.shape[0]
    span = kv_ref.shape[0]
    count = q_ref.shape[1] // HEAD_SIZE
    key_t = kv_ref[:, :HEAD_SIZE].T
    chunks = span // rows
    dkv_ref[...] = jnp.zeros_like(dkv_ref)
    for head in range(count):
        columns = slice(head * HEAD_SIZE, (head + 1) * HEAD_SIZE)
        query = q_ref[:, columns]
        dout = dout_ref[:, columns]
        lse = lse_ref[0, head : head + 1, :]
        probs, dprobs = [], []
        row_dot = jnp.zeros_like(lse)
        for c in range(chunks):
            part = slice(c * rows, (c + 1) * rows)
            raw = mxu(kv_ref[part, :HEAD_SIZE], query, FROM_LAST)
            prob = jnp.exp(raw * scale + bias_ref[part, :] - lse)
            dprob = mxu(kv_ref[part, HEAD_SIZE:], dout, FROM_LAST)
            row_dot = row_dot + jnp.sum(prob * dprob, axis=0, keepdims=True)
            probs.append(prob)
            dprobs.append(dprob)
        dq_t = jnp.zeros((HEAD_SIZE, rows), F32)
        for c in range(chunks):
            part = slice(c * rows, (c + 1) * rows)
            dscore = (probs[c] * (dprobs[c] - row_dot)).astype(BF16)
            dkv_ref[part, :HEAD_SIZE] += mxu(dscore, query)
            dkv_ref[part, HEAD_SIZE:] += mxu(probs[c].astype(BF16), dout)
            dq_t = dq_t + mxu(key_t[:, part], dscore)
        dq_ref[:, columns] = turn(dq_t.T * scale, cosine_ref[...], -sine_ref[...]).astype(BF16)
    dkv_ref[:, :HEAD_SIZE] = dkv_ref[:, :HEAD_SIZE] * scale
    dkv_far_ref[...] = dkv_ref[: span - rows, :].astype(BF16)
    dkv_own_ref[...] = dkv_ref[span - rows :, :]


def attention_back(
    place, segment_key, segment_query, queries, key_value, lse, dout, cosine, sine, seq_len
):
    rows, all_columns = queries.shape
    span = key_value.shape[0]
    pairs = key_value.shape[1] // (2 * HEAD_SIZE)
    columns = all_columns // pairs
    return pl.pallas_call(
        functools.partial(
            attention_back_kernel, seq_len=seq_len, scale=1.0 / math.sqrt(HEAD_SIZE)
        ),
        grid=(pairs,),
        in_specs=[
            pl.BlockSpec(memory_space=pltpu.SMEM),
            pl.BlockSpec((span, 1), lambda j: (0, 0)),
            pl.BlockSpec((1, rows), lambda j: (0, 0)),
            pl.BlockSpec((rows, columns), lambda j: (0, j)),
            pl.BlockSpec((span, 2 * HEAD_SIZE), lambda j: (0, j)),
            pl.BlockSpec((1, columns // HEAD_SIZE, rows), lambda j: (j, 0, 0)),
            pl.BlockSpec((rows, columns), lambda j: (0, j)),
            pl.BlockSpec((rows, HEAD_SIZE), lambda j: (0, 0)),
            pl.BlockSpec((rows, HEAD_SIZE), lambda j: (0, 0)),
        ],
        out_specs=[
            pl.BlockSpec((rows, columns), lambda j: (0, j)),
            pl.BlockSpec((span - rows, 2 * HEAD_SIZE), lambda j: (0, j)),
            pl.BlockSpec((rows, 2 * HEAD_SIZE), lambda j: (0, j)),
        ],
        out_shape=[
            jax.ShapeDtypeStruct((rows, all_columns), BF16),
            jax.ShapeDtypeStruct((span - rows, key_value.shape[1]), BF16),
            jax.ShapeDtypeStruct((rows, key_value.shape[1]), F32),
        ],
        scratch_shapes=[
            pltpu.VMEM((span, rows), F32),
            pltpu.VMEM((span, 2 * HEAD_SIZE), F32),
        ],
        compiler_params=pltpu.CompilerParams(vmem_limit_bytes=VMEM_LIMIT),
        cost_estimate=pl.CostEstimate(
            flops=150_000_000_000, bytes_accessed=10_000_000, transcendentals=0
        ),
        name="attention_back",
    )(place, segment_key, segment_query, queries, key_value, lse, dout, cosine, sine)


def expert_kernel(
    slot_row_ref,
    slot_column_ref,
    routed_ref,
    own_ref,
    router_ref,
    tokens_ref,
    cotangent_ref,
    gate_ref,
    up_ref,
    down_ref,
    grad_ref,
    moe_ref,
    rows_in_ref,
    grad_out_ref,
    hidden_ref,
    grad_gate_ref,
    grad_up_ref,
    router_grad_ref,
    *,
    capacity,
):
    group_rows = tokens_ref.shape[1]
    tokens = tokens_ref[0]
    gate_weight, up_weight, down_weight = (
        jnp.concatenate(
            [ref[:, 0, half].reshape(-1, ref.shape[4]) for half in range(ref.shape[2])], axis=1
        )
        for ref in (gate_ref, up_ref, down_ref)
    )
    cotangent = cotangent_ref[0]
    routed = routed_ref[0] > 0.0
    logits = jnp.where(routed, mxu(router_ref[...], tokens, FROM_LAST), -1e30)
    weights = jnp.exp(logits - jnp.max(logits, axis=0, keepdims=True))
    weights = jnp.where(routed, weights, 0.0)
    gates = weights / jnp.sum(weights, axis=0, keepdims=True)
    own = own_ref[...]
    gate_own = jnp.sum(gates * own, axis=0, keepdims=True)
    place = slot_row_ref[0] == lax.broadcasted_iota(jnp.int32, (capacity, group_rows), 0)
    place_wide = jnp.where(place, 1.0, 0.0)
    place_low = place_wide.astype(BF16)
    back = slot_column_ref[0] == lax.broadcasted_iota(jnp.int32, (group_rows, capacity), 1)
    back_low = jnp.where(back, 1.0, 0.0).astype(BF16)
    coefficient = jnp.sum(place_wide * gate_own, axis=1, keepdims=True)

    rows_in = mxu(place_low, tokens).astype(BF16)
    rows_in_ref[...] = rows_in
    gate_pre = mxu(rows_in, gate_weight)
    up_pre = mxu(rows_in, up_weight)
    sigmoid = 1.0 / (1.0 + jnp.exp(-gate_pre))
    silu = gate_pre * sigmoid
    hidden = (silu * up_pre).astype(BF16)
    hidden_ref[...] = hidden
    slot_cotangent = mxu(place_low, cotangent)
    grad_out = (coefficient * slot_cotangent).astype(BF16)
    grad_out_ref[...] = grad_out
    grad_hidden = mxu(grad_out, down_weight)
    grad_up = (grad_hidden * silu).astype(BF16)
    grad_gate = (grad_hidden * up_pre * sigmoid * (1.0 + gate_pre * (1.0 - sigmoid))).astype(BF16)
    grad_up_ref[...] = grad_up
    grad_gate_ref[...] = grad_gate
    expert_out = mxu(hidden, down_weight, FROM_LAST)
    grad_slot = jnp.sum(slot_cotangent * expert_out, axis=1, keepdims=True)
    moe_ref[0] = mxu(back_low, (coefficient * expert_out).astype(BF16)).astype(BF16)

    grad_token = jnp.sum(place_wide * grad_slot, axis=0, keepdims=True)
    share = (grad_token * gate_own) * (own - gates)
    share_high = share.astype(BF16)
    share_low = (share - share_high.astype(F32)).astype(BF16)
    router_grad = mxu(share_high, tokens) + mxu(share_low, tokens)

    @pl.when(pl.program_id(0) == 0)
    def _():
        router_grad_ref[...] = router_grad

    @pl.when(pl.program_id(0) > 0)
    def _():
        router_grad_ref[...] += router_grad

    grad_in = mxu(grad_gate, gate_weight, FROM_LAST) + mxu(grad_up, up_weight, FROM_LAST)
    grad_ref[0] = (
        mxu(back_low, grad_in.astype(BF16)) + mxu(share.T.astype(BF16), router_ref[...])
    ).astype(BF16)


def expert_groups(slot, routed, own, router_t, tokens, cotangent, weights, capacity):
    count, group_rows, width = tokens.shape
    ff = weights.shape[2] * weights.shape[4]
    experts = router_t.shape[0]
    weight = lambda at: pl.BlockSpec(
        (weights.shape[0], 1) + weights.shape[2:], lambda g: (0, at, 0, 0, 0)
    )
    whole = lambda g: (0, 0)
    by_group = lambda g: (g, 0, 0)
    slots = lambda columns: pl.BlockSpec((capacity, columns), lambda g: (g, 0))
    slots_shape = lambda columns: jax.ShapeDtypeStruct((count * capacity, columns), BF16)
    return pl.pallas_call(
        functools.partial(expert_kernel, capacity=capacity),
        grid=(count,),
        in_specs=[
            pl.BlockSpec((1, 1, group_rows), by_group),
            pl.BlockSpec((1, group_rows, 1), by_group),
            pl.BlockSpec((1, experts, group_rows), by_group),
            pl.BlockSpec((experts, 1), whole),
            pl.BlockSpec((experts, width), whole),
            pl.BlockSpec((1, group_rows, width), by_group),
            pl.BlockSpec((1, group_rows, width), by_group),
            weight(0),
            weight(1),
            weight(2),
        ],
        out_specs=[
            pl.BlockSpec((1, group_rows, width), by_group),
            pl.BlockSpec((1, group_rows, width), by_group),
            slots(width),
            slots(width),
            slots(ff),
            slots(ff),
            slots(ff),
            pl.BlockSpec((experts, width), whole),
        ],
        out_shape=[
            jax.ShapeDtypeStruct(tokens.shape, BF16),
            jax.ShapeDtypeStruct(tokens.shape, BF16),
            slots_shape(width),
            slots_shape(width),
            slots_shape(ff),
            slots_shape(ff),
            slots_shape(ff),
            jax.ShapeDtypeStruct((experts, width), F32),
        ],
        compiler_params=pltpu.CompilerParams(vmem_limit_bytes=VMEM_LIMIT),
        cost_estimate=LIGHT,
        name="expert",
    )(
        slot[:, None, :],
        slot[:, :, None],
        routed,
        own,
        router_t,
        tokens,
        cotangent,
        weights,
        weights,
        weights,
    )


def weight_grad_kernel(*refs, halves):
    rows, grad_out, hidden, grad_gate, grad_up, router = (
        refs[at : at + 2] for at in range(0, 12, 2)
    )
    moe_kept_ref, moe_got_ref, out_ref, moe_ref = refs[12:]
    moe_ref[...] = (moe_kept_ref[...].astype(F32) + moe_got_ref[...].astype(F32)).astype(BF16)
    columns = hidden[0].shape[1] // halves
    over = (((0,), (0,)), ((), ()))
    left_rows = [ref[...] for ref in rows]
    left_out = [ref[...] for ref in grad_out]
    router_columns = (router[0][...] + router[1][...]).T
    router_columns = jnp.concatenate(
        [
            router_columns,
            jnp.zeros((router_columns.shape[0], HEAD_SIZE - router_columns.shape[1]), F32),
        ],
        axis=1,
    ).astype(BF16)
    for half in range(halves):
        start = half * (3 * columns + HEAD_SIZE)
        part = slice(half * columns, (half + 1) * columns)
        for at, (left, right) in enumerate(
            ((left_rows, grad_gate), (left_rows, grad_up), (left_out, hidden))
        ):
            total = mxu(left[0], right[0][:, part], over) + mxu(left[1], right[1][:, part], over)
            out_ref[:, start + at * columns : start + (at + 1) * columns] = total.astype(BF16)
        out_ref[:, start + 3 * columns : start + 3 * columns + HEAD_SIZE] = router_columns


def weight_grads(near, far, moe_kept, moe_got, halves, block=256):
    rows_at, grad_out_at, hidden_at, grad_gate_at, grad_up_at, router_at = range(6)
    slots, width = near[rows_at].shape
    ff = near[hidden_at].shape[1]
    experts = near[router_at].shape[0]
    specs, operands = [], []
    for at in (rows_at, grad_out_at, hidden_at, grad_gate_at, grad_up_at, router_at):
        if at in (rows_at, grad_out_at):
            spec = pl.BlockSpec((slots, block), lambda i: (0, i))
        elif at == router_at:
            spec = pl.BlockSpec((experts, block), lambda i: (0, i))
        else:
            spec = pl.BlockSpec((slots, ff), lambda i: (0, 0))
        specs += [spec, spec]
        operands += [near[at], far[at]]
    columns = 3 * ff + halves * HEAD_SIZE
    moe_spec = pl.BlockSpec((moe_kept.shape[0], block), lambda i: (0, i))
    return pl.pallas_call(
        functools.partial(weight_grad_kernel, halves=halves),
        grid=(width // block,),
        in_specs=specs + [moe_spec, moe_spec],
        out_specs=[pl.BlockSpec((block, columns), lambda i: (i, 0)), moe_spec],
        out_shape=[
            jax.ShapeDtypeStruct((width, columns), BF16),
            jax.ShapeDtypeStruct(moe_kept.shape, BF16),
        ],
        compiler_params=pltpu.CompilerParams(vmem_limit_bytes=VMEM_LIMIT),
        cost_estimate=pl.CostEstimate(
            flops=15_000_000_000, bytes_accessed=50_000_000, transcendentals=0
        ),
        name="weight_grads",
    )(*operands, moe_kept, moe_got)


def on_device(
    block_input,
    norm_gains,
    router_weight,
    query_matrix,
    key_matrix,
    value_matrix,
    output_weight,
    gate_weight,
    up_weight,
    down_weight,
    segment_ids,
    routes,
    priority,
    cotangent,
):
    tensor_index = lax.axis_index("tensor")
    own_rows, width = block_input.shape
    group_rows = segment_ids.shape[0]
    halves = lax.axis_size("tensor")
    outer = lax.axis_size("outer")
    groups = lax.axis_size("x") * lax.axis_size("core")
    plane = groups * halves
    shard_rows = query_matrix.shape[0]
    dp_size = outer * groups
    seq_len = min(SEQ_MOST, group_rows * dp_size)
    own_start = lax.axis_index(ALL) * own_rows
    capacity = group_rows * TOPK // EXPERTS
    reach = ATTEND_SPAN // own_rows
    half_ff = gate_weight.shape[2]
    ff = half_ff * halves

    query_columns = query_matrix.shape[1]
    pair_columns = 2 * halves * HEAD_SIZE
    first = tensor_index == 0
    key_value_weight = jnp.concatenate([key_matrix, value_matrix], axis=1)
    other_weight = swap(key_value_weight, "tensor")
    early = jnp.concatenate(
        [
            jnp.where(first, key_value_weight, other_weight),
            jnp.where(first, other_weight, key_value_weight),
            query_matrix,
            output_weight,
        ],
        axis=1,
    )
    segment_near = jnp.concatenate(
        [shift_groups(segment_ids, 2), shift_groups(segment_ids, 1), segment_ids]
    )
    early, segment_near, gate_own, up_own, down_own = lax.optimization_barrier(
        (early, segment_near, gate_weight, up_weight, down_weight)
    )
    early = outer_gather(early)

    expert_shard = jnp.transpose(jnp.stack([gate_own, up_own, down_own]), (2, 0, 1, 3))
    expert_shard = lax.all_to_all(expert_shard, PLANE, 0, 0, tiled=True)
    pair_count = group_rows * TOPK
    rank = (
        jnp.zeros((pair_count,), jnp.int32)
        .at[priority]
        .set(jnp.arange(pair_count, dtype=jnp.int32))
        .reshape(group_rows, TOPK)
    )
    expert_ids = jnp.arange(EXPERTS, dtype=jnp.int32)
    named = routes[:, :, None] == expert_ids[None, None, :]
    ranked = jnp.sum(jnp.where(named, rank[:, :, None] + 1, 0), axis=1)
    ranked = jnp.where(ranked > 0, ranked, pair_count + 1)
    ranked_own = lax.dynamic_slice_in_dim(ranked, tensor_index * own_rows, own_rows, 0)
    digits = jnp.concatenate([ranked_own // 64, ranked_own % 64], axis=1).astype(BF16)
    digits = jnp.pad(digits, ((0, 0), (0, HEAD_SIZE - digits.shape[1])))
    cotangent_sent = jnp.concatenate([cotangent, digits], axis=1)
    expert_shard = expert_shard.reshape(groups, halves, 3, shard_rows, half_ff)
    expert_shard = jnp.transpose(expert_shard, (2, 1, 0, 3, 4)).reshape(-1, half_ff)
    early, expert_shard, cotangent_sent = lax.optimization_barrier(
        (early, expert_shard, cotangent_sent)
    )
    expert_full = lax.all_gather(expert_shard, "outer").reshape(
        outer, 3, halves, groups * shard_rows, half_ff
    )

    key_value_full = early[:, :, :pair_columns]
    key_value_full = in_order(key_value_full, swap(key_value_full, "x"), "x", 1)
    key_value_full = in_order(key_value_full, swap(key_value_full, "core"), "core", 2)
    key_value_full = key_value_full.reshape(width, pair_columns)
    query_parts = plane_parts(early[:, :, pair_columns : pair_columns + query_columns])

    input_wide = block_input.astype(F32)
    first_gain = norm_gains[:, 0]
    second_gain = norm_gains[:, 1]
    first_factor = norm_factor(input_wide)
    normed_in = (input_wide * first_factor * first_gain).astype(BF16)
    positions = own_start + jnp.arange(own_rows, dtype=jnp.int32)
    cosine, sine = rotary_tables(positions % seq_len)
    query_blocks = halves * query_columns // (2 * HEAD_SIZE)
    key_value_sent = project(
        normed_in, key_value_full, cosine, sine, 0, halves, (True, False)
    )
    one_back, two_back = shift_groups(key_value_sent, 1), shift_groups(key_value_sent, 2)
    query_parts, output_own, one_back, two_back = lax.optimization_barrier(
        (query_parts, early[:, :, pair_columns + query_columns :], one_back, two_back)
    )
    pair_sent = jnp.where(
        first,
        jnp.stack([one_back, key_value_sent]),
        jnp.stack([two_back, one_back]),
    )
    pair_got = swap(pair_sent, "tensor")
    query_near = plane_stack(query_parts)
    query_far, pair_got = lax.optimization_barrier((swap(query_near, "core"), pair_got))
    pieces = [two_back, pair_got[0], one_back, pair_got[1], key_value_sent]
    query_full = whole_weight(query_near, query_far)
    output_parts = plane_parts(output_own)
    queries = project(normed_in, query_full, cosine, sine, 0, query_blocks, (True, True))
    queries, output_parts = lax.optimization_barrier((queries, output_parts))
    output_near = plane_stack(output_parts)
    output_far = swap(output_near, "core")
    cotangent_sent, output_near = lax.optimization_barrier((cotangent_sent, output_near))
    cotangent_parts = plane_parts(cotangent_sent)
    key_value = jnp.concatenate(pieces, axis=0)
    span = ATTEND_SPAN + own_rows
    segment_ext = lax.dynamic_slice_in_dim(segment_near, tensor_index * own_rows, span)
    view = (
        jnp.reshape(own_start, (1,)),
        segment_ext[:, None],
        segment_ext[None, ATTEND_SPAN:],
        queries,
        key_value,
    )
    heads_low, log_total = attention(*view, seq_len)
    output_full = whole_weight(output_near, output_far)
    hidden_state = input_wide + dot(heads_low, output_full, ((1,), (1,)))
    second_factor = norm_factor(hidden_state)
    normed_mid_own = (hidden_state * second_factor * second_gain).astype(BF16)

    normed_parts, cotangent_parts = lax.optimization_barrier(
        (plane_parts(normed_mid_own), cotangent_parts)
    )
    normed_near = plane_stack(normed_parts)
    normed_far = swap(normed_near, "core")
    cotangent_near = plane_stack(cotangent_parts)
    cotangent_far = swap(cotangent_near, "core")
    expert = lax.axis_index(PLANE)
    own_expert = (expert_ids == expert).astype(F32)[:, None]
    router_t = router_weight.T

    def experts_on(tokens, cotangents):
        digits = cotangents[..., width:].reshape(2, group_rows, HEAD_SIZE).astype(jnp.int32)
        ranked_all = digits[..., :EXPERTS] * 64 + digits[..., EXPERTS : 2 * EXPERTS]
        routed = jnp.swapaxes((ranked_all <= pair_count).astype(F32), 1, 2)
        rank_own = jnp.sum(jnp.where(expert_ids == expert, ranked_all, 0), axis=-1)
        earlier = (rank_own[:, None, :] < rank_own[:, :, None]).astype(jnp.int32)
        slot = jnp.where(rank_own <= pair_count, jnp.sum(earlier, axis=-1), capacity)
        return expert_groups(
            slot,
            routed,
            own_expert,
            router_t,
            tokens.reshape(2, group_rows, width),
            cotangents.reshape(2, group_rows, -1),
            expert_full,
            capacity,
        )

    on_near = experts_on(normed_near, cotangent_near)
    on_far = experts_on(normed_far, cotangent_far)
    blocks = (2 * halves, own_rows, width)
    (grad_near, moe_near), (grad_far, moe_far) = (
        [array.reshape(blocks) for array in side[:2]] for side in (on_near, on_far)
    )
    grad_blocks = fold_blocks(grad_near, swap(grad_far, "core"))
    grad_blocks, moe_far, on_near, on_far = lax.optimization_barrier(
        (grad_blocks, moe_far, on_near[2:], on_far[2:])
    )
    grad_mid_parts = fold_plane(grad_blocks)
    moe_got = swap(moe_far, "core")
    expert_part, moe_total = weight_grads(
        on_near, on_far, moe_near.reshape(-1, width), moe_got.reshape(-1, width), halves
    )
    expert_sum = lax.psum_scatter(expert_part, "outer", scatter_dimension=0, tiled=True)
    grad_mid_parts, moe_total = lax.optimization_barrier((grad_mid_parts, moe_total))
    moe_parts = fold_plane(list(moe_total.reshape(blocks)))
    grad_mid = wide_sum(grad_mid_parts)

    norm_input_part = norm_back(hidden_state, second_factor, second_gain, grad_mid)
    grad_state = cotangent.astype(F32) + norm_input_part
    grad_attn = grad_state.astype(BF16)
    grad_heads = dot(grad_attn, output_full, ((1,), (0,))).astype(BF16)
    output_total = fold_columns(grad_attn, heads_low, shard_rows)
    grad_query_pre, grad_far_kv, grad_own = attention_back(
        *view, log_total, grad_heads, cosine, sine, seq_len
    )
    grad_query_pre, grad_far_kv, output_total, moe_parts = lax.optimization_barrier(
        (grad_query_pre, grad_far_kv, output_total, moe_parts)
    )
    output_parts = fold_plane(distance_blocks(output_total))
    two_back, pair_old, one_back, pair_new = grad_far_kv.reshape(reach, own_rows, -1)
    pair_old, pair_new = swap(jnp.stack([pair_old, pair_new]), "tensor").astype(F32)
    one_back = one_back.astype(F32) + jnp.where(first, pair_old, pair_new)
    two_back = two_back.astype(F32) + jnp.where(first, 0.0, pair_old)
    grad_own = grad_own + jnp.where(first, pair_new, 0.0)
    grad_own = grad_own + shift_groups(one_back.astype(BF16), -1).astype(F32)
    grad_own = grad_own + shift_groups(two_back.astype(BF16), -2).astype(F32)
    grad_own, output_parts = lax.optimization_barrier((grad_own, output_parts))
    output_weight_grad = outer_scatter(wide_sum(output_parts).astype(BF16))
    grad_key_value = []
    for half in range(halves):
        start = half * 2 * HEAD_SIZE
        key_part = grad_own[:, start : start + HEAD_SIZE]
        turned = jnp.concatenate(
            [key_part[:, HEAD_SIZE // 2 :], key_part[:, : HEAD_SIZE // 2]], axis=1
        )
        grad_key_value.append(key_part * cosine - turned * sine)
        grad_key_value.append(grad_own[:, start + HEAD_SIZE : start + 2 * HEAD_SIZE])
    grad_key_value_pre = jnp.concatenate(grad_key_value, axis=1).astype(BF16)
    grad_qkv_pre = jnp.concatenate(
        [
            grad_query_pre.reshape(own_rows, halves, -1),
            grad_key_value_pre.reshape(own_rows, halves, -1),
        ],
        axis=2,
    ).reshape(own_rows, -1)
    qkv_total = fold_columns(normed_in, grad_qkv_pre, shard_rows)
    qkv_parts = fold_plane(distance_blocks(qkv_total))
    grad_in = dot(grad_query_pre, query_full, ((1,), (1,))) + dot(
        grad_key_value_pre, key_value_full, ((1,), (1,))
    )
    input_grad = grad_state + norm_back(input_wide, first_factor, first_gain, grad_in)
    qkv_parts, expert_sum = lax.optimization_barrier((qkv_parts, expert_sum))
    qkv_grad = outer_scatter(wide_sum(qkv_parts).astype(BF16))
    block_output = hidden_state + wide_sum(moe_parts)
    expert_sum = expert_sum.reshape(groups, shard_rows, halves, -1)
    expert_sum = jnp.swapaxes(expert_sum, 1, 2).reshape(plane, shard_rows, -1)
    expert_sum = lax.all_to_all(expert_sum, PLANE, 0, 0, tiled=True)
    gate_grad, up_grad, down_grad = (
        jnp.swapaxes(expert_sum[:, :, at * half_ff : (at + 1) * half_ff], 0, 1).astype(F32)
        for at in range(3)
    )
    router_grad = jnp.sum(expert_sum[:, :, 3 * half_ff : 3 * half_ff + EXPERTS].astype(F32), axis=0)
    router_grad = lax.dynamic_slice_in_dim(
        router_grad, tensor_index * (shard_rows // 2), shard_rows // 2, 0
    )
    query_grad = qkv_grad[:, :query_columns]
    key_grad = qkv_grad[:, query_columns : query_columns + HEAD_SIZE]
    value_grad = qkv_grad[:, query_columns + HEAD_SIZE :]

    half_rows = shard_rows // 2
    own_gains = lax.dynamic_slice_in_dim(
        norm_gains, lax.axis_index(DP) * shard_rows, shard_rows, 0
    )
    qkv_own = jnp.concatenate([query_matrix, key_value_weight], axis=1)
    first_sum = jnp.sum(qkv_grad * qkv_own.astype(F32), axis=-1)
    second_sum = jnp.sum(
        gate_grad * gate_weight.astype(F32) + up_grad * up_weight.astype(F32), axis=(1, 2)
    )
    gain_sums = jnp.stack([first_sum, second_sum], axis=1) / own_gains
    kept = lax.dynamic_slice_in_dim(gain_sums, tensor_index * half_rows, half_rows, 0)
    sent = lax.dynamic_slice_in_dim(gain_sums, (1 - tensor_index) * half_rows, half_rows, 0)
    own_router = lax.dynamic_slice_in_dim(
        router_weight, lax.axis_index(ALL) * half_rows, half_rows, 0
    )
    router_sum = jnp.sum(router_grad * own_router.astype(F32), axis=-1)
    half_gains = lax.dynamic_slice_in_dim(own_gains, tensor_index * half_rows, half_rows, 0)
    router_sum = router_sum / half_gains[:, 1]
    gains_grad = (
        kept
        + swap(sent, "tensor")
        + jnp.stack([jnp.zeros_like(router_sum), router_sum], axis=1)
    )
    return (
        block_output,
        input_grad,
        gains_grad,
        router_grad,
        query_grad,
        key_grad,
        value_grad,
        output_weight_grad,
        gate_grad,
        up_grad,
        down_grad,
    )


def solution(mesh):
    dp_size, tensor_size = mesh.shape["dp"], mesh.shape["tensor"]
    split = Mesh(mesh.devices.reshape(dp_size // 4, 2, 2, tensor_size), ALL)
    return jax.shard_map(
        on_device,
        mesh=split,
        in_specs=(
            P(ALL, None),
            P(),
            P(),
            P(DP, "tensor"),
            P(DP, "tensor"),
            P(DP, "tensor"),
            P(DP, "tensor"),
            P(DP, None, "tensor"),
            P(DP, None, "tensor"),
            P(DP, None, "tensor"),
            P(DP),
            P(DP, None),
            P(DP),
            P(ALL, None),
        ),
        out_specs=(
            P(ALL, None),
            P(ALL, None),
            P(ALL, None),
            P(ALL, None),
            P(DP, "tensor"),
            P(DP, "tensor"),
            P(DP, "tensor"),
            P(DP, "tensor"),
            P(DP, None, "tensor"),
            P(DP, None, "tensor"),
            P(DP, None, "tensor"),
        ),
        check_vma=False,
    )
```

```python
import functools
import math

import jax
import jax.numpy as jnp
from jax import lax
from jax.experimental import pallas as pl
from jax.experimental.pallas import tpu as pltpu
from jax.sharding import Mesh
from jax.sharding import PartitionSpec as P

HEAD_SIZE = 128
TOPK = 4
EXPERTS = 8
ATTEND_SPAN = 1024
SEQ_MOST = 16384
EPSILON = 1e-06
ROPE_BASE = 10000.0
BF16 = jnp.bfloat16
F32 = jnp.float32

DP = ("outer", "x", "core")
PLANE = ("x", "core", "tensor")
ALL = ("outer", "x", "core", "tensor")


def shift_groups(x, by):
    length = lax.axis_size(DP)
    return lax.ppermute(x, DP, [(i, i + by) for i in range(length) if 0 <= i + by < length])


def swap(x, axis):
    length = lax.axis_size(axis)
    return lax.ppermute(x, axis, [(i, length - 1 - i) for i in range(length)])


def plane_parts(own):
    return [own, swap(own, "tensor"), swap(own, "x"), swap(own, ("x", "tensor"))]


def plane_stack(parts):
    return jnp.stack(parts).reshape((2, 2) + parts[0].shape)


def whole_weight(near, far):
    x, tensor = lax.axis_index("x"), lax.axis_index("tensor")
    first = lax.axis_index("core") == 0
    by_core = [jnp.where(first, near, far), jnp.where(first, far, near)]

    def piece(x_at, core_at, tensor_at):
        picked = lax.dynamic_index_in_dim(by_core[core_at], x ^ x_at, 0, keepdims=False)
        return lax.dynamic_index_in_dim(picked, tensor ^ tensor_at, 0, keepdims=False)

    places = [(x_at, core_at) for x_at in range(2) for core_at in range(2)]
    halves = [jnp.stack([piece(*place, at) for place in places], 1) for at in range(2)]
    return jnp.concatenate(halves, axis=-1).reshape(-1, 2 * near.shape[-1])


def fold_core(kept, sent):
    return (kept.astype(F32) + swap(sent, "core").astype(F32)).astype(BF16)


def fold_blocks(kept, got):
    return [
        (kept[at].astype(F32) + got[at].astype(F32)).astype(BF16) for at in range(kept.shape[0])
    ]


def in_order(own, other, axis_name, axis):
    first = lax.axis_index(axis_name) == 0
    return jnp.stack([jnp.where(first, own, other), jnp.where(first, other, own)], axis)


def fold_plane(blocks):
    return [
        blocks[0],
        swap(blocks[1], "tensor"),
        swap(blocks[2], "x"),
        swap(blocks[3], ("x", "tensor")),
    ]


def wide_sum(parts):
    return sum(part.astype(F32) for part in parts)


def outer_shift(x, by):
    length = lax.axis_size("outer")
    return lax.ppermute(x, "outer", [(i, (i + by) % length) for i in range(length)])


def outer_gather(shard):
    length, here = lax.axis_size("outer"), lax.axis_index("outer")
    if length > 4:
        return lax.all_gather(shard, "outer")
    full = jnp.zeros((length,) + shard.shape, shard.dtype)
    for by in range(length):
        piece = outer_shift(shard, by) if by else shard
        full = lax.dynamic_update_slice_in_dim(full, piece[None], (here - by) % length, 0)
    return full


def outer_scatter(parts, later=None):
    length, here = lax.axis_size("outer"), lax.axis_index("outer")
    if length > 4:
        total = lax.psum_scatter(parts, "outer", scatter_dimension=0, tiled=False).astype(F32)
        return total if later is None else (total, later)
    total = lax.dynamic_index_in_dim(parts, here, 0, keepdims=False)
    if later is not None:
        total, later = lax.optimization_barrier((total, later))
    total = total.astype(F32)
    for by in range(1, length):
        piece = lax.dynamic_index_in_dim(parts, (here + by) % length, 0, keepdims=False)
        total = total + outer_shift(piece, by).astype(F32)
    return total if later is None else (total, later)


def core_columns(rows, core_at, shard_rows):
    count = rows.shape[0]
    split = rows.reshape(count, -1, 2, shard_rows)
    return lax.dynamic_index_in_dim(split, core_at, 2, keepdims=False).reshape(count, -1)


def fold_columns(left, right, shard_rows):
    core = lax.axis_index("core")
    sent = dot(core_columns(left, 1 - core, shard_rows), right, ((0,), (0,))).astype(BF16)
    kept = dot(core_columns(left, core, shard_rows), right, ((0,), (0,))).astype(BF16)
    return fold_core(kept, sent).reshape(-1, 2, shard_rows, right.shape[1])


def distance_blocks(total):
    x, tensor = lax.axis_index("x"), lax.axis_index("tensor")
    columns = total.shape[3] // 2
    blocks = []
    for x_by in range(2):
        for tensor_by in range(2):
            block = lax.dynamic_index_in_dim(total, x ^ x_by, 1, keepdims=False)
            start = (tensor ^ tensor_by) * columns
            blocks.append(lax.dynamic_slice_in_dim(block, start, columns, 2))
    return blocks


def rotary_tables(position):
    halfway = HEAD_SIZE // 2
    inverse = jnp.exp(
        jnp.arange(halfway, dtype=F32) * (-2.0 * math.log(ROPE_BASE) / HEAD_SIZE)
    )
    angles = position.astype(F32)[:, None] * inverse[None, :]
    cosine, sine = jnp.cos(angles), jnp.sin(angles)
    return (
        jnp.concatenate([cosine, cosine], axis=1),
        jnp.concatenate([-sine, sine], axis=1),
    )


def norm_factor(value_rows):
    return lax.rsqrt(jnp.mean(value_rows * value_rows, axis=-1, keepdims=True) + EPSILON)


def norm_back(value_rows, factor, gain, upstream):
    weighted = upstream * gain
    return factor * weighted - value_rows * (factor * factor * factor) * jnp.mean(
        weighted * value_rows, axis=-1, keepdims=True
    )


def dot(a, b, dims):
    return lax.dot_general(a, b, (dims, ((), ())), preferred_element_type=F32)


VMEM_LIMIT = 60 * 1024 * 1024
LIGHT = pl.CostEstimate(flops=1000, bytes_accessed=1000, transcendentals=0)
FROM_LAST = (((1,), (1,)), ((), ()))
PLAIN = (((1,), (0,)), ((), ()))


def mxu(a, b, dims=PLAIN):
    return lax.dot_general(a, b, dims, preferred_element_type=F32)


def turn(rows, cosine, sine):
    return rows * cosine + pltpu.roll(rows, HEAD_SIZE // 2, 1) * sine


def project_kernel(rows_ref, weight_ref, cosine_ref, sine_ref, out_ref, *, turned):
    product = mxu(rows_ref[...], weight_ref[...])
    for at, turns in enumerate(turned):
        part = product[:, at * HEAD_SIZE : (at + 1) * HEAD_SIZE]
        if turns:
            part = turn(part, cosine_ref[...], sine_ref[...])
        out_ref[:, at * HEAD_SIZE : (at + 1) * HEAD_SIZE] = part.astype(BF16)


def project(rows, weight, cosine, sine, first, count, turned):
    high, width = rows.shape
    columns = len(turned) * HEAD_SIZE
    return pl.pallas_call(
        functools.partial(project_kernel, turned=turned),
        grid=(count,),
        in_specs=[
            pl.BlockSpec((high, width), lambda j: (0, 0)),
            pl.BlockSpec((width, columns), lambda j: (0, first + j)),
            pl.BlockSpec((high, HEAD_SIZE), lambda j: (0, 0)),
            pl.BlockSpec((high, HEAD_SIZE), lambda j: (0, 0)),
        ],
        out_specs=pl.BlockSpec((high, columns), lambda j: (0, j)),
        out_shape=jax.ShapeDtypeStruct((high, count * columns), BF16),
        compiler_params=pltpu.CompilerParams(vmem_limit_bytes=VMEM_LIMIT),
        cost_estimate=LIGHT,
        name="project",
    )(rows, weight, cosine, sine)


def mask_bias(place_ref, segment_key_ref, segment_query_ref, bias_ref, seq_len):
    span, rows = bias_ref.shape
    start = place_ref[0]
    key_at = lax.broadcasted_iota(jnp.int32, (span, rows), 0)
    query_at = lax.broadcasted_iota(jnp.int32, (span, rows), 1) + ATTEND_SPAN
    distance = query_at - key_at
    position = start + query_at - ATTEND_SPAN
    sequence_at = query_at - lax.rem(position, seq_len)
    allowed = (distance >= 0) & (distance < ATTEND_SPAN) & (key_at >= sequence_at)
    allowed = allowed & (segment_key_ref[...] == segment_query_ref[...])
    bias_ref[...] = jnp.where(allowed, 0.0, -1e30)


def attention_kernel(
    place_ref,
    segment_key_ref,
    segment_query_ref,
    q_ref,
    kv_ref,
    heads_ref,
    lse_ref,
    bias_ref,
    *,
    seq_len,
    scale,
):
    @pl.when(pl.program_id(0) == 0)
    def _():
        mask_bias(place_ref, segment_key_ref, segment_query_ref, bias_ref, seq_len)

    rows = q_ref.shape[0]
    span = kv_ref.shape[0]
    count = q_ref.shape[1] // HEAD_SIZE
    value_t = kv_ref[:, HEAD_SIZE:].T
    chunks = span // rows
    for head in range(count):
        columns = slice(head * HEAD_SIZE, (head + 1) * HEAD_SIZE)
        query = q_ref[:, columns]
        scores = []
        for c in range(chunks):
            part = slice(c * rows, (c + 1) * rows)
            raw = mxu(kv_ref[part, :HEAD_SIZE], query, FROM_LAST)
            scores.append(raw * scale + bias_ref[part, :])
        top = functools.reduce(jnp.maximum, scores)
        top = jnp.max(top, axis=0, keepdims=True)
        total = jnp.zeros_like(top)
        out_t = jnp.zeros((HEAD_SIZE, rows), F32)
        for c in range(chunks):
            weight = jnp.exp(scores[c] - top)
            total = total + jnp.sum(weight, axis=0, keepdims=True)
            out_t = out_t + mxu(value_t[:, c * rows : (c + 1) * rows], weight.astype(BF16))
        heads_ref[:, columns] = (out_t / total).T.astype(BF16)
        lse_ref[0, head : head + 1, :] = top + jnp.log(total)


def attention(place, segment_key, segment_query, queries, key_value, seq_len):
    rows, all_columns = queries.shape
    span = key_value.shape[0]
    pairs = key_value.shape[1] // (2 * HEAD_SIZE)
    columns = all_columns // pairs
    return pl.pallas_call(
        functools.partial(attention_kernel, seq_len=seq_len, scale=1.0 / math.sqrt(HEAD_SIZE)),
        grid=(pairs,),
        in_specs=[
            pl.BlockSpec(memory_space=pltpu.SMEM),
            pl.BlockSpec((span, 1), lambda j: (0, 0)),
            pl.BlockSpec((1, rows), lambda j: (0, 0)),
            pl.BlockSpec((rows, columns), lambda j: (0, j)),
            pl.BlockSpec((span, 2 * HEAD_SIZE), lambda j: (0, j)),
        ],
        out_specs=[
            pl.BlockSpec((rows, columns), lambda j: (0, j)),
            pl.BlockSpec((1, columns // HEAD_SIZE, rows), lambda j: (j, 0, 0)),
        ],
        out_shape=[
            jax.ShapeDtypeStruct((rows, all_columns), BF16),
            jax.ShapeDtypeStruct((pairs, columns // HEAD_SIZE, rows), F32),
        ],
        scratch_shapes=[pltpu.VMEM((span, rows), F32)],
        compiler_params=pltpu.CompilerParams(vmem_limit_bytes=VMEM_LIMIT),
        cost_estimate=LIGHT,
        name="attention",
    )(place, segment_key, segment_query, queries, key_value)


def attention_back_kernel(
    place_ref,
    segment_key_ref,
    segment_query_ref,
    q_ref,
    kv_ref,
    lse_ref,
    dout_ref,
    cosine_ref,
    sine_ref,
    dq_ref,
    dkv_far_ref,
    dkv_own_ref,
    bias_ref,
    dkv_ref,
    *,
    seq_len,
    scale,
):
    @pl.when(pl.program_id(0) == 0)
    def _():
        mask_bias(place_ref, segment_key_ref, segment_query_ref, bias_ref, seq_len)

    rows = q_ref.shape[0]
    span = kv_ref.shape[0]
    count = q_ref.shape[1] // HEAD_SIZE
    key_t = kv_ref[:, :HEAD_SIZE].T
    chunks = span // rows
    dkv_ref[...] = jnp.zeros_like(dkv_ref)
    for head in range(count):
        columns = slice(head * HEAD_SIZE, (head + 1) * HEAD_SIZE)
        query = q_ref[:, columns]
        dout = dout_ref[:, columns]
        lse = lse_ref[0, head : head + 1, :]
        probs, dprobs = [], []
        row_dot = jnp.zeros_like(lse)
        for c in range(chunks):
            part = slice(c * rows, (c + 1) * rows)
            raw = mxu(kv_ref[part, :HEAD_SIZE], query, FROM_LAST)
            prob = jnp.exp(raw * scale + bias_ref[part, :] - lse)
            dprob = mxu(kv_ref[part, HEAD_SIZE:], dout, FROM_LAST)
            row_dot = row_dot + jnp.sum(prob * dprob, axis=0, keepdims=True)
            probs.append(prob)
            dprobs.append(dprob)
        dq_t = jnp.zeros((HEAD_SIZE, rows), F32)
        for c in range(chunks):
            part = slice(c * rows, (c + 1) * rows)
            dscore = (probs[c] * (dprobs[c] - row_dot)).astype(BF16)
            dkv_ref[part, :HEAD_SIZE] += mxu(dscore, query)
            dkv_ref[part, HEAD_SIZE:] += mxu(probs[c].astype(BF16), dout)
            dq_t = dq_t + mxu(key_t[:, part], dscore)
        dq_ref[:, columns] = turn(dq_t.T * scale, cosine_ref[...], -sine_ref[...]).astype(BF16)
    dkv_ref[:, :HEAD_SIZE] = dkv_ref[:, :HEAD_SIZE] * scale
    dkv_far_ref[...] = dkv_ref[: span - rows, :].astype(BF16)
    dkv_own_ref[...] = dkv_ref[span - rows :, :]


def attention_back(
    place, segment_key, segment_query, queries, key_value, lse, dout, cosine, sine, seq_len
):
    rows, all_columns = queries.shape
    span = key_value.shape[0]
    pairs = key_value.shape[1] // (2 * HEAD_SIZE)
    columns = all_columns // pairs
    return pl.pallas_call(
        functools.partial(
            attention_back_kernel, seq_len=seq_len, scale=1.0 / math.sqrt(HEAD_SIZE)
        ),
        grid=(pairs,),
        in_specs=[
            pl.BlockSpec(memory_space=pltpu.SMEM),
            pl.BlockSpec((span, 1), lambda j: (0, 0)),
            pl.BlockSpec((1, rows), lambda j: (0, 0)),
            pl.BlockSpec((rows, columns), lambda j: (0, j)),
            pl.BlockSpec((span, 2 * HEAD_SIZE), lambda j: (0, j)),
            pl.BlockSpec((1, columns // HEAD_SIZE, rows), lambda j: (j, 0, 0)),
            pl.BlockSpec((rows, columns), lambda j: (0, j)),
            pl.BlockSpec((rows, HEAD_SIZE), lambda j: (0, 0)),
            pl.BlockSpec((rows, HEAD_SIZE), lambda j: (0, 0)),
        ],
        out_specs=[
            pl.BlockSpec((rows, columns), lambda j: (0, j)),
            pl.BlockSpec((span - rows, 2 * HEAD_SIZE), lambda j: (0, j)),
            pl.BlockSpec((rows, 2 * HEAD_SIZE), lambda j: (0, j)),
        ],
        out_shape=[
            jax.ShapeDtypeStruct((rows, all_columns), BF16),
            jax.ShapeDtypeStruct((span - rows, key_value.shape[1]), BF16),
            jax.ShapeDtypeStruct((rows, key_value.shape[1]), F32),
        ],
        scratch_shapes=[
            pltpu.VMEM((span, rows), F32),
            pltpu.VMEM((span, 2 * HEAD_SIZE), F32),
        ],
        compiler_params=pltpu.CompilerParams(vmem_limit_bytes=VMEM_LIMIT),
        cost_estimate=pl.CostEstimate(
            flops=70_000_000_000, bytes_accessed=10_000_000, transcendentals=0
        ),
        name="attention_back",
    )(place, segment_key, segment_query, queries, key_value, lse, dout, cosine, sine)


def expert_kernel(
    slot_row_ref,
    slot_column_ref,
    routed_ref,
    own_ref,
    router_ref,
    tokens_ref,
    cotangent_ref,
    gate_ref,
    up_ref,
    down_ref,
    grad_ref,
    moe_ref,
    rows_in_ref,
    grad_out_ref,
    hidden_ref,
    grad_gate_ref,
    grad_up_ref,
    router_grad_ref,
    *,
    capacity,
):
    group_rows = tokens_ref.shape[1]
    tokens = tokens_ref[0]
    gate_weight, up_weight, down_weight = (
        jnp.concatenate(
            [ref[:, half].reshape(-1, ref.shape[3]) for half in range(ref.shape[1])], axis=1
        )
        for ref in (gate_ref, up_ref, down_ref)
    )
    cotangent = cotangent_ref[0]
    routed = routed_ref[0] > 0.0
    logits = jnp.where(routed, mxu(router_ref[...], tokens, FROM_LAST), -1e30)
    weights = jnp.exp(logits - jnp.max(logits, axis=0, keepdims=True))
    weights = jnp.where(routed, weights, 0.0)
    gates = weights / jnp.sum(weights, axis=0, keepdims=True)
    own = own_ref[...]
    gate_own = jnp.sum(gates * own, axis=0, keepdims=True)
    place = slot_row_ref[0] == lax.broadcasted_iota(jnp.int32, (capacity, group_rows), 0)
    place_wide = jnp.where(place, 1.0, 0.0)
    place_low = place_wide.astype(BF16)
    back = slot_column_ref[0] == lax.broadcasted_iota(jnp.int32, (group_rows, capacity), 1)
    back_low = jnp.where(back, 1.0, 0.0).astype(BF16)
    coefficient = jnp.sum(place_wide * gate_own, axis=1, keepdims=True)

    rows_in = mxu(place_low, tokens).astype(BF16)
    rows_in_ref[...] = rows_in
    gate_pre = mxu(rows_in, gate_weight)
    up_pre = mxu(rows_in, up_weight)
    sigmoid = 1.0 / (1.0 + jnp.exp(-gate_pre))
    silu = gate_pre * sigmoid
    hidden = (silu * up_pre).astype(BF16)
    hidden_ref[...] = hidden
    slot_cotangent = mxu(place_low, cotangent)
    grad_out = (coefficient * slot_cotangent).astype(BF16)
    grad_out_ref[...] = grad_out
    grad_hidden = mxu(grad_out, down_weight)
    grad_up = (grad_hidden * silu).astype(BF16)
    grad_gate = (grad_hidden * up_pre * sigmoid * (1.0 + gate_pre * (1.0 - sigmoid))).astype(BF16)
    grad_up_ref[...] = grad_up
    grad_gate_ref[...] = grad_gate
    expert_out = mxu(hidden, down_weight, FROM_LAST)
    grad_slot = jnp.sum(slot_cotangent * expert_out, axis=1, keepdims=True)
    moe_ref[0] = mxu(back_low, (coefficient * expert_out).astype(BF16)).astype(BF16)

    grad_token = jnp.sum(place_wide * grad_slot, axis=0, keepdims=True)
    share = (grad_token * gate_own) * (own - gates)
    share_high = share.astype(BF16)
    share_low = (share - share_high.astype(F32)).astype(BF16)
    router_grad = mxu(share_high, tokens) + mxu(share_low, tokens)

    @pl.when(pl.program_id(0) == 0)
    def _():
        router_grad_ref[...] = router_grad

    @pl.when(pl.program_id(0) > 0)
    def _():
        router_grad_ref[...] += router_grad

    grad_in = mxu(grad_gate, gate_weight, FROM_LAST) + mxu(grad_up, up_weight, FROM_LAST)
    grad_ref[0] = (
        mxu(back_low, grad_in.astype(BF16)) + mxu(share.T.astype(BF16), router_ref[...])
    ).astype(BF16)


def expert_groups(slot, routed, own, router_t, tokens, cotangent, weights, capacity):
    count, group_rows, width = tokens.shape
    ff = weights[0].shape[1] * weights[0].shape[3]
    experts = router_t.shape[0]
    weight = pl.BlockSpec(weights[0].shape, lambda g: (0, 0, 0, 0))
    whole = lambda g: (0, 0)
    by_group = lambda g: (g, 0, 0)
    slots = lambda columns: pl.BlockSpec((capacity, columns), lambda g: (g, 0))
    slots_shape = lambda columns: jax.ShapeDtypeStruct((count * capacity, columns), BF16)
    return pl.pallas_call(
        functools.partial(expert_kernel, capacity=capacity),
        grid=(count,),
        in_specs=[
            pl.BlockSpec((1, 1, group_rows), by_group),
            pl.BlockSpec((1, group_rows, 1), by_group),
            pl.BlockSpec((1, experts, group_rows), by_group),
            pl.BlockSpec((experts, 1), whole),
            pl.BlockSpec((experts, width), whole),
            pl.BlockSpec((1, group_rows, width), by_group),
            pl.BlockSpec((1, group_rows, width), by_group),
            weight,
            weight,
            weight,
        ],
        out_specs=[
            pl.BlockSpec((1, group_rows, width), by_group),
            pl.BlockSpec((1, group_rows, width), by_group),
            slots(width),
            slots(width),
            slots(ff),
            slots(ff),
            slots(ff),
            pl.BlockSpec((experts, width), whole),
        ],
        out_shape=[
            jax.ShapeDtypeStruct(tokens.shape, BF16),
            jax.ShapeDtypeStruct(tokens.shape, BF16),
            slots_shape(width),
            slots_shape(width),
            slots_shape(ff),
            slots_shape(ff),
            slots_shape(ff),
            jax.ShapeDtypeStruct((experts, width), F32),
        ],
        compiler_params=pltpu.CompilerParams(vmem_limit_bytes=VMEM_LIMIT),
        cost_estimate=LIGHT,
        name="expert",
    )(
        slot[:, None, :],
        slot[:, :, None],
        routed,
        own,
        router_t,
        tokens,
        cotangent,
        *weights,
    )


def weight_grad_kernel(*refs, halves):
    rows, grad_out, hidden, grad_gate, grad_up, router = (
        refs[at : at + 2] for at in range(0, 12, 2)
    )
    moe_kept_ref, moe_got_ref, out_ref, moe_ref = refs[12:]
    moe_ref[...] = (moe_kept_ref[...].astype(F32) + moe_got_ref[...].astype(F32)).astype(BF16)
    columns = hidden[0].shape[1] // halves
    over = (((0,), (0,)), ((), ()))
    left_rows = [ref[...] for ref in rows]
    left_out = [ref[...] for ref in grad_out]
    router_columns = (router[0][...] + router[1][...]).T
    router_columns = jnp.concatenate(
        [
            router_columns,
            jnp.zeros((router_columns.shape[0], HEAD_SIZE - router_columns.shape[1]), F32),
        ],
        axis=1,
    ).astype(BF16)
    for half in range(halves):
        start = half * (3 * columns + HEAD_SIZE)
        part = slice(half * columns, (half + 1) * columns)
        for at, (left, right) in enumerate(
            ((left_rows, grad_gate), (left_rows, grad_up), (left_out, hidden))
        ):
            total = mxu(left[0], right[0][:, part], over) + mxu(left[1], right[1][:, part], over)
            out_ref[:, start + at * columns : start + (at + 1) * columns] = total.astype(BF16)
        out_ref[:, start + 3 * columns : start + 3 * columns + HEAD_SIZE] = router_columns


def weight_grads(near, far, moe_kept, moe_got, halves, block=256):
    rows_at, grad_out_at, hidden_at, grad_gate_at, grad_up_at, router_at = range(6)
    slots, width = near[rows_at].shape
    ff = near[hidden_at].shape[1]
    experts = near[router_at].shape[0]
    specs, operands = [], []
    for at in (rows_at, grad_out_at, hidden_at, grad_gate_at, grad_up_at, router_at):
        if at in (rows_at, grad_out_at):
            spec = pl.BlockSpec((slots, block), lambda i: (0, i))
        elif at == router_at:
            spec = pl.BlockSpec((experts, block), lambda i: (0, i))
        else:
            spec = pl.BlockSpec((slots, ff), lambda i: (0, 0))
        specs += [spec, spec]
        operands += [near[at], far[at]]
    columns = 3 * ff + halves * HEAD_SIZE
    moe_spec = pl.BlockSpec((moe_kept.shape[0], block), lambda i: (0, i))
    return pl.pallas_call(
        functools.partial(weight_grad_kernel, halves=halves),
        grid=(width // block,),
        in_specs=specs + [moe_spec, moe_spec],
        out_specs=[pl.BlockSpec((block, columns), lambda i: (i, 0)), moe_spec],
        out_shape=[
            jax.ShapeDtypeStruct((width, columns), BF16),
            jax.ShapeDtypeStruct(moe_kept.shape, BF16),
        ],
        compiler_params=pltpu.CompilerParams(vmem_limit_bytes=VMEM_LIMIT),
        cost_estimate=pl.CostEstimate(
            flops=15_000_000_000, bytes_accessed=50_000_000, transcendentals=0
        ),
        name="weight_grads",
    )(*operands, moe_kept, moe_got)


def on_device(
    block_input,
    norm_gains,
    router_weight,
    query_matrix,
    key_matrix,
    value_matrix,
    output_weight,
    gate_weight,
    up_weight,
    down_weight,
    segment_ids,
    routes,
    priority,
    cotangent,
):
    tensor_index = lax.axis_index("tensor")
    own_rows, width = block_input.shape
    group_rows = segment_ids.shape[0]
    halves = lax.axis_size("tensor")
    outer = lax.axis_size("outer")
    groups = lax.axis_size("x") * lax.axis_size("core")
    plane = groups * halves
    shard_rows = query_matrix.shape[0]
    dp_size = outer * groups
    seq_len = min(SEQ_MOST, group_rows * dp_size)
    own_start = lax.axis_index(ALL) * own_rows
    capacity = group_rows * TOPK // EXPERTS
    reach = ATTEND_SPAN // own_rows
    half_ff = gate_weight.shape[2]
    ff = half_ff * halves

    query_columns = query_matrix.shape[1]
    pair_columns = 2 * halves * HEAD_SIZE
    first = tensor_index == 0
    key_value_weight = jnp.concatenate([key_matrix, value_matrix], axis=1)
    other_weight = swap(key_value_weight, "tensor")
    early = jnp.concatenate(
        [
            jnp.where(first, key_value_weight, other_weight),
            jnp.where(first, other_weight, key_value_weight),
            query_matrix,
            output_weight,
        ],
        axis=1,
    )
    early, gate_own, up_own, down_own = lax.optimization_barrier(
        (early, gate_weight, up_weight, down_weight)
    )
    early = outer_gather(early)

    expert_shard = jnp.transpose(jnp.stack([gate_own, up_own, down_own]), (2, 0, 1, 3))
    expert_shard = lax.all_to_all(expert_shard, PLANE, 0, 0, tiled=True)
    pair_count = group_rows * TOPK
    rank = (
        jnp.zeros((pair_count,), jnp.int32)
        .at[priority]
        .set(jnp.arange(pair_count, dtype=jnp.int32))
        .reshape(group_rows, TOPK)
    )
    expert_ids = jnp.arange(EXPERTS, dtype=jnp.int32)
    named = routes[:, :, None] == expert_ids[None, None, :]
    ranked = jnp.sum(jnp.where(named, rank[:, :, None] + 1, 0), axis=1)
    ranked = jnp.where(ranked > 0, ranked, pair_count + 1)
    ranked_own = lax.dynamic_slice_in_dim(ranked, tensor_index * own_rows, own_rows, 0)
    digits = jnp.concatenate([ranked_own // 64, ranked_own % 64], axis=1).astype(BF16)
    digits = jnp.pad(digits, ((0, 0), (0, HEAD_SIZE - digits.shape[1])))
    cotangent_sent = jnp.concatenate([cotangent, digits], axis=1)
    expert_shard = expert_shard.reshape(groups, halves, 3, shard_rows, half_ff)
    expert_shard = [
        jnp.swapaxes(expert_shard[:, :, at], 0, 1).reshape(-1, half_ff) for at in range(3)
    ]
    early, expert_shard, segment_here = lax.optimization_barrier(
        (early, expert_shard, segment_ids)
    )
    segment_near = jnp.concatenate(
        [shift_groups(segment_here, 2), shift_groups(segment_here, 1), segment_here]
    )
    expert_full = [
        lax.all_gather(shard, "outer").reshape(outer, halves, groups * shard_rows, half_ff)
        for shard in expert_shard
    ]

    key_value_full = early[:, :, :pair_columns]
    key_value_full = in_order(key_value_full, swap(key_value_full, "x"), "x", 1)
    key_value_full = in_order(key_value_full, swap(key_value_full, "core"), "core", 2)
    key_value_full = key_value_full.reshape(width, pair_columns)
    query_parts = plane_parts(early[:, :, pair_columns : pair_columns + query_columns])

    input_wide = block_input.astype(F32)
    first_gain = norm_gains[:, 0]
    second_gain = norm_gains[:, 1]
    first_factor = norm_factor(input_wide)
    normed_in = (input_wide * first_factor * first_gain).astype(BF16)
    positions = own_start + jnp.arange(own_rows, dtype=jnp.int32)
    cosine, sine = rotary_tables(positions % seq_len)
    query_blocks = halves * query_columns // (2 * HEAD_SIZE)
    key_value_sent = project(
        normed_in, key_value_full, cosine, sine, 0, halves, (True, False)
    )
    one_back, two_back = shift_groups(key_value_sent, 1), shift_groups(key_value_sent, 2)
    query_parts, output_own, one_back, two_back, cotangent_sent = lax.optimization_barrier(
        (
            query_parts,
            early[:, :, pair_columns + query_columns :],
            one_back,
            two_back,
            cotangent_sent,
        )
    )
    pair_sent = jnp.where(
        first,
        jnp.stack([one_back, key_value_sent]),
        jnp.stack([two_back, one_back]),
    )
    pair_got = swap(pair_sent, "tensor")
    query_near = plane_stack(query_parts)
    query_far, pair_got = lax.optimization_barrier((swap(query_near, "core"), pair_got))
    pieces = [two_back, pair_got[0], one_back, pair_got[1], key_value_sent]
    query_full = whole_weight(query_near, query_far)
    output_parts = plane_parts(output_own)
    queries = project(normed_in, query_full, cosine, sine, 0, query_blocks, (True, True))
    queries, output_parts = lax.optimization_barrier((queries, output_parts))
    output_near = plane_stack(output_parts)
    output_far = swap(output_near, "core")
    cotangent_sent, output_near = lax.optimization_barrier((cotangent_sent, output_near))
    cotangent_parts = plane_parts(cotangent_sent)
    key_value = jnp.concatenate(pieces, axis=0)
    span = ATTEND_SPAN + own_rows
    segment_ext = lax.dynamic_slice_in_dim(segment_near, tensor_index * own_rows, span)
    view = (
        jnp.reshape(own_start, (1,)),
        segment_ext[:, None],
        segment_ext[None, ATTEND_SPAN:],
        queries,
        key_value,
    )
    heads_low, log_total = attention(*view, seq_len)
    output_full = whole_weight(output_near, output_far)
    hidden_state = input_wide + dot(heads_low, output_full, ((1,), (1,)))
    second_factor = norm_factor(hidden_state)
    normed_mid_own = (hidden_state * second_factor * second_gain).astype(BF16)

    normed_parts, cotangent_parts = lax.optimization_barrier(
        (plane_parts(normed_mid_own), cotangent_parts)
    )
    normed_near = plane_stack(normed_parts)
    normed_far = swap(normed_near, "core")
    cotangent_near = plane_stack(cotangent_parts)
    cotangent_far = swap(cotangent_near, "core")
    expert = lax.axis_index(PLANE)
    own_expert = (expert_ids == expert).astype(F32)[:, None]
    router_t = router_weight.T

    def experts_on(tokens, cotangents):
        digits = cotangents[..., width:].reshape(2, group_rows, HEAD_SIZE).astype(jnp.int32)
        ranked_all = digits[..., :EXPERTS] * 64 + digits[..., EXPERTS : 2 * EXPERTS]
        routed = jnp.swapaxes((ranked_all <= pair_count).astype(F32), 1, 2)
        rank_own = jnp.sum(jnp.where(expert_ids == expert, ranked_all, 0), axis=-1)
        earlier = (rank_own[:, None, :] < rank_own[:, :, None]).astype(jnp.int32)
        slot = jnp.where(rank_own <= pair_count, jnp.sum(earlier, axis=-1), capacity)
        return expert_groups(
            slot,
            routed,
            own_expert,
            router_t,
            tokens.reshape(2, group_rows, width),
            cotangents.reshape(2, group_rows, -1),
            expert_full,
            capacity,
        )

    on_near = experts_on(normed_near, cotangent_near)
    on_far = experts_on(normed_far, cotangent_far)
    blocks = (2 * halves, own_rows, width)
    (grad_near, moe_near), (grad_far, moe_far) = (
        [array.reshape(blocks) for array in side[:2]] for side in (on_near, on_far)
    )
    grad_blocks = fold_blocks(grad_near, swap(grad_far, "core"))
    grad_blocks, moe_far, on_near, on_far = lax.optimization_barrier(
        (grad_blocks, moe_far, on_near[2:], on_far[2:])
    )
    grad_mid_parts = fold_plane(grad_blocks)
    moe_got = swap(moe_far, "core")
    expert_part, moe_total = weight_grads(
        on_near, on_far, moe_near.reshape(-1, width), moe_got.reshape(-1, width), halves
    )
    expert_sum = lax.psum_scatter(expert_part, "outer", scatter_dimension=0, tiled=True)
    grad_mid_parts, moe_total = lax.optimization_barrier((grad_mid_parts, moe_total))
    moe_parts = fold_plane(list(moe_total.reshape(blocks)))
    grad_mid = wide_sum(grad_mid_parts)

    norm_input_part = norm_back(hidden_state, second_factor, second_gain, grad_mid)
    grad_state = cotangent.astype(F32) + norm_input_part
    grad_attn = grad_state.astype(BF16)
    grad_heads = dot(grad_attn, output_full, ((1,), (0,))).astype(BF16)
    output_total = fold_columns(grad_attn, heads_low, shard_rows)
    grad_query_pre, grad_far_kv, grad_own = attention_back(
        *view, log_total, grad_heads, cosine, sine, seq_len
    )
    grad_query_pre, output_total = lax.optimization_barrier((grad_query_pre, output_total))
    output_parts = fold_plane(distance_blocks(output_total))
    two_back, pair_old, one_back, pair_new = grad_far_kv.reshape(reach, own_rows, -1)
    pair_got, moe_parts = lax.optimization_barrier(
        (swap(jnp.stack([pair_old, pair_new]), "tensor"), moe_parts)
    )
    pair_old, pair_new = pair_got.astype(F32)
    one_back = one_back.astype(F32) + jnp.where(first, pair_old, pair_new)
    two_back = two_back.astype(F32) + jnp.where(first, 0.0, pair_old)
    grad_own = grad_own + jnp.where(first, pair_new, 0.0)
    grad_own = grad_own + shift_groups(one_back.astype(BF16), -1).astype(F32)
    grad_own = grad_own + shift_groups(two_back.astype(BF16), -2).astype(F32)
    grad_own, output_parts = lax.optimization_barrier((grad_own, output_parts))
    output_weight_grad = outer_scatter(wide_sum(output_parts).astype(BF16))
    grad_key_value = []
    for half in range(halves):
        start = half * 2 * HEAD_SIZE
        key_part = grad_own[:, start : start + HEAD_SIZE]
        turned = jnp.concatenate(
            [key_part[:, HEAD_SIZE // 2 :], key_part[:, : HEAD_SIZE // 2]], axis=1
        )
        grad_key_value.append(key_part * cosine - turned * sine)
        grad_key_value.append(grad_own[:, start + HEAD_SIZE : start + 2 * HEAD_SIZE])
    grad_key_value_pre = jnp.concatenate(grad_key_value, axis=1).astype(BF16)
    grad_qkv_pre = jnp.concatenate(
        [
            grad_query_pre.reshape(own_rows, halves, -1),
            grad_key_value_pre.reshape(own_rows, halves, -1),
        ],
        axis=2,
    ).reshape(own_rows, -1)
    qkv_total = fold_columns(normed_in, grad_qkv_pre, shard_rows)
    qkv_parts = fold_plane(distance_blocks(qkv_total))
    grad_in = dot(grad_query_pre, query_full, ((1,), (1,))) + dot(
        grad_key_value_pre, key_value_full, ((1,), (1,))
    )
    input_grad = grad_state + norm_back(input_wide, first_factor, first_gain, grad_in)
    qkv_grad, expert_sum = outer_scatter(wide_sum(qkv_parts).astype(BF16), expert_sum)
    block_output = hidden_state + wide_sum(moe_parts)
    expert_sum = expert_sum.reshape(groups, shard_rows, halves, -1)
    expert_sum = jnp.swapaxes(expert_sum, 1, 2).reshape(plane, shard_rows, -1)
    expert_sum = lax.all_to_all(expert_sum, PLANE, 0, 0, tiled=True)
    gate_grad, up_grad, down_grad = (
        jnp.swapaxes(expert_sum[:, :, at * half_ff : (at + 1) * half_ff], 0, 1).astype(F32)
        for at in range(3)
    )
    router_grad = jnp.sum(expert_sum[:, :, 3 * half_ff : 3 * half_ff + EXPERTS].astype(F32), axis=0)
    router_grad = lax.dynamic_slice_in_dim(
        router_grad, tensor_index * (shard_rows // 2), shard_rows // 2, 0
    )
    query_grad = qkv_grad[:, :query_columns]
    key_grad = qkv_grad[:, query_columns : query_columns + HEAD_SIZE]
    value_grad = qkv_grad[:, query_columns + HEAD_SIZE :]

    half_rows = shard_rows // 2
    own_gains = lax.dynamic_slice_in_dim(
        norm_gains, lax.axis_index(DP) * shard_rows, shard_rows, 0
    )
    qkv_own = jnp.concatenate([query_matrix, key_value_weight], axis=1)
    first_sum = jnp.sum(qkv_grad * qkv_own.astype(F32), axis=-1)
    second_sum = jnp.sum(
        gate_grad * gate_weight.astype(F32) + up_grad * up_weight.astype(F32), axis=(1, 2)
    )
    gain_sums = jnp.stack([first_sum, second_sum], axis=1) / own_gains
    kept = lax.dynamic_slice_in_dim(gain_sums, tensor_index * half_rows, half_rows, 0)
    sent = lax.dynamic_slice_in_dim(gain_sums, (1 - tensor_index) * half_rows, half_rows, 0)
    own_router = lax.dynamic_slice_in_dim(
        router_weight, lax.axis_index(ALL) * half_rows, half_rows, 0
    )
    router_sum = jnp.sum(router_grad * own_router.astype(F32), axis=-1)
    half_gains = lax.dynamic_slice_in_dim(own_gains, tensor_index * half_rows, half_rows, 0)
    router_sum = router_sum / half_gains[:, 1]
    gains_grad = (
        kept
        + swap(sent, "tensor")
        + jnp.stack([jnp.zeros_like(router_sum), router_sum], axis=1)
    )
    return (
        block_output,
        input_grad,
        gains_grad,
        router_grad,
        query_grad,
        key_grad,
        value_grad,
        output_weight_grad,
        gate_grad,
        up_grad,
        down_grad,
    )


def solution(mesh):
    dp_size, tensor_size = mesh.shape["dp"], mesh.shape["tensor"]
    split = Mesh(mesh.devices.reshape(dp_size // 4, 2, 2, tensor_size), ALL)
    return jax.shard_map(
        on_device,
        mesh=split,
        in_specs=(
            P(ALL, None),
            P(),
            P(),
            P(DP, "tensor"),
            P(DP, "tensor"),
            P(DP, "tensor"),
            P(DP, "tensor"),
            P(DP, None, "tensor"),
            P(DP, None, "tensor"),
            P(DP, None, "tensor"),
            P(DP),
            P(DP, None),
            P(DP),
            P(ALL, None),
        ),
        out_specs=(
            P(ALL, None),
            P(ALL, None),
            P(ALL, None),
            P(ALL, None),
            P(DP, "tensor"),
            P(DP, "tensor"),
            P(DP, "tensor"),
            P(DP, "tensor"),
            P(DP, None, "tensor"),
            P(DP, None, "tensor"),
            P(DP, None, "tensor"),
        ),
        check_vma=False,
    )
```

```python
import functools
import math

import jax
import jax.numpy as jnp
from jax import lax
from jax.experimental import pallas as pl
from jax.experimental.pallas import tpu as pltpu
from jax.sharding import Mesh
from jax.sharding import PartitionSpec as P

HEAD_SIZE = 128
TOPK = 4
EXPERTS = 8
ATTEND_SPAN = 1024
SEQ_MOST = 16384
EPSILON = 1e-06
ROPE_BASE = 10000.0
BF16 = jnp.bfloat16
F32 = jnp.float32

DP = ("outer", "x", "core")
PLANE = ("x", "core", "tensor")
ALL = ("outer", "x", "core", "tensor")


def shift_groups(x, by):
    length = lax.axis_size(DP)
    return lax.ppermute(x, DP, [(i, i + by) for i in range(length) if 0 <= i + by < length])


def swap(x, axis):
    length = lax.axis_size(axis)
    return lax.ppermute(x, axis, [(i, length - 1 - i) for i in range(length)])


def plane_parts(own):
    return [own, swap(own, "tensor"), swap(own, "x"), swap(own, ("x", "tensor"))]


def plane_stack(parts):
    return jnp.stack(parts).reshape((2, 2) + parts[0].shape)


def whole_weight(near, far):
    x, tensor = lax.axis_index("x"), lax.axis_index("tensor")
    first = lax.axis_index("core") == 0
    by_core = [jnp.where(first, near, far), jnp.where(first, far, near)]

    def piece(x_at, core_at, tensor_at):
        picked = lax.dynamic_index_in_dim(by_core[core_at], x ^ x_at, 0, keepdims=False)
        return lax.dynamic_index_in_dim(picked, tensor ^ tensor_at, 0, keepdims=False)

    places = [(x_at, core_at) for x_at in range(2) for core_at in range(2)]
    halves = [jnp.stack([piece(*place, at) for place in places], 1) for at in range(2)]
    return jnp.concatenate(halves, axis=-1).reshape(-1, 2 * near.shape[-1])


def fold_core(kept, sent):
    return (kept.astype(F32) + swap(sent, "core").astype(F32)).astype(BF16)


def fold_blocks(kept, got):
    return [
        (kept[at].astype(F32) + got[at].astype(F32)).astype(BF16) for at in range(kept.shape[0])
    ]


def in_order(own, other, axis_name, axis):
    first = lax.axis_index(axis_name) == 0
    return jnp.stack([jnp.where(first, own, other), jnp.where(first, other, own)], axis)


def fold_plane(blocks):
    return [
        blocks[0],
        swap(blocks[1], "tensor"),
        swap(blocks[2], "x"),
        swap(blocks[3], ("x", "tensor")),
    ]


def wide_sum(parts):
    return sum(part.astype(F32) for part in parts)


def outer_shift(x, by):
    length = lax.axis_size("outer")
    return lax.ppermute(x, "outer", [(i, (i + by) % length) for i in range(length)])


def outer_gather(shard):
    length, here = lax.axis_size("outer"), lax.axis_index("outer")
    if length > 4:
        return lax.all_gather(shard, "outer")
    full = jnp.zeros((length,) + shard.shape, shard.dtype)
    for by in range(length):
        piece = outer_shift(shard, by) if by else shard
        full = lax.dynamic_update_slice_in_dim(full, piece[None], (here - by) % length, 0)
    return full


def outer_scatter(parts, later=None):
    length, here = lax.axis_size("outer"), lax.axis_index("outer")
    if length > 4:
        total = lax.psum_scatter(parts, "outer", scatter_dimension=0, tiled=False).astype(F32)
        return total if later is None else (total, later)
    total = lax.dynamic_index_in_dim(parts, here, 0, keepdims=False)
    if later is not None:
        total, later = lax.optimization_barrier((total, later))
    total = total.astype(F32)
    for by in range(1, length):
        piece = lax.dynamic_index_in_dim(parts, (here + by) % length, 0, keepdims=False)
        total = total + outer_shift(piece, by).astype(F32)
    return total if later is None else (total, later)


def core_columns(rows, core_at, shard_rows):
    count = rows.shape[0]
    split = rows.reshape(count, -1, 2, shard_rows)
    return lax.dynamic_index_in_dim(split, core_at, 2, keepdims=False).reshape(count, -1)


def fold_columns(left, right, shard_rows):
    core = lax.axis_index("core")
    sent = dot(core_columns(left, 1 - core, shard_rows), right, ((0,), (0,))).astype(BF16)
    kept = dot(core_columns(left, core, shard_rows), right, ((0,), (0,))).astype(BF16)
    return fold_core(kept, sent).reshape(-1, 2, shard_rows, right.shape[1])


def distance_blocks(total):
    x, tensor = lax.axis_index("x"), lax.axis_index("tensor")
    columns = total.shape[3] // 2
    blocks = []
    for x_by in range(2):
        for tensor_by in range(2):
            block = lax.dynamic_index_in_dim(total, x ^ x_by, 1, keepdims=False)
            start = (tensor ^ tensor_by) * columns
            blocks.append(lax.dynamic_slice_in_dim(block, start, columns, 2))
    return blocks


def rotary_tables(position):
    halfway = HEAD_SIZE // 2
    inverse = jnp.exp(
        jnp.arange(halfway, dtype=F32) * (-2.0 * math.log(ROPE_BASE) / HEAD_SIZE)
    )
    angles = position.astype(F32)[:, None] * inverse[None, :]
    cosine, sine = jnp.cos(angles), jnp.sin(angles)
    return (
        jnp.concatenate([cosine, cosine], axis=1),
        jnp.concatenate([-sine, sine], axis=1),
    )


def norm_factor(value_rows):
    return lax.rsqrt(jnp.mean(value_rows * value_rows, axis=-1, keepdims=True) + EPSILON)


def norm_back(value_rows, factor, gain, upstream):
    weighted = upstream * gain
    return factor * weighted - value_rows * (factor * factor * factor) * jnp.mean(
        weighted * value_rows, axis=-1, keepdims=True
    )


def dot(a, b, dims):
    return lax.dot_general(a, b, (dims, ((), ())), preferred_element_type=F32)


VMEM_LIMIT = 60 * 1024 * 1024
LIGHT = pl.CostEstimate(flops=1000, bytes_accessed=1000, transcendentals=0)
FROM_LAST = (((1,), (1,)), ((), ()))
PLAIN = (((1,), (0,)), ((), ()))


def mxu(a, b, dims=PLAIN):
    return lax.dot_general(a, b, dims, preferred_element_type=F32)


def turn(rows, cosine, sine):
    return rows * cosine + pltpu.roll(rows, HEAD_SIZE // 2, 1) * sine


def project_kernel(rows_ref, weight_ref, cosine_ref, sine_ref, out_ref, *, turned):
    product = mxu(rows_ref[...], weight_ref[...])
    for at, turns in enumerate(turned):
        part = product[:, at * HEAD_SIZE : (at + 1) * HEAD_SIZE]
        if turns:
            part = turn(part, cosine_ref[...], sine_ref[...])
        out_ref[:, at * HEAD_SIZE : (at + 1) * HEAD_SIZE] = part.astype(BF16)


def project(rows, weight, cosine, sine, first, count, turned):
    high, width = rows.shape
    columns = len(turned) * HEAD_SIZE
    return pl.pallas_call(
        functools.partial(project_kernel, turned=turned),
        grid=(count,),
        in_specs=[
            pl.BlockSpec((high, width), lambda j: (0, 0)),
            pl.BlockSpec((width, columns), lambda j: (0, first + j)),
            pl.BlockSpec((high, HEAD_SIZE), lambda j: (0, 0)),
            pl.BlockSpec((high, HEAD_SIZE), lambda j: (0, 0)),
        ],
        out_specs=pl.BlockSpec((high, columns), lambda j: (0, j)),
        out_shape=jax.ShapeDtypeStruct((high, count * columns), BF16),
        compiler_params=pltpu.CompilerParams(vmem_limit_bytes=VMEM_LIMIT),
        cost_estimate=LIGHT,
        name="project",
    )(rows, weight, cosine, sine)


def mask_bias(place_ref, segment_key_ref, segment_query_ref, bias_ref, seq_len):
    span, rows = bias_ref.shape
    start = place_ref[0]
    key_at = lax.broadcasted_iota(jnp.int32, (span, rows), 0)
    query_at = lax.broadcasted_iota(jnp.int32, (span, rows), 1) + ATTEND_SPAN
    distance = query_at - key_at
    position = start + query_at - ATTEND_SPAN
    sequence_at = query_at - lax.rem(position, seq_len)
    allowed = (distance >= 0) & (distance < ATTEND_SPAN) & (key_at >= sequence_at)
    allowed = allowed & (segment_key_ref[...] == segment_query_ref[...])
    bias_ref[...] = jnp.where(allowed, 0.0, -1e30)


def attention_kernel(
    place_ref,
    segment_key_ref,
    segment_query_ref,
    q_ref,
    kv_ref,
    heads_ref,
    lse_ref,
    bias_ref,
    *,
    seq_len,
    scale,
):
    @pl.when(pl.program_id(0) == 0)
    def _():
        mask_bias(place_ref, segment_key_ref, segment_query_ref, bias_ref, seq_len)

    rows = q_ref.shape[0]
    span = kv_ref.shape[0]
    count = q_ref.shape[1] // HEAD_SIZE
    value_t = kv_ref[:, HEAD_SIZE:].T
    chunks = span // rows
    for head in range(count):
        columns = slice(head * HEAD_SIZE, (head + 1) * HEAD_SIZE)
        query = q_ref[:, columns]
        scores = []
        for c in range(chunks):
            part = slice(c * rows, (c + 1) * rows)
            raw = mxu(kv_ref[part, :HEAD_SIZE], query, FROM_LAST)
            scores.append(raw * scale + bias_ref[part, :])
        top = functools.reduce(jnp.maximum, scores)
        top = jnp.max(top, axis=0, keepdims=True)
        total = jnp.zeros_like(top)
        out_t = jnp.zeros((HEAD_SIZE, rows), F32)
        for c in range(chunks):
            weight = jnp.exp(scores[c] - top)
            total = total + jnp.sum(weight, axis=0, keepdims=True)
            out_t = out_t + mxu(value_t[:, c * rows : (c + 1) * rows], weight.astype(BF16))
        heads_ref[:, columns] = (out_t / total).T.astype(BF16)
        lse_ref[0, head : head + 1, :] = top + jnp.log(total)


def attention(place, segment_key, segment_query, queries, key_value, seq_len):
    rows, all_columns = queries.shape
    span = key_value.shape[0]
    pairs = key_value.shape[1] // (2 * HEAD_SIZE)
    columns = all_columns // pairs
    return pl.pallas_call(
        functools.partial(attention_kernel, seq_len=seq_len, scale=1.0 / math.sqrt(HEAD_SIZE)),
        grid=(pairs,),
        in_specs=[
            pl.BlockSpec(memory_space=pltpu.SMEM),
            pl.BlockSpec((span, 1), lambda j: (0, 0)),
            pl.BlockSpec((1, rows), lambda j: (0, 0)),
            pl.BlockSpec((rows, columns), lambda j: (0, j)),
            pl.BlockSpec((span, 2 * HEAD_SIZE), lambda j: (0, j)),
        ],
        out_specs=[
            pl.BlockSpec((rows, columns), lambda j: (0, j)),
            pl.BlockSpec((1, columns // HEAD_SIZE, rows), lambda j: (j, 0, 0)),
        ],
        out_shape=[
            jax.ShapeDtypeStruct((rows, all_columns), BF16),
            jax.ShapeDtypeStruct((pairs, columns // HEAD_SIZE, rows), F32),
        ],
        scratch_shapes=[pltpu.VMEM((span, rows), F32)],
        compiler_params=pltpu.CompilerParams(vmem_limit_bytes=VMEM_LIMIT),
        cost_estimate=LIGHT,
        name="attention",
    )(place, segment_key, segment_query, queries, key_value)


def attention_back_kernel(
    place_ref,
    segment_key_ref,
    segment_query_ref,
    q_ref,
    kv_ref,
    lse_ref,
    dout_ref,
    cosine_ref,
    sine_ref,
    dq_ref,
    dkv_far_ref,
    dkv_own_ref,
    bias_ref,
    dkv_ref,
    *,
    seq_len,
    scale,
):
    @pl.when(pl.program_id(0) == 0)
    def _():
        mask_bias(place_ref, segment_key_ref, segment_query_ref, bias_ref, seq_len)

    rows = q_ref.shape[0]
    span = kv_ref.shape[0]
    count = q_ref.shape[1] // HEAD_SIZE
    key_t = kv_ref[:, :HEAD_SIZE].T
    chunks = span // rows
    dkv_ref[...] = jnp.zeros_like(dkv_ref)
    for head in range(count):
        columns = slice(head * HEAD_SIZE, (head + 1) * HEAD_SIZE)
        query = q_ref[:, columns]
        dout = dout_ref[:, columns]
        lse = lse_ref[0, head : head + 1, :]
        probs, dprobs = [], []
        row_dot = jnp.zeros_like(lse)
        for c in range(chunks):
            part = slice(c * rows, (c + 1) * rows)
            raw = mxu(kv_ref[part, :HEAD_SIZE], query, FROM_LAST)
            prob = jnp.exp(raw * scale + bias_ref[part, :] - lse)
            dprob = mxu(kv_ref[part, HEAD_SIZE:], dout, FROM_LAST)
            row_dot = row_dot + jnp.sum(prob * dprob, axis=0, keepdims=True)
            probs.append(prob)
            dprobs.append(dprob)
        dq_t = jnp.zeros((HEAD_SIZE, rows), F32)
        for c in range(chunks):
            part = slice(c * rows, (c + 1) * rows)
            dscore = (probs[c] * (dprobs[c] - row_dot)).astype(BF16)
            dkv_ref[part, :HEAD_SIZE] += mxu(dscore, query)
            dkv_ref[part, HEAD_SIZE:] += mxu(probs[c].astype(BF16), dout)
            dq_t = dq_t + mxu(key_t[:, part], dscore)
        dq_ref[:, columns] = turn(dq_t.T * scale, cosine_ref[...], -sine_ref[...]).astype(BF16)
    dkv_ref[:, :HEAD_SIZE] = dkv_ref[:, :HEAD_SIZE] * scale
    dkv_far_ref[...] = dkv_ref[: span - rows, :].astype(BF16)
    dkv_own_ref[...] = dkv_ref[span - rows :, :]


def attention_back(
    place, segment_key, segment_query, queries, key_value, lse, dout, cosine, sine, seq_len
):
    rows, all_columns = queries.shape
    span = key_value.shape[0]
    pairs = key_value.shape[1] // (2 * HEAD_SIZE)
    columns = all_columns // pairs
    return pl.pallas_call(
        functools.partial(
            attention_back_kernel, seq_len=seq_len, scale=1.0 / math.sqrt(HEAD_SIZE)
        ),
        grid=(pairs,),
        in_specs=[
            pl.BlockSpec(memory_space=pltpu.SMEM),
            pl.BlockSpec((span, 1), lambda j: (0, 0)),
            pl.BlockSpec((1, rows), lambda j: (0, 0)),
            pl.BlockSpec((rows, columns), lambda j: (0, j)),
            pl.BlockSpec((span, 2 * HEAD_SIZE), lambda j: (0, j)),
            pl.BlockSpec((1, columns // HEAD_SIZE, rows), lambda j: (j, 0, 0)),
            pl.BlockSpec((rows, columns), lambda j: (0, j)),
            pl.BlockSpec((rows, HEAD_SIZE), lambda j: (0, 0)),
            pl.BlockSpec((rows, HEAD_SIZE), lambda j: (0, 0)),
        ],
        out_specs=[
            pl.BlockSpec((rows, columns), lambda j: (0, j)),
            pl.BlockSpec((span - rows, 2 * HEAD_SIZE), lambda j: (0, j)),
            pl.BlockSpec((rows, 2 * HEAD_SIZE), lambda j: (0, j)),
        ],
        out_shape=[
            jax.ShapeDtypeStruct((rows, all_columns), BF16),
            jax.ShapeDtypeStruct((span - rows, key_value.shape[1]), BF16),
            jax.ShapeDtypeStruct((rows, key_value.shape[1]), F32),
        ],
        scratch_shapes=[
            pltpu.VMEM((span, rows), F32),
            pltpu.VMEM((span, 2 * HEAD_SIZE), F32),
        ],
        compiler_params=pltpu.CompilerParams(vmem_limit_bytes=VMEM_LIMIT),
        cost_estimate=pl.CostEstimate(
            flops=70_000_000_000, bytes_accessed=10_000_000, transcendentals=0
        ),
        name="attention_back",
    )(place, segment_key, segment_query, queries, key_value, lse, dout, cosine, sine)


def expert_kernel(
    slot_row_ref,
    slot_column_ref,
    routed_ref,
    own_ref,
    router_ref,
    tokens_ref,
    cotangent_ref,
    gate_ref,
    up_ref,
    down_ref,
    grad_ref,
    moe_ref,
    rows_in_ref,
    grad_out_ref,
    hidden_ref,
    grad_gate_ref,
    grad_up_ref,
    router_grad_ref,
    *,
    capacity,
):
    group_rows = tokens_ref.shape[1]
    tokens = tokens_ref[0]
    gate_weight, up_weight, down_weight = (
        jnp.concatenate(
            [ref[:, half].reshape(-1, ref.shape[3]) for half in range(ref.shape[1])], axis=1
        )
        for ref in (gate_ref, up_ref, down_ref)
    )
    cotangent = cotangent_ref[0]
    routed = routed_ref[0] > 0.0
    logits = jnp.where(routed, mxu(router_ref[...], tokens, FROM_LAST), -1e30)
    weights = jnp.exp(logits - jnp.max(logits, axis=0, keepdims=True))
    weights = jnp.where(routed, weights, 0.0)
    gates = weights / jnp.sum(weights, axis=0, keepdims=True)
    own = own_ref[...]
    gate_own = jnp.sum(gates * own, axis=0, keepdims=True)
    place = slot_row_ref[0] == lax.broadcasted_iota(jnp.int32, (capacity, group_rows), 0)
    place_wide = jnp.where(place, 1.0, 0.0)
    place_low = place_wide.astype(BF16)
    back = slot_column_ref[0] == lax.broadcasted_iota(jnp.int32, (group_rows, capacity), 1)
    back_low = jnp.where(back, 1.0, 0.0).astype(BF16)
    coefficient = jnp.sum(place_wide * gate_own, axis=1, keepdims=True)

    rows_in = mxu(place_low, tokens).astype(BF16)
    rows_in_ref[...] = rows_in
    gate_pre = mxu(rows_in, gate_weight)
    up_pre = mxu(rows_in, up_weight)
    sigmoid = 1.0 / (1.0 + jnp.exp(-gate_pre))
    silu = gate_pre * sigmoid
    hidden = (silu * up_pre).astype(BF16)
    hidden_ref[...] = hidden
    slot_cotangent = mxu(place_low, cotangent)
    grad_out = (coefficient * slot_cotangent).astype(BF16)
    grad_out_ref[...] = grad_out
    grad_hidden = mxu(grad_out, down_weight)
    grad_up = (grad_hidden * silu).astype(BF16)
    grad_gate = (grad_hidden * up_pre * sigmoid * (1.0 + gate_pre * (1.0 - sigmoid))).astype(BF16)
    grad_up_ref[...] = grad_up
    grad_gate_ref[...] = grad_gate
    expert_out = mxu(hidden, down_weight, FROM_LAST)
    grad_slot = jnp.sum(slot_cotangent * expert_out, axis=1, keepdims=True)
    moe_ref[0] = mxu(back_low, (coefficient * expert_out).astype(BF16)).astype(BF16)

    grad_token = jnp.sum(place_wide * grad_slot, axis=0, keepdims=True)
    share = (grad_token * gate_own) * (own - gates)
    share_high = share.astype(BF16)
    share_low = (share - share_high.astype(F32)).astype(BF16)
    router_grad = mxu(share_high, tokens) + mxu(share_low, tokens)

    @pl.when(pl.program_id(0) == 0)
    def _():
        router_grad_ref[...] = router_grad

    @pl.when(pl.program_id(0) > 0)
    def _():
        router_grad_ref[...] += router_grad

    grad_in = mxu(grad_gate, gate_weight, FROM_LAST) + mxu(grad_up, up_weight, FROM_LAST)
    grad_ref[0] = (
        mxu(back_low, grad_in.astype(BF16)) + mxu(share.T.astype(BF16), router_ref[...])
    ).astype(BF16)


def expert_groups(slot, routed, own, router_t, tokens, cotangent, weights, capacity):
    count, group_rows, width = tokens.shape
    ff = weights[0].shape[1] * weights[0].shape[3]
    experts = router_t.shape[0]
    weight = pl.BlockSpec(weights[0].shape, lambda g: (0, 0, 0, 0))
    whole = lambda g: (0, 0)
    by_group = lambda g: (g, 0, 0)
    slots = lambda columns: pl.BlockSpec((capacity, columns), lambda g: (g, 0))
    slots_shape = lambda columns: jax.ShapeDtypeStruct((count * capacity, columns), BF16)
    return pl.pallas_call(
        functools.partial(expert_kernel, capacity=capacity),
        grid=(count,),
        in_specs=[
            pl.BlockSpec((1, 1, group_rows), by_group),
            pl.BlockSpec((1, group_rows, 1), by_group),
            pl.BlockSpec((1, experts, group_rows), by_group),
            pl.BlockSpec((experts, 1), whole),
            pl.BlockSpec((experts, width), whole),
            pl.BlockSpec((1, group_rows, width), by_group),
            pl.BlockSpec((1, group_rows, width), by_group),
            weight,
            weight,
            weight,
        ],
        out_specs=[
            pl.BlockSpec((1, group_rows, width), by_group),
            pl.BlockSpec((1, group_rows, width), by_group),
            slots(width),
            slots(width),
            slots(ff),
            slots(ff),
            slots(ff),
            pl.BlockSpec((experts, width), whole),
        ],
        out_shape=[
            jax.ShapeDtypeStruct(tokens.shape, BF16),
            jax.ShapeDtypeStruct(tokens.shape, BF16),
            slots_shape(width),
            slots_shape(width),
            slots_shape(ff),
            slots_shape(ff),
            slots_shape(ff),
            jax.ShapeDtypeStruct((experts, width), F32),
        ],
        compiler_params=pltpu.CompilerParams(vmem_limit_bytes=VMEM_LIMIT),
        cost_estimate=LIGHT,
        name="expert",
    )(
        slot[:, None, :],
        slot[:, :, None],
        routed,
        own,
        router_t,
        tokens,
        cotangent,
        *weights,
    )


def weight_grad_kernel(*refs, halves):
    rows, grad_out, hidden, grad_gate, grad_up, router = (
        refs[at : at + 2] for at in range(0, 12, 2)
    )
    moe_kept_ref, moe_got_ref, out_ref, moe_ref = refs[12:]
    moe_ref[...] = (moe_kept_ref[...].astype(F32) + moe_got_ref[...].astype(F32)).astype(BF16)
    columns = hidden[0].shape[1] // halves
    over = (((0,), (0,)), ((), ()))
    left_rows = [ref[...] for ref in rows]
    left_out = [ref[...] for ref in grad_out]
    router_columns = (router[0][...] + router[1][...]).T
    router_columns = jnp.concatenate(
        [
            router_columns,
            jnp.zeros((router_columns.shape[0], HEAD_SIZE - router_columns.shape[1]), F32),
        ],
        axis=1,
    ).astype(BF16)
    for half in range(halves):
        start = half * (3 * columns + HEAD_SIZE)
        part = slice(half * columns, (half + 1) * columns)
        for at, (left, right) in enumerate(
            ((left_rows, grad_gate), (left_rows, grad_up), (left_out, hidden))
        ):
            total = mxu(left[0], right[0][:, part], over) + mxu(left[1], right[1][:, part], over)
            out_ref[:, start + at * columns : start + (at + 1) * columns] = total.astype(BF16)
        out_ref[:, start + 3 * columns : start + 3 * columns + HEAD_SIZE] = router_columns


def weight_grads(near, far, moe_kept, moe_got, halves, block=256):
    rows_at, grad_out_at, hidden_at, grad_gate_at, grad_up_at, router_at = range(6)
    slots, width = near[rows_at].shape
    ff = near[hidden_at].shape[1]
    experts = near[router_at].shape[0]
    specs, operands = [], []
    for at in (rows_at, grad_out_at, hidden_at, grad_gate_at, grad_up_at, router_at):
        if at in (rows_at, grad_out_at):
            spec = pl.BlockSpec((slots, block), lambda i: (0, i))
        elif at == router_at:
            spec = pl.BlockSpec((experts, block), lambda i: (0, i))
        else:
            spec = pl.BlockSpec((slots, ff), lambda i: (0, 0))
        specs += [spec, spec]
        operands += [near[at], far[at]]
    columns = 3 * ff + halves * HEAD_SIZE
    moe_spec = pl.BlockSpec((moe_kept.shape[0], block), lambda i: (0, i))
    return pl.pallas_call(
        functools.partial(weight_grad_kernel, halves=halves),
        grid=(width // block,),
        in_specs=specs + [moe_spec, moe_spec],
        out_specs=[pl.BlockSpec((block, columns), lambda i: (i, 0)), moe_spec],
        out_shape=[
            jax.ShapeDtypeStruct((width, columns), BF16),
            jax.ShapeDtypeStruct(moe_kept.shape, BF16),
        ],
        compiler_params=pltpu.CompilerParams(vmem_limit_bytes=VMEM_LIMIT),
        cost_estimate=pl.CostEstimate(
            flops=15_000_000_000, bytes_accessed=50_000_000, transcendentals=0
        ),
        name="weight_grads",
    )(*operands, moe_kept, moe_got)


def on_device(
    block_input,
    norm_gains,
    router_weight,
    query_matrix,
    key_matrix,
    value_matrix,
    output_weight,
    gate_weight,
    up_weight,
    down_weight,
    segment_ids,
    routes,
    priority,
    cotangent,
):
    tensor_index = lax.axis_index("tensor")
    own_rows, width = block_input.shape
    group_rows = segment_ids.shape[0]
    halves = lax.axis_size("tensor")
    outer = lax.axis_size("outer")
    groups = lax.axis_size("x") * lax.axis_size("core")
    plane = groups * halves
    shard_rows = query_matrix.shape[0]
    dp_size = outer * groups
    seq_len = min(SEQ_MOST, group_rows * dp_size)
    own_start = lax.axis_index(ALL) * own_rows
    capacity = group_rows * TOPK // EXPERTS
    reach = ATTEND_SPAN // own_rows
    half_ff = gate_weight.shape[2]
    ff = half_ff * halves

    query_columns = query_matrix.shape[1]
    pair_columns = 2 * halves * HEAD_SIZE
    first = tensor_index == 0
    key_value_weight = jnp.concatenate([key_matrix, value_matrix], axis=1)
    other_weight = swap(key_value_weight, "tensor")
    early = jnp.concatenate(
        [
            jnp.where(first, key_value_weight, other_weight),
            jnp.where(first, other_weight, key_value_weight),
            query_matrix,
            output_weight,
        ],
        axis=1,
    )
    early, gate_own, up_own, down_own, cotangent_own = lax.optimization_barrier(
        (early, gate_weight, up_weight, down_weight, cotangent)
    )
    early = outer_gather(early)

    expert_shard = jnp.transpose(jnp.stack([gate_own, up_own, down_own]), (2, 0, 1, 3))
    expert_shard = lax.all_to_all(expert_shard, PLANE, 0, 0, tiled=True)
    pair_count = group_rows * TOPK
    rank = (
        jnp.zeros((pair_count,), jnp.int32)
        .at[priority]
        .set(jnp.arange(pair_count, dtype=jnp.int32))
        .reshape(group_rows, TOPK)
    )
    expert_ids = jnp.arange(EXPERTS, dtype=jnp.int32)
    named = routes[:, :, None] == expert_ids[None, None, :]
    ranked = jnp.sum(jnp.where(named, rank[:, :, None] + 1, 0), axis=1)
    ranked = jnp.where(ranked > 0, ranked, pair_count + 1)
    ranked_own = lax.dynamic_slice_in_dim(ranked, tensor_index * own_rows, own_rows, 0)
    digits = jnp.concatenate([ranked_own // 64, ranked_own % 64], axis=1).astype(BF16)
    digits = jnp.pad(digits, ((0, 0), (0, HEAD_SIZE - digits.shape[1])))
    cotangent_sent = jnp.concatenate([cotangent_own, digits], axis=1)
    expert_shard = expert_shard.reshape(groups, halves, 3, shard_rows, half_ff)
    expert_shard = [
        jnp.swapaxes(expert_shard[:, :, at], 0, 1).reshape(-1, half_ff) for at in range(3)
    ]
    early, expert_shard, segment_here = lax.optimization_barrier(
        (early, expert_shard, segment_ids)
    )
    segment_near = jnp.concatenate(
        [shift_groups(segment_here, 2), shift_groups(segment_here, 1), segment_here]
    )
    expert_full = [
        lax.all_gather(shard, "outer").reshape(outer, halves, groups * shard_rows, half_ff)
        for shard in expert_shard
    ]

    key_value_full = early[:, :, :pair_columns]
    key_value_full = in_order(key_value_full, swap(key_value_full, "x"), "x", 1)
    key_value_full = in_order(key_value_full, swap(key_value_full, "core"), "core", 2)
    key_value_full = key_value_full.reshape(width, pair_columns)
    query_parts = plane_parts(early[:, :, pair_columns : pair_columns + query_columns])

    input_wide = block_input.astype(F32)
    first_gain = norm_gains[:, 0]
    second_gain = norm_gains[:, 1]
    first_factor = norm_factor(input_wide)
    normed_in = (input_wide * first_factor * first_gain).astype(BF16)
    positions = own_start + jnp.arange(own_rows, dtype=jnp.int32)
    cosine, sine = rotary_tables(positions % seq_len)
    query_blocks = halves * query_columns // (2 * HEAD_SIZE)
    key_value_sent = project(
        normed_in, key_value_full, cosine, sine, 0, halves, (True, False)
    )
    one_back, two_back = shift_groups(key_value_sent, 1), shift_groups(key_value_sent, 2)
    (query_parts, output_own, one_back, two_back, cotangent_parts, segment_near) = (
        lax.optimization_barrier(
            (
                query_parts,
                early[:, :, pair_columns + query_columns :],
                one_back,
                two_back,
                plane_parts(cotangent_sent),
                segment_near,
            )
        )
    )
    pair_sent = jnp.where(
        first,
        jnp.stack([one_back, key_value_sent]),
        jnp.stack([two_back, one_back]),
    )
    pair_got = swap(pair_sent, "tensor")
    query_near = plane_stack(query_parts)
    query_far, pair_got = lax.optimization_barrier((swap(query_near, "core"), pair_got))
    pieces = [two_back, pair_got[0], one_back, pair_got[1], key_value_sent]
    query_full = whole_weight(query_near, query_far)
    output_parts = plane_parts(output_own)
    queries = project(normed_in, query_full, cosine, sine, 0, query_blocks, (True, True))
    queries, output_parts, expert_full[0] = lax.optimization_barrier(
        (queries, output_parts, expert_full[0])
    )
    output_near = plane_stack(output_parts)
    output_far = swap(output_near, "core")
    cotangent_near = plane_stack(cotangent_parts)
    cotangent_far = swap(cotangent_near, "core")
    expert = lax.axis_index(PLANE)

    def slots_of(cotangents):
        digits = cotangents[..., width:].reshape(2, group_rows, HEAD_SIZE).astype(jnp.int32)
        ranked_all = digits[..., :EXPERTS] * 64 + digits[..., EXPERTS : 2 * EXPERTS]
        routed = jnp.swapaxes((ranked_all <= pair_count).astype(F32), 1, 2)
        rank_own = jnp.sum(jnp.where(expert_ids == expert, ranked_all, 0), axis=-1)
        earlier = (rank_own[:, None, :] < rank_own[:, :, None]).astype(jnp.int32)
        slot = jnp.where(rank_own <= pair_count, jnp.sum(earlier, axis=-1), capacity)
        return slot, routed

    near_slots, far_slots = slots_of(cotangent_near), slots_of(cotangent_far)
    key_value = jnp.concatenate(pieces, axis=0)
    span = ATTEND_SPAN + own_rows
    segment_ext = lax.dynamic_slice_in_dim(segment_near, tensor_index * own_rows, span)
    view = (
        jnp.reshape(own_start, (1,)),
        segment_ext[:, None],
        segment_ext[None, ATTEND_SPAN:],
        queries,
        key_value,
    )
    heads_low, log_total = attention(*view, seq_len)
    heads_late, near_slots, far_slots = lax.optimization_barrier(
        (heads_low, near_slots, far_slots)
    )
    output_full, expert_full[1] = lax.optimization_barrier(
        (whole_weight(output_near, output_far), expert_full[1])
    )
    hidden_state = input_wide + dot(heads_low, output_full, ((1,), (1,)))
    second_factor = norm_factor(hidden_state)
    normed_mid_own = (hidden_state * second_factor * second_gain).astype(BF16)

    normed_parts, expert_full[2] = lax.optimization_barrier(
        (plane_parts(normed_mid_own), expert_full[2])
    )
    normed_near = plane_stack(normed_parts)
    normed_far = swap(normed_near, "core")
    own_expert = (expert_ids == expert).astype(F32)[:, None]
    router_t = router_weight.T

    def experts_on(tokens, cotangents, slots):
        slot, routed = slots
        return expert_groups(
            slot,
            routed,
            own_expert,
            router_t,
            tokens.reshape(2, group_rows, width),
            cotangents.reshape(2, group_rows, -1),
            expert_full,
            capacity,
        )

    on_near = experts_on(normed_near, cotangent_near, near_slots)
    on_far = experts_on(normed_far, cotangent_far, far_slots)
    blocks = (2 * halves, own_rows, width)
    (grad_near, moe_near), (grad_far, moe_far) = (
        [array.reshape(blocks) for array in side[:2]] for side in (on_near, on_far)
    )
    grad_blocks = fold_blocks(grad_near, swap(grad_far, "core"))
    grad_blocks, moe_far, on_near, on_far = lax.optimization_barrier(
        (grad_blocks, moe_far, on_near[2:], on_far[2:])
    )
    grad_mid_parts = fold_plane(grad_blocks)
    moe_got = swap(moe_far, "core")
    expert_part, moe_total = weight_grads(
        on_near, on_far, moe_near.reshape(-1, width), moe_got.reshape(-1, width), halves
    )
    expert_sum = lax.psum_scatter(expert_part, "outer", scatter_dimension=0, tiled=True)
    grad_mid_parts, moe_total = lax.optimization_barrier((grad_mid_parts, moe_total))
    moe_parts = fold_plane(list(moe_total.reshape(blocks)))
    grad_mid = wide_sum(grad_mid_parts)

    norm_input_part = norm_back(hidden_state, second_factor, second_gain, grad_mid)
    grad_state = cotangent.astype(F32) + norm_input_part
    grad_attn = grad_state.astype(BF16)
    grad_heads = dot(grad_attn, output_full, ((1,), (0,))).astype(BF16)
    output_total = fold_columns(grad_attn, heads_late, shard_rows)
    grad_query_pre, grad_far_kv, grad_own = attention_back(
        *view, log_total, grad_heads, cosine, sine, seq_len
    )
    query_total = fold_columns(normed_in, grad_query_pre, shard_rows)
    query_parts = fold_plane(distance_blocks(query_total))
    two_back, pair_old, one_back, pair_new = grad_far_kv.reshape(reach, own_rows, -1)
    pair_got, moe_parts = lax.optimization_barrier(
        (swap(jnp.stack([pair_old, pair_new]), "tensor"), moe_parts)
    )
    pair_old, pair_new = pair_got.astype(F32)
    one_back = one_back.astype(F32) + jnp.where(first, pair_old, pair_new)
    two_back = two_back.astype(F32) + jnp.where(first, 0.0, pair_old)
    grad_own = grad_own + jnp.where(first, pair_new, 0.0)
    grad_own = grad_own + shift_groups(one_back.astype(BF16), -1).astype(F32)
    grad_own = grad_own + shift_groups(two_back.astype(BF16), -2).astype(F32)
    grad_own, query_parts, output_total = lax.optimization_barrier(
        (grad_own, query_parts, output_total)
    )
    output_parts = fold_plane(distance_blocks(output_total))
    grad_key_value = []
    for half in range(halves):
        start = half * 2 * HEAD_SIZE
        key_part = grad_own[:, start : start + HEAD_SIZE]
        turned = jnp.concatenate(
            [key_part[:, HEAD_SIZE // 2 :], key_part[:, : HEAD_SIZE // 2]], axis=1
        )
        grad_key_value.append(key_part * cosine - turned * sine)
        grad_key_value.append(grad_own[:, start + HEAD_SIZE : start + 2 * HEAD_SIZE])
    grad_key_value_pre = jnp.concatenate(grad_key_value, axis=1).astype(BF16)
    key_value_total, output_parts = lax.optimization_barrier(
        (fold_columns(normed_in, grad_key_value_pre, shard_rows), output_parts)
    )
    output_weight_grad = outer_scatter(wide_sum(output_parts).astype(BF16))
    key_value_parts = fold_plane(distance_blocks(key_value_total))
    grad_in = dot(grad_query_pre, query_full, ((1,), (1,))) + dot(
        grad_key_value_pre, key_value_full, ((1,), (1,))
    )
    input_grad = grad_state + norm_back(input_wide, first_factor, first_gain, grad_in)
    qkv_grad, expert_sum = outer_scatter(
        jnp.concatenate([wide_sum(query_parts), wide_sum(key_value_parts)], axis=2).astype(BF16),
        expert_sum,
    )
    block_output = hidden_state + wide_sum(moe_parts)
    expert_sum = expert_sum.reshape(groups, shard_rows, halves, -1)
    expert_sum = jnp.swapaxes(expert_sum, 1, 2).reshape(plane, shard_rows, -1)
    expert_sum = lax.all_to_all(expert_sum, PLANE, 0, 0, tiled=True)
    gate_grad, up_grad, down_grad = (
        jnp.swapaxes(expert_sum[:, :, at * half_ff : (at + 1) * half_ff], 0, 1).astype(F32)
        for at in range(3)
    )
    router_grad = jnp.sum(expert_sum[:, :, 3 * half_ff : 3 * half_ff + EXPERTS].astype(F32), axis=0)
    router_grad = lax.dynamic_slice_in_dim(
        router_grad, tensor_index * (shard_rows // 2), shard_rows // 2, 0
    )
    query_grad = qkv_grad[:, :query_columns]
    key_grad = qkv_grad[:, query_columns : query_columns + HEAD_SIZE]
    value_grad = qkv_grad[:, query_columns + HEAD_SIZE :]

    half_rows = shard_rows // 2
    own_gains = lax.dynamic_slice_in_dim(
        norm_gains, lax.axis_index(DP) * shard_rows, shard_rows, 0
    )
    qkv_own = jnp.concatenate([query_matrix, key_value_weight], axis=1)
    first_sum = jnp.sum(qkv_grad * qkv_own.astype(F32), axis=-1)
    second_sum = jnp.sum(
        gate_grad * gate_weight.astype(F32) + up_grad * up_weight.astype(F32), axis=(1, 2)
    )
    gain_sums = jnp.stack([first_sum, second_sum], axis=1) / own_gains
    kept = lax.dynamic_slice_in_dim(gain_sums, tensor_index * half_rows, half_rows, 0)
    sent = lax.dynamic_slice_in_dim(gain_sums, (1 - tensor_index) * half_rows, half_rows, 0)
    own_router = lax.dynamic_slice_in_dim(
        router_weight, lax.axis_index(ALL) * half_rows, half_rows, 0
    )
    router_sum = jnp.sum(router_grad * own_router.astype(F32), axis=-1)
    half_gains = lax.dynamic_slice_in_dim(own_gains, tensor_index * half_rows, half_rows, 0)
    router_sum = router_sum / half_gains[:, 1]
    gains_grad = (
        kept
        + swap(sent, "tensor")
        + jnp.stack([jnp.zeros_like(router_sum), router_sum], axis=1)
    )
    return (
        block_output,
        input_grad,
        gains_grad,
        router_grad,
        query_grad,
        key_grad,
        value_grad,
        output_weight_grad,
        gate_grad,
        up_grad,
        down_grad,
    )


def solution(mesh):
    dp_size, tensor_size = mesh.shape["dp"], mesh.shape["tensor"]
    split = Mesh(mesh.devices.reshape(dp_size // 4, 2, 2, tensor_size), ALL)
    return jax.shard_map(
        on_device,
        mesh=split,
        in_specs=(
            P(ALL, None),
            P(),
            P(),
            P(DP, "tensor"),
            P(DP, "tensor"),
            P(DP, "tensor"),
            P(DP, "tensor"),
            P(DP, None, "tensor"),
            P(DP, None, "tensor"),
            P(DP, None, "tensor"),
            P(DP),
            P(DP, None),
            P(DP),
            P(ALL, None),
        ),
        out_specs=(
            P(ALL, None),
            P(ALL, None),
            P(ALL, None),
            P(ALL, None),
            P(DP, "tensor"),
            P(DP, "tensor"),
            P(DP, "tensor"),
            P(DP, "tensor"),
            P(DP, None, "tensor"),
            P(DP, None, "tensor"),
            P(DP, None, "tensor"),
        ),
        check_vma=False,
    )
```

```python
import functools
import math

import jax
import jax.numpy as jnp
from jax import lax
from jax.experimental import pallas as pl
from jax.experimental.pallas import tpu as pltpu
from jax.sharding import Mesh
from jax.sharding import PartitionSpec as P

HEAD_SIZE = 128
TOPK = 4
EXPERTS = 8
ATTEND_SPAN = 1024
SEQ_MOST = 16384
EPSILON = 1e-06
ROPE_BASE = 10000.0
BF16 = jnp.bfloat16
F32 = jnp.float32

DP = ("outer", "x", "core")
PLANE = ("x", "core", "tensor")
ALL = ("outer", "x", "core", "tensor")


def shift_groups(x, by):
    length = lax.axis_size(DP)
    return lax.ppermute(x, DP, [(i, i + by) for i in range(length) if 0 <= i + by < length])


def swap(x, axis):
    length = lax.axis_size(axis)
    return lax.ppermute(x, axis, [(i, length - 1 - i) for i in range(length)])


def plane_parts(own):
    return [own, swap(own, "tensor"), swap(own, "x"), swap(own, ("x", "tensor"))]


def plane_stack(parts):
    return jnp.stack(parts).reshape((2, 2) + parts[0].shape)


def whole_weight(near, far):
    x, tensor = lax.axis_index("x"), lax.axis_index("tensor")
    first = lax.axis_index("core") == 0
    by_core = [jnp.where(first, near, far), jnp.where(first, far, near)]

    def piece(x_at, core_at, tensor_at):
        picked = lax.dynamic_index_in_dim(by_core[core_at], x ^ x_at, 0, keepdims=False)
        return lax.dynamic_index_in_dim(picked, tensor ^ tensor_at, 0, keepdims=False)

    places = [(x_at, core_at) for x_at in range(2) for core_at in range(2)]
    halves = [jnp.stack([piece(*place, at) for place in places], 1) for at in range(2)]
    return jnp.concatenate(halves, axis=-1).reshape(-1, 2 * near.shape[-1])


def fold_core(kept, sent):
    return (kept.astype(F32) + swap(sent, "core").astype(F32)).astype(BF16)


def fold_blocks(kept, got):
    return [
        (kept[at].astype(F32) + got[at].astype(F32)).astype(BF16) for at in range(kept.shape[0])
    ]


def in_order(own, other, axis_name, axis):
    first = lax.axis_index(axis_name) == 0
    return jnp.stack([jnp.where(first, own, other), jnp.where(first, other, own)], axis)


def fold_plane(blocks):
    return [
        blocks[0],
        swap(blocks[1], "tensor"),
        swap(blocks[2], "x"),
        swap(blocks[3], ("x", "tensor")),
    ]


def wide_sum(parts):
    return sum(part.astype(F32) for part in parts)


def outer_shift(x, by):
    length = lax.axis_size("outer")
    return lax.ppermute(x, "outer", [(i, (i + by) % length) for i in range(length)])


def outer_gather(shard):
    length, here = lax.axis_size("outer"), lax.axis_index("outer")
    if length > 4:
        return lax.all_gather(shard, "outer")
    full = jnp.zeros((length,) + shard.shape, shard.dtype)
    for by in range(length):
        piece = outer_shift(shard, by) if by else shard
        full = lax.dynamic_update_slice_in_dim(full, piece[None], (here - by) % length, 0)
    return full


def outer_scatter(parts, later=None):
    length, here = lax.axis_size("outer"), lax.axis_index("outer")
    if length > 4:
        total = lax.psum_scatter(parts, "outer", scatter_dimension=0, tiled=False).astype(F32)
        return total if later is None else (total, later)
    total = lax.dynamic_index_in_dim(parts, here, 0, keepdims=False).astype(F32)
    for by in range(1, length):
        piece = lax.dynamic_index_in_dim(parts, (here + by) % length, 0, keepdims=False)
        piece = outer_shift(piece, by)
        if by == 1 and later is not None:
            piece, later = lax.optimization_barrier((piece, later))
        total = total + piece.astype(F32)
    return total if later is None else (total, later)


def core_columns(rows, core_at, shard_rows):
    count = rows.shape[0]
    split = rows.reshape(count, -1, 2, shard_rows)
    return lax.dynamic_index_in_dim(split, core_at, 2, keepdims=False).reshape(count, -1)


def fold_columns(left, right, shard_rows):
    core = lax.axis_index("core")
    sent = dot(core_columns(left, 1 - core, shard_rows), right, ((0,), (0,))).astype(BF16)
    kept = dot(core_columns(left, core, shard_rows), right, ((0,), (0,))).astype(BF16)
    return fold_core(kept, sent).reshape(-1, 2, shard_rows, right.shape[1])


def distance_blocks(total):
    x, tensor = lax.axis_index("x"), lax.axis_index("tensor")
    columns = total.shape[3] // 2
    blocks = []
    for x_by in range(2):
        for tensor_by in range(2):
            block = lax.dynamic_index_in_dim(total, x ^ x_by, 1, keepdims=False)
            start = (tensor ^ tensor_by) * columns
            blocks.append(lax.dynamic_slice_in_dim(block, start, columns, 2))
    return blocks


def rotary_tables(position):
    halfway = HEAD_SIZE // 2
    inverse = jnp.exp(
        jnp.arange(halfway, dtype=F32) * (-2.0 * math.log(ROPE_BASE) / HEAD_SIZE)
    )
    angles = position.astype(F32)[:, None] * inverse[None, :]
    cosine, sine = jnp.cos(angles), jnp.sin(angles)
    return (
        jnp.concatenate([cosine, cosine], axis=1),
        jnp.concatenate([-sine, sine], axis=1),
    )


def norm_factor(value_rows):
    return lax.rsqrt(jnp.mean(value_rows * value_rows, axis=-1, keepdims=True) + EPSILON)


def norm_back(value_rows, factor, gain, upstream):
    weighted = upstream * gain
    return factor * weighted - value_rows * (factor * factor * factor) * jnp.mean(
        weighted * value_rows, axis=-1, keepdims=True
    )


def dot(a, b, dims):
    return lax.dot_general(a, b, (dims, ((), ())), preferred_element_type=F32)


VMEM_LIMIT = 60 * 1024 * 1024
LIGHT = pl.CostEstimate(flops=1000, bytes_accessed=1000, transcendentals=0)
FROM_LAST = (((1,), (1,)), ((), ()))
PLAIN = (((1,), (0,)), ((), ()))


def mxu(a, b, dims=PLAIN):
    return lax.dot_general(a, b, dims, preferred_element_type=F32)


def turn(rows, cosine, sine):
    return rows * cosine + pltpu.roll(rows, HEAD_SIZE // 2, 1) * sine


def project_kernel(rows_ref, weight_ref, cosine_ref, sine_ref, out_ref, *, turned):
    product = mxu(rows_ref[...], weight_ref[...])
    for at, turns in enumerate(turned):
        part = product[:, at * HEAD_SIZE : (at + 1) * HEAD_SIZE]
        if turns:
            part = turn(part, cosine_ref[...], sine_ref[...])
        out_ref[:, at * HEAD_SIZE : (at + 1) * HEAD_SIZE] = part.astype(BF16)


def project(rows, weight, cosine, sine, first, count, turned):
    high, width = rows.shape
    columns = len(turned) * HEAD_SIZE
    return pl.pallas_call(
        functools.partial(project_kernel, turned=turned),
        grid=(count,),
        in_specs=[
            pl.BlockSpec((high, width), lambda j: (0, 0)),
            pl.BlockSpec((width, columns), lambda j: (0, first + j)),
            pl.BlockSpec((high, HEAD_SIZE), lambda j: (0, 0)),
            pl.BlockSpec((high, HEAD_SIZE), lambda j: (0, 0)),
        ],
        out_specs=pl.BlockSpec((high, columns), lambda j: (0, j)),
        out_shape=jax.ShapeDtypeStruct((high, count * columns), BF16),
        compiler_params=pltpu.CompilerParams(vmem_limit_bytes=VMEM_LIMIT),
        cost_estimate=LIGHT,
        name="project",
    )(rows, weight, cosine, sine)


def mask_bias(place_ref, segment_key_ref, segment_query_ref, bias_ref, seq_len):
    span, rows = bias_ref.shape
    start = place_ref[0]
    key_at = lax.broadcasted_iota(jnp.int32, (span, rows), 0)
    query_at = lax.broadcasted_iota(jnp.int32, (span, rows), 1) + ATTEND_SPAN
    distance = query_at - key_at
    position = start + query_at - ATTEND_SPAN
    sequence_at = query_at - lax.rem(position, seq_len)
    allowed = (distance >= 0) & (distance < ATTEND_SPAN) & (key_at >= sequence_at)
    allowed = allowed & (segment_key_ref[...] == segment_query_ref[...])
    bias_ref[...] = jnp.where(allowed, 0.0, -1e30)


def attention_kernel(
    place_ref,
    segment_key_ref,
    segment_query_ref,
    q_ref,
    kv_ref,
    heads_ref,
    lse_ref,
    bias_ref,
    *,
    seq_len,
    scale,
):
    @pl.when(pl.program_id(0) == 0)
    def _():
        mask_bias(place_ref, segment_key_ref, segment_query_ref, bias_ref, seq_len)

    rows = q_ref.shape[0]
    span = kv_ref.shape[0]
    count = q_ref.shape[1] // HEAD_SIZE
    value_t = kv_ref[:, HEAD_SIZE:].T
    chunks = span // rows
    for head in range(count):
        columns = slice(head * HEAD_SIZE, (head + 1) * HEAD_SIZE)
        query = q_ref[:, columns]
        scores = []
        for c in range(chunks):
            part = slice(c * rows, (c + 1) * rows)
            raw = mxu(kv_ref[part, :HEAD_SIZE], query, FROM_LAST)
            scores.append(raw * scale + bias_ref[part, :])
        top = functools.reduce(jnp.maximum, scores)
        top = jnp.max(top, axis=0, keepdims=True)
        total = jnp.zeros_like(top)
        out_t = jnp.zeros((HEAD_SIZE, rows), F32)
        for c in range(chunks):
            weight = jnp.exp(scores[c] - top)
            total = total + jnp.sum(weight, axis=0, keepdims=True)
            out_t = out_t + mxu(value_t[:, c * rows : (c + 1) * rows], weight.astype(BF16))
        heads_ref[:, columns] = (out_t / total).T.astype(BF16)
        lse_ref[0, head : head + 1, :] = top + jnp.log(total)


def attention(place, segment_key, segment_query, queries, key_value, seq_len):
    rows, all_columns = queries.shape
    span = key_value.shape[0]
    pairs = key_value.shape[1] // (2 * HEAD_SIZE)
    columns = all_columns // pairs
    return pl.pallas_call(
        functools.partial(attention_kernel, seq_len=seq_len, scale=1.0 / math.sqrt(HEAD_SIZE)),
        grid=(pairs,),
        in_specs=[
            pl.BlockSpec(memory_space=pltpu.SMEM),
            pl.BlockSpec((span, 1), lambda j: (0, 0)),
            pl.BlockSpec((1, rows), lambda j: (0, 0)),
            pl.BlockSpec((rows, columns), lambda j: (0, j)),
            pl.BlockSpec((span, 2 * HEAD_SIZE), lambda j: (0, j)),
        ],
        out_specs=[
            pl.BlockSpec((rows, columns), lambda j: (0, j)),
            pl.BlockSpec((1, columns // HEAD_SIZE, rows), lambda j: (j, 0, 0)),
        ],
        out_shape=[
            jax.ShapeDtypeStruct((rows, all_columns), BF16),
            jax.ShapeDtypeStruct((pairs, columns // HEAD_SIZE, rows), F32),
        ],
        scratch_shapes=[pltpu.VMEM((span, rows), F32)],
        compiler_params=pltpu.CompilerParams(vmem_limit_bytes=VMEM_LIMIT),
        cost_estimate=LIGHT,
        name="attention",
    )(place, segment_key, segment_query, queries, key_value)


def attention_back_kernel(
    place_ref,
    segment_key_ref,
    segment_query_ref,
    q_ref,
    kv_ref,
    lse_ref,
    dout_ref,
    cosine_ref,
    sine_ref,
    dq_ref,
    dkv_far_ref,
    dkv_own_ref,
    bias_ref,
    dkv_ref,
    *,
    seq_len,
    scale,
):
    @pl.when(pl.program_id(0) == 0)
    def _():
        mask_bias(place_ref, segment_key_ref, segment_query_ref, bias_ref, seq_len)

    rows = q_ref.shape[0]
    span = kv_ref.shape[0]
    count = q_ref.shape[1] // HEAD_SIZE
    key_t = kv_ref[:, :HEAD_SIZE].T
    chunks = span // rows
    dkv_ref[...] = jnp.zeros_like(dkv_ref)
    for head in range(count):
        columns = slice(head * HEAD_SIZE, (head + 1) * HEAD_SIZE)
        query = q_ref[:, columns]
        dout = dout_ref[:, columns]
        lse = lse_ref[0, head : head + 1, :]
        probs, dprobs = [], []
        row_dot = jnp.zeros_like(lse)
        for c in range(chunks):
            part = slice(c * rows, (c + 1) * rows)
            raw = mxu(kv_ref[part, :HEAD_SIZE], query, FROM_LAST)
            prob = jnp.exp(raw * scale + bias_ref[part, :] - lse)
            dprob = mxu(kv_ref[part, HEAD_SIZE:], dout, FROM_LAST)
            row_dot = row_dot + jnp.sum(prob * dprob, axis=0, keepdims=True)
            probs.append(prob)
            dprobs.append(dprob)
        dq_t = jnp.zeros((HEAD_SIZE, rows), F32)
        for c in range(chunks):
            part = slice(c * rows, (c + 1) * rows)
            dscore = (probs[c] * (dprobs[c] - row_dot)).astype(BF16)
            dkv_ref[part, :HEAD_SIZE] += mxu(dscore, query)
            dkv_ref[part, HEAD_SIZE:] += mxu(probs[c].astype(BF16), dout)
            dq_t = dq_t + mxu(key_t[:, part], dscore)
        dq_ref[:, columns] = turn(dq_t.T * scale, cosine_ref[...], -sine_ref[...]).astype(BF16)
    dkv_ref[:, :HEAD_SIZE] = dkv_ref[:, :HEAD_SIZE] * scale
    dkv_far_ref[...] = dkv_ref[: span - rows, :].astype(BF16)
    dkv_own_ref[...] = dkv_ref[span - rows :, :]


def attention_back(
    place, segment_key, segment_query, queries, key_value, lse, dout, cosine, sine, seq_len
):
    rows, all_columns = queries.shape
    span = key_value.shape[0]
    pairs = key_value.shape[1] // (2 * HEAD_SIZE)
    columns = all_columns // pairs
    return pl.pallas_call(
        functools.partial(
            attention_back_kernel, seq_len=seq_len, scale=1.0 / math.sqrt(HEAD_SIZE)
        ),
        grid=(pairs,),
        in_specs=[
            pl.BlockSpec(memory_space=pltpu.SMEM),
            pl.BlockSpec((span, 1), lambda j: (0, 0)),
            pl.BlockSpec((1, rows), lambda j: (0, 0)),
            pl.BlockSpec((rows, columns), lambda j: (0, j)),
            pl.BlockSpec((span, 2 * HEAD_SIZE), lambda j: (0, j)),
            pl.BlockSpec((1, columns // HEAD_SIZE, rows), lambda j: (j, 0, 0)),
            pl.BlockSpec((rows, columns), lambda j: (0, j)),
            pl.BlockSpec((rows, HEAD_SIZE), lambda j: (0, 0)),
            pl.BlockSpec((rows, HEAD_SIZE), lambda j: (0, 0)),
        ],
        out_specs=[
            pl.BlockSpec((rows, columns), lambda j: (0, j)),
            pl.BlockSpec((span - rows, 2 * HEAD_SIZE), lambda j: (0, j)),
            pl.BlockSpec((rows, 2 * HEAD_SIZE), lambda j: (0, j)),
        ],
        out_shape=[
            jax.ShapeDtypeStruct((rows, all_columns), BF16),
            jax.ShapeDtypeStruct((span - rows, key_value.shape[1]), BF16),
            jax.ShapeDtypeStruct((rows, key_value.shape[1]), F32),
        ],
        scratch_shapes=[
            pltpu.VMEM((span, rows), F32),
            pltpu.VMEM((span, 2 * HEAD_SIZE), F32),
        ],
        compiler_params=pltpu.CompilerParams(vmem_limit_bytes=VMEM_LIMIT),
        cost_estimate=pl.CostEstimate(
            flops=70_000_000_000, bytes_accessed=10_000_000, transcendentals=0
        ),
        name="attention_back",
    )(place, segment_key, segment_query, queries, key_value, lse, dout, cosine, sine)


def expert_kernel(
    slot_row_ref,
    slot_column_ref,
    routed_ref,
    own_ref,
    router_ref,
    tokens_ref,
    cotangent_ref,
    gate_ref,
    up_ref,
    down_ref,
    grad_ref,
    moe_ref,
    rows_in_ref,
    grad_out_ref,
    hidden_ref,
    grad_gate_ref,
    grad_up_ref,
    router_grad_ref,
    gate_full_ref,
    up_full_ref,
    down_full_ref,
    *,
    capacity,
):
    whole = ((gate_ref, gate_full_ref), (up_ref, up_full_ref), (down_ref, down_full_ref))

    @pl.when(pl.program_id(0) == 0)
    def _():
        for held, full in whole:
            columns = held.shape[3]
            for half in range(held.shape[1]):
                full[:, half * columns : (half + 1) * columns] = held[:, half].reshape(-1, columns)

    group_rows = tokens_ref.shape[1]
    tokens = tokens_ref[0]
    gate_weight, up_weight, down_weight = (full[...] for _, full in whole)
    cotangent = cotangent_ref[0]
    routed = routed_ref[0] > 0.0
    logits = jnp.where(routed, mxu(router_ref[...], tokens, FROM_LAST), -1e30)
    weights = jnp.exp(logits - jnp.max(logits, axis=0, keepdims=True))
    weights = jnp.where(routed, weights, 0.0)
    gates = weights / jnp.sum(weights, axis=0, keepdims=True)
    own = own_ref[...]
    gate_own = jnp.sum(gates * own, axis=0, keepdims=True)
    place = slot_row_ref[0] == lax.broadcasted_iota(jnp.int32, (capacity, group_rows), 0)
    place_wide = jnp.where(place, 1.0, 0.0)
    place_low = place_wide.astype(BF16)
    back = slot_column_ref[0] == lax.broadcasted_iota(jnp.int32, (group_rows, capacity), 1)
    back_low = jnp.where(back, 1.0, 0.0).astype(BF16)
    coefficient = jnp.sum(place_wide * gate_own, axis=1, keepdims=True)

    rows_in = mxu(place_low, tokens).astype(BF16)
    rows_in_ref[...] = rows_in
    gate_pre = mxu(rows_in, gate_weight)
    up_pre = mxu(rows_in, up_weight)
    sigmoid = 1.0 / (1.0 + jnp.exp(-gate_pre))
    silu = gate_pre * sigmoid
    hidden = (silu * up_pre).astype(BF16)
    hidden_ref[...] = hidden
    slot_cotangent = mxu(place_low, cotangent)
    grad_out = (coefficient * slot_cotangent).astype(BF16)
    grad_out_ref[...] = grad_out
    grad_hidden = mxu(grad_out, down_weight)
    grad_up = (grad_hidden * silu).astype(BF16)
    grad_gate = (grad_hidden * up_pre * sigmoid * (1.0 + gate_pre * (1.0 - sigmoid))).astype(BF16)
    grad_up_ref[...] = grad_up
    grad_gate_ref[...] = grad_gate
    expert_out = mxu(hidden, down_weight, FROM_LAST)
    grad_slot = jnp.sum(slot_cotangent * expert_out, axis=1, keepdims=True)
    moe_ref[0] = mxu(back_low, (coefficient * expert_out).astype(BF16)).astype(BF16)

    grad_token = jnp.sum(place_wide * grad_slot, axis=0, keepdims=True)
    share = (grad_token * gate_own) * (own - gates)
    share_high = share.astype(BF16)
    share_low = (share - share_high.astype(F32)).astype(BF16)
    router_grad = mxu(share_high, tokens) + mxu(share_low, tokens)

    @pl.when(pl.program_id(0) == 0)
    def _():
        router_grad_ref[...] = router_grad

    @pl.when(pl.program_id(0) > 0)
    def _():
        router_grad_ref[...] += router_grad

    grad_in = mxu(grad_gate, gate_weight, FROM_LAST) + mxu(grad_up, up_weight, FROM_LAST)
    grad_ref[0] = (
        mxu(back_low, grad_in.astype(BF16)) + mxu(share.T.astype(BF16), router_ref[...])
    ).astype(BF16)


def expert_groups(slot, routed, own, router_t, tokens, cotangent, weights, capacity):
    count, group_rows, width = tokens.shape
    ff = weights[0].shape[1] * weights[0].shape[3]
    experts = router_t.shape[0]
    weight = pl.BlockSpec(
        weights[0].shape, lambda g: (0, 0, 0, 0), pipeline_mode=pl.Buffered(1)
    )
    whole = lambda g: (0, 0)
    by_group = lambda g: (g, 0, 0)
    slots = lambda columns: pl.BlockSpec((capacity, columns), lambda g: (g, 0))
    slots_shape = lambda columns: jax.ShapeDtypeStruct((count * capacity, columns), BF16)
    return pl.pallas_call(
        functools.partial(expert_kernel, capacity=capacity),
        grid=(count,),
        in_specs=[
            pl.BlockSpec((1, 1, group_rows), by_group),
            pl.BlockSpec((1, group_rows, 1), by_group),
            pl.BlockSpec((1, experts, group_rows), by_group),
            pl.BlockSpec((experts, 1), whole),
            pl.BlockSpec((experts, width), whole),
            pl.BlockSpec((1, group_rows, width), by_group),
            pl.BlockSpec((1, group_rows, width), by_group),
            weight,
            weight,
            weight,
        ],
        out_specs=[
            pl.BlockSpec((1, group_rows, width), by_group),
            pl.BlockSpec((1, group_rows, width), by_group),
            slots(width),
            slots(width),
            slots(ff),
            slots(ff),
            slots(ff),
            pl.BlockSpec((experts, width), whole),
        ],
        out_shape=[
            jax.ShapeDtypeStruct(tokens.shape, BF16),
            jax.ShapeDtypeStruct(tokens.shape, BF16),
            slots_shape(width),
            slots_shape(width),
            slots_shape(ff),
            slots_shape(ff),
            slots_shape(ff),
            jax.ShapeDtypeStruct((experts, width), F32),
        ],
        scratch_shapes=[pltpu.VMEM((width, ff), BF16) for _ in range(3)],
        compiler_params=pltpu.CompilerParams(vmem_limit_bytes=VMEM_LIMIT),
        cost_estimate=LIGHT,
        name="expert",
    )(
        slot[:, None, :],
        slot[:, :, None],
        routed,
        own,
        router_t,
        tokens,
        cotangent,
        *weights,
    )


def weight_grad_kernel(*refs, halves):
    rows, grad_out, hidden, grad_gate, grad_up, router = (
        refs[at : at + 2] for at in range(0, 12, 2)
    )
    moe_kept_ref, moe_got_ref, out_ref = refs[12:15]
    for at, moe_ref in enumerate(refs[15:]):
        moe_ref[...] = (moe_kept_ref[at].astype(F32) + moe_got_ref[at].astype(F32)).astype(BF16)
    columns = hidden[0].shape[1] // halves
    over = (((0,), (0,)), ((), ()))
    left_rows = [ref[...] for ref in rows]
    left_out = [ref[...] for ref in grad_out]
    router_columns = (router[0][...] + router[1][...]).T
    router_columns = jnp.concatenate(
        [
            router_columns,
            jnp.zeros((router_columns.shape[0], HEAD_SIZE - router_columns.shape[1]), F32),
        ],
        axis=1,
    ).astype(BF16)
    for half in range(halves):
        start = half * (3 * columns + HEAD_SIZE)
        part = slice(half * columns, (half + 1) * columns)
        for at, (left, right) in enumerate(
            ((left_rows, grad_gate), (left_rows, grad_up), (left_out, hidden))
        ):
            total = mxu(left[0], right[0][:, part], over) + mxu(left[1], right[1][:, part], over)
            out_ref[:, start + at * columns : start + (at + 1) * columns] = total.astype(BF16)
        out_ref[:, start + 3 * columns : start + 3 * columns + HEAD_SIZE] = router_columns


def weight_grads(near, far, moe_kept, moe_got, halves, block=256):
    rows_at, grad_out_at, hidden_at, grad_gate_at, grad_up_at, router_at = range(6)
    slots, width = near[rows_at].shape
    ff = near[hidden_at].shape[1]
    experts = near[router_at].shape[0]
    specs, operands = [], []
    for at in (rows_at, grad_out_at, hidden_at, grad_gate_at, grad_up_at, router_at):
        if at in (rows_at, grad_out_at):
            spec = pl.BlockSpec((slots, block), lambda i: (0, i))
        elif at == router_at:
            spec = pl.BlockSpec((experts, block), lambda i: (0, i))
        else:
            spec = pl.BlockSpec((slots, ff), lambda i: (0, 0))
        specs += [spec, spec]
        operands += [near[at], far[at]]
    columns = 3 * ff + halves * HEAD_SIZE
    moe_count, moe_rows, _ = moe_kept.shape
    moe_spec = pl.BlockSpec((moe_count, moe_rows, block), lambda i: (0, 0, i))
    moe_out_spec = pl.BlockSpec((moe_rows, block), lambda i: (0, i))
    return pl.pallas_call(
        functools.partial(weight_grad_kernel, halves=halves),
        grid=(width // block,),
        in_specs=specs + [moe_spec, moe_spec],
        out_specs=[pl.BlockSpec((block, columns), lambda i: (i, 0))] + [moe_out_spec] * moe_count,
        out_shape=[jax.ShapeDtypeStruct((width, columns), BF16)]
        + [jax.ShapeDtypeStruct((moe_rows, width), BF16)] * moe_count,
        compiler_params=pltpu.CompilerParams(vmem_limit_bytes=VMEM_LIMIT),
        cost_estimate=pl.CostEstimate(
            flops=15_000_000_000, bytes_accessed=50_000_000, transcendentals=0
        ),
        name="weight_grads",
    )(*operands, moe_kept, moe_got)


def on_device(
    block_input,
    norm_gains,
    router_weight,
    query_matrix,
    key_matrix,
    value_matrix,
    output_weight,
    gate_weight,
    up_weight,
    down_weight,
    segment_ids,
    routes,
    priority,
    cotangent,
):
    tensor_index = lax.axis_index("tensor")
    own_rows, width = block_input.shape
    group_rows = segment_ids.shape[0]
    halves = lax.axis_size("tensor")
    outer = lax.axis_size("outer")
    groups = lax.axis_size("x") * lax.axis_size("core")
    plane = groups * halves
    shard_rows = query_matrix.shape[0]
    dp_size = outer * groups
    seq_len = min(SEQ_MOST, group_rows * dp_size)
    own_start = lax.axis_index(ALL) * own_rows
    capacity = group_rows * TOPK // EXPERTS
    reach = ATTEND_SPAN // own_rows
    half_ff = gate_weight.shape[2]
    ff = half_ff * halves

    query_columns = query_matrix.shape[1]
    pair_columns = 2 * halves * HEAD_SIZE
    first = tensor_index == 0
    key_value_weight = jnp.concatenate([key_matrix, value_matrix], axis=1)
    other_weight = swap(key_value_weight, "tensor")
    early = jnp.concatenate(
        [
            jnp.where(first, key_value_weight, other_weight),
            jnp.where(first, other_weight, key_value_weight),
            query_matrix,
            output_weight,
        ],
        axis=1,
    )
    early, gate_own, up_own, down_own, cotangent_own = lax.optimization_barrier(
        (early, gate_weight, up_weight, down_weight, cotangent)
    )
    early = outer_gather(early)

    expert_shard = jnp.transpose(jnp.stack([gate_own, up_own, down_own]), (2, 0, 1, 3))
    expert_shard = lax.all_to_all(expert_shard, PLANE, 0, 0, tiled=True)
    pair_count = group_rows * TOPK
    rank = (
        jnp.zeros((pair_count,), jnp.int32)
        .at[priority]
        .set(jnp.arange(pair_count, dtype=jnp.int32))
        .reshape(group_rows, TOPK)
    )
    expert_ids = jnp.arange(EXPERTS, dtype=jnp.int32)
    named = routes[:, :, None] == expert_ids[None, None, :]
    ranked = jnp.sum(jnp.where(named, rank[:, :, None] + 1, 0), axis=1)
    ranked = jnp.where(ranked > 0, ranked, pair_count + 1)
    ranked_own = lax.dynamic_slice_in_dim(ranked, tensor_index * own_rows, own_rows, 0)
    digits = jnp.concatenate([ranked_own // 64, ranked_own % 64], axis=1).astype(BF16)
    digits = jnp.pad(digits, ((0, 0), (0, HEAD_SIZE - digits.shape[1])))
    cotangent_sent = jnp.concatenate([cotangent_own, digits], axis=1)
    expert_shard = expert_shard.reshape(groups, halves, 3, shard_rows, half_ff)
    expert_shard = [
        jnp.swapaxes(expert_shard[:, :, at], 0, 1).reshape(-1, half_ff) for at in range(3)
    ]
    early, expert_shard, segment_here = lax.optimization_barrier(
        (early, expert_shard, segment_ids)
    )
    segment_near = jnp.concatenate(
        [shift_groups(segment_here, 2), shift_groups(segment_here, 1), segment_here]
    )
    expert_full = [
        lax.all_gather(shard, "outer").reshape(outer, halves, groups * shard_rows, half_ff)
        for shard in expert_shard
    ]

    key_value_full = early[:, :, :pair_columns]
    key_value_full = in_order(key_value_full, swap(key_value_full, "x"), "x", 1)
    key_value_full = in_order(key_value_full, swap(key_value_full, "core"), "core", 2)
    key_value_full = key_value_full.reshape(width, pair_columns)
    query_parts = plane_parts(early[:, :, pair_columns : pair_columns + query_columns])

    input_wide = block_input.astype(F32)
    first_gain = norm_gains[:, 0]
    second_gain = norm_gains[:, 1]
    first_factor = norm_factor(input_wide)
    normed_in = (input_wide * first_factor * first_gain).astype(BF16)
    positions = own_start + jnp.arange(own_rows, dtype=jnp.int32)
    cosine, sine = rotary_tables(positions % seq_len)
    query_blocks = halves * query_columns // (2 * HEAD_SIZE)
    key_value_sent = project(
        normed_in, key_value_full, cosine, sine, 0, halves, (True, False)
    )
    one_back, two_back = shift_groups(key_value_sent, 1), shift_groups(key_value_sent, 2)
    query_parts, one_back, two_back, segment_near, cotangent_sent = lax.optimization_barrier(
        (query_parts, one_back, two_back, segment_near, cotangent_sent)
    )
    cotangent_parts = plane_parts(cotangent_sent)
    output_own = early[:, :, pair_columns + query_columns :]
    pair_sent = jnp.where(
        first,
        jnp.stack([one_back, key_value_sent]),
        jnp.stack([two_back, one_back]),
    )
    pair_got = swap(pair_sent, "tensor")
    query_near = plane_stack(query_parts)
    query_far, pair_got, expert_full[0] = lax.optimization_barrier(
        (swap(query_near, "core"), pair_got, expert_full[0])
    )
    pieces = [two_back, pair_got[0], one_back, pair_got[1], key_value_sent]
    query_full = whole_weight(query_near, query_far)
    queries = project(normed_in, query_full, cosine, sine, 0, query_blocks, (True, True))
    queries, cotangent_parts, output_own = lax.optimization_barrier(
        (queries, cotangent_parts, output_own)
    )
    output_parts = plane_parts(output_own)
    cotangent_near = plane_stack(cotangent_parts)
    cotangent_far = swap(cotangent_near, "core")
    expert = lax.axis_index(PLANE)

    def slots_of(cotangents):
        digits = cotangents[..., width:].reshape(2, group_rows, HEAD_SIZE).astype(jnp.int32)
        ranked_all = digits[..., :EXPERTS] * 64 + digits[..., EXPERTS : 2 * EXPERTS]
        routed = jnp.swapaxes((ranked_all <= pair_count).astype(F32), 1, 2)
        rank_own = jnp.sum(jnp.where(expert_ids == expert, ranked_all, 0), axis=-1)
        earlier = (rank_own[:, None, :] < rank_own[:, :, None]).astype(jnp.int32)
        slot = jnp.where(rank_own <= pair_count, jnp.sum(earlier, axis=-1), capacity)
        return slot, routed

    near_slots, far_slots = slots_of(cotangent_near), slots_of(cotangent_far)
    key_value = jnp.concatenate(pieces, axis=0)
    span = ATTEND_SPAN + own_rows
    segment_ext = lax.dynamic_slice_in_dim(segment_near, tensor_index * own_rows, span)
    view = (
        jnp.reshape(own_start, (1,)),
        segment_ext[:, None],
        segment_ext[None, ATTEND_SPAN:],
        queries,
        key_value,
    )
    heads_low, log_total = attention(*view, seq_len)
    heads_late, output_parts, near_slots, far_slots = lax.optimization_barrier(
        (heads_low, output_parts, near_slots, far_slots)
    )
    output_near = plane_stack(output_parts)
    output_far = swap(output_near, "core")
    output_full, expert_full[1] = lax.optimization_barrier(
        (whole_weight(output_near, output_far), expert_full[1])
    )
    hidden_state = input_wide + dot(heads_low, output_full, ((1,), (1,)))
    second_factor = norm_factor(hidden_state)
    normed_mid_own = (hidden_state * second_factor * second_gain).astype(BF16)

    normed_parts, expert_full[2] = lax.optimization_barrier(
        (plane_parts(normed_mid_own), expert_full[2])
    )
    normed_near = plane_stack(normed_parts)
    normed_far = swap(normed_near, "core")
    own_expert = (expert_ids == expert).astype(F32)[:, None]
    router_t = router_weight.T

    def experts_on(tokens, cotangents, slots):
        slot, routed = slots
        return expert_groups(
            slot,
            routed,
            own_expert,
            router_t,
            tokens.reshape(2, group_rows, width),
            cotangents.reshape(2, group_rows, -1),
            expert_full,
            capacity,
        )

    on_near = experts_on(normed_near, cotangent_near, near_slots)
    on_far = experts_on(normed_far, cotangent_far, far_slots)
    blocks = (2 * halves, own_rows, width)
    (grad_near, moe_near), (grad_far, moe_far) = (
        [array.reshape(blocks) for array in side[:2]] for side in (on_near, on_far)
    )
    grad_blocks = fold_blocks(grad_near, swap(grad_far, "core"))
    grad_blocks, moe_far, on_near, on_far = lax.optimization_barrier(
        (grad_blocks, moe_far, on_near[2:], on_far[2:])
    )
    grad_mid_parts = fold_plane(grad_blocks)
    expert_part, *moe_blocks = weight_grads(
        on_near, on_far, moe_near, swap(moe_far, "core"), halves
    )
    expert_sum = lax.psum_scatter(expert_part, "outer", scatter_dimension=0, tiled=True)
    grad_mid_parts, moe_blocks = lax.optimization_barrier((grad_mid_parts, moe_blocks))
    moe_parts = fold_plane(moe_blocks)
    grad_mid = wide_sum(grad_mid_parts)

    norm_input_part = norm_back(hidden_state, second_factor, second_gain, grad_mid)
    grad_state = cotangent.astype(F32) + norm_input_part
    grad_attn = grad_state.astype(BF16)
    grad_heads = dot(grad_attn, output_full, ((1,), (0,))).astype(BF16)
    output_total = fold_columns(grad_attn, heads_late, shard_rows)
    grad_query_pre, grad_far_kv, grad_own = attention_back(
        *view, log_total, grad_heads, cosine, sine, seq_len
    )
    grad_query_pre, moe_parts = lax.optimization_barrier((grad_query_pre, moe_parts))
    query_total = fold_columns(normed_in, grad_query_pre, shard_rows)
    query_parts = fold_plane(distance_blocks(query_total))
    two_back, pair_old, one_back, pair_new = grad_far_kv.reshape(reach, own_rows, -1)
    pair_old, pair_new = swap(jnp.stack([pair_old, pair_new]), "tensor").astype(F32)
    one_back = one_back.astype(F32) + jnp.where(first, pair_old, pair_new)
    two_back = two_back.astype(F32) + jnp.where(first, 0.0, pair_old)
    grad_own = grad_own + jnp.where(first, pair_new, 0.0)
    grad_own = grad_own + shift_groups(one_back.astype(BF16), -1).astype(F32)
    grad_own = grad_own + shift_groups(two_back.astype(BF16), -2).astype(F32)
    grad_own, query_parts, output_total = lax.optimization_barrier(
        (grad_own, query_parts, output_total)
    )
    output_parts = fold_plane(distance_blocks(output_total))
    grad_key_value = []
    for half in range(halves):
        start = half * 2 * HEAD_SIZE
        key_part = grad_own[:, start : start + HEAD_SIZE]
        turned = jnp.concatenate(
            [key_part[:, HEAD_SIZE // 2 :], key_part[:, : HEAD_SIZE // 2]], axis=1
        )
        grad_key_value.append(key_part * cosine - turned * sine)
        grad_key_value.append(grad_own[:, start + HEAD_SIZE : start + 2 * HEAD_SIZE])
    grad_key_value_pre = jnp.concatenate(grad_key_value, axis=1).astype(BF16)
    key_value_total, output_parts = lax.optimization_barrier(
        (fold_columns(normed_in, grad_key_value_pre, shard_rows), output_parts)
    )
    output_weight_grad = outer_scatter(wide_sum(output_parts).astype(BF16))
    key_value_parts = fold_plane(distance_blocks(key_value_total))
    grad_in = dot(grad_query_pre, query_full, ((1,), (1,))) + dot(
        grad_key_value_pre, key_value_full, ((1,), (1,))
    )
    input_grad = grad_state + norm_back(input_wide, first_factor, first_gain, grad_in)
    qkv_grad, expert_sum = outer_scatter(
        jnp.concatenate([wide_sum(query_parts), wide_sum(key_value_parts)], axis=2).astype(BF16),
        expert_sum,
    )
    block_output = hidden_state + wide_sum(moe_parts)
    expert_sum = expert_sum.reshape(groups, shard_rows, halves, -1)
    expert_sum = jnp.swapaxes(expert_sum, 1, 2).reshape(plane, shard_rows, -1)
    expert_sum = lax.all_to_all(expert_sum, PLANE, 0, 0, tiled=True)
    gate_grad, up_grad, down_grad = (
        jnp.swapaxes(expert_sum[:, :, at * half_ff : (at + 1) * half_ff], 0, 1).astype(F32)
        for at in range(3)
    )
    router_grad = jnp.sum(expert_sum[:, :, 3 * half_ff : 3 * half_ff + EXPERTS].astype(F32), axis=0)
    router_grad = lax.dynamic_slice_in_dim(
        router_grad, tensor_index * (shard_rows // 2), shard_rows // 2, 0
    )
    query_grad = qkv_grad[:, :query_columns]
    key_grad = qkv_grad[:, query_columns : query_columns + HEAD_SIZE]
    value_grad = qkv_grad[:, query_columns + HEAD_SIZE :]

    half_rows = shard_rows // 2
    own_gains = lax.dynamic_slice_in_dim(
        norm_gains, lax.axis_index(DP) * shard_rows, shard_rows, 0
    )
    qkv_own = jnp.concatenate([query_matrix, key_value_weight], axis=1)
    first_sum = jnp.sum(qkv_grad * qkv_own.astype(F32), axis=-1)
    second_sum = jnp.sum(
        gate_grad * gate_weight.astype(F32) + up_grad * up_weight.astype(F32), axis=(1, 2)
    )
    gain_sums = jnp.stack([first_sum, second_sum], axis=1) / own_gains
    kept = lax.dynamic_slice_in_dim(gain_sums, tensor_index * half_rows, half_rows, 0)
    sent = lax.dynamic_slice_in_dim(gain_sums, (1 - tensor_index) * half_rows, half_rows, 0)
    own_router = lax.dynamic_slice_in_dim(
        router_weight, lax.axis_index(ALL) * half_rows, half_rows, 0
    )
    router_sum = jnp.sum(router_grad * own_router.astype(F32), axis=-1)
    half_gains = lax.dynamic_slice_in_dim(own_gains, tensor_index * half_rows, half_rows, 0)
    router_sum = router_sum / half_gains[:, 1]
    gains_grad = (
        kept
        + swap(sent, "tensor")
        + jnp.stack([jnp.zeros_like(router_sum), router_sum], axis=1)
    )
    return (
        block_output,
        input_grad,
        gains_grad,
        router_grad,
        query_grad,
        key_grad,
        value_grad,
        output_weight_grad,
        gate_grad,
        up_grad,
        down_grad,
    )


def solution(mesh):
    dp_size, tensor_size = mesh.shape["dp"], mesh.shape["tensor"]
    split = Mesh(mesh.devices.reshape(dp_size // 4, 2, 2, tensor_size), ALL)
    return jax.shard_map(
        on_device,
        mesh=split,
        in_specs=(
            P(ALL, None),
            P(),
            P(),
            P(DP, "tensor"),
            P(DP, "tensor"),
            P(DP, "tensor"),
            P(DP, "tensor"),
            P(DP, None, "tensor"),
            P(DP, None, "tensor"),
            P(DP, None, "tensor"),
            P(DP),
            P(DP, None),
            P(DP),
            P(ALL, None),
        ),
        out_specs=(
            P(ALL, None),
            P(ALL, None),
            P(ALL, None),
            P(ALL, None),
            P(DP, "tensor"),
            P(DP, "tensor"),
            P(DP, "tensor"),
            P(DP, "tensor"),
            P(DP, None, "tensor"),
            P(DP, None, "tensor"),
            P(DP, None, "tensor"),
        ),
        check_vma=False,
    )
```

```python
import functools
import math

import jax
import jax.numpy as jnp
from jax import lax
from jax.experimental import pallas as pl
from jax.experimental.pallas import tpu as pltpu
from jax.sharding import Mesh
from jax.sharding import PartitionSpec as P

HEAD_SIZE = 128
TOPK = 4
EXPERTS = 8
ATTEND_SPAN = 1024
SEQ_MOST = 16384
EPSILON = 1e-06
ROPE_BASE = 10000.0
BF16 = jnp.bfloat16
F32 = jnp.float32

DP = ("outer", "x", "core")
PLANE = ("x", "core", "tensor")
ALL = ("outer", "x", "core", "tensor")


def shift_groups(x, by):
    length = lax.axis_size(DP)
    return lax.ppermute(x, DP, [(i, i + by) for i in range(length) if 0 <= i + by < length])


def swap(x, axis):
    length = lax.axis_size(axis)
    return lax.ppermute(x, axis, [(i, length - 1 - i) for i in range(length)])


def plane_parts(own):
    return [own, swap(own, "tensor"), swap(own, "x"), swap(own, ("x", "tensor"))]


def plane_stack(parts):
    return jnp.stack(parts).reshape((2, 2) + parts[0].shape)


def whole_weight(near, far):
    x, tensor = lax.axis_index("x"), lax.axis_index("tensor")
    first = lax.axis_index("core") == 0
    by_core = [jnp.where(first, near, far), jnp.where(first, far, near)]

    def piece(x_at, core_at, tensor_at):
        picked = lax.dynamic_index_in_dim(by_core[core_at], x ^ x_at, 0, keepdims=False)
        return lax.dynamic_index_in_dim(picked, tensor ^ tensor_at, 0, keepdims=False)

    places = [(x_at, core_at) for x_at in range(2) for core_at in range(2)]
    halves = [jnp.stack([piece(*place, at) for place in places], 1) for at in range(2)]
    return jnp.concatenate(halves, axis=-1).reshape(-1, 2 * near.shape[-1])


def fold_core(kept, sent):
    return (kept.astype(F32) + swap(sent, "core").astype(F32)).astype(BF16)


def fold_blocks(kept, got):
    return [
        (kept[at].astype(F32) + got[at].astype(F32)).astype(BF16) for at in range(kept.shape[0])
    ]


def in_order(own, other, axis_name, axis):
    first = lax.axis_index(axis_name) == 0
    return jnp.stack([jnp.where(first, own, other), jnp.where(first, other, own)], axis)


def fold_plane(blocks):
    return [
        blocks[0],
        swap(blocks[1], "tensor"),
        swap(blocks[2], "x"),
        swap(blocks[3], ("x", "tensor")),
    ]


def wide_sum(parts):
    return sum(part.astype(F32) for part in parts)


def outer_shift(x, by):
    length = lax.axis_size("outer")
    return lax.ppermute(x, "outer", [(i, (i + by) % length) for i in range(length)])


def outer_gather(shard):
    length, here = lax.axis_size("outer"), lax.axis_index("outer")
    if length > 4:
        return lax.all_gather(shard, "outer")
    full = jnp.zeros((length,) + shard.shape, shard.dtype)
    for by in range(length):
        piece = outer_shift(shard, by) if by else shard
        full = lax.dynamic_update_slice_in_dim(full, piece[None], (here - by) % length, 0)
    return full


def outer_scatter(parts, later=None):
    length, here = lax.axis_size("outer"), lax.axis_index("outer")
    if length > 4:
        total = lax.psum_scatter(parts, "outer", scatter_dimension=0, tiled=False).astype(F32)
        return total if later is None else (total, later)
    total = lax.dynamic_index_in_dim(parts, here, 0, keepdims=False).astype(F32)
    pieces = [
        outer_shift(lax.dynamic_index_in_dim(parts, (here + by) % length, 0, keepdims=False), by)
        for by in range(1, length)
    ]
    if later is not None:
        pieces, later = lax.optimization_barrier((pieces, later))
    total = total + wide_sum(pieces)
    return total if later is None else (total, later)


def core_columns(rows, core_at, shard_rows):
    count = rows.shape[0]
    split = rows.reshape(count, -1, 2, shard_rows)
    return lax.dynamic_index_in_dim(split, core_at, 2, keepdims=False).reshape(count, -1)


def fold_columns(left, right, shard_rows):
    core = lax.axis_index("core")
    sent = dot(core_columns(left, 1 - core, shard_rows), right, ((0,), (0,))).astype(BF16)
    kept = dot(core_columns(left, core, shard_rows), right, ((0,), (0,))).astype(BF16)
    return fold_core(kept, sent).reshape(-1, 2, shard_rows, right.shape[1])


def distance_blocks(total):
    x, tensor = lax.axis_index("x"), lax.axis_index("tensor")
    columns = total.shape[3] // 2
    blocks = []
    for x_by in range(2):
        for tensor_by in range(2):
            block = lax.dynamic_index_in_dim(total, x ^ x_by, 1, keepdims=False)
            start = (tensor ^ tensor_by) * columns
            blocks.append(lax.dynamic_slice_in_dim(block, start, columns, 2))
    return blocks


def rotary_tables(position):
    halfway = HEAD_SIZE // 2
    inverse = jnp.exp(
        jnp.arange(halfway, dtype=F32) * (-2.0 * math.log(ROPE_BASE) / HEAD_SIZE)
    )
    angles = position.astype(F32)[:, None] * inverse[None, :]
    cosine, sine = jnp.cos(angles), jnp.sin(angles)
    return (
        jnp.concatenate([cosine, cosine], axis=1),
        jnp.concatenate([-sine, sine], axis=1),
    )


def norm_factor(value_rows):
    return lax.rsqrt(jnp.mean(value_rows * value_rows, axis=-1, keepdims=True) + EPSILON)


def norm_back(value_rows, factor, gain, upstream):
    weighted = upstream * gain
    return factor * weighted - value_rows * (factor * factor * factor) * jnp.mean(
        weighted * value_rows, axis=-1, keepdims=True
    )


def dot(a, b, dims):
    return lax.dot_general(a, b, (dims, ((), ())), preferred_element_type=F32)


VMEM_LIMIT = 60 * 1024 * 1024
LIGHT = pl.CostEstimate(flops=1000, bytes_accessed=1000, transcendentals=0)
FROM_LAST = (((1,), (1,)), ((), ()))
PLAIN = (((1,), (0,)), ((), ()))


def mxu(a, b, dims=PLAIN):
    return lax.dot_general(a, b, dims, preferred_element_type=F32)


def turn(rows, cosine, sine):
    return rows * cosine + pltpu.roll(rows, HEAD_SIZE // 2, 1) * sine


def project_kernel(rows_ref, weight_ref, cosine_ref, sine_ref, out_ref, *, turned):
    product = mxu(rows_ref[...], weight_ref[...])
    for at, turns in enumerate(turned):
        part = product[:, at * HEAD_SIZE : (at + 1) * HEAD_SIZE]
        if turns:
            part = turn(part, cosine_ref[...], sine_ref[...])
        out_ref[:, at * HEAD_SIZE : (at + 1) * HEAD_SIZE] = part.astype(BF16)


def project(rows, weight, cosine, sine, first, count, turned):
    high, width = rows.shape
    columns = len(turned) * HEAD_SIZE
    return pl.pallas_call(
        functools.partial(project_kernel, turned=turned),
        grid=(count,),
        in_specs=[
            pl.BlockSpec((high, width), lambda j: (0, 0)),
            pl.BlockSpec((width, columns), lambda j: (0, first + j)),
            pl.BlockSpec((high, HEAD_SIZE), lambda j: (0, 0)),
            pl.BlockSpec((high, HEAD_SIZE), lambda j: (0, 0)),
        ],
        out_specs=pl.BlockSpec((high, columns), lambda j: (0, j)),
        out_shape=jax.ShapeDtypeStruct((high, count * columns), BF16),
        compiler_params=pltpu.CompilerParams(vmem_limit_bytes=VMEM_LIMIT),
        cost_estimate=LIGHT,
        name="project",
    )(rows, weight, cosine, sine)


def mask_bias(place_ref, segment_key_ref, segment_query_ref, bias_ref, seq_len):
    span, rows = bias_ref.shape
    start = place_ref[0]
    key_at = lax.broadcasted_iota(jnp.int32, (span, rows), 0)
    query_at = lax.broadcasted_iota(jnp.int32, (span, rows), 1) + ATTEND_SPAN
    distance = query_at - key_at
    position = start + query_at - ATTEND_SPAN
    sequence_at = query_at - lax.rem(position, seq_len)
    allowed = (distance >= 0) & (distance < ATTEND_SPAN) & (key_at >= sequence_at)
    allowed = allowed & (segment_key_ref[...] == segment_query_ref[...])
    bias_ref[...] = jnp.where(allowed, 0.0, -1e30)


def attention_kernel(
    place_ref,
    segment_key_ref,
    segment_query_ref,
    q_ref,
    kv_ref,
    heads_ref,
    lse_ref,
    bias_ref,
    *,
    seq_len,
    scale,
):
    @pl.when(pl.program_id(0) == 0)
    def _():
        mask_bias(place_ref, segment_key_ref, segment_query_ref, bias_ref, seq_len)

    rows = q_ref.shape[0]
    span = kv_ref.shape[0]
    count = q_ref.shape[1] // HEAD_SIZE
    value_t = kv_ref[:, HEAD_SIZE:].T
    chunks = span // rows
    for head in range(count):
        columns = slice(head * HEAD_SIZE, (head + 1) * HEAD_SIZE)
        query = q_ref[:, columns]
        scores = []
        for c in range(chunks):
            part = slice(c * rows, (c + 1) * rows)
            raw = mxu(kv_ref[part, :HEAD_SIZE], query, FROM_LAST)
            scores.append(raw * scale + bias_ref[part, :])
        top = functools.reduce(jnp.maximum, scores)
        top = jnp.max(top, axis=0, keepdims=True)
        total = jnp.zeros_like(top)
        out_t = jnp.zeros((HEAD_SIZE, rows), F32)
        for c in range(chunks):
            weight = jnp.exp(scores[c] - top)
            total = total + jnp.sum(weight, axis=0, keepdims=True)
            out_t = out_t + mxu(value_t[:, c * rows : (c + 1) * rows], weight.astype(BF16))
        heads_ref[:, columns] = (out_t / total).T.astype(BF16)
        lse_ref[0, head : head + 1, :] = top + jnp.log(total)


def attention(place, segment_key, segment_query, queries, key_value, seq_len):
    rows, all_columns = queries.shape
    span = key_value.shape[0]
    pairs = key_value.shape[1] // (2 * HEAD_SIZE)
    columns = all_columns // pairs
    return pl.pallas_call(
        functools.partial(attention_kernel, seq_len=seq_len, scale=1.0 / math.sqrt(HEAD_SIZE)),
        grid=(pairs,),
        in_specs=[
            pl.BlockSpec(memory_space=pltpu.SMEM),
            pl.BlockSpec((span, 1), lambda j: (0, 0)),
            pl.BlockSpec((1, rows), lambda j: (0, 0)),
            pl.BlockSpec((rows, columns), lambda j: (0, j)),
            pl.BlockSpec((span, 2 * HEAD_SIZE), lambda j: (0, j)),
        ],
        out_specs=[
            pl.BlockSpec((rows, columns), lambda j: (0, j)),
            pl.BlockSpec((1, columns // HEAD_SIZE, rows), lambda j: (j, 0, 0)),
        ],
        out_shape=[
            jax.ShapeDtypeStruct((rows, all_columns), BF16),
            jax.ShapeDtypeStruct((pairs, columns // HEAD_SIZE, rows), F32),
        ],
        scratch_shapes=[pltpu.VMEM((span, rows), F32)],
        compiler_params=pltpu.CompilerParams(vmem_limit_bytes=VMEM_LIMIT),
        cost_estimate=LIGHT,
        name="attention",
    )(place, segment_key, segment_query, queries, key_value)


def attention_back_kernel(
    place_ref,
    segment_key_ref,
    segment_query_ref,
    q_ref,
    kv_ref,
    lse_ref,
    dout_ref,
    cosine_ref,
    sine_ref,
    dq_ref,
    dkv_far_ref,
    dkv_own_ref,
    bias_ref,
    dkv_ref,
    *,
    seq_len,
    scale,
):
    @pl.when(pl.program_id(0) == 0)
    def _():
        mask_bias(place_ref, segment_key_ref, segment_query_ref, bias_ref, seq_len)

    rows = q_ref.shape[0]
    span = kv_ref.shape[0]
    count = q_ref.shape[1] // HEAD_SIZE
    key_t = kv_ref[:, :HEAD_SIZE].T
    chunks = span // rows
    dkv_ref[...] = jnp.zeros_like(dkv_ref)
    for head in range(count):
        columns = slice(head * HEAD_SIZE, (head + 1) * HEAD_SIZE)
        query = q_ref[:, columns]
        dout = dout_ref[:, columns]
        lse = lse_ref[0, head : head + 1, :]
        probs, dprobs = [], []
        row_dot = jnp.zeros_like(lse)
        for c in range(chunks):
            part = slice(c * rows, (c + 1) * rows)
            raw = mxu(kv_ref[part, :HEAD_SIZE], query, FROM_LAST)
            prob = jnp.exp(raw * scale + bias_ref[part, :] - lse)
            dprob = mxu(kv_ref[part, HEAD_SIZE:], dout, FROM_LAST)
            row_dot = row_dot + jnp.sum(prob * dprob, axis=0, keepdims=True)
            probs.append(prob)
            dprobs.append(dprob)
        dq_t = jnp.zeros((HEAD_SIZE, rows), F32)
        for c in range(chunks):
            part = slice(c * rows, (c + 1) * rows)
            dscore = (probs[c] * (dprobs[c] - row_dot)).astype(BF16)
            dkv_ref[part, :HEAD_SIZE] += mxu(dscore, query)
            dkv_ref[part, HEAD_SIZE:] += mxu(probs[c].astype(BF16), dout)
            dq_t = dq_t + mxu(key_t[:, part], dscore)
        dq_ref[:, columns] = turn(dq_t.T * scale, cosine_ref[...], -sine_ref[...]).astype(BF16)
    dkv_ref[:, :HEAD_SIZE] = dkv_ref[:, :HEAD_SIZE] * scale
    dkv_far_ref[...] = dkv_ref[: span - rows, :].astype(BF16)
    dkv_own_ref[...] = dkv_ref[span - rows :, :]


def attention_back(
    place, segment_key, segment_query, queries, key_value, lse, dout, cosine, sine, seq_len
):
    rows, all_columns = queries.shape
    span = key_value.shape[0]
    pairs = key_value.shape[1] // (2 * HEAD_SIZE)
    columns = all_columns // pairs
    return pl.pallas_call(
        functools.partial(
            attention_back_kernel, seq_len=seq_len, scale=1.0 / math.sqrt(HEAD_SIZE)
        ),
        grid=(pairs,),
        in_specs=[
            pl.BlockSpec(memory_space=pltpu.SMEM),
            pl.BlockSpec((span, 1), lambda j: (0, 0)),
            pl.BlockSpec((1, rows), lambda j: (0, 0)),
            pl.BlockSpec((rows, columns), lambda j: (0, j)),
            pl.BlockSpec((span, 2 * HEAD_SIZE), lambda j: (0, j)),
            pl.BlockSpec((1, columns // HEAD_SIZE, rows), lambda j: (j, 0, 0)),
            pl.BlockSpec((rows, columns), lambda j: (0, j)),
            pl.BlockSpec((rows, HEAD_SIZE), lambda j: (0, 0)),
            pl.BlockSpec((rows, HEAD_SIZE), lambda j: (0, 0)),
        ],
        out_specs=[
            pl.BlockSpec((rows, columns), lambda j: (0, j)),
            pl.BlockSpec((span - rows, 2 * HEAD_SIZE), lambda j: (0, j)),
            pl.BlockSpec((rows, 2 * HEAD_SIZE), lambda j: (0, j)),
        ],
        out_shape=[
            jax.ShapeDtypeStruct((rows, all_columns), BF16),
            jax.ShapeDtypeStruct((span - rows, key_value.shape[1]), BF16),
            jax.ShapeDtypeStruct((rows, key_value.shape[1]), F32),
        ],
        scratch_shapes=[
            pltpu.VMEM((span, rows), F32),
            pltpu.VMEM((span, 2 * HEAD_SIZE), F32),
        ],
        compiler_params=pltpu.CompilerParams(vmem_limit_bytes=VMEM_LIMIT),
        cost_estimate=pl.CostEstimate(
            flops=35_000_000_000, bytes_accessed=10_000_000, transcendentals=0
        ),
        name="attention_back",
    )(place, segment_key, segment_query, queries, key_value, lse, dout, cosine, sine)


def expert_kernel(
    slot_row_ref,
    slot_column_ref,
    routed_ref,
    own_ref,
    router_ref,
    tokens_ref,
    cotangent_ref,
    gate_ref,
    up_ref,
    down_ref,
    grad_ref,
    moe_ref,
    rows_in_ref,
    grad_out_ref,
    hidden_ref,
    grad_gate_ref,
    grad_up_ref,
    router_grad_ref,
    gate_full_ref,
    up_full_ref,
    down_full_ref,
    *,
    capacity,
):
    whole = ((gate_ref, gate_full_ref), (up_ref, up_full_ref), (down_ref, down_full_ref))

    @pl.when(pl.program_id(0) == 0)
    def _():
        for held, full in whole:
            columns = held.shape[3]
            for half in range(held.shape[1]):
                full[:, half * columns : (half + 1) * columns] = held[:, half].reshape(-1, columns)

    group_rows = tokens_ref.shape[1]
    tokens = tokens_ref[0]
    gate_weight, up_weight, down_weight = (full[...] for _, full in whole)
    cotangent = cotangent_ref[0]
    routed = routed_ref[0] > 0.0
    logits = jnp.where(routed, mxu(router_ref[...], tokens, FROM_LAST), -1e30)
    weights = jnp.exp(logits - jnp.max(logits, axis=0, keepdims=True))
    weights = jnp.where(routed, weights, 0.0)
    gates = weights / jnp.sum(weights, axis=0, keepdims=True)
    own = own_ref[...]
    gate_own = jnp.sum(gates * own, axis=0, keepdims=True)
    place = slot_row_ref[0] == lax.broadcasted_iota(jnp.int32, (capacity, group_rows), 0)
    place_wide = jnp.where(place, 1.0, 0.0)
    place_low = place_wide.astype(BF16)
    back = slot_column_ref[0] == lax.broadcasted_iota(jnp.int32, (group_rows, capacity), 1)
    back_low = jnp.where(back, 1.0, 0.0).astype(BF16)
    coefficient = jnp.sum(place_wide * gate_own, axis=1, keepdims=True)

    rows_in = mxu(place_low, tokens).astype(BF16)
    rows_in_ref[...] = rows_in
    gate_pre = mxu(rows_in, gate_weight)
    up_pre = mxu(rows_in, up_weight)
    sigmoid = 1.0 / (1.0 + jnp.exp(-gate_pre))
    silu = gate_pre * sigmoid
    hidden = (silu * up_pre).astype(BF16)
    hidden_ref[...] = hidden
    slot_cotangent = mxu(place_low, cotangent)
    grad_out = (coefficient * slot_cotangent).astype(BF16)
    grad_out_ref[...] = grad_out
    grad_hidden = mxu(grad_out, down_weight)
    grad_up = (grad_hidden * silu).astype(BF16)
    grad_gate = (grad_hidden * up_pre * sigmoid * (1.0 + gate_pre * (1.0 - sigmoid))).astype(BF16)
    grad_up_ref[...] = grad_up
    grad_gate_ref[...] = grad_gate
    expert_out = mxu(hidden, down_weight, FROM_LAST)
    grad_slot = jnp.sum(slot_cotangent * expert_out, axis=1, keepdims=True)
    moe_ref[0] = mxu(back_low, (coefficient * expert_out).astype(BF16)).astype(BF16)

    grad_token = jnp.sum(place_wide * grad_slot, axis=0, keepdims=True)
    share = (grad_token * gate_own) * (own - gates)
    share_high = share.astype(BF16)
    share_low = (share - share_high.astype(F32)).astype(BF16)
    router_grad = mxu(share_high, tokens) + mxu(share_low, tokens)

    @pl.when(pl.program_id(0) == 0)
    def _():
        router_grad_ref[...] = router_grad

    @pl.when(pl.program_id(0) > 0)
    def _():
        router_grad_ref[...] += router_grad

    grad_in = mxu(grad_gate, gate_weight, FROM_LAST) + mxu(grad_up, up_weight, FROM_LAST)
    grad_ref[0] = (
        mxu(back_low, grad_in.astype(BF16)) + mxu(share.T.astype(BF16), router_ref[...])
    ).astype(BF16)


def expert_groups(slot, routed, own, router_t, tokens, cotangent, weights, capacity):
    count, group_rows, width = tokens.shape
    ff = weights[0].shape[1] * weights[0].shape[3]
    experts = router_t.shape[0]
    weight = pl.BlockSpec(
        weights[0].shape, lambda g: (0, 0, 0, 0), pipeline_mode=pl.Buffered(1)
    )
    whole = lambda g: (0, 0)
    by_group = lambda g: (g, 0, 0)
    slots = lambda columns: pl.BlockSpec((capacity, columns), lambda g: (g, 0))
    slots_shape = lambda columns: jax.ShapeDtypeStruct((count * capacity, columns), BF16)
    return pl.pallas_call(
        functools.partial(expert_kernel, capacity=capacity),
        grid=(count,),
        in_specs=[
            pl.BlockSpec((1, 1, group_rows), by_group),
            pl.BlockSpec((1, group_rows, 1), by_group),
            pl.BlockSpec((1, experts, group_rows), by_group),
            pl.BlockSpec((experts, 1), whole),
            pl.BlockSpec((experts, width), whole),
            pl.BlockSpec((1, group_rows, width), by_group),
            pl.BlockSpec((1, group_rows, width), by_group),
            weight,
            weight,
            weight,
        ],
        out_specs=[
            pl.BlockSpec((1, group_rows, width), by_group),
            pl.BlockSpec((1, group_rows, width), by_group),
            slots(width),
            slots(width),
            slots(ff),
            slots(ff),
            slots(ff),
            pl.BlockSpec((experts, width), whole),
        ],
        out_shape=[
            jax.ShapeDtypeStruct(tokens.shape, BF16),
            jax.ShapeDtypeStruct(tokens.shape, BF16),
            slots_shape(width),
            slots_shape(width),
            slots_shape(ff),
            slots_shape(ff),
            slots_shape(ff),
            jax.ShapeDtypeStruct((experts, width), F32),
        ],
        scratch_shapes=[pltpu.VMEM((width, ff), BF16) for _ in range(3)],
        compiler_params=pltpu.CompilerParams(vmem_limit_bytes=VMEM_LIMIT),
        cost_estimate=LIGHT,
        name="expert",
    )(
        slot[:, None, :],
        slot[:, :, None],
        routed,
        own,
        router_t,
        tokens,
        cotangent,
        *weights,
    )


def weight_grad_kernel(*refs, halves):
    rows, grad_out, hidden, grad_gate, grad_up, router = (
        refs[at : at + 2] for at in range(0, 12, 2)
    )
    moe_kept_ref, moe_got_ref, out_ref = refs[12:15]
    for at, moe_ref in enumerate(refs[15:]):
        moe_ref[...] = (moe_kept_ref[at].astype(F32) + moe_got_ref[at].astype(F32)).astype(BF16)
    columns = hidden[0].shape[1] // halves
    over = (((0,), (0,)), ((), ()))
    left_rows = [ref[...] for ref in rows]
    left_out = [ref[...] for ref in grad_out]
    router_columns = (router[0][...] + router[1][...]).T
    router_columns = jnp.concatenate(
        [
            router_columns,
            jnp.zeros((router_columns.shape[0], HEAD_SIZE - router_columns.shape[1]), F32),
        ],
        axis=1,
    ).astype(BF16)
    for half in range(halves):
        start = half * (3 * columns + HEAD_SIZE)
        part = slice(half * columns, (half + 1) * columns)
        for at, (left, right) in enumerate(
            ((left_rows, grad_gate), (left_rows, grad_up), (left_out, hidden))
        ):
            total = mxu(left[0], right[0][:, part], over) + mxu(left[1], right[1][:, part], over)
            out_ref[:, start + at * columns : start + (at + 1) * columns] = total.astype(BF16)
        out_ref[:, start + 3 * columns : start + 3 * columns + HEAD_SIZE] = router_columns


def weight_grads(near, far, moe_kept, moe_got, halves, block=256):
    rows_at, grad_out_at, hidden_at, grad_gate_at, grad_up_at, router_at = range(6)
    slots, width = near[rows_at].shape
    ff = near[hidden_at].shape[1]
    experts = near[router_at].shape[0]
    specs, operands = [], []
    for at in (rows_at, grad_out_at, hidden_at, grad_gate_at, grad_up_at, router_at):
        if at in (rows_at, grad_out_at):
            spec = pl.BlockSpec((slots, block), lambda i: (0, i))
        elif at == router_at:
            spec = pl.BlockSpec((experts, block), lambda i: (0, i))
        else:
            spec = pl.BlockSpec((slots, ff), lambda i: (0, 0))
        specs += [spec, spec]
        operands += [near[at], far[at]]
    columns = 3 * ff + halves * HEAD_SIZE
    moe_count, moe_rows, _ = moe_kept.shape
    moe_spec = pl.BlockSpec((moe_count, moe_rows, block), lambda i: (0, 0, i))
    moe_out_spec = pl.BlockSpec((moe_rows, block), lambda i: (0, i))
    return pl.pallas_call(
        functools.partial(weight_grad_kernel, halves=halves),
        grid=(width // block,),
        in_specs=specs + [moe_spec, moe_spec],
        out_specs=[pl.BlockSpec((block, columns), lambda i: (i, 0))] + [moe_out_spec] * moe_count,
        out_shape=[jax.ShapeDtypeStruct((width, columns), BF16)]
        + [jax.ShapeDtypeStruct((moe_rows, width), BF16)] * moe_count,
        compiler_params=pltpu.CompilerParams(vmem_limit_bytes=VMEM_LIMIT),
        cost_estimate=pl.CostEstimate(
            flops=15_000_000_000, bytes_accessed=50_000_000, transcendentals=0
        ),
        name="weight_grads",
    )(*operands, moe_kept, moe_got)


def on_device(
    block_input,
    norm_gains,
    router_weight,
    query_matrix,
    key_matrix,
    value_matrix,
    output_weight,
    gate_weight,
    up_weight,
    down_weight,
    segment_ids,
    routes,
    priority,
    cotangent,
):
    tensor_index = lax.axis_index("tensor")
    own_rows, width = block_input.shape
    group_rows = segment_ids.shape[0]
    halves = lax.axis_size("tensor")
    outer = lax.axis_size("outer")
    groups = lax.axis_size("x") * lax.axis_size("core")
    plane = groups * halves
    shard_rows = query_matrix.shape[0]
    dp_size = outer * groups
    seq_len = min(SEQ_MOST, group_rows * dp_size)
    own_start = lax.axis_index(ALL) * own_rows
    capacity = group_rows * TOPK // EXPERTS
    reach = ATTEND_SPAN // own_rows
    half_ff = gate_weight.shape[2]
    ff = half_ff * halves

    query_columns = query_matrix.shape[1]
    pair_columns = 2 * halves * HEAD_SIZE
    first = tensor_index == 0
    key_value_weight = jnp.concatenate([key_matrix, value_matrix], axis=1)
    other_weight = swap(key_value_weight, "tensor")
    early = jnp.concatenate(
        [
            jnp.where(first, key_value_weight, other_weight),
            jnp.where(first, other_weight, key_value_weight),
            query_matrix,
            output_weight,
        ],
        axis=1,
    )
    early, gate_own, up_own, down_own, cotangent_own = lax.optimization_barrier(
        (early, gate_weight, up_weight, down_weight, cotangent)
    )
    early = outer_gather(early)

    expert_shard = jnp.transpose(jnp.stack([gate_own, up_own, down_own]), (2, 0, 1, 3))
    expert_shard = lax.all_to_all(expert_shard, PLANE, 0, 0, tiled=True)
    expert_shard = expert_shard.reshape(groups, halves, 3, shard_rows, half_ff)
    expert_shard = [
        jnp.swapaxes(expert_shard[:, :, at], 0, 1).reshape(-1, half_ff) for at in range(3)
    ]
    early, expert_shard, segment_here, priority_here = lax.optimization_barrier(
        (early, expert_shard, segment_ids, priority)
    )
    pair_count = group_rows * TOPK
    rank = (
        jnp.zeros((pair_count,), jnp.int32)
        .at[priority_here]
        .set(jnp.arange(pair_count, dtype=jnp.int32))
        .reshape(group_rows, TOPK)
    )
    expert_ids = jnp.arange(EXPERTS, dtype=jnp.int32)
    named = routes[:, :, None] == expert_ids[None, None, :]
    ranked = jnp.sum(jnp.where(named, rank[:, :, None] + 1, 0), axis=1)
    ranked = jnp.where(ranked > 0, ranked, pair_count + 1)
    ranked_own = lax.dynamic_slice_in_dim(ranked, tensor_index * own_rows, own_rows, 0)
    digits = jnp.concatenate([ranked_own // 64, ranked_own % 64], axis=1).astype(BF16)
    digits = jnp.pad(digits, ((0, 0), (0, HEAD_SIZE - digits.shape[1])))
    cotangent_sent = jnp.concatenate([cotangent_own, digits], axis=1)
    segment_near = jnp.concatenate(
        [shift_groups(segment_here, 2), shift_groups(segment_here, 1), segment_here]
    )
    expert_full = [
        lax.all_gather(shard, "outer").reshape(outer, halves, groups * shard_rows, half_ff)
        for shard in expert_shard
    ]

    key_value_full = early[:, :, :pair_columns]
    key_value_full = in_order(key_value_full, swap(key_value_full, "x"), "x", 1)
    key_value_full = in_order(key_value_full, swap(key_value_full, "core"), "core", 2)
    key_value_full = key_value_full.reshape(width, pair_columns)
    query_parts = plane_parts(early[:, :, pair_columns : pair_columns + query_columns])

    input_wide = block_input.astype(F32)
    first_gain = norm_gains[:, 0]
    second_gain = norm_gains[:, 1]
    first_factor = norm_factor(input_wide)
    normed_in = (input_wide * first_factor * first_gain).astype(BF16)
    positions = own_start + jnp.arange(own_rows, dtype=jnp.int32)
    cosine, sine = rotary_tables(positions % seq_len)
    query_blocks = halves * query_columns // (2 * HEAD_SIZE)
    key_value_sent = project(
        normed_in, key_value_full, cosine, sine, 0, halves, (True, False)
    )
    one_back, two_back = shift_groups(key_value_sent, 1), shift_groups(key_value_sent, 2)
    query_parts, one_back, two_back, segment_near, cotangent_sent = lax.optimization_barrier(
        (query_parts, one_back, two_back, segment_near, cotangent_sent)
    )
    cotangent_parts = plane_parts(cotangent_sent)
    output_own = early[:, :, pair_columns + query_columns :]
    pair_sent = jnp.where(
        first,
        jnp.stack([one_back, key_value_sent]),
        jnp.stack([two_back, one_back]),
    )
    pair_got = swap(pair_sent, "tensor")
    query_near = plane_stack(query_parts)
    query_far, pair_got, expert_full[0] = lax.optimization_barrier(
        (swap(query_near, "core"), pair_got, expert_full[0])
    )
    pieces = [two_back, pair_got[0], one_back, pair_got[1], key_value_sent]
    query_full = whole_weight(query_near, query_far)
    queries = project(normed_in, query_full, cosine, sine, 0, query_blocks, (True, True))
    output_parts = plane_parts(output_own)
    expert = lax.axis_index(PLANE)

    def slots_of(cotangents):
        digits = cotangents[..., width:].reshape(2, group_rows, HEAD_SIZE).astype(jnp.int32)
        ranked_all = digits[..., :EXPERTS] * 64 + digits[..., EXPERTS : 2 * EXPERTS]
        routed = jnp.swapaxes((ranked_all <= pair_count).astype(F32), 1, 2)
        rank_own = jnp.sum(jnp.where(expert_ids == expert, ranked_all, 0), axis=-1)
        earlier = (rank_own[:, None, :] < rank_own[:, :, None]).astype(jnp.int32)
        slot = jnp.where(rank_own <= pair_count, jnp.sum(earlier, axis=-1), capacity)
        return slot, routed

    key_value = jnp.concatenate(pieces, axis=0)
    span = ATTEND_SPAN + own_rows
    segment_ext = lax.dynamic_slice_in_dim(segment_near, tensor_index * own_rows, span)
    view = (
        jnp.reshape(own_start, (1,)),
        segment_ext[:, None],
        segment_ext[None, ATTEND_SPAN:],
        queries,
        key_value,
    )
    heads_low, log_total = attention(*view, seq_len)
    heads_late, output_parts = lax.optimization_barrier((heads_low, output_parts))
    output_near = plane_stack(output_parts)
    output_far = swap(output_near, "core")
    output_full, expert_full[1], cotangent_parts = lax.optimization_barrier(
        (whole_weight(output_near, output_far), expert_full[1], cotangent_parts)
    )
    cotangent_near = plane_stack(cotangent_parts)
    cotangent_far = swap(cotangent_near, "core")
    near_slots, far_slots = slots_of(cotangent_near), slots_of(cotangent_far)
    hidden_state = input_wide + dot(heads_low, output_full, ((1,), (1,)))
    second_factor = norm_factor(hidden_state)
    normed_mid_own = (hidden_state * second_factor * second_gain).astype(BF16)

    normed_parts, near_slots, far_slots, expert_full[2] = lax.optimization_barrier(
        (plane_parts(normed_mid_own), near_slots, far_slots, expert_full[2])
    )
    normed_near = plane_stack(normed_parts)
    normed_far = swap(normed_near, "core")
    own_expert = (expert_ids == expert).astype(F32)[:, None]
    router_t = router_weight.T

    def experts_on(tokens, cotangents, slots):
        slot, routed = slots
        return expert_groups(
            slot,
            routed,
            own_expert,
            router_t,
            tokens.reshape(2, group_rows, width),
            cotangents.reshape(2, group_rows, -1),
            expert_full,
            capacity,
        )

    on_near = experts_on(normed_near, cotangent_near, near_slots)
    on_far = experts_on(normed_far, cotangent_far, far_slots)
    blocks = (2 * halves, own_rows, width)
    (grad_near, moe_near), (grad_far, moe_far) = (
        [array.reshape(blocks) for array in side[:2]] for side in (on_near, on_far)
    )
    grad_blocks = fold_blocks(grad_near, swap(grad_far, "core"))
    grad_blocks, moe_far, on_near, on_far = lax.optimization_barrier(
        (grad_blocks, moe_far, on_near[2:], on_far[2:])
    )
    grad_mid_parts = fold_plane(grad_blocks)
    expert_part, *moe_blocks = weight_grads(
        on_near, on_far, moe_near, swap(moe_far, "core"), halves
    )
    expert_sum = lax.psum_scatter(expert_part, "outer", scatter_dimension=0, tiled=True)
    grad_mid_parts, moe_blocks = lax.optimization_barrier((grad_mid_parts, moe_blocks))
    moe_parts = fold_plane(moe_blocks)
    grad_mid = wide_sum(grad_mid_parts)

    norm_input_part = norm_back(hidden_state, second_factor, second_gain, grad_mid)
    grad_state = cotangent.astype(F32) + norm_input_part
    grad_attn = grad_state.astype(BF16)
    grad_heads = dot(grad_attn, output_full, ((1,), (0,))).astype(BF16)
    output_total = fold_columns(grad_attn, heads_late, shard_rows)
    grad_query_pre, grad_far_kv, grad_own = attention_back(
        *view, log_total, grad_heads, cosine, sine, seq_len
    )
    grad_query_pre, output_total, moe_parts = lax.optimization_barrier(
        (grad_query_pre, output_total, moe_parts)
    )
    output_parts = fold_plane(distance_blocks(output_total))
    query_total, output_parts = lax.optimization_barrier(
        (fold_columns(normed_in, grad_query_pre, shard_rows), output_parts)
    )
    query_parts = fold_plane(distance_blocks(query_total))
    output_weight_grad = outer_scatter(wide_sum(output_parts).astype(BF16))
    two_back, pair_old, one_back, pair_new = grad_far_kv.reshape(reach, own_rows, -1)
    pair_old, pair_new = swap(jnp.stack([pair_old, pair_new]), "tensor").astype(F32)
    one_back = one_back.astype(F32) + jnp.where(first, pair_old, pair_new)
    two_back = two_back.astype(F32) + jnp.where(first, 0.0, pair_old)
    grad_own = grad_own + jnp.where(first, pair_new, 0.0)
    grad_own = grad_own + shift_groups(one_back.astype(BF16), -1).astype(F32)
    grad_own = grad_own + shift_groups(two_back.astype(BF16), -2).astype(F32)
    grad_own, query_parts = lax.optimization_barrier((grad_own, query_parts))
    grad_key_value = []
    for half in range(halves):
        start = half * 2 * HEAD_SIZE
        key_part = grad_own[:, start : start + HEAD_SIZE]
        turned = jnp.concatenate(
            [key_part[:, HEAD_SIZE // 2 :], key_part[:, : HEAD_SIZE // 2]], axis=1
        )
        grad_key_value.append(key_part * cosine - turned * sine)
        grad_key_value.append(grad_own[:, start + HEAD_SIZE : start + 2 * HEAD_SIZE])
    grad_key_value_pre = jnp.concatenate(grad_key_value, axis=1).astype(BF16)
    key_value_total = fold_columns(normed_in, grad_key_value_pre, shard_rows)
    key_value_parts = fold_plane(distance_blocks(key_value_total))
    grad_in = dot(grad_query_pre, query_full, ((1,), (1,))) + dot(
        grad_key_value_pre, key_value_full, ((1,), (1,))
    )
    input_grad = grad_state + norm_back(input_wide, first_factor, first_gain, grad_in)
    qkv_grad, expert_sum = outer_scatter(
        jnp.concatenate([wide_sum(query_parts), wide_sum(key_value_parts)], axis=2).astype(BF16),
        expert_sum,
    )
    block_output = hidden_state + wide_sum(moe_parts)
    expert_sum = expert_sum.reshape(groups, shard_rows, halves, -1)
    expert_sum = jnp.swapaxes(expert_sum, 1, 2).reshape(plane, shard_rows, -1)
    expert_sum = lax.all_to_all(expert_sum, PLANE, 0, 0, tiled=True)
    gate_grad, up_grad, down_grad = (
        jnp.swapaxes(expert_sum[:, :, at * half_ff : (at + 1) * half_ff], 0, 1).astype(F32)
        for at in range(3)
    )
    router_grad = jnp.sum(expert_sum[:, :, 3 * half_ff : 3 * half_ff + EXPERTS].astype(F32), axis=0)
    router_grad = lax.dynamic_slice_in_dim(
        router_grad, tensor_index * (shard_rows // 2), shard_rows // 2, 0
    )
    query_grad = qkv_grad[:, :query_columns]
    key_grad = qkv_grad[:, query_columns : query_columns + HEAD_SIZE]
    value_grad = qkv_grad[:, query_columns + HEAD_SIZE :]

    half_rows = shard_rows // 2
    own_gains = lax.dynamic_slice_in_dim(
        norm_gains, lax.axis_index(DP) * shard_rows, shard_rows, 0
    )
    qkv_own = jnp.concatenate([query_matrix, key_value_weight], axis=1)
    first_sum = jnp.sum(qkv_grad * qkv_own.astype(F32), axis=-1)
    second_sum = jnp.sum(
        gate_grad * gate_weight.astype(F32) + up_grad * up_weight.astype(F32), axis=(1, 2)
    )
    gain_sums = jnp.stack([first_sum, second_sum], axis=1) / own_gains
    kept = lax.dynamic_slice_in_dim(gain_sums, tensor_index * half_rows, half_rows, 0)
    sent = lax.dynamic_slice_in_dim(gain_sums, (1 - tensor_index) * half_rows, half_rows, 0)
    own_router = lax.dynamic_slice_in_dim(
        router_weight, lax.axis_index(ALL) * half_rows, half_rows, 0
    )
    router_sum = jnp.sum(router_grad * own_router.astype(F32), axis=-1)
    half_gains = lax.dynamic_slice_in_dim(own_gains, tensor_index * half_rows, half_rows, 0)
    router_sum = router_sum / half_gains[:, 1]
    gains_grad = (
        kept
        + swap(sent, "tensor")
        + jnp.stack([jnp.zeros_like(router_sum), router_sum], axis=1)
    )
    return (
        block_output,
        input_grad,
        gains_grad,
        router_grad,
        query_grad,
        key_grad,
        value_grad,
        output_weight_grad,
        gate_grad,
        up_grad,
        down_grad,
    )


def solution(mesh):
    dp_size, tensor_size = mesh.shape["dp"], mesh.shape["tensor"]
    split = Mesh(mesh.devices.reshape(dp_size // 4, 2, 2, tensor_size), ALL)
    return jax.shard_map(
        on_device,
        mesh=split,
        in_specs=(
            P(ALL, None),
            P(),
            P(),
            P(DP, "tensor"),
            P(DP, "tensor"),
            P(DP, "tensor"),
            P(DP, "tensor"),
            P(DP, None, "tensor"),
            P(DP, None, "tensor"),
            P(DP, None, "tensor"),
            P(DP),
            P(DP, None),
            P(DP),
            P(ALL, None),
        ),
        out_specs=(
            P(ALL, None),
            P(ALL, None),
            P(ALL, None),
            P(ALL, None),
            P(DP, "tensor"),
            P(DP, "tensor"),
            P(DP, "tensor"),
            P(DP, "tensor"),
            P(DP, None, "tensor"),
            P(DP, None, "tensor"),
            P(DP, None, "tensor"),
        ),
        check_vma=False,
    )
```

```python
import functools
import math

import jax
import jax.numpy as jnp
from jax import lax
from jax.experimental import pallas as pl
from jax.experimental.pallas import tpu as pltpu
from jax.sharding import Mesh
from jax.sharding import PartitionSpec as P

HEAD_SIZE = 128
TOPK = 4
EXPERTS = 8
ATTEND_SPAN = 1024
SEQ_MOST = 16384
EPSILON = 1e-06
ROPE_BASE = 10000.0
BF16 = jnp.bfloat16
F32 = jnp.float32

DP = ("outer", "x", "core")
PLANE = ("x", "core", "tensor")
ALL = ("outer", "x", "core", "tensor")


def shift_groups(x, by):
    length = lax.axis_size(DP)
    return lax.ppermute(x, DP, [(i, i + by) for i in range(length) if 0 <= i + by < length])


def swap(x, axis):
    length = lax.axis_size(axis)
    return lax.ppermute(x, axis, [(i, length - 1 - i) for i in range(length)])


def plane_parts(own):
    return [own, swap(own, "tensor"), swap(own, "x"), swap(own, ("x", "tensor"))]


def plane_stack(parts):
    return jnp.stack(parts).reshape((2, 2) + parts[0].shape)


def whole_weight(near, far):
    x, tensor = lax.axis_index("x"), lax.axis_index("tensor")
    first = lax.axis_index("core") == 0
    by_core = [jnp.where(first, near, far), jnp.where(first, far, near)]

    def piece(x_at, core_at, tensor_at):
        picked = lax.dynamic_index_in_dim(by_core[core_at], x ^ x_at, 0, keepdims=False)
        return lax.dynamic_index_in_dim(picked, tensor ^ tensor_at, 0, keepdims=False)

    places = [(x_at, core_at) for x_at in range(2) for core_at in range(2)]
    halves = [jnp.stack([piece(*place, at) for place in places], 1) for at in range(2)]
    return jnp.concatenate(halves, axis=-1).reshape(-1, 2 * near.shape[-1])


def fold_core(kept, sent):
    return (kept.astype(F32) + swap(sent, "core").astype(F32)).astype(BF16)


def fold_blocks(kept, got):
    return [
        (kept[at].astype(F32) + got[at].astype(F32)).astype(BF16) for at in range(kept.shape[0])
    ]


def in_order(own, other, axis_name, axis):
    first = lax.axis_index(axis_name) == 0
    return jnp.stack([jnp.where(first, own, other), jnp.where(first, other, own)], axis)


def fold_plane(blocks):
    return [
        blocks[0],
        swap(blocks[1], "tensor"),
        swap(blocks[2], "x"),
        swap(blocks[3], ("x", "tensor")),
    ]


def wide_sum(parts):
    return sum(part.astype(F32) for part in parts)


def outer_shift(x, by):
    length = lax.axis_size("outer")
    return lax.ppermute(x, "outer", [(i, (i + by) % length) for i in range(length)])


def outer_gather(shard):
    length, here = lax.axis_size("outer"), lax.axis_index("outer")
    if length > 4:
        return lax.all_gather(shard, "outer")
    full = jnp.zeros((length,) + shard.shape, shard.dtype)
    for by in range(length):
        piece = outer_shift(shard, by) if by else shard
        full = lax.dynamic_update_slice_in_dim(full, piece[None], (here - by) % length, 0)
    return full


def outer_scatter(parts):
    length, here = lax.axis_size("outer"), lax.axis_index("outer")
    if length > 4:
        return lax.psum_scatter(parts, "outer", scatter_dimension=0, tiled=False).astype(F32)
    pieces = [
        lax.dynamic_index_in_dim(parts, (here + by) % length, 0, keepdims=False)
        for by in range(length)
    ]
    return wide_sum([pieces[0]] + [outer_shift(pieces[by], by) for by in range(1, length)])


def core_columns(rows, core_at, shard_rows):
    count = rows.shape[0]
    split = rows.reshape(count, -1, 2, shard_rows)
    return lax.dynamic_index_in_dim(split, core_at, 2, keepdims=False).reshape(count, -1)


def fold_columns(left, right, shard_rows):
    core = lax.axis_index("core")
    sent = dot(core_columns(left, 1 - core, shard_rows), right, ((0,), (0,))).astype(BF16)
    kept = dot(core_columns(left, core, shard_rows), right, ((0,), (0,))).astype(BF16)
    return fold_core(kept, sent).reshape(-1, 2, shard_rows, right.shape[1])


def distance_blocks(total):
    x, tensor = lax.axis_index("x"), lax.axis_index("tensor")
    columns = total.shape[3] // 2
    blocks = []
    for x_by in range(2):
        for tensor_by in range(2):
            block = lax.dynamic_index_in_dim(total, x ^ x_by, 1, keepdims=False)
            start = (tensor ^ tensor_by) * columns
            blocks.append(lax.dynamic_slice_in_dim(block, start, columns, 2))
    return blocks


def rotary_tables(position):
    halfway = HEAD_SIZE // 2
    inverse = jnp.exp(
        jnp.arange(halfway, dtype=F32) * (-2.0 * math.log(ROPE_BASE) / HEAD_SIZE)
    )
    angles = position.astype(F32)[:, None] * inverse[None, :]
    cosine, sine = jnp.cos(angles), jnp.sin(angles)
    return (
        jnp.concatenate([cosine, cosine], axis=1),
        jnp.concatenate([-sine, sine], axis=1),
    )


def norm_factor(value_rows):
    return lax.rsqrt(jnp.mean(value_rows * value_rows, axis=-1, keepdims=True) + EPSILON)


def norm_back(value_rows, factor, gain, upstream):
    weighted = upstream * gain
    return factor * weighted - value_rows * (factor * factor * factor) * jnp.mean(
        weighted * value_rows, axis=-1, keepdims=True
    )


def dot(a, b, dims):
    return lax.dot_general(a, b, (dims, ((), ())), preferred_element_type=F32)


VMEM_LIMIT = 60 * 1024 * 1024
LIGHT = pl.CostEstimate(flops=1000, bytes_accessed=1000, transcendentals=0)
FROM_LAST = (((1,), (1,)), ((), ()))
PLAIN = (((1,), (0,)), ((), ()))


def mxu(a, b, dims=PLAIN):
    return lax.dot_general(a, b, dims, preferred_element_type=F32)


def turn(rows, cosine, sine):
    return rows * cosine + pltpu.roll(rows, HEAD_SIZE // 2, 1) * sine


def project_kernel(rows_ref, weight_ref, cosine_ref, sine_ref, out_ref, *, turned):
    product = mxu(rows_ref[...], weight_ref[...])
    for at, turns in enumerate(turned):
        part = product[:, at * HEAD_SIZE : (at + 1) * HEAD_SIZE]
        if turns:
            part = turn(part, cosine_ref[...], sine_ref[...])
        out_ref[:, at * HEAD_SIZE : (at + 1) * HEAD_SIZE] = part.astype(BF16)


def project(rows, weight, cosine, sine, first, count, turned):
    high, width = rows.shape
    columns = len(turned) * HEAD_SIZE
    return pl.pallas_call(
        functools.partial(project_kernel, turned=turned),
        grid=(count,),
        in_specs=[
            pl.BlockSpec((high, width), lambda j: (0, 0)),
            pl.BlockSpec((width, columns), lambda j: (0, first + j)),
            pl.BlockSpec((high, HEAD_SIZE), lambda j: (0, 0)),
            pl.BlockSpec((high, HEAD_SIZE), lambda j: (0, 0)),
        ],
        out_specs=pl.BlockSpec((high, columns), lambda j: (0, j)),
        out_shape=jax.ShapeDtypeStruct((high, count * columns), BF16),
        compiler_params=pltpu.CompilerParams(vmem_limit_bytes=VMEM_LIMIT),
        cost_estimate=LIGHT,
        name="project",
    )(rows, weight, cosine, sine)


def mask_bias(place_ref, segment_key_ref, segment_query_ref, bias_ref, seq_len):
    span, rows = bias_ref.shape
    start = place_ref[0]
    key_at = lax.broadcasted_iota(jnp.int32, (span, rows), 0)
    query_at = lax.broadcasted_iota(jnp.int32, (span, rows), 1) + ATTEND_SPAN
    distance = query_at - key_at
    position = start + query_at - ATTEND_SPAN
    sequence_at = query_at - lax.rem(position, seq_len)
    allowed = (distance >= 0) & (distance < ATTEND_SPAN) & (key_at >= sequence_at)
    allowed = allowed & (segment_key_ref[...] == segment_query_ref[...])
    bias_ref[...] = jnp.where(allowed, 0.0, -1e30)


def attention_kernel(
    place_ref,
    segment_key_ref,
    segment_query_ref,
    q_ref,
    kv_ref,
    heads_ref,
    lse_ref,
    bias_ref,
    *,
    seq_len,
    scale,
):
    @pl.when(pl.program_id(0) == 0)
    def _():
        mask_bias(place_ref, segment_key_ref, segment_query_ref, bias_ref, seq_len)

    rows = q_ref.shape[0]
    span = kv_ref.shape[0]
    count = q_ref.shape[1] // HEAD_SIZE
    value_t = kv_ref[:, HEAD_SIZE:].T
    chunks = span // rows
    for head in range(count):
        columns = slice(head * HEAD_SIZE, (head + 1) * HEAD_SIZE)
        query = q_ref[:, columns]
        scores = []
        for c in range(chunks):
            part = slice(c * rows, (c + 1) * rows)
            raw = mxu(kv_ref[part, :HEAD_SIZE], query, FROM_LAST)
            scores.append(raw * scale + bias_ref[part, :])
        top = functools.reduce(jnp.maximum, scores)
        top = jnp.max(top, axis=0, keepdims=True)
        total = jnp.zeros_like(top)
        out_t = jnp.zeros((HEAD_SIZE, rows), F32)
        for c in range(chunks):
            weight = jnp.exp(scores[c] - top)
            total = total + jnp.sum(weight, axis=0, keepdims=True)
            out_t = out_t + mxu(value_t[:, c * rows : (c + 1) * rows], weight.astype(BF16))
        heads_ref[:, columns] = (out_t / total).T.astype(BF16)
        lse_ref[0, head : head + 1, :] = top + jnp.log(total)


def attention(place, segment_key, segment_query, queries, key_value, seq_len):
    rows, all_columns = queries.shape
    span = key_value.shape[0]
    pairs = key_value.shape[1] // (2 * HEAD_SIZE)
    columns = all_columns // pairs
    return pl.pallas_call(
        functools.partial(attention_kernel, seq_len=seq_len, scale=1.0 / math.sqrt(HEAD_SIZE)),
        grid=(pairs,),
        in_specs=[
            pl.BlockSpec(memory_space=pltpu.SMEM),
            pl.BlockSpec((span, 1), lambda j: (0, 0)),
            pl.BlockSpec((1, rows), lambda j: (0, 0)),
            pl.BlockSpec((rows, columns), lambda j: (0, j)),
            pl.BlockSpec((span, 2 * HEAD_SIZE), lambda j: (0, j)),
        ],
        out_specs=[
            pl.BlockSpec((rows, columns), lambda j: (0, j)),
            pl.BlockSpec((1, columns // HEAD_SIZE, rows), lambda j: (j, 0, 0)),
        ],
        out_shape=[
            jax.ShapeDtypeStruct((rows, all_columns), BF16),
            jax.ShapeDtypeStruct((pairs, columns // HEAD_SIZE, rows), F32),
        ],
        scratch_shapes=[pltpu.VMEM((span, rows), F32)],
        compiler_params=pltpu.CompilerParams(vmem_limit_bytes=VMEM_LIMIT),
        cost_estimate=LIGHT,
        name="attention",
    )(place, segment_key, segment_query, queries, key_value)


def attention_back_kernel(
    place_ref,
    segment_key_ref,
    segment_query_ref,
    q_ref,
    kv_ref,
    lse_ref,
    dout_ref,
    cosine_ref,
    sine_ref,
    dq_ref,
    dkv_far_ref,
    dkv_own_ref,
    bias_ref,
    dkv_ref,
    *,
    seq_len,
    scale,
):
    @pl.when(pl.program_id(0) == 0)
    def _():
        mask_bias(place_ref, segment_key_ref, segment_query_ref, bias_ref, seq_len)

    rows = q_ref.shape[0]
    span = kv_ref.shape[0]
    count = q_ref.shape[1] // HEAD_SIZE
    key_t = kv_ref[:, :HEAD_SIZE].T
    chunks = span // rows
    dkv_ref[...] = jnp.zeros_like(dkv_ref)
    for head in range(count):
        columns = slice(head * HEAD_SIZE, (head + 1) * HEAD_SIZE)
        query = q_ref[:, columns]
        dout = dout_ref[:, columns]
        lse = lse_ref[0, head : head + 1, :]
        probs, dprobs = [], []
        row_dot = jnp.zeros_like(lse)
        for c in range(chunks):
            part = slice(c * rows, (c + 1) * rows)
            raw = mxu(kv_ref[part, :HEAD_SIZE], query, FROM_LAST)
            prob = jnp.exp(raw * scale + bias_ref[part, :] - lse)
            dprob = mxu(kv_ref[part, HEAD_SIZE:], dout, FROM_LAST)
            row_dot = row_dot + jnp.sum(prob * dprob, axis=0, keepdims=True)
            probs.append(prob)
            dprobs.append(dprob)
        dq_t = jnp.zeros((HEAD_SIZE, rows), F32)
        for c in range(chunks):
            part = slice(c * rows, (c + 1) * rows)
            dscore = (probs[c] * (dprobs[c] - row_dot)).astype(BF16)
            dkv_ref[part, :HEAD_SIZE] += mxu(dscore, query)
            dkv_ref[part, HEAD_SIZE:] += mxu(probs[c].astype(BF16), dout)
            dq_t = dq_t + mxu(key_t[:, part], dscore)
        dq_ref[:, columns] = turn(dq_t.T * scale, cosine_ref[...], -sine_ref[...]).astype(BF16)
    dkv_ref[:, :HEAD_SIZE] = dkv_ref[:, :HEAD_SIZE] * scale
    dkv_far_ref[...] = dkv_ref[: span - rows, :].astype(BF16)
    dkv_own_ref[...] = dkv_ref[span - rows :, :]


def attention_back(
    place, segment_key, segment_query, queries, key_value, lse, dout, cosine, sine, seq_len
):
    rows, all_columns = queries.shape
    span = key_value.shape[0]
    pairs = key_value.shape[1] // (2 * HEAD_SIZE)
    columns = all_columns // pairs
    return pl.pallas_call(
        functools.partial(
            attention_back_kernel, seq_len=seq_len, scale=1.0 / math.sqrt(HEAD_SIZE)
        ),
        grid=(pairs,),
        in_specs=[
            pl.BlockSpec(memory_space=pltpu.SMEM),
            pl.BlockSpec((span, 1), lambda j: (0, 0)),
            pl.BlockSpec((1, rows), lambda j: (0, 0)),
            pl.BlockSpec((rows, columns), lambda j: (0, j)),
            pl.BlockSpec((span, 2 * HEAD_SIZE), lambda j: (0, j)),
            pl.BlockSpec((1, columns // HEAD_SIZE, rows), lambda j: (j, 0, 0)),
            pl.BlockSpec((rows, columns), lambda j: (0, j)),
            pl.BlockSpec((rows, HEAD_SIZE), lambda j: (0, 0)),
            pl.BlockSpec((rows, HEAD_SIZE), lambda j: (0, 0)),
        ],
        out_specs=[
            pl.BlockSpec((rows, columns), lambda j: (0, j)),
            pl.BlockSpec((span - rows, 2 * HEAD_SIZE), lambda j: (0, j)),
            pl.BlockSpec((rows, 2 * HEAD_SIZE), lambda j: (0, j)),
        ],
        out_shape=[
            jax.ShapeDtypeStruct((rows, all_columns), BF16),
            jax.ShapeDtypeStruct((span - rows, key_value.shape[1]), BF16),
            jax.ShapeDtypeStruct((rows, key_value.shape[1]), F32),
        ],
        scratch_shapes=[
            pltpu.VMEM((span, rows), F32),
            pltpu.VMEM((span, 2 * HEAD_SIZE), F32),
        ],
        compiler_params=pltpu.CompilerParams(vmem_limit_bytes=VMEM_LIMIT),
        cost_estimate=pl.CostEstimate(
            flops=70_000_000_000, bytes_accessed=10_000_000, transcendentals=0
        ),
        name="attention_back",
    )(place, segment_key, segment_query, queries, key_value, lse, dout, cosine, sine)


def expert_kernel(
    slot_row_ref,
    slot_column_ref,
    routed_ref,
    own_ref,
    router_ref,
    tokens_ref,
    cotangent_ref,
    gate_ref,
    up_ref,
    down_ref,
    grad_ref,
    moe_ref,
    rows_in_ref,
    grad_out_ref,
    hidden_ref,
    grad_gate_ref,
    grad_up_ref,
    router_grad_ref,
    gate_full_ref,
    up_full_ref,
    down_full_ref,
    *,
    capacity,
):
    whole = ((gate_ref, gate_full_ref), (up_ref, up_full_ref), (down_ref, down_full_ref))

    @pl.when(pl.program_id(0) == 0)
    def _():
        for held, full in whole:
            columns = held.shape[3]
            for half in range(held.shape[1]):
                full[:, half * columns : (half + 1) * columns] = held[:, half].reshape(-1, columns)

    group_rows = tokens_ref.shape[1]
    tokens = tokens_ref[0]
    gate_weight, up_weight, down_weight = (full[...] for _, full in whole)
    cotangent = cotangent_ref[0]
    routed = routed_ref[0] > 0.0
    logits = jnp.where(routed, mxu(router_ref[...], tokens, FROM_LAST), -1e30)
    weights = jnp.exp(logits - jnp.max(logits, axis=0, keepdims=True))
    weights = jnp.where(routed, weights, 0.0)
    gates = weights / jnp.sum(weights, axis=0, keepdims=True)
    own = own_ref[...]
    gate_own = jnp.sum(gates * own, axis=0, keepdims=True)
    place = slot_row_ref[0] == lax.broadcasted_iota(jnp.int32, (capacity, group_rows), 0)
    place_wide = jnp.where(place, 1.0, 0.0)
    place_low = place_wide.astype(BF16)
    back = slot_column_ref[0] == lax.broadcasted_iota(jnp.int32, (group_rows, capacity), 1)
    back_low = jnp.where(back, 1.0, 0.0).astype(BF16)
    coefficient = jnp.sum(place_wide * gate_own, axis=1, keepdims=True)

    rows_in = mxu(place_low, tokens).astype(BF16)
    rows_in_ref[...] = rows_in
    gate_pre = mxu(rows_in, gate_weight)
    up_pre = mxu(rows_in, up_weight)
    sigmoid = 1.0 / (1.0 + jnp.exp(-gate_pre))
    silu = gate_pre * sigmoid
    hidden = (silu * up_pre).astype(BF16)
    hidden_ref[...] = hidden
    slot_cotangent = mxu(place_low, cotangent)
    grad_out = (coefficient * slot_cotangent).astype(BF16)
    grad_out_ref[...] = grad_out
    grad_hidden = mxu(grad_out, down_weight)
    grad_up = (grad_hidden * silu).astype(BF16)
    grad_gate = (grad_hidden * up_pre * sigmoid * (1.0 + gate_pre * (1.0 - sigmoid))).astype(BF16)
    grad_up_ref[...] = grad_up
    grad_gate_ref[...] = grad_gate
    expert_out = mxu(hidden, down_weight, FROM_LAST)
    grad_slot = jnp.sum(slot_cotangent * expert_out, axis=1, keepdims=True)
    moe_ref[0] = mxu(back_low, (coefficient * expert_out).astype(BF16)).astype(BF16)

    grad_token = jnp.sum(place_wide * grad_slot, axis=0, keepdims=True)
    share = (grad_token * gate_own) * (own - gates)
    share_high = share.astype(BF16)
    share_low = (share - share_high.astype(F32)).astype(BF16)
    router_grad = mxu(share_high, tokens) + mxu(share_low, tokens)

    @pl.when(pl.program_id(0) == 0)
    def _():
        router_grad_ref[...] = router_grad

    @pl.when(pl.program_id(0) > 0)
    def _():
        router_grad_ref[...] += router_grad

    grad_in = mxu(grad_gate, gate_weight, FROM_LAST) + mxu(grad_up, up_weight, FROM_LAST)
    grad_ref[0] = (
        mxu(back_low, grad_in.astype(BF16)) + mxu(share.T.astype(BF16), router_ref[...])
    ).astype(BF16)


def expert_groups(slot, routed, own, router_t, tokens, cotangent, weights, capacity):
    count, group_rows, width = tokens.shape
    ff = weights[0].shape[1] * weights[0].shape[3]
    experts = router_t.shape[0]
    weight = pl.BlockSpec(
        weights[0].shape, lambda g: (0, 0, 0, 0), pipeline_mode=pl.Buffered(1)
    )
    whole = lambda g: (0, 0)
    by_group = lambda g: (g, 0, 0)
    slots = lambda columns: pl.BlockSpec((capacity, columns), lambda g: (g, 0))
    slots_shape = lambda columns: jax.ShapeDtypeStruct((count * capacity, columns), BF16)
    return pl.pallas_call(
        functools.partial(expert_kernel, capacity=capacity),
        grid=(count,),
        in_specs=[
            pl.BlockSpec((1, 1, group_rows), by_group),
            pl.BlockSpec((1, group_rows, 1), by_group),
            pl.BlockSpec((1, experts, group_rows), by_group),
            pl.BlockSpec((experts, 1), whole),
            pl.BlockSpec((experts, width), whole),
            pl.BlockSpec((1, group_rows, width), by_group),
            pl.BlockSpec((1, group_rows, width), by_group),
            weight,
            weight,
            weight,
        ],
        out_specs=[
            pl.BlockSpec((1, group_rows, width), by_group),
            pl.BlockSpec((1, group_rows, width), by_group),
            slots(width),
            slots(width),
            slots(ff),
            slots(ff),
            slots(ff),
            pl.BlockSpec((experts, width), whole),
        ],
        out_shape=[
            jax.ShapeDtypeStruct(tokens.shape, BF16),
            jax.ShapeDtypeStruct(tokens.shape, BF16),
            slots_shape(width),
            slots_shape(width),
            slots_shape(ff),
            slots_shape(ff),
            slots_shape(ff),
            jax.ShapeDtypeStruct((experts, width), F32),
        ],
        scratch_shapes=[pltpu.VMEM((width, ff), BF16) for _ in range(3)],
        compiler_params=pltpu.CompilerParams(vmem_limit_bytes=VMEM_LIMIT),
        cost_estimate=LIGHT,
        name="expert",
    )(
        slot[:, None, :],
        slot[:, :, None],
        routed,
        own,
        router_t,
        tokens,
        cotangent,
        *weights,
    )


def weight_grad_kernel(*refs, halves):
    rows, grad_out, hidden, grad_gate, grad_up, router = (
        refs[at : at + 2] for at in range(0, 12, 2)
    )
    moe_kept_ref, moe_got_ref, out_ref = refs[12:15]
    for at, moe_ref in enumerate(refs[15:]):
        moe_ref[...] = (moe_kept_ref[at].astype(F32) + moe_got_ref[at].astype(F32)).astype(BF16)
    columns = hidden[0].shape[1] // halves
    over = (((0,), (0,)), ((), ()))
    left_rows = [ref[...] for ref in rows]
    left_out = [ref[...] for ref in grad_out]
    router_columns = (router[0][...] + router[1][...]).T
    router_columns = jnp.concatenate(
        [
            router_columns,
            jnp.zeros((router_columns.shape[0], HEAD_SIZE - router_columns.shape[1]), F32),
        ],
        axis=1,
    ).astype(BF16)
    for half in range(halves):
        start = half * (3 * columns + HEAD_SIZE)
        part = slice(half * columns, (half + 1) * columns)
        for at, (left, right) in enumerate(
            ((left_rows, grad_gate), (left_rows, grad_up), (left_out, hidden))
        ):
            total = mxu(left[0], right[0][:, part], over) + mxu(left[1], right[1][:, part], over)
            out_ref[:, start + at * columns : start + (at + 1) * columns] = total.astype(BF16)
        out_ref[:, start + 3 * columns : start + 3 * columns + HEAD_SIZE] = router_columns


def weight_grads(near, far, moe_kept, moe_got, halves, block=256):
    rows_at, grad_out_at, hidden_at, grad_gate_at, grad_up_at, router_at = range(6)
    slots, width = near[rows_at].shape
    ff = near[hidden_at].shape[1]
    experts = near[router_at].shape[0]
    specs, operands = [], []
    for at in (rows_at, grad_out_at, hidden_at, grad_gate_at, grad_up_at, router_at):
        if at in (rows_at, grad_out_at):
            spec = pl.BlockSpec((slots, block), lambda i: (0, i))
        elif at == router_at:
            spec = pl.BlockSpec((experts, block), lambda i: (0, i))
        else:
            spec = pl.BlockSpec((slots, ff), lambda i: (0, 0))
        specs += [spec, spec]
        operands += [near[at], far[at]]
    columns = 3 * ff + halves * HEAD_SIZE
    moe_count, moe_rows, _ = moe_kept.shape
    moe_spec = pl.BlockSpec((moe_count, moe_rows, block), lambda i: (0, 0, i))
    moe_out_spec = pl.BlockSpec((moe_rows, block), lambda i: (0, i))
    return pl.pallas_call(
        functools.partial(weight_grad_kernel, halves=halves),
        grid=(width // block,),
        in_specs=specs + [moe_spec, moe_spec],
        out_specs=[pl.BlockSpec((block, columns), lambda i: (i, 0))] + [moe_out_spec] * moe_count,
        out_shape=[jax.ShapeDtypeStruct((width, columns), BF16)]
        + [jax.ShapeDtypeStruct((moe_rows, width), BF16)] * moe_count,
        compiler_params=pltpu.CompilerParams(vmem_limit_bytes=VMEM_LIMIT),
        cost_estimate=pl.CostEstimate(
            flops=15_000_000_000, bytes_accessed=50_000_000, transcendentals=0
        ),
        name="weight_grads",
    )(*operands, moe_kept, moe_got)


def on_device(
    block_input,
    norm_gains,
    router_weight,
    query_matrix,
    key_matrix,
    value_matrix,
    output_weight,
    gate_weight,
    up_weight,
    down_weight,
    segment_ids,
    routes,
    priority,
    cotangent,
):
    tensor_index = lax.axis_index("tensor")
    own_rows, width = block_input.shape
    group_rows = segment_ids.shape[0]
    halves = lax.axis_size("tensor")
    outer = lax.axis_size("outer")
    groups = lax.axis_size("x") * lax.axis_size("core")
    plane = groups * halves
    shard_rows = query_matrix.shape[0]
    dp_size = outer * groups
    seq_len = min(SEQ_MOST, group_rows * dp_size)
    own_start = lax.axis_index(ALL) * own_rows
    capacity = group_rows * TOPK // EXPERTS
    reach = ATTEND_SPAN // own_rows
    half_ff = gate_weight.shape[2]
    ff = half_ff * halves

    query_columns = query_matrix.shape[1]
    pair_columns = 2 * halves * HEAD_SIZE
    first = tensor_index == 0
    key_value_weight = jnp.concatenate([key_matrix, value_matrix], axis=1)
    other_weight = swap(key_value_weight, "tensor")
    early = jnp.concatenate(
        [
            jnp.where(first, key_value_weight, other_weight),
            jnp.where(first, other_weight, key_value_weight),
            query_matrix,
            output_weight,
        ],
        axis=1,
    )
    early, gate_own, up_own, down_own, cotangent_own = lax.optimization_barrier(
        (early, gate_weight, up_weight, down_weight, cotangent)
    )
    early = outer_gather(early)

    expert_shard = jnp.transpose(jnp.stack([gate_own, up_own, down_own]), (2, 0, 1, 3))
    expert_shard = lax.all_to_all(expert_shard, PLANE, 0, 0, tiled=True)
    expert_shard = expert_shard.reshape(groups, halves, 3, shard_rows, half_ff)
    expert_shard = [
        jnp.swapaxes(expert_shard[:, :, at], 0, 1).reshape(-1, half_ff) for at in range(3)
    ]
    early, expert_shard, segment_here, priority_here = lax.optimization_barrier(
        (early, expert_shard, segment_ids, priority)
    )
    pair_count = group_rows * TOPK
    rank = (
        jnp.zeros((pair_count,), jnp.int32)
        .at[priority_here]
        .set(jnp.arange(pair_count, dtype=jnp.int32))
        .reshape(group_rows, TOPK)
    )
    expert_ids = jnp.arange(EXPERTS, dtype=jnp.int32)
    named = routes[:, :, None] == expert_ids[None, None, :]
    ranked = jnp.sum(jnp.where(named, rank[:, :, None] + 1, 0), axis=1)
    ranked = jnp.where(ranked > 0, ranked, pair_count + 1)
    ranked_own = lax.dynamic_slice_in_dim(ranked, tensor_index * own_rows, own_rows, 0)
    digits = jnp.concatenate([ranked_own // 64, ranked_own % 64], axis=1).astype(BF16)
    digits = jnp.pad(digits, ((0, 0), (0, HEAD_SIZE - digits.shape[1])))
    cotangent_sent = jnp.concatenate([cotangent_own, digits], axis=1)
    segment_near = jnp.concatenate(
        [shift_groups(segment_here, 2), shift_groups(segment_here, 1), segment_here]
    )
    expert_full = [
        lax.all_gather(shard, "outer").reshape(outer, halves, groups * shard_rows, half_ff)
        for shard in expert_shard
    ]

    key_value_full = early[:, :, :pair_columns]
    key_value_full = in_order(key_value_full, swap(key_value_full, "x"), "x", 1)
    key_value_full = in_order(key_value_full, swap(key_value_full, "core"), "core", 2)
    key_value_full = key_value_full.reshape(width, pair_columns)
    query_parts = plane_parts(early[:, :, pair_columns : pair_columns + query_columns])

    input_wide = block_input.astype(F32)
    first_gain = norm_gains[:, 0]
    second_gain = norm_gains[:, 1]
    first_factor = norm_factor(input_wide)
    normed_in = (input_wide * first_factor * first_gain).astype(BF16)
    positions = own_start + jnp.arange(own_rows, dtype=jnp.int32)
    cosine, sine = rotary_tables(positions % seq_len)
    query_blocks = halves * query_columns // (2 * HEAD_SIZE)
    key_value_sent = project(
        normed_in, key_value_full, cosine, sine, 0, halves, (True, False)
    )
    one_back, two_back = shift_groups(key_value_sent, 1), shift_groups(key_value_sent, 2)
    query_parts, one_back, two_back, segment_near, cotangent_sent = lax.optimization_barrier(
        (query_parts, one_back, two_back, segment_near, cotangent_sent)
    )
    cotangent_parts = plane_parts(cotangent_sent)
    output_own = early[:, :, pair_columns + query_columns :]
    pair_sent = jnp.where(
        first,
        jnp.stack([one_back, key_value_sent]),
        jnp.stack([two_back, one_back]),
    )
    pair_got = swap(pair_sent, "tensor")
    query_near = plane_stack(query_parts)
    query_far, pair_got, expert_full[0] = lax.optimization_barrier(
        (swap(query_near, "core"), pair_got, expert_full[0])
    )
    pieces = [two_back, pair_got[0], one_back, pair_got[1], key_value_sent]
    query_full = whole_weight(query_near, query_far)
    queries = project(normed_in, query_full, cosine, sine, 0, query_blocks, (True, True))
    output_parts = plane_parts(output_own)
    expert = lax.axis_index(PLANE)

    def slots_of(cotangents):
        digits = cotangents[..., width:].reshape(2, group_rows, HEAD_SIZE).astype(jnp.int32)
        ranked_all = digits[..., :EXPERTS] * 64 + digits[..., EXPERTS : 2 * EXPERTS]
        routed = jnp.swapaxes((ranked_all <= pair_count).astype(F32), 1, 2)
        rank_own = jnp.sum(jnp.where(expert_ids == expert, ranked_all, 0), axis=-1)
        earlier = (rank_own[:, None, :] < rank_own[:, :, None]).astype(jnp.int32)
        slot = jnp.where(rank_own <= pair_count, jnp.sum(earlier, axis=-1), capacity)
        return slot, routed

    key_value = jnp.concatenate(pieces, axis=0)
    span = ATTEND_SPAN + own_rows
    segment_ext = lax.dynamic_slice_in_dim(segment_near, tensor_index * own_rows, span)
    view = (
        jnp.reshape(own_start, (1,)),
        segment_ext[:, None],
        segment_ext[None, ATTEND_SPAN:],
        queries,
        key_value,
    )
    heads_low, log_total = attention(*view, seq_len)
    heads_late, output_parts, cotangent_parts = lax.optimization_barrier(
        (heads_low, output_parts, cotangent_parts)
    )
    output_near = plane_stack(output_parts)
    output_far = swap(output_near, "core")
    output_full, expert_full[1] = lax.optimization_barrier(
        (whole_weight(output_near, output_far), expert_full[1])
    )
    hidden_state = input_wide + dot(heads_low, output_full, ((1,), (1,)))
    second_factor = norm_factor(hidden_state)
    normed_mid_own = (hidden_state * second_factor * second_gain).astype(BF16)

    cotangent_near = plane_stack(cotangent_parts)
    cotangent_far = swap(cotangent_near, "core")
    near_slots, far_slots = slots_of(cotangent_near), slots_of(cotangent_far)
    normed_parts, near_slots, far_slots, expert_full[2] = lax.optimization_barrier(
        (plane_parts(normed_mid_own), near_slots, far_slots, expert_full[2])
    )
    normed_near = plane_stack(normed_parts)
    normed_far = swap(normed_near, "core")
    own_expert = (expert_ids == expert).astype(F32)[:, None]
    router_t = router_weight.T

    def experts_on(tokens, cotangents, slots):
        slot, routed = slots
        return expert_groups(
            slot,
            routed,
            own_expert,
            router_t,
            tokens.reshape(2, group_rows, width),
            cotangents.reshape(2, group_rows, -1),
            expert_full,
            capacity,
        )

    on_near = experts_on(normed_near, cotangent_near, near_slots)
    on_far = experts_on(normed_far, cotangent_far, far_slots)
    blocks = (2 * halves, own_rows, width)
    (grad_near, moe_near), (grad_far, moe_far) = (
        [array.reshape(blocks) for array in side[:2]] for side in (on_near, on_far)
    )
    grad_blocks = fold_blocks(grad_near, swap(grad_far, "core"))
    grad_blocks, moe_far, on_near, on_far = lax.optimization_barrier(
        (grad_blocks, moe_far, on_near[2:], on_far[2:])
    )
    grad_mid_parts = fold_plane(grad_blocks)
    expert_part, *moe_blocks = weight_grads(
        on_near, on_far, moe_near, swap(moe_far, "core"), halves
    )
    expert_sum = lax.psum_scatter(expert_part, "outer", scatter_dimension=0, tiled=True)
    grad_mid_parts, moe_blocks = lax.optimization_barrier((grad_mid_parts, moe_blocks))
    moe_parts = fold_plane(moe_blocks)
    grad_mid = wide_sum(grad_mid_parts)

    norm_input_part = norm_back(hidden_state, second_factor, second_gain, grad_mid)
    grad_state = cotangent.astype(F32) + norm_input_part
    grad_attn = grad_state.astype(BF16)
    grad_heads = dot(grad_attn, output_full, ((1,), (0,))).astype(BF16)
    output_total = fold_columns(grad_attn, heads_late, shard_rows)
    grad_query_pre, grad_far_kv, grad_own = attention_back(
        *view, log_total, grad_heads, cosine, sine, seq_len
    )
    grad_query_pre, output_total, moe_parts = lax.optimization_barrier(
        (grad_query_pre, output_total, moe_parts)
    )
    output_parts = fold_plane(distance_blocks(output_total))
    query_total = fold_columns(normed_in, grad_query_pre, shard_rows)
    two_back, pair_old, one_back, pair_new = grad_far_kv.reshape(reach, own_rows, -1)
    pair_got, output_parts, query_total = lax.optimization_barrier(
        (swap(jnp.stack([pair_old, pair_new]), "tensor"), output_parts, query_total)
    )
    query_parts = fold_plane(distance_blocks(query_total))
    output_weight_grad = outer_scatter(wide_sum(output_parts).astype(BF16))
    pair_old, pair_new = pair_got.astype(F32)
    one_back = one_back.astype(F32) + jnp.where(first, pair_old, pair_new)
    two_back = two_back.astype(F32) + jnp.where(first, 0.0, pair_old)
    grad_own = grad_own + jnp.where(first, pair_new, 0.0)
    grad_own = grad_own + shift_groups(one_back.astype(BF16), -1).astype(F32)
    grad_own = grad_own + shift_groups(two_back.astype(BF16), -2).astype(F32)
    grad_own, query_parts, expert_sum = lax.optimization_barrier(
        (grad_own, query_parts, expert_sum)
    )
    grad_key_value = []
    for half in range(halves):
        start = half * 2 * HEAD_SIZE
        key_part = grad_own[:, start : start + HEAD_SIZE]
        turned = jnp.concatenate(
            [key_part[:, HEAD_SIZE // 2 :], key_part[:, : HEAD_SIZE // 2]], axis=1
        )
        grad_key_value.append(key_part * cosine - turned * sine)
        grad_key_value.append(grad_own[:, start + HEAD_SIZE : start + 2 * HEAD_SIZE])
    grad_key_value_pre = jnp.concatenate(grad_key_value, axis=1).astype(BF16)
    key_value_total = fold_columns(normed_in, grad_key_value_pre, shard_rows)
    key_value_parts = fold_plane(distance_blocks(key_value_total))
    grad_in = dot(grad_query_pre, query_full, ((1,), (1,))) + dot(
        grad_key_value_pre, key_value_full, ((1,), (1,))
    )
    input_grad = grad_state + norm_back(input_wide, first_factor, first_gain, grad_in)
    qkv_grad = outer_scatter(
        jnp.concatenate([wide_sum(query_parts), wide_sum(key_value_parts)], axis=2).astype(BF16)
    )
    block_output = hidden_state + wide_sum(moe_parts)
    expert_sum = expert_sum.reshape(groups, shard_rows, halves, -1)
    expert_sum = jnp.swapaxes(expert_sum, 1, 2).reshape(plane, shard_rows, -1)
    expert_sum = lax.all_to_all(expert_sum, PLANE, 0, 0, tiled=True)
    gate_grad, up_grad, down_grad = (
        jnp.swapaxes(expert_sum[:, :, at * half_ff : (at + 1) * half_ff], 0, 1).astype(F32)
        for at in range(3)
    )
    router_grad = jnp.sum(expert_sum[:, :, 3 * half_ff : 3 * half_ff + EXPERTS].astype(F32), axis=0)
    router_grad = lax.dynamic_slice_in_dim(
        router_grad, tensor_index * (shard_rows // 2), shard_rows // 2, 0
    )
    query_grad = qkv_grad[:, :query_columns]
    key_grad = qkv_grad[:, query_columns : query_columns + HEAD_SIZE]
    value_grad = qkv_grad[:, query_columns + HEAD_SIZE :]

    half_rows = shard_rows // 2
    own_gains = lax.dynamic_slice_in_dim(
        norm_gains, lax.axis_index(DP) * shard_rows, shard_rows, 0
    )
    qkv_own = jnp.concatenate([query_matrix, key_value_weight], axis=1)
    first_sum = jnp.sum(qkv_grad * qkv_own.astype(F32), axis=-1)
    second_sum = jnp.sum(
        gate_grad * gate_weight.astype(F32) + up_grad * up_weight.astype(F32), axis=(1, 2)
    )
    gain_sums = jnp.stack([first_sum, second_sum], axis=1) / own_gains
    kept = lax.dynamic_slice_in_dim(gain_sums, tensor_index * half_rows, half_rows, 0)
    sent = lax.dynamic_slice_in_dim(gain_sums, (1 - tensor_index) * half_rows, half_rows, 0)
    own_router = lax.dynamic_slice_in_dim(
        router_weight, lax.axis_index(ALL) * half_rows, half_rows, 0
    )
    router_sum = jnp.sum(router_grad * own_router.astype(F32), axis=-1)
    half_gains = lax.dynamic_slice_in_dim(own_gains, tensor_index * half_rows, half_rows, 0)
    router_sum = router_sum / half_gains[:, 1]
    gains_grad = (
        kept
        + swap(sent, "tensor")
        + jnp.stack([jnp.zeros_like(router_sum), router_sum], axis=1)
    )
    return (
        block_output,
        input_grad,
        gains_grad,
        router_grad,
        query_grad,
        key_grad,
        value_grad,
        output_weight_grad,
        gate_grad,
        up_grad,
        down_grad,
    )


def solution(mesh):
    dp_size, tensor_size = mesh.shape["dp"], mesh.shape["tensor"]
    split = Mesh(mesh.devices.reshape(dp_size // 4, 2, 2, tensor_size), ALL)
    return jax.shard_map(
        on_device,
        mesh=split,
        in_specs=(
            P(ALL, None),
            P(),
            P(),
            P(DP, "tensor"),
            P(DP, "tensor"),
            P(DP, "tensor"),
            P(DP, "tensor"),
            P(DP, None, "tensor"),
            P(DP, None, "tensor"),
            P(DP, None, "tensor"),
            P(DP),
            P(DP, None),
            P(DP),
            P(ALL, None),
        ),
        out_specs=(
            P(ALL, None),
            P(ALL, None),
            P(ALL, None),
            P(ALL, None),
            P(DP, "tensor"),
            P(DP, "tensor"),
            P(DP, "tensor"),
            P(DP, "tensor"),
            P(DP, None, "tensor"),
            P(DP, None, "tensor"),
            P(DP, None, "tensor"),
        ),
        check_vma=False,
    )
```

```python
import functools
import math

import jax
import jax.numpy as jnp
from jax import lax
from jax.experimental import pallas as pl
from jax.experimental.pallas import tpu as pltpu
from jax.sharding import Mesh
from jax.sharding import PartitionSpec as P

HEAD_SIZE = 128
TOPK = 4
EXPERTS = 8
ATTEND_SPAN = 1024
SEQ_MOST = 16384
EPSILON = 1e-06
ROPE_BASE = 10000.0
BF16 = jnp.bfloat16
F32 = jnp.float32

DP = ("outer", "x", "core")
PLANE = ("x", "core", "tensor")
ALL = ("outer", "x", "core", "tensor")


def shift_groups(x, by):
    length = lax.axis_size(DP)
    return lax.ppermute(x, DP, [(i, i + by) for i in range(length) if 0 <= i + by < length])


def swap(x, axis):
    length = lax.axis_size(axis)
    return lax.ppermute(x, axis, [(i, length - 1 - i) for i in range(length)])


def plane_parts(own):
    return [own, swap(own, "tensor"), swap(own, "x"), swap(own, ("x", "tensor"))]


def plane_stack(parts):
    return jnp.stack(parts).reshape((2, 2) + parts[0].shape)


def whole_weight(near, far):
    x, tensor = lax.axis_index("x"), lax.axis_index("tensor")
    first = lax.axis_index("core") == 0
    by_core = [jnp.where(first, near, far), jnp.where(first, far, near)]

    def piece(x_at, core_at, tensor_at):
        picked = lax.dynamic_index_in_dim(by_core[core_at], x ^ x_at, 0, keepdims=False)
        return lax.dynamic_index_in_dim(picked, tensor ^ tensor_at, 0, keepdims=False)

    places = [(x_at, core_at) for x_at in range(2) for core_at in range(2)]
    halves = [jnp.stack([piece(*place, at) for place in places], 1) for at in range(2)]
    return jnp.concatenate(halves, axis=-1).reshape(-1, 2 * near.shape[-1])


def fold_core(kept, sent):
    return (kept.astype(F32) + swap(sent, "core").astype(F32)).astype(BF16)


def fold_blocks(kept, got):
    return [
        (kept[at].astype(F32) + got[at].astype(F32)).astype(BF16) for at in range(kept.shape[0])
    ]


def in_order(own, other, axis_name, axis):
    first = lax.axis_index(axis_name) == 0
    return jnp.stack([jnp.where(first, own, other), jnp.where(first, other, own)], axis)


def fold_plane(blocks):
    return [
        blocks[0],
        swap(blocks[1], "tensor"),
        swap(blocks[2], "x"),
        swap(blocks[3], ("x", "tensor")),
    ]


def wide_sum(parts):
    return sum(part.astype(F32) for part in parts)


def outer_shift(x, by):
    length = lax.axis_size("outer")
    return lax.ppermute(x, "outer", [(i, (i + by) % length) for i in range(length)])


def outer_gather(shard):
    length, here = lax.axis_size("outer"), lax.axis_index("outer")
    if length > 4:
        return lax.all_gather(shard, "outer")
    full = jnp.zeros((length,) + shard.shape, shard.dtype)
    for by in range(length):
        piece = outer_shift(shard, by) if by else shard
        full = lax.dynamic_update_slice_in_dim(full, piece[None], (here - by) % length, 0)
    return full


def outer_scatter(parts):
    length, here = lax.axis_size("outer"), lax.axis_index("outer")
    if length > 4:
        return lax.psum_scatter(parts, "outer", scatter_dimension=0, tiled=False).astype(F32)
    pieces = [
        lax.dynamic_index_in_dim(parts, (here + by) % length, 0, keepdims=False)
        for by in range(length)
    ]
    return wide_sum([pieces[0]] + [outer_shift(pieces[by], by) for by in range(1, length)])


def core_columns(rows, core_at, shard_rows):
    count = rows.shape[0]
    split = rows.reshape(count, -1, 2, shard_rows)
    return lax.dynamic_index_in_dim(split, core_at, 2, keepdims=False).reshape(count, -1)


def fold_columns(left, right, shard_rows):
    core = lax.axis_index("core")
    sent = dot(core_columns(left, 1 - core, shard_rows), right, ((0,), (0,))).astype(BF16)
    kept = dot(core_columns(left, core, shard_rows), right, ((0,), (0,))).astype(BF16)
    return fold_core(kept, sent).reshape(-1, 2, shard_rows, right.shape[1])


def distance_blocks(total):
    x, tensor = lax.axis_index("x"), lax.axis_index("tensor")
    columns = total.shape[3] // 2
    blocks = []
    for x_by in range(2):
        for tensor_by in range(2):
            block = lax.dynamic_index_in_dim(total, x ^ x_by, 1, keepdims=False)
            start = (tensor ^ tensor_by) * columns
            blocks.append(lax.dynamic_slice_in_dim(block, start, columns, 2))
    return blocks


def rotary_tables(position):
    halfway = HEAD_SIZE // 2
    inverse = jnp.exp(
        jnp.arange(halfway, dtype=F32) * (-2.0 * math.log(ROPE_BASE) / HEAD_SIZE)
    )
    angles = position.astype(F32)[:, None] * inverse[None, :]
    cosine, sine = jnp.cos(angles), jnp.sin(angles)
    return (
        jnp.concatenate([cosine, cosine], axis=1),
        jnp.concatenate([-sine, sine], axis=1),
    )


def norm_factor(value_rows):
    return lax.rsqrt(jnp.mean(value_rows * value_rows, axis=-1, keepdims=True) + EPSILON)


def norm_back(value_rows, factor, gain, upstream):
    weighted = upstream * gain
    return factor * weighted - value_rows * (factor * factor * factor) * jnp.mean(
        weighted * value_rows, axis=-1, keepdims=True
    )


def dot(a, b, dims):
    return lax.dot_general(a, b, (dims, ((), ())), preferred_element_type=F32)


VMEM_LIMIT = 60 * 1024 * 1024
LIGHT = pl.CostEstimate(flops=1000, bytes_accessed=1000, transcendentals=0)
FROM_LAST = (((1,), (1,)), ((), ()))
PLAIN = (((1,), (0,)), ((), ()))


def mxu(a, b, dims=PLAIN):
    return lax.dot_general(a, b, dims, preferred_element_type=F32)


def turn(rows, cosine, sine):
    return rows * cosine + pltpu.roll(rows, HEAD_SIZE // 2, 1) * sine


def project_kernel(rows_ref, weight_ref, cosine_ref, sine_ref, out_ref, *, turned):
    product = mxu(rows_ref[...], weight_ref[...])
    for at, turns in enumerate(turned):
        part = product[:, at * HEAD_SIZE : (at + 1) * HEAD_SIZE]
        if turns:
            part = turn(part, cosine_ref[...], sine_ref[...])
        out_ref[:, at * HEAD_SIZE : (at + 1) * HEAD_SIZE] = part.astype(BF16)


def project(rows, weight, cosine, sine, first, count, turned):
    high, width = rows.shape
    columns = len(turned) * HEAD_SIZE
    return pl.pallas_call(
        functools.partial(project_kernel, turned=turned),
        grid=(count,),
        in_specs=[
            pl.BlockSpec((high, width), lambda j: (0, 0)),
            pl.BlockSpec((width, columns), lambda j: (0, first + j)),
            pl.BlockSpec((high, HEAD_SIZE), lambda j: (0, 0)),
            pl.BlockSpec((high, HEAD_SIZE), lambda j: (0, 0)),
        ],
        out_specs=pl.BlockSpec((high, columns), lambda j: (0, j)),
        out_shape=jax.ShapeDtypeStruct((high, count * columns), BF16),
        compiler_params=pltpu.CompilerParams(vmem_limit_bytes=VMEM_LIMIT),
        cost_estimate=LIGHT,
        name="project",
    )(rows, weight, cosine, sine)


def mask_bias(place_ref, segment_key_ref, segment_query_ref, bias_ref, seq_len):
    span, rows = bias_ref.shape
    start = place_ref[0]
    key_at = lax.broadcasted_iota(jnp.int32, (span, rows), 0)
    query_at = lax.broadcasted_iota(jnp.int32, (span, rows), 1) + ATTEND_SPAN
    distance = query_at - key_at
    position = start + query_at - ATTEND_SPAN
    sequence_at = query_at - lax.rem(position, seq_len)
    allowed = (distance >= 0) & (distance < ATTEND_SPAN) & (key_at >= sequence_at)
    allowed = allowed & (segment_key_ref[...] == segment_query_ref[...])
    bias_ref[...] = jnp.where(allowed, 0.0, -1e30)


def attention_kernel(
    place_ref,
    segment_key_ref,
    segment_query_ref,
    q_ref,
    kv_ref,
    heads_ref,
    lse_ref,
    bias_ref,
    *,
    seq_len,
    scale,
):
    @pl.when(pl.program_id(0) == 0)
    def _():
        mask_bias(place_ref, segment_key_ref, segment_query_ref, bias_ref, seq_len)

    rows = q_ref.shape[0]
    span = kv_ref.shape[0]
    count = q_ref.shape[1] // HEAD_SIZE
    value_t = kv_ref[:, HEAD_SIZE:].T
    chunks = span // rows
    for head in range(count):
        columns = slice(head * HEAD_SIZE, (head + 1) * HEAD_SIZE)
        query = q_ref[:, columns]
        scores = []
        for c in range(chunks):
            part = slice(c * rows, (c + 1) * rows)
            raw = mxu(kv_ref[part, :HEAD_SIZE], query, FROM_LAST)
            scores.append(raw * scale + bias_ref[part, :])
        top = functools.reduce(jnp.maximum, scores)
        top = jnp.max(top, axis=0, keepdims=True)
        total = jnp.zeros_like(top)
        out_t = jnp.zeros((HEAD_SIZE, rows), F32)
        for c in range(chunks):
            weight = jnp.exp(scores[c] - top)
            total = total + jnp.sum(weight, axis=0, keepdims=True)
            out_t = out_t + mxu(value_t[:, c * rows : (c + 1) * rows], weight.astype(BF16))
        heads_ref[:, columns] = (out_t / total).T.astype(BF16)
        lse_ref[0, head : head + 1, :] = top + jnp.log(total)


def attention(place, segment_key, segment_query, queries, key_value, seq_len):
    rows, all_columns = queries.shape
    span = key_value.shape[0]
    pairs = key_value.shape[1] // (2 * HEAD_SIZE)
    columns = all_columns // pairs
    return pl.pallas_call(
        functools.partial(attention_kernel, seq_len=seq_len, scale=1.0 / math.sqrt(HEAD_SIZE)),
        grid=(pairs,),
        in_specs=[
            pl.BlockSpec(memory_space=pltpu.SMEM),
            pl.BlockSpec((span, 1), lambda j: (0, 0)),
            pl.BlockSpec((1, rows), lambda j: (0, 0)),
            pl.BlockSpec((rows, columns), lambda j: (0, j)),
            pl.BlockSpec((span, 2 * HEAD_SIZE), lambda j: (0, j)),
        ],
        out_specs=[
            pl.BlockSpec((rows, columns), lambda j: (0, j)),
            pl.BlockSpec((1, columns // HEAD_SIZE, rows), lambda j: (j, 0, 0)),
        ],
        out_shape=[
            jax.ShapeDtypeStruct((rows, all_columns), BF16),
            jax.ShapeDtypeStruct((pairs, columns // HEAD_SIZE, rows), F32),
        ],
        scratch_shapes=[pltpu.VMEM((span, rows), F32)],
        compiler_params=pltpu.CompilerParams(vmem_limit_bytes=VMEM_LIMIT),
        cost_estimate=LIGHT,
        name="attention",
    )(place, segment_key, segment_query, queries, key_value)


def attention_back_kernel(
    place_ref,
    segment_key_ref,
    segment_query_ref,
    q_ref,
    kv_ref,
    lse_ref,
    dout_ref,
    cosine_ref,
    sine_ref,
    dq_ref,
    dkv_far_ref,
    dkv_own_ref,
    bias_ref,
    dkv_ref,
    *,
    seq_len,
    scale,
):
    @pl.when(pl.program_id(0) == 0)
    def _():
        mask_bias(place_ref, segment_key_ref, segment_query_ref, bias_ref, seq_len)

    rows = q_ref.shape[0]
    span = kv_ref.shape[0]
    count = q_ref.shape[1] // HEAD_SIZE
    key_t = kv_ref[:, :HEAD_SIZE].T
    chunks = span // rows
    dkv_ref[...] = jnp.zeros_like(dkv_ref)
    for head in range(count):
        columns = slice(head * HEAD_SIZE, (head + 1) * HEAD_SIZE)
        query = q_ref[:, columns]
        dout = dout_ref[:, columns]
        lse = lse_ref[0, head : head + 1, :]
        probs, dprobs = [], []
        row_dot = jnp.zeros_like(lse)
        for c in range(chunks):
            part = slice(c * rows, (c + 1) * rows)
            raw = mxu(kv_ref[part, :HEAD_SIZE], query, FROM_LAST)
            prob = jnp.exp(raw * scale + bias_ref[part, :] - lse)
            dprob = mxu(kv_ref[part, HEAD_SIZE:], dout, FROM_LAST)
            row_dot = row_dot + jnp.sum(prob * dprob, axis=0, keepdims=True)
            probs.append(prob)
            dprobs.append(dprob)
        dq_t = jnp.zeros((HEAD_SIZE, rows), F32)
        for c in range(chunks):
            part = slice(c * rows, (c + 1) * rows)
            dscore = (probs[c] * (dprobs[c] - row_dot)).astype(BF16)
            dkv_ref[part, :HEAD_SIZE] += mxu(dscore, query)
            dkv_ref[part, HEAD_SIZE:] += mxu(probs[c].astype(BF16), dout)
            dq_t = dq_t + mxu(key_t[:, part], dscore)
        dq_ref[:, columns] = turn(dq_t.T * scale, cosine_ref[...], -sine_ref[...]).astype(BF16)
    dkv_ref[:, :HEAD_SIZE] = dkv_ref[:, :HEAD_SIZE] * scale
    dkv_far_ref[...] = dkv_ref[: span - rows, :].astype(BF16)
    dkv_own_ref[...] = dkv_ref[span - rows :, :]


def attention_back(
    place, segment_key, segment_query, queries, key_value, lse, dout, cosine, sine, seq_len
):
    rows, all_columns = queries.shape
    span = key_value.shape[0]
    pairs = key_value.shape[1] // (2 * HEAD_SIZE)
    columns = all_columns // pairs
    return pl.pallas_call(
        functools.partial(
            attention_back_kernel, seq_len=seq_len, scale=1.0 / math.sqrt(HEAD_SIZE)
        ),
        grid=(pairs,),
        in_specs=[
            pl.BlockSpec(memory_space=pltpu.SMEM),
            pl.BlockSpec((span, 1), lambda j: (0, 0)),
            pl.BlockSpec((1, rows), lambda j: (0, 0)),
            pl.BlockSpec((rows, columns), lambda j: (0, j)),
            pl.BlockSpec((span, 2 * HEAD_SIZE), lambda j: (0, j)),
            pl.BlockSpec((1, columns // HEAD_SIZE, rows), lambda j: (j, 0, 0)),
            pl.BlockSpec((rows, columns), lambda j: (0, j)),
            pl.BlockSpec((rows, HEAD_SIZE), lambda j: (0, 0)),
            pl.BlockSpec((rows, HEAD_SIZE), lambda j: (0, 0)),
        ],
        out_specs=[
            pl.BlockSpec((rows, columns), lambda j: (0, j)),
            pl.BlockSpec((span - rows, 2 * HEAD_SIZE), lambda j: (0, j)),
            pl.BlockSpec((rows, 2 * HEAD_SIZE), lambda j: (0, j)),
        ],
        out_shape=[
            jax.ShapeDtypeStruct((rows, all_columns), BF16),
            jax.ShapeDtypeStruct((span - rows, key_value.shape[1]), BF16),
            jax.ShapeDtypeStruct((rows, key_value.shape[1]), F32),
        ],
        scratch_shapes=[
            pltpu.VMEM((span, rows), F32),
            pltpu.VMEM((span, 2 * HEAD_SIZE), F32),
        ],
        compiler_params=pltpu.CompilerParams(vmem_limit_bytes=VMEM_LIMIT),
        cost_estimate=pl.CostEstimate(
            flops=70_000_000_000, bytes_accessed=10_000_000, transcendentals=0
        ),
        name="attention_back",
    )(place, segment_key, segment_query, queries, key_value, lse, dout, cosine, sine)


def expert_kernel(
    slot_row_ref,
    slot_column_ref,
    routed_ref,
    own_ref,
    router_ref,
    tokens_ref,
    cotangent_ref,
    gate_ref,
    up_ref,
    down_ref,
    grad_ref,
    moe_ref,
    rows_in_ref,
    grad_out_ref,
    hidden_ref,
    grad_gate_ref,
    grad_up_ref,
    router_grad_ref,
    gate_full_ref,
    up_full_ref,
    down_full_ref,
    *,
    capacity,
):
    whole = ((gate_ref, gate_full_ref), (up_ref, up_full_ref), (down_ref, down_full_ref))

    @pl.when(pl.program_id(0) == 0)
    def _():
        for held, full in whole:
            columns = held.shape[3]
            for half in range(held.shape[1]):
                full[:, half * columns : (half + 1) * columns] = held[:, half].reshape(-1, columns)

    group_rows = tokens_ref.shape[1]
    tokens = tokens_ref[0]
    gate_weight, up_weight, down_weight = (full[...] for _, full in whole)
    cotangent = cotangent_ref[0]
    routed = routed_ref[0] > 0.0
    logits = jnp.where(routed, mxu(router_ref[...], tokens, FROM_LAST), -1e30)
    weights = jnp.exp(logits - jnp.max(logits, axis=0, keepdims=True))
    weights = jnp.where(routed, weights, 0.0)
    gates = weights / jnp.sum(weights, axis=0, keepdims=True)
    own = own_ref[...]
    gate_own = jnp.sum(gates * own, axis=0, keepdims=True)
    place = slot_row_ref[0] == lax.broadcasted_iota(jnp.int32, (capacity, group_rows), 0)
    place_wide = jnp.where(place, 1.0, 0.0)
    place_low = place_wide.astype(BF16)
    back = slot_column_ref[0] == lax.broadcasted_iota(jnp.int32, (group_rows, capacity), 1)
    back_low = jnp.where(back, 1.0, 0.0).astype(BF16)
    coefficient = jnp.sum(place_wide * gate_own, axis=1, keepdims=True)

    rows_in = mxu(place_low, tokens).astype(BF16)
    rows_in_ref[...] = rows_in
    gate_pre = mxu(rows_in, gate_weight)
    up_pre = mxu(rows_in, up_weight)
    sigmoid = 1.0 / (1.0 + jnp.exp(-gate_pre))
    silu = gate_pre * sigmoid
    hidden = (silu * up_pre).astype(BF16)
    hidden_ref[...] = hidden
    slot_cotangent = mxu(place_low, cotangent)
    grad_out = (coefficient * slot_cotangent).astype(BF16)
    grad_out_ref[...] = grad_out
    grad_hidden = mxu(grad_out, down_weight)
    grad_up = (grad_hidden * silu).astype(BF16)
    grad_gate = (grad_hidden * up_pre * sigmoid * (1.0 + gate_pre * (1.0 - sigmoid))).astype(BF16)
    grad_up_ref[...] = grad_up
    grad_gate_ref[...] = grad_gate
    expert_out = mxu(hidden, down_weight, FROM_LAST)
    grad_slot = jnp.sum(slot_cotangent * expert_out, axis=1, keepdims=True)
    moe_ref[0] = mxu(back_low, (coefficient * expert_out).astype(BF16)).astype(BF16)

    grad_token = jnp.sum(place_wide * grad_slot, axis=0, keepdims=True)
    share = (grad_token * gate_own) * (own - gates)
    share_high = share.astype(BF16)
    share_low = (share - share_high.astype(F32)).astype(BF16)
    router_grad = mxu(share_high, tokens) + mxu(share_low, tokens)

    @pl.when(pl.program_id(0) == 0)
    def _():
        router_grad_ref[...] = router_grad

    @pl.when(pl.program_id(0) > 0)
    def _():
        router_grad_ref[...] += router_grad

    grad_in = mxu(grad_gate, gate_weight, FROM_LAST) + mxu(grad_up, up_weight, FROM_LAST)
    grad_ref[0] = (
        mxu(back_low, grad_in.astype(BF16)) + mxu(share.T.astype(BF16), router_ref[...])
    ).astype(BF16)


def expert_groups(slot, routed, own, router_t, tokens, cotangent, weights, capacity):
    count, group_rows, width = tokens.shape
    ff = weights[0].shape[1] * weights[0].shape[3]
    experts = router_t.shape[0]
    weight = pl.BlockSpec(
        weights[0].shape, lambda g: (0, 0, 0, 0), pipeline_mode=pl.Buffered(1)
    )
    whole = lambda g: (0, 0)
    by_group = lambda g: (g, 0, 0)
    slots = lambda columns: pl.BlockSpec((capacity, columns), lambda g: (g, 0))
    slots_shape = lambda columns: jax.ShapeDtypeStruct((count * capacity, columns), BF16)
    return pl.pallas_call(
        functools.partial(expert_kernel, capacity=capacity),
        grid=(count,),
        in_specs=[
            pl.BlockSpec((1, 1, group_rows), by_group),
            pl.BlockSpec((1, group_rows, 1), by_group),
            pl.BlockSpec((1, experts, group_rows), by_group),
            pl.BlockSpec((experts, 1), whole),
            pl.BlockSpec((experts, width), whole),
            pl.BlockSpec((1, group_rows, width), by_group),
            pl.BlockSpec((1, group_rows, width), by_group),
            weight,
            weight,
            weight,
        ],
        out_specs=[
            pl.BlockSpec((1, group_rows, width), by_group),
            pl.BlockSpec((1, group_rows, width), by_group),
            slots(width),
            slots(width),
            slots(ff),
            slots(ff),
            slots(ff),
            pl.BlockSpec((experts, width), whole),
        ],
        out_shape=[
            jax.ShapeDtypeStruct(tokens.shape, BF16),
            jax.ShapeDtypeStruct(tokens.shape, BF16),
            slots_shape(width),
            slots_shape(width),
            slots_shape(ff),
            slots_shape(ff),
            slots_shape(ff),
            jax.ShapeDtypeStruct((experts, width), F32),
        ],
        scratch_shapes=[pltpu.VMEM((width, ff), BF16) for _ in range(3)],
        compiler_params=pltpu.CompilerParams(vmem_limit_bytes=VMEM_LIMIT),
        cost_estimate=LIGHT,
        name="expert",
    )(
        slot[:, None, :],
        slot[:, :, None],
        routed,
        own,
        router_t,
        tokens,
        cotangent,
        *weights,
    )


def weight_grad_kernel(*refs, halves):
    rows, grad_out, hidden, grad_gate, grad_up, router = (
        refs[at : at + 2] for at in range(0, 12, 2)
    )
    moe_kept_ref, moe_got_ref, out_ref = refs[12:15]
    for at, moe_ref in enumerate(refs[15:]):
        moe_ref[...] = (moe_kept_ref[at].astype(F32) + moe_got_ref[at].astype(F32)).astype(BF16)
    columns = hidden[0].shape[1] // halves
    over = (((0,), (0,)), ((), ()))
    left_rows = [ref[...] for ref in rows]
    left_out = [ref[...] for ref in grad_out]
    router_columns = (router[0][...] + router[1][...]).T
    router_columns = jnp.concatenate(
        [
            router_columns,
            jnp.zeros((router_columns.shape[0], HEAD_SIZE - router_columns.shape[1]), F32),
        ],
        axis=1,
    ).astype(BF16)
    for half in range(halves):
        start = half * (3 * columns + HEAD_SIZE)
        part = slice(half * columns, (half + 1) * columns)
        for at, (left, right) in enumerate(
            ((left_rows, grad_gate), (left_rows, grad_up), (left_out, hidden))
        ):
            total = mxu(left[0], right[0][:, part], over) + mxu(left[1], right[1][:, part], over)
            out_ref[:, start + at * columns : start + (at + 1) * columns] = total.astype(BF16)
        out_ref[:, start + 3 * columns : start + 3 * columns + HEAD_SIZE] = router_columns


def weight_grads(near, far, moe_kept, moe_got, halves, block=256):
    rows_at, grad_out_at, hidden_at, grad_gate_at, grad_up_at, router_at = range(6)
    slots, width = near[rows_at].shape
    ff = near[hidden_at].shape[1]
    experts = near[router_at].shape[0]
    specs, operands = [], []
    for at in (rows_at, grad_out_at, hidden_at, grad_gate_at, grad_up_at, router_at):
        if at in (rows_at, grad_out_at):
            spec = pl.BlockSpec((slots, block), lambda i: (0, i))
        elif at == router_at:
            spec = pl.BlockSpec((experts, block), lambda i: (0, i))
        else:
            spec = pl.BlockSpec((slots, ff), lambda i: (0, 0))
        specs += [spec, spec]
        operands += [near[at], far[at]]
    columns = 3 * ff + halves * HEAD_SIZE
    moe_count, moe_rows, _ = moe_kept.shape
    moe_spec = pl.BlockSpec((moe_count, moe_rows, block), lambda i: (0, 0, i))
    moe_out_spec = pl.BlockSpec((moe_rows, block), lambda i: (0, i))
    return pl.pallas_call(
        functools.partial(weight_grad_kernel, halves=halves),
        grid=(width // block,),
        in_specs=specs + [moe_spec, moe_spec],
        out_specs=[pl.BlockSpec((block, columns), lambda i: (i, 0))] + [moe_out_spec] * moe_count,
        out_shape=[jax.ShapeDtypeStruct((width, columns), BF16)]
        + [jax.ShapeDtypeStruct((moe_rows, width), BF16)] * moe_count,
        compiler_params=pltpu.CompilerParams(vmem_limit_bytes=VMEM_LIMIT),
        cost_estimate=pl.CostEstimate(
            flops=15_000_000_000, bytes_accessed=50_000_000, transcendentals=0
        ),
        name="weight_grads",
    )(*operands, moe_kept, moe_got)


def on_device(
    block_input,
    norm_gains,
    router_weight,
    query_matrix,
    key_matrix,
    value_matrix,
    output_weight,
    gate_weight,
    up_weight,
    down_weight,
    segment_ids,
    routes,
    priority,
    cotangent,
):
    tensor_index = lax.axis_index("tensor")
    own_rows, width = block_input.shape
    group_rows = segment_ids.shape[0]
    halves = lax.axis_size("tensor")
    outer = lax.axis_size("outer")
    groups = lax.axis_size("x") * lax.axis_size("core")
    plane = groups * halves
    shard_rows = query_matrix.shape[0]
    dp_size = outer * groups
    seq_len = min(SEQ_MOST, group_rows * dp_size)
    own_start = lax.axis_index(ALL) * own_rows
    capacity = group_rows * TOPK // EXPERTS
    reach = ATTEND_SPAN // own_rows
    half_ff = gate_weight.shape[2]
    ff = half_ff * halves

    query_columns = query_matrix.shape[1]
    pair_columns = 2 * halves * HEAD_SIZE
    first = tensor_index == 0
    key_value_weight = jnp.concatenate([key_matrix, value_matrix], axis=1)
    other_weight = swap(key_value_weight, "tensor")
    early = jnp.concatenate(
        [
            jnp.where(first, key_value_weight, other_weight),
            jnp.where(first, other_weight, key_value_weight),
            query_matrix,
            output_weight,
        ],
        axis=1,
    )
    early, gate_own, up_own, down_own, cotangent_own = lax.optimization_barrier(
        (early, gate_weight, up_weight, down_weight, cotangent)
    )
    early = outer_gather(early)

    expert_shard = jnp.transpose(jnp.stack([gate_own, up_own, down_own]), (2, 0, 1, 3))
    expert_shard = lax.all_to_all(expert_shard, PLANE, 0, 0, tiled=True)
    expert_shard = expert_shard.reshape(groups, halves, 3, shard_rows, half_ff)
    expert_shard = [
        jnp.swapaxes(expert_shard[:, :, at], 0, 1).reshape(-1, half_ff) for at in range(3)
    ]
    early, expert_shard, segment_here, priority_here = lax.optimization_barrier(
        (early, expert_shard, segment_ids, priority)
    )
    pair_count = group_rows * TOPK
    rank = (
        jnp.zeros((pair_count,), jnp.int32)
        .at[priority_here]
        .set(jnp.arange(pair_count, dtype=jnp.int32))
        .reshape(group_rows, TOPK)
    )
    expert_ids = jnp.arange(EXPERTS, dtype=jnp.int32)
    named = routes[:, :, None] == expert_ids[None, None, :]
    ranked = jnp.sum(jnp.where(named, rank[:, :, None] + 1, 0), axis=1)
    ranked = jnp.where(ranked > 0, ranked, pair_count + 1)
    ranked_own = lax.dynamic_slice_in_dim(ranked, tensor_index * own_rows, own_rows, 0)
    digits = jnp.concatenate([ranked_own // 64, ranked_own % 64], axis=1).astype(BF16)
    digits = jnp.pad(digits, ((0, 0), (0, HEAD_SIZE - digits.shape[1])))
    cotangent_sent = jnp.concatenate([cotangent_own, digits], axis=1)
    segment_near = jnp.concatenate(
        [shift_groups(segment_here, 2), shift_groups(segment_here, 1), segment_here]
    )
    expert_full = [
        lax.all_gather(shard, "outer").reshape(outer, halves, groups * shard_rows, half_ff)
        for shard in expert_shard
    ]

    key_value_full = early[:, :, :pair_columns]
    key_value_full = in_order(key_value_full, swap(key_value_full, "x"), "x", 1)
    key_value_full = in_order(key_value_full, swap(key_value_full, "core"), "core", 2)
    key_value_full = key_value_full.reshape(width, pair_columns)
    query_parts = plane_parts(early[:, :, pair_columns : pair_columns + query_columns])

    input_wide = block_input.astype(F32)
    first_gain = norm_gains[:, 0]
    second_gain = norm_gains[:, 1]
    first_factor = norm_factor(input_wide)
    normed_in = (input_wide * first_factor * first_gain).astype(BF16)
    positions = own_start + jnp.arange(own_rows, dtype=jnp.int32)
    cosine, sine = rotary_tables(positions % seq_len)
    query_blocks = halves * query_columns // (2 * HEAD_SIZE)
    key_value_sent = project(
        normed_in, key_value_full, cosine, sine, 0, halves, (True, False)
    )
    one_back, two_back = shift_groups(key_value_sent, 1), shift_groups(key_value_sent, 2)
    query_parts, one_back, two_back, segment_near, cotangent_sent, expert_full[0] = (
        lax.optimization_barrier(
            (query_parts, one_back, two_back, segment_near, cotangent_sent, expert_full[0])
        )
    )
    cotangent_parts = plane_parts(cotangent_sent)
    output_own = early[:, :, pair_columns + query_columns :]
    pair_sent = jnp.where(
        first,
        jnp.stack([one_back, key_value_sent]),
        jnp.stack([two_back, one_back]),
    )
    pair_got = swap(pair_sent, "tensor")
    query_near = plane_stack(query_parts)
    query_far, pair_got = lax.optimization_barrier((swap(query_near, "core"), pair_got))
    pieces = [two_back, pair_got[0], one_back, pair_got[1], key_value_sent]
    query_full = whole_weight(query_near, query_far)
    queries = project(normed_in, query_full, cosine, sine, 0, query_blocks, (True, True))
    output_parts = plane_parts(output_own)
    expert = lax.axis_index(PLANE)

    def slots_of(cotangents):
        digits = cotangents[..., width:].reshape(2, group_rows, HEAD_SIZE).astype(jnp.int32)
        ranked_all = digits[..., :EXPERTS] * 64 + digits[..., EXPERTS : 2 * EXPERTS]
        routed = jnp.swapaxes((ranked_all <= pair_count).astype(F32), 1, 2)
        rank_own = jnp.sum(jnp.where(expert_ids == expert, ranked_all, 0), axis=-1)
        earlier = (rank_own[:, None, :] < rank_own[:, :, None]).astype(jnp.int32)
        slot = jnp.where(rank_own <= pair_count, jnp.sum(earlier, axis=-1), capacity)
        return slot, routed

    key_value = jnp.concatenate(pieces, axis=0)
    span = ATTEND_SPAN + own_rows
    segment_ext = lax.dynamic_slice_in_dim(segment_near, tensor_index * own_rows, span)
    view = (
        jnp.reshape(own_start, (1,)),
        segment_ext[:, None],
        segment_ext[None, ATTEND_SPAN:],
        queries,
        key_value,
    )
    heads_low, log_total = attention(*view, seq_len)
    heads_late, output_parts, cotangent_parts = lax.optimization_barrier(
        (heads_low, output_parts, cotangent_parts)
    )
    output_near = plane_stack(output_parts)
    output_far = swap(output_near, "core")
    output_full, expert_full[1] = lax.optimization_barrier(
        (whole_weight(output_near, output_far), expert_full[1])
    )
    hidden_state = input_wide + dot(heads_low, output_full, ((1,), (1,)))
    second_factor = norm_factor(hidden_state)
    normed_mid_own = (hidden_state * second_factor * second_gain).astype(BF16)

    cotangent_near = plane_stack(cotangent_parts)
    cotangent_far = swap(cotangent_near, "core")
    near_slots, far_slots = slots_of(cotangent_near), slots_of(cotangent_far)
    normed_parts, near_slots, far_slots, expert_full[2] = lax.optimization_barrier(
        (plane_parts(normed_mid_own), near_slots, far_slots, expert_full[2])
    )
    normed_near = plane_stack(normed_parts)
    normed_far = swap(normed_near, "core")
    own_expert = (expert_ids == expert).astype(F32)[:, None]
    router_t = router_weight.T

    def experts_on(tokens, cotangents, slots):
        slot, routed = slots
        return expert_groups(
            slot,
            routed,
            own_expert,
            router_t,
            tokens.reshape(2, group_rows, width),
            cotangents.reshape(2, group_rows, -1),
            expert_full,
            capacity,
        )

    on_near = experts_on(normed_near, cotangent_near, near_slots)
    on_far = experts_on(normed_far, cotangent_far, far_slots)
    blocks = (2 * halves, own_rows, width)
    (grad_near, moe_near), (grad_far, moe_far) = (
        [array.reshape(blocks) for array in side[:2]] for side in (on_near, on_far)
    )
    grad_blocks = fold_blocks(grad_near, swap(grad_far, "core"))
    grad_blocks, moe_far, on_near, on_far = lax.optimization_barrier(
        (grad_blocks, moe_far, on_near[2:], on_far[2:])
    )
    grad_mid_parts = fold_plane(grad_blocks)
    expert_part, *moe_blocks = weight_grads(
        on_near, on_far, moe_near, swap(moe_far, "core"), halves
    )
    expert_sum = lax.psum_scatter(expert_part, "outer", scatter_dimension=0, tiled=True)
    grad_mid_parts, moe_blocks = lax.optimization_barrier((grad_mid_parts, moe_blocks))
    moe_parts = fold_plane(moe_blocks)
    grad_mid = wide_sum(grad_mid_parts)

    norm_input_part = norm_back(hidden_state, second_factor, second_gain, grad_mid)
    grad_state = cotangent.astype(F32) + norm_input_part
    grad_attn = grad_state.astype(BF16)
    grad_heads = dot(grad_attn, output_full, ((1,), (0,))).astype(BF16)
    output_total = fold_columns(grad_attn, heads_late, shard_rows)
    grad_query_pre, grad_far_kv, grad_own = attention_back(
        *view, log_total, grad_heads, cosine, sine, seq_len
    )
    grad_query_pre, output_total, moe_parts = lax.optimization_barrier(
        (grad_query_pre, output_total, moe_parts)
    )
    output_parts = fold_plane(distance_blocks(output_total))
    query_total = fold_columns(normed_in, grad_query_pre, shard_rows)
    two_back, pair_old, one_back, pair_new = grad_far_kv.reshape(reach, own_rows, -1)
    pair_got, output_parts, query_total = lax.optimization_barrier(
        (swap(jnp.stack([pair_old, pair_new]), "tensor"), output_parts, query_total)
    )
    query_parts = fold_plane(distance_blocks(query_total))
    pair_old, pair_new = pair_got.astype(F32)
    one_back = one_back.astype(F32) + jnp.where(first, pair_old, pair_new)
    two_back = two_back.astype(F32) + jnp.where(first, 0.0, pair_old)
    grad_own = grad_own + jnp.where(first, pair_new, 0.0)
    grad_own = grad_own + shift_groups(one_back.astype(BF16), -1).astype(F32)
    grad_own = grad_own + shift_groups(two_back.astype(BF16), -2).astype(F32)
    grad_own, query_parts, output_parts, expert_sum = lax.optimization_barrier(
        (grad_own, query_parts, output_parts, expert_sum)
    )
    output_weight_grad = outer_scatter(wide_sum(output_parts).astype(BF16))
    grad_key_value = []
    for half in range(halves):
        start = half * 2 * HEAD_SIZE
        key_part = grad_own[:, start : start + HEAD_SIZE]
        turned = jnp.concatenate(
            [key_part[:, HEAD_SIZE // 2 :], key_part[:, : HEAD_SIZE // 2]], axis=1
        )
        grad_key_value.append(key_part * cosine - turned * sine)
        grad_key_value.append(grad_own[:, start + HEAD_SIZE : start + 2 * HEAD_SIZE])
    grad_key_value_pre = jnp.concatenate(grad_key_value, axis=1).astype(BF16)
    key_value_total = fold_columns(normed_in, grad_key_value_pre, shard_rows)
    key_value_parts = fold_plane(distance_blocks(key_value_total))
    grad_in = dot(grad_query_pre, query_full, ((1,), (1,))) + dot(
        grad_key_value_pre, key_value_full, ((1,), (1,))
    )
    input_grad = grad_state + norm_back(input_wide, first_factor, first_gain, grad_in)
    qkv_grad = outer_scatter(
        jnp.concatenate([wide_sum(query_parts), wide_sum(key_value_parts)], axis=2).astype(BF16)
    )
    block_output = hidden_state + wide_sum(moe_parts)
    expert_sum = expert_sum.reshape(groups, shard_rows, halves, -1)
    expert_sum = jnp.swapaxes(expert_sum, 1, 2).reshape(plane, shard_rows, -1)
    expert_sum = lax.all_to_all(expert_sum, PLANE, 0, 0, tiled=True)
    gate_grad, up_grad, down_grad = (
        jnp.swapaxes(expert_sum[:, :, at * half_ff : (at + 1) * half_ff], 0, 1).astype(F32)
        for at in range(3)
    )
    router_grad = jnp.sum(expert_sum[:, :, 3 * half_ff : 3 * half_ff + EXPERTS].astype(F32), axis=0)
    router_grad = lax.dynamic_slice_in_dim(
        router_grad, tensor_index * (shard_rows // 2), shard_rows // 2, 0
    )
    query_grad = qkv_grad[:, :query_columns]
    key_grad = qkv_grad[:, query_columns : query_columns + HEAD_SIZE]
    value_grad = qkv_grad[:, query_columns + HEAD_SIZE :]

    half_rows = shard_rows // 2
    own_gains = lax.dynamic_slice_in_dim(
        norm_gains, lax.axis_index(DP) * shard_rows, shard_rows, 0
    )
    qkv_own = jnp.concatenate([query_matrix, key_value_weight], axis=1)
    first_sum = jnp.sum(qkv_grad * qkv_own.astype(F32), axis=-1)
    second_sum = jnp.sum(
        gate_grad * gate_weight.astype(F32) + up_grad * up_weight.astype(F32), axis=(1, 2)
    )
    gain_sums = jnp.stack([first_sum, second_sum], axis=1) / own_gains
    kept = lax.dynamic_slice_in_dim(gain_sums, tensor_index * half_rows, half_rows, 0)
    sent = lax.dynamic_slice_in_dim(gain_sums, (1 - tensor_index) * half_rows, half_rows, 0)
    own_router = lax.dynamic_slice_in_dim(
        router_weight, lax.axis_index(ALL) * half_rows, half_rows, 0
    )
    router_sum = jnp.sum(router_grad * own_router.astype(F32), axis=-1)
    half_gains = lax.dynamic_slice_in_dim(own_gains, tensor_index * half_rows, half_rows, 0)
    router_sum = router_sum / half_gains[:, 1]
    gains_grad = (
        kept
        + swap(sent, "tensor")
        + jnp.stack([jnp.zeros_like(router_sum), router_sum], axis=1)
    )
    return (
        block_output,
        input_grad,
        gains_grad,
        router_grad,
        query_grad,
        key_grad,
        value_grad,
        output_weight_grad,
        gate_grad,
        up_grad,
        down_grad,
    )


def solution(mesh):
    dp_size, tensor_size = mesh.shape["dp"], mesh.shape["tensor"]
    split = Mesh(mesh.devices.reshape(dp_size // 4, 2, 2, tensor_size), ALL)
    return jax.shard_map(
        on_device,
        mesh=split,
        in_specs=(
            P(ALL, None),
            P(),
            P(),
            P(DP, "tensor"),
            P(DP, "tensor"),
            P(DP, "tensor"),
            P(DP, "tensor"),
            P(DP, None, "tensor"),
            P(DP, None, "tensor"),
            P(DP, None, "tensor"),
            P(DP),
            P(DP, None),
            P(DP),
            P(ALL, None),
        ),
        out_specs=(
            P(ALL, None),
            P(ALL, None),
            P(ALL, None),
            P(ALL, None),
            P(DP, "tensor"),
            P(DP, "tensor"),
            P(DP, "tensor"),
            P(DP, "tensor"),
            P(DP, None, "tensor"),
            P(DP, None, "tensor"),
            P(DP, None, "tensor"),
        ),
        check_vma=False,
    )
```

```python
import functools
import math

import jax
import jax.numpy as jnp
from jax import lax
from jax.experimental import pallas as pl
from jax.experimental.pallas import tpu as pltpu
from jax.sharding import Mesh
from jax.sharding import PartitionSpec as P

HEAD_SIZE = 128
TOPK = 4
EXPERTS = 8
ATTEND_SPAN = 1024
SEQ_MOST = 16384
EPSILON = 1e-06
ROPE_BASE = 10000.0
BF16 = jnp.bfloat16
F32 = jnp.float32

DP = ("outer", "x", "core")
PLANE = ("x", "core", "tensor")
ALL = ("outer", "x", "core", "tensor")


def shift_groups(x, by):
    length = lax.axis_size(DP)
    return lax.ppermute(x, DP, [(i, i + by) for i in range(length) if 0 <= i + by < length])


def swap(x, axis):
    length = lax.axis_size(axis)
    return lax.ppermute(x, axis, [(i, length - 1 - i) for i in range(length)])


def plane_parts(own):
    return [own, swap(own, "tensor"), swap(own, "x"), swap(own, ("x", "tensor"))]


def plane_stack(parts):
    return jnp.stack(parts).reshape((2, 2) + parts[0].shape)


def whole_weight(near, far):
    x, tensor = lax.axis_index("x"), lax.axis_index("tensor")
    first = lax.axis_index("core") == 0
    by_core = [jnp.where(first, near, far), jnp.where(first, far, near)]

    def piece(x_at, core_at, tensor_at):
        picked = lax.dynamic_index_in_dim(by_core[core_at], x ^ x_at, 0, keepdims=False)
        return lax.dynamic_index_in_dim(picked, tensor ^ tensor_at, 0, keepdims=False)

    places = [(x_at, core_at) for x_at in range(2) for core_at in range(2)]
    halves = [jnp.stack([piece(*place, at) for place in places], 1) for at in range(2)]
    return jnp.concatenate(halves, axis=-1).reshape(-1, 2 * near.shape[-1])


def fold_core(kept, sent):
    return (kept.astype(F32) + swap(sent, "core").astype(F32)).astype(BF16)


def fold_blocks(kept, got):
    return [
        (kept[at].astype(F32) + got[at].astype(F32)).astype(BF16) for at in range(kept.shape[0])
    ]


def in_order(own, other, axis_name, axis):
    first = lax.axis_index(axis_name) == 0
    return jnp.stack([jnp.where(first, own, other), jnp.where(first, other, own)], axis)


def fold_plane(blocks):
    return [
        blocks[0],
        swap(blocks[1], "tensor"),
        swap(blocks[2], "x"),
        swap(blocks[3], ("x", "tensor")),
    ]


def wide_sum(parts):
    return sum(part.astype(F32) for part in parts)


def outer_shift(x, by):
    length = lax.axis_size("outer")
    return lax.ppermute(x, "outer", [(i, (i + by) % length) for i in range(length)])


def outer_gather(shard):
    length, here = lax.axis_size("outer"), lax.axis_index("outer")
    if length > 4:
        return lax.all_gather(shard, "outer")
    full = jnp.zeros((length,) + shard.shape, shard.dtype)
    for by in range(length):
        piece = outer_shift(shard, by) if by else shard
        full = lax.dynamic_update_slice_in_dim(full, piece[None], (here - by) % length, 0)
    return full


def outer_scatter(parts):
    length, here = lax.axis_size("outer"), lax.axis_index("outer")
    if length > 4:
        return lax.psum_scatter(parts, "outer", scatter_dimension=0, tiled=False).astype(F32)
    pieces = [
        lax.dynamic_index_in_dim(parts, (here + by) % length, 0, keepdims=False)
        for by in range(length)
    ]
    return wide_sum([pieces[0]] + [outer_shift(pieces[by], by) for by in range(1, length)])


def core_columns(rows, core_at, shard_rows):
    count = rows.shape[0]
    split = rows.reshape(count, -1, 2, shard_rows)
    return lax.dynamic_index_in_dim(split, core_at, 2, keepdims=False).reshape(count, -1)


def fold_columns(left, right, shard_rows):
    core = lax.axis_index("core")
    sent = dot(core_columns(left, 1 - core, shard_rows), right, ((0,), (0,))).astype(BF16)
    kept = dot(core_columns(left, core, shard_rows), right, ((0,), (0,))).astype(BF16)
    return fold_core(kept, sent).reshape(-1, 2, shard_rows, right.shape[1])


def distance_blocks(total):
    x, tensor = lax.axis_index("x"), lax.axis_index("tensor")
    columns = total.shape[3] // 2
    blocks = []
    for x_by in range(2):
        for tensor_by in range(2):
            block = lax.dynamic_index_in_dim(total, x ^ x_by, 1, keepdims=False)
            start = (tensor ^ tensor_by) * columns
            blocks.append(lax.dynamic_slice_in_dim(block, start, columns, 2))
    return blocks


def rotary_tables(position):
    halfway = HEAD_SIZE // 2
    inverse = jnp.exp(
        jnp.arange(halfway, dtype=F32) * (-2.0 * math.log(ROPE_BASE) / HEAD_SIZE)
    )
    angles = position.astype(F32)[:, None] * inverse[None, :]
    cosine, sine = jnp.cos(angles), jnp.sin(angles)
    return (
        jnp.concatenate([cosine, cosine], axis=1),
        jnp.concatenate([-sine, sine], axis=1),
    )


def norm_factor(value_rows):
    return lax.rsqrt(jnp.mean(value_rows * value_rows, axis=-1, keepdims=True) + EPSILON)


def norm_back(value_rows, factor, gain, upstream):
    weighted = upstream * gain
    return factor * weighted - value_rows * (factor * factor * factor) * jnp.mean(
        weighted * value_rows, axis=-1, keepdims=True
    )


def dot(a, b, dims):
    return lax.dot_general(a, b, (dims, ((), ())), preferred_element_type=F32)


VMEM_LIMIT = 60 * 1024 * 1024
LIGHT = pl.CostEstimate(flops=1000, bytes_accessed=1000, transcendentals=0)
FROM_LAST = (((1,), (1,)), ((), ()))
PLAIN = (((1,), (0,)), ((), ()))


def mxu(a, b, dims=PLAIN):
    return lax.dot_general(a, b, dims, preferred_element_type=F32)


def turn(rows, cosine, sine):
    return rows * cosine + pltpu.roll(rows, HEAD_SIZE // 2, 1) * sine


def project_kernel(rows_ref, weight_ref, cosine_ref, sine_ref, out_ref, *, turned):
    product = mxu(rows_ref[...], weight_ref[...])
    for at, turns in enumerate(turned):
        part = product[:, at * HEAD_SIZE : (at + 1) * HEAD_SIZE]
        if turns:
            part = turn(part, cosine_ref[...], sine_ref[...])
        out_ref[:, at * HEAD_SIZE : (at + 1) * HEAD_SIZE] = part.astype(BF16)


def project(rows, weight, cosine, sine, first, count, turned):
    high, width = rows.shape
    columns = len(turned) * HEAD_SIZE
    return pl.pallas_call(
        functools.partial(project_kernel, turned=turned),
        grid=(count,),
        in_specs=[
            pl.BlockSpec((high, width), lambda j: (0, 0)),
            pl.BlockSpec((width, columns), lambda j: (0, first + j)),
            pl.BlockSpec((high, HEAD_SIZE), lambda j: (0, 0)),
            pl.BlockSpec((high, HEAD_SIZE), lambda j: (0, 0)),
        ],
        out_specs=pl.BlockSpec((high, columns), lambda j: (0, j)),
        out_shape=jax.ShapeDtypeStruct((high, count * columns), BF16),
        compiler_params=pltpu.CompilerParams(vmem_limit_bytes=VMEM_LIMIT),
        cost_estimate=LIGHT,
        name="project",
    )(rows, weight, cosine, sine)


def mask_bias(place_ref, segment_key_ref, segment_query_ref, bias_ref, seq_len):
    span, rows = bias_ref.shape
    start = place_ref[0]
    key_at = lax.broadcasted_iota(jnp.int32, (span, rows), 0)
    query_at = lax.broadcasted_iota(jnp.int32, (span, rows), 1) + ATTEND_SPAN
    distance = query_at - key_at
    position = start + query_at - ATTEND_SPAN
    sequence_at = query_at - lax.rem(position, seq_len)
    allowed = (distance >= 0) & (distance < ATTEND_SPAN) & (key_at >= sequence_at)
    allowed = allowed & (segment_key_ref[...] == segment_query_ref[...])
    bias_ref[...] = jnp.where(allowed, 0.0, -1e30)


def attention_kernel(
    place_ref,
    segment_key_ref,
    segment_query_ref,
    q_ref,
    kv_ref,
    heads_ref,
    lse_ref,
    bias_ref,
    *,
    seq_len,
    scale,
):
    @pl.when(pl.program_id(0) == 0)
    def _():
        mask_bias(place_ref, segment_key_ref, segment_query_ref, bias_ref, seq_len)

    rows = q_ref.shape[0]
    span = kv_ref.shape[0]
    count = q_ref.shape[1] // HEAD_SIZE
    value_t = kv_ref[:, HEAD_SIZE:].T
    chunks = span // rows
    for head in range(count):
        columns = slice(head * HEAD_SIZE, (head + 1) * HEAD_SIZE)
        query = q_ref[:, columns]
        scores = []
        for c in range(chunks):
            part = slice(c * rows, (c + 1) * rows)
            raw = mxu(kv_ref[part, :HEAD_SIZE], query, FROM_LAST)
            scores.append(raw * scale + bias_ref[part, :])
        top = functools.reduce(jnp.maximum, scores)
        top = jnp.max(top, axis=0, keepdims=True)
        total = jnp.zeros_like(top)
        out_t = jnp.zeros((HEAD_SIZE, rows), F32)
        for c in range(chunks):
            weight = jnp.exp(scores[c] - top)
            total = total + jnp.sum(weight, axis=0, keepdims=True)
            out_t = out_t + mxu(value_t[:, c * rows : (c + 1) * rows], weight.astype(BF16))
        heads_ref[:, columns] = (out_t / total).T.astype(BF16)
        lse_ref[0, head : head + 1, :] = top + jnp.log(total)


def attention(place, segment_key, segment_query, queries, key_value, seq_len):
    rows, all_columns = queries.shape
    span = key_value.shape[0]
    pairs = key_value.shape[1] // (2 * HEAD_SIZE)
    columns = all_columns // pairs
    return pl.pallas_call(
        functools.partial(attention_kernel, seq_len=seq_len, scale=1.0 / math.sqrt(HEAD_SIZE)),
        grid=(pairs,),
        in_specs=[
            pl.BlockSpec(memory_space=pltpu.SMEM),
            pl.BlockSpec((span, 1), lambda j: (0, 0)),
            pl.BlockSpec((1, rows), lambda j: (0, 0)),
            pl.BlockSpec((rows, columns), lambda j: (0, j)),
            pl.BlockSpec((span, 2 * HEAD_SIZE), lambda j: (0, j)),
        ],
        out_specs=[
            pl.BlockSpec((rows, columns), lambda j: (0, j)),
            pl.BlockSpec((1, columns // HEAD_SIZE, rows), lambda j: (j, 0, 0)),
        ],
        out_shape=[
            jax.ShapeDtypeStruct((rows, all_columns), BF16),
            jax.ShapeDtypeStruct((pairs, columns // HEAD_SIZE, rows), F32),
        ],
        scratch_shapes=[pltpu.VMEM((span, rows), F32)],
        compiler_params=pltpu.CompilerParams(vmem_limit_bytes=VMEM_LIMIT),
        cost_estimate=LIGHT,
        name="attention",
    )(place, segment_key, segment_query, queries, key_value)


def attention_back_kernel(
    place_ref,
    segment_key_ref,
    segment_query_ref,
    q_ref,
    kv_ref,
    lse_ref,
    dout_ref,
    cosine_ref,
    sine_ref,
    dq_ref,
    dkv_far_ref,
    dkv_own_ref,
    bias_ref,
    dkv_ref,
    *,
    seq_len,
    scale,
):
    @pl.when(pl.program_id(0) == 0)
    def _():
        mask_bias(place_ref, segment_key_ref, segment_query_ref, bias_ref, seq_len)

    rows = q_ref.shape[0]
    span = kv_ref.shape[0]
    count = q_ref.shape[1] // HEAD_SIZE
    key_t = kv_ref[:, :HEAD_SIZE].T
    chunks = span // rows
    dkv_ref[...] = jnp.zeros_like(dkv_ref)
    for head in range(count):
        columns = slice(head * HEAD_SIZE, (head + 1) * HEAD_SIZE)
        query = q_ref[:, columns]
        dout = dout_ref[:, columns]
        lse = lse_ref[0, head : head + 1, :]
        probs, dprobs = [], []
        row_dot = jnp.zeros_like(lse)
        for c in range(chunks):
            part = slice(c * rows, (c + 1) * rows)
            raw = mxu(kv_ref[part, :HEAD_SIZE], query, FROM_LAST)
            prob = jnp.exp(raw * scale + bias_ref[part, :] - lse)
            dprob = mxu(kv_ref[part, HEAD_SIZE:], dout, FROM_LAST)
            row_dot = row_dot + jnp.sum(prob * dprob, axis=0, keepdims=True)
            probs.append(prob)
            dprobs.append(dprob)
        dq_t = jnp.zeros((HEAD_SIZE, rows), F32)
        for c in range(chunks):
            part = slice(c * rows, (c + 1) * rows)
            dscore = (probs[c] * (dprobs[c] - row_dot)).astype(BF16)
            dkv_ref[part, :HEAD_SIZE] += mxu(dscore, query)
            dkv_ref[part, HEAD_SIZE:] += mxu(probs[c].astype(BF16), dout)
            dq_t = dq_t + mxu(key_t[:, part], dscore)
        dq_ref[:, columns] = turn(dq_t.T * scale, cosine_ref[...], -sine_ref[...]).astype(BF16)
    dkv_ref[:, :HEAD_SIZE] = dkv_ref[:, :HEAD_SIZE] * scale
    dkv_far_ref[...] = dkv_ref[: span - rows, :].astype(BF16)
    dkv_own_ref[...] = dkv_ref[span - rows :, :]


def attention_back(
    place, segment_key, segment_query, queries, key_value, lse, dout, cosine, sine, seq_len
):
    rows, all_columns = queries.shape
    span = key_value.shape[0]
    pairs = key_value.shape[1] // (2 * HEAD_SIZE)
    columns = all_columns // pairs
    return pl.pallas_call(
        functools.partial(
            attention_back_kernel, seq_len=seq_len, scale=1.0 / math.sqrt(HEAD_SIZE)
        ),
        grid=(pairs,),
        in_specs=[
            pl.BlockSpec(memory_space=pltpu.SMEM),
            pl.BlockSpec((span, 1), lambda j: (0, 0)),
            pl.BlockSpec((1, rows), lambda j: (0, 0)),
            pl.BlockSpec((rows, columns), lambda j: (0, j)),
            pl.BlockSpec((span, 2 * HEAD_SIZE), lambda j: (0, j)),
            pl.BlockSpec((1, columns // HEAD_SIZE, rows), lambda j: (j, 0, 0)),
            pl.BlockSpec((rows, columns), lambda j: (0, j)),
            pl.BlockSpec((rows, HEAD_SIZE), lambda j: (0, 0)),
            pl.BlockSpec((rows, HEAD_SIZE), lambda j: (0, 0)),
        ],
        out_specs=[
            pl.BlockSpec((rows, columns), lambda j: (0, j)),
            pl.BlockSpec((span - rows, 2 * HEAD_SIZE), lambda j: (0, j)),
            pl.BlockSpec((rows, 2 * HEAD_SIZE), lambda j: (0, j)),
        ],
        out_shape=[
            jax.ShapeDtypeStruct((rows, all_columns), BF16),
            jax.ShapeDtypeStruct((span - rows, key_value.shape[1]), BF16),
            jax.ShapeDtypeStruct((rows, key_value.shape[1]), F32),
        ],
        scratch_shapes=[
            pltpu.VMEM((span, rows), F32),
            pltpu.VMEM((span, 2 * HEAD_SIZE), F32),
        ],
        compiler_params=pltpu.CompilerParams(vmem_limit_bytes=VMEM_LIMIT),
        cost_estimate=pl.CostEstimate(
            flops=100_000_000_000, bytes_accessed=10_000_000, transcendentals=0
        ),
        name="attention_back",
    )(place, segment_key, segment_query, queries, key_value, lse, dout, cosine, sine)


def expert_kernel(
    slot_row_ref,
    slot_column_ref,
    routed_ref,
    own_ref,
    router_ref,
    tokens_ref,
    cotangent_ref,
    gate_ref,
    up_ref,
    down_ref,
    grad_ref,
    moe_ref,
    rows_in_ref,
    grad_out_ref,
    hidden_ref,
    grad_gate_ref,
    grad_up_ref,
    router_grad_ref,
    gate_full_ref,
    up_full_ref,
    down_full_ref,
    *,
    capacity,
):
    whole = ((gate_ref, gate_full_ref), (up_ref, up_full_ref), (down_ref, down_full_ref))

    @pl.when(pl.program_id(0) == 0)
    def _():
        for held, full in whole:
            columns = held.shape[3]
            for half in range(held.shape[1]):
                full[:, half * columns : (half + 1) * columns] = held[:, half].reshape(-1, columns)

    group_rows = tokens_ref.shape[1]
    tokens = tokens_ref[0]
    gate_weight, up_weight, down_weight = (full[...] for _, full in whole)
    cotangent = cotangent_ref[0]
    routed = routed_ref[0] > 0.0
    logits = jnp.where(routed, mxu(router_ref[...], tokens, FROM_LAST), -1e30)
    weights = jnp.exp(logits - jnp.max(logits, axis=0, keepdims=True))
    weights = jnp.where(routed, weights, 0.0)
    gates = weights / jnp.sum(weights, axis=0, keepdims=True)
    own = own_ref[...]
    gate_own = jnp.sum(gates * own, axis=0, keepdims=True)
    place = slot_row_ref[0] == lax.broadcasted_iota(jnp.int32, (capacity, group_rows), 0)
    place_wide = jnp.where(place, 1.0, 0.0)
    place_low = place_wide.astype(BF16)
    back = slot_column_ref[0] == lax.broadcasted_iota(jnp.int32, (group_rows, capacity), 1)
    back_low = jnp.where(back, 1.0, 0.0).astype(BF16)
    coefficient = jnp.sum(place_wide * gate_own, axis=1, keepdims=True)

    rows_in = mxu(place_low, tokens).astype(BF16)
    rows_in_ref[...] = rows_in
    gate_pre = mxu(rows_in, gate_weight)
    up_pre = mxu(rows_in, up_weight)
    sigmoid = 1.0 / (1.0 + jnp.exp(-gate_pre))
    silu = gate_pre * sigmoid
    hidden = (silu * up_pre).astype(BF16)
    hidden_ref[...] = hidden
    slot_cotangent = mxu(place_low, cotangent)
    grad_out = (coefficient * slot_cotangent).astype(BF16)
    grad_out_ref[...] = grad_out
    grad_hidden = mxu(grad_out, down_weight)
    grad_up = (grad_hidden * silu).astype(BF16)
    grad_gate = (grad_hidden * up_pre * sigmoid * (1.0 + gate_pre * (1.0 - sigmoid))).astype(BF16)
    grad_up_ref[...] = grad_up
    grad_gate_ref[...] = grad_gate
    expert_out = mxu(hidden, down_weight, FROM_LAST)
    grad_slot = jnp.sum(slot_cotangent * expert_out, axis=1, keepdims=True)
    moe_ref[0] = mxu(back_low, (coefficient * expert_out).astype(BF16)).astype(BF16)

    grad_token = jnp.sum(place_wide * grad_slot, axis=0, keepdims=True)
    share = (grad_token * gate_own) * (own - gates)
    share_high = share.astype(BF16)
    share_low = (share - share_high.astype(F32)).astype(BF16)
    router_grad = mxu(share_high, tokens) + mxu(share_low, tokens)

    @pl.when(pl.program_id(0) == 0)
    def _():
        router_grad_ref[...] = router_grad

    @pl.when(pl.program_id(0) > 0)
    def _():
        router_grad_ref[...] += router_grad

    grad_in = mxu(grad_gate, gate_weight, FROM_LAST) + mxu(grad_up, up_weight, FROM_LAST)
    grad_ref[0] = (
        mxu(back_low, grad_in.astype(BF16)) + mxu(share.T.astype(BF16), router_ref[...])
    ).astype(BF16)


def expert_groups(slot, routed, own, router_t, tokens, cotangent, weights, capacity):
    count, group_rows, width = tokens.shape
    ff = weights[0].shape[1] * weights[0].shape[3]
    experts = router_t.shape[0]
    weight = pl.BlockSpec(
        weights[0].shape, lambda g: (0, 0, 0, 0), pipeline_mode=pl.Buffered(1)
    )
    whole = lambda g: (0, 0)
    by_group = lambda g: (g, 0, 0)
    slots = lambda columns: pl.BlockSpec((capacity, columns), lambda g: (g, 0))
    slots_shape = lambda columns: jax.ShapeDtypeStruct((count * capacity, columns), BF16)
    return pl.pallas_call(
        functools.partial(expert_kernel, capacity=capacity),
        grid=(count,),
        in_specs=[
            pl.BlockSpec((1, 1, group_rows), by_group),
            pl.BlockSpec((1, group_rows, 1), by_group),
            pl.BlockSpec((1, experts, group_rows), by_group),
            pl.BlockSpec((experts, 1), whole),
            pl.BlockSpec((experts, width), whole),
            pl.BlockSpec((1, group_rows, width), by_group),
            pl.BlockSpec((1, group_rows, width), by_group),
            weight,
            weight,
            weight,
        ],
        out_specs=[
            pl.BlockSpec((1, group_rows, width), by_group),
            pl.BlockSpec((1, group_rows, width), by_group),
            slots(width),
            slots(width),
            slots(ff),
            slots(ff),
            slots(ff),
            pl.BlockSpec((experts, width), whole),
        ],
        out_shape=[
            jax.ShapeDtypeStruct(tokens.shape, BF16),
            jax.ShapeDtypeStruct(tokens.shape, BF16),
            slots_shape(width),
            slots_shape(width),
            slots_shape(ff),
            slots_shape(ff),
            slots_shape(ff),
            jax.ShapeDtypeStruct((experts, width), F32),
        ],
        scratch_shapes=[pltpu.VMEM((width, ff), BF16) for _ in range(3)],
        compiler_params=pltpu.CompilerParams(vmem_limit_bytes=VMEM_LIMIT),
        cost_estimate=LIGHT,
        name="expert",
    )(
        slot[:, None, :],
        slot[:, :, None],
        routed,
        own,
        router_t,
        tokens,
        cotangent,
        *weights,
    )


def weight_grad_kernel(*refs, halves):
    rows, grad_out, hidden, grad_gate, grad_up, router = (
        refs[at : at + 2] for at in range(0, 12, 2)
    )
    moe_kept_ref, moe_got_ref, out_ref = refs[12:15]
    for at, moe_ref in enumerate(refs[15:]):
        moe_ref[...] = (moe_kept_ref[at].astype(F32) + moe_got_ref[at].astype(F32)).astype(BF16)
    columns = hidden[0].shape[1] // halves
    over = (((0,), (0,)), ((), ()))
    left_rows = [ref[...] for ref in rows]
    left_out = [ref[...] for ref in grad_out]
    router_columns = (router[0][...] + router[1][...]).T
    router_columns = jnp.concatenate(
        [
            router_columns,
            jnp.zeros((router_columns.shape[0], HEAD_SIZE - router_columns.shape[1]), F32),
        ],
        axis=1,
    ).astype(BF16)
    for half in range(halves):
        start = half * (3 * columns + HEAD_SIZE)
        part = slice(half * columns, (half + 1) * columns)
        for at, (left, right) in enumerate(
            ((left_rows, grad_gate), (left_rows, grad_up), (left_out, hidden))
        ):
            total = mxu(left[0], right[0][:, part], over) + mxu(left[1], right[1][:, part], over)
            out_ref[:, start + at * columns : start + (at + 1) * columns] = total.astype(BF16)
        out_ref[:, start + 3 * columns : start + 3 * columns + HEAD_SIZE] = router_columns


def weight_grads(near, far, moe_kept, moe_got, halves, block=256):
    rows_at, grad_out_at, hidden_at, grad_gate_at, grad_up_at, router_at = range(6)
    slots, width = near[rows_at].shape
    ff = near[hidden_at].shape[1]
    experts = near[router_at].shape[0]
    specs, operands = [], []
    for at in (rows_at, grad_out_at, hidden_at, grad_gate_at, grad_up_at, router_at):
        if at in (rows_at, grad_out_at):
            spec = pl.BlockSpec((slots, block), lambda i: (0, i))
        elif at == router_at:
            spec = pl.BlockSpec((experts, block), lambda i: (0, i))
        else:
            spec = pl.BlockSpec((slots, ff), lambda i: (0, 0))
        specs += [spec, spec]
        operands += [near[at], far[at]]
    columns = 3 * ff + halves * HEAD_SIZE
    moe_count, moe_rows, _ = moe_kept.shape
    moe_spec = pl.BlockSpec((moe_count, moe_rows, block), lambda i: (0, 0, i))
    moe_out_spec = pl.BlockSpec((moe_rows, block), lambda i: (0, i))
    return pl.pallas_call(
        functools.partial(weight_grad_kernel, halves=halves),
        grid=(width // block,),
        in_specs=specs + [moe_spec, moe_spec],
        out_specs=[pl.BlockSpec((block, columns), lambda i: (i, 0))] + [moe_out_spec] * moe_count,
        out_shape=[jax.ShapeDtypeStruct((width, columns), BF16)]
        + [jax.ShapeDtypeStruct((moe_rows, width), BF16)] * moe_count,
        compiler_params=pltpu.CompilerParams(vmem_limit_bytes=VMEM_LIMIT),
        cost_estimate=pl.CostEstimate(
            flops=15_000_000_000, bytes_accessed=50_000_000, transcendentals=0
        ),
        name="weight_grads",
    )(*operands, moe_kept, moe_got)


def on_device(
    block_input,
    norm_gains,
    router_weight,
    query_matrix,
    key_matrix,
    value_matrix,
    output_weight,
    gate_weight,
    up_weight,
    down_weight,
    segment_ids,
    routes,
    priority,
    cotangent,
):
    tensor_index = lax.axis_index("tensor")
    own_rows, width = block_input.shape
    group_rows = segment_ids.shape[0]
    halves = lax.axis_size("tensor")
    outer = lax.axis_size("outer")
    groups = lax.axis_size("x") * lax.axis_size("core")
    plane = groups * halves
    shard_rows = query_matrix.shape[0]
    dp_size = outer * groups
    seq_len = min(SEQ_MOST, group_rows * dp_size)
    own_start = lax.axis_index(ALL) * own_rows
    capacity = group_rows * TOPK // EXPERTS
    reach = ATTEND_SPAN // own_rows
    half_ff = gate_weight.shape[2]
    ff = half_ff * halves

    query_columns = query_matrix.shape[1]
    pair_columns = 2 * halves * HEAD_SIZE
    first = tensor_index == 0
    key_value_weight = jnp.concatenate([key_matrix, value_matrix], axis=1)
    other_weight = swap(key_value_weight, "tensor")
    early = jnp.concatenate(
        [
            jnp.where(first, key_value_weight, other_weight),
            jnp.where(first, other_weight, key_value_weight),
            query_matrix,
            output_weight,
        ],
        axis=1,
    )
    early, gate_own, up_own, down_own, cotangent_own = lax.optimization_barrier(
        (early, gate_weight, up_weight, down_weight, cotangent)
    )
    early = outer_gather(early)

    expert_shard = jnp.transpose(jnp.stack([gate_own, up_own, down_own]), (2, 0, 1, 3))
    expert_shard = lax.all_to_all(expert_shard, PLANE, 0, 0, tiled=True)
    expert_shard = expert_shard.reshape(groups, halves, 3, shard_rows, half_ff)
    expert_shard = [
        jnp.swapaxes(expert_shard[:, :, at], 0, 1).reshape(-1, half_ff) for at in range(3)
    ]
    early, expert_shard, segment_here, priority_here = lax.optimization_barrier(
        (early, expert_shard, segment_ids, priority)
    )
    pair_count = group_rows * TOPK
    rank = (
        jnp.zeros((pair_count,), jnp.int32)
        .at[priority_here]
        .set(jnp.arange(pair_count, dtype=jnp.int32))
        .reshape(group_rows, TOPK)
    )
    expert_ids = jnp.arange(EXPERTS, dtype=jnp.int32)
    named = routes[:, :, None] == expert_ids[None, None, :]
    ranked = jnp.sum(jnp.where(named, rank[:, :, None] + 1, 0), axis=1)
    ranked = jnp.where(ranked > 0, ranked, pair_count + 1)
    ranked_own = lax.dynamic_slice_in_dim(ranked, tensor_index * own_rows, own_rows, 0)
    digits = jnp.concatenate([ranked_own // 64, ranked_own % 64], axis=1).astype(BF16)
    digits = jnp.pad(digits, ((0, 0), (0, HEAD_SIZE - digits.shape[1])))
    cotangent_sent = jnp.concatenate([cotangent_own, digits], axis=1)
    segment_near = jnp.concatenate(
        [shift_groups(segment_here, 2), shift_groups(segment_here, 1), segment_here]
    )
    expert_full = [
        lax.all_gather(shard, "outer").reshape(outer, halves, groups * shard_rows, half_ff)
        for shard in expert_shard
    ]

    key_value_full = early[:, :, :pair_columns]
    key_value_full = in_order(key_value_full, swap(key_value_full, "x"), "x", 1)
    key_value_full = in_order(key_value_full, swap(key_value_full, "core"), "core", 2)
    key_value_full = key_value_full.reshape(width, pair_columns)
    query_parts = plane_parts(early[:, :, pair_columns : pair_columns + query_columns])

    input_wide = block_input.astype(F32)
    first_gain = norm_gains[:, 0]
    second_gain = norm_gains[:, 1]
    first_factor = norm_factor(input_wide)
    normed_in = (input_wide * first_factor * first_gain).astype(BF16)
    positions = own_start + jnp.arange(own_rows, dtype=jnp.int32)
    cosine, sine = rotary_tables(positions % seq_len)
    query_blocks = halves * query_columns // (2 * HEAD_SIZE)
    key_value_sent = project(
        normed_in, key_value_full, cosine, sine, 0, halves, (True, False)
    )
    one_back, two_back = shift_groups(key_value_sent, 1), shift_groups(key_value_sent, 2)
    query_parts, one_back, two_back, segment_near, cotangent_sent, expert_full[0] = (
        lax.optimization_barrier(
            (query_parts, one_back, two_back, segment_near, cotangent_sent, expert_full[0])
        )
    )
    cotangent_parts = plane_parts(cotangent_sent)
    output_own = early[:, :, pair_columns + query_columns :]
    pair_sent = jnp.where(
        first,
        jnp.stack([one_back, key_value_sent]),
        jnp.stack([two_back, one_back]),
    )
    pair_got = swap(pair_sent, "tensor")
    query_near = plane_stack(query_parts)
    query_far, pair_got = lax.optimization_barrier((swap(query_near, "core"), pair_got))
    pieces = [two_back, pair_got[0], one_back, pair_got[1], key_value_sent]
    query_full = whole_weight(query_near, query_far)
    queries = project(normed_in, query_full, cosine, sine, 0, query_blocks, (True, True))
    output_parts = plane_parts(output_own)
    expert = lax.axis_index(PLANE)

    def slots_of(cotangents):
        digits = cotangents[..., width:].reshape(2, group_rows, HEAD_SIZE).astype(jnp.int32)
        ranked_all = digits[..., :EXPERTS] * 64 + digits[..., EXPERTS : 2 * EXPERTS]
        routed = jnp.swapaxes((ranked_all <= pair_count).astype(F32), 1, 2)
        rank_own = jnp.sum(jnp.where(expert_ids == expert, ranked_all, 0), axis=-1)
        earlier = (rank_own[:, None, :] < rank_own[:, :, None]).astype(jnp.int32)
        slot = jnp.where(rank_own <= pair_count, jnp.sum(earlier, axis=-1), capacity)
        return slot, routed

    key_value = jnp.concatenate(pieces, axis=0)
    span = ATTEND_SPAN + own_rows
    segment_ext = lax.dynamic_slice_in_dim(segment_near, tensor_index * own_rows, span)
    view = (
        jnp.reshape(own_start, (1,)),
        segment_ext[:, None],
        segment_ext[None, ATTEND_SPAN:],
        queries,
        key_value,
    )
    heads_low, log_total = attention(*view, seq_len)
    heads_late, output_parts, cotangent_parts = lax.optimization_barrier(
        (heads_low, output_parts, cotangent_parts)
    )
    output_near = plane_stack(output_parts)
    output_far = swap(output_near, "core")
    output_full, expert_full[1] = lax.optimization_barrier(
        (whole_weight(output_near, output_far), expert_full[1])
    )
    hidden_state = input_wide + dot(heads_low, output_full, ((1,), (1,)))
    second_factor = norm_factor(hidden_state)
    normed_mid_own = (hidden_state * second_factor * second_gain).astype(BF16)

    cotangent_near = plane_stack(cotangent_parts)
    cotangent_far = swap(cotangent_near, "core")
    near_slots, far_slots = slots_of(cotangent_near), slots_of(cotangent_far)
    normed_parts, near_slots, far_slots, expert_full[2] = lax.optimization_barrier(
        (plane_parts(normed_mid_own), near_slots, far_slots, expert_full[2])
    )
    normed_near = plane_stack(normed_parts)
    normed_far = swap(normed_near, "core")
    own_expert = (expert_ids == expert).astype(F32)[:, None]
    router_t = router_weight.T

    def experts_on(tokens, cotangents, slots):
        slot, routed = slots
        return expert_groups(
            slot,
            routed,
            own_expert,
            router_t,
            tokens.reshape(2, group_rows, width),
            cotangents.reshape(2, group_rows, -1),
            expert_full,
            capacity,
        )

    on_near = experts_on(normed_near, cotangent_near, near_slots)
    on_far = experts_on(normed_far, cotangent_far, far_slots)
    blocks = (2 * halves, own_rows, width)
    (grad_near, moe_near), (grad_far, moe_far) = (
        [array.reshape(blocks) for array in side[:2]] for side in (on_near, on_far)
    )
    grad_blocks = fold_blocks(grad_near, swap(grad_far, "core"))
    grad_blocks, moe_far, on_near, on_far = lax.optimization_barrier(
        (grad_blocks, moe_far, on_near[2:], on_far[2:])
    )
    grad_mid_parts = fold_plane(grad_blocks)
    expert_part, *moe_blocks = weight_grads(
        on_near, on_far, moe_near, swap(moe_far, "core"), halves
    )
    expert_sum = lax.psum_scatter(expert_part, "outer", scatter_dimension=0, tiled=True)
    grad_mid_parts, moe_blocks = lax.optimization_barrier((grad_mid_parts, moe_blocks))
    moe_parts = fold_plane(moe_blocks)
    grad_mid = wide_sum(grad_mid_parts)

    norm_input_part = norm_back(hidden_state, second_factor, second_gain, grad_mid)
    grad_state = cotangent.astype(F32) + norm_input_part
    grad_attn = grad_state.astype(BF16)
    grad_heads = dot(grad_attn, output_full, ((1,), (0,))).astype(BF16)
    output_total = fold_columns(grad_attn, heads_late, shard_rows)
    grad_query_pre, grad_far_kv, grad_own = attention_back(
        *view, log_total, grad_heads, cosine, sine, seq_len
    )
    grad_query_pre, output_total, moe_parts = lax.optimization_barrier(
        (grad_query_pre, output_total, moe_parts)
    )
    output_parts = fold_plane(distance_blocks(output_total))
    query_total = fold_columns(normed_in, grad_query_pre, shard_rows)
    two_back, pair_old, one_back, pair_new = grad_far_kv.reshape(reach, own_rows, -1)
    pair_got, output_parts, query_total = lax.optimization_barrier(
        (swap(jnp.stack([pair_old, pair_new]), "tensor"), output_parts, query_total)
    )
    query_parts = fold_plane(distance_blocks(query_total))
    pair_old, pair_new = pair_got.astype(F32)
    one_back = one_back.astype(F32) + jnp.where(first, pair_old, pair_new)
    two_back = two_back.astype(F32) + jnp.where(first, 0.0, pair_old)
    grad_own = grad_own + jnp.where(first, pair_new, 0.0)
    grad_own = grad_own + shift_groups(one_back.astype(BF16), -1).astype(F32)
    grad_own = grad_own + shift_groups(two_back.astype(BF16), -2).astype(F32)
    query_parts, output_parts, expert_sum = lax.optimization_barrier(
        (query_parts, output_parts, expert_sum)
    )
    output_weight_grad = outer_scatter(wide_sum(output_parts).astype(BF16))
    grad_key_value = []
    for half in range(halves):
        start = half * 2 * HEAD_SIZE
        key_part = grad_own[:, start : start + HEAD_SIZE]
        turned = jnp.concatenate(
            [key_part[:, HEAD_SIZE // 2 :], key_part[:, : HEAD_SIZE // 2]], axis=1
        )
        grad_key_value.append(key_part * cosine - turned * sine)
        grad_key_value.append(grad_own[:, start + HEAD_SIZE : start + 2 * HEAD_SIZE])
    grad_key_value_pre = jnp.concatenate(grad_key_value, axis=1).astype(BF16)
    key_value_total = fold_columns(normed_in, grad_key_value_pre, shard_rows)
    key_value_parts = fold_plane(distance_blocks(key_value_total))
    grad_in = dot(grad_query_pre, query_full, ((1,), (1,))) + dot(
        grad_key_value_pre, key_value_full, ((1,), (1,))
    )
    input_grad = grad_state + norm_back(input_wide, first_factor, first_gain, grad_in)
    qkv_grad = outer_scatter(
        jnp.concatenate([wide_sum(query_parts), wide_sum(key_value_parts)], axis=2).astype(BF16)
    )
    block_output = hidden_state + wide_sum(moe_parts)
    expert_sum = expert_sum.reshape(groups, shard_rows, halves, -1)
    expert_sum = jnp.swapaxes(expert_sum, 1, 2).reshape(plane, shard_rows, -1)
    expert_sum = lax.all_to_all(expert_sum, PLANE, 0, 0, tiled=True)
    gate_grad, up_grad, down_grad = (
        jnp.swapaxes(expert_sum[:, :, at * half_ff : (at + 1) * half_ff], 0, 1).astype(F32)
        for at in range(3)
    )
    router_grad = jnp.sum(expert_sum[:, :, 3 * half_ff : 3 * half_ff + EXPERTS].astype(F32), axis=0)
    router_grad = lax.dynamic_slice_in_dim(
        router_grad, tensor_index * (shard_rows // 2), shard_rows // 2, 0
    )
    query_grad = qkv_grad[:, :query_columns]
    key_grad = qkv_grad[:, query_columns : query_columns + HEAD_SIZE]
    value_grad = qkv_grad[:, query_columns + HEAD_SIZE :]

    half_rows = shard_rows // 2
    own_gains = lax.dynamic_slice_in_dim(
        norm_gains, lax.axis_index(DP) * shard_rows, shard_rows, 0
    )
    qkv_own = jnp.concatenate([query_matrix, key_value_weight], axis=1)
    first_sum = jnp.sum(qkv_grad * qkv_own.astype(F32), axis=-1)
    second_sum = jnp.sum(
        gate_grad * gate_weight.astype(F32) + up_grad * up_weight.astype(F32), axis=(1, 2)
    )
    gain_sums = jnp.stack([first_sum, second_sum], axis=1) / own_gains
    kept = lax.dynamic_slice_in_dim(gain_sums, tensor_index * half_rows, half_rows, 0)
    sent = lax.dynamic_slice_in_dim(gain_sums, (1 - tensor_index) * half_rows, half_rows, 0)
    own_router = lax.dynamic_slice_in_dim(
        router_weight, lax.axis_index(ALL) * half_rows, half_rows, 0
    )
    router_sum = jnp.sum(router_grad * own_router.astype(F32), axis=-1)
    half_gains = lax.dynamic_slice_in_dim(own_gains, tensor_index * half_rows, half_rows, 0)
    router_sum = router_sum / half_gains[:, 1]
    gains_grad = (
        kept
        + swap(sent, "tensor")
        + jnp.stack([jnp.zeros_like(router_sum), router_sum], axis=1)
    )
    return (
        block_output,
        input_grad,
        gains_grad,
        router_grad,
        query_grad,
        key_grad,
        value_grad,
        output_weight_grad,
        gate_grad,
        up_grad,
        down_grad,
    )


def solution(mesh):
    dp_size, tensor_size = mesh.shape["dp"], mesh.shape["tensor"]
    split = Mesh(mesh.devices.reshape(dp_size // 4, 2, 2, tensor_size), ALL)
    return jax.shard_map(
        on_device,
        mesh=split,
        in_specs=(
            P(ALL, None),
            P(),
            P(),
            P(DP, "tensor"),
            P(DP, "tensor"),
            P(DP, "tensor"),
            P(DP, "tensor"),
            P(DP, None, "tensor"),
            P(DP, None, "tensor"),
            P(DP, None, "tensor"),
            P(DP),
            P(DP, None),
            P(DP),
            P(ALL, None),
        ),
        out_specs=(
            P(ALL, None),
            P(ALL, None),
            P(ALL, None),
            P(ALL, None),
            P(DP, "tensor"),
            P(DP, "tensor"),
            P(DP, "tensor"),
            P(DP, "tensor"),
            P(DP, None, "tensor"),
            P(DP, None, "tensor"),
            P(DP, None, "tensor"),
        ),
        check_vma=False,
    )
```

```python
import functools
import math

import jax
import jax.numpy as jnp
from jax import lax
from jax.experimental import pallas as pl
from jax.experimental.pallas import tpu as pltpu
from jax.sharding import Mesh
from jax.sharding import PartitionSpec as P

HEAD_SIZE = 128
TOPK = 4
EXPERTS = 8
ATTEND_SPAN = 1024
SEQ_MOST = 16384
EPSILON = 1e-06
ROPE_BASE = 10000.0
BF16 = jnp.bfloat16
F32 = jnp.float32

DP = ("outer", "x", "core")
PLANE = ("x", "core", "tensor")
ALL = ("outer", "x", "core", "tensor")


def shift_groups(x, by):
    length = lax.axis_size(DP)
    return lax.ppermute(x, DP, [(i, i + by) for i in range(length) if 0 <= i + by < length])


def swap(x, axis):
    length = lax.axis_size(axis)
    return lax.ppermute(x, axis, [(i, length - 1 - i) for i in range(length)])


def plane_parts(own):
    return [own, swap(own, "tensor"), swap(own, "x"), swap(own, ("x", "tensor"))]


def plane_stack(parts):
    return jnp.stack(parts).reshape((2, 2) + parts[0].shape)


def whole_weight(near, far):
    x, tensor = lax.axis_index("x"), lax.axis_index("tensor")
    first = lax.axis_index("core") == 0
    by_core = [jnp.where(first, near, far), jnp.where(first, far, near)]

    def piece(x_at, core_at, tensor_at):
        picked = lax.dynamic_index_in_dim(by_core[core_at], x ^ x_at, 0, keepdims=False)
        return lax.dynamic_index_in_dim(picked, tensor ^ tensor_at, 0, keepdims=False)

    places = [(x_at, core_at) for x_at in range(2) for core_at in range(2)]
    halves = [jnp.stack([piece(*place, at) for place in places], 1) for at in range(2)]
    return jnp.concatenate(halves, axis=-1).reshape(-1, 2 * near.shape[-1])


def fold_core(kept, sent):
    return (kept.astype(F32) + swap(sent, "core").astype(F32)).astype(BF16)


def fold_blocks(kept, got):
    return [
        (kept[at].astype(F32) + got[at].astype(F32)).astype(BF16) for at in range(kept.shape[0])
    ]


def in_order(own, other, axis_name, axis):
    first = lax.axis_index(axis_name) == 0
    return jnp.stack([jnp.where(first, own, other), jnp.where(first, other, own)], axis)


def fold_plane(blocks):
    return [
        blocks[0],
        swap(blocks[1], "tensor"),
        swap(blocks[2], "x"),
        swap(blocks[3], ("x", "tensor")),
    ]


def wide_sum(parts):
    return sum(part.astype(F32) for part in parts)


def outer_shift(x, by):
    length = lax.axis_size("outer")
    return lax.ppermute(x, "outer", [(i, (i + by) % length) for i in range(length)])


def outer_gather(shard):
    length, here = lax.axis_size("outer"), lax.axis_index("outer")
    if length > 4:
        return lax.all_gather(shard, "outer")
    full = jnp.zeros((length,) + shard.shape, shard.dtype)
    for by in range(length):
        piece = outer_shift(shard, by) if by else shard
        full = lax.dynamic_update_slice_in_dim(full, piece[None], (here - by) % length, 0)
    return full


def outer_scatter(parts):
    length, here = lax.axis_size("outer"), lax.axis_index("outer")
    if length > 4:
        return lax.psum_scatter(parts, "outer", scatter_dimension=0, tiled=False).astype(F32)
    pieces = [
        lax.dynamic_index_in_dim(parts, (here + by) % length, 0, keepdims=False)
        for by in range(length)
    ]
    return wide_sum([pieces[0]] + [outer_shift(pieces[by], by) for by in range(1, length)])


def core_columns(rows, core_at, shard_rows):
    count = rows.shape[0]
    split = rows.reshape(count, -1, 2, shard_rows)
    return lax.dynamic_index_in_dim(split, core_at, 2, keepdims=False).reshape(count, -1)


def fold_columns(left, right, shard_rows):
    core = lax.axis_index("core")
    sent = dot(core_columns(left, 1 - core, shard_rows), right, ((0,), (0,))).astype(BF16)
    kept = dot(core_columns(left, core, shard_rows), right, ((0,), (0,))).astype(BF16)
    return fold_core(kept, sent).reshape(-1, 2, shard_rows, right.shape[1])


def distance_blocks(total):
    x, tensor = lax.axis_index("x"), lax.axis_index("tensor")
    columns = total.shape[3] // 2
    blocks = []
    for x_by in range(2):
        for tensor_by in range(2):
            block = lax.dynamic_index_in_dim(total, x ^ x_by, 1, keepdims=False)
            start = (tensor ^ tensor_by) * columns
            blocks.append(lax.dynamic_slice_in_dim(block, start, columns, 2))
    return blocks


def rotary_tables(position):
    halfway = HEAD_SIZE // 2
    inverse = jnp.exp(
        jnp.arange(halfway, dtype=F32) * (-2.0 * math.log(ROPE_BASE) / HEAD_SIZE)
    )
    angles = position.astype(F32)[:, None] * inverse[None, :]
    cosine, sine = jnp.cos(angles), jnp.sin(angles)
    return (
        jnp.concatenate([cosine, cosine], axis=1),
        jnp.concatenate([-sine, sine], axis=1),
    )


def norm_factor(value_rows):
    return lax.rsqrt(jnp.mean(value_rows * value_rows, axis=-1, keepdims=True) + EPSILON)


def norm_back(value_rows, factor, gain, upstream):
    weighted = upstream * gain
    return factor * weighted - value_rows * (factor * factor * factor) * jnp.mean(
        weighted * value_rows, axis=-1, keepdims=True
    )


def dot(a, b, dims):
    return lax.dot_general(a, b, (dims, ((), ())), preferred_element_type=F32)


VMEM_LIMIT = 60 * 1024 * 1024
LIGHT = pl.CostEstimate(flops=1000, bytes_accessed=1000, transcendentals=0)
FROM_LAST = (((1,), (1,)), ((), ()))
PLAIN = (((1,), (0,)), ((), ()))


def mxu(a, b, dims=PLAIN):
    return lax.dot_general(a, b, dims, preferred_element_type=F32)


def turn(rows, cosine, sine):
    return rows * cosine + pltpu.roll(rows, HEAD_SIZE // 2, 1) * sine


def project_kernel(rows_ref, weight_ref, cosine_ref, sine_ref, out_ref, *, turned):
    product = mxu(rows_ref[...], weight_ref[...])
    for at, turns in enumerate(turned):
        part = product[:, at * HEAD_SIZE : (at + 1) * HEAD_SIZE]
        if turns:
            part = turn(part, cosine_ref[...], sine_ref[...])
        out_ref[:, at * HEAD_SIZE : (at + 1) * HEAD_SIZE] = part.astype(BF16)


def project(rows, weight, cosine, sine, first, count, turned):
    high, width = rows.shape
    columns = len(turned) * HEAD_SIZE
    return pl.pallas_call(
        functools.partial(project_kernel, turned=turned),
        grid=(count,),
        in_specs=[
            pl.BlockSpec((high, width), lambda j: (0, 0)),
            pl.BlockSpec((width, columns), lambda j: (0, first + j)),
            pl.BlockSpec((high, HEAD_SIZE), lambda j: (0, 0)),
            pl.BlockSpec((high, HEAD_SIZE), lambda j: (0, 0)),
        ],
        out_specs=pl.BlockSpec((high, columns), lambda j: (0, j)),
        out_shape=jax.ShapeDtypeStruct((high, count * columns), BF16),
        compiler_params=pltpu.CompilerParams(vmem_limit_bytes=VMEM_LIMIT),
        cost_estimate=LIGHT,
        name="project",
    )(rows, weight, cosine, sine)


def mask_bias(place_ref, segment_key_ref, segment_query_ref, bias_ref, seq_len):
    span, rows = bias_ref.shape
    start = place_ref[0]
    key_at = lax.broadcasted_iota(jnp.int32, (span, rows), 0)
    query_at = lax.broadcasted_iota(jnp.int32, (span, rows), 1) + ATTEND_SPAN
    distance = query_at - key_at
    position = start + query_at - ATTEND_SPAN
    sequence_at = query_at - lax.rem(position, seq_len)
    allowed = (distance >= 0) & (distance < ATTEND_SPAN) & (key_at >= sequence_at)
    allowed = allowed & (segment_key_ref[...] == segment_query_ref[...])
    bias_ref[...] = jnp.where(allowed, 0.0, -1e30)


def attention_kernel(
    place_ref,
    segment_key_ref,
    segment_query_ref,
    q_ref,
    kv_ref,
    heads_ref,
    lse_ref,
    bias_ref,
    *,
    seq_len,
    scale,
):
    @pl.when(pl.program_id(0) == 0)
    def _():
        mask_bias(place_ref, segment_key_ref, segment_query_ref, bias_ref, seq_len)

    rows = q_ref.shape[0]
    span = kv_ref.shape[0]
    count = q_ref.shape[1] // HEAD_SIZE
    value_t = kv_ref[:, HEAD_SIZE:].T
    chunks = span // rows
    for head in range(count):
        columns = slice(head * HEAD_SIZE, (head + 1) * HEAD_SIZE)
        query = q_ref[:, columns]
        scores = []
        for c in range(chunks):
            part = slice(c * rows, (c + 1) * rows)
            raw = mxu(kv_ref[part, :HEAD_SIZE], query, FROM_LAST)
            scores.append(raw * scale + bias_ref[part, :])
        top = functools.reduce(jnp.maximum, scores)
        top = jnp.max(top, axis=0, keepdims=True)
        total = jnp.zeros_like(top)
        out_t = jnp.zeros((HEAD_SIZE, rows), F32)
        for c in range(chunks):
            weight = jnp.exp(scores[c] - top)
            total = total + jnp.sum(weight, axis=0, keepdims=True)
            out_t = out_t + mxu(value_t[:, c * rows : (c + 1) * rows], weight.astype(BF16))
        heads_ref[:, columns] = (out_t / total).T.astype(BF16)
        lse_ref[0, head : head + 1, :] = top + jnp.log(total)


def attention(place, segment_key, segment_query, queries, key_value, seq_len):
    rows, all_columns = queries.shape
    span = key_value.shape[0]
    pairs = key_value.shape[1] // (2 * HEAD_SIZE)
    columns = all_columns // pairs
    return pl.pallas_call(
        functools.partial(attention_kernel, seq_len=seq_len, scale=1.0 / math.sqrt(HEAD_SIZE)),
        grid=(pairs,),
        in_specs=[
            pl.BlockSpec(memory_space=pltpu.SMEM),
            pl.BlockSpec((span, 1), lambda j: (0, 0)),
            pl.BlockSpec((1, rows), lambda j: (0, 0)),
            pl.BlockSpec((rows, columns), lambda j: (0, j)),
            pl.BlockSpec((span, 2 * HEAD_SIZE), lambda j: (0, j)),
        ],
        out_specs=[
            pl.BlockSpec((rows, columns), lambda j: (0, j)),
            pl.BlockSpec((1, columns // HEAD_SIZE, rows), lambda j: (j, 0, 0)),
        ],
        out_shape=[
            jax.ShapeDtypeStruct((rows, all_columns), BF16),
            jax.ShapeDtypeStruct((pairs, columns // HEAD_SIZE, rows), F32),
        ],
        scratch_shapes=[pltpu.VMEM((span, rows), F32)],
        compiler_params=pltpu.CompilerParams(vmem_limit_bytes=VMEM_LIMIT),
        cost_estimate=LIGHT,
        name="attention",
    )(place, segment_key, segment_query, queries, key_value)


def attention_back_kernel(
    place_ref,
    segment_key_ref,
    segment_query_ref,
    q_ref,
    kv_ref,
    lse_ref,
    dout_ref,
    cosine_ref,
    sine_ref,
    dq_ref,
    dkv_far_ref,
    dkv_own_ref,
    bias_ref,
    dkv_ref,
    *,
    seq_len,
    scale,
):
    @pl.when(pl.program_id(0) == 0)
    def _():
        mask_bias(place_ref, segment_key_ref, segment_query_ref, bias_ref, seq_len)

    rows = q_ref.shape[0]
    span = kv_ref.shape[0]
    count = q_ref.shape[1] // HEAD_SIZE
    key_t = kv_ref[:, :HEAD_SIZE].T
    chunks = span // rows
    dkv_ref[...] = jnp.zeros_like(dkv_ref)
    for head in range(count):
        columns = slice(head * HEAD_SIZE, (head + 1) * HEAD_SIZE)
        query = q_ref[:, columns]
        dout = dout_ref[:, columns]
        lse = lse_ref[0, head : head + 1, :]
        probs, dprobs = [], []
        row_dot = jnp.zeros_like(lse)
        for c in range(chunks):
            part = slice(c * rows, (c + 1) * rows)
            raw = mxu(kv_ref[part, :HEAD_SIZE], query, FROM_LAST)
            prob = jnp.exp(raw * scale + bias_ref[part, :] - lse)
            dprob = mxu(kv_ref[part, HEAD_SIZE:], dout, FROM_LAST)
            row_dot = row_dot + jnp.sum(prob * dprob, axis=0, keepdims=True)
            probs.append(prob)
            dprobs.append(dprob)
        dq_t = jnp.zeros((HEAD_SIZE, rows), F32)
        for c in range(chunks):
            part = slice(c * rows, (c + 1) * rows)
            dscore = (probs[c] * (dprobs[c] - row_dot)).astype(BF16)
            dkv_ref[part, :HEAD_SIZE] += mxu(dscore, query)
            dkv_ref[part, HEAD_SIZE:] += mxu(probs[c].astype(BF16), dout)
            dq_t = dq_t + mxu(key_t[:, part], dscore)
        dq_ref[:, columns] = turn(dq_t.T * scale, cosine_ref[...], -sine_ref[...]).astype(BF16)
    dkv_ref[:, :HEAD_SIZE] = dkv_ref[:, :HEAD_SIZE] * scale
    dkv_far_ref[...] = dkv_ref[: span - rows, :].astype(BF16)
    dkv_own_ref[...] = dkv_ref[span - rows :, :]


def attention_back(
    place, segment_key, segment_query, queries, key_value, lse, dout, cosine, sine, seq_len
):
    rows, all_columns = queries.shape
    span = key_value.shape[0]
    pairs = key_value.shape[1] // (2 * HEAD_SIZE)
    columns = all_columns // pairs
    return pl.pallas_call(
        functools.partial(
            attention_back_kernel, seq_len=seq_len, scale=1.0 / math.sqrt(HEAD_SIZE)
        ),
        grid=(pairs,),
        in_specs=[
            pl.BlockSpec(memory_space=pltpu.SMEM),
            pl.BlockSpec((span, 1), lambda j: (0, 0)),
            pl.BlockSpec((1, rows), lambda j: (0, 0)),
            pl.BlockSpec((rows, columns), lambda j: (0, j)),
            pl.BlockSpec((span, 2 * HEAD_SIZE), lambda j: (0, j)),
            pl.BlockSpec((1, columns // HEAD_SIZE, rows), lambda j: (j, 0, 0)),
            pl.BlockSpec((rows, columns), lambda j: (0, j)),
            pl.BlockSpec((rows, HEAD_SIZE), lambda j: (0, 0)),
            pl.BlockSpec((rows, HEAD_SIZE), lambda j: (0, 0)),
        ],
        out_specs=[
            pl.BlockSpec((rows, columns), lambda j: (0, j)),
            pl.BlockSpec((span - rows, 2 * HEAD_SIZE), lambda j: (0, j)),
            pl.BlockSpec((rows, 2 * HEAD_SIZE), lambda j: (0, j)),
        ],
        out_shape=[
            jax.ShapeDtypeStruct((rows, all_columns), BF16),
            jax.ShapeDtypeStruct((span - rows, key_value.shape[1]), BF16),
            jax.ShapeDtypeStruct((rows, key_value.shape[1]), F32),
        ],
        scratch_shapes=[
            pltpu.VMEM((span, rows), F32),
            pltpu.VMEM((span, 2 * HEAD_SIZE), F32),
        ],
        compiler_params=pltpu.CompilerParams(vmem_limit_bytes=VMEM_LIMIT),
        cost_estimate=pl.CostEstimate(
            flops=70_000_000_000, bytes_accessed=10_000_000, transcendentals=0
        ),
        name="attention_back",
    )(place, segment_key, segment_query, queries, key_value, lse, dout, cosine, sine)


def expert_kernel(
    slot_row_ref,
    slot_column_ref,
    routed_ref,
    own_ref,
    router_ref,
    tokens_ref,
    cotangent_ref,
    gate_ref,
    up_ref,
    down_ref,
    grad_ref,
    moe_ref,
    rows_in_ref,
    grad_out_ref,
    hidden_ref,
    grad_gate_ref,
    grad_up_ref,
    router_grad_ref,
    gate_full_ref,
    up_full_ref,
    down_full_ref,
    *,
    capacity,
):
    whole = ((gate_ref, gate_full_ref), (up_ref, up_full_ref), (down_ref, down_full_ref))

    @pl.when(pl.program_id(0) == 0)
    def _():
        for held, full in whole:
            columns = held.shape[3]
            for half in range(held.shape[1]):
                full[:, half * columns : (half + 1) * columns] = held[:, half].reshape(-1, columns)

    group_rows = tokens_ref.shape[1]
    tokens = tokens_ref[0]
    gate_weight, up_weight, down_weight = (full[...] for _, full in whole)
    cotangent = cotangent_ref[0]
    routed = routed_ref[0] > 0.0
    logits = jnp.where(routed, mxu(router_ref[...], tokens, FROM_LAST), -1e30)
    weights = jnp.exp(logits - jnp.max(logits, axis=0, keepdims=True))
    weights = jnp.where(routed, weights, 0.0)
    gates = weights / jnp.sum(weights, axis=0, keepdims=True)
    own = own_ref[...]
    gate_own = jnp.sum(gates * own, axis=0, keepdims=True)
    place = slot_row_ref[0] == lax.broadcasted_iota(jnp.int32, (capacity, group_rows), 0)
    place_wide = jnp.where(place, 1.0, 0.0)
    place_low = place_wide.astype(BF16)
    back = slot_column_ref[0] == lax.broadcasted_iota(jnp.int32, (group_rows, capacity), 1)
    back_low = jnp.where(back, 1.0, 0.0).astype(BF16)
    coefficient = jnp.sum(place_wide * gate_own, axis=1, keepdims=True)

    rows_in = mxu(place_low, tokens).astype(BF16)
    rows_in_ref[...] = rows_in
    gate_pre = mxu(rows_in, gate_weight)
    up_pre = mxu(rows_in, up_weight)
    sigmoid = 1.0 / (1.0 + jnp.exp(-gate_pre))
    silu = gate_pre * sigmoid
    hidden = (silu * up_pre).astype(BF16)
    hidden_ref[...] = hidden
    slot_cotangent = mxu(place_low, cotangent)
    grad_out = (coefficient * slot_cotangent).astype(BF16)
    grad_out_ref[...] = grad_out
    grad_hidden = mxu(grad_out, down_weight)
    grad_up = (grad_hidden * silu).astype(BF16)
    grad_gate = (grad_hidden * up_pre * sigmoid * (1.0 + gate_pre * (1.0 - sigmoid))).astype(BF16)
    grad_up_ref[...] = grad_up
    grad_gate_ref[...] = grad_gate
    expert_out = mxu(hidden, down_weight, FROM_LAST)
    grad_slot = jnp.sum(slot_cotangent * expert_out, axis=1, keepdims=True)
    moe_ref[0] = mxu(back_low, (coefficient * expert_out).astype(BF16)).astype(BF16)

    grad_token = jnp.sum(place_wide * grad_slot, axis=0, keepdims=True)
    share = (grad_token * gate_own) * (own - gates)
    share_high = share.astype(BF16)
    share_low = (share - share_high.astype(F32)).astype(BF16)
    router_grad = mxu(share_high, tokens) + mxu(share_low, tokens)

    @pl.when(pl.program_id(0) == 0)
    def _():
        router_grad_ref[...] = router_grad

    @pl.when(pl.program_id(0) > 0)
    def _():
        router_grad_ref[...] += router_grad

    grad_in = mxu(grad_gate, gate_weight, FROM_LAST) + mxu(grad_up, up_weight, FROM_LAST)
    grad_ref[0] = (
        mxu(back_low, grad_in.astype(BF16)) + mxu(share.T.astype(BF16), router_ref[...])
    ).astype(BF16)


def expert_groups(slot, routed, own, router_t, tokens, cotangent, weights, capacity):
    count, group_rows, width = tokens.shape
    ff = weights[0].shape[1] * weights[0].shape[3]
    experts = router_t.shape[0]
    weight = pl.BlockSpec(
        weights[0].shape, lambda g: (0, 0, 0, 0), pipeline_mode=pl.Buffered(1)
    )
    whole = lambda g: (0, 0)
    by_group = lambda g: (g, 0, 0)
    slots = lambda columns: pl.BlockSpec((capacity, columns), lambda g: (g, 0))
    slots_shape = lambda columns: jax.ShapeDtypeStruct((count * capacity, columns), BF16)
    return pl.pallas_call(
        functools.partial(expert_kernel, capacity=capacity),
        grid=(count,),
        in_specs=[
            pl.BlockSpec((1, 1, group_rows), by_group),
            pl.BlockSpec((1, group_rows, 1), by_group),
            pl.BlockSpec((1, experts, group_rows), by_group),
            pl.BlockSpec((experts, 1), whole),
            pl.BlockSpec((experts, width), whole),
            pl.BlockSpec((1, group_rows, width), by_group),
            pl.BlockSpec((1, group_rows, width), by_group),
            weight,
            weight,
            weight,
        ],
        out_specs=[
            pl.BlockSpec((1, group_rows, width), by_group),
            pl.BlockSpec((1, group_rows, width), by_group),
            slots(width),
            slots(width),
            slots(ff),
            slots(ff),
            slots(ff),
            pl.BlockSpec((experts, width), whole),
        ],
        out_shape=[
            jax.ShapeDtypeStruct(tokens.shape, BF16),
            jax.ShapeDtypeStruct(tokens.shape, BF16),
            slots_shape(width),
            slots_shape(width),
            slots_shape(ff),
            slots_shape(ff),
            slots_shape(ff),
            jax.ShapeDtypeStruct((experts, width), F32),
        ],
        scratch_shapes=[pltpu.VMEM((width, ff), BF16) for _ in range(3)],
        compiler_params=pltpu.CompilerParams(vmem_limit_bytes=VMEM_LIMIT),
        cost_estimate=LIGHT,
        name="expert",
    )(
        slot[:, None, :],
        slot[:, :, None],
        routed,
        own,
        router_t,
        tokens,
        cotangent,
        *weights,
    )


def weight_grad_kernel(*refs, halves):
    rows, grad_out, hidden, grad_gate, grad_up, router = (
        refs[at : at + 2] for at in range(0, 12, 2)
    )
    moe_kept_ref, moe_got_ref, out_ref = refs[12:15]
    for at, moe_ref in enumerate(refs[15:]):
        moe_ref[...] = (moe_kept_ref[at].astype(F32) + moe_got_ref[at].astype(F32)).astype(BF16)
    columns = hidden[0].shape[1] // halves
    over = (((0,), (0,)), ((), ()))
    left_rows = [ref[...] for ref in rows]
    left_out = [ref[...] for ref in grad_out]
    router_columns = (router[0][...] + router[1][...]).T
    router_columns = jnp.concatenate(
        [
            router_columns,
            jnp.zeros((router_columns.shape[0], HEAD_SIZE - router_columns.shape[1]), F32),
        ],
        axis=1,
    ).astype(BF16)
    for half in range(halves):
        start = half * (3 * columns + HEAD_SIZE)
        part = slice(half * columns, (half + 1) * columns)
        for at, (left, right) in enumerate(
            ((left_rows, grad_gate), (left_rows, grad_up), (left_out, hidden))
        ):
            total = mxu(left[0], right[0][:, part], over) + mxu(left[1], right[1][:, part], over)
            out_ref[:, start + at * columns : start + (at + 1) * columns] = total.astype(BF16)
        out_ref[:, start + 3 * columns : start + 3 * columns + HEAD_SIZE] = router_columns


def weight_grads(near, far, moe_kept, moe_got, halves, block=256):
    rows_at, grad_out_at, hidden_at, grad_gate_at, grad_up_at, router_at = range(6)
    slots, width = near[rows_at].shape
    ff = near[hidden_at].shape[1]
    experts = near[router_at].shape[0]
    specs, operands = [], []
    for at in (rows_at, grad_out_at, hidden_at, grad_gate_at, grad_up_at, router_at):
        if at in (rows_at, grad_out_at):
            spec = pl.BlockSpec((slots, block), lambda i: (0, i))
        elif at == router_at:
            spec = pl.BlockSpec((experts, block), lambda i: (0, i))
        else:
            spec = pl.BlockSpec((slots, ff), lambda i: (0, 0))
        specs += [spec, spec]
        operands += [near[at], far[at]]
    columns = 3 * ff + halves * HEAD_SIZE
    moe_count, moe_rows, _ = moe_kept.shape
    moe_spec = pl.BlockSpec((moe_count, moe_rows, block), lambda i: (0, 0, i))
    moe_out_spec = pl.BlockSpec((moe_rows, block), lambda i: (0, i))
    return pl.pallas_call(
        functools.partial(weight_grad_kernel, halves=halves),
        grid=(width // block,),
        in_specs=specs + [moe_spec, moe_spec],
        out_specs=[pl.BlockSpec((block, columns), lambda i: (i, 0))] + [moe_out_spec] * moe_count,
        out_shape=[jax.ShapeDtypeStruct((width, columns), BF16)]
        + [jax.ShapeDtypeStruct((moe_rows, width), BF16)] * moe_count,
        compiler_params=pltpu.CompilerParams(vmem_limit_bytes=VMEM_LIMIT),
        cost_estimate=pl.CostEstimate(
            flops=15_000_000_000, bytes_accessed=50_000_000, transcendentals=0
        ),
        name="weight_grads",
    )(*operands, moe_kept, moe_got)


def on_device(
    block_input,
    norm_gains,
    router_weight,
    query_matrix,
    key_matrix,
    value_matrix,
    output_weight,
    gate_weight,
    up_weight,
    down_weight,
    segment_ids,
    routes,
    priority,
    cotangent,
):
    tensor_index = lax.axis_index("tensor")
    own_rows, width = block_input.shape
    group_rows = segment_ids.shape[0]
    halves = lax.axis_size("tensor")
    outer = lax.axis_size("outer")
    groups = lax.axis_size("x") * lax.axis_size("core")
    plane = groups * halves
    shard_rows = query_matrix.shape[0]
    dp_size = outer * groups
    seq_len = min(SEQ_MOST, group_rows * dp_size)
    own_start = lax.axis_index(ALL) * own_rows
    capacity = group_rows * TOPK // EXPERTS
    reach = ATTEND_SPAN // own_rows
    half_ff = gate_weight.shape[2]
    ff = half_ff * halves

    query_columns = query_matrix.shape[1]
    pair_columns = 2 * halves * HEAD_SIZE
    first = tensor_index == 0
    key_value_weight = jnp.concatenate([key_matrix, value_matrix], axis=1)
    other_weight = swap(key_value_weight, "tensor")
    early = jnp.concatenate(
        [
            jnp.where(first, key_value_weight, other_weight),
            jnp.where(first, other_weight, key_value_weight),
            query_matrix,
            output_weight,
        ],
        axis=1,
    )
    early, gate_own, up_own, down_own, cotangent_own = lax.optimization_barrier(
        (early, gate_weight, up_weight, down_weight, cotangent)
    )
    early = outer_gather(early)

    expert_shard = jnp.transpose(jnp.stack([gate_own, up_own, down_own]), (2, 0, 1, 3))
    expert_shard = lax.all_to_all(expert_shard, PLANE, 0, 0, tiled=True)
    expert_shard = expert_shard.reshape(groups, halves, 3, shard_rows, half_ff)
    expert_shard = [
        jnp.swapaxes(expert_shard[:, :, at], 0, 1).reshape(-1, half_ff) for at in range(3)
    ]
    early, expert_shard, segment_here, priority_here = lax.optimization_barrier(
        (early, expert_shard, segment_ids, priority)
    )
    pair_count = group_rows * TOPK
    rank = (
        jnp.zeros((pair_count,), jnp.int32)
        .at[priority_here]
        .set(jnp.arange(pair_count, dtype=jnp.int32))
        .reshape(group_rows, TOPK)
    )
    expert_ids = jnp.arange(EXPERTS, dtype=jnp.int32)
    named = routes[:, :, None] == expert_ids[None, None, :]
    ranked = jnp.sum(jnp.where(named, rank[:, :, None] + 1, 0), axis=1)
    ranked = jnp.where(ranked > 0, ranked, pair_count + 1)
    ranked_own = lax.dynamic_slice_in_dim(ranked, tensor_index * own_rows, own_rows, 0)
    digits = jnp.concatenate([ranked_own // 64, ranked_own % 64], axis=1).astype(BF16)
    digits = jnp.pad(digits, ((0, 0), (0, HEAD_SIZE - digits.shape[1])))
    cotangent_sent = jnp.concatenate([cotangent_own, digits], axis=1)
    segment_near = jnp.concatenate(
        [shift_groups(segment_here, 2), shift_groups(segment_here, 1), segment_here]
    )
    expert_full = [
        lax.all_gather(shard, "outer").reshape(outer, halves, groups * shard_rows, half_ff)
        for shard in expert_shard
    ]

    key_value_full = early[:, :, :pair_columns]
    key_value_full = in_order(key_value_full, swap(key_value_full, "x"), "x", 1)
    key_value_full = in_order(key_value_full, swap(key_value_full, "core"), "core", 2)
    key_value_full = key_value_full.reshape(width, pair_columns)
    query_parts = plane_parts(early[:, :, pair_columns : pair_columns + query_columns])

    input_wide = block_input.astype(F32)
    first_gain = norm_gains[:, 0]
    second_gain = norm_gains[:, 1]
    first_factor = norm_factor(input_wide)
    normed_in = (input_wide * first_factor * first_gain).astype(BF16)
    positions = own_start + jnp.arange(own_rows, dtype=jnp.int32)
    cosine, sine = rotary_tables(positions % seq_len)
    query_blocks = halves * query_columns // (2 * HEAD_SIZE)
    key_value_sent = project(
        normed_in, key_value_full, cosine, sine, 0, halves, (True, False)
    )
    one_back, two_back = shift_groups(key_value_sent, 1), shift_groups(key_value_sent, 2)
    query_parts, one_back, two_back, segment_near, cotangent_sent, expert_full[0] = (
        lax.optimization_barrier(
            (query_parts, one_back, two_back, segment_near, cotangent_sent, expert_full[0])
        )
    )
    cotangent_parts = plane_parts(cotangent_sent)
    output_own = early[:, :, pair_columns + query_columns :]
    pair_sent = jnp.where(
        first,
        jnp.stack([one_back, key_value_sent]),
        jnp.stack([two_back, one_back]),
    )
    pair_got = swap(pair_sent, "tensor")
    query_near = plane_stack(query_parts)
    query_far, pair_got = lax.optimization_barrier((swap(query_near, "core"), pair_got))
    pieces = [two_back, pair_got[0], one_back, pair_got[1], key_value_sent]
    query_full = whole_weight(query_near, query_far)
    queries = project(normed_in, query_full, cosine, sine, 0, query_blocks, (True, True))
    output_parts = plane_parts(output_own)
    expert = lax.axis_index(PLANE)

    def slots_of(cotangents):
        digits = cotangents[..., width:].reshape(2, group_rows, HEAD_SIZE).astype(jnp.int32)
        ranked_all = digits[..., :EXPERTS] * 64 + digits[..., EXPERTS : 2 * EXPERTS]
        routed = jnp.swapaxes((ranked_all <= pair_count).astype(F32), 1, 2)
        rank_own = jnp.sum(jnp.where(expert_ids == expert, ranked_all, 0), axis=-1)
        earlier = (rank_own[:, None, :] < rank_own[:, :, None]).astype(jnp.int32)
        slot = jnp.where(rank_own <= pair_count, jnp.sum(earlier, axis=-1), capacity)
        return slot, routed

    key_value = jnp.concatenate(pieces, axis=0)
    span = ATTEND_SPAN + own_rows
    segment_ext = lax.dynamic_slice_in_dim(segment_near, tensor_index * own_rows, span)
    view = (
        jnp.reshape(own_start, (1,)),
        segment_ext[:, None],
        segment_ext[None, ATTEND_SPAN:],
        queries,
        key_value,
    )
    heads_low, log_total = attention(*view, seq_len)
    heads_late, output_parts, cotangent_parts = lax.optimization_barrier(
        (heads_low, output_parts, cotangent_parts)
    )
    output_near = plane_stack(output_parts)
    output_far = swap(output_near, "core")
    output_full, expert_full[1] = lax.optimization_barrier(
        (whole_weight(output_near, output_far), expert_full[1])
    )
    hidden_state = input_wide + dot(heads_low, output_full, ((1,), (1,)))
    second_factor = norm_factor(hidden_state)
    normed_mid_own = (hidden_state * second_factor * second_gain).astype(BF16)

    cotangent_near = plane_stack(cotangent_parts)
    cotangent_far = swap(cotangent_near, "core")
    near_slots, far_slots = slots_of(cotangent_near), slots_of(cotangent_far)
    normed_parts, near_slots, far_slots, expert_full[2] = lax.optimization_barrier(
        (plane_parts(normed_mid_own), near_slots, far_slots, expert_full[2])
    )
    normed_near = plane_stack(normed_parts)
    normed_far = swap(normed_near, "core")
    own_expert = (expert_ids == expert).astype(F32)[:, None]
    router_t = router_weight.T

    def experts_on(tokens, cotangents, slots):
        slot, routed = slots
        return expert_groups(
            slot,
            routed,
            own_expert,
            router_t,
            tokens.reshape(2, group_rows, width),
            cotangents.reshape(2, group_rows, -1),
            expert_full,
            capacity,
        )

    on_near = experts_on(normed_near, cotangent_near, near_slots)
    on_far = experts_on(normed_far, cotangent_far, far_slots)
    blocks = (2 * halves, own_rows, width)
    (grad_near, moe_near), (grad_far, moe_far) = (
        [array.reshape(blocks) for array in side[:2]] for side in (on_near, on_far)
    )
    grad_blocks = fold_blocks(grad_near, swap(grad_far, "core"))
    grad_blocks, moe_far, on_near, on_far = lax.optimization_barrier(
        (grad_blocks, moe_far, on_near[2:], on_far[2:])
    )
    grad_mid_parts = fold_plane(grad_blocks)
    expert_part, *moe_blocks = weight_grads(
        on_near, on_far, moe_near, swap(moe_far, "core"), halves
    )
    expert_sum = lax.psum_scatter(expert_part, "outer", scatter_dimension=0, tiled=True)
    grad_mid_parts, moe_blocks = lax.optimization_barrier((grad_mid_parts, moe_blocks))
    moe_parts = fold_plane(moe_blocks)
    grad_mid = wide_sum(grad_mid_parts)

    norm_input_part = norm_back(hidden_state, second_factor, second_gain, grad_mid)
    grad_state = cotangent.astype(F32) + norm_input_part
    grad_attn = grad_state.astype(BF16)
    grad_heads = dot(grad_attn, output_full, ((1,), (0,))).astype(BF16)
    output_total = fold_columns(grad_attn, heads_late, shard_rows)
    grad_query_pre, grad_far_kv, grad_own = attention_back(
        *view, log_total, grad_heads, cosine, sine, seq_len
    )
    grad_query_pre, output_total, moe_parts = lax.optimization_barrier(
        (grad_query_pre, output_total, moe_parts)
    )
    output_parts = fold_plane(distance_blocks(output_total))
    query_total = fold_columns(normed_in, grad_query_pre, shard_rows)
    two_back, pair_old, one_back, pair_new = grad_far_kv.reshape(reach, own_rows, -1)
    pair_got, output_parts, query_total = lax.optimization_barrier(
        (swap(jnp.stack([pair_old, pair_new]), "tensor"), output_parts, query_total)
    )
    query_parts = fold_plane(distance_blocks(query_total))
    pair_old, pair_new = pair_got.astype(F32)
    one_back = one_back.astype(F32) + jnp.where(first, pair_old, pair_new)
    two_back = two_back.astype(F32) + jnp.where(first, 0.0, pair_old)
    grad_own = grad_own + jnp.where(first, pair_new, 0.0)
    grad_own = grad_own + shift_groups(one_back.astype(BF16), -1).astype(F32)
    grad_own = grad_own + shift_groups(two_back.astype(BF16), -2).astype(F32)
    query_parts, output_parts = lax.optimization_barrier((query_parts, output_parts))
    output_weight_grad = outer_scatter(wide_sum(output_parts).astype(BF16))
    grad_key_value = []
    for half in range(halves):
        start = half * 2 * HEAD_SIZE
        key_part = grad_own[:, start : start + HEAD_SIZE]
        turned = jnp.concatenate(
            [key_part[:, HEAD_SIZE // 2 :], key_part[:, : HEAD_SIZE // 2]], axis=1
        )
        grad_key_value.append(key_part * cosine - turned * sine)
        grad_key_value.append(grad_own[:, start + HEAD_SIZE : start + 2 * HEAD_SIZE])
    grad_key_value_pre = jnp.concatenate(grad_key_value, axis=1).astype(BF16)
    key_value_total = fold_columns(normed_in, grad_key_value_pre, shard_rows)
    key_value_parts = fold_plane(distance_blocks(key_value_total))
    grad_in = dot(grad_query_pre, query_full, ((1,), (1,))) + dot(
        grad_key_value_pre, key_value_full, ((1,), (1,))
    )
    grad_in, expert_sum = lax.optimization_barrier((grad_in, expert_sum))
    input_grad = grad_state + norm_back(input_wide, first_factor, first_gain, grad_in)
    qkv_grad = outer_scatter(
        jnp.concatenate([wide_sum(query_parts), wide_sum(key_value_parts)], axis=2).astype(BF16)
    )
    block_output = hidden_state + wide_sum(moe_parts)
    expert_sum = expert_sum.reshape(groups, shard_rows, halves, -1)
    expert_sum = jnp.swapaxes(expert_sum, 1, 2).reshape(plane, shard_rows, -1)
    expert_sum = lax.all_to_all(expert_sum, PLANE, 0, 0, tiled=True)
    gate_grad, up_grad, down_grad = (
        jnp.swapaxes(expert_sum[:, :, at * half_ff : (at + 1) * half_ff], 0, 1).astype(F32)
        for at in range(3)
    )
    router_grad = jnp.sum(expert_sum[:, :, 3 * half_ff : 3 * half_ff + EXPERTS].astype(F32), axis=0)
    router_grad = lax.dynamic_slice_in_dim(
        router_grad, tensor_index * (shard_rows // 2), shard_rows // 2, 0
    )
    query_grad = qkv_grad[:, :query_columns]
    key_grad = qkv_grad[:, query_columns : query_columns + HEAD_SIZE]
    value_grad = qkv_grad[:, query_columns + HEAD_SIZE :]

    half_rows = shard_rows // 2
    own_gains = lax.dynamic_slice_in_dim(
        norm_gains, lax.axis_index(DP) * shard_rows, shard_rows, 0
    )
    qkv_own = jnp.concatenate([query_matrix, key_value_weight], axis=1)
    first_sum = jnp.sum(qkv_grad * qkv_own.astype(F32), axis=-1)
    second_sum = jnp.sum(
        gate_grad * gate_weight.astype(F32) + up_grad * up_weight.astype(F32), axis=(1, 2)
    )
    gain_sums = jnp.stack([first_sum, second_sum], axis=1) / own_gains
    kept = lax.dynamic_slice_in_dim(gain_sums, tensor_index * half_rows, half_rows, 0)
    sent = lax.dynamic_slice_in_dim(gain_sums, (1 - tensor_index) * half_rows, half_rows, 0)
    own_router = lax.dynamic_slice_in_dim(
        router_weight, lax.axis_index(ALL) * half_rows, half_rows, 0
    )
    router_sum = jnp.sum(router_grad * own_router.astype(F32), axis=-1)
    half_gains = lax.dynamic_slice_in_dim(own_gains, tensor_index * half_rows, half_rows, 0)
    router_sum = router_sum / half_gains[:, 1]
    gains_grad = (
        kept
        + swap(sent, "tensor")
        + jnp.stack([jnp.zeros_like(router_sum), router_sum], axis=1)
    )
    return (
        block_output,
        input_grad,
        gains_grad,
        router_grad,
        query_grad,
        key_grad,
        value_grad,
        output_weight_grad,
        gate_grad,
        up_grad,
        down_grad,
    )


def solution(mesh):
    dp_size, tensor_size = mesh.shape["dp"], mesh.shape["tensor"]
    split = Mesh(mesh.devices.reshape(dp_size // 4, 2, 2, tensor_size), ALL)
    return jax.shard_map(
        on_device,
        mesh=split,
        in_specs=(
            P(ALL, None),
            P(),
            P(),
            P(DP, "tensor"),
            P(DP, "tensor"),
            P(DP, "tensor"),
            P(DP, "tensor"),
            P(DP, None, "tensor"),
            P(DP, None, "tensor"),
            P(DP, None, "tensor"),
            P(DP),
            P(DP, None),
            P(DP),
            P(ALL, None),
        ),
        out_specs=(
            P(ALL, None),
            P(ALL, None),
            P(ALL, None),
            P(ALL, None),
            P(DP, "tensor"),
            P(DP, "tensor"),
            P(DP, "tensor"),
            P(DP, "tensor"),
            P(DP, None, "tensor"),
            P(DP, None, "tensor"),
            P(DP, None, "tensor"),
        ),
        check_vma=False,
    )
```

```python
import functools
import math

import jax
import jax.numpy as jnp
from jax import lax
from jax.experimental import pallas as pl
from jax.experimental.pallas import tpu as pltpu
from jax.sharding import Mesh
from jax.sharding import PartitionSpec as P

HEAD_SIZE = 128
TOPK = 4
EXPERTS = 8
ATTEND_SPAN = 1024
SEQ_MOST = 16384
EPSILON = 1e-06
ROPE_BASE = 10000.0
BF16 = jnp.bfloat16
F32 = jnp.float32

DP = ("outer", "x", "core")
PLANE = ("x", "core", "tensor")
ALL = ("outer", "x", "core", "tensor")


def shift_groups(x, by):
    length = lax.axis_size(DP)
    return lax.ppermute(x, DP, [(i, i + by) for i in range(length) if 0 <= i + by < length])


def swap(x, axis):
    length = lax.axis_size(axis)
    return lax.ppermute(x, axis, [(i, length - 1 - i) for i in range(length)])


def plane_parts(own):
    return [own, swap(own, "tensor"), swap(own, "x"), swap(own, ("x", "tensor"))]


def plane_stack(parts):
    return jnp.stack(parts).reshape((2, 2) + parts[0].shape)


def whole_weight(near, far):
    x, tensor = lax.axis_index("x"), lax.axis_index("tensor")
    first = lax.axis_index("core") == 0
    by_core = [jnp.where(first, near, far), jnp.where(first, far, near)]

    def piece(x_at, core_at, tensor_at):
        picked = lax.dynamic_index_in_dim(by_core[core_at], x ^ x_at, 0, keepdims=False)
        return lax.dynamic_index_in_dim(picked, tensor ^ tensor_at, 0, keepdims=False)

    places = [(x_at, core_at) for x_at in range(2) for core_at in range(2)]
    halves = [jnp.stack([piece(*place, at) for place in places], 1) for at in range(2)]
    return jnp.concatenate(halves, axis=-1).reshape(-1, 2 * near.shape[-1])


def fold_core(kept, sent):
    return (kept.astype(F32) + swap(sent, "core").astype(F32)).astype(BF16)


def fold_blocks(kept, got):
    return [
        (kept[at].astype(F32) + got[at].astype(F32)).astype(BF16) for at in range(kept.shape[0])
    ]


def in_order(own, other, axis_name, axis):
    first = lax.axis_index(axis_name) == 0
    return jnp.stack([jnp.where(first, own, other), jnp.where(first, other, own)], axis)


def fold_plane(blocks):
    return [
        blocks[0],
        swap(blocks[1], "tensor"),
        swap(blocks[2], "x"),
        swap(blocks[3], ("x", "tensor")),
    ]


def wide_sum(parts):
    return sum(part.astype(F32) for part in parts)


def outer_shift(x, by):
    length = lax.axis_size("outer")
    return lax.ppermute(x, "outer", [(i, (i + by) % length) for i in range(length)])


def outer_gather(shard):
    length, here = lax.axis_size("outer"), lax.axis_index("outer")
    if length > 4:
        return lax.all_gather(shard, "outer")
    full = jnp.zeros((length,) + shard.shape, shard.dtype)
    for by in range(length):
        piece = outer_shift(shard, by) if by else shard
        full = lax.dynamic_update_slice_in_dim(full, piece[None], (here - by) % length, 0)
    return full


def outer_scatter(parts):
    length, here = lax.axis_size("outer"), lax.axis_index("outer")
    if length > 4:
        return lax.psum_scatter(parts, "outer", scatter_dimension=0, tiled=False).astype(F32)
    pieces = [
        lax.dynamic_index_in_dim(parts, (here + by) % length, 0, keepdims=False)
        for by in range(length)
    ]
    return wide_sum([pieces[0]] + [outer_shift(pieces[by], by) for by in range(1, length)])


def core_columns(rows, core_at, shard_rows):
    count = rows.shape[0]
    split = rows.reshape(count, -1, 2, shard_rows)
    return lax.dynamic_index_in_dim(split, core_at, 2, keepdims=False).reshape(count, -1)


def fold_columns(left, right, shard_rows):
    core = lax.axis_index("core")
    sent = dot(core_columns(left, 1 - core, shard_rows), right, ((0,), (0,))).astype(BF16)
    kept = dot(core_columns(left, core, shard_rows), right, ((0,), (0,))).astype(BF16)
    return fold_core(kept, sent).reshape(-1, 2, shard_rows, right.shape[1])


def distance_blocks(total):
    x, tensor = lax.axis_index("x"), lax.axis_index("tensor")
    columns = total.shape[3] // 2
    blocks = []
    for x_by in range(2):
        for tensor_by in range(2):
            block = lax.dynamic_index_in_dim(total, x ^ x_by, 1, keepdims=False)
            start = (tensor ^ tensor_by) * columns
            blocks.append(lax.dynamic_slice_in_dim(block, start, columns, 2))
    return blocks


def rotary_tables(position):
    halfway = HEAD_SIZE // 2
    inverse = jnp.exp(
        jnp.arange(halfway, dtype=F32) * (-2.0 * math.log(ROPE_BASE) / HEAD_SIZE)
    )
    angles = position.astype(F32)[:, None] * inverse[None, :]
    cosine, sine = jnp.cos(angles), jnp.sin(angles)
    return (
        jnp.concatenate([cosine, cosine], axis=1),
        jnp.concatenate([-sine, sine], axis=1),
    )


def norm_factor(value_rows):
    return lax.rsqrt(jnp.mean(value_rows * value_rows, axis=-1, keepdims=True) + EPSILON)


def norm_back(value_rows, factor, gain, upstream):
    weighted = upstream * gain
    return factor * weighted - value_rows * (factor * factor * factor) * jnp.mean(
        weighted * value_rows, axis=-1, keepdims=True
    )


def dot(a, b, dims):
    return lax.dot_general(a, b, (dims, ((), ())), preferred_element_type=F32)


VMEM_LIMIT = 60 * 1024 * 1024
LIGHT = pl.CostEstimate(flops=1000, bytes_accessed=1000, transcendentals=0)
FROM_LAST = (((1,), (1,)), ((), ()))
PLAIN = (((1,), (0,)), ((), ()))


def mxu(a, b, dims=PLAIN):
    return lax.dot_general(a, b, dims, preferred_element_type=F32)


def turn(rows, cosine, sine):
    return rows * cosine + pltpu.roll(rows, HEAD_SIZE // 2, 1) * sine


def project_kernel(rows_ref, weight_ref, cosine_ref, sine_ref, out_ref, *, turned):
    product = mxu(rows_ref[...], weight_ref[...])
    for at, turns in enumerate(turned):
        part = product[:, at * HEAD_SIZE : (at + 1) * HEAD_SIZE]
        if turns:
            part = turn(part, cosine_ref[...], sine_ref[...])
        out_ref[:, at * HEAD_SIZE : (at + 1) * HEAD_SIZE] = part.astype(BF16)


def project(rows, weight, cosine, sine, first, count, turned):
    high, width = rows.shape
    columns = len(turned) * HEAD_SIZE
    return pl.pallas_call(
        functools.partial(project_kernel, turned=turned),
        grid=(count,),
        in_specs=[
            pl.BlockSpec((high, width), lambda j: (0, 0)),
            pl.BlockSpec((width, columns), lambda j: (0, first + j)),
            pl.BlockSpec((high, HEAD_SIZE), lambda j: (0, 0)),
            pl.BlockSpec((high, HEAD_SIZE), lambda j: (0, 0)),
        ],
        out_specs=pl.BlockSpec((high, columns), lambda j: (0, j)),
        out_shape=jax.ShapeDtypeStruct((high, count * columns), BF16),
        compiler_params=pltpu.CompilerParams(vmem_limit_bytes=VMEM_LIMIT),
        cost_estimate=LIGHT,
        name="project",
    )(rows, weight, cosine, sine)


def mask_bias(place_ref, segment_key_ref, segment_query_ref, bias_ref, seq_len):
    span, rows = bias_ref.shape
    start = place_ref[0]
    key_at = lax.broadcasted_iota(jnp.int32, (span, rows), 0)
    query_at = lax.broadcasted_iota(jnp.int32, (span, rows), 1) + ATTEND_SPAN
    distance = query_at - key_at
    position = start + query_at - ATTEND_SPAN
    sequence_at = query_at - lax.rem(position, seq_len)
    allowed = (distance >= 0) & (distance < ATTEND_SPAN) & (key_at >= sequence_at)
    allowed = allowed & (segment_key_ref[...] == segment_query_ref[...])
    bias_ref[...] = jnp.where(allowed, 0.0, -1e30)


def attention_kernel(
    place_ref,
    segment_key_ref,
    segment_query_ref,
    q_ref,
    kv_ref,
    heads_ref,
    lse_ref,
    bias_ref,
    *,
    seq_len,
    scale,
):
    @pl.when(pl.program_id(0) == 0)
    def _():
        mask_bias(place_ref, segment_key_ref, segment_query_ref, bias_ref, seq_len)

    rows = q_ref.shape[0]
    span = kv_ref.shape[0]
    count = q_ref.shape[1] // HEAD_SIZE
    value_t = kv_ref[:, HEAD_SIZE:].T
    chunks = span // rows
    for head in range(count):
        columns = slice(head * HEAD_SIZE, (head + 1) * HEAD_SIZE)
        query = q_ref[:, columns]
        scores = []
        for c in range(chunks):
            part = slice(c * rows, (c + 1) * rows)
            raw = mxu(kv_ref[part, :HEAD_SIZE], query, FROM_LAST)
            scores.append(raw * scale + bias_ref[part, :])
        top = functools.reduce(jnp.maximum, scores)
        top = jnp.max(top, axis=0, keepdims=True)
        total = jnp.zeros_like(top)
        out_t = jnp.zeros((HEAD_SIZE, rows), F32)
        for c in range(chunks):
            weight = jnp.exp(scores[c] - top)
            total = total + jnp.sum(weight, axis=0, keepdims=True)
            out_t = out_t + mxu(value_t[:, c * rows : (c + 1) * rows], weight.astype(BF16))
        heads_ref[:, columns] = (out_t / total).T.astype(BF16)
        lse_ref[0, head : head + 1, :] = top + jnp.log(total)


def attention(place, segment_key, segment_query, queries, key_value, seq_len):
    rows, all_columns = queries.shape
    span = key_value.shape[0]
    pairs = key_value.shape[1] // (2 * HEAD_SIZE)
    columns = all_columns // pairs
    return pl.pallas_call(
        functools.partial(attention_kernel, seq_len=seq_len, scale=1.0 / math.sqrt(HEAD_SIZE)),
        grid=(pairs,),
        in_specs=[
            pl.BlockSpec(memory_space=pltpu.SMEM),
            pl.BlockSpec((span, 1), lambda j: (0, 0)),
            pl.BlockSpec((1, rows), lambda j: (0, 0)),
            pl.BlockSpec((rows, columns), lambda j: (0, j)),
            pl.BlockSpec((span, 2 * HEAD_SIZE), lambda j: (0, j)),
        ],
        out_specs=[
            pl.BlockSpec((rows, columns), lambda j: (0, j)),
            pl.BlockSpec((1, columns // HEAD_SIZE, rows), lambda j: (j, 0, 0)),
        ],
        out_shape=[
            jax.ShapeDtypeStruct((rows, all_columns), BF16),
            jax.ShapeDtypeStruct((pairs, columns // HEAD_SIZE, rows), F32),
        ],
        scratch_shapes=[pltpu.VMEM((span, rows), F32)],
        compiler_params=pltpu.CompilerParams(vmem_limit_bytes=VMEM_LIMIT),
        cost_estimate=LIGHT,
        name="attention",
    )(place, segment_key, segment_query, queries, key_value)


def attention_back_kernel(
    place_ref,
    segment_key_ref,
    segment_query_ref,
    q_ref,
    kv_ref,
    lse_ref,
    dout_ref,
    cosine_ref,
    sine_ref,
    dq_ref,
    dkv_far_ref,
    dkv_own_ref,
    bias_ref,
    dkv_ref,
    *,
    seq_len,
    scale,
):
    @pl.when(pl.program_id(0) == 0)
    def _():
        mask_bias(place_ref, segment_key_ref, segment_query_ref, bias_ref, seq_len)

    rows = q_ref.shape[0]
    span = kv_ref.shape[0]
    count = q_ref.shape[1] // HEAD_SIZE
    key_t = kv_ref[:, :HEAD_SIZE].T
    chunks = span // rows
    dkv_ref[...] = jnp.zeros_like(dkv_ref)
    for head in range(count):
        columns = slice(head * HEAD_SIZE, (head + 1) * HEAD_SIZE)
        query = q_ref[:, columns]
        dout = dout_ref[:, columns]
        lse = lse_ref[0, head : head + 1, :]
        probs, dprobs = [], []
        row_dot = jnp.zeros_like(lse)
        for c in range(chunks):
            part = slice(c * rows, (c + 1) * rows)
            raw = mxu(kv_ref[part, :HEAD_SIZE], query, FROM_LAST)
            prob = jnp.exp(raw * scale + bias_ref[part, :] - lse)
            dprob = mxu(kv_ref[part, HEAD_SIZE:], dout, FROM_LAST)
            row_dot = row_dot + jnp.sum(prob * dprob, axis=0, keepdims=True)
            probs.append(prob)
            dprobs.append(dprob)
        dq_t = jnp.zeros((HEAD_SIZE, rows), F32)
        for c in range(chunks):
            part = slice(c * rows, (c + 1) * rows)
            dscore = (probs[c] * (dprobs[c] - row_dot)).astype(BF16)
            dkv_ref[part, :HEAD_SIZE] += mxu(dscore, query)
            dkv_ref[part, HEAD_SIZE:] += mxu(probs[c].astype(BF16), dout)
            dq_t = dq_t + mxu(key_t[:, part], dscore)
        dq_ref[:, columns] = turn(dq_t.T * scale, cosine_ref[...], -sine_ref[...]).astype(BF16)
    dkv_ref[:, :HEAD_SIZE] = dkv_ref[:, :HEAD_SIZE] * scale
    dkv_far_ref[...] = dkv_ref[: span - rows, :].astype(BF16)
    dkv_own_ref[...] = dkv_ref[span - rows :, :]


def attention_back(
    place, segment_key, segment_query, queries, key_value, lse, dout, cosine, sine, seq_len
):
    rows, all_columns = queries.shape
    span = key_value.shape[0]
    pairs = key_value.shape[1] // (2 * HEAD_SIZE)
    columns = all_columns // pairs
    return pl.pallas_call(
        functools.partial(
            attention_back_kernel, seq_len=seq_len, scale=1.0 / math.sqrt(HEAD_SIZE)
        ),
        grid=(pairs,),
        in_specs=[
            pl.BlockSpec(memory_space=pltpu.SMEM),
            pl.BlockSpec((span, 1), lambda j: (0, 0)),
            pl.BlockSpec((1, rows), lambda j: (0, 0)),
            pl.BlockSpec((rows, columns), lambda j: (0, j)),
            pl.BlockSpec((span, 2 * HEAD_SIZE), lambda j: (0, j)),
            pl.BlockSpec((1, columns // HEAD_SIZE, rows), lambda j: (j, 0, 0)),
            pl.BlockSpec((rows, columns), lambda j: (0, j)),
            pl.BlockSpec((rows, HEAD_SIZE), lambda j: (0, 0)),
            pl.BlockSpec((rows, HEAD_SIZE), lambda j: (0, 0)),
        ],
        out_specs=[
            pl.BlockSpec((rows, columns), lambda j: (0, j)),
            pl.BlockSpec((span - rows, 2 * HEAD_SIZE), lambda j: (0, j)),
            pl.BlockSpec((rows, 2 * HEAD_SIZE), lambda j: (0, j)),
        ],
        out_shape=[
            jax.ShapeDtypeStruct((rows, all_columns), BF16),
            jax.ShapeDtypeStruct((span - rows, key_value.shape[1]), BF16),
            jax.ShapeDtypeStruct((rows, key_value.shape[1]), F32),
        ],
        scratch_shapes=[
            pltpu.VMEM((span, rows), F32),
            pltpu.VMEM((span, 2 * HEAD_SIZE), F32),
        ],
        compiler_params=pltpu.CompilerParams(vmem_limit_bytes=VMEM_LIMIT),
        cost_estimate=pl.CostEstimate(
            flops=52_000_000_000, bytes_accessed=10_000_000, transcendentals=0
        ),
        name="attention_back",
    )(place, segment_key, segment_query, queries, key_value, lse, dout, cosine, sine)


def expert_kernel(
    slot_row_ref,
    slot_column_ref,
    routed_ref,
    own_ref,
    router_ref,
    tokens_ref,
    cotangent_ref,
    gate_ref,
    up_ref,
    down_ref,
    grad_ref,
    moe_ref,
    rows_in_ref,
    grad_out_ref,
    hidden_ref,
    grad_gate_ref,
    grad_up_ref,
    router_grad_ref,
    gate_full_ref,
    up_full_ref,
    down_full_ref,
    *,
    capacity,
):
    whole = ((gate_ref, gate_full_ref), (up_ref, up_full_ref), (down_ref, down_full_ref))

    @pl.when(pl.program_id(0) == 0)
    def _():
        for held, full in whole:
            columns = held.shape[3]
            for half in range(held.shape[1]):
                full[:, half * columns : (half + 1) * columns] = held[:, half].reshape(-1, columns)

    group_rows = tokens_ref.shape[1]
    tokens = tokens_ref[0]
    gate_weight, up_weight, down_weight = (full[...] for _, full in whole)
    cotangent = cotangent_ref[0]
    routed = routed_ref[0] > 0.0
    logits = jnp.where(routed, mxu(router_ref[...], tokens, FROM_LAST), -1e30)
    weights = jnp.exp(logits - jnp.max(logits, axis=0, keepdims=True))
    weights = jnp.where(routed, weights, 0.0)
    gates = weights / jnp.sum(weights, axis=0, keepdims=True)
    own = own_ref[...]
    gate_own = jnp.sum(gates * own, axis=0, keepdims=True)
    place = slot_row_ref[0] == lax.broadcasted_iota(jnp.int32, (capacity, group_rows), 0)
    place_wide = jnp.where(place, 1.0, 0.0)
    place_low = place_wide.astype(BF16)
    back = slot_column_ref[0] == lax.broadcasted_iota(jnp.int32, (group_rows, capacity), 1)
    back_low = jnp.where(back, 1.0, 0.0).astype(BF16)
    coefficient = jnp.sum(place_wide * gate_own, axis=1, keepdims=True)

    rows_in = mxu(place_low, tokens).astype(BF16)
    rows_in_ref[...] = rows_in
    gate_pre = mxu(rows_in, gate_weight)
    up_pre = mxu(rows_in, up_weight)
    sigmoid = 1.0 / (1.0 + jnp.exp(-gate_pre))
    silu = gate_pre * sigmoid
    hidden = (silu * up_pre).astype(BF16)
    hidden_ref[...] = hidden
    slot_cotangent = mxu(place_low, cotangent)
    grad_out = (coefficient * slot_cotangent).astype(BF16)
    grad_out_ref[...] = grad_out
    grad_hidden = mxu(grad_out, down_weight)
    grad_up = (grad_hidden * silu).astype(BF16)
    grad_gate = (grad_hidden * up_pre * sigmoid * (1.0 + gate_pre * (1.0 - sigmoid))).astype(BF16)
    grad_up_ref[...] = grad_up
    grad_gate_ref[...] = grad_gate
    expert_out = mxu(hidden, down_weight, FROM_LAST)
    grad_slot = jnp.sum(slot_cotangent * expert_out, axis=1, keepdims=True)
    moe_ref[0] = mxu(back_low, (coefficient * expert_out).astype(BF16)).astype(BF16)

    grad_token = jnp.sum(place_wide * grad_slot, axis=0, keepdims=True)
    share = (grad_token * gate_own) * (own - gates)
    share_high = share.astype(BF16)
    share_low = (share - share_high.astype(F32)).astype(BF16)
    router_grad = mxu(share_high, tokens) + mxu(share_low, tokens)

    @pl.when(pl.program_id(0) == 0)
    def _():
        router_grad_ref[...] = router_grad

    @pl.when(pl.program_id(0) > 0)
    def _():
        router_grad_ref[...] += router_grad

    grad_in = mxu(grad_gate, gate_weight, FROM_LAST) + mxu(grad_up, up_weight, FROM_LAST)
    grad_ref[0] = (
        mxu(back_low, grad_in.astype(BF16)) + mxu(share.T.astype(BF16), router_ref[...])
    ).astype(BF16)


def expert_groups(slot, routed, own, router_t, tokens, cotangent, weights, capacity):
    count, group_rows, width = tokens.shape
    ff = weights[0].shape[1] * weights[0].shape[3]
    experts = router_t.shape[0]
    weight = pl.BlockSpec(
        weights[0].shape, lambda g: (0, 0, 0, 0), pipeline_mode=pl.Buffered(1)
    )
    whole = lambda g: (0, 0)
    by_group = lambda g: (g, 0, 0)
    slots = lambda columns: pl.BlockSpec((capacity, columns), lambda g: (g, 0))
    slots_shape = lambda columns: jax.ShapeDtypeStruct((count * capacity, columns), BF16)
    return pl.pallas_call(
        functools.partial(expert_kernel, capacity=capacity),
        grid=(count,),
        in_specs=[
            pl.BlockSpec((1, 1, group_rows), by_group),
            pl.BlockSpec((1, group_rows, 1), by_group),
            pl.BlockSpec((1, experts, group_rows), by_group),
            pl.BlockSpec((experts, 1), whole),
            pl.BlockSpec((experts, width), whole),
            pl.BlockSpec((1, group_rows, width), by_group),
            pl.BlockSpec((1, group_rows, width), by_group),
            weight,
            weight,
            weight,
        ],
        out_specs=[
            pl.BlockSpec((1, group_rows, width), by_group),
            pl.BlockSpec((1, group_rows, width), by_group),
            slots(width),
            slots(width),
            slots(ff),
            slots(ff),
            slots(ff),
            pl.BlockSpec((experts, width), whole),
        ],
        out_shape=[
            jax.ShapeDtypeStruct(tokens.shape, BF16),
            jax.ShapeDtypeStruct(tokens.shape, BF16),
            slots_shape(width),
            slots_shape(width),
            slots_shape(ff),
            slots_shape(ff),
            slots_shape(ff),
            jax.ShapeDtypeStruct((experts, width), F32),
        ],
        scratch_shapes=[pltpu.VMEM((width, ff), BF16) for _ in range(3)],
        compiler_params=pltpu.CompilerParams(vmem_limit_bytes=VMEM_LIMIT),
        cost_estimate=LIGHT,
        name="expert",
    )(
        slot[:, None, :],
        slot[:, :, None],
        routed,
        own,
        router_t,
        tokens,
        cotangent,
        *weights,
    )


def weight_grad_kernel(*refs, halves):
    rows, grad_out, hidden, grad_gate, grad_up, router = (
        refs[at : at + 2] for at in range(0, 12, 2)
    )
    moe_kept_ref, moe_got_ref, out_ref = refs[12:15]
    for at, moe_ref in enumerate(refs[15:]):
        moe_ref[...] = (moe_kept_ref[at].astype(F32) + moe_got_ref[at].astype(F32)).astype(BF16)
    columns = hidden[0].shape[1] // halves
    over = (((0,), (0,)), ((), ()))
    left_rows = [ref[...] for ref in rows]
    left_out = [ref[...] for ref in grad_out]
    router_columns = (router[0][...] + router[1][...]).T
    router_columns = jnp.concatenate(
        [
            router_columns,
            jnp.zeros((router_columns.shape[0], HEAD_SIZE - router_columns.shape[1]), F32),
        ],
        axis=1,
    ).astype(BF16)
    for half in range(halves):
        start = half * (3 * columns + HEAD_SIZE)
        part = slice(half * columns, (half + 1) * columns)
        for at, (left, right) in enumerate(
            ((left_rows, grad_gate), (left_rows, grad_up), (left_out, hidden))
        ):
            total = mxu(left[0], right[0][:, part], over) + mxu(left[1], right[1][:, part], over)
            out_ref[:, start + at * columns : start + (at + 1) * columns] = total.astype(BF16)
        out_ref[:, start + 3 * columns : start + 3 * columns + HEAD_SIZE] = router_columns


def weight_grads(near, far, moe_kept, moe_got, halves, block=256):
    rows_at, grad_out_at, hidden_at, grad_gate_at, grad_up_at, router_at = range(6)
    slots, width = near[rows_at].shape
    ff = near[hidden_at].shape[1]
    experts = near[router_at].shape[0]
    specs, operands = [], []
    for at in (rows_at, grad_out_at, hidden_at, grad_gate_at, grad_up_at, router_at):
        if at in (rows_at, grad_out_at):
            spec = pl.BlockSpec((slots, block), lambda i: (0, i))
        elif at == router_at:
            spec = pl.BlockSpec((experts, block), lambda i: (0, i))
        else:
            spec = pl.BlockSpec((slots, ff), lambda i: (0, 0))
        specs += [spec, spec]
        operands += [near[at], far[at]]
    columns = 3 * ff + halves * HEAD_SIZE
    moe_count, moe_rows, _ = moe_kept.shape
    moe_spec = pl.BlockSpec((moe_count, moe_rows, block), lambda i: (0, 0, i))
    moe_out_spec = pl.BlockSpec((moe_rows, block), lambda i: (0, i))
    return pl.pallas_call(
        functools.partial(weight_grad_kernel, halves=halves),
        grid=(width // block,),
        in_specs=specs + [moe_spec, moe_spec],
        out_specs=[pl.BlockSpec((block, columns), lambda i: (i, 0))] + [moe_out_spec] * moe_count,
        out_shape=[jax.ShapeDtypeStruct((width, columns), BF16)]
        + [jax.ShapeDtypeStruct((moe_rows, width), BF16)] * moe_count,
        compiler_params=pltpu.CompilerParams(vmem_limit_bytes=VMEM_LIMIT),
        cost_estimate=pl.CostEstimate(
            flops=15_000_000_000, bytes_accessed=50_000_000, transcendentals=0
        ),
        name="weight_grads",
    )(*operands, moe_kept, moe_got)


def on_device(
    block_input,
    norm_gains,
    router_weight,
    query_matrix,
    key_matrix,
    value_matrix,
    output_weight,
    gate_weight,
    up_weight,
    down_weight,
    segment_ids,
    routes,
    priority,
    cotangent,
):
    tensor_index = lax.axis_index("tensor")
    own_rows, width = block_input.shape
    group_rows = segment_ids.shape[0]
    halves = lax.axis_size("tensor")
    outer = lax.axis_size("outer")
    groups = lax.axis_size("x") * lax.axis_size("core")
    plane = groups * halves
    shard_rows = query_matrix.shape[0]
    dp_size = outer * groups
    seq_len = min(SEQ_MOST, group_rows * dp_size)
    own_start = lax.axis_index(ALL) * own_rows
    capacity = group_rows * TOPK // EXPERTS
    reach = ATTEND_SPAN // own_rows
    half_ff = gate_weight.shape[2]
    ff = half_ff * halves

    query_columns = query_matrix.shape[1]
    pair_columns = 2 * halves * HEAD_SIZE
    first = tensor_index == 0
    key_value_weight = jnp.concatenate([key_matrix, value_matrix], axis=1)
    other_weight = swap(key_value_weight, "tensor")
    early = jnp.concatenate(
        [
            jnp.where(first, key_value_weight, other_weight),
            jnp.where(first, other_weight, key_value_weight),
            query_matrix,
            output_weight,
        ],
        axis=1,
    )
    early, gate_own, up_own, down_own, cotangent_own = lax.optimization_barrier(
        (early, gate_weight, up_weight, down_weight, cotangent)
    )
    early = outer_gather(early)

    expert_shard = jnp.transpose(jnp.stack([gate_own, up_own, down_own]), (2, 0, 1, 3))
    expert_shard = lax.all_to_all(expert_shard, PLANE, 0, 0, tiled=True)
    expert_shard = expert_shard.reshape(groups, halves, 3, shard_rows, half_ff)
    expert_shard = [
        jnp.swapaxes(expert_shard[:, :, at], 0, 1).reshape(-1, half_ff) for at in range(3)
    ]
    early, expert_shard, segment_here, priority_here = lax.optimization_barrier(
        (early, expert_shard, segment_ids, priority)
    )
    pair_count = group_rows * TOPK
    rank = (
        jnp.zeros((pair_count,), jnp.int32)
        .at[priority_here]
        .set(jnp.arange(pair_count, dtype=jnp.int32))
        .reshape(group_rows, TOPK)
    )
    expert_ids = jnp.arange(EXPERTS, dtype=jnp.int32)
    named = routes[:, :, None] == expert_ids[None, None, :]
    ranked = jnp.sum(jnp.where(named, rank[:, :, None] + 1, 0), axis=1)
    ranked = jnp.where(ranked > 0, ranked, pair_count + 1)
    ranked_own = lax.dynamic_slice_in_dim(ranked, tensor_index * own_rows, own_rows, 0)
    digits = jnp.concatenate([ranked_own // 64, ranked_own % 64], axis=1).astype(BF16)
    digits = jnp.pad(digits, ((0, 0), (0, HEAD_SIZE - digits.shape[1])))
    cotangent_sent = jnp.concatenate([cotangent_own, digits], axis=1)
    segment_near = jnp.concatenate(
        [shift_groups(segment_here, 2), shift_groups(segment_here, 1), segment_here]
    )
    expert_full = [
        lax.all_gather(shard, "outer").reshape(outer, halves, groups * shard_rows, half_ff)
        for shard in expert_shard
    ]

    key_value_full = early[:, :, :pair_columns]
    key_value_full = in_order(key_value_full, swap(key_value_full, "x"), "x", 1)
    key_value_full = in_order(key_value_full, swap(key_value_full, "core"), "core", 2)
    key_value_full = key_value_full.reshape(width, pair_columns)
    query_parts = plane_parts(early[:, :, pair_columns : pair_columns + query_columns])

    input_wide = block_input.astype(F32)
    first_gain = norm_gains[:, 0]
    second_gain = norm_gains[:, 1]
    first_factor = norm_factor(input_wide)
    normed_in = (input_wide * first_factor * first_gain).astype(BF16)
    positions = own_start + jnp.arange(own_rows, dtype=jnp.int32)
    cosine, sine = rotary_tables(positions % seq_len)
    query_blocks = halves * query_columns // (2 * HEAD_SIZE)
    key_value_sent = project(
        normed_in, key_value_full, cosine, sine, 0, halves, (True, False)
    )
    one_back, two_back = shift_groups(key_value_sent, 1), shift_groups(key_value_sent, 2)
    query_parts, one_back, two_back, segment_near, cotangent_sent, expert_full[0] = (
        lax.optimization_barrier(
            (query_parts, one_back, two_back, segment_near, cotangent_sent, expert_full[0])
        )
    )
    cotangent_parts = plane_parts(cotangent_sent)
    output_own = early[:, :, pair_columns + query_columns :]
    pair_sent = jnp.where(
        first,
        jnp.stack([one_back, key_value_sent]),
        jnp.stack([two_back, one_back]),
    )
    pair_got = swap(pair_sent, "tensor")
    query_near = plane_stack(query_parts)
    query_far, pair_got = lax.optimization_barrier((swap(query_near, "core"), pair_got))
    pieces = [two_back, pair_got[0], one_back, pair_got[1], key_value_sent]
    query_full = whole_weight(query_near, query_far)
    queries = project(normed_in, query_full, cosine, sine, 0, query_blocks, (True, True))
    output_parts = plane_parts(output_own)
    expert = lax.axis_index(PLANE)

    def slots_of(cotangents):
        digits = cotangents[..., width:].reshape(2, group_rows, HEAD_SIZE).astype(jnp.int32)
        ranked_all = digits[..., :EXPERTS] * 64 + digits[..., EXPERTS : 2 * EXPERTS]
        routed = jnp.swapaxes((ranked_all <= pair_count).astype(F32), 1, 2)
        rank_own = jnp.sum(jnp.where(expert_ids == expert, ranked_all, 0), axis=-1)
        earlier = (rank_own[:, None, :] < rank_own[:, :, None]).astype(jnp.int32)
        slot = jnp.where(rank_own <= pair_count, jnp.sum(earlier, axis=-1), capacity)
        return slot, routed

    key_value = jnp.concatenate(pieces, axis=0)
    span = ATTEND_SPAN + own_rows
    segment_ext = lax.dynamic_slice_in_dim(segment_near, tensor_index * own_rows, span)
    view = (
        jnp.reshape(own_start, (1,)),
        segment_ext[:, None],
        segment_ext[None, ATTEND_SPAN:],
        queries,
        key_value,
    )
    heads_low, log_total = attention(*view, seq_len)
    heads_late, output_parts, cotangent_parts = lax.optimization_barrier(
        (heads_low, output_parts, cotangent_parts)
    )
    output_near = plane_stack(output_parts)
    output_far = swap(output_near, "core")
    output_full, expert_full[1] = lax.optimization_barrier(
        (whole_weight(output_near, output_far), expert_full[1])
    )
    hidden_state = input_wide + dot(heads_low, output_full, ((1,), (1,)))
    second_factor = norm_factor(hidden_state)
    normed_mid_own = (hidden_state * second_factor * second_gain).astype(BF16)

    cotangent_near = plane_stack(cotangent_parts)
    cotangent_far = swap(cotangent_near, "core")
    near_slots, far_slots = slots_of(cotangent_near), slots_of(cotangent_far)
    normed_parts, near_slots, far_slots, expert_full[2] = lax.optimization_barrier(
        (plane_parts(normed_mid_own), near_slots, far_slots, expert_full[2])
    )
    normed_near = plane_stack(normed_parts)
    normed_far = swap(normed_near, "core")
    own_expert = (expert_ids == expert).astype(F32)[:, None]
    router_t = router_weight.T

    def experts_on(tokens, cotangents, slots):
        slot, routed = slots
        return expert_groups(
            slot,
            routed,
            own_expert,
            router_t,
            tokens.reshape(2, group_rows, width),
            cotangents.reshape(2, group_rows, -1),
            expert_full,
            capacity,
        )

    on_near = experts_on(normed_near, cotangent_near, near_slots)
    on_far = experts_on(normed_far, cotangent_far, far_slots)
    blocks = (2 * halves, own_rows, width)
    (grad_near, moe_near), (grad_far, moe_far) = (
        [array.reshape(blocks) for array in side[:2]] for side in (on_near, on_far)
    )
    grad_blocks = fold_blocks(grad_near, swap(grad_far, "core"))
    grad_blocks, moe_far, on_near, on_far = lax.optimization_barrier(
        (grad_blocks, moe_far, on_near[2:], on_far[2:])
    )
    grad_mid_parts = fold_plane(grad_blocks)
    expert_part, *moe_blocks = weight_grads(
        on_near, on_far, moe_near, swap(moe_far, "core"), halves
    )
    expert_sum = lax.psum_scatter(expert_part, "outer", scatter_dimension=0, tiled=True)
    grad_mid_parts, moe_blocks = lax.optimization_barrier((grad_mid_parts, moe_blocks))
    moe_parts = fold_plane(moe_blocks)
    grad_mid = wide_sum(grad_mid_parts)

    norm_input_part = norm_back(hidden_state, second_factor, second_gain, grad_mid)
    grad_state = cotangent.astype(F32) + norm_input_part
    grad_attn = grad_state.astype(BF16)
    grad_heads = dot(grad_attn, output_full, ((1,), (0,))).astype(BF16)
    output_total = fold_columns(grad_attn, heads_late, shard_rows)
    grad_query_pre, grad_far_kv, grad_own = attention_back(
        *view, log_total, grad_heads, cosine, sine, seq_len
    )
    grad_query_pre, output_total = lax.optimization_barrier((grad_query_pre, output_total))
    output_parts = fold_plane(distance_blocks(output_total))
    query_total = fold_columns(normed_in, grad_query_pre, shard_rows)
    two_back, pair_old, one_back, pair_new = grad_far_kv.reshape(reach, own_rows, -1)
    pair_got, output_parts, query_total, moe_parts = lax.optimization_barrier(
        (swap(jnp.stack([pair_old, pair_new]), "tensor"), output_parts, query_total, moe_parts)
    )
    query_parts = fold_plane(distance_blocks(query_total))
    pair_old, pair_new = pair_got.astype(F32)
    one_back = one_back.astype(F32) + jnp.where(first, pair_old, pair_new)
    two_back = two_back.astype(F32) + jnp.where(first, 0.0, pair_old)
    grad_own = grad_own + jnp.where(first, pair_new, 0.0)
    grad_own = grad_own + shift_groups(one_back.astype(BF16), -1).astype(F32)
    grad_own = grad_own + shift_groups(two_back.astype(BF16), -2).astype(F32)
    query_parts, output_parts = lax.optimization_barrier((query_parts, output_parts))
    output_weight_grad = outer_scatter(wide_sum(output_parts).astype(BF16))
    grad_key_value = []
    for half in range(halves):
        start = half * 2 * HEAD_SIZE
        key_part = grad_own[:, start : start + HEAD_SIZE]
        turned = jnp.concatenate(
            [key_part[:, HEAD_SIZE // 2 :], key_part[:, : HEAD_SIZE // 2]], axis=1
        )
        grad_key_value.append(key_part * cosine - turned * sine)
        grad_key_value.append(grad_own[:, start + HEAD_SIZE : start + 2 * HEAD_SIZE])
    grad_key_value_pre = jnp.concatenate(grad_key_value, axis=1).astype(BF16)
    key_value_total = fold_columns(normed_in, grad_key_value_pre, shard_rows)
    key_value_parts = fold_plane(distance_blocks(key_value_total))
    grad_in = dot(grad_query_pre, query_full, ((1,), (1,))) + dot(
        grad_key_value_pre, key_value_full, ((1,), (1,))
    )
    grad_in, expert_sum = lax.optimization_barrier((grad_in, expert_sum))
    input_grad = grad_state + norm_back(input_wide, first_factor, first_gain, grad_in)
    qkv_grad = outer_scatter(
        jnp.concatenate([wide_sum(query_parts), wide_sum(key_value_parts)], axis=2).astype(BF16)
    )
    block_output = hidden_state + wide_sum(moe_parts)
    expert_sum = expert_sum.reshape(groups, shard_rows, halves, -1)
    expert_sum = jnp.swapaxes(expert_sum, 1, 2).reshape(plane, shard_rows, -1)
    expert_sum = lax.all_to_all(expert_sum, PLANE, 0, 0, tiled=True)
    gate_grad, up_grad, down_grad = (
        jnp.swapaxes(expert_sum[:, :, at * half_ff : (at + 1) * half_ff], 0, 1).astype(F32)
        for at in range(3)
    )
    router_grad = jnp.sum(expert_sum[:, :, 3 * half_ff : 3 * half_ff + EXPERTS].astype(F32), axis=0)
    router_grad = lax.dynamic_slice_in_dim(
        router_grad, tensor_index * (shard_rows // 2), shard_rows // 2, 0
    )
    query_grad = qkv_grad[:, :query_columns]
    key_grad = qkv_grad[:, query_columns : query_columns + HEAD_SIZE]
    value_grad = qkv_grad[:, query_columns + HEAD_SIZE :]

    half_rows = shard_rows // 2
    own_gains = lax.dynamic_slice_in_dim(
        norm_gains, lax.axis_index(DP) * shard_rows, shard_rows, 0
    )
    qkv_own = jnp.concatenate([query_matrix, key_value_weight], axis=1)
    first_sum = jnp.sum(qkv_grad * qkv_own.astype(F32), axis=-1)
    second_sum = jnp.sum(
        gate_grad * gate_weight.astype(F32) + up_grad * up_weight.astype(F32), axis=(1, 2)
    )
    gain_sums = jnp.stack([first_sum, second_sum], axis=1) / own_gains
    kept = lax.dynamic_slice_in_dim(gain_sums, tensor_index * half_rows, half_rows, 0)
    sent = lax.dynamic_slice_in_dim(gain_sums, (1 - tensor_index) * half_rows, half_rows, 0)
    own_router = lax.dynamic_slice_in_dim(
        router_weight, lax.axis_index(ALL) * half_rows, half_rows, 0
    )
    router_sum = jnp.sum(router_grad * own_router.astype(F32), axis=-1)
    half_gains = lax.dynamic_slice_in_dim(own_gains, tensor_index * half_rows, half_rows, 0)
    router_sum = router_sum / half_gains[:, 1]
    gains_grad = (
        kept
        + swap(sent, "tensor")
        + jnp.stack([jnp.zeros_like(router_sum), router_sum], axis=1)
    )
    return (
        block_output,
        input_grad,
        gains_grad,
        router_grad,
        query_grad,
        key_grad,
        value_grad,
        output_weight_grad,
        gate_grad,
        up_grad,
        down_grad,
    )


def solution(mesh):
    dp_size, tensor_size = mesh.shape["dp"], mesh.shape["tensor"]
    split = Mesh(mesh.devices.reshape(dp_size // 4, 2, 2, tensor_size), ALL)
    return jax.shard_map(
        on_device,
        mesh=split,
        in_specs=(
            P(ALL, None),
            P(),
            P(),
            P(DP, "tensor"),
            P(DP, "tensor"),
            P(DP, "tensor"),
            P(DP, "tensor"),
            P(DP, None, "tensor"),
            P(DP, None, "tensor"),
            P(DP, None, "tensor"),
            P(DP),
            P(DP, None),
            P(DP),
            P(ALL, None),
        ),
        out_specs=(
            P(ALL, None),
            P(ALL, None),
            P(ALL, None),
            P(ALL, None),
            P(DP, "tensor"),
            P(DP, "tensor"),
            P(DP, "tensor"),
            P(DP, "tensor"),
            P(DP, None, "tensor"),
            P(DP, None, "tensor"),
            P(DP, None, "tensor"),
        ),
        check_vma=False,
    )
```

```python
import functools
import math

import jax
import jax.numpy as jnp
from jax import lax
from jax.experimental import pallas as pl
from jax.experimental.pallas import tpu as pltpu
from jax.sharding import Mesh
from jax.sharding import PartitionSpec as P

HEAD_SIZE = 128
TOPK = 4
EXPERTS = 8
ATTEND_SPAN = 1024
SEQ_MOST = 16384
EPSILON = 1e-06
ROPE_BASE = 10000.0
BF16 = jnp.bfloat16
F32 = jnp.float32

DP = ("outer", "x", "core")
PLANE = ("x", "core", "tensor")
ALL = ("outer", "x", "core", "tensor")


def shift_groups(x, by):
    length = lax.axis_size(DP)
    return lax.ppermute(x, DP, [(i, i + by) for i in range(length) if 0 <= i + by < length])


def swap(x, axis):
    length = lax.axis_size(axis)
    return lax.ppermute(x, axis, [(i, length - 1 - i) for i in range(length)])


def plane_parts(own):
    return [own, swap(own, "tensor"), swap(own, "x"), swap(own, ("x", "tensor"))]


def plane_stack(parts):
    return jnp.stack(parts).reshape((2, 2) + parts[0].shape)


def whole_weight(near, far):
    x, tensor = lax.axis_index("x"), lax.axis_index("tensor")
    first = lax.axis_index("core") == 0
    by_core = [jnp.where(first, near, far), jnp.where(first, far, near)]

    def piece(x_at, core_at, tensor_at):
        picked = lax.dynamic_index_in_dim(by_core[core_at], x ^ x_at, 0, keepdims=False)
        return lax.dynamic_index_in_dim(picked, tensor ^ tensor_at, 0, keepdims=False)

    places = [(x_at, core_at) for x_at in range(2) for core_at in range(2)]
    halves = [jnp.stack([piece(*place, at) for place in places], 1) for at in range(2)]
    return jnp.concatenate(halves, axis=-1).reshape(-1, 2 * near.shape[-1])


def fold_core(kept, sent):
    return (kept.astype(F32) + swap(sent, "core").astype(F32)).astype(BF16)


def fold_blocks(kept, got):
    return [
        (kept[at].astype(F32) + got[at].astype(F32)).astype(BF16) for at in range(kept.shape[0])
    ]


def in_order(own, other, axis_name, axis):
    first = lax.axis_index(axis_name) == 0
    return jnp.stack([jnp.where(first, own, other), jnp.where(first, other, own)], axis)


def fold_plane(blocks):
    return [
        blocks[0],
        swap(blocks[1], "tensor"),
        swap(blocks[2], "x"),
        swap(blocks[3], ("x", "tensor")),
    ]


def wide_sum(parts):
    return sum(part.astype(F32) for part in parts)


def outer_shift(x, by):
    length = lax.axis_size("outer")
    return lax.ppermute(x, "outer", [(i, (i + by) % length) for i in range(length)])


def outer_gather(shard):
    length, here = lax.axis_size("outer"), lax.axis_index("outer")
    if length > 4:
        return lax.all_gather(shard, "outer")
    full = jnp.zeros((length,) + shard.shape, shard.dtype)
    for by in range(length):
        piece = outer_shift(shard, by) if by else shard
        full = lax.dynamic_update_slice_in_dim(full, piece[None], (here - by) % length, 0)
    return full


def outer_scatter(parts):
    length, here = lax.axis_size("outer"), lax.axis_index("outer")
    if length > 4:
        return lax.psum_scatter(parts, "outer", scatter_dimension=0, tiled=False).astype(F32)
    pieces = [
        lax.dynamic_index_in_dim(parts, (here + by) % length, 0, keepdims=False)
        for by in range(length)
    ]
    return wide_sum([pieces[0]] + [outer_shift(pieces[by], by) for by in range(1, length)])


def core_columns(rows, core_at, shard_rows):
    count = rows.shape[0]
    split = rows.reshape(count, -1, 2, shard_rows)
    return lax.dynamic_index_in_dim(split, core_at, 2, keepdims=False).reshape(count, -1)


def fold_columns(left, right, shard_rows):
    core = lax.axis_index("core")
    sent = dot(core_columns(left, 1 - core, shard_rows), right, ((0,), (0,))).astype(BF16)
    kept = dot(core_columns(left, core, shard_rows), right, ((0,), (0,))).astype(BF16)
    return fold_core(kept, sent).reshape(-1, 2, shard_rows, right.shape[1])


def distance_blocks(total):
    x, tensor = lax.axis_index("x"), lax.axis_index("tensor")
    columns = total.shape[3] // 2
    blocks = []
    for x_by in range(2):
        for tensor_by in range(2):
            block = lax.dynamic_index_in_dim(total, x ^ x_by, 1, keepdims=False)
            start = (tensor ^ tensor_by) * columns
            blocks.append(lax.dynamic_slice_in_dim(block, start, columns, 2))
    return blocks


def rotary_tables(position):
    halfway = HEAD_SIZE // 2
    inverse = jnp.exp(
        jnp.arange(halfway, dtype=F32) * (-2.0 * math.log(ROPE_BASE) / HEAD_SIZE)
    )
    angles = position.astype(F32)[:, None] * inverse[None, :]
    cosine, sine = jnp.cos(angles), jnp.sin(angles)
    return (
        jnp.concatenate([cosine, cosine], axis=1),
        jnp.concatenate([-sine, sine], axis=1),
    )


def norm_factor(value_rows):
    return lax.rsqrt(jnp.mean(value_rows * value_rows, axis=-1, keepdims=True) + EPSILON)


def norm_back(value_rows, factor, gain, upstream):
    weighted = upstream * gain
    return factor * weighted - value_rows * (factor * factor * factor) * jnp.mean(
        weighted * value_rows, axis=-1, keepdims=True
    )


def dot(a, b, dims):
    return lax.dot_general(a, b, (dims, ((), ())), preferred_element_type=F32)


VMEM_LIMIT = 60 * 1024 * 1024
LIGHT = pl.CostEstimate(flops=1000, bytes_accessed=1000, transcendentals=0)
FROM_LAST = (((1,), (1,)), ((), ()))
PLAIN = (((1,), (0,)), ((), ()))


def mxu(a, b, dims=PLAIN):
    return lax.dot_general(a, b, dims, preferred_element_type=F32)


def turn(rows, cosine, sine):
    return rows * cosine + pltpu.roll(rows, HEAD_SIZE // 2, 1) * sine


def project_kernel(rows_ref, weight_ref, cosine_ref, sine_ref, out_ref, *, turned):
    product = mxu(rows_ref[...], weight_ref[...])
    for at, turns in enumerate(turned):
        part = product[:, at * HEAD_SIZE : (at + 1) * HEAD_SIZE]
        if turns:
            part = turn(part, cosine_ref[...], sine_ref[...])
        out_ref[:, at * HEAD_SIZE : (at + 1) * HEAD_SIZE] = part.astype(BF16)


def project(rows, weight, cosine, sine, first, count, turned):
    high, width = rows.shape
    columns = len(turned) * HEAD_SIZE
    return pl.pallas_call(
        functools.partial(project_kernel, turned=turned),
        grid=(count,),
        in_specs=[
            pl.BlockSpec((high, width), lambda j: (0, 0)),
            pl.BlockSpec((width, columns), lambda j: (0, first + j)),
            pl.BlockSpec((high, HEAD_SIZE), lambda j: (0, 0)),
            pl.BlockSpec((high, HEAD_SIZE), lambda j: (0, 0)),
        ],
        out_specs=pl.BlockSpec((high, columns), lambda j: (0, j)),
        out_shape=jax.ShapeDtypeStruct((high, count * columns), BF16),
        compiler_params=pltpu.CompilerParams(vmem_limit_bytes=VMEM_LIMIT),
        cost_estimate=LIGHT,
        name="project",
    )(rows, weight, cosine, sine)


def mask_bias(place_ref, segment_key_ref, segment_query_ref, bias_ref, seq_len):
    span, rows = bias_ref.shape
    start = place_ref[0]
    key_at = lax.broadcasted_iota(jnp.int32, (span, rows), 0)
    query_at = lax.broadcasted_iota(jnp.int32, (span, rows), 1) + ATTEND_SPAN
    distance = query_at - key_at
    position = start + query_at - ATTEND_SPAN
    sequence_at = query_at - lax.rem(position, seq_len)
    allowed = (distance >= 0) & (distance < ATTEND_SPAN) & (key_at >= sequence_at)
    allowed = allowed & (segment_key_ref[...] == segment_query_ref[...])
    bias_ref[...] = jnp.where(allowed, 0.0, -1e30)


def attention_kernel(
    place_ref,
    segment_key_ref,
    segment_query_ref,
    q_ref,
    kv_ref,
    heads_ref,
    lse_ref,
    bias_ref,
    *,
    seq_len,
    scale,
):
    @pl.when(pl.program_id(0) == 0)
    def _():
        mask_bias(place_ref, segment_key_ref, segment_query_ref, bias_ref, seq_len)

    rows = q_ref.shape[0]
    span = kv_ref.shape[0]
    count = q_ref.shape[1] // HEAD_SIZE
    value_t = kv_ref[:, HEAD_SIZE:].T
    chunks = span // rows
    for head in range(count):
        columns = slice(head * HEAD_SIZE, (head + 1) * HEAD_SIZE)
        query = q_ref[:, columns]
        scores = []
        for c in range(chunks):
            part = slice(c * rows, (c + 1) * rows)
            raw = mxu(kv_ref[part, :HEAD_SIZE], query, FROM_LAST)
            scores.append(raw * scale + bias_ref[part, :])
        top = functools.reduce(jnp.maximum, scores)
        top = jnp.max(top, axis=0, keepdims=True)
        total = jnp.zeros_like(top)
        out_t = jnp.zeros((HEAD_SIZE, rows), F32)
        for c in range(chunks):
            weight = jnp.exp(scores[c] - top)
            total = total + jnp.sum(weight, axis=0, keepdims=True)
            out_t = out_t + mxu(value_t[:, c * rows : (c + 1) * rows], weight.astype(BF16))
        heads_ref[:, columns] = (out_t / total).T.astype(BF16)
        lse_ref[0, head : head + 1, :] = top + jnp.log(total)


def attention(place, segment_key, segment_query, queries, key_value, seq_len):
    rows, all_columns = queries.shape
    span = key_value.shape[0]
    pairs = key_value.shape[1] // (2 * HEAD_SIZE)
    columns = all_columns // pairs
    return pl.pallas_call(
        functools.partial(attention_kernel, seq_len=seq_len, scale=1.0 / math.sqrt(HEAD_SIZE)),
        grid=(pairs,),
        in_specs=[
            pl.BlockSpec(memory_space=pltpu.SMEM),
            pl.BlockSpec((span, 1), lambda j: (0, 0)),
            pl.BlockSpec((1, rows), lambda j: (0, 0)),
            pl.BlockSpec((rows, columns), lambda j: (0, j)),
            pl.BlockSpec((span, 2 * HEAD_SIZE), lambda j: (0, j)),
        ],
        out_specs=[
            pl.BlockSpec((rows, columns), lambda j: (0, j)),
            pl.BlockSpec((1, columns // HEAD_SIZE, rows), lambda j: (j, 0, 0)),
        ],
        out_shape=[
            jax.ShapeDtypeStruct((rows, all_columns), BF16),
            jax.ShapeDtypeStruct((pairs, columns // HEAD_SIZE, rows), F32),
        ],
        scratch_shapes=[pltpu.VMEM((span, rows), F32)],
        compiler_params=pltpu.CompilerParams(vmem_limit_bytes=VMEM_LIMIT),
        cost_estimate=LIGHT,
        name="attention",
    )(place, segment_key, segment_query, queries, key_value)


def attention_back_kernel(
    place_ref,
    segment_key_ref,
    segment_query_ref,
    q_ref,
    kv_ref,
    lse_ref,
    dout_ref,
    cosine_ref,
    sine_ref,
    dq_ref,
    dkv_far_ref,
    dkv_own_ref,
    bias_ref,
    dkv_ref,
    *,
    seq_len,
    scale,
):
    @pl.when(pl.program_id(0) == 0)
    def _():
        mask_bias(place_ref, segment_key_ref, segment_query_ref, bias_ref, seq_len)

    rows = q_ref.shape[0]
    span = kv_ref.shape[0]
    count = q_ref.shape[1] // HEAD_SIZE
    key_t = kv_ref[:, :HEAD_SIZE].T
    chunks = span // rows
    dkv_ref[...] = jnp.zeros_like(dkv_ref)
    for head in range(count):
        columns = slice(head * HEAD_SIZE, (head + 1) * HEAD_SIZE)
        query = q_ref[:, columns]
        dout = dout_ref[:, columns]
        lse = lse_ref[0, head : head + 1, :]
        probs, dprobs = [], []
        row_dot = jnp.zeros_like(lse)
        for c in range(chunks):
            part = slice(c * rows, (c + 1) * rows)
            raw = mxu(kv_ref[part, :HEAD_SIZE], query, FROM_LAST)
            prob = jnp.exp(raw * scale + bias_ref[part, :] - lse)
            dprob = mxu(kv_ref[part, HEAD_SIZE:], dout, FROM_LAST)
            row_dot = row_dot + jnp.sum(prob * dprob, axis=0, keepdims=True)
            probs.append(prob)
            dprobs.append(dprob)
        dq_t = jnp.zeros((HEAD_SIZE, rows), F32)
        for c in range(chunks):
            part = slice(c * rows, (c + 1) * rows)
            dscore = (probs[c] * (dprobs[c] - row_dot)).astype(BF16)
            dkv_ref[part, :HEAD_SIZE] += mxu(dscore, query)
            dkv_ref[part, HEAD_SIZE:] += mxu(probs[c].astype(BF16), dout)
            dq_t = dq_t + mxu(key_t[:, part], dscore)
        dq_ref[:, columns] = turn(dq_t.T * scale, cosine_ref[...], -sine_ref[...]).astype(BF16)
    dkv_ref[:, :HEAD_SIZE] = dkv_ref[:, :HEAD_SIZE] * scale
    dkv_far_ref[...] = dkv_ref[: span - rows, :].astype(BF16)
    dkv_own_ref[...] = dkv_ref[span - rows :, :]


def attention_back(
    place, segment_key, segment_query, queries, key_value, lse, dout, cosine, sine, seq_len
):
    rows, all_columns = queries.shape
    span = key_value.shape[0]
    pairs = key_value.shape[1] // (2 * HEAD_SIZE)
    columns = all_columns // pairs
    return pl.pallas_call(
        functools.partial(
            attention_back_kernel, seq_len=seq_len, scale=1.0 / math.sqrt(HEAD_SIZE)
        ),
        grid=(pairs,),
        in_specs=[
            pl.BlockSpec(memory_space=pltpu.SMEM),
            pl.BlockSpec((span, 1), lambda j: (0, 0)),
            pl.BlockSpec((1, rows), lambda j: (0, 0)),
            pl.BlockSpec((rows, columns), lambda j: (0, j)),
            pl.BlockSpec((span, 2 * HEAD_SIZE), lambda j: (0, j)),
            pl.BlockSpec((1, columns // HEAD_SIZE, rows), lambda j: (j, 0, 0)),
            pl.BlockSpec((rows, columns), lambda j: (0, j)),
            pl.BlockSpec((rows, HEAD_SIZE), lambda j: (0, 0)),
            pl.BlockSpec((rows, HEAD_SIZE), lambda j: (0, 0)),
        ],
        out_specs=[
            pl.BlockSpec((rows, columns), lambda j: (0, j)),
            pl.BlockSpec((span - rows, 2 * HEAD_SIZE), lambda j: (0, j)),
            pl.BlockSpec((rows, 2 * HEAD_SIZE), lambda j: (0, j)),
        ],
        out_shape=[
            jax.ShapeDtypeStruct((rows, all_columns), BF16),
            jax.ShapeDtypeStruct((span - rows, key_value.shape[1]), BF16),
            jax.ShapeDtypeStruct((rows, key_value.shape[1]), F32),
        ],
        scratch_shapes=[
            pltpu.VMEM((span, rows), F32),
            pltpu.VMEM((span, 2 * HEAD_SIZE), F32),
        ],
        compiler_params=pltpu.CompilerParams(vmem_limit_bytes=VMEM_LIMIT),
        cost_estimate=pl.CostEstimate(
            flops=85_000_000_000, bytes_accessed=10_000_000, transcendentals=0
        ),
        name="attention_back",
    )(place, segment_key, segment_query, queries, key_value, lse, dout, cosine, sine)


def expert_kernel(
    slot_row_ref,
    slot_column_ref,
    routed_ref,
    own_ref,
    router_ref,
    tokens_ref,
    cotangent_ref,
    gate_ref,
    up_ref,
    down_ref,
    grad_ref,
    moe_ref,
    rows_in_ref,
    grad_out_ref,
    hidden_ref,
    grad_gate_ref,
    grad_up_ref,
    router_grad_ref,
    gate_full_ref,
    up_full_ref,
    down_full_ref,
    *,
    capacity,
):
    whole = ((gate_ref, gate_full_ref), (up_ref, up_full_ref), (down_ref, down_full_ref))

    @pl.when(pl.program_id(0) == 0)
    def _():
        for held, full in whole:
            columns = held.shape[3]
            for half in range(held.shape[1]):
                full[:, half * columns : (half + 1) * columns] = held[:, half].reshape(-1, columns)

    group_rows = tokens_ref.shape[1]
    tokens = tokens_ref[0]
    gate_weight, up_weight, down_weight = (full[...] for _, full in whole)
    cotangent = cotangent_ref[0]
    routed = routed_ref[0] > 0.0
    logits = jnp.where(routed, mxu(router_ref[...], tokens, FROM_LAST), -1e30)
    weights = jnp.exp(logits - jnp.max(logits, axis=0, keepdims=True))
    weights = jnp.where(routed, weights, 0.0)
    gates = weights / jnp.sum(weights, axis=0, keepdims=True)
    own = own_ref[...]
    gate_own = jnp.sum(gates * own, axis=0, keepdims=True)
    place = slot_row_ref[0] == lax.broadcasted_iota(jnp.int32, (capacity, group_rows), 0)
    place_wide = jnp.where(place, 1.0, 0.0)
    place_low = place_wide.astype(BF16)
    back = slot_column_ref[0] == lax.broadcasted_iota(jnp.int32, (group_rows, capacity), 1)
    back_low = jnp.where(back, 1.0, 0.0).astype(BF16)
    coefficient = jnp.sum(place_wide * gate_own, axis=1, keepdims=True)

    rows_in = mxu(place_low, tokens).astype(BF16)
    rows_in_ref[...] = rows_in
    gate_pre = mxu(rows_in, gate_weight)
    up_pre = mxu(rows_in, up_weight)
    sigmoid = 1.0 / (1.0 + jnp.exp(-gate_pre))
    silu = gate_pre * sigmoid
    hidden = (silu * up_pre).astype(BF16)
    hidden_ref[...] = hidden
    slot_cotangent = mxu(place_low, cotangent)
    grad_out = (coefficient * slot_cotangent).astype(BF16)
    grad_out_ref[...] = grad_out
    grad_hidden = mxu(grad_out, down_weight)
    grad_up = (grad_hidden * silu).astype(BF16)
    grad_gate = (grad_hidden * up_pre * sigmoid * (1.0 + gate_pre * (1.0 - sigmoid))).astype(BF16)
    grad_up_ref[...] = grad_up
    grad_gate_ref[...] = grad_gate
    expert_out = mxu(hidden, down_weight, FROM_LAST)
    grad_slot = jnp.sum(slot_cotangent * expert_out, axis=1, keepdims=True)
    moe_ref[0] = mxu(back_low, (coefficient * expert_out).astype(BF16)).astype(BF16)

    grad_token = jnp.sum(place_wide * grad_slot, axis=0, keepdims=True)
    share = (grad_token * gate_own) * (own - gates)
    share_high = share.astype(BF16)
    share_low = (share - share_high.astype(F32)).astype(BF16)
    router_grad = mxu(share_high, tokens) + mxu(share_low, tokens)

    @pl.when(pl.program_id(0) == 0)
    def _():
        router_grad_ref[...] = router_grad

    @pl.when(pl.program_id(0) > 0)
    def _():
        router_grad_ref[...] += router_grad

    grad_in = mxu(grad_gate, gate_weight, FROM_LAST) + mxu(grad_up, up_weight, FROM_LAST)
    grad_ref[0] = (
        mxu(back_low, grad_in.astype(BF16)) + mxu(share.T.astype(BF16), router_ref[...])
    ).astype(BF16)


def expert_groups(slot, routed, own, router_t, tokens, cotangent, weights, capacity):
    count, group_rows, width = tokens.shape
    ff = weights[0].shape[1] * weights[0].shape[3]
    experts = router_t.shape[0]
    weight = pl.BlockSpec(
        weights[0].shape, lambda g: (0, 0, 0, 0), pipeline_mode=pl.Buffered(1)
    )
    whole = lambda g: (0, 0)
    by_group = lambda g: (g, 0, 0)
    slots = lambda columns: pl.BlockSpec((capacity, columns), lambda g: (g, 0))
    slots_shape = lambda columns: jax.ShapeDtypeStruct((count * capacity, columns), BF16)
    return pl.pallas_call(
        functools.partial(expert_kernel, capacity=capacity),
        grid=(count,),
        in_specs=[
            pl.BlockSpec((1, 1, group_rows), by_group),
            pl.BlockSpec((1, group_rows, 1), by_group),
            pl.BlockSpec((1, experts, group_rows), by_group),
            pl.BlockSpec((experts, 1), whole),
            pl.BlockSpec((experts, width), whole),
            pl.BlockSpec((1, group_rows, width), by_group),
            pl.BlockSpec((1, group_rows, width), by_group),
            weight,
            weight,
            weight,
        ],
        out_specs=[
            pl.BlockSpec((1, group_rows, width), by_group),
            pl.BlockSpec((1, group_rows, width), by_group),
            slots(width),
            slots(width),
            slots(ff),
            slots(ff),
            slots(ff),
            pl.BlockSpec((experts, width), whole),
        ],
        out_shape=[
            jax.ShapeDtypeStruct(tokens.shape, BF16),
            jax.ShapeDtypeStruct(tokens.shape, BF16),
            slots_shape(width),
            slots_shape(width),
            slots_shape(ff),
            slots_shape(ff),
            slots_shape(ff),
            jax.ShapeDtypeStruct((experts, width), F32),
        ],
        scratch_shapes=[pltpu.VMEM((width, ff), BF16) for _ in range(3)],
        compiler_params=pltpu.CompilerParams(vmem_limit_bytes=VMEM_LIMIT),
        cost_estimate=LIGHT,
        name="expert",
    )(
        slot[:, None, :],
        slot[:, :, None],
        routed,
        own,
        router_t,
        tokens,
        cotangent,
        *weights,
    )


def weight_grad_kernel(*refs, halves):
    rows, grad_out, hidden, grad_gate, grad_up, router = (
        refs[at : at + 2] for at in range(0, 12, 2)
    )
    moe_kept_ref, moe_got_ref, out_ref = refs[12:15]
    for at, moe_ref in enumerate(refs[15:]):
        moe_ref[...] = (moe_kept_ref[at].astype(F32) + moe_got_ref[at].astype(F32)).astype(BF16)
    columns = hidden[0].shape[1] // halves
    over = (((0,), (0,)), ((), ()))
    left_rows = [ref[...] for ref in rows]
    left_out = [ref[...] for ref in grad_out]
    router_columns = (router[0][...] + router[1][...]).T
    router_columns = jnp.concatenate(
        [
            router_columns,
            jnp.zeros((router_columns.shape[0], HEAD_SIZE - router_columns.shape[1]), F32),
        ],
        axis=1,
    ).astype(BF16)
    for half in range(halves):
        start = half * (3 * columns + HEAD_SIZE)
        part = slice(half * columns, (half + 1) * columns)
        for at, (left, right) in enumerate(
            ((left_rows, grad_gate), (left_rows, grad_up), (left_out, hidden))
        ):
            total = mxu(left[0], right[0][:, part], over) + mxu(left[1], right[1][:, part], over)
            out_ref[:, start + at * columns : start + (at + 1) * columns] = total.astype(BF16)
        out_ref[:, start + 3 * columns : start + 3 * columns + HEAD_SIZE] = router_columns


def weight_grads(near, far, moe_kept, moe_got, halves, block=256):
    rows_at, grad_out_at, hidden_at, grad_gate_at, grad_up_at, router_at = range(6)
    slots, width = near[rows_at].shape
    ff = near[hidden_at].shape[1]
    experts = near[router_at].shape[0]
    specs, operands = [], []
    for at in (rows_at, grad_out_at, hidden_at, grad_gate_at, grad_up_at, router_at):
        if at in (rows_at, grad_out_at):
            spec = pl.BlockSpec((slots, block), lambda i: (0, i))
        elif at == router_at:
            spec = pl.BlockSpec((experts, block), lambda i: (0, i))
        else:
            spec = pl.BlockSpec((slots, ff), lambda i: (0, 0))
        specs += [spec, spec]
        operands += [near[at], far[at]]
    columns = 3 * ff + halves * HEAD_SIZE
    moe_count, moe_rows, _ = moe_kept.shape
    moe_spec = pl.BlockSpec((moe_count, moe_rows, block), lambda i: (0, 0, i))
    moe_out_spec = pl.BlockSpec((moe_rows, block), lambda i: (0, i))
    return pl.pallas_call(
        functools.partial(weight_grad_kernel, halves=halves),
        grid=(width // block,),
        in_specs=specs + [moe_spec, moe_spec],
        out_specs=[pl.BlockSpec((block, columns), lambda i: (i, 0))] + [moe_out_spec] * moe_count,
        out_shape=[jax.ShapeDtypeStruct((width, columns), BF16)]
        + [jax.ShapeDtypeStruct((moe_rows, width), BF16)] * moe_count,
        compiler_params=pltpu.CompilerParams(vmem_limit_bytes=VMEM_LIMIT),
        cost_estimate=pl.CostEstimate(
            flops=15_000_000_000, bytes_accessed=50_000_000, transcendentals=0
        ),
        name="weight_grads",
    )(*operands, moe_kept, moe_got)


def on_device(
    block_input,
    norm_gains,
    router_weight,
    query_matrix,
    key_matrix,
    value_matrix,
    output_weight,
    gate_weight,
    up_weight,
    down_weight,
    segment_ids,
    routes,
    priority,
    cotangent,
):
    tensor_index = lax.axis_index("tensor")
    own_rows, width = block_input.shape
    group_rows = segment_ids.shape[0]
    halves = lax.axis_size("tensor")
    outer = lax.axis_size("outer")
    groups = lax.axis_size("x") * lax.axis_size("core")
    plane = groups * halves
    shard_rows = query_matrix.shape[0]
    dp_size = outer * groups
    seq_len = min(SEQ_MOST, group_rows * dp_size)
    own_start = lax.axis_index(ALL) * own_rows
    capacity = group_rows * TOPK // EXPERTS
    reach = ATTEND_SPAN // own_rows
    half_ff = gate_weight.shape[2]
    ff = half_ff * halves

    query_columns = query_matrix.shape[1]
    pair_columns = 2 * halves * HEAD_SIZE
    first = tensor_index == 0
    key_value_weight = jnp.concatenate([key_matrix, value_matrix], axis=1)
    other_weight = swap(key_value_weight, "tensor")
    early = jnp.concatenate(
        [
            jnp.where(first, key_value_weight, other_weight),
            jnp.where(first, other_weight, key_value_weight),
            query_matrix,
            output_weight,
        ],
        axis=1,
    )
    early, gate_own, up_own, down_own, cotangent_own = lax.optimization_barrier(
        (early, gate_weight, up_weight, down_weight, cotangent)
    )
    early = outer_gather(early)

    expert_shard = jnp.transpose(jnp.stack([gate_own, up_own, down_own]), (2, 0, 1, 3))
    expert_shard = lax.all_to_all(expert_shard, PLANE, 0, 0, tiled=True)
    expert_shard = expert_shard.reshape(groups, halves, 3, shard_rows, half_ff)
    expert_shard = [
        jnp.swapaxes(expert_shard[:, :, at], 0, 1).reshape(-1, half_ff) for at in range(3)
    ]
    early, expert_shard, segment_here, priority_here = lax.optimization_barrier(
        (early, expert_shard, segment_ids, priority)
    )
    pair_count = group_rows * TOPK
    rank = (
        jnp.zeros((pair_count,), jnp.int32)
        .at[priority_here]
        .set(jnp.arange(pair_count, dtype=jnp.int32))
        .reshape(group_rows, TOPK)
    )
    expert_ids = jnp.arange(EXPERTS, dtype=jnp.int32)
    named = routes[:, :, None] == expert_ids[None, None, :]
    ranked = jnp.sum(jnp.where(named, rank[:, :, None] + 1, 0), axis=1)
    ranked = jnp.where(ranked > 0, ranked, pair_count + 1)
    ranked_own = lax.dynamic_slice_in_dim(ranked, tensor_index * own_rows, own_rows, 0)
    digits = jnp.concatenate([ranked_own // 64, ranked_own % 64], axis=1).astype(BF16)
    digits = jnp.pad(digits, ((0, 0), (0, HEAD_SIZE - digits.shape[1])))
    cotangent_sent = jnp.concatenate([cotangent_own, digits], axis=1)
    segment_near = jnp.concatenate(
        [shift_groups(segment_here, 2), shift_groups(segment_here, 1), segment_here]
    )
    expert_full = [
        lax.all_gather(shard, "outer").reshape(outer, halves, groups * shard_rows, half_ff)
        for shard in expert_shard
    ]

    key_value_full = early[:, :, :pair_columns]
    key_value_full = in_order(key_value_full, swap(key_value_full, "x"), "x", 1)
    key_value_full = in_order(key_value_full, swap(key_value_full, "core"), "core", 2)
    key_value_full = key_value_full.reshape(width, pair_columns)
    query_parts = plane_parts(early[:, :, pair_columns : pair_columns + query_columns])

    input_wide = block_input.astype(F32)
    first_gain = norm_gains[:, 0]
    second_gain = norm_gains[:, 1]
    first_factor = norm_factor(input_wide)
    normed_in = (input_wide * first_factor * first_gain).astype(BF16)
    positions = own_start + jnp.arange(own_rows, dtype=jnp.int32)
    cosine, sine = rotary_tables(positions % seq_len)
    query_blocks = halves * query_columns // (2 * HEAD_SIZE)
    key_value_sent = project(
        normed_in, key_value_full, cosine, sine, 0, halves, (True, False)
    )
    one_back, two_back = shift_groups(key_value_sent, 1), shift_groups(key_value_sent, 2)
    query_parts, one_back, two_back, segment_near, cotangent_sent, expert_full[0] = (
        lax.optimization_barrier(
            (query_parts, one_back, two_back, segment_near, cotangent_sent, expert_full[0])
        )
    )
    cotangent_parts = plane_parts(cotangent_sent)
    output_own = early[:, :, pair_columns + query_columns :]
    pair_sent = jnp.where(
        first,
        jnp.stack([one_back, key_value_sent]),
        jnp.stack([two_back, one_back]),
    )
    pair_got = swap(pair_sent, "tensor")
    query_near = plane_stack(query_parts)
    query_far, pair_got = lax.optimization_barrier((swap(query_near, "core"), pair_got))
    pieces = [two_back, pair_got[0], one_back, pair_got[1], key_value_sent]
    query_full = whole_weight(query_near, query_far)
    queries = project(normed_in, query_full, cosine, sine, 0, query_blocks, (True, True))
    output_parts = plane_parts(output_own)
    expert = lax.axis_index(PLANE)

    def slots_of(cotangents):
        digits = cotangents[..., width:].reshape(2, group_rows, HEAD_SIZE).astype(jnp.int32)
        ranked_all = digits[..., :EXPERTS] * 64 + digits[..., EXPERTS : 2 * EXPERTS]
        routed = jnp.swapaxes((ranked_all <= pair_count).astype(F32), 1, 2)
        rank_own = jnp.sum(jnp.where(expert_ids == expert, ranked_all, 0), axis=-1)
        earlier = (rank_own[:, None, :] < rank_own[:, :, None]).astype(jnp.int32)
        slot = jnp.where(rank_own <= pair_count, jnp.sum(earlier, axis=-1), capacity)
        return slot, routed

    key_value = jnp.concatenate(pieces, axis=0)
    span = ATTEND_SPAN + own_rows
    segment_ext = lax.dynamic_slice_in_dim(segment_near, tensor_index * own_rows, span)
    view = (
        jnp.reshape(own_start, (1,)),
        segment_ext[:, None],
        segment_ext[None, ATTEND_SPAN:],
        queries,
        key_value,
    )
    heads_low, log_total = attention(*view, seq_len)
    heads_late, output_parts, cotangent_parts = lax.optimization_barrier(
        (heads_low, output_parts, cotangent_parts)
    )
    output_near = plane_stack(output_parts)
    output_far = swap(output_near, "core")
    output_full, expert_full[1] = lax.optimization_barrier(
        (whole_weight(output_near, output_far), expert_full[1])
    )
    hidden_state = input_wide + dot(heads_low, output_full, ((1,), (1,)))
    second_factor = norm_factor(hidden_state)
    normed_mid_own = (hidden_state * second_factor * second_gain).astype(BF16)

    cotangent_near = plane_stack(cotangent_parts)
    cotangent_far = swap(cotangent_near, "core")
    near_slots, far_slots = slots_of(cotangent_near), slots_of(cotangent_far)
    normed_parts, near_slots, far_slots, expert_full[2] = lax.optimization_barrier(
        (plane_parts(normed_mid_own), near_slots, far_slots, expert_full[2])
    )
    normed_near = plane_stack(normed_parts)
    normed_far = swap(normed_near, "core")
    own_expert = (expert_ids == expert).astype(F32)[:, None]
    router_t = router_weight.T

    def experts_on(tokens, cotangents, slots):
        slot, routed = slots
        return expert_groups(
            slot,
            routed,
            own_expert,
            router_t,
            tokens.reshape(2, group_rows, width),
            cotangents.reshape(2, group_rows, -1),
            expert_full,
            capacity,
        )

    on_near = experts_on(normed_near, cotangent_near, near_slots)
    on_far = experts_on(normed_far, cotangent_far, far_slots)
    blocks = (2 * halves, own_rows, width)
    (grad_near, moe_near), (grad_far, moe_far) = (
        [array.reshape(blocks) for array in side[:2]] for side in (on_near, on_far)
    )
    grad_blocks = fold_blocks(grad_near, swap(grad_far, "core"))
    grad_blocks, moe_far, on_near, on_far = lax.optimization_barrier(
        (grad_blocks, moe_far, on_near[2:], on_far[2:])
    )
    grad_mid_parts = fold_plane(grad_blocks)
    expert_part, *moe_blocks = weight_grads(
        on_near, on_far, moe_near, swap(moe_far, "core"), halves
    )
    expert_sum = lax.psum_scatter(expert_part, "outer", scatter_dimension=0, tiled=True)
    grad_mid_parts, moe_blocks = lax.optimization_barrier((grad_mid_parts, moe_blocks))
    moe_parts = fold_plane(moe_blocks)
    grad_mid = wide_sum(grad_mid_parts)

    norm_input_part = norm_back(hidden_state, second_factor, second_gain, grad_mid)
    grad_state = cotangent.astype(F32) + norm_input_part
    grad_attn = grad_state.astype(BF16)
    grad_heads = dot(grad_attn, output_full, ((1,), (0,))).astype(BF16)
    output_total = fold_columns(grad_attn, heads_late, shard_rows)
    grad_query_pre, grad_far_kv, grad_own = attention_back(
        *view, log_total, grad_heads, cosine, sine, seq_len
    )
    grad_query_pre, output_total, moe_parts = lax.optimization_barrier(
        (grad_query_pre, output_total, moe_parts)
    )
    output_parts = fold_plane(distance_blocks(output_total))
    query_total = fold_columns(normed_in, grad_query_pre, shard_rows)
    two_back, pair_old, one_back, pair_new = grad_far_kv.reshape(reach, own_rows, -1)
    pair_got, output_parts, query_total = lax.optimization_barrier(
        (swap(jnp.stack([pair_old, pair_new]), "tensor"), output_parts, query_total)
    )
    query_parts = fold_plane(distance_blocks(query_total))
    pair_old, pair_new = pair_got.astype(F32)
    one_back = one_back.astype(F32) + jnp.where(first, pair_old, pair_new)
    two_back = two_back.astype(F32) + jnp.where(first, 0.0, pair_old)
    grad_own = grad_own + jnp.where(first, pair_new, 0.0)
    grad_own = grad_own + shift_groups(one_back.astype(BF16), -1).astype(F32)
    grad_own = grad_own + shift_groups(two_back.astype(BF16), -2).astype(F32)
    query_parts, output_parts, expert_sum = lax.optimization_barrier(
        (query_parts, output_parts, expert_sum)
    )
    output_weight_grad = outer_scatter(wide_sum(output_parts).astype(BF16))
    grad_key_value = []
    for half in range(halves):
        start = half * 2 * HEAD_SIZE
        key_part = grad_own[:, start : start + HEAD_SIZE]
        turned = jnp.concatenate(
            [key_part[:, HEAD_SIZE // 2 :], key_part[:, : HEAD_SIZE // 2]], axis=1
        )
        grad_key_value.append(key_part * cosine - turned * sine)
        grad_key_value.append(grad_own[:, start + HEAD_SIZE : start + 2 * HEAD_SIZE])
    grad_key_value_pre = jnp.concatenate(grad_key_value, axis=1).astype(BF16)
    key_value_total = fold_columns(normed_in, grad_key_value_pre, shard_rows)
    key_value_parts = fold_plane(distance_blocks(key_value_total))
    grad_in = dot(grad_query_pre, query_full, ((1,), (1,))) + dot(
        grad_key_value_pre, key_value_full, ((1,), (1,))
    )
    input_grad = grad_state + norm_back(input_wide, first_factor, first_gain, grad_in)
    qkv_grad = outer_scatter(
        jnp.concatenate([wide_sum(query_parts), wide_sum(key_value_parts)], axis=2).astype(BF16)
    )
    block_output = hidden_state + wide_sum(moe_parts)
    expert_sum = expert_sum.reshape(groups, shard_rows, halves, -1)
    expert_sum = jnp.swapaxes(expert_sum, 1, 2).reshape(plane, shard_rows, -1)
    expert_sum = lax.all_to_all(expert_sum, PLANE, 0, 0, tiled=True)
    gate_grad, up_grad, down_grad = (
        jnp.swapaxes(expert_sum[:, :, at * half_ff : (at + 1) * half_ff], 0, 1).astype(F32)
        for at in range(3)
    )
    router_grad = jnp.sum(expert_sum[:, :, 3 * half_ff : 3 * half_ff + EXPERTS].astype(F32), axis=0)
    router_grad = lax.dynamic_slice_in_dim(
        router_grad, tensor_index * (shard_rows // 2), shard_rows // 2, 0
    )
    query_grad = qkv_grad[:, :query_columns]
    key_grad = qkv_grad[:, query_columns : query_columns + HEAD_SIZE]
    value_grad = qkv_grad[:, query_columns + HEAD_SIZE :]

    half_rows = shard_rows // 2
    own_gains = lax.dynamic_slice_in_dim(
        norm_gains, lax.axis_index(DP) * shard_rows, shard_rows, 0
    )
    qkv_own = jnp.concatenate([query_matrix, key_value_weight], axis=1)
    first_sum = jnp.sum(qkv_grad * qkv_own.astype(F32), axis=-1)
    second_sum = jnp.sum(
        gate_grad * gate_weight.astype(F32) + up_grad * up_weight.astype(F32), axis=(1, 2)
    )
    gain_sums = jnp.stack([first_sum, second_sum], axis=1) / own_gains
    kept = lax.dynamic_slice_in_dim(gain_sums, tensor_index * half_rows, half_rows, 0)
    sent = lax.dynamic_slice_in_dim(gain_sums, (1 - tensor_index) * half_rows, half_rows, 0)
    own_router = lax.dynamic_slice_in_dim(
        router_weight, lax.axis_index(ALL) * half_rows, half_rows, 0
    )
    router_sum = jnp.sum(router_grad * own_router.astype(F32), axis=-1)
    half_gains = lax.dynamic_slice_in_dim(own_gains, tensor_index * half_rows, half_rows, 0)
    router_sum = router_sum / half_gains[:, 1]
    gains_grad = (
        kept
        + swap(sent, "tensor")
        + jnp.stack([jnp.zeros_like(router_sum), router_sum], axis=1)
    )
    return (
        block_output,
        input_grad,
        gains_grad,
        router_grad,
        query_grad,
        key_grad,
        value_grad,
        output_weight_grad,
        gate_grad,
        up_grad,
        down_grad,
    )


def solution(mesh):
    dp_size, tensor_size = mesh.shape["dp"], mesh.shape["tensor"]
    split = Mesh(mesh.devices.reshape(dp_size // 4, 2, 2, tensor_size), ALL)
    return jax.shard_map(
        on_device,
        mesh=split,
        in_specs=(
            P(ALL, None),
            P(),
            P(),
            P(DP, "tensor"),
            P(DP, "tensor"),
            P(DP, "tensor"),
            P(DP, "tensor"),
            P(DP, None, "tensor"),
            P(DP, None, "tensor"),
            P(DP, None, "tensor"),
            P(DP),
            P(DP, None),
            P(DP),
            P(ALL, None),
        ),
        out_specs=(
            P(ALL, None),
            P(ALL, None),
            P(ALL, None),
            P(ALL, None),
            P(DP, "tensor"),
            P(DP, "tensor"),
            P(DP, "tensor"),
            P(DP, "tensor"),
            P(DP, None, "tensor"),
            P(DP, None, "tensor"),
            P(DP, None, "tensor"),
        ),
        check_vma=False,
    )
```

```python
import functools
import math

import jax
import jax.numpy as jnp
from jax import lax
from jax.experimental import pallas as pl
from jax.experimental.pallas import tpu as pltpu
from jax.sharding import Mesh
from jax.sharding import PartitionSpec as P

HEAD_SIZE = 128
TOPK = 4
EXPERTS = 8
ATTEND_SPAN = 1024
SEQ_MOST = 16384
EPSILON = 1e-06
ROPE_BASE = 10000.0
BF16 = jnp.bfloat16
F32 = jnp.float32

DP = ("outer", "x", "core")
PLANE = ("x", "core", "tensor")
ALL = ("outer", "x", "core", "tensor")


def shift_groups(x, by):
    length = lax.axis_size(DP)
    return lax.ppermute(x, DP, [(i, i + by) for i in range(length) if 0 <= i + by < length])


def swap(x, axis):
    length = lax.axis_size(axis)
    return lax.ppermute(x, axis, [(i, length - 1 - i) for i in range(length)])


def plane_parts(own):
    return [own, swap(own, "tensor"), swap(own, "x"), swap(own, ("x", "tensor"))]


def plane_stack(parts):
    return jnp.stack(parts).reshape((2, 2) + parts[0].shape)


def whole_weight(near, far):
    x, tensor = lax.axis_index("x"), lax.axis_index("tensor")
    first = lax.axis_index("core") == 0
    by_core = [jnp.where(first, near, far), jnp.where(first, far, near)]

    def piece(x_at, core_at, tensor_at):
        picked = lax.dynamic_index_in_dim(by_core[core_at], x ^ x_at, 0, keepdims=False)
        return lax.dynamic_index_in_dim(picked, tensor ^ tensor_at, 0, keepdims=False)

    places = [(x_at, core_at) for x_at in range(2) for core_at in range(2)]
    halves = [jnp.stack([piece(*place, at) for place in places], 1) for at in range(2)]
    return jnp.concatenate(halves, axis=-1).reshape(-1, 2 * near.shape[-1])


def fold_core(kept, sent):
    return (kept.astype(F32) + swap(sent, "core").astype(F32)).astype(BF16)


def fold_blocks(kept, got):
    return [
        (kept[at].astype(F32) + got[at].astype(F32)).astype(BF16) for at in range(kept.shape[0])
    ]


def in_order(own, other, axis_name, axis):
    first = lax.axis_index(axis_name) == 0
    return jnp.stack([jnp.where(first, own, other), jnp.where(first, other, own)], axis)


def fold_plane(blocks):
    return [
        blocks[0],
        swap(blocks[1], "tensor"),
        swap(blocks[2], "x"),
        swap(blocks[3], ("x", "tensor")),
    ]


def wide_sum(parts):
    return sum(part.astype(F32) for part in parts)


def outer_shift(x, by):
    length = lax.axis_size("outer")
    return lax.ppermute(x, "outer", [(i, (i + by) % length) for i in range(length)])


def outer_gather(shard):
    length, here = lax.axis_size("outer"), lax.axis_index("outer")
    if length > 4:
        return lax.all_gather(shard, "outer")
    full = jnp.zeros((length,) + shard.shape, shard.dtype)
    for by in range(length):
        piece = outer_shift(shard, by) if by else shard
        full = lax.dynamic_update_slice_in_dim(full, piece[None], (here - by) % length, 0)
    return full


def outer_scatter(parts):
    length, here = lax.axis_size("outer"), lax.axis_index("outer")
    if length > 4:
        return lax.psum_scatter(parts, "outer", scatter_dimension=0, tiled=False).astype(F32)
    pieces = [
        lax.dynamic_index_in_dim(parts, (here + by) % length, 0, keepdims=False)
        for by in range(length)
    ]
    return wide_sum([pieces[0]] + [outer_shift(pieces[by], by) for by in range(1, length)])


def core_columns(rows, core_at, shard_rows):
    count = rows.shape[0]
    split = rows.reshape(count, -1, 2, shard_rows)
    return lax.dynamic_index_in_dim(split, core_at, 2, keepdims=False).reshape(count, -1)


def fold_columns(left, right, shard_rows):
    core = lax.axis_index("core")
    sent = dot(core_columns(left, 1 - core, shard_rows), right, ((0,), (0,))).astype(BF16)
    kept = dot(core_columns(left, core, shard_rows), right, ((0,), (0,))).astype(BF16)
    return fold_core(kept, sent).reshape(-1, 2, shard_rows, right.shape[1])


def distance_blocks(total):
    x, tensor = lax.axis_index("x"), lax.axis_index("tensor")
    columns = total.shape[3] // 2
    blocks = []
    for x_by in range(2):
        for tensor_by in range(2):
            block = lax.dynamic_index_in_dim(total, x ^ x_by, 1, keepdims=False)
            start = (tensor ^ tensor_by) * columns
            blocks.append(lax.dynamic_slice_in_dim(block, start, columns, 2))
    return blocks


def rotary_tables(position):
    halfway = HEAD_SIZE // 2
    inverse = jnp.exp(
        jnp.arange(halfway, dtype=F32) * (-2.0 * math.log(ROPE_BASE) / HEAD_SIZE)
    )
    angles = position.astype(F32)[:, None] * inverse[None, :]
    cosine, sine = jnp.cos(angles), jnp.sin(angles)
    return (
        jnp.concatenate([cosine, cosine], axis=1),
        jnp.concatenate([-sine, sine], axis=1),
    )


def norm_factor(value_rows):
    return lax.rsqrt(jnp.mean(value_rows * value_rows, axis=-1, keepdims=True) + EPSILON)


def norm_back(value_rows, factor, gain, upstream):
    weighted = upstream * gain
    return factor * weighted - value_rows * (factor * factor * factor) * jnp.mean(
        weighted * value_rows, axis=-1, keepdims=True
    )


def dot(a, b, dims):
    return lax.dot_general(a, b, (dims, ((), ())), preferred_element_type=F32)


VMEM_LIMIT = 60 * 1024 * 1024
LIGHT = pl.CostEstimate(flops=1000, bytes_accessed=1000, transcendentals=0)
FROM_LAST = (((1,), (1,)), ((), ()))
PLAIN = (((1,), (0,)), ((), ()))


def mxu(a, b, dims=PLAIN):
    return lax.dot_general(a, b, dims, preferred_element_type=F32)


def turn(rows, cosine, sine):
    return rows * cosine + pltpu.roll(rows, HEAD_SIZE // 2, 1) * sine


def project_kernel(rows_ref, weight_ref, cosine_ref, sine_ref, out_ref, *, turned):
    product = mxu(rows_ref[...], weight_ref[...])
    for at, turns in enumerate(turned):
        part = product[:, at * HEAD_SIZE : (at + 1) * HEAD_SIZE]
        if turns:
            part = turn(part, cosine_ref[...], sine_ref[...])
        out_ref[:, at * HEAD_SIZE : (at + 1) * HEAD_SIZE] = part.astype(BF16)


def project(rows, weight, cosine, sine, first, count, turned):
    high, width = rows.shape
    columns = len(turned) * HEAD_SIZE
    return pl.pallas_call(
        functools.partial(project_kernel, turned=turned),
        grid=(count,),
        in_specs=[
            pl.BlockSpec((high, width), lambda j: (0, 0)),
            pl.BlockSpec((width, columns), lambda j: (0, first + j)),
            pl.BlockSpec((high, HEAD_SIZE), lambda j: (0, 0)),
            pl.BlockSpec((high, HEAD_SIZE), lambda j: (0, 0)),
        ],
        out_specs=pl.BlockSpec((high, columns), lambda j: (0, j)),
        out_shape=jax.ShapeDtypeStruct((high, count * columns), BF16),
        compiler_params=pltpu.CompilerParams(vmem_limit_bytes=VMEM_LIMIT),
        cost_estimate=LIGHT,
        name="project",
    )(rows, weight, cosine, sine)


def mask_bias(place_ref, segment_key_ref, segment_query_ref, bias_ref, seq_len):
    span, rows = bias_ref.shape
    start = place_ref[0]
    key_at = lax.broadcasted_iota(jnp.int32, (span, rows), 0)
    query_at = lax.broadcasted_iota(jnp.int32, (span, rows), 1) + ATTEND_SPAN
    distance = query_at - key_at
    position = start + query_at - ATTEND_SPAN
    sequence_at = query_at - lax.rem(position, seq_len)
    allowed = (distance >= 0) & (distance < ATTEND_SPAN) & (key_at >= sequence_at)
    allowed = allowed & (segment_key_ref[...] == segment_query_ref[...])
    bias_ref[...] = jnp.where(allowed, 0.0, -1e30)


def attention_kernel(
    place_ref,
    segment_key_ref,
    segment_query_ref,
    q_ref,
    kv_ref,
    heads_ref,
    lse_ref,
    bias_ref,
    *,
    seq_len,
    scale,
):
    @pl.when(pl.program_id(0) == 0)
    def _():
        mask_bias(place_ref, segment_key_ref, segment_query_ref, bias_ref, seq_len)

    rows = q_ref.shape[0]
    span = kv_ref.shape[0]
    count = q_ref.shape[1] // HEAD_SIZE
    value_t = kv_ref[:, HEAD_SIZE:].T
    chunks = span // rows
    for head in range(count):
        columns = slice(head * HEAD_SIZE, (head + 1) * HEAD_SIZE)
        query = q_ref[:, columns]
        scores = []
        for c in range(chunks):
            part = slice(c * rows, (c + 1) * rows)
            raw = mxu(kv_ref[part, :HEAD_SIZE], query, FROM_LAST)
            scores.append(raw * scale + bias_ref[part, :])
        top = functools.reduce(jnp.maximum, scores)
        top = jnp.max(top, axis=0, keepdims=True)
        total = jnp.zeros_like(top)
        out_t = jnp.zeros((HEAD_SIZE, rows), F32)
        for c in range(chunks):
            weight = jnp.exp(scores[c] - top)
            total = total + jnp.sum(weight, axis=0, keepdims=True)
            out_t = out_t + mxu(value_t[:, c * rows : (c + 1) * rows], weight.astype(BF16))
        heads_ref[:, columns] = (out_t / total).T.astype(BF16)
        lse_ref[0, head : head + 1, :] = top + jnp.log(total)


def attention(place, segment_key, segment_query, queries, key_value, seq_len):
    rows, all_columns = queries.shape
    span = key_value.shape[0]
    pairs = key_value.shape[1] // (2 * HEAD_SIZE)
    columns = all_columns // pairs
    return pl.pallas_call(
        functools.partial(attention_kernel, seq_len=seq_len, scale=1.0 / math.sqrt(HEAD_SIZE)),
        grid=(pairs,),
        in_specs=[
            pl.BlockSpec(memory_space=pltpu.SMEM),
            pl.BlockSpec((span, 1), lambda j: (0, 0)),
            pl.BlockSpec((1, rows), lambda j: (0, 0)),
            pl.BlockSpec((rows, columns), lambda j: (0, j)),
            pl.BlockSpec((span, 2 * HEAD_SIZE), lambda j: (0, j)),
        ],
        out_specs=[
            pl.BlockSpec((rows, columns), lambda j: (0, j)),
            pl.BlockSpec((1, columns // HEAD_SIZE, rows), lambda j: (j, 0, 0)),
        ],
        out_shape=[
            jax.ShapeDtypeStruct((rows, all_columns), BF16),
            jax.ShapeDtypeStruct((pairs, columns // HEAD_SIZE, rows), F32),
        ],
        scratch_shapes=[pltpu.VMEM((span, rows), F32)],
        compiler_params=pltpu.CompilerParams(vmem_limit_bytes=VMEM_LIMIT),
        cost_estimate=LIGHT,
        name="attention",
    )(place, segment_key, segment_query, queries, key_value)


def attention_back_kernel(
    place_ref,
    segment_key_ref,
    segment_query_ref,
    q_ref,
    kv_ref,
    lse_ref,
    dout_ref,
    cosine_ref,
    sine_ref,
    dq_ref,
    dkv_far_ref,
    dkv_own_ref,
    bias_ref,
    dkv_ref,
    *,
    seq_len,
    scale,
):
    @pl.when(pl.program_id(0) == 0)
    def _():
        mask_bias(place_ref, segment_key_ref, segment_query_ref, bias_ref, seq_len)

    rows = q_ref.shape[0]
    span = kv_ref.shape[0]
    count = q_ref.shape[1] // HEAD_SIZE
    key_t = kv_ref[:, :HEAD_SIZE].T
    chunks = span // rows
    dkv_ref[...] = jnp.zeros_like(dkv_ref)
    for head in range(count):
        columns = slice(head * HEAD_SIZE, (head + 1) * HEAD_SIZE)
        query = q_ref[:, columns]
        dout = dout_ref[:, columns]
        lse = lse_ref[0, head : head + 1, :]
        probs, dprobs = [], []
        row_dot = jnp.zeros_like(lse)
        for c in range(chunks):
            part = slice(c * rows, (c + 1) * rows)
            raw = mxu(kv_ref[part, :HEAD_SIZE], query, FROM_LAST)
            prob = jnp.exp(raw * scale + bias_ref[part, :] - lse)
            dprob = mxu(kv_ref[part, HEAD_SIZE:], dout, FROM_LAST)
            row_dot = row_dot + jnp.sum(prob * dprob, axis=0, keepdims=True)
            probs.append(prob)
            dprobs.append(dprob)
        dq_t = jnp.zeros((HEAD_SIZE, rows), F32)
        for c in range(chunks):
            part = slice(c * rows, (c + 1) * rows)
            dscore = (probs[c] * (dprobs[c] - row_dot)).astype(BF16)
            dkv_ref[part, :HEAD_SIZE] += mxu(dscore, query)
            dkv_ref[part, HEAD_SIZE:] += mxu(probs[c].astype(BF16), dout)
            dq_t = dq_t + mxu(key_t[:, part], dscore)
        dq_ref[:, columns] = turn(dq_t.T * scale, cosine_ref[...], -sine_ref[...]).astype(BF16)
    dkv_ref[:, :HEAD_SIZE] = dkv_ref[:, :HEAD_SIZE] * scale
    dkv_far_ref[...] = dkv_ref[: span - rows, :].astype(BF16)
    dkv_own_ref[...] = dkv_ref[span - rows :, :]


def attention_back(
    place, segment_key, segment_query, queries, key_value, lse, dout, cosine, sine, seq_len
):
    rows, all_columns = queries.shape
    span = key_value.shape[0]
    pairs = key_value.shape[1] // (2 * HEAD_SIZE)
    columns = all_columns // pairs
    return pl.pallas_call(
        functools.partial(
            attention_back_kernel, seq_len=seq_len, scale=1.0 / math.sqrt(HEAD_SIZE)
        ),
        grid=(pairs,),
        in_specs=[
            pl.BlockSpec(memory_space=pltpu.SMEM),
            pl.BlockSpec((span, 1), lambda j: (0, 0)),
            pl.BlockSpec((1, rows), lambda j: (0, 0)),
            pl.BlockSpec((rows, columns), lambda j: (0, j)),
            pl.BlockSpec((span, 2 * HEAD_SIZE), lambda j: (0, j)),
            pl.BlockSpec((1, columns // HEAD_SIZE, rows), lambda j: (j, 0, 0)),
            pl.BlockSpec((rows, columns), lambda j: (0, j)),
            pl.BlockSpec((rows, HEAD_SIZE), lambda j: (0, 0)),
            pl.BlockSpec((rows, HEAD_SIZE), lambda j: (0, 0)),
        ],
        out_specs=[
            pl.BlockSpec((rows, columns), lambda j: (0, j)),
            pl.BlockSpec((span - rows, 2 * HEAD_SIZE), lambda j: (0, j)),
            pl.BlockSpec((rows, 2 * HEAD_SIZE), lambda j: (0, j)),
        ],
        out_shape=[
            jax.ShapeDtypeStruct((rows, all_columns), BF16),
            jax.ShapeDtypeStruct((span - rows, key_value.shape[1]), BF16),
            jax.ShapeDtypeStruct((rows, key_value.shape[1]), F32),
        ],
        scratch_shapes=[
            pltpu.VMEM((span, rows), F32),
            pltpu.VMEM((span, 2 * HEAD_SIZE), F32),
        ],
        compiler_params=pltpu.CompilerParams(vmem_limit_bytes=VMEM_LIMIT),
        cost_estimate=pl.CostEstimate(
            flops=52_000_000_000, bytes_accessed=10_000_000, transcendentals=0
        ),
        name="attention_back",
    )(place, segment_key, segment_query, queries, key_value, lse, dout, cosine, sine)


def expert_kernel(
    slot_row_ref,
    slot_column_ref,
    routed_ref,
    own_ref,
    router_ref,
    tokens_ref,
    cotangent_ref,
    gate_ref,
    up_ref,
    down_ref,
    grad_ref,
    moe_ref,
    rows_in_ref,
    grad_out_ref,
    hidden_ref,
    grad_gate_ref,
    grad_up_ref,
    router_grad_ref,
    gate_full_ref,
    up_full_ref,
    down_full_ref,
    *,
    capacity,
):
    whole = ((gate_ref, gate_full_ref), (up_ref, up_full_ref), (down_ref, down_full_ref))

    @pl.when(pl.program_id(0) == 0)
    def _():
        for held, full in whole:
            columns = held.shape[3]
            for half in range(held.shape[1]):
                full[:, half * columns : (half + 1) * columns] = held[:, half].reshape(-1, columns)

    group_rows = tokens_ref.shape[1]
    tokens = tokens_ref[0]
    gate_weight, up_weight, down_weight = (full[...] for _, full in whole)
    cotangent = cotangent_ref[0]
    routed = routed_ref[0] > 0.0
    logits = jnp.where(routed, mxu(router_ref[...], tokens, FROM_LAST), -1e30)
    weights = jnp.exp(logits - jnp.max(logits, axis=0, keepdims=True))
    weights = jnp.where(routed, weights, 0.0)
    gates = weights / jnp.sum(weights, axis=0, keepdims=True)
    own = own_ref[...]
    gate_own = jnp.sum(gates * own, axis=0, keepdims=True)
    place = slot_row_ref[0] == lax.broadcasted_iota(jnp.int32, (capacity, group_rows), 0)
    place_wide = jnp.where(place, 1.0, 0.0)
    place_low = place_wide.astype(BF16)
    back = slot_column_ref[0] == lax.broadcasted_iota(jnp.int32, (group_rows, capacity), 1)
    back_low = jnp.where(back, 1.0, 0.0).astype(BF16)
    coefficient = jnp.sum(place_wide * gate_own, axis=1, keepdims=True)

    rows_in = mxu(place_low, tokens).astype(BF16)
    rows_in_ref[...] = rows_in
    gate_pre = mxu(rows_in, gate_weight)
    up_pre = mxu(rows_in, up_weight)
    sigmoid = 1.0 / (1.0 + jnp.exp(-gate_pre))
    silu = gate_pre * sigmoid
    hidden = (silu * up_pre).astype(BF16)
    hidden_ref[...] = hidden
    slot_cotangent = mxu(place_low, cotangent)
    grad_out = (coefficient * slot_cotangent).astype(BF16)
    grad_out_ref[...] = grad_out
    grad_hidden = mxu(grad_out, down_weight)
    grad_up = (grad_hidden * silu).astype(BF16)
    grad_gate = (grad_hidden * up_pre * sigmoid * (1.0 + gate_pre * (1.0 - sigmoid))).astype(BF16)
    grad_up_ref[...] = grad_up
    grad_gate_ref[...] = grad_gate
    expert_out = mxu(hidden, down_weight, FROM_LAST)
    grad_slot = jnp.sum(slot_cotangent * expert_out, axis=1, keepdims=True)
    moe_ref[0] = mxu(back_low, (coefficient * expert_out).astype(BF16)).astype(BF16)

    grad_token = jnp.sum(place_wide * grad_slot, axis=0, keepdims=True)
    share = (grad_token * gate_own) * (own - gates)
    share_high = share.astype(BF16)
    share_low = (share - share_high.astype(F32)).astype(BF16)
    router_grad = mxu(share_high, tokens) + mxu(share_low, tokens)

    @pl.when(pl.program_id(0) == 0)
    def _():
        router_grad_ref[...] = router_grad

    @pl.when(pl.program_id(0) > 0)
    def _():
        router_grad_ref[...] += router_grad

    grad_in = mxu(grad_gate, gate_weight, FROM_LAST) + mxu(grad_up, up_weight, FROM_LAST)
    grad_ref[0] = (
        mxu(back_low, grad_in.astype(BF16)) + mxu(share.T.astype(BF16), router_ref[...])
    ).astype(BF16)


def expert_groups(slot, routed, own, router_t, tokens, cotangent, weights, capacity):
    count, group_rows, width = tokens.shape
    ff = weights[0].shape[1] * weights[0].shape[3]
    experts = router_t.shape[0]
    weight = pl.BlockSpec(
        weights[0].shape, lambda g: (0, 0, 0, 0), pipeline_mode=pl.Buffered(1)
    )
    whole = lambda g: (0, 0)
    by_group = lambda g: (g, 0, 0)
    slots = lambda columns: pl.BlockSpec((capacity, columns), lambda g: (g, 0))
    slots_shape = lambda columns: jax.ShapeDtypeStruct((count * capacity, columns), BF16)
    return pl.pallas_call(
        functools.partial(expert_kernel, capacity=capacity),
        grid=(count,),
        in_specs=[
            pl.BlockSpec((1, 1, group_rows), by_group),
            pl.BlockSpec((1, group_rows, 1), by_group),
            pl.BlockSpec((1, experts, group_rows), by_group),
            pl.BlockSpec((experts, 1), whole),
            pl.BlockSpec((experts, width), whole),
            pl.BlockSpec((1, group_rows, width), by_group),
            pl.BlockSpec((1, group_rows, width), by_group),
            weight,
            weight,
            weight,
        ],
        out_specs=[
            pl.BlockSpec((1, group_rows, width), by_group),
            pl.BlockSpec((1, group_rows, width), by_group),
            slots(width),
            slots(width),
            slots(ff),
            slots(ff),
            slots(ff),
            pl.BlockSpec((experts, width), whole),
        ],
        out_shape=[
            jax.ShapeDtypeStruct(tokens.shape, BF16),
            jax.ShapeDtypeStruct(tokens.shape, BF16),
            slots_shape(width),
            slots_shape(width),
            slots_shape(ff),
            slots_shape(ff),
            slots_shape(ff),
            jax.ShapeDtypeStruct((experts, width), F32),
        ],
        scratch_shapes=[pltpu.VMEM((width, ff), BF16) for _ in range(3)],
        compiler_params=pltpu.CompilerParams(vmem_limit_bytes=VMEM_LIMIT),
        cost_estimate=LIGHT,
        name="expert",
    )(
        slot[:, None, :],
        slot[:, :, None],
        routed,
        own,
        router_t,
        tokens,
        cotangent,
        *weights,
    )


def weight_grad_kernel(*refs, halves):
    rows, grad_out, hidden, grad_gate, grad_up, router = (
        refs[at : at + 2] for at in range(0, 12, 2)
    )
    moe_kept_ref, moe_got_ref, out_ref = refs[12:15]
    for at, moe_ref in enumerate(refs[15:]):
        moe_ref[...] = (moe_kept_ref[at].astype(F32) + moe_got_ref[at].astype(F32)).astype(BF16)
    columns = hidden[0].shape[1] // halves
    over = (((0,), (0,)), ((), ()))
    left_rows = [ref[...] for ref in rows]
    left_out = [ref[...] for ref in grad_out]
    router_columns = (router[0][...] + router[1][...]).T
    router_columns = jnp.concatenate(
        [
            router_columns,
            jnp.zeros((router_columns.shape[0], HEAD_SIZE - router_columns.shape[1]), F32),
        ],
        axis=1,
    ).astype(BF16)
    for half in range(halves):
        start = half * (3 * columns + HEAD_SIZE)
        part = slice(half * columns, (half + 1) * columns)
        for at, (left, right) in enumerate(
            ((left_rows, grad_gate), (left_rows, grad_up), (left_out, hidden))
        ):
            total = mxu(left[0], right[0][:, part], over) + mxu(left[1], right[1][:, part], over)
            out_ref[:, start + at * columns : start + (at + 1) * columns] = total.astype(BF16)
        out_ref[:, start + 3 * columns : start + 3 * columns + HEAD_SIZE] = router_columns


def weight_grads(near, far, moe_kept, moe_got, halves, block=256):
    rows_at, grad_out_at, hidden_at, grad_gate_at, grad_up_at, router_at = range(6)
    slots, width = near[rows_at].shape
    ff = near[hidden_at].shape[1]
    experts = near[router_at].shape[0]
    specs, operands = [], []
    for at in (rows_at, grad_out_at, hidden_at, grad_gate_at, grad_up_at, router_at):
        if at in (rows_at, grad_out_at):
            spec = pl.BlockSpec((slots, block), lambda i: (0, i))
        elif at == router_at:
            spec = pl.BlockSpec((experts, block), lambda i: (0, i))
        else:
            spec = pl.BlockSpec((slots, ff), lambda i: (0, 0))
        specs += [spec, spec]
        operands += [near[at], far[at]]
    columns = 3 * ff + halves * HEAD_SIZE
    moe_count, moe_rows, _ = moe_kept.shape
    moe_spec = pl.BlockSpec((moe_count, moe_rows, block), lambda i: (0, 0, i))
    moe_out_spec = pl.BlockSpec((moe_rows, block), lambda i: (0, i))
    return pl.pallas_call(
        functools.partial(weight_grad_kernel, halves=halves),
        grid=(width // block,),
        in_specs=specs + [moe_spec, moe_spec],
        out_specs=[pl.BlockSpec((block, columns), lambda i: (i, 0))] + [moe_out_spec] * moe_count,
        out_shape=[jax.ShapeDtypeStruct((width, columns), BF16)]
        + [jax.ShapeDtypeStruct((moe_rows, width), BF16)] * moe_count,
        compiler_params=pltpu.CompilerParams(vmem_limit_bytes=VMEM_LIMIT),
        cost_estimate=pl.CostEstimate(
            flops=15_000_000_000, bytes_accessed=50_000_000, transcendentals=0
        ),
        name="weight_grads",
    )(*operands, moe_kept, moe_got)


def on_device(
    block_input,
    norm_gains,
    router_weight,
    query_matrix,
    key_matrix,
    value_matrix,
    output_weight,
    gate_weight,
    up_weight,
    down_weight,
    segment_ids,
    routes,
    priority,
    cotangent,
):
    tensor_index = lax.axis_index("tensor")
    own_rows, width = block_input.shape
    group_rows = segment_ids.shape[0]
    halves = lax.axis_size("tensor")
    outer = lax.axis_size("outer")
    groups = lax.axis_size("x") * lax.axis_size("core")
    plane = groups * halves
    shard_rows = query_matrix.shape[0]
    dp_size = outer * groups
    seq_len = min(SEQ_MOST, group_rows * dp_size)
    own_start = lax.axis_index(ALL) * own_rows
    capacity = group_rows * TOPK // EXPERTS
    reach = ATTEND_SPAN // own_rows
    half_ff = gate_weight.shape[2]
    ff = half_ff * halves

    query_columns = query_matrix.shape[1]
    pair_columns = 2 * halves * HEAD_SIZE
    first = tensor_index == 0
    key_value_weight = jnp.concatenate([key_matrix, value_matrix], axis=1)
    other_weight = swap(key_value_weight, "tensor")
    early = jnp.concatenate(
        [
            jnp.where(first, key_value_weight, other_weight),
            jnp.where(first, other_weight, key_value_weight),
            query_matrix,
            output_weight,
        ],
        axis=1,
    )
    early, gate_own, up_own, down_own, cotangent_own = lax.optimization_barrier(
        (early, gate_weight, up_weight, down_weight, cotangent)
    )
    early = outer_gather(early)

    expert_shard = jnp.transpose(jnp.stack([gate_own, up_own, down_own]), (2, 0, 1, 3))
    expert_shard = lax.all_to_all(expert_shard, PLANE, 0, 0, tiled=True)
    expert_shard = expert_shard.reshape(groups, halves, 3, shard_rows, half_ff)
    expert_shard = [
        jnp.swapaxes(expert_shard[:, :, at], 0, 1).reshape(-1, half_ff) for at in range(3)
    ]
    early, expert_shard, segment_here, priority_here = lax.optimization_barrier(
        (early, expert_shard, segment_ids, priority)
    )
    pair_count = group_rows * TOPK
    rank = (
        jnp.zeros((pair_count,), jnp.int32)
        .at[priority_here]
        .set(jnp.arange(pair_count, dtype=jnp.int32))
        .reshape(group_rows, TOPK)
    )
    expert_ids = jnp.arange(EXPERTS, dtype=jnp.int32)
    named = routes[:, :, None] == expert_ids[None, None, :]
    ranked = jnp.sum(jnp.where(named, rank[:, :, None] + 1, 0), axis=1)
    ranked = jnp.where(ranked > 0, ranked, pair_count + 1)
    ranked_own = lax.dynamic_slice_in_dim(ranked, tensor_index * own_rows, own_rows, 0)
    digits = jnp.concatenate([ranked_own // 64, ranked_own % 64], axis=1).astype(BF16)
    digits = jnp.pad(digits, ((0, 0), (0, HEAD_SIZE - digits.shape[1])))
    cotangent_sent = jnp.concatenate([cotangent_own, digits], axis=1)
    segment_near = jnp.concatenate(
        [shift_groups(segment_here, 2), shift_groups(segment_here, 1), segment_here]
    )
    expert_full = [
        lax.all_gather(shard, "outer").reshape(outer, halves, groups * shard_rows, half_ff)
        for shard in expert_shard
    ]

    key_value_full = early[:, :, :pair_columns]
    key_value_full = in_order(key_value_full, swap(key_value_full, "x"), "x", 1)
    key_value_full = in_order(key_value_full, swap(key_value_full, "core"), "core", 2)
    key_value_full = key_value_full.reshape(width, pair_columns)
    query_parts = plane_parts(early[:, :, pair_columns : pair_columns + query_columns])

    input_wide = block_input.astype(F32)
    first_gain = norm_gains[:, 0]
    second_gain = norm_gains[:, 1]
    first_factor = norm_factor(input_wide)
    normed_in = (input_wide * first_factor * first_gain).astype(BF16)
    positions = own_start + jnp.arange(own_rows, dtype=jnp.int32)
    cosine, sine = rotary_tables(positions % seq_len)
    query_blocks = halves * query_columns // (2 * HEAD_SIZE)
    key_value_sent = project(
        normed_in, key_value_full, cosine, sine, 0, halves, (True, False)
    )
    one_back, two_back = shift_groups(key_value_sent, 1), shift_groups(key_value_sent, 2)
    query_parts, one_back, two_back, segment_near, cotangent_sent, expert_full[0] = (
        lax.optimization_barrier(
            (query_parts, one_back, two_back, segment_near, cotangent_sent, expert_full[0])
        )
    )
    cotangent_parts = plane_parts(cotangent_sent)
    output_own = early[:, :, pair_columns + query_columns :]
    pair_sent = jnp.where(
        first,
        jnp.stack([one_back, key_value_sent]),
        jnp.stack([two_back, one_back]),
    )
    pair_got = swap(pair_sent, "tensor")
    query_near = plane_stack(query_parts)
    query_far, pair_got = lax.optimization_barrier((swap(query_near, "core"), pair_got))
    pieces = [two_back, pair_got[0], one_back, pair_got[1], key_value_sent]
    query_full = whole_weight(query_near, query_far)
    queries = project(normed_in, query_full, cosine, sine, 0, query_blocks, (True, True))
    output_parts = plane_parts(output_own)
    expert = lax.axis_index(PLANE)

    def slots_of(cotangents):
        digits = cotangents[..., width:].reshape(2, group_rows, HEAD_SIZE).astype(jnp.int32)
        ranked_all = digits[..., :EXPERTS] * 64 + digits[..., EXPERTS : 2 * EXPERTS]
        routed = jnp.swapaxes((ranked_all <= pair_count).astype(F32), 1, 2)
        rank_own = jnp.sum(jnp.where(expert_ids == expert, ranked_all, 0), axis=-1)
        earlier = (rank_own[:, None, :] < rank_own[:, :, None]).astype(jnp.int32)
        slot = jnp.where(rank_own <= pair_count, jnp.sum(earlier, axis=-1), capacity)
        return slot, routed

    key_value = jnp.concatenate(pieces, axis=0)
    span = ATTEND_SPAN + own_rows
    segment_ext = lax.dynamic_slice_in_dim(segment_near, tensor_index * own_rows, span)
    view = (
        jnp.reshape(own_start, (1,)),
        segment_ext[:, None],
        segment_ext[None, ATTEND_SPAN:],
        queries,
        key_value,
    )
    heads_low, log_total = attention(*view, seq_len)
    heads_late, output_parts, cotangent_parts = lax.optimization_barrier(
        (heads_low, output_parts, cotangent_parts)
    )
    output_near = plane_stack(output_parts)
    output_far = swap(output_near, "core")
    output_full, expert_full[1] = lax.optimization_barrier(
        (whole_weight(output_near, output_far), expert_full[1])
    )
    hidden_state = input_wide + dot(heads_low, output_full, ((1,), (1,)))
    second_factor = norm_factor(hidden_state)
    normed_mid_own = (hidden_state * second_factor * second_gain).astype(BF16)

    cotangent_near = plane_stack(cotangent_parts)
    cotangent_far = swap(cotangent_near, "core")
    near_slots, far_slots = slots_of(cotangent_near), slots_of(cotangent_far)
    normed_parts, expert_full[2] = lax.optimization_barrier(
        (plane_parts(normed_mid_own), expert_full[2])
    )
    normed_near = plane_stack(normed_parts)
    normed_far = swap(normed_near, "core")
    own_expert = (expert_ids == expert).astype(F32)[:, None]
    router_t = router_weight.T

    def experts_on(tokens, cotangents, slots):
        slot, routed = slots
        return expert_groups(
            slot,
            routed,
            own_expert,
            router_t,
            tokens.reshape(2, group_rows, width),
            cotangents.reshape(2, group_rows, -1),
            expert_full,
            capacity,
        )

    on_near = experts_on(normed_near, cotangent_near, near_slots)
    on_far = experts_on(normed_far, cotangent_far, far_slots)
    blocks = (2 * halves, own_rows, width)
    (grad_near, moe_near), (grad_far, moe_far) = (
        [array.reshape(blocks) for array in side[:2]] for side in (on_near, on_far)
    )
    grad_blocks = fold_blocks(grad_near, swap(grad_far, "core"))
    grad_blocks, moe_far, on_near, on_far = lax.optimization_barrier(
        (grad_blocks, moe_far, on_near[2:], on_far[2:])
    )
    grad_mid_parts = fold_plane(grad_blocks)
    expert_part, *moe_blocks = weight_grads(
        on_near, on_far, moe_near, swap(moe_far, "core"), halves
    )
    expert_sum = lax.psum_scatter(expert_part, "outer", scatter_dimension=0, tiled=True)
    grad_mid_parts, moe_blocks = lax.optimization_barrier((grad_mid_parts, moe_blocks))
    moe_parts = fold_plane(moe_blocks)
    grad_mid = wide_sum(grad_mid_parts)

    norm_input_part = norm_back(hidden_state, second_factor, second_gain, grad_mid)
    grad_state = cotangent.astype(F32) + norm_input_part
    grad_attn = grad_state.astype(BF16)
    grad_heads = dot(grad_attn, output_full, ((1,), (0,))).astype(BF16)
    output_total = fold_columns(grad_attn, heads_late, shard_rows)
    grad_query_pre, grad_far_kv, grad_own = attention_back(
        *view, log_total, grad_heads, cosine, sine, seq_len
    )
    grad_query_pre, output_total, moe_parts = lax.optimization_barrier(
        (grad_query_pre, output_total, moe_parts)
    )
    output_parts = fold_plane(distance_blocks(output_total))
    query_total = fold_columns(normed_in, grad_query_pre, shard_rows)
    two_back, pair_old, one_back, pair_new = grad_far_kv.reshape(reach, own_rows, -1)
    pair_got, output_parts, query_total = lax.optimization_barrier(
        (swap(jnp.stack([pair_old, pair_new]), "tensor"), output_parts, query_total)
    )
    query_parts = fold_plane(distance_blocks(query_total))
    pair_old, pair_new = pair_got.astype(F32)
    one_back = one_back.astype(F32) + jnp.where(first, pair_old, pair_new)
    two_back = two_back.astype(F32) + jnp.where(first, 0.0, pair_old)
    grad_own = grad_own + jnp.where(first, pair_new, 0.0)
    grad_own = grad_own + shift_groups(one_back.astype(BF16), -1).astype(F32)
    grad_own = grad_own + shift_groups(two_back.astype(BF16), -2).astype(F32)
    query_parts, output_parts = lax.optimization_barrier((query_parts, output_parts))
    output_weight_grad = outer_scatter(wide_sum(output_parts).astype(BF16))
    grad_key_value = []
    for half in range(halves):
        start = half * 2 * HEAD_SIZE
        key_part = grad_own[:, start : start + HEAD_SIZE]
        turned = jnp.concatenate(
            [key_part[:, HEAD_SIZE // 2 :], key_part[:, : HEAD_SIZE // 2]], axis=1
        )
        grad_key_value.append(key_part * cosine - turned * sine)
        grad_key_value.append(grad_own[:, start + HEAD_SIZE : start + 2 * HEAD_SIZE])
    grad_key_value_pre = jnp.concatenate(grad_key_value, axis=1).astype(BF16)
    key_value_total = fold_columns(normed_in, grad_key_value_pre, shard_rows)
    key_value_total, expert_sum = lax.optimization_barrier((key_value_total, expert_sum))
    key_value_parts = fold_plane(distance_blocks(key_value_total))
    grad_in = dot(grad_query_pre, query_full, ((1,), (1,))) + dot(
        grad_key_value_pre, key_value_full, ((1,), (1,))
    )
    input_grad = grad_state + norm_back(input_wide, first_factor, first_gain, grad_in)
    qkv_grad = outer_scatter(
        jnp.concatenate([wide_sum(query_parts), wide_sum(key_value_parts)], axis=2).astype(BF16)
    )
    block_output = hidden_state + wide_sum(moe_parts)
    expert_sum = expert_sum.reshape(groups, shard_rows, halves, -1)
    expert_sum = jnp.swapaxes(expert_sum, 1, 2).reshape(plane, shard_rows, -1)
    expert_sum = lax.all_to_all(expert_sum, PLANE, 0, 0, tiled=True)
    gate_grad, up_grad, down_grad = (
        jnp.swapaxes(expert_sum[:, :, at * half_ff : (at + 1) * half_ff], 0, 1).astype(F32)
        for at in range(3)
    )
    router_grad = jnp.sum(expert_sum[:, :, 3 * half_ff : 3 * half_ff + EXPERTS].astype(F32), axis=0)
    router_grad = lax.dynamic_slice_in_dim(
        router_grad, tensor_index * (shard_rows // 2), shard_rows // 2, 0
    )
    query_grad = qkv_grad[:, :query_columns]
    key_grad = qkv_grad[:, query_columns : query_columns + HEAD_SIZE]
    value_grad = qkv_grad[:, query_columns + HEAD_SIZE :]

    half_rows = shard_rows // 2
    own_gains = lax.dynamic_slice_in_dim(
        norm_gains, lax.axis_index(DP) * shard_rows, shard_rows, 0
    )
    qkv_own = jnp.concatenate([query_matrix, key_value_weight], axis=1)
    first_sum = jnp.sum(qkv_grad * qkv_own.astype(F32), axis=-1)
    second_sum = jnp.sum(
        gate_grad * gate_weight.astype(F32) + up_grad * up_weight.astype(F32), axis=(1, 2)
    )
    gain_sums = jnp.stack([first_sum, second_sum], axis=1) / own_gains
    kept = lax.dynamic_slice_in_dim(gain_sums, tensor_index * half_rows, half_rows, 0)
    sent = lax.dynamic_slice_in_dim(gain_sums, (1 - tensor_index) * half_rows, half_rows, 0)
    own_router = lax.dynamic_slice_in_dim(
        router_weight, lax.axis_index(ALL) * half_rows, half_rows, 0
    )
    router_sum = jnp.sum(router_grad * own_router.astype(F32), axis=-1)
    half_gains = lax.dynamic_slice_in_dim(own_gains, tensor_index * half_rows, half_rows, 0)
    router_sum = router_sum / half_gains[:, 1]
    gains_grad = (
        kept
        + swap(sent, "tensor")
        + jnp.stack([jnp.zeros_like(router_sum), router_sum], axis=1)
    )
    return (
        block_output,
        input_grad,
        gains_grad,
        router_grad,
        query_grad,
        key_grad,
        value_grad,
        output_weight_grad,
        gate_grad,
        up_grad,
        down_grad,
    )


def solution(mesh):
    dp_size, tensor_size = mesh.shape["dp"], mesh.shape["tensor"]
    split = Mesh(mesh.devices.reshape(dp_size // 4, 2, 2, tensor_size), ALL)
    return jax.shard_map(
        on_device,
        mesh=split,
        in_specs=(
            P(ALL, None),
            P(),
            P(),
            P(DP, "tensor"),
            P(DP, "tensor"),
            P(DP, "tensor"),
            P(DP, "tensor"),
            P(DP, None, "tensor"),
            P(DP, None, "tensor"),
            P(DP, None, "tensor"),
            P(DP),
            P(DP, None),
            P(DP),
            P(ALL, None),
        ),
        out_specs=(
            P(ALL, None),
            P(ALL, None),
            P(ALL, None),
            P(ALL, None),
            P(DP, "tensor"),
            P(DP, "tensor"),
            P(DP, "tensor"),
            P(DP, "tensor"),
            P(DP, None, "tensor"),
            P(DP, None, "tensor"),
            P(DP, None, "tensor"),
        ),
        check_vma=False,
    )
```

```python
import functools
import math

import jax
import jax.numpy as jnp
from jax import lax
from jax.experimental import pallas as pl
from jax.experimental.pallas import tpu as pltpu
from jax.sharding import Mesh
from jax.sharding import PartitionSpec as P

HEAD_SIZE = 128
TOPK = 4
EXPERTS = 8
ATTEND_SPAN = 1024
SEQ_MOST = 16384
EPSILON = 1e-06
ROPE_BASE = 10000.0
BF16 = jnp.bfloat16
F32 = jnp.float32

DP = ("outer", "x", "core")
PLANE = ("x", "core", "tensor")
ALL = ("outer", "x", "core", "tensor")


def shift_groups(x, by):
    length = lax.axis_size(DP)
    return lax.ppermute(x, DP, [(i, i + by) for i in range(length) if 0 <= i + by < length])


def swap(x, axis):
    length = lax.axis_size(axis)
    return lax.ppermute(x, axis, [(i, length - 1 - i) for i in range(length)])


def plane_parts(own):
    return [own, swap(own, "tensor"), swap(own, "x"), swap(own, ("x", "tensor"))]


def plane_stack(parts):
    return jnp.stack(parts).reshape((2, 2) + parts[0].shape)


def whole_weight(near, far):
    x, tensor = lax.axis_index("x"), lax.axis_index("tensor")
    first = lax.axis_index("core") == 0
    by_core = [jnp.where(first, near, far), jnp.where(first, far, near)]

    def piece(x_at, core_at, tensor_at):
        picked = lax.dynamic_index_in_dim(by_core[core_at], x ^ x_at, 0, keepdims=False)
        return lax.dynamic_index_in_dim(picked, tensor ^ tensor_at, 0, keepdims=False)

    places = [(x_at, core_at) for x_at in range(2) for core_at in range(2)]
    halves = [jnp.stack([piece(*place, at) for place in places], 1) for at in range(2)]
    return jnp.concatenate(halves, axis=-1).reshape(-1, 2 * near.shape[-1])


def fold_core(kept, sent):
    return (kept.astype(F32) + swap(sent, "core").astype(F32)).astype(BF16)


def fold_blocks(kept, got):
    return [
        (kept[at].astype(F32) + got[at].astype(F32)).astype(BF16) for at in range(kept.shape[0])
    ]


def in_order(own, other, axis_name, axis):
    first = lax.axis_index(axis_name) == 0
    return jnp.stack([jnp.where(first, own, other), jnp.where(first, other, own)], axis)


def fold_plane(blocks):
    return [
        blocks[0],
        swap(blocks[1], "tensor"),
        swap(blocks[2], "x"),
        swap(blocks[3], ("x", "tensor")),
    ]


def wide_sum(parts):
    return sum(part.astype(F32) for part in parts)


def outer_shift(x, by):
    length = lax.axis_size("outer")
    return lax.ppermute(x, "outer", [(i, (i + by) % length) for i in range(length)])


def outer_gather(shard):
    length, here = lax.axis_size("outer"), lax.axis_index("outer")
    if length > 4:
        return lax.all_gather(shard, "outer")
    full = jnp.zeros((length,) + shard.shape, shard.dtype)
    for by in range(length):
        piece = outer_shift(shard, by) if by else shard
        full = lax.dynamic_update_slice_in_dim(full, piece[None], (here - by) % length, 0)
    return full


def outer_scatter(parts):
    length, here = lax.axis_size("outer"), lax.axis_index("outer")
    if length > 4:
        return lax.psum_scatter(parts, "outer", scatter_dimension=0, tiled=False).astype(F32)
    pieces = [
        lax.dynamic_index_in_dim(parts, (here + by) % length, 0, keepdims=False)
        for by in range(length)
    ]
    return wide_sum([pieces[0]] + [outer_shift(pieces[by], by) for by in range(1, length)])


def core_columns(rows, core_at, shard_rows):
    count = rows.shape[0]
    split = rows.reshape(count, -1, 2, shard_rows)
    return lax.dynamic_index_in_dim(split, core_at, 2, keepdims=False).reshape(count, -1)


def fold_columns(left, right, shard_rows):
    core = lax.axis_index("core")
    sent = dot(core_columns(left, 1 - core, shard_rows), right, ((0,), (0,))).astype(BF16)
    kept = dot(core_columns(left, core, shard_rows), right, ((0,), (0,))).astype(BF16)
    return fold_core(kept, sent).reshape(-1, 2, shard_rows, right.shape[1])


def distance_blocks(total):
    x, tensor = lax.axis_index("x"), lax.axis_index("tensor")
    columns = total.shape[3] // 2
    blocks = []
    for x_by in range(2):
        for tensor_by in range(2):
            block = lax.dynamic_index_in_dim(total, x ^ x_by, 1, keepdims=False)
            start = (tensor ^ tensor_by) * columns
            blocks.append(lax.dynamic_slice_in_dim(block, start, columns, 2))
    return blocks


def rotary_tables(position):
    halfway = HEAD_SIZE // 2
    inverse = jnp.exp(
        jnp.arange(halfway, dtype=F32) * (-2.0 * math.log(ROPE_BASE) / HEAD_SIZE)
    )
    angles = position.astype(F32)[:, None] * inverse[None, :]
    cosine, sine = jnp.cos(angles), jnp.sin(angles)
    return (
        jnp.concatenate([cosine, cosine], axis=1),
        jnp.concatenate([-sine, sine], axis=1),
    )


def norm_factor(value_rows):
    return lax.rsqrt(jnp.mean(value_rows * value_rows, axis=-1, keepdims=True) + EPSILON)


def norm_back(value_rows, factor, gain, upstream):
    weighted = upstream * gain
    return factor * weighted - value_rows * (factor * factor * factor) * jnp.mean(
        weighted * value_rows, axis=-1, keepdims=True
    )


def dot(a, b, dims):
    return lax.dot_general(a, b, (dims, ((), ())), preferred_element_type=F32)


VMEM_LIMIT = 60 * 1024 * 1024
LIGHT = pl.CostEstimate(flops=1000, bytes_accessed=1000, transcendentals=0)
FROM_LAST = (((1,), (1,)), ((), ()))
PLAIN = (((1,), (0,)), ((), ()))


def mxu(a, b, dims=PLAIN):
    return lax.dot_general(a, b, dims, preferred_element_type=F32)


def turn(rows, cosine, sine):
    return rows * cosine + pltpu.roll(rows, HEAD_SIZE // 2, 1) * sine


def project_kernel(rows_ref, weight_ref, cosine_ref, sine_ref, out_ref, *, turned):
    product = mxu(rows_ref[...], weight_ref[...])
    for at, turns in enumerate(turned):
        part = product[:, at * HEAD_SIZE : (at + 1) * HEAD_SIZE]
        if turns:
            part = turn(part, cosine_ref[...], sine_ref[...])
        out_ref[:, at * HEAD_SIZE : (at + 1) * HEAD_SIZE] = part.astype(BF16)


def project(rows, weight, cosine, sine, first, count, turned):
    high, width = rows.shape
    columns = len(turned) * HEAD_SIZE
    return pl.pallas_call(
        functools.partial(project_kernel, turned=turned),
        grid=(count,),
        in_specs=[
            pl.BlockSpec((high, width), lambda j: (0, 0)),
            pl.BlockSpec((width, columns), lambda j: (0, first + j)),
            pl.BlockSpec((high, HEAD_SIZE), lambda j: (0, 0)),
            pl.BlockSpec((high, HEAD_SIZE), lambda j: (0, 0)),
        ],
        out_specs=pl.BlockSpec((high, columns), lambda j: (0, j)),
        out_shape=jax.ShapeDtypeStruct((high, count * columns), BF16),
        compiler_params=pltpu.CompilerParams(vmem_limit_bytes=VMEM_LIMIT),
        cost_estimate=LIGHT,
        name="project",
    )(rows, weight, cosine, sine)


def mask_bias(place_ref, segment_key_ref, segment_query_ref, bias_ref, seq_len):
    span, rows = bias_ref.shape
    start = place_ref[0]
    key_at = lax.broadcasted_iota(jnp.int32, (span, rows), 0)
    query_at = lax.broadcasted_iota(jnp.int32, (span, rows), 1) + ATTEND_SPAN
    distance = query_at - key_at
    position = start + query_at - ATTEND_SPAN
    sequence_at = query_at - lax.rem(position, seq_len)
    allowed = (distance >= 0) & (distance < ATTEND_SPAN) & (key_at >= sequence_at)
    allowed = allowed & (segment_key_ref[...] == segment_query_ref[...])
    bias_ref[...] = jnp.where(allowed, 0.0, -1e30)


def attention_kernel(
    place_ref,
    segment_key_ref,
    segment_query_ref,
    q_ref,
    kv_ref,
    heads_ref,
    lse_ref,
    bias_ref,
    *,
    seq_len,
    scale,
):
    @pl.when(pl.program_id(0) == 0)
    def _():
        mask_bias(place_ref, segment_key_ref, segment_query_ref, bias_ref, seq_len)

    rows = q_ref.shape[0]
    span = kv_ref.shape[0]
    count = q_ref.shape[1] // HEAD_SIZE
    value_t = kv_ref[:, HEAD_SIZE:].T
    chunks = span // rows
    for head in range(count):
        columns = slice(head * HEAD_SIZE, (head + 1) * HEAD_SIZE)
        query = q_ref[:, columns]
        scores = []
        for c in range(chunks):
            part = slice(c * rows, (c + 1) * rows)
            raw = mxu(kv_ref[part, :HEAD_SIZE], query, FROM_LAST)
            scores.append(raw * scale + bias_ref[part, :])
        top = functools.reduce(jnp.maximum, scores)
        top = jnp.max(top, axis=0, keepdims=True)
        total = jnp.zeros_like(top)
        out_t = jnp.zeros((HEAD_SIZE, rows), F32)
        for c in range(chunks):
            weight = jnp.exp(scores[c] - top)
            total = total + jnp.sum(weight, axis=0, keepdims=True)
            out_t = out_t + mxu(value_t[:, c * rows : (c + 1) * rows], weight.astype(BF16))
        heads_ref[:, columns] = (out_t / total).T.astype(BF16)
        lse_ref[0, head : head + 1, :] = top + jnp.log(total)


def attention(place, segment_key, segment_query, queries, key_value, seq_len):
    rows, all_columns = queries.shape
    span = key_value.shape[0]
    pairs = key_value.shape[1] // (2 * HEAD_SIZE)
    columns = all_columns // pairs
    return pl.pallas_call(
        functools.partial(attention_kernel, seq_len=seq_len, scale=1.0 / math.sqrt(HEAD_SIZE)),
        grid=(pairs,),
        in_specs=[
            pl.BlockSpec(memory_space=pltpu.SMEM),
            pl.BlockSpec((span, 1), lambda j: (0, 0)),
            pl.BlockSpec((1, rows), lambda j: (0, 0)),
            pl.BlockSpec((rows, columns), lambda j: (0, j)),
            pl.BlockSpec((span, 2 * HEAD_SIZE), lambda j: (0, j)),
        ],
        out_specs=[
            pl.BlockSpec((rows, columns), lambda j: (0, j)),
            pl.BlockSpec((1, columns // HEAD_SIZE, rows), lambda j: (j, 0, 0)),
        ],
        out_shape=[
            jax.ShapeDtypeStruct((rows, all_columns), BF16),
            jax.ShapeDtypeStruct((pairs, columns // HEAD_SIZE, rows), F32),
        ],
        scratch_shapes=[pltpu.VMEM((span, rows), F32)],
        compiler_params=pltpu.CompilerParams(vmem_limit_bytes=VMEM_LIMIT),
        cost_estimate=LIGHT,
        name="attention",
    )(place, segment_key, segment_query, queries, key_value)


def attention_back_kernel(
    place_ref,
    segment_key_ref,
    segment_query_ref,
    q_ref,
    kv_ref,
    lse_ref,
    dout_ref,
    cosine_ref,
    sine_ref,
    dq_ref,
    dkv_far_ref,
    dkv_own_ref,
    bias_ref,
    dkv_ref,
    *,
    seq_len,
    scale,
):
    @pl.when(pl.program_id(0) == 0)
    def _():
        mask_bias(place_ref, segment_key_ref, segment_query_ref, bias_ref, seq_len)

    rows = q_ref.shape[0]
    span = kv_ref.shape[0]
    count = q_ref.shape[1] // HEAD_SIZE
    key_t = kv_ref[:, :HEAD_SIZE].T
    chunks = span // rows
    dkv_ref[...] = jnp.zeros_like(dkv_ref)
    for head in range(count):
        columns = slice(head * HEAD_SIZE, (head + 1) * HEAD_SIZE)
        query = q_ref[:, columns]
        dout = dout_ref[:, columns]
        lse = lse_ref[0, head : head + 1, :]
        probs, dprobs = [], []
        row_dot = jnp.zeros_like(lse)
        for c in range(chunks):
            part = slice(c * rows, (c + 1) * rows)
            raw = mxu(kv_ref[part, :HEAD_SIZE], query, FROM_LAST)
            prob = jnp.exp(raw * scale + bias_ref[part, :] - lse)
            dprob = mxu(kv_ref[part, HEAD_SIZE:], dout, FROM_LAST)
            row_dot = row_dot + jnp.sum(prob * dprob, axis=0, keepdims=True)
            probs.append(prob)
            dprobs.append(dprob)
        dq_t = jnp.zeros((HEAD_SIZE, rows), F32)
        for c in range(chunks):
            part = slice(c * rows, (c + 1) * rows)
            dscore = (probs[c] * (dprobs[c] - row_dot)).astype(BF16)
            dkv_ref[part, :HEAD_SIZE] += mxu(dscore, query)
            dkv_ref[part, HEAD_SIZE:] += mxu(probs[c].astype(BF16), dout)
            dq_t = dq_t + mxu(key_t[:, part], dscore)
        dq_ref[:, columns] = turn(dq_t.T * scale, cosine_ref[...], -sine_ref[...]).astype(BF16)
    dkv_ref[:, :HEAD_SIZE] = dkv_ref[:, :HEAD_SIZE] * scale
    dkv_far_ref[...] = dkv_ref[: span - rows, :].astype(BF16)
    dkv_own_ref[...] = dkv_ref[span - rows :, :]


def attention_back(
    place, segment_key, segment_query, queries, key_value, lse, dout, cosine, sine, seq_len
):
    rows, all_columns = queries.shape
    span = key_value.shape[0]
    pairs = key_value.shape[1] // (2 * HEAD_SIZE)
    columns = all_columns // pairs
    return pl.pallas_call(
        functools.partial(
            attention_back_kernel, seq_len=seq_len, scale=1.0 / math.sqrt(HEAD_SIZE)
        ),
        grid=(pairs,),
        in_specs=[
            pl.BlockSpec(memory_space=pltpu.SMEM),
            pl.BlockSpec((span, 1), lambda j: (0, 0)),
            pl.BlockSpec((1, rows), lambda j: (0, 0)),
            pl.BlockSpec((rows, columns), lambda j: (0, j)),
            pl.BlockSpec((span, 2 * HEAD_SIZE), lambda j: (0, j)),
            pl.BlockSpec((1, columns // HEAD_SIZE, rows), lambda j: (j, 0, 0)),
            pl.BlockSpec((rows, columns), lambda j: (0, j)),
            pl.BlockSpec((rows, HEAD_SIZE), lambda j: (0, 0)),
            pl.BlockSpec((rows, HEAD_SIZE), lambda j: (0, 0)),
        ],
        out_specs=[
            pl.BlockSpec((rows, columns), lambda j: (0, j)),
            pl.BlockSpec((span - rows, 2 * HEAD_SIZE), lambda j: (0, j)),
            pl.BlockSpec((rows, 2 * HEAD_SIZE), lambda j: (0, j)),
        ],
        out_shape=[
            jax.ShapeDtypeStruct((rows, all_columns), BF16),
            jax.ShapeDtypeStruct((span - rows, key_value.shape[1]), BF16),
            jax.ShapeDtypeStruct((rows, key_value.shape[1]), F32),
        ],
        scratch_shapes=[
            pltpu.VMEM((span, rows), F32),
            pltpu.VMEM((span, 2 * HEAD_SIZE), F32),
        ],
        compiler_params=pltpu.CompilerParams(vmem_limit_bytes=VMEM_LIMIT),
        cost_estimate=pl.CostEstimate(
            flops=52_000_000_000, bytes_accessed=10_000_000, transcendentals=0
        ),
        name="attention_back",
    )(place, segment_key, segment_query, queries, key_value, lse, dout, cosine, sine)


def expert_kernel(
    slot_row_ref,
    slot_column_ref,
    routed_ref,
    own_ref,
    router_ref,
    tokens_ref,
    cotangent_ref,
    gate_ref,
    up_ref,
    down_ref,
    grad_ref,
    moe_ref,
    rows_in_ref,
    grad_out_ref,
    hidden_ref,
    grad_gate_ref,
    grad_up_ref,
    router_grad_ref,
    gate_full_ref,
    up_full_ref,
    down_full_ref,
    *,
    capacity,
):
    whole = ((gate_ref, gate_full_ref), (up_ref, up_full_ref), (down_ref, down_full_ref))

    @pl.when(pl.program_id(0) == 0)
    def _():
        for held, full in whole:
            columns = held.shape[3]
            for half in range(held.shape[1]):
                full[:, half * columns : (half + 1) * columns] = held[:, half].reshape(-1, columns)

    group_rows = tokens_ref.shape[1]
    tokens = tokens_ref[0]
    gate_weight, up_weight, down_weight = (full[...] for _, full in whole)
    cotangent = cotangent_ref[0]
    routed = routed_ref[0] > 0.0
    logits = jnp.where(routed, mxu(router_ref[...], tokens, FROM_LAST), -1e30)
    weights = jnp.exp(logits - jnp.max(logits, axis=0, keepdims=True))
    weights = jnp.where(routed, weights, 0.0)
    gates = weights / jnp.sum(weights, axis=0, keepdims=True)
    own = own_ref[...]
    gate_own = jnp.sum(gates * own, axis=0, keepdims=True)
    place = slot_row_ref[0] == lax.broadcasted_iota(jnp.int32, (capacity, group_rows), 0)
    place_wide = jnp.where(place, 1.0, 0.0)
    place_low = place_wide.astype(BF16)
    back = slot_column_ref[0] == lax.broadcasted_iota(jnp.int32, (group_rows, capacity), 1)
    back_low = jnp.where(back, 1.0, 0.0).astype(BF16)
    coefficient = jnp.sum(place_wide * gate_own, axis=1, keepdims=True)

    rows_in = mxu(place_low, tokens).astype(BF16)
    rows_in_ref[...] = rows_in
    gate_pre = mxu(rows_in, gate_weight)
    up_pre = mxu(rows_in, up_weight)
    sigmoid = 1.0 / (1.0 + jnp.exp(-gate_pre))
    silu = gate_pre * sigmoid
    hidden = (silu * up_pre).astype(BF16)
    hidden_ref[...] = hidden
    slot_cotangent = mxu(place_low, cotangent)
    grad_out = (coefficient * slot_cotangent).astype(BF16)
    grad_out_ref[...] = grad_out
    grad_hidden = mxu(grad_out, down_weight)
    grad_up = (grad_hidden * silu).astype(BF16)
    grad_gate = (grad_hidden * up_pre * sigmoid * (1.0 + gate_pre * (1.0 - sigmoid))).astype(BF16)
    grad_up_ref[...] = grad_up
    grad_gate_ref[...] = grad_gate
    expert_out = mxu(hidden, down_weight, FROM_LAST)
    grad_slot = jnp.sum(slot_cotangent * expert_out, axis=1, keepdims=True)
    moe_ref[0] = mxu(back_low, (coefficient * expert_out).astype(BF16)).astype(BF16)

    grad_token = jnp.sum(place_wide * grad_slot, axis=0, keepdims=True)
    share = (grad_token * gate_own) * (own - gates)
    share_high = share.astype(BF16)
    share_low = (share - share_high.astype(F32)).astype(BF16)
    router_grad = mxu(share_high, tokens) + mxu(share_low, tokens)

    @pl.when(pl.program_id(0) == 0)
    def _():
        router_grad_ref[...] = router_grad

    @pl.when(pl.program_id(0) > 0)
    def _():
        router_grad_ref[...] += router_grad

    grad_in = mxu(grad_gate, gate_weight, FROM_LAST) + mxu(grad_up, up_weight, FROM_LAST)
    grad_ref[0] = (
        mxu(back_low, grad_in.astype(BF16)) + mxu(share.T.astype(BF16), router_ref[...])
    ).astype(BF16)


def expert_groups(slot, routed, own, router_t, tokens, cotangent, weights, capacity):
    count, group_rows, width = tokens.shape
    ff = weights[0].shape[1] * weights[0].shape[3]
    experts = router_t.shape[0]
    weight = pl.BlockSpec(
        weights[0].shape, lambda g: (0, 0, 0, 0), pipeline_mode=pl.Buffered(1)
    )
    whole = lambda g: (0, 0)
    by_group = lambda g: (g, 0, 0)
    slots = lambda columns: pl.BlockSpec((capacity, columns), lambda g: (g, 0))
    slots_shape = lambda columns: jax.ShapeDtypeStruct((count * capacity, columns), BF16)
    return pl.pallas_call(
        functools.partial(expert_kernel, capacity=capacity),
        grid=(count,),
        in_specs=[
            pl.BlockSpec((1, 1, group_rows), by_group),
            pl.BlockSpec((1, group_rows, 1), by_group),
            pl.BlockSpec((1, experts, group_rows), by_group),
            pl.BlockSpec((experts, 1), whole),
            pl.BlockSpec((experts, width), whole),
            pl.BlockSpec((1, group_rows, width), by_group),
            pl.BlockSpec((1, group_rows, width), by_group),
            weight,
            weight,
            weight,
        ],
        out_specs=[
            pl.BlockSpec((1, group_rows, width), by_group),
            pl.BlockSpec((1, group_rows, width), by_group),
            slots(width),
            slots(width),
            slots(ff),
            slots(ff),
            slots(ff),
            pl.BlockSpec((experts, width), whole),
        ],
        out_shape=[
            jax.ShapeDtypeStruct(tokens.shape, BF16),
            jax.ShapeDtypeStruct(tokens.shape, BF16),
            slots_shape(width),
            slots_shape(width),
            slots_shape(ff),
            slots_shape(ff),
            slots_shape(ff),
            jax.ShapeDtypeStruct((experts, width), F32),
        ],
        scratch_shapes=[pltpu.VMEM((width, ff), BF16) for _ in range(3)],
        compiler_params=pltpu.CompilerParams(vmem_limit_bytes=VMEM_LIMIT),
        cost_estimate=LIGHT,
        name="expert",
    )(
        slot[:, None, :],
        slot[:, :, None],
        routed,
        own,
        router_t,
        tokens,
        cotangent,
        *weights,
    )


def weight_grad_kernel(*refs, halves):
    rows, grad_out, hidden, grad_gate, grad_up, router = (
        refs[at : at + 2] for at in range(0, 12, 2)
    )
    moe_kept_ref, moe_got_ref, out_ref = refs[12:15]
    for at, moe_ref in enumerate(refs[15:]):
        moe_ref[...] = (moe_kept_ref[at].astype(F32) + moe_got_ref[at].astype(F32)).astype(BF16)
    columns = hidden[0].shape[1] // halves
    over = (((0,), (0,)), ((), ()))
    left_rows = [ref[...] for ref in rows]
    left_out = [ref[...] for ref in grad_out]
    router_columns = (router[0][...] + router[1][...]).T
    router_columns = jnp.concatenate(
        [
            router_columns,
            jnp.zeros((router_columns.shape[0], HEAD_SIZE - router_columns.shape[1]), F32),
        ],
        axis=1,
    ).astype(BF16)
    for half in range(halves):
        start = half * (3 * columns + HEAD_SIZE)
        part = slice(half * columns, (half + 1) * columns)
        for at, (left, right) in enumerate(
            ((left_rows, grad_gate), (left_rows, grad_up), (left_out, hidden))
        ):
            total = mxu(left[0], right[0][:, part], over) + mxu(left[1], right[1][:, part], over)
            out_ref[:, start + at * columns : start + (at + 1) * columns] = total.astype(BF16)
        out_ref[:, start + 3 * columns : start + 3 * columns + HEAD_SIZE] = router_columns


def weight_grads(near, far, moe_kept, moe_got, halves, block=256):
    rows_at, grad_out_at, hidden_at, grad_gate_at, grad_up_at, router_at = range(6)
    slots, width = near[rows_at].shape
    ff = near[hidden_at].shape[1]
    experts = near[router_at].shape[0]
    specs, operands = [], []
    for at in (rows_at, grad_out_at, hidden_at, grad_gate_at, grad_up_at, router_at):
        if at in (rows_at, grad_out_at):
            spec = pl.BlockSpec((slots, block), lambda i: (0, i))
        elif at == router_at:
            spec = pl.BlockSpec((experts, block), lambda i: (0, i))
        else:
            spec = pl.BlockSpec((slots, ff), lambda i: (0, 0))
        specs += [spec, spec]
        operands += [near[at], far[at]]
    columns = 3 * ff + halves * HEAD_SIZE
    moe_count, moe_rows, _ = moe_kept.shape
    moe_spec = pl.BlockSpec((moe_count, moe_rows, block), lambda i: (0, 0, i))
    moe_out_spec = pl.BlockSpec((moe_rows, block), lambda i: (0, i))
    return pl.pallas_call(
        functools.partial(weight_grad_kernel, halves=halves),
        grid=(width // block,),
        in_specs=specs + [moe_spec, moe_spec],
        out_specs=[pl.BlockSpec((block, columns), lambda i: (i, 0))] + [moe_out_spec] * moe_count,
        out_shape=[jax.ShapeDtypeStruct((width, columns), BF16)]
        + [jax.ShapeDtypeStruct((moe_rows, width), BF16)] * moe_count,
        compiler_params=pltpu.CompilerParams(vmem_limit_bytes=VMEM_LIMIT),
        cost_estimate=pl.CostEstimate(
            flops=15_000_000_000, bytes_accessed=50_000_000, transcendentals=0
        ),
        name="weight_grads",
    )(*operands, moe_kept, moe_got)


def on_device(
    block_input,
    norm_gains,
    router_weight,
    query_matrix,
    key_matrix,
    value_matrix,
    output_weight,
    gate_weight,
    up_weight,
    down_weight,
    segment_ids,
    routes,
    priority,
    cotangent,
):
    tensor_index = lax.axis_index("tensor")
    own_rows, width = block_input.shape
    group_rows = segment_ids.shape[0]
    halves = lax.axis_size("tensor")
    outer = lax.axis_size("outer")
    groups = lax.axis_size("x") * lax.axis_size("core")
    plane = groups * halves
    shard_rows = query_matrix.shape[0]
    dp_size = outer * groups
    seq_len = min(SEQ_MOST, group_rows * dp_size)
    own_start = lax.axis_index(ALL) * own_rows
    capacity = group_rows * TOPK // EXPERTS
    reach = ATTEND_SPAN // own_rows
    half_ff = gate_weight.shape[2]
    ff = half_ff * halves

    query_columns = query_matrix.shape[1]
    pair_columns = 2 * halves * HEAD_SIZE
    first = tensor_index == 0
    key_value_weight = jnp.concatenate([key_matrix, value_matrix], axis=1)
    other_weight = swap(key_value_weight, "tensor")
    early = jnp.concatenate(
        [
            jnp.where(first, key_value_weight, other_weight),
            jnp.where(first, other_weight, key_value_weight),
            query_matrix,
            output_weight,
        ],
        axis=1,
    )
    early, gate_own, up_own, down_own, cotangent_own = lax.optimization_barrier(
        (early, gate_weight, up_weight, down_weight, cotangent)
    )
    early = outer_gather(early)

    expert_shard = jnp.transpose(jnp.stack([gate_own, up_own, down_own]), (2, 0, 1, 3))
    expert_shard = lax.all_to_all(expert_shard, PLANE, 0, 0, tiled=True)
    expert_shard = expert_shard.reshape(groups, halves, 3, shard_rows, half_ff)
    expert_shard = [
        jnp.swapaxes(expert_shard[:, :, at], 0, 1).reshape(-1, half_ff) for at in range(3)
    ]
    early, expert_shard, segment_here, priority_here = lax.optimization_barrier(
        (early, expert_shard, segment_ids, priority)
    )
    pair_count = group_rows * TOPK
    rank = (
        jnp.zeros((pair_count,), jnp.int32)
        .at[priority_here]
        .set(jnp.arange(pair_count, dtype=jnp.int32))
        .reshape(group_rows, TOPK)
    )
    expert_ids = jnp.arange(EXPERTS, dtype=jnp.int32)
    named = routes[:, :, None] == expert_ids[None, None, :]
    ranked = jnp.sum(jnp.where(named, rank[:, :, None] + 1, 0), axis=1)
    ranked = jnp.where(ranked > 0, ranked, pair_count + 1)
    ranked_own = lax.dynamic_slice_in_dim(ranked, tensor_index * own_rows, own_rows, 0)
    digits = jnp.concatenate([ranked_own // 64, ranked_own % 64], axis=1).astype(BF16)
    digits = jnp.pad(digits, ((0, 0), (0, HEAD_SIZE - digits.shape[1])))
    cotangent_sent = jnp.concatenate([cotangent_own, digits], axis=1)
    segment_near = jnp.concatenate(
        [shift_groups(segment_here, 2), shift_groups(segment_here, 1), segment_here]
    )
    expert_full = [
        lax.all_gather(shard, "outer").reshape(outer, halves, groups * shard_rows, half_ff)
        for shard in expert_shard
    ]

    key_value_full = early[:, :, :pair_columns]
    key_value_full = in_order(key_value_full, swap(key_value_full, "x"), "x", 1)
    key_value_full = in_order(key_value_full, swap(key_value_full, "core"), "core", 2)
    key_value_full = key_value_full.reshape(width, pair_columns)
    query_parts = plane_parts(early[:, :, pair_columns : pair_columns + query_columns])

    input_wide = block_input.astype(F32)
    first_gain = norm_gains[:, 0]
    second_gain = norm_gains[:, 1]
    first_factor = norm_factor(input_wide)
    normed_in = (input_wide * first_factor * first_gain).astype(BF16)
    positions = own_start + jnp.arange(own_rows, dtype=jnp.int32)
    cosine, sine = rotary_tables(positions % seq_len)
    query_blocks = halves * query_columns // (2 * HEAD_SIZE)
    key_value_sent = project(
        normed_in, key_value_full, cosine, sine, 0, halves, (True, False)
    )
    one_back, two_back = shift_groups(key_value_sent, 1), shift_groups(key_value_sent, 2)
    query_parts, one_back, two_back, segment_near, cotangent_sent, expert_full[0] = (
        lax.optimization_barrier(
            (query_parts, one_back, two_back, segment_near, cotangent_sent, expert_full[0])
        )
    )
    cotangent_parts = plane_parts(cotangent_sent)
    output_own = early[:, :, pair_columns + query_columns :]
    pair_sent = jnp.where(
        first,
        jnp.stack([one_back, key_value_sent]),
        jnp.stack([two_back, one_back]),
    )
    pair_got = swap(pair_sent, "tensor")
    query_near = plane_stack(query_parts)
    query_far, pair_got = lax.optimization_barrier((swap(query_near, "core"), pair_got))
    pieces = [two_back, pair_got[0], one_back, pair_got[1], key_value_sent]
    query_full = whole_weight(query_near, query_far)
    queries = project(normed_in, query_full, cosine, sine, 0, query_blocks, (True, True))
    output_parts = plane_parts(output_own)
    expert = lax.axis_index(PLANE)

    def slots_of(cotangents):
        digits = cotangents[..., width:].reshape(2, group_rows, HEAD_SIZE).astype(jnp.int32)
        ranked_all = digits[..., :EXPERTS] * 64 + digits[..., EXPERTS : 2 * EXPERTS]
        routed = jnp.swapaxes((ranked_all <= pair_count).astype(F32), 1, 2)
        rank_own = jnp.sum(jnp.where(expert_ids == expert, ranked_all, 0), axis=-1)
        earlier = (rank_own[:, None, :] < rank_own[:, :, None]).astype(jnp.int32)
        slot = jnp.where(rank_own <= pair_count, jnp.sum(earlier, axis=-1), capacity)
        return slot, routed

    key_value = jnp.concatenate(pieces, axis=0)
    span = ATTEND_SPAN + own_rows
    segment_ext = lax.dynamic_slice_in_dim(segment_near, tensor_index * own_rows, span)
    view = (
        jnp.reshape(own_start, (1,)),
        segment_ext[:, None],
        segment_ext[None, ATTEND_SPAN:],
        queries,
        key_value,
    )
    heads_low, log_total = attention(*view, seq_len)
    heads_late, output_parts, cotangent_parts = lax.optimization_barrier(
        (heads_low, output_parts, cotangent_parts)
    )
    output_near = plane_stack(output_parts)
    output_far = swap(output_near, "core")
    output_full, expert_full[1] = lax.optimization_barrier(
        (whole_weight(output_near, output_far), expert_full[1])
    )
    hidden_state = input_wide + dot(heads_low, output_full, ((1,), (1,)))
    second_factor = norm_factor(hidden_state)
    normed_mid_own = (hidden_state * second_factor * second_gain).astype(BF16)

    cotangent_near = plane_stack(cotangent_parts)
    cotangent_far = swap(cotangent_near, "core")
    near_slots, far_slots = slots_of(cotangent_near), slots_of(cotangent_far)
    normed_parts, expert_full[2] = lax.optimization_barrier(
        (plane_parts(normed_mid_own), expert_full[2])
    )
    normed_near = plane_stack(normed_parts)
    normed_far = swap(normed_near, "core")
    own_expert = (expert_ids == expert).astype(F32)[:, None]
    router_t = router_weight.T

    def experts_on(tokens, cotangents, slots):
        slot, routed = slots
        return expert_groups(
            slot,
            routed,
            own_expert,
            router_t,
            tokens.reshape(2, group_rows, width),
            cotangents.reshape(2, group_rows, -1),
            expert_full,
            capacity,
        )

    on_near = experts_on(normed_near, cotangent_near, near_slots)
    on_far = experts_on(normed_far, cotangent_far, far_slots)
    blocks = (2 * halves, own_rows, width)
    (grad_near, moe_near), (grad_far, moe_far) = (
        [array.reshape(blocks) for array in side[:2]] for side in (on_near, on_far)
    )
    grad_blocks = fold_blocks(grad_near, swap(grad_far, "core"))
    grad_blocks, moe_far, on_near, on_far = lax.optimization_barrier(
        (grad_blocks, moe_far, on_near[2:], on_far[2:])
    )
    grad_mid_parts = fold_plane(grad_blocks)
    expert_part, *moe_blocks = weight_grads(
        on_near, on_far, moe_near, swap(moe_far, "core"), halves
    )
    expert_sum = lax.psum_scatter(expert_part, "outer", scatter_dimension=0, tiled=True)
    grad_mid_parts, moe_blocks = lax.optimization_barrier((grad_mid_parts, moe_blocks))
    moe_parts = fold_plane(moe_blocks)
    grad_mid = wide_sum(grad_mid_parts)

    norm_input_part = norm_back(hidden_state, second_factor, second_gain, grad_mid)
    grad_state = cotangent.astype(F32) + norm_input_part
    grad_attn = grad_state.astype(BF16)
    grad_heads = dot(grad_attn, output_full, ((1,), (0,))).astype(BF16)
    output_total = fold_columns(grad_attn, heads_late, shard_rows)
    grad_query_pre, grad_far_kv, grad_own = attention_back(
        *view, log_total, grad_heads, cosine, sine, seq_len
    )
    grad_query_pre, output_total, moe_parts = lax.optimization_barrier(
        (grad_query_pre, output_total, moe_parts)
    )
    output_parts = fold_plane(distance_blocks(output_total))
    query_total = fold_columns(normed_in, grad_query_pre, shard_rows)
    two_back, pair_old, one_back, pair_new = grad_far_kv.reshape(reach, own_rows, -1)
    pair_got, output_parts, query_total = lax.optimization_barrier(
        (swap(jnp.stack([pair_old, pair_new]), "tensor"), output_parts, query_total)
    )
    query_parts = fold_plane(distance_blocks(query_total))
    pair_old, pair_new = pair_got.astype(F32)
    one_back = one_back.astype(F32) + jnp.where(first, pair_old, pair_new)
    two_back = two_back.astype(F32) + jnp.where(first, 0.0, pair_old)
    grad_own = grad_own + jnp.where(first, pair_new, 0.0)
    grad_own = grad_own + shift_groups(one_back.astype(BF16), -1).astype(F32)
    grad_own = grad_own + shift_groups(two_back.astype(BF16), -2).astype(F32)
    query_parts, output_parts = lax.optimization_barrier((query_parts, output_parts))
    output_weight_grad = outer_scatter(wide_sum(output_parts).astype(BF16))
    grad_key_value = []
    for half in range(halves):
        start = half * 2 * HEAD_SIZE
        key_part = grad_own[:, start : start + HEAD_SIZE]
        turned = jnp.concatenate(
            [key_part[:, HEAD_SIZE // 2 :], key_part[:, : HEAD_SIZE // 2]], axis=1
        )
        grad_key_value.append(key_part * cosine - turned * sine)
        grad_key_value.append(grad_own[:, start + HEAD_SIZE : start + 2 * HEAD_SIZE])
    grad_key_value_pre = jnp.concatenate(grad_key_value, axis=1).astype(BF16)
    key_value_total = fold_columns(normed_in, grad_key_value_pre, shard_rows)
    key_value_parts = fold_plane(distance_blocks(key_value_total))
    grad_in = dot(grad_query_pre, query_full, ((1,), (1,))) + dot(
        grad_key_value_pre, key_value_full, ((1,), (1,))
    )
    grad_in, expert_sum = lax.optimization_barrier((grad_in, expert_sum))
    input_grad = grad_state + norm_back(input_wide, first_factor, first_gain, grad_in)
    qkv_grad = outer_scatter(
        jnp.concatenate([wide_sum(query_parts), wide_sum(key_value_parts)], axis=2).astype(BF16)
    )
    block_output = hidden_state + wide_sum(moe_parts)
    expert_sum = expert_sum.reshape(groups, shard_rows, halves, -1)
    expert_sum = jnp.swapaxes(expert_sum, 1, 2).reshape(plane, shard_rows, -1)
    expert_sum = lax.all_to_all(expert_sum, PLANE, 0, 0, tiled=True)
    gate_grad, up_grad, down_grad = (
        jnp.swapaxes(expert_sum[:, :, at * half_ff : (at + 1) * half_ff], 0, 1).astype(F32)
        for at in range(3)
    )
    router_grad = jnp.sum(expert_sum[:, :, 3 * half_ff : 3 * half_ff + EXPERTS].astype(F32), axis=0)
    router_grad = lax.dynamic_slice_in_dim(
        router_grad, tensor_index * (shard_rows // 2), shard_rows // 2, 0
    )
    query_grad = qkv_grad[:, :query_columns]
    key_grad = qkv_grad[:, query_columns : query_columns + HEAD_SIZE]
    value_grad = qkv_grad[:, query_columns + HEAD_SIZE :]

    half_rows = shard_rows // 2
    own_gains = lax.dynamic_slice_in_dim(
        norm_gains, lax.axis_index(DP) * shard_rows, shard_rows, 0
    )
    qkv_own = jnp.concatenate([query_matrix, key_value_weight], axis=1)
    first_sum = jnp.sum(qkv_grad * qkv_own.astype(F32), axis=-1)
    second_sum = jnp.sum(
        gate_grad * gate_weight.astype(F32) + up_grad * up_weight.astype(F32), axis=(1, 2)
    )
    gain_sums = jnp.stack([first_sum, second_sum], axis=1) / own_gains
    kept = lax.dynamic_slice_in_dim(gain_sums, tensor_index * half_rows, half_rows, 0)
    sent = lax.dynamic_slice_in_dim(gain_sums, (1 - tensor_index) * half_rows, half_rows, 0)
    own_router = lax.dynamic_slice_in_dim(
        router_weight, lax.axis_index(ALL) * half_rows, half_rows, 0
    )
    router_sum = jnp.sum(router_grad * own_router.astype(F32), axis=-1)
    half_gains = lax.dynamic_slice_in_dim(own_gains, tensor_index * half_rows, half_rows, 0)
    router_sum = router_sum / half_gains[:, 1]
    gains_grad = (
        kept
        + swap(sent, "tensor")
        + jnp.stack([jnp.zeros_like(router_sum), router_sum], axis=1)
    )
    return (
        block_output,
        input_grad,
        gains_grad,
        router_grad,
        query_grad,
        key_grad,
        value_grad,
        output_weight_grad,
        gate_grad,
        up_grad,
        down_grad,
    )


def solution(mesh):
    dp_size, tensor_size = mesh.shape["dp"], mesh.shape["tensor"]
    split = Mesh(mesh.devices.reshape(dp_size // 4, 2, 2, tensor_size), ALL)
    return jax.shard_map(
        on_device,
        mesh=split,
        in_specs=(
            P(ALL, None),
            P(),
            P(),
            P(DP, "tensor"),
            P(DP, "tensor"),
            P(DP, "tensor"),
            P(DP, "tensor"),
            P(DP, None, "tensor"),
            P(DP, None, "tensor"),
            P(DP, None, "tensor"),
            P(DP),
            P(DP, None),
            P(DP),
            P(ALL, None),
        ),
        out_specs=(
            P(ALL, None),
            P(ALL, None),
            P(ALL, None),
            P(ALL, None),
            P(DP, "tensor"),
            P(DP, "tensor"),
            P(DP, "tensor"),
            P(DP, "tensor"),
            P(DP, None, "tensor"),
            P(DP, None, "tensor"),
            P(DP, None, "tensor"),
        ),
        check_vma=False,
    )
```
